32 devices in a mesh: section: 2 (over core), dp: 16 (over z, y, x).
Axes of the slice: x: 2, y: 2, z: 4, core: 2. Of those that a mesh axis runs over, the one named last changes fastest.
Arguments:
- z_noise: float32 [96, 256, 256], P('dp'), may hold values from -6 to 6
- eps_noise: float32 [96, 256, 256], P('dp'), may hold values from -6 to 6
- levels: int32 [96], P('dp'), may hold values from 0 to 999
- counts: int32 [16], P('dp'), may hold values from 1 to 6, as said below
- gen_w: float32 [2, 6656, 256], P('section', 'dp')
- gen_m: float32 [2, 6656, 256], P('section', 'dp'), may hold values from -9.536743e-07 to 9.536743e-07
- gen_v: float32 [2, 6656, 256], P('section', 'dp'), may hold values from 1.4648437e-16 to 2.3498534e-15
- gen_ema: float32 [2, 6656, 256], P('section', 'dp')
- gen_small: float32 [2, 13, 256], P('section')
- gen_small_m: float32 [2, 13, 256], P('section'), may hold values from -3.8146973e-06 to 3.8146973e-06
- gen_small_v: float32 [2, 13, 256], P('section'), may hold values from 2.3498534e-15 to 3.753662e-14
- gen_small_ema: float32 [2, 13, 256], P('section')
- fake_w: float32 [2, 6656, 256], P('section', 'dp')
- fake_m: float32 [2, 6656, 256], P('section', 'dp'), may hold values from -9.536743e-07 to 9.536743e-07
- fake_v: float32 [2, 6656, 256], P('section', 'dp'), may hold values from 1.4648437e-16 to 2.3498534e-15
- fake_small: float32 [2, 13, 256], P('section')
- fake_small_m: float32 [2, 13, 256], P('section'), may hold values from -3.8146973e-06 to 3.8146973e-06
- fake_small_v: float32 [2, 13, 256], P('section'), may hold values from 2.3498534e-15 to 3.753662e-14
- teacher_w: bfloat16 [2, 6656, 256], P('section', 'dp')
- teacher_small: float32 [2, 13, 256], P('section')
Outputs:
- gen_w_out: float32 [2, 6656, 256], P('section', 'dp')
- gen_m_out: float32 [2, 6656, 256], P('section', 'dp')
- gen_v_out: float32 [2, 6656, 256], P('section', 'dp')
- gen_ema_out: float32 [2, 6656, 256], P('section', 'dp')
- gen_small_out: float32 [2, 13, 256], P('section')
- gen_small_m_out: float32 [2, 13, 256], P('section')
- gen_small_v_out: float32 [2, 13, 256], P('section')
- gen_small_ema_out: float32 [2, 13, 256], P('section')
- fake_w_out: float32 [2, 6656, 256], P('section', 'dp')
- fake_m_out: float32 [2, 6656, 256], P('section', 'dp')
- fake_v_out: float32 [2, 6656, 256], P('section', 'dp')
- fake_small_out: float32 [2, 13, 256], P('section')
- fake_small_m_out: float32 [2, 13, 256], P('section')
- fake_small_v_out: float32 [2, 13, 256], P('section')
- norms: float32 [2], replicated
- losses: float32 [2], replicated
The draws below stay inside these ranges and needn't reach their ends.
Inputs may be any that keep to these rules, and one draw needn't show every extreme that they name: `counts`: some group has all 6 images counting and some group exactly one.
All inputs are finite; a program needn't handle non-finite values.
Results may differ from the reference program's by a relative error of at most 0.0093.
Values may be sent and summed in bfloat16 or wider, within the bound.
A program may use at most 192 MiB of HBM per device.

```python
import math
import jax
import jax.numpy as jnp
from jax import lax

C = 256
GROUPS = 32
SIDE = 16
MICRO = 3
IMG_MB = 2
LEVELS = 1000
STEP = 10
P_SIZE = 256
ROWS = 6656
IMAGES = 96
N_DP = 16


def base_noise(key, shape):
    return jax.random.normal(key, shape, jnp.float32)


def big_law(key, salt):
    own_key = jax.random.fold_in(key, salt)
    num_rows = 26 * C
    values = base_noise(own_key, (2, num_rows, C))
    row_ids = jnp.arange(num_rows)
    spread = jnp.where(row_ids < 18 * C, (9.0 * C) ** (-0.5), jnp.where(row_ids < 22 * C, (2.0 * C) ** (-0.5), jnp.where(row_ids < 25 * C, (1.0 * C) ** (-0.5), (1.0 * (C // SIDE)) ** (-0.5))))
    return values * spread[None, :, None]


def small_law(key, salt):
    own_key = jax.random.fold_in(key, salt)
    values = base_noise(own_key, (2, 13, C))
    row_ids = jnp.arange(13)
    gain_rows = (row_ids == 0) | (row_ids == 3) | (row_ids == 8)
    return jnp.where(gain_rows[None, :, None], 1.0 + 0.3 * values, 0.3 * values)


def draw_counts(key, part):
    per_group = MICRO * IMG_MB
    num_groups = IMAGES // per_group
    values = jax.random.randint(jax.random.fold_in(key, 11), (num_groups,), 1, per_group + 1)
    return values.at[0].set(per_group).at[num_groups - 1].set(1)


def draw_gen_w(key, part):
    return big_law(key, 101)


def draw_gen_ema(key, part):
    return big_law(key, 102)


def draw_fake_w(key, part):
    return big_law(key, 103)


def draw_teacher_w(key, part):
    return big_law(key, 104).astype(jnp.bfloat16)


def draw_gen_small(key, part):
    return small_law(key, 201)


def draw_gen_small_ema(key, part):
    return small_law(key, 202)


def draw_fake_small(key, part):
    return small_law(key, 203)


def draw_teacher_small(key, part):
    return small_law(key, 204)


def with_ends(array, key, least, largest):
    index_at = [jax.random.randint(jax.random.fold_in(key, axis), (), 0, length) for axis, length in enumerate(array.shape)]
    longest = array.shape.index(max(array.shape))
    beside = index_at[:longest] + [(index_at[longest] + 1) % array.shape[longest]] + index_at[longest + 1:]
    return array.at[tuple(index_at)].set(least).at[tuple(beside)].set(largest)


def block_scale(stream_key, shape, cuts, low, high):
    def one(position, parts):
        heights = jax.random.uniform(jax.random.fold_in(jax.random.fold_in(stream_key, 6), position), (parts,), jnp.float32, low / len(cuts), high / len(cuts))
        return jnp.repeat(jnp.exp(heights), shape[position] // parts).reshape((-1,) + (1,) * (len(shape) - position - 1))

    level = one(*cuts[0])
    for cut in cuts[1:]:
        level = level * one(*cut)
    return level


def gaussian(rng, shape, scale, bound, cuts=(), kind=jnp.bfloat16):
    values = jax.random.normal(rng, shape, jnp.float32) * scale
    if len(cuts) > 0:
        values = block_scale(rng, shape, cuts, -0.22, 0.18) * values
    return jnp.clip(values, min=-bound, max=bound).astype(kind)


def setup_inputs(seed: int = 0) -> dict:
    streams_of = jax.random.split(jax.random.key(seed), 21)
    return {
        "z_noise": gaussian(streams_of[0], (IMAGES, P_SIZE, C), 1.0, 6.0, ((0, 16),), jnp.float32),
        "eps_noise": gaussian(streams_of[1], (IMAGES, P_SIZE, C), 1.0, 6.0, ((0, 16),), jnp.float32),
        "levels": with_ends(jax.random.randint(streams_of[2], (IMAGES,), 0, LEVELS), jax.random.fold_in(streams_of[2], 1), 0, LEVELS - 1).astype(jnp.int32),
        "counts": draw_counts(jax.random.fold_in(streams_of[20], 71), 0),
        "gen_w": draw_gen_w(jax.random.fold_in(streams_of[20], 71), 0),
        "gen_m": gaussian(streams_of[5], (2, ROWS, C), (154 * 10 ** -7 * C ** -1), 9.5367431640625e-07, ((0, 2), (1, 16)), jnp.float32),
        "gen_v": jnp.clip(jnp.exp(math.log(2.34985341359122e-15) - 2.7751895 * jax.random.uniform(streams_of[6], (2, ROWS, C), jnp.float32) ** block_scale(streams_of[6], (2, ROWS, C), ((0, 2), (1, 16)), -0.2, 0.2)), 1.464843691207214e-16, 2.34985341359122e-15),
        "gen_ema": draw_gen_ema(jax.random.fold_in(streams_of[20], 71), 0),
        "gen_small": draw_gen_small(jax.random.fold_in(streams_of[20], 71), 0),
        "gen_small_m": gaussian(streams_of[9], (2, 13, C), (616 * 10 ** -7 * C ** -1), 3.814697265625e-06, ((0, 2),), jnp.float32),
        "gen_small_v": jnp.clip(jnp.exp(math.log(3.7536620811412166e-14) - 2.7709641 * jax.random.uniform(streams_of[10], (2, 13, C), jnp.float32) ** block_scale(streams_of[10], (2, 13, C), ((0, 2),), -0.2, 0.2)), 2.34985341359122e-15, 3.7536620811412166e-14),
        "gen_small_ema": draw_gen_small_ema(jax.random.fold_in(streams_of[20], 71), 0),
        "fake_w": draw_fake_w(jax.random.fold_in(streams_of[20], 71), 0),
        "fake_m": gaussian(streams_of[13], (2, ROWS, C), (154 * 10 ** -7 * C ** -1), 9.5367431640625e-07, ((0, 2), (1, 16)), jnp.float32),
        "fake_v": jnp.clip(jnp.exp(math.log(2.34985341359122e-15) - 2.7751895 * jax.random.uniform(streams_of[14], (2, ROWS, C), jnp.float32) ** block_scale(streams_of[14], (2, ROWS, C), ((0, 2), (1, 16)), -0.2, 0.2)), 1.464843691207214e-16, 2.34985341359122e-15),
        "fake_small": draw_fake_small(jax.random.fold_in(streams_of[20], 71), 0),
        "fake_small_m": gaussian(streams_of[16], (2, 13, C), (616 * 10 ** -7 * C ** -1), 3.814697265625e-06, ((0, 2),), jnp.float32),
        "fake_small_v": jnp.clip(jnp.exp(math.log(3.7536620811412166e-14) - 2.7709641 * jax.random.uniform(streams_of[17], (2, 13, C), jnp.float32) ** block_scale(streams_of[17], (2, 13, C), ((0, 2),), -0.2, 0.2)), 2.34985341359122e-15, 3.7536620811412166e-14),
        "teacher_w": draw_teacher_w(jax.random.fold_in(streams_of[20], 71), 0),
        "teacher_small": draw_teacher_small(jax.random.fold_in(streams_of[20], 71), 0),
    }


@jax.custom_vjp
def low(v):
    return lax.optimization_barrier(v.astype(jnp.bfloat16)).astype(jnp.float32)

@jax.custom_vjp
def low_back(v):
    return v

def low_keep(v):
    return (low(v), None)

def low_pass(kept, grad):
    return (grad,)

def back_keep(v):
    return (v, None)

def back_low(kept, grad):
    return (low(grad),)
low.defvjp(low_keep, low_pass)
low_back.defvjp(back_keep, back_low)
SIGMA_DATA = 0.5
SIGMA_INIT = 2.5
SIGMA_LOW = 0.05
SIGMA_HIGH = 20.0
RHO_POWER = 7.0
ALPHA_MIX = 1.2
RESIDUAL_SCALE = 0.7071067811865476
NORM_EPS = 1e-05
CLIP_NORM = 0.001
LEARN_RATE = 0.15
BETA_ONE = 0.9
BETA_TWO = 0.999
ADAM_EPS = 1e-08
WEIGHT_DECAY = 0.01
TOP_PRECISION = lax.Precision.HIGHEST

def sigma_levels(level_ids):
    fraction = level_ids.astype(jnp.float32) / (LEVELS - 1)
    top_root = SIGMA_HIGH ** (1.0 / RHO_POWER)
    bottom_root = SIGMA_LOW ** (1.0 / RHO_POWER)
    return (top_root + fraction * (bottom_root - top_root)) ** RHO_POWER

def precondition(sigma_vals):
    total = sigma_vals * sigma_vals + SIGMA_DATA ** 2
    return (lax.rsqrt(total), SIGMA_DATA ** 2 / total, sigma_vals * SIGMA_DATA * lax.rsqrt(total), total / (sigma_vals * sigma_vals * SIGMA_DATA ** 2))

def noise_embed(sigma_vals, channel_count):
    frequency = (1.0 / 10000.0) ** (jnp.arange(channel_count, dtype=jnp.float32) / channel_count)
    angles = (jnp.log(sigma_vals) / 4.0)[..., None] * frequency
    return jnp.concatenate([jnp.cos(angles), jnp.sin(angles)], axis=-1)

def group_norm(values, gain_vec, bias_vec):
    img_count, pos_count, channel_count = values.shape
    grouped = values.reshape(img_count, pos_count, GROUPS, channel_count // GROUPS)
    mean_val = lax.optimization_barrier(jnp.mean(grouped, axis=(1, 3), keepdims=True))
    centred = grouped - mean_val
    inv_std = lax.rsqrt(lax.optimization_barrier(jnp.mean(centred * centred, axis=(1, 3), keepdims=True)) + NORM_EPS)
    return (centred * inv_std).reshape(values.shape) * gain_vec + bias_vec

def conv_columns(acts):
    img_count, pos_count, channel_count = acts.shape
    grid_vals = acts.reshape(img_count, SIDE, SIDE, channel_count)
    padded = jnp.pad(grid_vals, ((0, 0), (1, 1), (1, 1), (0, 0)))
    pieces = [padded[:, row_off:row_off + SIDE, col_off:col_off + SIDE, :] for row_off in range(3) for col_off in range(3)]
    return jnp.concatenate(pieces, axis=-1).reshape(img_count, pos_count, 9 * channel_count)

def split_big(big_w):
    channel_count = big_w.shape[1]
    return (big_w[:9 * channel_count], big_w[9 * channel_count:18 * channel_count], big_w[18 * channel_count:22 * channel_count].reshape(2 * channel_count, 2 * channel_count), big_w[22 * channel_count:25 * channel_count].reshape(channel_count, 3 * channel_count), big_w[25 * channel_count:])

def layer_apply(big_w, small_w, inputs, embed):
    channel_count = inputs.shape[2]
    conv_one, conv_two, embed_w, qkv_w, proj_w = split_big(big_w)
    act_one = low(jax.nn.silu(group_norm(inputs, small_w[0], small_w[1])))
    hidden_one = low_back(jnp.einsum('bpk,kc->bpc', conv_columns(act_one), conv_one, precision=TOP_PRECISION) + small_w[2])
    modul = jnp.dot(low(embed), embed_w, precision=TOP_PRECISION) + jnp.concatenate([small_w[5], small_w[6]])
    pre_two = group_norm(hidden_one, small_w[3], small_w[4]) * (1.0 + modul[:, None, :channel_count]) + modul[:, None, channel_count:]
    act_two = low(jax.nn.silu(pre_two))
    hidden_two = low_back(jnp.einsum('bpk,kc->bpc', conv_columns(act_two), conv_two, precision=TOP_PRECISION) + small_w[7])
    middle = (inputs + hidden_two) * RESIDUAL_SCALE
    normed = low(group_norm(middle, small_w[8], small_w[9]))
    qkv_bias = jnp.concatenate([small_w[10], jnp.zeros_like(small_w[10]), small_w[11]])
    qkv_all = low(low_back(jnp.einsum('bpc,cd->bpd', normed, qkv_w, precision=TOP_PRECISION) + qkv_bias))
    query_rows = qkv_all[..., :channel_count]
    gathered_keys = qkv_all[..., channel_count:2 * channel_count]
    gathered_values = qkv_all[..., 2 * channel_count:]
    attention_scores = low_back(jnp.einsum('zhr,zmr->zhm', query_rows, gathered_keys, precision=TOP_PRECISION) * channel_count ** (-0.5))
    attention_probabilities = jax.nn.softmax(attention_scores, axis=-1)
    attention_output = low(low_back(jnp.einsum('ous,osg->oug', low(attention_probabilities), gathered_values, precision=TOP_PRECISION)))
    projected = low_back(jnp.einsum('bpc,cd->bpd', attention_output, proj_w, precision=TOP_PRECISION) + small_w[12])
    return (middle + projected) * RESIDUAL_SCALE

def network(big_w, small_w, raw_in, sigma_vals):
    c_in, c_skip, c_out, unused_lam = precondition(sigma_vals)
    embed = noise_embed(sigma_vals, raw_in.shape[2])
    hidden = c_in[:, None, None] * raw_in
    for depth in range(2):
        hidden = layer_apply(big_w[depth], small_w[depth], hidden, embed)
    return c_skip[:, None, None] * raw_in + c_out[:, None, None] * hidden

def adam_step(master, first_mom, second_mom, grad):
    first_new = BETA_ONE * first_mom + (1.0 - BETA_ONE) * grad
    second_new = BETA_TWO * second_mom + (1.0 - BETA_TWO) * grad * grad
    direction = first_new / (1.0 - BETA_ONE ** STEP) / (jnp.sqrt(second_new / (1.0 - BETA_TWO ** STEP)) + ADAM_EPS)
    return (master - LEARN_RATE * (direction + WEIGHT_DECAY * master), first_new, second_new)

def reference(z_noise, eps_noise, levels, counts, gen_w, gen_m, gen_v, gen_ema, gen_small, gen_small_m, gen_small_v, gen_small_ema, fake_w, fake_m, fake_v, fake_small, fake_small_m, fake_small_v, teacher_w, teacher_small):
    per_group = MICRO * IMG_MB
    elements = P_SIZE * C
    ema_rate = 0.5 ** (20.0 / STEP)
    teacher_big = teacher_w.astype(jnp.float32)
    fake_frozen = low(fake_w)

    def group_step(carry, group):
        z_grp, eps_grp, level_grp, count_grp = group
        valid_mask = (jnp.arange(per_group) < count_grp).astype(jnp.float32)
        sigma_vals = sigma_levels(level_grp)
        lam_vals = precondition(sigma_vals)[3]
        init_sigma = jnp.full((per_group,), SIGMA_INIT, jnp.float32)

        def gen_objective(gen_big, gen_part):
            samples = network(low(gen_big), gen_part, SIGMA_INIT * z_grp, init_sigma)
            noisy_in = samples + sigma_vals[:, None, None] * eps_grp
            teacher_den = network(teacher_big, teacher_small, noisy_in, sigma_vals)
            fake_den = network(fake_frozen, fake_small, noisy_in, sigma_vals)
            gap_den = teacher_den - fake_den
            miss_den = fake_den - samples
            per_image = (1.0 - ALPHA_MIX) * lax.optimization_barrier(jnp.sum(gap_den * gap_den, axis=(1, 2))) + lax.optimization_barrier(jnp.sum(gap_den * miss_den, axis=(1, 2)))
            return (jnp.sum(valid_mask * lam_vals * per_image) / elements, samples)
        gen_loss, gen_back, samples = jax.vjp(gen_objective, gen_w, gen_small, has_aux=True)
        gen_big_g, gen_small_g = gen_back(jnp.ones_like(gen_loss))
        noisy_in = samples + sigma_vals[:, None, None] * eps_grp

        def fake_objective(fake_big, fake_part):
            fake_den = network(low(fake_big), fake_part, noisy_in, sigma_vals)
            miss_den = fake_den - samples
            return jnp.sum(valid_mask * lam_vals * lax.optimization_barrier(jnp.sum(miss_den * miss_den, axis=(1, 2)))) / elements
        fake_loss, fake_back = jax.vjp(fake_objective, fake_w, fake_small)
        fake_big_g, fake_small_g = fake_back(jnp.ones_like(fake_loss))
        updates = (gen_big_g, gen_small_g, fake_big_g, fake_small_g, gen_loss, fake_loss)
        return (tuple((running + addend for running, addend in zip(carry, updates))), None)
    initial = (jnp.zeros_like(gen_w), jnp.zeros_like(gen_small), jnp.zeros_like(fake_w), jnp.zeros_like(fake_small), jnp.zeros((), jnp.float32), jnp.zeros((), jnp.float32))
    groups_in = (z_noise.reshape(N_DP, per_group, P_SIZE, C), eps_noise.reshape(N_DP, per_group, P_SIZE, C), levels.reshape(N_DP, per_group), counts)
    totals, unused_out = lax.scan(group_step, initial, groups_in)
    gen_big_g, gen_small_g, fake_big_g, fake_small_g, gen_total, fake_total = totals
    count_total = jnp.sum(counts).astype(jnp.float32)
    gen_big_g = gen_big_g / count_total
    gen_small_g = gen_small_g / count_total
    fake_big_g = fake_big_g / count_total
    fake_small_g = fake_small_g / count_total
    norm_gen = jnp.sqrt(jnp.sum(gen_big_g * gen_big_g) + jnp.sum(gen_small_g * gen_small_g))
    norm_fake = jnp.sqrt(jnp.sum(fake_big_g * fake_big_g) + jnp.sum(fake_small_g * fake_small_g))
    clip_gen = jnp.minimum(1.0, CLIP_NORM / norm_gen)
    clip_fake = jnp.minimum(1.0, CLIP_NORM / norm_fake)
    gen_w_out, gen_m_out, gen_v_out = adam_step(gen_w, gen_m, gen_v, gen_big_g * clip_gen)
    gen_small_out, gen_small_m_out, gen_small_v_out = adam_step(gen_small, gen_small_m, gen_small_v, gen_small_g * clip_gen)
    fake_w_out, fake_m_out, fake_v_out = adam_step(fake_w, fake_m, fake_v, fake_big_g * clip_fake)
    fake_small_out, fake_small_m_out, fake_small_v_out = adam_step(fake_small, fake_small_m, fake_small_v, fake_small_g * clip_fake)
    gen_ema_out = ema_rate * gen_ema + (1.0 - ema_rate) * gen_w_out
    gen_small_ema_out = ema_rate * gen_small_ema + (1.0 - ema_rate) * gen_small_out
    norms = jnp.stack([norm_gen, norm_fake])
    losses = jnp.stack([gen_total, fake_total]) / count_total
    return (gen_w_out, gen_m_out, gen_v_out, gen_ema_out, gen_small_out, gen_small_m_out, gen_small_v_out, gen_small_ema_out, fake_w_out, fake_m_out, fake_v_out, fake_small_out, fake_small_m_out, fake_small_v_out, norms, losses)
```

```python
import functools

import jax
import jax.numpy as jnp
from jax import lax
from jax.experimental import pallas as pl
from jax.experimental.pallas import tpu as pltpu
from jax.sharding import PartitionSpec as P

GROUPS = 32
SIDE = 16
LEVELS = 1000
STEP = 10

SIGMA_DATA = 0.5
SIGMA_INIT = 2.5
SIGMA_LOW = 0.05
SIGMA_HIGH = 20.0
RHO_POWER = 7.0
ALPHA_MIX = 1.2
RS = 0.7071067811865476
NORM_EPS = 1e-05
CLIP_NORM = 0.001
LEARN_RATE = 0.15
BETA_ONE = 0.9
BETA_TWO = 0.999
ADAM_EPS = 1e-08
WEIGHT_DECAY = 0.01

C = 256
HALF = 128
POS = 256
ROWS = 26 * C
CHUNK = 64
PAD = SIDE
F32 = jnp.float32
BF16 = jnp.bfloat16
VMEM_LIMIT = 58 * 2**20

R_CONV1, R_CONV2, R_EMB, R_QKV, R_PROJ = 0, 9 * C, 18 * C, 22 * C, 25 * C
S_M1, S_I1, S_M2, S_I2, S_M3, S_I3, S_MA, S_MB = range(8)


def sigma_levels(level_ids):
    fraction = level_ids.astype(F32) / (LEVELS - 1)
    top_root = SIGMA_HIGH ** (1.0 / RHO_POWER)
    bottom_root = SIGMA_LOW ** (1.0 / RHO_POWER)
    return (top_root + fraction * (bottom_root - top_root)) ** RHO_POWER


def precondition(sigma_vals):
    total = sigma_vals * sigma_vals + SIGMA_DATA**2
    return (
        lax.rsqrt(total),
        SIGMA_DATA**2 / total,
        sigma_vals * SIGMA_DATA * lax.rsqrt(total),
        total / (sigma_vals * sigma_vals * SIGMA_DATA**2),
    )


def noise_embed(sigma_vals, channel_count):
    frequency = (1.0 / 10000.0) ** (jnp.arange(channel_count, dtype=F32) / channel_count)
    angles = (jnp.log(sigma_vals) / 4.0)[..., None] * frequency
    return jnp.concatenate([jnp.cos(angles), jnp.sin(angles)], axis=-1)


def spread_embed(sigma_vals):
    emb = noise_embed(sigma_vals, C).astype(BF16)
    images = emb.shape[0]
    zero = jnp.zeros_like(emb)
    low = jnp.stack([emb, zero], axis=-1).reshape(images, 4 * C)
    high = jnp.stack([zero, emb], axis=-1).reshape(images, 4 * C)
    fill = jnp.zeros((4 - images, 4 * C), BF16)
    return jnp.concatenate([low, fill, high, fill], axis=0)


def dot_nn(a, b):
    return lax.dot_general(a, b, (((1,), (0,)), ((), ())), preferred_element_type=F32)


def dot_nt(a, b):
    return lax.dot_general(a, b, (((1,), (1,)), ((), ())), preferred_element_type=F32)


def dot_tn(a, b):
    return lax.dot_general(a, b, (((0,), (0,)), ((), ())), preferred_element_type=F32)


def group_mean(row):
    v = jnp.broadcast_to(row, (8, C))
    lane = lax.broadcasted_iota(jnp.int32, (8, C), 1)
    for sh in (1, 2, 4):
        v = v + jnp.where((lane & sh) != 0, pltpu.roll(v, sh, 1), pltpu.roll(v, C - sh, 1))
    return v[0:1] * (1.0 / (POS * 8))


def colsum(v):
    return jnp.sum(v, axis=0, keepdims=True)


def norm_stats(ref, *at):
    x = ref[at]
    mean = group_mean(colsum(x))
    d = x - mean
    inv = lax.rsqrt(group_mean(colsum(d * d)) + NORM_EPS)
    return mean, inv


def put_shifted(bufs, i, r, v):
    rows = v.shape[0]
    col = lax.broadcasted_iota(jnp.int32, (rows, C), 0) & (SIDE - 1)
    at = pl.ds(PAD + r, rows)
    bufs[0, i, at, :] = jnp.where(col == 0, 0.0, pltpu.roll(v, 1, 0)).astype(BF16)
    bufs[1, i, at, :] = v.astype(BF16)
    bufs[2, i, at, :] = jnp.where(col == SIDE - 1, 0.0, pltpu.roll(v, rows - 1, 0)).astype(BF16)


def taps(bufs, flip):
    images = bufs.shape[1]
    out = []
    for dr in (-1, 0, 1):
        for dc in (-1, 0, 1):
            sr, sc = (-dr, -dc) if flip else (dr, dc)
            piece = bufs[sc + 1, :, PAD + SIDE * sr : PAD + SIDE * sr + POS, :]
            out.append(piece.reshape(images * POS, C))
    return out


def conv_forward(bufs, w, l, row):
    return dot_nn(jnp.concatenate(taps(bufs, False), axis=1), w[l, row : row + 9 * C, :])


def conv_input_grad(bufs, w, l, row):
    parts = [w[l, row + t * C : row + (t + 1) * C, :] for t in range(9)]
    return dot_nt(jnp.concatenate(taps(bufs, True), axis=1), jnp.concatenate(parts, axis=1))


def conv_weight_grad(act_t, bufs, grad, l, row):
    left = act_t[...]
    for t, piece in enumerate(taps(bufs, True)):
        grad[l, row + t * C : row + (t + 1) * C, :] = dot_nn(left, piece)


def silu(v):
    h = 0.5 * v
    return h + h * jnp.tanh(h)


def silu_parts(v):
    s = 0.5 + 0.5 * jnp.tanh(0.5 * v)
    return s, s * (1.0 + v * (1.0 - s))


def clear_pads(bufs):
    zero = jnp.zeros(bufs.shape[:2] + (PAD, C), BF16)
    bufs[:, :, 0:PAD, :] = zero
    bufs[:, :, PAD + POS :, :] = zero


def split_qkv(w, l, qkvw, tmp):
    for h in range(2):
        tmp[h] = w[l, R_QKV : R_QKV + 3 * C, h * HALF : (h + 1) * HALF].astype(F32)
    for j in range(3):
        for h in range(2):
            at = j * C + h * HALF
            qkvw[:, at : at + HALF] = tmp[h, pl.ds(j, C, stride=3), :].astype(BF16)


def layer_forward(l, w, small, eo, xs, h1, y, qkv, att, o, st, bufs, nbuf, qkvw, tmp):
    images = h1.shape[1]
    flat = images * POS
    split_qkv(w, l, qkvw, tmp)
    mod = dot_nn(eo[...], w[l, R_EMB : R_EMB + 4 * C, :])
    ma = mod[0:4] + small[l, 5:6, :]
    mb = mod[4:8] + small[l, 6:7, :]
    for i in range(images):
        st[l, i, S_MA : S_MA + 1, :] = ma[i : i + 1]
        st[l, i, S_MB : S_MB + 1, :] = mb[i : i + 1]

    def first(i, _):
        mean, inv = norm_stats(xs, l, i)
        st[l, i, S_M1 : S_M1 + 1, :] = mean
        st[l, i, S_I1 : S_I1 + 1, :] = inv
        a = inv * small[l, 0:1, :]
        b = small[l, 1:2, :]
        for r in range(0, POS, CHUNK):
            put_shifted(bufs, i, r, silu((xs[l, i, r : r + CHUNK, :] - mean) * a + b))
        return 0

    lax.fori_loop(0, images, first, 0)
    h1[l] = (conv_forward(bufs, w, l, R_CONV1) + small[l, 2:3, :]).reshape(images, POS, C)

    def second(i, _):
        mean, inv = norm_stats(h1, l, i)
        st[l, i, S_M2 : S_M2 + 1, :] = mean
        st[l, i, S_I2 : S_I2 + 1, :] = inv
        gain = 1.0 + st[l, i, S_MA : S_MA + 1, :]
        a = inv * small[l, 3:4, :] * gain
        b = small[l, 4:5, :] * gain + st[l, i, S_MB : S_MB + 1, :]
        for r in range(0, POS, CHUNK):
            put_shifted(bufs, i, r, silu((h1[l, i, r : r + CHUNK, :] - mean) * a + b))
        return 0

    lax.fori_loop(0, images, second, 0)
    h2 = conv_forward(bufs, w, l, R_CONV2) + small[l, 7:8, :]
    y[l] = (xs[l] + h2.reshape(images, POS, C)) * RS

    def third(i, _):
        mean, inv = norm_stats(y, l, i)
        st[l, i, S_M3 : S_M3 + 1, :] = mean
        st[l, i, S_I3 : S_I3 + 1, :] = inv
        a = inv * small[l, 8:9, :]
        b = small[l, 9:10, :]
        for r in range(0, POS, CHUNK):
            nbuf[i, r : r + CHUNK, :] = ((y[l, i, r : r + CHUNK, :] - mean) * a + b).astype(BF16)
        return 0

    lax.fori_loop(0, images, third, 0)
    n = nbuf[...].reshape(flat, C)
    for j, row in ((0, 10), (1, None), (2, 11)):
        part = dot_nn(n, qkvw[:, j * C : (j + 1) * C])
        if row is not None:
            part = part + small[l, row : row + 1, :]
        qkv[l, :, :, j * C : (j + 1) * C] = part.astype(BF16).reshape(images, POS, C)

    def attend(i, _):
        s = dot_nt(qkv[l, i, :, 0:C], qkv[l, i, :, C : 2 * C])
        e = jnp.exp((s - jnp.max(s, axis=1, keepdims=True)) * (C**-0.5))
        p = (e * (1.0 / jnp.sum(e, axis=1, keepdims=True))).astype(BF16)
        att[l, i] = p
        o[l, i] = dot_nn(p, qkv[l, i, :, 2 * C :]).astype(BF16)
        return 0

    lax.fori_loop(0, images, attend, 0)
    out = dot_nn(o[l].reshape(flat, C), w[l, R_PROJ:, :]) + small[l, 12:13, :]
    xs[l + 1] = (y[l] + out.reshape(images, POS, C)) * RS


def layer_backward(
    l, w, small, eot, xs, h1, y, qkv, att, o, st, g, bufs, nbuf, qkvw, tmp, dn, dqkv, act_t,
    grad, sgrad,
):
    want = grad is not None
    images = h1.shape[1]
    flat = images * POS
    scale = C**-0.5
    zrow = jnp.zeros((1, C), F32)
    split_qkv(w, l, qkvw, tmp)
    gp = (g[...] * RS).astype(BF16).reshape(flat, C)
    nbuf[...] = dot_nt(gp, w[l, R_PROJ:, :]).astype(BF16).reshape(images, POS, C)
    if want:
        grad[l, R_PROJ:, :] = dot_tn(o[l].reshape(flat, C), gp)
        sgrad[l, 12:13, :] = colsum(gp.astype(F32))

    def attend(i, _):
        p = att[l, i]
        pf = p.astype(F32)
        do = nbuf[i]
        dp = dot_nt(do, qkv[l, i, :, 2 * C :])
        ds = (pf * (dp - jnp.sum(dp * pf, axis=1, keepdims=True))).astype(BF16)
        dqkv[i, :, 0:C] = (dot_nn(ds, qkv[l, i, :, C : 2 * C]) * scale).astype(BF16)
        dqkv[i, :, C : 2 * C] = (dot_tn(ds, qkv[l, i, :, 0:C]) * scale).astype(BF16)
        dqkv[i, :, 2 * C :] = dot_tn(p, do).astype(BF16)
        return 0

    lax.fori_loop(0, images, attend, 0)
    dq = dqkv[...].reshape(flat, 3 * C)
    dn[...] = dot_nt(dq, qkvw[...]).reshape(images, POS, C)

    def third(i, carry):
        db7, dg8, db9 = carry
        mean, inv = st[l, i, S_M3 : S_M3 + 1, :], st[l, i, S_I3 : S_I3 + 1, :]
        gain = small[l, 8:9, :]
        nh = (y[l, i] - mean) * inv
        c1 = colsum(dn[i])
        c2 = colsum(dn[i] * nh)
        mg = group_mean(gain * c1)
        mc = group_mean(gain * c2)
        for r in range(0, POS, CHUNK):
            nhr = (y[l, i, r : r + CHUNK, :] - mean) * inv
            gm = g[i, r : r + CHUNK, :] * RS + inv * (
                gain * dn[i, r : r + CHUNK, :] - mg - nhr * mc
            )
            gm = gm * RS
            g[i, r : r + CHUNK, :] = gm
            put_shifted(bufs, i, r, gm)
            if want:
                nbuf[i, r : r + CHUNK, :] = (nhr * gain + small[l, 9:10, :]).astype(BF16)
                db7 = db7 + colsum(gm.astype(BF16).astype(F32))
        return db7, dg8 + c2, db9 + c1

    db7, dg8, db9 = lax.fori_loop(0, images, third, (zrow, zrow, zrow))
    if want:
        sgrad[l, 7:8, :] = db7
        sgrad[l, 8:9, :] = dg8
        sgrad[l, 9:10, :] = db9
        act_t[...] = nbuf[...].reshape(flat, C).T
        for j in range(3):
            dj = dqkv[:, :, j * C : (j + 1) * C].reshape(flat, C)
            wide = dot_nn(act_t[...], dj)
            for h in range(2):
                tmp[h, pl.ds(j, C, stride=3), :] = wide[:, h * HALF : (h + 1) * HALF]
            if j != 1:
                sgrad[l, 10 + j // 2 : 11 + j // 2, :] = colsum(dj.astype(F32))
        for h in range(2):
            grad[l, R_QKV : R_QKV + 3 * C, h * HALF : (h + 1) * HALF] = tmp[h]
    dn[...] = conv_input_grad(bufs, w, l, R_CONV2).reshape(images, POS, C)

    def second_a(i, _):
        mean, inv = st[l, i, S_M2 : S_M2 + 1, :], st[l, i, S_I2 : S_I2 + 1, :]
        gain = 1.0 + st[l, i, S_MA : S_MA + 1, :]
        a = inv * small[l, 3:4, :] * gain
        b = small[l, 4:5, :] * gain + st[l, i, S_MB : S_MB + 1, :]
        for r in range(0, POS, CHUNK):
            pre = (h1[l, i, r : r + CHUNK, :] - mean) * a + b
            s, slope = silu_parts(pre)
            dn[i, r : r + CHUNK, :] = dn[i, r : r + CHUNK, :] * slope
            if want:
                nbuf[i, r : r + CHUNK, :] = (pre * s).astype(BF16)
        return 0

    lax.fori_loop(0, images, second_a, 0)
    if want:
        act_t[...] = nbuf[...].reshape(flat, C).T
        conv_weight_grad(act_t, bufs, grad, l, R_CONV2)
    row8 = lax.broadcasted_iota(jnp.int32, (8, C), 0)

    def second_b(i, carry):
        db2, dg3, db4, dm = carry
        mean, inv = st[l, i, S_M2 : S_M2 + 1, :], st[l, i, S_I2 : S_I2 + 1, :]
        modgain = 1.0 + st[l, i, S_MA : S_MA + 1, :]
        gain = small[l, 3:4, :]
        nh = (h1[l, i] - mean) * inv
        p1 = colsum(dn[i])
        p2 = colsum(dn[i] * nh)
        full = gain * modgain
        mg = group_mean(full * p1)
        mc = group_mean(full * p2)
        for r in range(0, POS, CHUNK):
            nhr = (h1[l, i, r : r + CHUNK, :] - mean) * inv
            dh = inv * (full * dn[i, r : r + CHUNK, :] - mg - nhr * mc)
            put_shifted(bufs, i, r, dh)
            if want:
                db2 = db2 + colsum(dh.astype(BF16).astype(F32))
        dma = gain * p2 + small[l, 4:5, :] * p1
        dm = jnp.where(row8 == i, dma, jnp.where(row8 == i + 4, p1, dm))
        return db2, dg3 + modgain * p2, db4 + modgain * p1, dm

    db2, dg3, db4, dm = lax.fori_loop(
        0, images, second_b, (zrow, zrow, zrow, jnp.zeros((8, C), F32))
    )
    if want:
        sgrad[l, 2:3, :] = db2
        sgrad[l, 3:4, :] = dg3
        sgrad[l, 4:5, :] = db4
        sgrad[l, 5:6, :] = colsum(dm[0:4])
        sgrad[l, 6:7, :] = colsum(dm[4:8])
        grad[l, R_EMB : R_EMB + 4 * C, :] = lax.dot_general(
            eot[...], dm, (((1,), (0,)), ((), ())),
            precision=lax.Precision.HIGHEST, preferred_element_type=F32,
        )
    dn[...] = conv_input_grad(bufs, w, l, R_CONV1).reshape(images, POS, C)

    def first(i, carry):
        dg0, db1 = carry
        mean, inv = st[l, i, S_M1 : S_M1 + 1, :], st[l, i, S_I1 : S_I1 + 1, :]
        gain = small[l, 0:1, :]
        b = small[l, 1:2, :]
        c1, c2 = zrow, zrow
        for r in range(0, POS, CHUNK):
            nhr = (xs[l, i, r : r + CHUNK, :] - mean) * inv
            pre = nhr * gain + b
            s, slope = silu_parts(pre)
            d = dn[i, r : r + CHUNK, :] * slope
            dn[i, r : r + CHUNK, :] = d
            c1 = c1 + colsum(d)
            c2 = c2 + colsum(d * nhr)
            if want:
                nbuf[i, r : r + CHUNK, :] = (pre * s).astype(BF16)
        mg = group_mean(gain * c1)
        mc = group_mean(gain * c2)
        for r in range(0, POS, CHUNK):
            nhr = (xs[l, i, r : r + CHUNK, :] - mean) * inv
            dx = inv * (gain * dn[i, r : r + CHUNK, :] - mg - nhr * mc)
            g[i, r : r + CHUNK, :] = g[i, r : r + CHUNK, :] + dx
        return dg0 + c2, db1 + c1

    dg0, db1 = lax.fori_loop(0, images, first, (zrow, zrow))
    if want:
        sgrad[l, 0:1, :] = dg0
        sgrad[l, 1:2, :] = db1
        act_t[...] = nbuf[...].reshape(flat, C).T
        conv_weight_grad(act_t, bufs, grad, l, R_CONV1)


def saved_shapes(images):
    return [
        jax.ShapeDtypeStruct((3, images, POS, C), F32),
        jax.ShapeDtypeStruct((2, images, POS, C), F32),
        jax.ShapeDtypeStruct((2, images, POS, C), F32),
        jax.ShapeDtypeStruct((2, images, POS, 3 * C), BF16),
        jax.ShapeDtypeStruct((2, images, POS, POS), BF16),
        jax.ShapeDtypeStruct((2, images, POS, C), BF16),
        jax.ShapeDtypeStruct((2, images, 8, C), F32),
    ]


def forward_kernel(x0, w, small, eo, xs, h1, y, qkv, att, o, st, bufs, nbuf, qkvw, tmp):
    clear_pads(bufs)
    xs[0] = x0[...]

    def body(l, _):
        layer_forward(l, w, small, eo, xs, h1, y, qkv, att, o, st, bufs, nbuf, qkvw, tmp)
        return 0

    lax.fori_loop(0, 2, body, 0)


def backward_kernel(want, *refs):
    cot, w, small, eot, xs, h1, y, qkv, att, o, st, g = refs[:12]
    refs = refs[12:]
    if want:
        grad, sgrad = refs[:2]
        refs = refs[2:]
    else:
        grad, sgrad = None, None
    bufs, nbuf, qkvw, tmp, dn, dqkv, act_t = refs
    clear_pads(bufs)
    g[...] = cot[...]
    if want:
        sgrad[...] = jnp.zeros(sgrad.shape, F32)

    def body(k, _):
        layer_backward(
            1 - k, w, small, eot, xs, h1, y, qkv, att, o, st, g, bufs, nbuf, qkvw, tmp, dn,
            dqkv, act_t, grad, sgrad,
        )
        return 0

    lax.fori_loop(0, 2, body, 0)


def vm(n):
    return [pl.BlockSpec(memory_space=pltpu.VMEM)] * n


def scratch_forward(images):
    return [
        pltpu.VMEM((3, images, POS + 2 * PAD, C), BF16),
        pltpu.VMEM((images, POS, C), BF16),
        pltpu.VMEM((C, 3 * C), BF16),
        pltpu.VMEM((2, 3 * C, HALF), F32),
    ]


def run_forward(x0, w, small, eo):
    images = x0.shape[0]
    return pl.pallas_call(
        forward_kernel,
        out_shape=saved_shapes(images),
        in_specs=vm(4),
        out_specs=vm(7),
        scratch_shapes=scratch_forward(images),
        compiler_params=pltpu.CompilerParams(vmem_limit_bytes=VMEM_LIMIT),
    )(x0, w, small, eo)


def run_backward(cot, w, small, eot, saved, want):
    images = cot.shape[0]
    outs = [jax.ShapeDtypeStruct(cot.shape, F32)]
    if want:
        outs += [
            jax.ShapeDtypeStruct((2, ROWS, C), F32),
            jax.ShapeDtypeStruct((2, 16, C), F32),
        ]
    return pl.pallas_call(
        functools.partial(backward_kernel, want),
        out_shape=outs,
        in_specs=vm(11),
        out_specs=vm(len(outs)),
        scratch_shapes=scratch_forward(images)
        + [
            pltpu.VMEM((images, POS, C), F32),
            pltpu.VMEM((images, POS, 3 * C), BF16),
            pltpu.VMEM((C, images * POS), BF16),
        ],
        compiler_params=pltpu.CompilerParams(vmem_limit_bytes=VMEM_LIMIT),
    )(cot, w, small, eot, *saved)


def adam_step(master, first_mom, second_mom, grad):
    first_new = BETA_ONE * first_mom + (1.0 - BETA_ONE) * grad
    second_new = BETA_TWO * second_mom + (1.0 - BETA_TWO) * grad * grad
    direction = (
        first_new
        / (1.0 - BETA_ONE**STEP)
        / (jnp.sqrt(second_new / (1.0 - BETA_TWO**STEP)) + ADAM_EPS)
    )
    return (master - LEARN_RATE * (direction + WEIGHT_DECAY * master), first_new, second_new)


def gather_net(shard, small):
    rows = lax.all_gather(shard.astype(BF16), "dp", axis=1, tiled=True)
    return (
        lax.all_gather(rows, "section", axis=0, tiled=True),
        lax.all_gather(small, "section", axis=0, tiled=True),
    )


def shards(
    z_noise, eps_noise, levels, counts,
    gen_w, gen_m, gen_v, gen_ema, gen_small, gen_small_m, gen_small_v, gen_small_ema,
    fake_w, fake_m, fake_v, fake_small, fake_small_m, fake_small_v,
    teacher_w, teacher_small,
):
    section_idx = lax.axis_index("section")
    sections = lax.axis_size("section")
    per_group = z_noise.shape[0]
    images = per_group // sections
    start = section_idx * images
    elements = POS * C
    ema_rate = 0.5 ** (20.0 / STEP)

    def mine(a):
        return lax.dynamic_slice_in_dim(a, start, images, 0)

    def wide(a):
        return a[:, None, None]

    z = mine(z_noise)
    eps = mine(eps_noise)
    local_count = counts[0]
    valid = ((start + jnp.arange(images)) < local_count).astype(F32)
    sigma = sigma_levels(mine(levels))
    s_in, s_skip, s_out, s_lam = [wide(t) for t in precondition(sigma)]
    init = jnp.full((images,), SIGMA_INIT, F32)
    g_in, g_skip, g_out, _ = [wide(t) for t in precondition(init)]
    gen_eo, score_eo = spread_embed(init), spread_embed(sigma)
    gen_eot, score_eot = gen_eo.astype(F32).T, score_eo.astype(F32).T

    gw, gs = gather_net(gen_w, gen_small)
    fw, fs = gather_net(fake_w, fake_small)
    tw, ts = gather_net(teacher_w, teacher_small)

    raw = SIGMA_INIT * z
    gen_saved = run_forward(g_in * raw, gw, gs, gen_eo)
    samples = g_skip * raw + g_out * gen_saved[0][2]
    noisy = samples + wide(sigma) * eps
    x0 = s_in * noisy
    fake_saved = run_forward(x0, fw, fs, score_eo)
    fake_den = s_skip * noisy + s_out * fake_saved[0][2]
    factor = wide(valid) * s_lam / elements
    miss = fake_den - samples
    _, fake_g, fake_sg = run_backward(s_out * 2.0 * factor * miss, fw, fs, score_eot, fake_saved, True)
    teacher_saved = run_forward(x0, tw, ts, score_eo)
    teacher_den = s_skip * noisy + s_out * teacher_saved[0][2]
    gap = teacher_den - fake_den
    loss_gen = jnp.sum(factor * ((1.0 - ALPHA_MIX) * gap * gap + gap * miss))
    loss_fake = jnp.sum(factor * miss * miss)
    grad_teacher = factor * (2.0 * (1.0 - ALPHA_MIX) * gap + miss)
    grad_fake = factor * (gap - 2.0 * (1.0 - ALPHA_MIX) * gap - miss)
    direct = s_skip * (grad_teacher + grad_fake) - factor * gap
    (back_t,) = run_backward(s_out * grad_teacher, tw, ts, score_eot, teacher_saved, False)
    (back_f,) = run_backward(s_out * grad_fake, fw, fs, score_eot, fake_saved, False)
    gen_cot = g_out * (direct + s_in * (back_t + back_f))
    _, gen_g, gen_sg = run_backward(gen_cot, gw, gs, gen_eot, gen_saved, True)

    def reduce_net(big, small):
        own = lax.psum_scatter(big, "section", scatter_dimension=0, tiled=True)
        own = lax.psum_scatter(own, "dp", scatter_dimension=1, tiled=True)
        small = lax.psum_scatter(small, "section", scatter_dimension=0, tiled=True)
        return own[0], lax.psum(small, "dp")[0, :13]

    fake_shard, fake_small_sum = reduce_net(fake_g, fake_sg)
    gen_shard, gen_small_sum = reduce_net(gen_g, gen_sg)
    first_dp = (lax.axis_index("dp") == 0).astype(F32)
    square_gen = jnp.sum(gen_shard * gen_shard) + first_dp * jnp.sum(gen_small_sum * gen_small_sum)
    square_fake = jnp.sum(fake_shard * fake_shard) + first_dp * jnp.sum(
        fake_small_sum * fake_small_sum
    )
    on_first = (section_idx == 0).astype(F32)
    sums = jnp.stack(
        [square_gen, square_fake, loss_gen, loss_fake, on_first * local_count.astype(F32)]
    )
    square_gen, square_fake, gen_total, fake_total, count_total = lax.psum(sums, ("section", "dp"))
    norm_gen = jnp.sqrt(square_gen) / count_total
    norm_fake = jnp.sqrt(square_fake) / count_total
    scale_gen = jnp.minimum(1.0, CLIP_NORM / norm_gen) / count_total
    scale_fake = jnp.minimum(1.0, CLIP_NORM / norm_fake) / count_total
    gw_o, gm_o, gv_o = adam_step(gen_w[0], gen_m[0], gen_v[0], gen_shard * scale_gen)
    gs_o, gsm_o, gsv_o = adam_step(
        gen_small[0], gen_small_m[0], gen_small_v[0], gen_small_sum * scale_gen
    )
    fw_o, fm_o, fv_o = adam_step(fake_w[0], fake_m[0], fake_v[0], fake_shard * scale_fake)
    fs_o, fsm_o, fsv_o = adam_step(
        fake_small[0], fake_small_m[0], fake_small_v[0], fake_small_sum * scale_fake
    )
    ge_o = ema_rate * gen_ema[0] + (1.0 - ema_rate) * gw_o
    gse_o = ema_rate * gen_small_ema[0] + (1.0 - ema_rate) * gs_o
    norms = jnp.stack([norm_gen, norm_fake])
    losses = jnp.stack([gen_total, fake_total]) / count_total
    outs = (gw_o, gm_o, gv_o, ge_o, gs_o, gsm_o, gsv_o, gse_o, fw_o, fm_o, fv_o, fs_o, fsm_o, fsv_o)
    return tuple(a[None] for a in outs) + (norms, losses)


def solution(mesh):
    images = P("dp", None, None)
    big = P("section", "dp", None)
    small = P("section", None, None)
    return jax.shard_map(
        shards,
        mesh=mesh,
        in_specs=(images, images, P("dp"), P("dp"))
        + (big,) * 4 + (small,) * 4 + (big,) * 3 + (small,) * 3 + (big, small),
        out_specs=(big,) * 4 + (small,) * 4 + (big,) * 3 + (small,) * 3 + (P(), P()),
        check_vma=False,
    )
```

```python
import functools

import jax
import jax.numpy as jnp
from jax import lax
from jax.experimental import pallas as pl
from jax.experimental.pallas import tpu as pltpu
from jax.sharding import PartitionSpec as P

GROUPS = 32
SIDE = 16
LEVELS = 1000
STEP = 10

SIGMA_DATA = 0.5
SIGMA_INIT = 2.5
SIGMA_LOW = 0.05
SIGMA_HIGH = 20.0
RHO_POWER = 7.0
ALPHA_MIX = 1.2
RS = 0.7071067811865476
NORM_EPS = 1e-05
CLIP_NORM = 0.001
LEARN_RATE = 0.15
BETA_ONE = 0.9
BETA_TWO = 0.999
ADAM_EPS = 1e-08
WEIGHT_DECAY = 0.01

C = 256
HALF = 128
POS = 256
ROWS = 26 * C
CHUNK = 64
PAD = SIDE
F32 = jnp.float32
BF16 = jnp.bfloat16
VMEM_LIMIT = 58 * 2**20

R_CONV1, R_CONV2, R_EMB, R_QKV, R_PROJ = 0, 9 * C, 18 * C, 22 * C, 25 * C
S_M1, S_I1, S_M2, S_I2, S_M3, S_I3, S_MA, S_MB = range(8)


def sigma_levels(level_ids):
    fraction = level_ids.astype(F32) / (LEVELS - 1)
    top_root = SIGMA_HIGH ** (1.0 / RHO_POWER)
    bottom_root = SIGMA_LOW ** (1.0 / RHO_POWER)
    return (top_root + fraction * (bottom_root - top_root)) ** RHO_POWER


def precondition(sigma_vals):
    total = sigma_vals * sigma_vals + SIGMA_DATA**2
    return (
        lax.rsqrt(total),
        SIGMA_DATA**2 / total,
        sigma_vals * SIGMA_DATA * lax.rsqrt(total),
        total / (sigma_vals * sigma_vals * SIGMA_DATA**2),
    )


def noise_embed(sigma_vals, channel_count):
    frequency = (1.0 / 10000.0) ** (jnp.arange(channel_count, dtype=F32) / channel_count)
    angles = (jnp.log(sigma_vals) / 4.0)[..., None] * frequency
    return jnp.concatenate([jnp.cos(angles), jnp.sin(angles)], axis=-1)


def spread_embed(sigma_vals):
    emb = noise_embed(sigma_vals, C).astype(BF16)
    images = emb.shape[0]
    zero = jnp.zeros_like(emb)
    low = jnp.stack([emb, zero], axis=-1).reshape(images, 4 * C)
    high = jnp.stack([zero, emb], axis=-1).reshape(images, 4 * C)
    fill = jnp.zeros((4 - images, 4 * C), BF16)
    return jnp.concatenate([low, fill, high, fill], axis=0)


def dot_nn(a, b):
    return lax.dot_general(a, b, (((1,), (0,)), ((), ())), preferred_element_type=F32)


def dot_nt(a, b):
    return lax.dot_general(a, b, (((1,), (1,)), ((), ())), preferred_element_type=F32)


def dot_tn(a, b):
    return lax.dot_general(a, b, (((0,), (0,)), ((), ())), preferred_element_type=F32)


def group_mean(row):
    v = jnp.broadcast_to(row, (8, C))
    lane = lax.broadcasted_iota(jnp.int32, (8, C), 1)
    for sh in (1, 2, 4):
        v = v + jnp.where((lane & sh) != 0, pltpu.roll(v, sh, 1), pltpu.roll(v, C - sh, 1))
    return v[0:1] * (1.0 / (POS * 8))


def colsum(v):
    return jnp.sum(v, axis=0, keepdims=True)


def norm_stats(ref, *at):
    x = ref[at]
    mean = group_mean(colsum(x))
    d = x - mean
    inv = lax.rsqrt(group_mean(colsum(d * d)) + NORM_EPS)
    return mean, inv


def put_shifted(bufs, i, r, v):
    rows = v.shape[0]
    col = lax.broadcasted_iota(jnp.int32, (rows, C), 0) & (SIDE - 1)
    at = pl.ds(PAD + r, rows)
    bufs[0, i, at, :] = jnp.where(col == 0, 0.0, pltpu.roll(v, 1, 0)).astype(BF16)
    bufs[1, i, at, :] = v.astype(BF16)
    bufs[2, i, at, :] = jnp.where(col == SIDE - 1, 0.0, pltpu.roll(v, rows - 1, 0)).astype(BF16)


def taps(bufs, flip):
    images = bufs.shape[1]
    out = []
    for dr in (-1, 0, 1):
        for dc in (-1, 0, 1):
            sr, sc = (-dr, -dc) if flip else (dr, dc)
            piece = bufs[sc + 1, :, PAD + SIDE * sr : PAD + SIDE * sr + POS, :]
            out.append(piece.reshape(images * POS, C))
    return out


def conv_forward(bufs, w, l, row):
    return dot_nn(jnp.concatenate(taps(bufs, False), axis=1), w[l, row : row + 9 * C, :])


def conv_input_grad(bufs, w, l, row):
    parts = [w[l, row + t * C : row + (t + 1) * C, :] for t in range(9)]
    return dot_nt(jnp.concatenate(taps(bufs, True), axis=1), jnp.concatenate(parts, axis=1))


def conv_weight_grad(act_t, bufs, grad, l, row):
    left = act_t[...]
    for t, piece in enumerate(taps(bufs, True)):
        grad[l, row + t * C : row + (t + 1) * C, :] = dot_nn(left, piece).astype(BF16)


def silu(v):
    h = 0.5 * v
    return h + h * jnp.tanh(h)


def silu_parts(v):
    s = 0.5 + 0.5 * jnp.tanh(0.5 * v)
    return s, s * (1.0 + v * (1.0 - s))


def clear_pads(bufs):
    zero = jnp.zeros(bufs.shape[:2] + (PAD, C), BF16)
    bufs[:, :, 0:PAD, :] = zero
    bufs[:, :, PAD + POS :, :] = zero


def split_qkv(w, l, qkvw, tmp):
    for h in range(2):
        tmp[h] = w[l, R_QKV : R_QKV + 3 * C, h * HALF : (h + 1) * HALF].astype(F32)
    for j in range(3):
        for h in range(2):
            at = j * C + h * HALF
            qkvw[:, at : at + HALF] = tmp[h, pl.ds(j, C, stride=3), :].astype(BF16)


def layer_forward(l, w, small, eo, xs, h1, y, qkv, att, o, st, bufs, nbuf, qkvw, tmp):
    images = h1.shape[1]
    flat = images * POS
    split_qkv(w, l, qkvw, tmp)
    mod = dot_nn(eo[...], w[l, R_EMB : R_EMB + 4 * C, :])
    ma = mod[0:4] + small[l, 5:6, :]
    mb = mod[4:8] + small[l, 6:7, :]
    for i in range(images):
        st[l, i, S_MA : S_MA + 1, :] = ma[i : i + 1]
        st[l, i, S_MB : S_MB + 1, :] = mb[i : i + 1]

    def first(i, _):
        mean, inv = norm_stats(xs, l, i)
        st[l, i, S_M1 : S_M1 + 1, :] = mean
        st[l, i, S_I1 : S_I1 + 1, :] = inv
        a = inv * small[l, 0:1, :]
        b = small[l, 1:2, :]
        for r in range(0, POS, CHUNK):
            put_shifted(bufs, i, r, silu((xs[l, i, r : r + CHUNK, :] - mean) * a + b))
        return 0

    lax.fori_loop(0, images, first, 0)
    h1[l] = (conv_forward(bufs, w, l, R_CONV1) + small[l, 2:3, :]).reshape(images, POS, C)

    def second(i, _):
        mean, inv = norm_stats(h1, l, i)
        st[l, i, S_M2 : S_M2 + 1, :] = mean
        st[l, i, S_I2 : S_I2 + 1, :] = inv
        gain = 1.0 + st[l, i, S_MA : S_MA + 1, :]
        a = inv * small[l, 3:4, :] * gain
        b = small[l, 4:5, :] * gain + st[l, i, S_MB : S_MB + 1, :]
        for r in range(0, POS, CHUNK):
            put_shifted(bufs, i, r, silu((h1[l, i, r : r + CHUNK, :] - mean) * a + b))
        return 0

    lax.fori_loop(0, images, second, 0)
    h2 = conv_forward(bufs, w, l, R_CONV2) + small[l, 7:8, :]
    y[l] = (xs[l] + h2.reshape(images, POS, C)) * RS

    def third(i, _):
        mean, inv = norm_stats(y, l, i)
        st[l, i, S_M3 : S_M3 + 1, :] = mean
        st[l, i, S_I3 : S_I3 + 1, :] = inv
        a = inv * small[l, 8:9, :]
        b = small[l, 9:10, :]
        for r in range(0, POS, CHUNK):
            nbuf[i, r : r + CHUNK, :] = ((y[l, i, r : r + CHUNK, :] - mean) * a + b).astype(BF16)
        return 0

    lax.fori_loop(0, images, third, 0)
    n = nbuf[...].reshape(flat, C)
    for j, row in ((0, 10), (1, None), (2, 11)):
        part = dot_nn(n, qkvw[:, j * C : (j + 1) * C])
        if row is not None:
            part = part + small[l, row : row + 1, :]
        qkv[l, :, :, j * C : (j + 1) * C] = part.astype(BF16).reshape(images, POS, C)

    def attend(i, _):
        s = dot_nt(qkv[l, i, :, 0:C], qkv[l, i, :, C : 2 * C])
        e = jnp.exp((s - jnp.max(s, axis=1, keepdims=True)) * (C**-0.5))
        p = (e * (1.0 / jnp.sum(e, axis=1, keepdims=True))).astype(BF16)
        att[l, i] = p
        o[l, i] = dot_nn(p, qkv[l, i, :, 2 * C :]).astype(BF16)
        return 0

    lax.fori_loop(0, images, attend, 0)
    out = dot_nn(o[l].reshape(flat, C), w[l, R_PROJ:, :]) + small[l, 12:13, :]
    xs[l + 1] = (y[l] + out.reshape(images, POS, C)) * RS


def layer_backward(
    l, w, small, eot, xs, h1, y, qkv, att, o, st, g, bufs, nbuf, qkvw, tmp, dn, dqkv, act_t,
    grad, sgrad,
):
    want = grad is not None
    images = h1.shape[1]
    flat = images * POS
    scale = C**-0.5
    zrow = jnp.zeros((1, C), F32)
    split_qkv(w, l, qkvw, tmp)
    gp = (g[...] * RS).astype(BF16).reshape(flat, C)
    nbuf[...] = dot_nt(gp, w[l, R_PROJ:, :]).astype(BF16).reshape(images, POS, C)
    if want:
        grad[l, R_PROJ:, :] = dot_tn(o[l].reshape(flat, C), gp).astype(BF16)
        sgrad[l, 12:13, :] = colsum(gp.astype(F32))

    def attend(i, _):
        p = att[l, i]
        pf = p.astype(F32)
        do = nbuf[i]
        dp = dot_nt(do, qkv[l, i, :, 2 * C :])
        ds = (pf * (dp - jnp.sum(dp * pf, axis=1, keepdims=True))).astype(BF16)
        dqkv[i, :, 0:C] = (dot_nn(ds, qkv[l, i, :, C : 2 * C]) * scale).astype(BF16)
        dqkv[i, :, C : 2 * C] = (dot_tn(ds, qkv[l, i, :, 0:C]) * scale).astype(BF16)
        dqkv[i, :, 2 * C :] = dot_tn(p, do).astype(BF16)
        return 0

    lax.fori_loop(0, images, attend, 0)
    dq = dqkv[...].reshape(flat, 3 * C)
    dn[...] = dot_nt(dq, qkvw[...]).reshape(images, POS, C)

    def third(i, carry):
        db7, dg8, db9 = carry
        mean, inv = st[l, i, S_M3 : S_M3 + 1, :], st[l, i, S_I3 : S_I3 + 1, :]
        gain = small[l, 8:9, :]
        nh = (y[l, i] - mean) * inv
        c1 = colsum(dn[i])
        c2 = colsum(dn[i] * nh)
        mg = group_mean(gain * c1)
        mc = group_mean(gain * c2)
        for r in range(0, POS, CHUNK):
            nhr = (y[l, i, r : r + CHUNK, :] - mean) * inv
            gm = g[i, r : r + CHUNK, :] * RS + inv * (
                gain * dn[i, r : r + CHUNK, :] - mg - nhr * mc
            )
            gm = gm * RS
            g[i, r : r + CHUNK, :] = gm
            put_shifted(bufs, i, r, gm)
            if want:
                nbuf[i, r : r + CHUNK, :] = (nhr * gain + small[l, 9:10, :]).astype(BF16)
                db7 = db7 + colsum(gm.astype(BF16).astype(F32))
        return db7, dg8 + c2, db9 + c1

    db7, dg8, db9 = lax.fori_loop(0, images, third, (zrow, zrow, zrow))
    if want:
        sgrad[l, 7:8, :] = db7
        sgrad[l, 8:9, :] = dg8
        sgrad[l, 9:10, :] = db9
        act_t[...] = nbuf[...].reshape(flat, C).T
        for j in range(3):
            dj = dqkv[:, :, j * C : (j + 1) * C].reshape(flat, C)
            wide = dot_nn(act_t[...], dj)
            for h in range(2):
                tmp[h, pl.ds(j, C, stride=3), :] = wide[:, h * HALF : (h + 1) * HALF]
            if j != 1:
                sgrad[l, 10 + j // 2 : 11 + j // 2, :] = colsum(dj.astype(F32))
        for h in range(2):
            grad[l, R_QKV : R_QKV + 3 * C, h * HALF : (h + 1) * HALF] = tmp[h].astype(BF16)
    dn[...] = conv_input_grad(bufs, w, l, R_CONV2).reshape(images, POS, C)

    def second_a(i, _):
        mean, inv = st[l, i, S_M2 : S_M2 + 1, :], st[l, i, S_I2 : S_I2 + 1, :]
        gain = 1.0 + st[l, i, S_MA : S_MA + 1, :]
        a = inv * small[l, 3:4, :] * gain
        b = small[l, 4:5, :] * gain + st[l, i, S_MB : S_MB + 1, :]
        for r in range(0, POS, CHUNK):
            pre = (h1[l, i, r : r + CHUNK, :] - mean) * a + b
            s, slope = silu_parts(pre)
            dn[i, r : r + CHUNK, :] = dn[i, r : r + CHUNK, :] * slope
            if want:
                nbuf[i, r : r + CHUNK, :] = (pre * s).astype(BF16)
        return 0

    lax.fori_loop(0, images, second_a, 0)
    if want:
        act_t[...] = nbuf[...].reshape(flat, C).T
        conv_weight_grad(act_t, bufs, grad, l, R_CONV2)
    row8 = lax.broadcasted_iota(jnp.int32, (8, C), 0)

    def second_b(i, carry):
        db2, dg3, db4, dm = carry
        mean, inv = st[l, i, S_M2 : S_M2 + 1, :], st[l, i, S_I2 : S_I2 + 1, :]
        modgain = 1.0 + st[l, i, S_MA : S_MA + 1, :]
        gain = small[l, 3:4, :]
        nh = (h1[l, i] - mean) * inv
        p1 = colsum(dn[i])
        p2 = colsum(dn[i] * nh)
        full = gain * modgain
        mg = group_mean(full * p1)
        mc = group_mean(full * p2)
        for r in range(0, POS, CHUNK):
            nhr = (h1[l, i, r : r + CHUNK, :] - mean) * inv
            dh = inv * (full * dn[i, r : r + CHUNK, :] - mg - nhr * mc)
            put_shifted(bufs, i, r, dh)
            if want:
                db2 = db2 + colsum(dh.astype(BF16).astype(F32))
        dma = gain * p2 + small[l, 4:5, :] * p1
        dm = jnp.where(row8 == i, dma, jnp.where(row8 == i + 4, p1, dm))
        return db2, dg3 + modgain * p2, db4 + modgain * p1, dm

    db2, dg3, db4, dm = lax.fori_loop(
        0, images, second_b, (zrow, zrow, zrow, jnp.zeros((8, C), F32))
    )
    if want:
        sgrad[l, 2:3, :] = db2
        sgrad[l, 3:4, :] = dg3
        sgrad[l, 4:5, :] = db4
        sgrad[l, 5:6, :] = colsum(dm[0:4])
        sgrad[l, 6:7, :] = colsum(dm[4:8])
        grad[l, R_EMB : R_EMB + 4 * C, :] = lax.dot_general(
            eot[...], dm, (((1,), (0,)), ((), ())),
            precision=lax.Precision.HIGHEST, preferred_element_type=F32,
        ).astype(BF16)
    dn[...] = conv_input_grad(bufs, w, l, R_CONV1).reshape(images, POS, C)

    def first(i, carry):
        dg0, db1 = carry
        mean, inv = st[l, i, S_M1 : S_M1 + 1, :], st[l, i, S_I1 : S_I1 + 1, :]
        gain = small[l, 0:1, :]
        b = small[l, 1:2, :]
        c1, c2 = zrow, zrow
        for r in range(0, POS, CHUNK):
            nhr = (xs[l, i, r : r + CHUNK, :] - mean) * inv
            pre = nhr * gain + b
            s, slope = silu_parts(pre)
            d = dn[i, r : r + CHUNK, :] * slope
            dn[i, r : r + CHUNK, :] = d
            c1 = c1 + colsum(d)
            c2 = c2 + colsum(d * nhr)
            if want:
                nbuf[i, r : r + CHUNK, :] = (pre * s).astype(BF16)
        mg = group_mean(gain * c1)
        mc = group_mean(gain * c2)
        for r in range(0, POS, CHUNK):
            nhr = (xs[l, i, r : r + CHUNK, :] - mean) * inv
            dx = inv * (gain * dn[i, r : r + CHUNK, :] - mg - nhr * mc)
            g[i, r : r + CHUNK, :] = g[i, r : r + CHUNK, :] + dx
        return dg0 + c2, db1 + c1

    dg0, db1 = lax.fori_loop(0, images, first, (zrow, zrow))
    if want:
        sgrad[l, 0:1, :] = dg0
        sgrad[l, 1:2, :] = db1
        act_t[...] = nbuf[...].reshape(flat, C).T
        conv_weight_grad(act_t, bufs, grad, l, R_CONV1)


def saved_shapes(images):
    return [
        jax.ShapeDtypeStruct((3, images, POS, C), F32),
        jax.ShapeDtypeStruct((2, images, POS, C), F32),
        jax.ShapeDtypeStruct((2, images, POS, C), F32),
        jax.ShapeDtypeStruct((2, images, POS, 3 * C), BF16),
        jax.ShapeDtypeStruct((2, images, POS, POS), BF16),
        jax.ShapeDtypeStruct((2, images, POS, C), BF16),
        jax.ShapeDtypeStruct((2, images, 8, C), F32),
    ]


def forward_kernel(x0, w, small, eo, xs, h1, y, qkv, att, o, st, bufs, nbuf, qkvw, tmp):
    clear_pads(bufs)
    xs[0] = x0[...]

    def body(l, _):
        layer_forward(l, w, small, eo, xs, h1, y, qkv, att, o, st, bufs, nbuf, qkvw, tmp)
        return 0

    lax.fori_loop(0, 2, body, 0)


def backward_kernel(want, *refs):
    cot, w, small, eot, xs, h1, y, qkv, att, o, st, g = refs[:12]
    refs = refs[12:]
    if want:
        grad, sgrad = refs[:2]
        refs = refs[2:]
    else:
        grad, sgrad = None, None
    bufs, nbuf, qkvw, tmp, dn, dqkv, act_t = refs
    clear_pads(bufs)
    g[...] = cot[...]
    if want:
        sgrad[...] = jnp.zeros(sgrad.shape, F32)

    def body(k, _):
        layer_backward(
            1 - k, w, small, eot, xs, h1, y, qkv, att, o, st, g, bufs, nbuf, qkvw, tmp, dn,
            dqkv, act_t, grad, sgrad,
        )
        return 0

    lax.fori_loop(0, 2, body, 0)


def vm(n):
    return [pl.BlockSpec(memory_space=pltpu.VMEM)] * n


def scratch_forward(images):
    return [
        pltpu.VMEM((3, images, POS + 2 * PAD, C), BF16),
        pltpu.VMEM((images, POS, C), BF16),
        pltpu.VMEM((C, 3 * C), BF16),
        pltpu.VMEM((2, 3 * C, HALF), F32),
    ]


def run_forward(x0, w, small, eo):
    images = x0.shape[0]
    return pl.pallas_call(
        forward_kernel,
        out_shape=saved_shapes(images),
        in_specs=vm(4),
        out_specs=vm(7),
        scratch_shapes=scratch_forward(images),
        compiler_params=pltpu.CompilerParams(vmem_limit_bytes=VMEM_LIMIT),
    )(x0, w, small, eo)


def run_backward(cot, w, small, eot, saved, want):
    images = cot.shape[0]
    outs = [jax.ShapeDtypeStruct(cot.shape, F32)]
    if want:
        outs += [
            jax.ShapeDtypeStruct((2, ROWS, C), BF16),
            jax.ShapeDtypeStruct((2, 16, C), F32),
        ]
    return pl.pallas_call(
        functools.partial(backward_kernel, want),
        out_shape=outs,
        in_specs=vm(11),
        out_specs=vm(len(outs)),
        scratch_shapes=scratch_forward(images)
        + [
            pltpu.VMEM((images, POS, C), F32),
            pltpu.VMEM((images, POS, 3 * C), BF16),
            pltpu.VMEM((C, images * POS), BF16),
        ],
        compiler_params=pltpu.CompilerParams(vmem_limit_bytes=VMEM_LIMIT),
    )(cot, w, small, eot, *saved)


PLANES, PLANE = 4, 4
MESH = pl.DeviceIdType.MESH


class Place:
    def __init__(self):
        self.sec = lax.axis_index("section")
        self.d = lax.axis_index("dp")
        self.x = lax.rem(self.d, 2)
        self.y = lax.rem(self.d // 2, 2)
        self.z = self.d // PLANE
        self.sib = {"section": 1 - self.sec}
        self.xn = {"dp": self.d + 1 - 2 * self.x}
        self.yn = {"dp": self.d + 2 - 4 * self.y}

    def plane(self, j):
        return lax.rem(self.z + j + PLANES, PLANES)

    def zpeer(self, j):
        return {"dp": self.plane(j) * PLANE + lax.rem(self.d, PLANE)}

    def meet(self):
        barrier = pltpu.get_barrier_semaphore()
        others = [self.sib, self.xn, self.yn] + [self.zpeer(j) for j in (1, 2, 3)]
        for other in others:
            pl.semaphore_signal(barrier, inc=1, device_id=other, device_id_type=MESH)
        pl.semaphore_wait(barrier, len(others))


def remote(src, dst, send, recv, target):
    return pltpu.make_async_remote_copy(
        src_ref=src, dst_ref=dst, send_sem=send, recv_sem=recv,
        device_id=target, device_id_type=MESH,
    )


Z1, X1, Y1, X2, Y2, S_OWN, S_X, S_Y, S_DA, S_DB = 0, 3, 7, 11, 15, 19, 23, 27, 31, 35
SLOTS = 39


def gather_kernel(*refs):
    nets = (len(refs) - 4) // 2
    ws, outs = refs[:nets], refs[nets : 2 * nets]
    stage, local_sem, send_sem, recv_sem = refs[2 * nets :]
    part = stage.shape[1]
    half = part // 2
    me = Place()
    for n in range(nets):
        stage[n] = ws[n][...].astype(BF16)
    me.meet()

    def rows(plane, y, x, lo, count):
        at = me.sec * ROWS + (plane * PLANE + y * 2 + x) * part + lo
        return pl.ds(pl.multiple_of(at, 16), count)

    sends = []

    def send(n, slot, where, target, src=None):
        piece = outs[n].at[where]
        copy = remote(
            piece if src is None else src, piece, send_sem.at[n, slot], recv_sem.at[n, slot], target
        )
        copy.start()
        sends.append(copy)

    def arrived(n, slot, where):
        piece = outs[n].at[where]
        remote(piece, piece, send_sem.at[n, slot], recv_sem.at[n, slot], me.sib).wait_recv()

    def own(j):
        return rows(me.plane(-j), me.y, me.x, 0, part)

    def begin(n):
        for j in (1, 2, 3):
            send(n, Z1 + j - 1, own(0), me.zpeer(j), stage.at[n])
        for slot, target in ((X1, me.xn), (Y1, me.yn), (S_OWN, me.sib)):
            send(n, slot, own(0), target, stage.at[n])
        copy = pltpu.make_async_copy(stage.at[n], outs[n].at[own(0)], local_sem.at[n])
        copy.start()
        return copy

    def phase1(n):
        for j in (1, 2, 3):
            arrived(n, Z1 + j - 1, own(j))
            for slot, target in ((X1, me.xn), (Y1, me.yn), (S_OWN, me.sib)):
                send(n, slot + j, own(j), target)

    def phase2(n):
        for j in range(PLANES):
            plane = me.plane(-j)
            arrived(n, X1 + j, rows(plane, me.y, 1 - me.x, 0, part))
            send(n, Y2 + j, rows(plane, me.y, 1 - me.x, 0, half), me.yn)
            send(n, S_X + j, rows(plane, me.y, 1 - me.x, 0, part), me.sib)
            arrived(n, Y1 + j, rows(plane, 1 - me.y, me.x, 0, part))
            send(n, X2 + j, rows(plane, 1 - me.y, me.x, half, half), me.xn)
            send(n, S_Y + j, rows(plane, 1 - me.y, me.x, 0, part), me.sib)

    def phase3(n):
        for j in range(PLANES):
            plane = me.plane(-j)
            for slot, to, lo in ((Y2, S_DA, 0), (X2, S_DB, half)):
                where = rows(plane, 1 - me.y, 1 - me.x, lo, half)
                arrived(n, slot + j, where)
                send(n, to + j, where, me.sib)

    def finish(n):
        for slot in range(S_OWN, SLOTS):
            arrived(n, slot, pl.ds(0, part if slot < S_DA else half))

    locals_ = [begin(n) for n in range(nets)]
    phase1(0)
    phase2(0)
    for n in range(1, nets):
        phase1(n)
        phase3(n - 1)
        phase2(n)
    phase3(nets - 1)
    for n in range(nets):
        finish(n)
    for copy in locals_:
        copy.wait()
    for copy in sends:
        copy.wait_send()


def gather_nets(*ws):
    part = ws[0].shape[0]
    nets = len(ws)
    outs = pl.pallas_call(
        gather_kernel,
        out_shape=[jax.ShapeDtypeStruct((2 * ROWS, C), BF16)] * nets,
        in_specs=vm(nets),
        out_specs=[pl.BlockSpec(memory_space=pl.ANY)] * nets,
        scratch_shapes=[
            pltpu.VMEM((nets, part, C), BF16),
            pltpu.SemaphoreType.DMA((nets,)),
            pltpu.SemaphoreType.DMA((nets, SLOTS)),
            pltpu.SemaphoreType.DMA((nets, SLOTS)),
        ],
        compiler_params=pltpu.CompilerParams(
            collective_id=0, has_side_effects=True, vmem_limit_bytes=VMEM_LIMIT
        ),
    )(*ws)
    return [a.reshape(2, ROWS, C) for a in outs]


A_SLOT, B_SLOT, C_SLOT, D_SLOT = 0, 4, 20, 28
R_SLOTS = 31


def reduce_kernel(*refs):
    nets = 2
    gb, sg = refs[:nets], refs[nets]
    shard, stot, sqtot = refs[nets + 1 : nets + 4]
    own, sib, rb, rc, rd, sbuf, srecv, qbuf, qrecv, lsem, ssem, rsem, tsem, urem = refs[nets + 4 :]
    part = shard.shape[1]
    half = part // 2
    span = PLANE * part
    me = Place()
    me.meet()
    sends = []

    def send(src, dst, s, r, target):
        copy = remote(src, dst, s, r, target)
        copy.start()
        sends.append(copy)

    def arrived(dst, s, r):
        remote(dst, dst, s, r, me.sib).wait_recv()

    def zt(k):
        return me.plane(1 + k)

    def block(base, k):
        return pl.ds(pl.multiple_of(base + zt(k) * span, 16), span)

    def piece(k, y, x, lo, count):
        at = (zt(k) * PLANE + y * 2 + x) * part + lo
        return pl.ds(pl.multiple_of(at, 16), count)

    loads = {}
    for n in range(nets):
        for k in range(PLANES):
            there, here = block((1 - me.sec) * ROWS, k), block(me.sec * ROWS, k)
            slot = A_SLOT + k
            send(
                gb[n].at[there], sib.at[n, block(0, k)], ssem.at[n, slot], rsem.at[n, slot], me.sib
            )
            copy = pltpu.make_async_copy(gb[n].at[here], own.at[n, block(0, k)], lsem.at[n, k])
            copy.start()
            loads[n, k] = copy

    def totals(buf, recv, sem_s, sem_r, base, first):
        steps = ((0, me.sib), (1, me.xn), (2, me.yn))
        for slot, target in steps:
            if slot == 0 and first is not None:
                src = first
            else:
                src = buf.at[slot]
            send(src, recv.at[slot], sem_s.at[base + slot], sem_r.at[base + slot], target)
            arrived(recv.at[slot], sem_s.at[base + slot], sem_r.at[base + slot])
            buf[slot + 1] = buf[slot] + recv[slot]
        recv[3 + me.z] = buf[3]
        for j in (1, 2, 3):
            at = base + 2 + j
            send(buf.at[3], recv.at[3 + me.z], sem_s.at[at], sem_r.at[at], me.zpeer(j))
        for j in (1, 2, 3):
            at = base + 2 + j
            arrived(recv.at[3 + me.plane(-j)], sem_s.at[at], sem_r.at[at])
        return (recv[3] + recv[4]) + (recv[5] + recv[6])

    def add_rows(dst, src, n_rows, step):
        def body(i, _):
            r = pl.multiple_of(i * step, 16)
            a, at = dst(r, step)
            b, bt = src(r, step)
            a[at] = (a[at].astype(F32) + b[bt].astype(F32)).astype(BF16)
            return 0

        lax.fori_loop(0, n_rows // step, body, 0)

    def stage_a(n, k):
        slot = A_SLOT + k
        loads[n, k].wait()
        arrived(sib.at[n, block(0, k)], ssem.at[n, slot], rsem.at[n, slot])
        base = zt(k) * span
        step = part

        def at(ref):
            return lambda r, c: (ref, (n, pl.ds(pl.multiple_of(base + r, 16), c), slice(None)))

        add_rows(at(own), at(sib), span, step)
        for j in range(2):
            slot = B_SLOT + 4 * k + j
            send(
                own.at[n, piece(k, 1 - me.y, j, 0, half)], rb.at[n, k, j],
                ssem.at[n, slot], rsem.at[n, slot], me.yn,
            )
            slot = B_SLOT + 4 * k + 2 + j
            send(
                own.at[n, piece(k, j, 1 - me.x, half, half)], rb.at[n, k, 2 + j],
                ssem.at[n, slot], rsem.at[n, slot], me.xn,
            )

    def join(n, where, recv_ref, at):
        own[(n, where, slice(None))] = (
            own[(n, where, slice(None))].astype(F32) + recv_ref[at].astype(F32)
        ).astype(BF16)

    def stage_c(n, k):
        for j in range(4):
            slot = B_SLOT + 4 * k + j
            arrived(rb.at[n, k, j], ssem.at[n, slot], rsem.at[n, slot])
            where = piece(k, me.y, j, 0, half) if j < 2 else piece(k, j - 2, me.x, half, half)
            join(n, where, rb, (n, k, j))
        slot = C_SLOT + 2 * k
        send(
            own.at[n, piece(k, me.y, 1 - me.x, 0, half)], rc.at[n, k, 0],
            ssem.at[n, slot], rsem.at[n, slot], me.xn,
        )
        slot += 1
        send(
            own.at[n, piece(k, 1 - me.y, me.x, half, half)], rc.at[n, k, 1],
            ssem.at[n, slot], rsem.at[n, slot], me.yn,
        )

    def stage_d(n, k):
        for j in range(2):
            slot = C_SLOT + 2 * k + j
            arrived(rc.at[n, k, j], ssem.at[n, slot], rsem.at[n, slot])
            where = piece(k, me.y, me.x, j * half, half)
            if k < PLANES - 1:
                join(n, where, rc, (n, k, j))
            else:
                shard[n, j * half : (j + 1) * half, :] = (
                    own[(n, where, slice(None))].astype(F32) + rc[n, k, j].astype(F32)
                )
        if k < PLANES - 1:
            slot = D_SLOT + k
            send(
                own.at[n, piece(k, me.y, me.x, 0, part)], rd.at[n, k],
                ssem.at[n, slot], rsem.at[n, slot], me.zpeer(1 + k),
            )

    def stage_e(n):
        for k in range(PLANES - 1):
            slot = D_SLOT + k
            arrived(rd.at[n, k], ssem.at[n, slot], rsem.at[n, slot])
        shard[n] = (
            shard[n] + rd[n, 0].astype(F32) + (rd[n, 1].astype(F32) + rd[n, 2].astype(F32))
        )

    order = [(n, k) for n in range(nets) for k in range(PLANES)]
    lag_c, lag_d = 1, 2
    for t in range(len(order) + lag_d):
        if t < len(order):
            stage_a(*order[t])
        if 0 <= t - lag_c < len(order):
            stage_c(*order[t - lag_c])
        if 0 <= t - lag_d < len(order):
            stage_d(*order[t - lag_d])
    sbuf[0] = sg[me.sec]
    stot[...] = totals(sbuf, srecv, tsem, urem, 0, sg.at[1 - me.sec])
    for n in range(nets):
        stage_e(n)
    lane = lax.broadcasted_iota(jnp.int32, (8, HALF), 1)
    tile = jnp.zeros((8, HALF), F32)
    for n in range(nets):
        big = jnp.sum(shard[n] * shard[n])
        low = jnp.sum(stot[16 * n : 16 * n + 13, :] * stot[16 * n : 16 * n + 13, :])
        tile = jnp.where(lane == n, big + jnp.where(me.d == 0, low, 0.0), tile)
    qbuf[0] = tile
    sqtot[...] = totals(qbuf, qrecv, tsem, urem, 6, None)
    for copy in sends:
        copy.wait_send()


def reduce_nets(bigs, small, part):
    nets = len(bigs)
    half = part // 2
    return pl.pallas_call(
        reduce_kernel,
        out_shape=[
            jax.ShapeDtypeStruct((nets, part, C), F32),
            jax.ShapeDtypeStruct(small.shape[1:], F32),
            jax.ShapeDtypeStruct((8, HALF), F32),
        ],
        in_specs=[pl.BlockSpec(memory_space=pl.ANY)] * nets + vm(1),
        out_specs=vm(3),
        scratch_shapes=[
            pltpu.VMEM((nets, ROWS, C), BF16),
            pltpu.VMEM((nets, ROWS, C), BF16),
            pltpu.VMEM((nets, PLANES, 4, half, C), BF16),
            pltpu.VMEM((nets, PLANES, 2, half, C), BF16),
            pltpu.VMEM((nets, PLANES - 1, part, C), BF16),
            pltpu.VMEM((4,) + small.shape[1:], F32),
            pltpu.VMEM((7,) + small.shape[1:], F32),
            pltpu.VMEM((4, 8, HALF), F32),
            pltpu.VMEM((7, 8, HALF), F32),
            pltpu.SemaphoreType.DMA((nets, PLANES)),
            pltpu.SemaphoreType.DMA((nets, R_SLOTS)),
            pltpu.SemaphoreType.DMA((nets, R_SLOTS)),
            pltpu.SemaphoreType.DMA((12,)),
            pltpu.SemaphoreType.DMA((12,)),
        ],
        compiler_params=pltpu.CompilerParams(
            collective_id=1, has_side_effects=True, vmem_limit_bytes=VMEM_LIMIT
        ),
    )(*[b.reshape(2 * ROWS, C) for b in bigs], small)


def adam_step(master, first_mom, second_mom, grad):
    first_new = BETA_ONE * first_mom + (1.0 - BETA_ONE) * grad
    second_new = BETA_TWO * second_mom + (1.0 - BETA_TWO) * grad * grad
    direction = (
        first_new
        / (1.0 - BETA_ONE**STEP)
        / (jnp.sqrt(second_new / (1.0 - BETA_TWO**STEP)) + ADAM_EPS)
    )
    return (master - LEARN_RATE * (direction + WEIGHT_DECAY * master), first_new, second_new)


EMA_RATE = 0.5 ** (20.0 / STEP)


def update_kernel(shard, stot, sqtot, *refs):
    ins, outs = refs[:14], refs[14:]
    nums = outs[14]
    count = stot[15:16, 0:1]
    sq = sqtot[0:1, :]
    lane = lax.broadcasted_iota(jnp.int32, sq.shape, 1)
    total = jnp.zeros_like(sq)
    scales = []
    for n in range(2):
        norm = jnp.sqrt(jnp.sum(jnp.where(lane == n, sq, 0.0), axis=1, keepdims=True)) / count
        scales.append(jnp.minimum(1.0, CLIP_NORM / norm) / count)
        total = jnp.where(lane == n, norm, total)
        total = jnp.where(lane == 2 + n, stot[13 + n : 14 + n, 0:1] / count, total)
    nums[...] = jnp.broadcast_to(total, nums.shape)

    def one(scale, grad, w, m, v, ema, ow, om, ov, oe):
        new, first, second = adam_step(w[0], m[0], v[0], grad * scale)
        ow[0] = new
        om[0] = first
        ov[0] = second
        if ema is not None:
            oe[0] = EMA_RATE * ema[0] + (1.0 - EMA_RATE) * new

    one(scales[0], shard[0], *ins[0:4], *outs[0:4])
    one(scales[0], stot[0:13], *ins[4:8], *outs[4:8])
    one(scales[1], shard[1], *ins[8:11], None, *outs[8:11], None)
    one(scales[1], stot[16:29], *ins[11:14], None, *outs[11:14], None)


def update_nets(shard, stot, sqtot, states):
    res = pl.pallas_call(
        update_kernel,
        out_shape=[jax.ShapeDtypeStruct(a.shape, F32) for a in states]
        + [jax.ShapeDtypeStruct((8, HALF), F32)],
        in_specs=vm(3 + len(states)),
        out_specs=vm(len(states) + 1),
        compiler_params=pltpu.CompilerParams(vmem_limit_bytes=VMEM_LIMIT),
    )(shard, stot, sqtot, *states)
    nums = res[-1]
    return tuple(res[:-1]) + (nums[0, 0:2], nums[0, 2:4])


def gather_plain(shard):
    rows = lax.all_gather(shard.astype(BF16), "dp", axis=1, tiled=True)
    return lax.all_gather(rows, "section", axis=0, tiled=True)


def reduce_plain(bigs, small):
    shards_, squares = [], []
    own = lax.psum_scatter(small, "section", scatter_dimension=0, tiled=True)
    stot = lax.psum(own, "dp")[0]
    first = lax.axis_index("dp") == 0
    for n, big in enumerate(bigs):
        own = lax.psum_scatter(big, "section", scatter_dimension=0, tiled=True)
        own = lax.psum_scatter(own, "dp", scatter_dimension=1, tiled=True)[0].astype(F32)
        shards_.append(own)
        low = jnp.sum(jnp.square(stot[16 * n : 16 * n + 13]))
        squares.append(jnp.sum(own * own) + jnp.where(first, low, 0.0))
    sq = lax.psum(jnp.stack(squares), ("section", "dp"))
    return jnp.stack(shards_), stot, jnp.zeros((8, HALF), F32).at[:, 0:2].set(sq)


def shards(
    z_noise, eps_noise, levels, counts,
    gen_w, gen_m, gen_v, gen_ema, gen_small, gen_small_m, gen_small_v, gen_small_ema,
    fake_w, fake_m, fake_v, fake_small, fake_small_m, fake_small_v,
    teacher_w, teacher_small,
):
    section_idx = lax.axis_index("section")
    sections = lax.axis_size("section")
    custom = lax.axis_size("dp") == PLANES * PLANE
    per_group = z_noise.shape[0]
    images = per_group // sections
    start = section_idx * images
    elements = POS * C

    def mine(a):
        return lax.dynamic_slice_in_dim(a, start, images, 0)

    def wide(a):
        return a[:, None, None]

    z = mine(z_noise)
    eps = mine(eps_noise)
    local_count = counts[0]
    valid = ((start + jnp.arange(images)) < local_count).astype(F32)
    sigma = sigma_levels(mine(levels))
    s_in, s_skip, s_out, s_lam = [wide(t) for t in precondition(sigma)]
    init = jnp.full((images,), SIGMA_INIT, F32)
    g_in, g_skip, g_out, _ = [wide(t) for t in precondition(init)]
    gen_eo, score_eo = spread_embed(init), spread_embed(sigma)
    gen_eot, score_eot = gen_eo.astype(F32).T, score_eo.astype(F32).T

    smalls = lax.all_gather(
        jnp.concatenate([gen_small, fake_small, teacher_small]), "section", axis=0
    )
    gs, fs, ts = smalls[:, 0], smalls[:, 1], smalls[:, 2]
    if custom:
        gw, fw, tw = gather_nets(gen_w[0], fake_w[0], teacher_w[0])
    else:
        gw, fw, tw = gather_plain(gen_w), gather_plain(fake_w), gather_plain(teacher_w)

    raw = SIGMA_INIT * z
    gen_saved = run_forward(g_in * raw, gw, gs, gen_eo)
    samples = g_skip * raw + g_out * gen_saved[0][2]
    noisy = samples + wide(sigma) * eps
    x0 = s_in * noisy
    fake_saved = run_forward(x0, fw, fs, score_eo)
    fake_den = s_skip * noisy + s_out * fake_saved[0][2]
    factor = wide(valid) * s_lam / elements
    miss = fake_den - samples
    _, fake_g, fake_sg = run_backward(s_out * 2.0 * factor * miss, fw, fs, score_eot, fake_saved, True)
    teacher_saved = run_forward(x0, tw, ts, score_eo)
    teacher_den = s_skip * noisy + s_out * teacher_saved[0][2]
    gap = teacher_den - fake_den
    loss_gen = jnp.sum(factor * ((1.0 - ALPHA_MIX) * gap * gap + gap * miss))
    loss_fake = jnp.sum(factor * miss * miss)
    grad_teacher = factor * (2.0 * (1.0 - ALPHA_MIX) * gap + miss)
    grad_fake = factor * (gap - 2.0 * (1.0 - ALPHA_MIX) * gap - miss)
    direct = s_skip * (grad_teacher + grad_fake) - factor * gap
    (back_t,) = run_backward(s_out * grad_teacher, tw, ts, score_eot, teacher_saved, False)
    (back_f,) = run_backward(s_out * grad_fake, fw, fs, score_eot, fake_saved, False)
    gen_cot = g_out * (direct + s_in * (back_t + back_f))
    _, gen_g, gen_sg = run_backward(gen_cot, gw, gs, gen_eot, gen_saved, True)

    scalars = jnp.broadcast_to(jnp.stack([loss_gen, loss_fake, jnp.sum(valid)])[:, None], (3, C))
    small_sums = jnp.concatenate(
        [gen_sg[:, :13], jnp.broadcast_to(scalars, (2, 3, C)), fake_sg], axis=1
    )
    if custom:
        reduced = reduce_nets((gen_g, fake_g), small_sums, gen_w.shape[1])
    else:
        reduced = reduce_plain((gen_g, fake_g), small_sums)
    return update_nets(
        *reduced,
        (
            gen_w, gen_m, gen_v, gen_ema, gen_small, gen_small_m, gen_small_v, gen_small_ema,
            fake_w, fake_m, fake_v, fake_small, fake_small_m, fake_small_v,
        ),
    )


def solution(mesh):
    images = P("dp", None, None)
    big = P("section", "dp", None)
    small = P("section", None, None)
    return jax.shard_map(
        shards,
        mesh=mesh,
        in_specs=(images, images, P("dp"), P("dp"))
        + (big,) * 4 + (small,) * 4 + (big,) * 3 + (small,) * 3 + (big, small),
        out_specs=(big,) * 4 + (small,) * 4 + (big,) * 3 + (small,) * 3 + (P(), P()),
        check_vma=False,
    )
```

```python
import functools

import jax
import jax.numpy as jnp
from jax import lax
from jax.experimental import pallas as pl
from jax.experimental.pallas import tpu as pltpu
from jax.sharding import PartitionSpec as P

GROUPS = 32
SIDE = 16
LEVELS = 1000
STEP = 10

SIGMA_DATA = 0.5
SIGMA_INIT = 2.5
SIGMA_LOW = 0.05
SIGMA_HIGH = 20.0
RHO_POWER = 7.0
ALPHA_MIX = 1.2
RS = 0.7071067811865476
NORM_EPS = 1e-05
CLIP_NORM = 0.001
LEARN_RATE = 0.15
BETA_ONE = 0.9
BETA_TWO = 0.999
ADAM_EPS = 1e-08
WEIGHT_DECAY = 0.01

C = 256
HALF = 128
POS = 256
ROWS = 26 * C
CHUNK = 64
PAD = SIDE
F32 = jnp.float32
BF16 = jnp.bfloat16
VMEM_LIMIT = 58 * 2**20

R_CONV1, R_CONV2, R_EMB, R_QKV, R_PROJ = 0, 9 * C, 18 * C, 22 * C, 25 * C
S_M1, S_I1, S_M2, S_I2, S_M3, S_I3, S_MA, S_MB = range(8)


def sigma_levels(level_ids):
    fraction = level_ids.astype(F32) / (LEVELS - 1)
    top_root = SIGMA_HIGH ** (1.0 / RHO_POWER)
    bottom_root = SIGMA_LOW ** (1.0 / RHO_POWER)
    return (top_root + fraction * (bottom_root - top_root)) ** RHO_POWER


def precondition(sigma_vals):
    total = sigma_vals * sigma_vals + SIGMA_DATA**2
    return (
        lax.rsqrt(total),
        SIGMA_DATA**2 / total,
        sigma_vals * SIGMA_DATA * lax.rsqrt(total),
        total / (sigma_vals * sigma_vals * SIGMA_DATA**2),
    )


def noise_embed(sigma_vals, channel_count):
    frequency = (1.0 / 10000.0) ** (jnp.arange(channel_count, dtype=F32) / channel_count)
    angles = (jnp.log(sigma_vals) / 4.0)[..., None] * frequency
    return jnp.concatenate([jnp.cos(angles), jnp.sin(angles)], axis=-1)


def spread_embed(sigma_vals):
    emb = noise_embed(sigma_vals, C).astype(BF16)
    images = emb.shape[0]
    zero = jnp.zeros_like(emb)
    low = jnp.stack([emb, zero], axis=-1).reshape(images, 4 * C)
    high = jnp.stack([zero, emb], axis=-1).reshape(images, 4 * C)
    fill = jnp.zeros((4 - images, 4 * C), BF16)
    return jnp.concatenate([low, fill, high, fill], axis=0)


def dot_nn(a, b):
    return lax.dot_general(a, b, (((1,), (0,)), ((), ())), preferred_element_type=F32)


def dot_nt(a, b):
    return lax.dot_general(a, b, (((1,), (1,)), ((), ())), preferred_element_type=F32)


def dot_tn(a, b):
    return lax.dot_general(a, b, (((0,), (0,)), ((), ())), preferred_element_type=F32)


def group_mean(v):
    lane = lax.broadcasted_iota(jnp.int32, (8, C), 1)
    for sh in (1, 2, 4):
        v = v + jnp.where((lane & sh) != 0, pltpu.roll(v, sh, 1), pltpu.roll(v, C - sh, 1))
    return v * (1.0 / (POS * 8))


def colsum(v):
    return jnp.sum(v, axis=0, keepdims=True)


def put_shifted(bufs, i, r, v):
    rows = v.shape[0]
    col = lax.broadcasted_iota(jnp.int32, (rows, C), 0) & (SIDE - 1)
    at = pl.ds(PAD + r, rows)
    bufs[0, i, at, :] = jnp.where(col == 0, 0.0, pltpu.roll(v, 1, 0)).astype(BF16)
    bufs[1, i, at, :] = v.astype(BF16)
    bufs[2, i, at, :] = jnp.where(col == SIDE - 1, 0.0, pltpu.roll(v, rows - 1, 0)).astype(BF16)


def taps(bufs, flip):
    images = bufs.shape[1]
    out = []
    for dr in (-1, 0, 1):
        for dc in (-1, 0, 1):
            sr, sc = (-dr, -dc) if flip else (dr, dc)
            piece = bufs[sc + 1, :, PAD + SIDE * sr : PAD + SIDE * sr + POS, :]
            out.append(piece.reshape(images * POS, C))
    return out


def conv_forward(bufs, w, l, row):
    return dot_nn(jnp.concatenate(taps(bufs, False), axis=1), w[l, row : row + 9 * C, :])


def conv_input_grad(bufs, w, l, row):
    parts = [w[l, row + t * C : row + (t + 1) * C, :] for t in range(9)]
    return dot_nt(jnp.concatenate(taps(bufs, True), axis=1), jnp.concatenate(parts, axis=1))


def conv_weight_grad(act_t, bufs, grad, l, row):
    left = act_t[...]
    for t, piece in enumerate(taps(bufs, True)):
        grad[l, row + t * C : row + (t + 1) * C, :] = dot_nn(left, piece).astype(BF16)


def silu(v):
    h = 0.5 * v
    return h + h * jnp.tanh(h)


def silu_parts(v):
    s = 0.5 + 0.5 * jnp.tanh(0.5 * v)
    return s, s * (1.0 + v * (1.0 - s))


def clear_pads(bufs):
    zero = jnp.zeros(bufs.shape[:2] + (PAD, C), BF16)
    bufs[:, :, 0:PAD, :] = zero
    bufs[:, :, PAD + POS :, :] = zero


def split_qkv(w, l, qkvw, tmp):
    for h in range(2):
        tmp[h] = w[l, R_QKV : R_QKV + 3 * C, h * HALF : (h + 1) * HALF].astype(F32)
    for j in range(3):
        for h in range(2):
            at = j * C + h * HALF
            qkvw[:, at : at + HALF] = tmp[h, pl.ds(j, C, stride=3), :].astype(BF16)


def norm_stats(views):
    fill = [jnp.zeros((8 - len(views), C), F32)]
    sums = jnp.concatenate([colsum(x) for x in views] + fill, axis=0)
    mean = group_mean(sums)
    squares = [colsum(jnp.square(x - mean[i : i + 1])) for i, x in enumerate(views)]
    return mean, lax.rsqrt(group_mean(jnp.concatenate(squares + fill, axis=0)) + NORM_EPS)


def tap_rows(bufs, flip, which):
    out = []
    for dr in (-1, 0, 1):
        for dc in (-1, 0, 1):
            sr, sc = (-dr, -dc) if flip else (dr, dc)
            at = slice(PAD + SIDE * sr, PAD + SIDE * sr + POS)
            piece = jnp.concatenate([bufs[sc + 1, i, at, :] for i in which], axis=0)
            out.append(piece)
    return out


def layer_forward(l, w, small, eo, xs, h1, y, qkv, att, o, st, bufs, nbuf, qkvw, tmp, staged):
    images = h1.shape[1]
    split_qkv(w, l, qkvw, tmp)
    mod = dot_nn(eo[...], w[l, R_EMB : R_EMB + 4 * C, :])
    ma = mod[0:4] + small[l, 5:6, :]
    mb = mod[4:8] + small[l, 6:7, :]
    for i in range(images):
        st[l, i, S_MA : S_MA + 1, :] = ma[i : i + 1]
        st[l, i, S_MB : S_MB + 1, :] = mb[i : i + 1]

    def row(k):
        return small[l, k : k + 1, :]

    def keep(which, mean, inv, at):
        for k, i in enumerate(which):
            st[l, i, at : at + 1, :] = mean[k : k + 1]
            st[l, i, at + 1 : at + 2, :] = inv[k : k + 1]

    def first(which):
        mean, inv = norm_stats([xs[l, i] for i in which])
        keep(which, mean, inv, S_M1)
        for k, i in enumerate(which):
            a = inv[k : k + 1] * row(0)
            for r in range(0, POS, CHUNK):
                v = (xs[l, i, r : r + CHUNK, :] - mean[k : k + 1]) * a + row(1)
                put_shifted(bufs, i, r, silu(v))

    def conv(which, at):
        left = jnp.concatenate(tap_rows(bufs, False, which), axis=1)
        return dot_nn(left, w[l, at : at + 9 * C, :])

    def conv_one(which):
        out = conv(which, R_CONV1) + row(2)
        for k, i in enumerate(which):
            h1[l, i] = out[k * POS : (k + 1) * POS]

    def second(which):
        mean, inv = norm_stats([h1[l, i] for i in which])
        keep(which, mean, inv, S_M2)
        for k, i in enumerate(which):
            gain = 1.0 + ma[i : i + 1]
            a = inv[k : k + 1] * row(3) * gain
            b = row(4) * gain + mb[i : i + 1]
            for r in range(0, POS, CHUNK):
                v = (h1[l, i, r : r + CHUNK, :] - mean[k : k + 1]) * a + b
                put_shifted(bufs, i, r, silu(v))

    def conv_two(which):
        out = conv(which, R_CONV2) + row(7)
        for k, i in enumerate(which):
            y[l, i] = (xs[l, i] + out[k * POS : (k + 1) * POS]) * RS

    def third(which):
        mean, inv = norm_stats([y[l, i] for i in which])
        keep(which, mean, inv, S_M3)
        for k, i in enumerate(which):
            a = inv[k : k + 1] * row(8)
            for r in range(0, POS, CHUNK):
                v = (y[l, i, r : r + CHUNK, :] - mean[k : k + 1]) * a + row(9)
                nbuf[i, r : r + CHUNK, :] = v.astype(BF16)

    def project_in(which):
        n = jnp.concatenate([nbuf[i] for i in which], axis=0)
        for j, at in ((0, 10), (1, None), (2, 11)):
            part = dot_nn(n, qkvw[:, j * C : (j + 1) * C])
            if at is not None:
                part = part + row(at)
            part = part.astype(BF16)
            for k, i in enumerate(which):
                qkv[l, i, :, j * C : (j + 1) * C] = part[k * POS : (k + 1) * POS]

    def attend(which):
        scores = [dot_nt(qkv[l, i, :, 0:C], qkv[l, i, :, C : 2 * C]) for i in which]
        for s, i in zip(scores, which):
            e = jnp.exp((s - jnp.max(s, axis=1, keepdims=True)) * (C**-0.5))
            p = (e * (1.0 / jnp.sum(e, axis=1, keepdims=True))).astype(BF16)
            att[l, i] = p
            o[l, i] = dot_nn(p, qkv[l, i, :, 2 * C :]).astype(BF16)

    def project_out(which):
        left = jnp.concatenate([o[l, i] for i in which], axis=0)
        out = dot_nn(left, w[l, R_PROJ:, :]) + row(12)
        for k, i in enumerate(which):
            xs[l + 1, i] = (y[l, i] + out[k * POS : (k + 1) * POS]) * RS

    steps = (first, conv_one, second, conv_two, third, project_in, attend, project_out)
    if not staged:
        for step in steps:
            step(range(images))
    else:
        for t in range(len(steps) + images - 1):
            for i in range(images):
                if 0 <= t - i < len(steps):
                    steps[t - i]([i])


def layer_backward(
    l, w, small, eot, xs, h1, y, qkv, att, o, st, g, bufs, nbuf, qkvw, tmp, dn, dqkv, act_t,
    grad, sgrad,
):
    want = grad is not None
    images = h1.shape[1]
    which = range(images)
    flat = images * POS
    scale = C**-0.5
    split_qkv(w, l, qkvw, tmp)

    def row(k):
        return small[l, k : k + 1, :]

    def rows8(rows):
        return jnp.concatenate(list(rows) + [jnp.zeros((8 - len(rows), C), F32)], axis=0)

    def stat(at):
        return [(st[l, i, at : at + 1, :], st[l, i, at + 1 : at + 2, :]) for i in which]

    gp = (g[...] * RS).astype(BF16).reshape(flat, C)
    nbuf[...] = dot_nt(gp, w[l, R_PROJ:, :]).astype(BF16).reshape(images, POS, C)
    if want:
        grad[l, R_PROJ:, :] = dot_tn(o[l].reshape(flat, C), gp).astype(BF16)
        sgrad[l, 12:13, :] = colsum(gp.astype(F32))
    dps = [dot_nt(nbuf[i], qkv[l, i, :, 2 * C :]) for i in which]
    for i, dp in zip(which, dps):
        p = att[l, i]
        pf = p.astype(F32)
        ds = (pf * (dp - jnp.sum(dp * pf, axis=1, keepdims=True))).astype(BF16)
        dqkv[i, :, 0:C] = (dot_nn(ds, qkv[l, i, :, C : 2 * C]) * scale).astype(BF16)
        dqkv[i, :, C : 2 * C] = (dot_tn(ds, qkv[l, i, :, 0:C]) * scale).astype(BF16)
        dqkv[i, :, 2 * C :] = dot_tn(p, nbuf[i]).astype(BF16)
    dn[...] = dot_nt(dqkv[...].reshape(flat, 3 * C), qkvw[...]).reshape(images, POS, C)

    stats = stat(S_M3)
    c1 = rows8([colsum(dn[i]) for i in which])
    c2 = rows8([colsum(dn[i] * ((y[l, i] - stats[i][0]) * stats[i][1])) for i in which])
    mg = group_mean(row(8) * c1)
    mc = group_mean(row(8) * c2)
    db7 = jnp.zeros((1, C), F32)
    for i in which:
        mean, inv = stats[i]
        for r in range(0, POS, CHUNK):
            nh = (y[l, i, r : r + CHUNK, :] - mean) * inv
            gm = g[i, r : r + CHUNK, :] * RS + inv * (
                row(8) * dn[i, r : r + CHUNK, :] - mg[i : i + 1] - nh * mc[i : i + 1]
            )
            gm = gm * RS
            g[i, r : r + CHUNK, :] = gm
            put_shifted(bufs, i, r, gm)
            if want:
                nbuf[i, r : r + CHUNK, :] = (nh * row(8) + row(9)).astype(BF16)
                db7 = db7 + colsum(gm)
    if want:
        sgrad[l, 7:8, :] = db7
        sgrad[l, 8:9, :] = colsum(c2)
        sgrad[l, 9:10, :] = colsum(c1)
        act_t[...] = nbuf[...].reshape(flat, C).T
        for j in range(3):
            dj = dqkv[:, :, j * C : (j + 1) * C].reshape(flat, C)
            part = dot_nn(act_t[...], dj)
            for h in range(2):
                tmp[h, pl.ds(j, C, stride=3), :] = part[:, h * HALF : (h + 1) * HALF]
            if j != 1:
                sgrad[l, 10 + j // 2 : 11 + j // 2, :] = colsum(dj.astype(F32))
        for h in range(2):
            grad[l, R_QKV : R_QKV + 3 * C, h * HALF : (h + 1) * HALF] = tmp[h].astype(BF16)
    dn[...] = conv_input_grad(bufs, w, l, R_CONV2).reshape(images, POS, C)

    stats = stat(S_M2)
    gains = [1.0 + st[l, i, S_MA : S_MA + 1, :] for i in which]
    p1, p2 = [], []
    for i in which:
        mean, inv = stats[i]
        a = row(3) * gains[i]
        b = row(4) * gains[i] + st[l, i, S_MB : S_MB + 1, :]
        s1 = jnp.zeros((1, C), F32)
        s2 = jnp.zeros((1, C), F32)
        for r in range(0, POS, CHUNK):
            nh = (h1[l, i, r : r + CHUNK, :] - mean) * inv
            pre = nh * a + b
            s, slope = silu_parts(pre)
            d = dn[i, r : r + CHUNK, :] * slope
            dn[i, r : r + CHUNK, :] = d
            s1 = s1 + colsum(d)
            s2 = s2 + colsum(d * nh)
            if want:
                nbuf[i, r : r + CHUNK, :] = (pre * s).astype(BF16)
        p1.append(s1)
        p2.append(s2)
    if want:
        act_t[...] = nbuf[...].reshape(flat, C).T
        conv_weight_grad(act_t, bufs, grad, l, R_CONV2)
    full = rows8([row(3) * gains[i] for i in which])
    p18, p28 = rows8(p1), rows8(p2)
    mg = group_mean(full * p18)
    mc = group_mean(full * p28)
    db2 = jnp.zeros((1, C), F32)
    for i in which:
        mean, inv = stats[i]
        for r in range(0, POS, CHUNK):
            nh = (h1[l, i, r : r + CHUNK, :] - mean) * inv
            dh = inv * (full[i : i + 1] * dn[i, r : r + CHUNK, :] - mg[i : i + 1] - nh * mc[i : i + 1])
            put_shifted(bufs, i, r, dh)
            if want:
                db2 = db2 + colsum(dh)
    if want:
        modgain = rows8(gains)
        dma = row(3) * p28 + row(4) * p18
        dm = jnp.concatenate([dma[0:4], p18[0:4]], axis=0)
        sgrad[l, 2:3, :] = db2
        sgrad[l, 3:4, :] = colsum(modgain * p28)
        sgrad[l, 4:5, :] = colsum(modgain * p18)
        sgrad[l, 5:6, :] = colsum(dma)
        sgrad[l, 6:7, :] = colsum(p18)
        grad[l, R_EMB : R_EMB + 4 * C, :] = lax.dot_general(
            eot[...], dm, (((1,), (0,)), ((), ())),
            precision=lax.Precision.HIGHEST, preferred_element_type=F32,
        ).astype(BF16)
    dn[...] = conv_input_grad(bufs, w, l, R_CONV1).reshape(images, POS, C)

    stats = stat(S_M1)
    p1, p2 = [], []
    for i in which:
        mean, inv = stats[i]
        s1 = jnp.zeros((1, C), F32)
        s2 = jnp.zeros((1, C), F32)
        for r in range(0, POS, CHUNK):
            nh = (xs[l, i, r : r + CHUNK, :] - mean) * inv
            pre = nh * row(0) + row(1)
            s, slope = silu_parts(pre)
            d = dn[i, r : r + CHUNK, :] * slope
            dn[i, r : r + CHUNK, :] = d
            s1 = s1 + colsum(d)
            s2 = s2 + colsum(d * nh)
            if want:
                nbuf[i, r : r + CHUNK, :] = (pre * s).astype(BF16)
        p1.append(s1)
        p2.append(s2)
    if want:
        act_t[...] = nbuf[...].reshape(flat, C).T
        conv_weight_grad(act_t, bufs, grad, l, R_CONV1)
    c1, c2 = rows8(p1), rows8(p2)
    mg = group_mean(row(0) * c1)
    mc = group_mean(row(0) * c2)
    for i in which:
        mean, inv = stats[i]
        for r in range(0, POS, CHUNK):
            nh = (xs[l, i, r : r + CHUNK, :] - mean) * inv
            dx = inv * (row(0) * dn[i, r : r + CHUNK, :] - mg[i : i + 1] - nh * mc[i : i + 1])
            g[i, r : r + CHUNK, :] = g[i, r : r + CHUNK, :] + dx
    if want:
        sgrad[l, 0:1, :] = colsum(c2)
        sgrad[l, 1:2, :] = colsum(c1)


def saved_shapes(images):
    return [
        jax.ShapeDtypeStruct((3, images, POS, C), F32),
        jax.ShapeDtypeStruct((2, images, POS, C), F32),
        jax.ShapeDtypeStruct((2, images, POS, C), F32),
        jax.ShapeDtypeStruct((2, images, POS, 3 * C), BF16),
        jax.ShapeDtypeStruct((2, images, POS, POS), BF16),
        jax.ShapeDtypeStruct((2, images, POS, C), BF16),
        jax.ShapeDtypeStruct((2, images, 8, C), F32),
    ]


def forward_kernel(staged, x0, w, small, eo, xs, h1, y, qkv, att, o, st, bufs, nbuf, qkvw, tmp):
    clear_pads(bufs)
    xs[0] = x0[...]

    def body(l, _):
        layer_forward(
            l, w, small, eo, xs, h1, y, qkv, att, o, st, bufs, nbuf, qkvw, tmp, staged
        )
        return 0

    lax.fori_loop(0, 2, body, 0)


def backward_kernel(want, *refs):
    cot, w, small, eot, xs, h1, y, qkv, att, o, st, g = refs[:12]
    refs = refs[12:]
    if want:
        grad, sgrad = refs[:2]
        refs = refs[2:]
    else:
        grad, sgrad = None, None
    bufs, nbuf, qkvw, tmp, dn, dqkv, act_t = refs
    clear_pads(bufs)
    g[...] = cot[...]
    if want:
        sgrad[...] = jnp.zeros(sgrad.shape, F32)

    def body(k, _):
        layer_backward(
            1 - k, w, small, eot, xs, h1, y, qkv, att, o, st, g, bufs, nbuf, qkvw, tmp, dn,
            dqkv, act_t, grad, sgrad,
        )
        return 0

    lax.fori_loop(0, 2, body, 0)


def vm(n):
    return [pl.BlockSpec(memory_space=pltpu.VMEM)] * n


def scratch_forward(images):
    return [
        pltpu.VMEM((3, images, POS + 2 * PAD, C), BF16),
        pltpu.VMEM((images, POS, C), BF16),
        pltpu.VMEM((C, 3 * C), BF16),
        pltpu.VMEM((2, 3 * C, HALF), F32),
    ]


def run_forward(x0, w, small, eo, staged=False):
    images = x0.shape[0]
    return pl.pallas_call(
        functools.partial(forward_kernel, staged),
        out_shape=saved_shapes(images),
        in_specs=vm(4),
        out_specs=vm(7),
        scratch_shapes=scratch_forward(images),
        compiler_params=pltpu.CompilerParams(vmem_limit_bytes=VMEM_LIMIT),
    )(x0, w, small, eo)


def run_backward(cot, w, small, eot, saved, want):
    images = cot.shape[0]
    outs = [jax.ShapeDtypeStruct(cot.shape, F32)]
    if want:
        outs += [
            jax.ShapeDtypeStruct((2, ROWS, C), BF16),
            jax.ShapeDtypeStruct((2, 16, C), F32),
        ]
    return pl.pallas_call(
        functools.partial(backward_kernel, want),
        out_shape=outs,
        in_specs=vm(11),
        out_specs=vm(len(outs)),
        scratch_shapes=scratch_forward(images)
        + [
            pltpu.VMEM((images, POS, C), F32),
            pltpu.VMEM((images, POS, 3 * C), BF16),
            pltpu.VMEM((C, images * POS), BF16),
        ],
        compiler_params=pltpu.CompilerParams(vmem_limit_bytes=VMEM_LIMIT),
    )(cot, w, small, eot, *saved)


PLANES, PLANE = 4, 4
MESH = pl.DeviceIdType.MESH


class Place:
    def __init__(self):
        self.sec = lax.axis_index("section")
        self.d = lax.axis_index("dp")
        self.x = lax.rem(self.d, 2)
        self.y = lax.rem(self.d // 2, 2)
        self.z = self.d // PLANE
        self.sib = {"section": 1 - self.sec}
        self.xn = {"dp": self.d + 1 - 2 * self.x}
        self.yn = {"dp": self.d + 2 - 4 * self.y}

    def plane(self, j):
        return lax.rem(self.z + j + PLANES, PLANES)

    def zpeer(self, j):
        return {"dp": self.plane(j) * PLANE + lax.rem(self.d, PLANE)}

    def meet(self):
        barrier = pltpu.get_barrier_semaphore()
        others = [self.sib, self.xn, self.yn] + [self.zpeer(j) for j in (1, 2, 3)]
        for other in others:
            pl.semaphore_signal(barrier, inc=1, device_id=other, device_id_type=MESH)
        pl.semaphore_wait(barrier, len(others))


def remote(src, dst, send, recv, target):
    return pltpu.make_async_remote_copy(
        src_ref=src, dst_ref=dst, send_sem=send, recv_sem=recv,
        device_id=target, device_id_type=MESH,
    )


Z1, X1, Y1, X2, Y2, S_OWN, S_X, S_Y, S_DA, S_DB = 0, 3, 7, 11, 15, 19, 23, 27, 31, 35
SLOTS = 39


def gather_kernel(*refs):
    nets = (len(refs) - 4) // 2
    ws, outs = refs[:nets], refs[nets : 2 * nets]
    stage, local_sem, send_sem, recv_sem = refs[2 * nets :]
    part = stage.shape[1]
    half = part // 2
    me = Place()
    for n in range(nets):
        stage[n] = ws[n][...].astype(BF16)
    me.meet()

    def rows(plane, y, x, lo, count):
        at = me.sec * ROWS + (plane * PLANE + y * 2 + x) * part + lo
        return pl.ds(pl.multiple_of(at, 16), count)

    sends = []

    def send(n, slot, where, target, src=None):
        piece = outs[n].at[where]
        copy = remote(
            piece if src is None else src, piece, send_sem.at[n, slot], recv_sem.at[n, slot], target
        )
        copy.start()
        sends.append(copy)

    def arrived(n, slot, where):
        piece = outs[n].at[where]
        remote(piece, piece, send_sem.at[n, slot], recv_sem.at[n, slot], me.sib).wait_recv()

    def own(j):
        return rows(me.plane(-j), me.y, me.x, 0, part)

    def begin(n):
        for j in (1, 2, 3):
            send(n, Z1 + j - 1, own(0), me.zpeer(j), stage.at[n])
        for slot, target in ((X1, me.xn), (Y1, me.yn), (S_OWN, me.sib)):
            send(n, slot, own(0), target, stage.at[n])
        copy = pltpu.make_async_copy(stage.at[n], outs[n].at[own(0)], local_sem.at[n])
        copy.start()
        return copy

    def phase1(n):
        for j in (1, 2, 3):
            arrived(n, Z1 + j - 1, own(j))
            for slot, target in ((X1, me.xn), (Y1, me.yn), (S_OWN, me.sib)):
                send(n, slot + j, own(j), target)

    def phase2(n):
        for j in range(PLANES):
            plane = me.plane(-j)
            arrived(n, X1 + j, rows(plane, me.y, 1 - me.x, 0, part))
            send(n, Y2 + j, rows(plane, me.y, 1 - me.x, 0, half), me.yn)
            send(n, S_X + j, rows(plane, me.y, 1 - me.x, 0, part), me.sib)
            arrived(n, Y1 + j, rows(plane, 1 - me.y, me.x, 0, part))
            send(n, X2 + j, rows(plane, 1 - me.y, me.x, half, half), me.xn)
            send(n, S_Y + j, rows(plane, 1 - me.y, me.x, 0, part), me.sib)

    def phase3(n):
        for j in range(PLANES):
            plane = me.plane(-j)
            for slot, to, lo in ((Y2, S_DA, 0), (X2, S_DB, half)):
                where = rows(plane, 1 - me.y, 1 - me.x, lo, half)
                arrived(n, slot + j, where)
                send(n, to + j, where, me.sib)

    def finish(n):
        for slot in range(S_OWN, SLOTS):
            arrived(n, slot, pl.ds(0, part if slot < S_DA else half))

    locals_ = [begin(n) for n in range(nets)]
    phase1(0)
    phase2(0)
    for n in range(1, nets):
        phase1(n)
        phase3(n - 1)
        phase2(n)
    phase3(nets - 1)
    for n in range(nets):
        finish(n)
    for copy in locals_:
        copy.wait()
    for copy in sends:
        copy.wait_send()


def gather_nets(*ws):
    part = ws[0].shape[0]
    nets = len(ws)
    outs = pl.pallas_call(
        gather_kernel,
        out_shape=[jax.ShapeDtypeStruct((2 * ROWS, C), BF16)] * nets,
        in_specs=vm(nets),
        out_specs=[pl.BlockSpec(memory_space=pl.ANY)] * nets,
        scratch_shapes=[
            pltpu.VMEM((nets, part, C), BF16),
            pltpu.SemaphoreType.DMA((nets,)),
            pltpu.SemaphoreType.DMA((nets, SLOTS)),
            pltpu.SemaphoreType.DMA((nets, SLOTS)),
        ],
        compiler_params=pltpu.CompilerParams(
            collective_id=0, has_side_effects=True, vmem_limit_bytes=VMEM_LIMIT
        ),
    )(*ws)
    return [a.reshape(2, ROWS, C) for a in outs]


A_SLOT, B_SLOT, C_SLOT, D_SLOT = 0, 4, 20, 28
R_SLOTS = 31


def reduce_kernel(*refs):
    nets = 2
    gb, sg = refs[:nets], refs[nets]
    shard, stot, sqtot = refs[nets + 1 : nets + 4]
    own, sib, rb, rc, rd, sbuf, srecv, qbuf, qrecv, lsem, ssem, rsem, tsem, urem = refs[nets + 4 :]
    part = shard.shape[1]
    half = part // 2
    span = PLANE * part
    me = Place()
    me.meet()
    sends = []

    def send(src, dst, s, r, target):
        copy = remote(src, dst, s, r, target)
        copy.start()
        sends.append(copy)

    def arrived(dst, s, r):
        remote(dst, dst, s, r, me.sib).wait_recv()

    def zt(k):
        return me.plane(1 + k)

    def block(base, k):
        return pl.ds(pl.multiple_of(base + zt(k) * span, 16), span)

    def piece(k, y, x, lo, count):
        at = (zt(k) * PLANE + y * 2 + x) * part + lo
        return pl.ds(pl.multiple_of(at, 16), count)

    loads = {}
    for n in range(nets):
        for k in range(PLANES):
            there, here = block((1 - me.sec) * ROWS, k), block(me.sec * ROWS, k)
            slot = A_SLOT + k
            send(
                gb[n].at[there], sib.at[n, block(0, k)], ssem.at[n, slot], rsem.at[n, slot], me.sib
            )
            copy = pltpu.make_async_copy(gb[n].at[here], own.at[n, block(0, k)], lsem.at[n, k])
            copy.start()
            loads[n, k] = copy

    def totals(buf, recv, sem_s, sem_r, base, first):
        steps = ((0, me.sib), (1, me.xn), (2, me.yn))
        for slot, target in steps:
            if slot == 0 and first is not None:
                src = first
            else:
                src = buf.at[slot]
            send(src, recv.at[slot], sem_s.at[base + slot], sem_r.at[base + slot], target)
            arrived(recv.at[slot], sem_s.at[base + slot], sem_r.at[base + slot])
            buf[slot + 1] = buf[slot] + recv[slot]
        recv[3 + me.z] = buf[3]
        for j in (1, 2, 3):
            at = base + 2 + j
            send(buf.at[3], recv.at[3 + me.z], sem_s.at[at], sem_r.at[at], me.zpeer(j))
        for j in (1, 2, 3):
            at = base + 2 + j
            arrived(recv.at[3 + me.plane(-j)], sem_s.at[at], sem_r.at[at])
        return (recv[3] + recv[4]) + (recv[5] + recv[6])

    def add_rows(dst, src, n_rows, step):
        def body(i, _):
            r = pl.multiple_of(i * step, 16)
            a, at = dst(r, step)
            b, bt = src(r, step)
            a[at] = (a[at].astype(F32) + b[bt].astype(F32)).astype(BF16)
            return 0

        lax.fori_loop(0, n_rows // step, body, 0)

    def stage_a(n, k):
        slot = A_SLOT + k
        loads[n, k].wait()
        arrived(sib.at[n, block(0, k)], ssem.at[n, slot], rsem.at[n, slot])
        base = zt(k) * span
        step = part

        def at(ref):
            return lambda r, c: (ref, (n, pl.ds(pl.multiple_of(base + r, 16), c), slice(None)))

        add_rows(at(own), at(sib), span, step)
        for j in range(2):
            slot = B_SLOT + 4 * k + j
            send(
                own.at[n, piece(k, 1 - me.y, j, 0, half)], rb.at[n, k, j],
                ssem.at[n, slot], rsem.at[n, slot], me.yn,
            )
            slot = B_SLOT + 4 * k + 2 + j
            send(
                own.at[n, piece(k, j, 1 - me.x, half, half)], rb.at[n, k, 2 + j],
                ssem.at[n, slot], rsem.at[n, slot], me.xn,
            )

    def join(n, where, recv_ref, at):
        own[(n, where, slice(None))] = (
            own[(n, where, slice(None))].astype(F32) + recv_ref[at].astype(F32)
        ).astype(BF16)

    def stage_c(n, k):
        for j in range(4):
            slot = B_SLOT + 4 * k + j
            arrived(rb.at[n, k, j], ssem.at[n, slot], rsem.at[n, slot])
            where = piece(k, me.y, j, 0, half) if j < 2 else piece(k, j - 2, me.x, half, half)
            join(n, where, rb, (n, k, j))
        slot = C_SLOT + 2 * k
        send(
            own.at[n, piece(k, me.y, 1 - me.x, 0, half)], rc.at[n, k, 0],
            ssem.at[n, slot], rsem.at[n, slot], me.xn,
        )
        slot += 1
        send(
            own.at[n, piece(k, 1 - me.y, me.x, half, half)], rc.at[n, k, 1],
            ssem.at[n, slot], rsem.at[n, slot], me.yn,
        )

    def stage_d(n, k):
        for j in range(2):
            slot = C_SLOT + 2 * k + j
            arrived(rc.at[n, k, j], ssem.at[n, slot], rsem.at[n, slot])
            where = piece(k, me.y, me.x, j * half, half)
            if k < PLANES - 1:
                join(n, where, rc, (n, k, j))
            else:
                shard[n, j * half : (j + 1) * half, :] = (
                    own[(n, where, slice(None))].astype(F32) + rc[n, k, j].astype(F32)
                )
        if k < PLANES - 1:
            slot = D_SLOT + k
            send(
                own.at[n, piece(k, me.y, me.x, 0, part)], rd.at[n, k],
                ssem.at[n, slot], rsem.at[n, slot], me.zpeer(1 + k),
            )

    def stage_e(n):
        for k in range(PLANES - 1):
            slot = D_SLOT + k
            arrived(rd.at[n, k], ssem.at[n, slot], rsem.at[n, slot])
        shard[n] = (
            shard[n] + rd[n, 0].astype(F32) + (rd[n, 1].astype(F32) + rd[n, 2].astype(F32))
        )

    order = [(n, k) for n in range(nets) for k in range(PLANES)]
    lag_c, lag_d = 1, 2
    for t in range(len(order) + lag_d):
        if t < len(order):
            stage_a(*order[t])
        if 0 <= t - lag_c < len(order):
            stage_c(*order[t - lag_c])
        if 0 <= t - lag_d < len(order):
            stage_d(*order[t - lag_d])
    sbuf[0] = sg[me.sec]
    stot[...] = totals(sbuf, srecv, tsem, urem, 0, sg.at[1 - me.sec])
    for n in range(nets):
        stage_e(n)
    lane = lax.broadcasted_iota(jnp.int32, (8, HALF), 1)
    tile = jnp.zeros((8, HALF), F32)
    for n in range(nets):
        big = jnp.sum(shard[n] * shard[n])
        low = jnp.sum(stot[16 * n : 16 * n + 13, :] * stot[16 * n : 16 * n + 13, :])
        tile = jnp.where(lane == n, big + jnp.where(me.d == 0, low, 0.0), tile)
    qbuf[0] = tile
    sqtot[...] = totals(qbuf, qrecv, tsem, urem, 6, None)
    for copy in sends:
        copy.wait_send()


def reduce_nets(bigs, small, part):
    nets = len(bigs)
    half = part // 2
    return pl.pallas_call(
        reduce_kernel,
        out_shape=[
            jax.ShapeDtypeStruct((nets, part, C), F32),
            jax.ShapeDtypeStruct(small.shape[1:], F32),
            jax.ShapeDtypeStruct((8, HALF), F32),
        ],
        in_specs=[pl.BlockSpec(memory_space=pl.ANY)] * nets + vm(1),
        out_specs=vm(3),
        scratch_shapes=[
            pltpu.VMEM((nets, ROWS, C), BF16),
            pltpu.VMEM((nets, ROWS, C), BF16),
            pltpu.VMEM((nets, PLANES, 4, half, C), BF16),
            pltpu.VMEM((nets, PLANES, 2, half, C), BF16),
            pltpu.VMEM((nets, PLANES - 1, part, C), BF16),
            pltpu.VMEM((4,) + small.shape[1:], F32),
            pltpu.VMEM((7,) + small.shape[1:], F32),
            pltpu.VMEM((4, 8, HALF), F32),
            pltpu.VMEM((7, 8, HALF), F32),
            pltpu.SemaphoreType.DMA((nets, PLANES)),
            pltpu.SemaphoreType.DMA((nets, R_SLOTS)),
            pltpu.SemaphoreType.DMA((nets, R_SLOTS)),
            pltpu.SemaphoreType.DMA((12,)),
            pltpu.SemaphoreType.DMA((12,)),
        ],
        compiler_params=pltpu.CompilerParams(
            collective_id=1, has_side_effects=True, vmem_limit_bytes=VMEM_LIMIT
        ),
    )(*[b.reshape(2 * ROWS, C) for b in bigs], small)


def adam_step(master, first_mom, second_mom, grad):
    first_new = BETA_ONE * first_mom + (1.0 - BETA_ONE) * grad
    second_new = BETA_TWO * second_mom + (1.0 - BETA_TWO) * grad * grad
    direction = (
        first_new
        / (1.0 - BETA_ONE**STEP)
        / (jnp.sqrt(second_new / (1.0 - BETA_TWO**STEP)) + ADAM_EPS)
    )
    return (master - LEARN_RATE * (direction + WEIGHT_DECAY * master), first_new, second_new)


EMA_RATE = 0.5 ** (20.0 / STEP)
SMALL_STATES = (4, 5, 6, 7, 11, 12, 13)


def update_kernel(shard, stot, sqtot, *refs):
    ins, outs = refs[:14], refs[14:]
    nums = outs[14]
    count = stot[15:16, 0:1]
    sq = sqtot[0:1, :]
    lane = lax.broadcasted_iota(jnp.int32, sq.shape, 1)
    total = jnp.zeros_like(sq)
    scales = []
    for n in range(2):
        norm = jnp.sqrt(jnp.sum(jnp.where(lane == n, sq, 0.0), axis=1, keepdims=True)) / count
        scales.append(jnp.minimum(1.0, CLIP_NORM / norm) / count)
        total = jnp.where(lane == n, norm, total)
        total = jnp.where(lane == 2 + n, stot[13 + n : 14 + n, 0:1] / count, total)
    nums[...] = jnp.broadcast_to(total, nums.shape)

    def one(at, grad, w, m, v, ema, ow, om, ov, oe):
        new, first, second = adam_step(w[at], m[at], v[at], grad)
        ow[at] = new
        om[at] = first
        ov[at] = second
        if ema is not None:
            oe[at] = EMA_RATE * ema[at] + (1.0 - EMA_RATE) * new

    one(0, shard[0] * scales[0], *ins[0:4], *outs[0:4])
    one(0, shard[1] * scales[1], *ins[8:11], None, *outs[8:11], None)
    for k in range(13):
        one(k, stot[k : k + 1, :] * scales[0], *ins[4:8], *outs[4:8])
        one(k, stot[16 + k : 17 + k, :] * scales[1], *ins[11:14], None, *outs[11:14], None)


def update_nets(shard, stot, sqtot, states):
    def turned(arrays):
        return [a.swapaxes(0, 1) if k in SMALL_STATES else a for k, a in enumerate(arrays)]

    states = turned(states)
    res = pl.pallas_call(
        update_kernel,
        out_shape=[jax.ShapeDtypeStruct(a.shape, F32) for a in states]
        + [jax.ShapeDtypeStruct((8, HALF), F32)],
        in_specs=vm(3 + len(states)),
        out_specs=vm(len(states) + 1),
        compiler_params=pltpu.CompilerParams(vmem_limit_bytes=VMEM_LIMIT),
    )(shard, stot, sqtot, *states)
    nums = res[-1]
    return tuple(turned(res[:-1])) + (nums[0, 0:2], nums[0, 2:4])


def gather_plain(shard):
    rows = lax.all_gather(shard.astype(BF16), "dp", axis=1, tiled=True)
    return lax.all_gather(rows, "section", axis=0, tiled=True)


def reduce_plain(bigs, small):
    shards_, squares = [], []
    own = lax.psum_scatter(small, "section", scatter_dimension=0, tiled=True)
    stot = lax.psum(own, "dp")[0]
    first = lax.axis_index("dp") == 0
    for n, big in enumerate(bigs):
        own = lax.psum_scatter(big, "section", scatter_dimension=0, tiled=True)
        own = lax.psum_scatter(own, "dp", scatter_dimension=1, tiled=True)[0].astype(F32)
        shards_.append(own)
        low = jnp.sum(jnp.square(stot[16 * n : 16 * n + 13]))
        squares.append(jnp.sum(own * own) + jnp.where(first, low, 0.0))
    sq = lax.psum(jnp.stack(squares), ("section", "dp"))
    return jnp.stack(shards_), stot, jnp.zeros((8, HALF), F32).at[:, 0:2].set(sq)


def shards(
    z_noise, eps_noise, levels, counts,
    gen_w, gen_m, gen_v, gen_ema, gen_small, gen_small_m, gen_small_v, gen_small_ema,
    fake_w, fake_m, fake_v, fake_small, fake_small_m, fake_small_v,
    teacher_w, teacher_small,
):
    section_idx = lax.axis_index("section")
    sections = lax.axis_size("section")
    custom = lax.axis_size("dp") == PLANES * PLANE
    per_group = z_noise.shape[0]
    images = per_group // sections
    start = section_idx * images
    elements = POS * C

    def mine(a):
        return lax.dynamic_slice_in_dim(a, start, images, 0)

    def wide(a):
        return a[:, None, None]

    z = mine(z_noise)
    eps = mine(eps_noise)
    local_count = counts[0]
    valid = ((start + jnp.arange(images)) < local_count).astype(F32)
    sigma = sigma_levels(mine(levels))
    s_in, s_skip, s_out, s_lam = [wide(t) for t in precondition(sigma)]
    init = jnp.full((images,), SIGMA_INIT, F32)
    g_in, g_skip, g_out, _ = [wide(t) for t in precondition(init)]
    gen_eo, score_eo = spread_embed(init), spread_embed(sigma)
    gen_eot, score_eot = gen_eo.astype(F32).T, score_eo.astype(F32).T

    smalls = lax.all_gather(
        jnp.concatenate([gen_small, fake_small, teacher_small]), "section", axis=0
    )
    gs, fs, ts = smalls[:, 0], smalls[:, 1], smalls[:, 2]
    if custom:
        gw, fw, tw = gather_nets(gen_w[0], fake_w[0], teacher_w[0])
    else:
        gw, fw, tw = gather_plain(gen_w), gather_plain(fake_w), gather_plain(teacher_w)

    raw = SIGMA_INIT * z
    gen_saved = run_forward(g_in * raw, gw, gs, gen_eo, True)
    samples = g_skip * raw + g_out * gen_saved[0][2]
    noisy = samples + wide(sigma) * eps
    x0 = s_in * noisy
    fake_saved = run_forward(x0, fw, fs, score_eo)
    fake_den = s_skip * noisy + s_out * fake_saved[0][2]
    factor = wide(valid) * s_lam / elements
    miss = fake_den - samples
    _, fake_g, fake_sg = run_backward(s_out * 2.0 * factor * miss, fw, fs, score_eot, fake_saved, True)
    teacher_saved = run_forward(x0, tw, ts, score_eo)
    teacher_den = s_skip * noisy + s_out * teacher_saved[0][2]
    gap = teacher_den - fake_den
    loss_gen = jnp.sum(factor * ((1.0 - ALPHA_MIX) * gap * gap + gap * miss))
    loss_fake = jnp.sum(factor * miss * miss)
    grad_teacher = factor * (2.0 * (1.0 - ALPHA_MIX) * gap + miss)
    grad_fake = factor * (gap - 2.0 * (1.0 - ALPHA_MIX) * gap - miss)
    direct = s_skip * (grad_teacher + grad_fake) - factor * gap
    (back_t,) = run_backward(s_out * grad_teacher, tw, ts, score_eot, teacher_saved, False)
    (back_f,) = run_backward(s_out * grad_fake, fw, fs, score_eot, fake_saved, False)
    gen_cot = g_out * (direct + s_in * (back_t + back_f))
    _, gen_g, gen_sg = run_backward(gen_cot, gw, gs, gen_eot, gen_saved, True)

    scalars = jnp.broadcast_to(jnp.stack([loss_gen, loss_fake, jnp.sum(valid)])[:, None], (3, C))
    small_sums = jnp.concatenate(
        [gen_sg[:, :13], jnp.broadcast_to(scalars, (2, 3, C)), fake_sg], axis=1
    )
    if custom:
        reduced = reduce_nets((gen_g, fake_g), small_sums, gen_w.shape[1])
    else:
        reduced = reduce_plain((gen_g, fake_g), small_sums)
    return update_nets(
        *reduced,
        (
            gen_w, gen_m, gen_v, gen_ema, gen_small, gen_small_m, gen_small_v, gen_small_ema,
            fake_w, fake_m, fake_v, fake_small, fake_small_m, fake_small_v,
        ),
    )


def solution(mesh):
    images = P("dp", None, None)
    big = P("section", "dp", None)
    small = P("section", None, None)
    return jax.shard_map(
        shards,
        mesh=mesh,
        in_specs=(images, images, P("dp"), P("dp"))
        + (big,) * 4 + (small,) * 4 + (big,) * 3 + (small,) * 3 + (big, small),
        out_specs=(big,) * 4 + (small,) * 4 + (big,) * 3 + (small,) * 3 + (P(), P()),
        check_vma=False,
    )
```

```python
import functools

import jax
import jax.numpy as jnp
from jax import lax
from jax.experimental import pallas as pl
from jax.experimental.pallas import tpu as pltpu
from jax.sharding import PartitionSpec as P

GROUPS = 32
SIDE = 16
LEVELS = 1000
STEP = 10

SIGMA_DATA = 0.5
SIGMA_INIT = 2.5
SIGMA_LOW = 0.05
SIGMA_HIGH = 20.0
RHO_POWER = 7.0
ALPHA_MIX = 1.2
RS = 0.7071067811865476
NORM_EPS = 1e-05
CLIP_NORM = 0.001
LEARN_RATE = 0.15
BETA_ONE = 0.9
BETA_TWO = 0.999
ADAM_EPS = 1e-08
WEIGHT_DECAY = 0.01

C = 256
HALF = 128
POS = 256
ROWS = 26 * C
CHUNK = 64
PAD = SIDE
F32 = jnp.float32
BF16 = jnp.bfloat16
VMEM_LIMIT = 58 * 2**20

R_CONV1, R_CONV2, R_EMB, R_QKV, R_PROJ = 0, 9 * C, 18 * C, 22 * C, 25 * C
S_M1, S_I1, S_M2, S_I2, S_M3, S_I3, S_MA, S_MB = range(8)


def sigma_levels(level_ids):
    fraction = level_ids.astype(F32) / (LEVELS - 1)
    top_root = SIGMA_HIGH ** (1.0 / RHO_POWER)
    bottom_root = SIGMA_LOW ** (1.0 / RHO_POWER)
    return (top_root + fraction * (bottom_root - top_root)) ** RHO_POWER


def precondition(sigma_vals):
    total = sigma_vals * sigma_vals + SIGMA_DATA**2
    return (
        lax.rsqrt(total),
        SIGMA_DATA**2 / total,
        sigma_vals * SIGMA_DATA * lax.rsqrt(total),
        total / (sigma_vals * sigma_vals * SIGMA_DATA**2),
    )


def noise_embed(sigma_vals, channel_count):
    frequency = (1.0 / 10000.0) ** (jnp.arange(channel_count, dtype=F32) / channel_count)
    angles = (jnp.log(sigma_vals) / 4.0)[..., None] * frequency
    return jnp.concatenate([jnp.cos(angles), jnp.sin(angles)], axis=-1)


def spread_embed(sigma_vals):
    emb = noise_embed(sigma_vals, C).astype(BF16)
    images = emb.shape[0]
    zero = jnp.zeros_like(emb)
    low = jnp.stack([emb, zero], axis=-1).reshape(images, 4 * C)
    high = jnp.stack([zero, emb], axis=-1).reshape(images, 4 * C)
    fill = jnp.zeros((4 - images, 4 * C), BF16)
    return jnp.concatenate([low, fill, high, fill], axis=0)


def dot_nn(a, b):
    return lax.dot_general(a, b, (((1,), (0,)), ((), ())), preferred_element_type=F32)


def dot_nt(a, b):
    return lax.dot_general(a, b, (((1,), (1,)), ((), ())), preferred_element_type=F32)


def dot_tn(a, b):
    return lax.dot_general(a, b, (((0,), (0,)), ((), ())), preferred_element_type=F32)


def group_mean(v):
    lane = lax.broadcasted_iota(jnp.int32, (8, C), 1)
    for sh in (1, 2, 4):
        v = v + jnp.where((lane & sh) != 0, pltpu.roll(v, sh, 1), pltpu.roll(v, C - sh, 1))
    return v * (1.0 / (POS * 8))


def colsum(v):
    return jnp.sum(v, axis=0, keepdims=True)


def no_pump(l):
    pass


FORWARD_POINTS, BACKWARD_POINTS = 10, 8


class Pump:
    def __init__(self, steps, points, layers, lo=0.0, hi=1.0):
        self.table = {l: [[] for _ in range(points)] for l in layers}
        self.at = 0
        for k, step in enumerate(steps):
            place = int((lo + (hi - lo) * (k + 0.5) / len(steps)) * points * len(layers))
            self.table[layers[place // points]][place % points].append(step)

    def __call__(self, l):
        for layer, points in self.table.items():
            if points[self.at]:

                @pl.when(l == layer)
                def _(todo=points[self.at]):
                    for step in todo:
                        step()

        self.at += 1


def put_shifted(bufs, i, r, v):
    rows = v.shape[0]
    col = lax.broadcasted_iota(jnp.int32, (rows, C), 0) & (SIDE - 1)
    at = pl.ds(PAD + r, rows)
    bufs[0, i, at, :] = jnp.where(col == 0, 0.0, pltpu.roll(v, 1, 0)).astype(BF16)
    bufs[1, i, at, :] = v.astype(BF16)
    bufs[2, i, at, :] = jnp.where(col == SIDE - 1, 0.0, pltpu.roll(v, rows - 1, 0)).astype(BF16)


def taps(bufs, flip):
    images = bufs.shape[1]
    out = []
    for dr in (-1, 0, 1):
        for dc in (-1, 0, 1):
            sr, sc = (-dr, -dc) if flip else (dr, dc)
            piece = bufs[sc + 1, :, PAD + SIDE * sr : PAD + SIDE * sr + POS, :]
            out.append(piece.reshape(images * POS, C))
    return out


def conv_forward(bufs, w, l, row):
    return dot_nn(jnp.concatenate(taps(bufs, False), axis=1), w[l, row : row + 9 * C, :])


def conv_input_grad(bufs, w, l, row):
    parts = [w[l, row + t * C : row + (t + 1) * C, :] for t in range(9)]
    return dot_nt(jnp.concatenate(taps(bufs, True), axis=1), jnp.concatenate(parts, axis=1))


def conv_weight_grad(act_t, bufs, grad, l, row):
    left = act_t[...]
    for t, piece in enumerate(taps(bufs, True)):
        grad[l, row + t * C : row + (t + 1) * C, :] = dot_nn(left, piece).astype(BF16)


def silu(v):
    h = 0.5 * v
    return h + h * jnp.tanh(h)


def silu_parts(v):
    s = 0.5 + 0.5 * jnp.tanh(0.5 * v)
    return s, s * (1.0 + v * (1.0 - s))


def clear_pads(bufs):
    zero = jnp.zeros(bufs.shape[:2] + (PAD, C), BF16)
    bufs[:, :, 0:PAD, :] = zero
    bufs[:, :, PAD + POS :, :] = zero


def split_qkv(w, l, qkvw, tmp):
    for h in range(2):
        tmp[h] = w[l, R_QKV : R_QKV + 3 * C, h * HALF : (h + 1) * HALF].astype(F32)
    for j in range(3):
        for h in range(2):
            at = j * C + h * HALF
            qkvw[:, at : at + HALF] = tmp[h, pl.ds(j, C, stride=3), :].astype(BF16)


def norm_stats(views):
    fill = [jnp.zeros((8 - len(views), C), F32)]
    sums = jnp.concatenate([colsum(x) for x in views] + fill, axis=0)
    mean = group_mean(sums)
    squares = [colsum(jnp.square(x - mean[i : i + 1])) for i, x in enumerate(views)]
    return mean, lax.rsqrt(group_mean(jnp.concatenate(squares + fill, axis=0)) + NORM_EPS)


def tap_rows(bufs, flip, which):
    out = []
    for dr in (-1, 0, 1):
        for dc in (-1, 0, 1):
            sr, sc = (-dr, -dc) if flip else (dr, dc)
            at = slice(PAD + SIDE * sr, PAD + SIDE * sr + POS)
            piece = jnp.concatenate([bufs[sc + 1, i, at, :] for i in which], axis=0)
            out.append(piece)
    return out


def layer_forward(l, w, small, eo, xs, h1, y, qkv, att, o, st, bufs, nbuf, qkvw, tmp, staged, pump):
    images = h1.shape[1]
    split_qkv(w, l, qkvw, tmp)
    mod = dot_nn(eo[...], w[l, R_EMB : R_EMB + 4 * C, :])
    ma = mod[0:4] + small[l, 5:6, :]
    mb = mod[4:8] + small[l, 6:7, :]
    for i in range(images):
        st[l, i, S_MA : S_MA + 1, :] = ma[i : i + 1]
        st[l, i, S_MB : S_MB + 1, :] = mb[i : i + 1]

    def row(k):
        return small[l, k : k + 1, :]

    def keep(which, mean, inv, at):
        for k, i in enumerate(which):
            st[l, i, at : at + 1, :] = mean[k : k + 1]
            st[l, i, at + 1 : at + 2, :] = inv[k : k + 1]

    def first(which):
        mean, inv = norm_stats([xs[l, i] for i in which])
        keep(which, mean, inv, S_M1)
        for k, i in enumerate(which):
            a = inv[k : k + 1] * row(0)
            for r in range(0, POS, CHUNK):
                v = (xs[l, i, r : r + CHUNK, :] - mean[k : k + 1]) * a + row(1)
                put_shifted(bufs, i, r, silu(v))

    def conv(which, at):
        left = jnp.concatenate(tap_rows(bufs, False, which), axis=1)
        return dot_nn(left, w[l, at : at + 9 * C, :])

    def conv_one(which):
        out = conv(which, R_CONV1) + row(2)
        for k, i in enumerate(which):
            h1[l, i] = out[k * POS : (k + 1) * POS]

    def second(which):
        mean, inv = norm_stats([h1[l, i] for i in which])
        keep(which, mean, inv, S_M2)
        for k, i in enumerate(which):
            gain = 1.0 + ma[i : i + 1]
            a = inv[k : k + 1] * row(3) * gain
            b = row(4) * gain + mb[i : i + 1]
            for r in range(0, POS, CHUNK):
                v = (h1[l, i, r : r + CHUNK, :] - mean[k : k + 1]) * a + b
                put_shifted(bufs, i, r, silu(v))

    def conv_two(which):
        out = conv(which, R_CONV2) + row(7)
        for k, i in enumerate(which):
            y[l, i] = (xs[l, i] + out[k * POS : (k + 1) * POS]) * RS

    def third(which):
        mean, inv = norm_stats([y[l, i] for i in which])
        keep(which, mean, inv, S_M3)
        for k, i in enumerate(which):
            a = inv[k : k + 1] * row(8)
            for r in range(0, POS, CHUNK):
                v = (y[l, i, r : r + CHUNK, :] - mean[k : k + 1]) * a + row(9)
                nbuf[i, r : r + CHUNK, :] = v.astype(BF16)

    def project_in(which):
        n = jnp.concatenate([nbuf[i] for i in which], axis=0)
        for j, at in ((0, 10), (1, None), (2, 11)):
            part = dot_nn(n, qkvw[:, j * C : (j + 1) * C])
            if at is not None:
                part = part + row(at)
            part = part.astype(BF16)
            for k, i in enumerate(which):
                qkv[l, i, :, j * C : (j + 1) * C] = part[k * POS : (k + 1) * POS]

    def attend(which):
        scores = [dot_nt(qkv[l, i, :, 0:C], qkv[l, i, :, C : 2 * C]) for i in which]
        for s, i in zip(scores, which):
            e = jnp.exp((s - jnp.max(s, axis=1, keepdims=True)) * (C**-0.5))
            p = (e * (1.0 / jnp.sum(e, axis=1, keepdims=True))).astype(BF16)
            att[l, i] = p
            o[l, i] = dot_nn(p, qkv[l, i, :, 2 * C :]).astype(BF16)

    def project_out(which):
        left = jnp.concatenate([o[l, i] for i in which], axis=0)
        out = dot_nn(left, w[l, R_PROJ:, :]) + row(12)
        for k, i in enumerate(which):
            xs[l + 1, i] = (y[l, i] + out[k * POS : (k + 1) * POS]) * RS

    steps = (first, conv_one, second, conv_two, third, project_in, attend, project_out)
    if not staged:
        for step in steps:
            step(range(images))
            pump(l)
    else:
        for t in range(len(steps) + images - 1):
            for i in range(images):
                if 0 <= t - i < len(steps):
                    steps[t - i]([i])
            pump(l)


def layer_backward(
    l, w, small, eot, xs, h1, y, qkv, att, o, st, g, bufs, nbuf, qkvw, tmp, dn, dqkv, act_t,
    grad, sgrad, pump,
):
    want = grad is not None
    images = h1.shape[1]
    which = range(images)
    flat = images * POS
    scale = C**-0.5
    split_qkv(w, l, qkvw, tmp)

    def row(k):
        return small[l, k : k + 1, :]

    def rows8(rows):
        return jnp.concatenate(list(rows) + [jnp.zeros((8 - len(rows), C), F32)], axis=0)

    def stat(at):
        return [(st[l, i, at : at + 1, :], st[l, i, at + 1 : at + 2, :]) for i in which]

    gp = (g[...] * RS).astype(BF16).reshape(flat, C)
    nbuf[...] = dot_nt(gp, w[l, R_PROJ:, :]).astype(BF16).reshape(images, POS, C)
    if want:
        grad[l, R_PROJ:, :] = dot_tn(o[l].reshape(flat, C), gp).astype(BF16)
        sgrad[l, 12:13, :] = colsum(gp.astype(F32))
    dps = [dot_nt(nbuf[i], qkv[l, i, :, 2 * C :]) for i in which]
    for i, dp in zip(which, dps):
        p = att[l, i]
        pf = p.astype(F32)
        ds = (pf * (dp - jnp.sum(dp * pf, axis=1, keepdims=True))).astype(BF16)
        dqkv[i, :, 0:C] = (dot_nn(ds, qkv[l, i, :, C : 2 * C]) * scale).astype(BF16)
        dqkv[i, :, C : 2 * C] = (dot_tn(ds, qkv[l, i, :, 0:C]) * scale).astype(BF16)
        dqkv[i, :, 2 * C :] = dot_tn(p, nbuf[i]).astype(BF16)
    pump(l)
    dn[...] = dot_nt(dqkv[...].reshape(flat, 3 * C), qkvw[...]).reshape(images, POS, C)
    pump(l)

    stats = stat(S_M3)
    c1 = rows8([colsum(dn[i]) for i in which])
    c2 = rows8([colsum(dn[i] * ((y[l, i] - stats[i][0]) * stats[i][1])) for i in which])
    mg = group_mean(row(8) * c1)
    mc = group_mean(row(8) * c2)
    db7 = jnp.zeros((1, C), F32)
    for i in which:
        mean, inv = stats[i]
        for r in range(0, POS, CHUNK):
            nh = (y[l, i, r : r + CHUNK, :] - mean) * inv
            gm = g[i, r : r + CHUNK, :] * RS + inv * (
                row(8) * dn[i, r : r + CHUNK, :] - mg[i : i + 1] - nh * mc[i : i + 1]
            )
            gm = gm * RS
            g[i, r : r + CHUNK, :] = gm
            put_shifted(bufs, i, r, gm)
            if want:
                nbuf[i, r : r + CHUNK, :] = (nh * row(8) + row(9)).astype(BF16)
                db7 = db7 + colsum(gm)
    pump(l)
    if want:
        sgrad[l, 7:8, :] = db7
        sgrad[l, 8:9, :] = colsum(c2)
        sgrad[l, 9:10, :] = colsum(c1)
        act_t[...] = nbuf[...].reshape(flat, C).T
        for j in range(3):
            dj = dqkv[:, :, j * C : (j + 1) * C].reshape(flat, C)
            part = dot_nn(act_t[...], dj)
            for h in range(2):
                tmp[h, pl.ds(j, C, stride=3), :] = part[:, h * HALF : (h + 1) * HALF]
            if j != 1:
                sgrad[l, 10 + j // 2 : 11 + j // 2, :] = colsum(dj.astype(F32))
        for h in range(2):
            grad[l, R_QKV : R_QKV + 3 * C, h * HALF : (h + 1) * HALF] = tmp[h].astype(BF16)
    dn[...] = conv_input_grad(bufs, w, l, R_CONV2).reshape(images, POS, C)
    pump(l)

    stats = stat(S_M2)
    gains = [1.0 + st[l, i, S_MA : S_MA + 1, :] for i in which]
    p1, p2 = [], []
    for i in which:
        mean, inv = stats[i]
        a = row(3) * gains[i]
        b = row(4) * gains[i] + st[l, i, S_MB : S_MB + 1, :]
        s1 = jnp.zeros((1, C), F32)
        s2 = jnp.zeros((1, C), F32)
        for r in range(0, POS, CHUNK):
            nh = (h1[l, i, r : r + CHUNK, :] - mean) * inv
            pre = nh * a + b
            s, slope = silu_parts(pre)
            d = dn[i, r : r + CHUNK, :] * slope
            dn[i, r : r + CHUNK, :] = d
            s1 = s1 + colsum(d)
            s2 = s2 + colsum(d * nh)
            if want:
                nbuf[i, r : r + CHUNK, :] = (pre * s).astype(BF16)
        p1.append(s1)
        p2.append(s2)
    if want:
        act_t[...] = nbuf[...].reshape(flat, C).T
        conv_weight_grad(act_t, bufs, grad, l, R_CONV2)
    pump(l)
    full = rows8([row(3) * gains[i] for i in which])
    p18, p28 = rows8(p1), rows8(p2)
    mg = group_mean(full * p18)
    mc = group_mean(full * p28)
    db2 = jnp.zeros((1, C), F32)
    for i in which:
        mean, inv = stats[i]
        for r in range(0, POS, CHUNK):
            nh = (h1[l, i, r : r + CHUNK, :] - mean) * inv
            dh = inv * (full[i : i + 1] * dn[i, r : r + CHUNK, :] - mg[i : i + 1] - nh * mc[i : i + 1])
            put_shifted(bufs, i, r, dh)
            if want:
                db2 = db2 + colsum(dh)
    pump(l)
    if want:
        modgain = rows8(gains)
        dma = row(3) * p28 + row(4) * p18
        dm = jnp.concatenate([dma[0:4], p18[0:4]], axis=0)
        sgrad[l, 2:3, :] = db2
        sgrad[l, 3:4, :] = colsum(modgain * p28)
        sgrad[l, 4:5, :] = colsum(modgain * p18)
        sgrad[l, 5:6, :] = colsum(dma)
        sgrad[l, 6:7, :] = colsum(p18)
        grad[l, R_EMB : R_EMB + 4 * C, :] = lax.dot_general(
            eot[...], dm, (((1,), (0,)), ((), ())),
            precision=lax.Precision.HIGHEST, preferred_element_type=F32,
        ).astype(BF16)
    dn[...] = conv_input_grad(bufs, w, l, R_CONV1).reshape(images, POS, C)
    pump(l)

    stats = stat(S_M1)
    p1, p2 = [], []
    for i in which:
        mean, inv = stats[i]
        s1 = jnp.zeros((1, C), F32)
        s2 = jnp.zeros((1, C), F32)
        for r in range(0, POS, CHUNK):
            nh = (xs[l, i, r : r + CHUNK, :] - mean) * inv
            pre = nh * row(0) + row(1)
            s, slope = silu_parts(pre)
            d = dn[i, r : r + CHUNK, :] * slope
            dn[i, r : r + CHUNK, :] = d
            s1 = s1 + colsum(d)
            s2 = s2 + colsum(d * nh)
            if want:
                nbuf[i, r : r + CHUNK, :] = (pre * s).astype(BF16)
        p1.append(s1)
        p2.append(s2)
    if want:
        act_t[...] = nbuf[...].reshape(flat, C).T
        conv_weight_grad(act_t, bufs, grad, l, R_CONV1)
    pump(l)
    c1, c2 = rows8(p1), rows8(p2)
    mg = group_mean(row(0) * c1)
    mc = group_mean(row(0) * c2)
    for i in which:
        mean, inv = stats[i]
        for r in range(0, POS, CHUNK):
            nh = (xs[l, i, r : r + CHUNK, :] - mean) * inv
            dx = inv * (row(0) * dn[i, r : r + CHUNK, :] - mg[i : i + 1] - nh * mc[i : i + 1])
            g[i, r : r + CHUNK, :] = g[i, r : r + CHUNK, :] + dx
    if want:
        sgrad[l, 0:1, :] = colsum(c2)
        sgrad[l, 1:2, :] = colsum(c1)


def saved_shapes(images):
    return [
        jax.ShapeDtypeStruct((3, images, POS, C), F32),
        jax.ShapeDtypeStruct((2, images, POS, C), F32),
        jax.ShapeDtypeStruct((2, images, POS, C), F32),
        jax.ShapeDtypeStruct((2, images, POS, 3 * C), BF16),
        jax.ShapeDtypeStruct((2, images, POS, POS), BF16),
        jax.ShapeDtypeStruct((2, images, POS, C), BF16),
        jax.ShapeDtypeStruct((2, images, 8, C), F32),
    ]


def forward_kernel(staged, x0, w, small, eo, xs, h1, y, qkv, att, o, st, bufs, nbuf, qkvw, tmp):
    clear_pads(bufs)
    xs[0] = x0[...]

    def body(l, _):
        layer_forward(
            l, w, small, eo, xs, h1, y, qkv, att, o, st, bufs, nbuf, qkvw, tmp, staged, no_pump
        )
        return 0

    lax.fori_loop(0, 2, body, 0)


def backward_kernel(want, *refs):
    cot, w, small, eot, xs, h1, y, qkv, att, o, st, g = refs[:12]
    refs = refs[12:]
    if want:
        grad, sgrad = refs[:2]
        refs = refs[2:]
    else:
        grad, sgrad = None, None
    bufs, nbuf, qkvw, tmp, dn, dqkv, act_t = refs
    clear_pads(bufs)
    g[...] = cot[...]
    if want:
        sgrad[...] = jnp.zeros(sgrad.shape, F32)

    def body(k, _):
        layer_backward(
            1 - k, w, small, eot, xs, h1, y, qkv, att, o, st, g, bufs, nbuf, qkvw, tmp, dn,
            dqkv, act_t, grad, sgrad, no_pump,
        )
        return 0

    lax.fori_loop(0, 2, body, 0)


def vm(n):
    return [pl.BlockSpec(memory_space=pltpu.VMEM)] * n


def scratch_forward(images):
    return [
        pltpu.VMEM((3, images, POS + 2 * PAD, C), BF16),
        pltpu.VMEM((images, POS, C), BF16),
        pltpu.VMEM((C, 3 * C), BF16),
        pltpu.VMEM((2, 3 * C, HALF), F32),
    ]


def run_forward(x0, w, small, eo, staged=False):
    images = x0.shape[0]
    return pl.pallas_call(
        functools.partial(forward_kernel, staged),
        out_shape=saved_shapes(images),
        in_specs=vm(4),
        out_specs=vm(7),
        scratch_shapes=scratch_forward(images),
        compiler_params=pltpu.CompilerParams(vmem_limit_bytes=VMEM_LIMIT),
    )(x0, w, small, eo)


def run_backward(cot, w, small, eot, saved, want):
    images = cot.shape[0]
    outs = [jax.ShapeDtypeStruct(cot.shape, F32)]
    if want:
        outs += [
            jax.ShapeDtypeStruct((2, ROWS, C), BF16),
            jax.ShapeDtypeStruct((2, 16, C), F32),
        ]
    return pl.pallas_call(
        functools.partial(backward_kernel, want),
        out_shape=outs,
        in_specs=vm(11),
        out_specs=vm(len(outs)),
        scratch_shapes=scratch_forward(images)
        + [
            pltpu.VMEM((images, POS, C), F32),
            pltpu.VMEM((images, POS, 3 * C), BF16),
            pltpu.VMEM((C, images * POS), BF16),
        ],
        compiler_params=pltpu.CompilerParams(vmem_limit_bytes=VMEM_LIMIT),
    )(cot, w, small, eot, *saved)


PLANES, PLANE = 4, 4
MESH = pl.DeviceIdType.MESH


class Place:
    def __init__(self):
        self.sec = lax.axis_index("section")
        self.d = lax.axis_index("dp")
        self.x = lax.rem(self.d, 2)
        self.y = lax.rem(self.d // 2, 2)
        self.z = self.d // PLANE
        self.sib = {"section": 1 - self.sec}
        self.xn = {"dp": self.d + 1 - 2 * self.x}
        self.yn = {"dp": self.d + 2 - 4 * self.y}

    def plane(self, j):
        return lax.rem(self.z + j + PLANES, PLANES)

    def zpeer(self, j):
        return {"dp": self.plane(j) * PLANE + lax.rem(self.d, PLANE)}

    def meet(self):
        barrier = pltpu.get_barrier_semaphore()
        others = [self.sib, self.xn, self.yn] + [self.zpeer(j) for j in (1, 2, 3)]
        for other in others:
            pl.semaphore_signal(barrier, inc=1, device_id=other, device_id_type=MESH)
        pl.semaphore_wait(barrier, len(others))


def remote(src, dst, send, recv, target):
    return pltpu.make_async_remote_copy(
        src_ref=src, dst_ref=dst, send_sem=send, recv_sem=recv,
        device_id=target, device_id_type=MESH,
    )


Z1, X1, Y1, X2, Y2, S_OWN, S_X, S_Y, S_DA, S_DB = 0, 3, 7, 11, 15, 19, 23, 27, 31, 35
SLOTS = 39


class Gather:
    def __init__(self, me, net, stage, local_sem, send_sem, recv_sem):
        self.me, self.net, self.stage = me, net, stage
        self.local_sem, self.send_sem, self.recv_sem = local_sem, send_sem, recv_sem
        self.part = stage.shape[0]
        self.half = self.part // 2

    def rows(self, plane, y, x, lo, count):
        at = (plane * PLANE + y * 2 + x) * self.part + lo
        return self.net.at[self.me.sec, pl.ds(pl.multiple_of(at, 16), count)]

    def own(self, j):
        return self.rows(self.me.plane(-j), self.me.y, self.me.x, 0, self.part)

    def send(self, slot, piece, target, src=None):
        src = piece if src is None else src
        remote(src, piece, self.send_sem.at[slot], self.recv_sem.at[slot], target).start()

    def arrived(self, slot, piece):
        remote(
            piece, piece, self.send_sem.at[slot], self.recv_sem.at[slot], self.me.sib
        ).wait_recv()

    def local(self):
        return pltpu.make_async_copy(self.stage, self.own(0), self.local_sem)

    def begin(self):
        me = self.me
        for j in (1, 2, 3):
            self.send(Z1 + j - 1, self.own(0), me.zpeer(j), self.stage)
        for slot, target in ((X1, me.xn), (Y1, me.yn), (S_OWN, me.sib)):
            self.send(slot, self.own(0), target, self.stage)
        self.local().start()

    def phase1(self):
        def step(j):
            me = self.me
            self.arrived(Z1 + j - 1, self.own(j))
            for slot, target in ((X1, me.xn), (Y1, me.yn), (S_OWN, me.sib)):
                self.send(slot + j, self.own(j), target)

        return [lambda j=j: step(j) for j in (1, 2, 3)]

    def phase2(self):
        me, part, half = self.me, self.part, self.half

        def step_x(j):
            plane = me.plane(-j)
            self.arrived(X1 + j, self.rows(plane, me.y, 1 - me.x, 0, part))
            self.send(Y2 + j, self.rows(plane, me.y, 1 - me.x, 0, half), me.yn)
            self.send(S_X + j, self.rows(plane, me.y, 1 - me.x, 0, part), me.sib)

        def step_y(j):
            plane = me.plane(-j)
            self.arrived(Y1 + j, self.rows(plane, 1 - me.y, me.x, 0, part))
            self.send(X2 + j, self.rows(plane, 1 - me.y, me.x, half, half), me.xn)
            self.send(S_Y + j, self.rows(plane, 1 - me.y, me.x, 0, part), me.sib)

        return [lambda f=f, j=j: f(j) for j in range(PLANES) for f in (step_x, step_y)]

    def phase3(self):
        def step(j, slot, to, lo):
            me = self.me
            where = self.rows(me.plane(-j), 1 - me.y, 1 - me.x, lo, self.half)
            self.arrived(slot + j, where)
            self.send(to + j, where, me.sib)

        return [
            lambda j=j, a=a: step(j, *a)
            for j in range(PLANES)
            for a in ((Y2, S_DA, 0), (X2, S_DB, self.half))
        ]

    def finish(self):
        def step():
            for slot in range(S_OWN, SLOTS):
                count = self.part if slot < S_DA else self.half
                self.arrived(slot, self.rows(0, 0, 0, 0, count))
            self.local().wait()

        return [step]

    def drain(self):
        for slot in range(SLOTS):
            whole = slot < X2 or S_OWN <= slot < S_DA
            piece = self.rows(0, 0, 0, 0, self.part if whole else self.half)
            remote(
                piece, piece, self.send_sem.at[slot], self.recv_sem.at[slot], self.me.sib
            ).wait_send()


A_SLOT, B_SLOT, C_SLOT, D_SLOT = 0, 4, 20, 28
R_SLOTS = 31


class Reduce:
    def __init__(self, me, big, shard, sib, rb, rc, rd, ssem, rsem):
        self.me, self.big, self.shard = me, big, shard
        self.sib, self.rb, self.rc, self.rd = sib, rb, rc, rd
        self.ssem, self.rsem = ssem, rsem
        self.part = shard.shape[0]
        self.half = self.part // 2
        self.span = PLANE * self.part

    def zt(self, k):
        return self.me.plane(1 + k)

    def block(self, k):
        return pl.ds(pl.multiple_of(self.zt(k) * self.span, 16), self.span)

    def piece(self, k, y, x, lo, count):
        at = (self.zt(k) * PLANE + y * 2 + x) * self.part + lo
        return pl.ds(pl.multiple_of(at, 16), count)

    def send(self, src, dst, slot, target):
        remote(src, dst, self.ssem.at[slot], self.rsem.at[slot], target).start()

    def arrived(self, dst, slot):
        remote(dst, dst, self.ssem.at[slot], self.rsem.at[slot], self.me.sib).wait_recv()

    def begin(self):
        for k in range(PLANES):
            at = self.block(k)
            self.send(self.big.at[1 - self.me.sec, at], self.sib.at[at], A_SLOT + k, self.me.sib)

    def stage_a(self, k):
        me, half = self.me, self.half
        self.arrived(self.sib.at[self.block(k)], A_SLOT + k)
        base = self.zt(k) * self.span

        def body(i, _):
            at = pl.ds(pl.multiple_of(base + i * half, 16), half)
            self.big[me.sec, at, :] = (
                self.big[me.sec, at, :].astype(F32) + self.sib[at, :].astype(F32)
            ).astype(BF16)
            return 0

        lax.fori_loop(0, 2 * PLANE, body, 0)
        for j in range(2):
            self.send(
                self.big.at[me.sec, self.piece(k, 1 - me.y, j, 0, half)], self.rb.at[k, j],
                B_SLOT + 4 * k + j, me.yn,
            )
            self.send(
                self.big.at[me.sec, self.piece(k, j, 1 - me.x, half, half)], self.rb.at[k, 2 + j],
                B_SLOT + 4 * k + 2 + j, me.xn,
            )

    def join(self, where, other):
        self.big[self.me.sec, where, :] = (
            self.big[self.me.sec, where, :].astype(F32) + other.astype(F32)
        ).astype(BF16)

    def stage_c(self, k):
        me, half = self.me, self.half
        for j in range(4):
            self.arrived(self.rb.at[k, j], B_SLOT + 4 * k + j)
            y, x, lo = (me.y, j, 0) if j < 2 else (j - 2, me.x, half)
            self.join(self.piece(k, y, x, lo, half), self.rb[k, j])
        self.send(
            self.big.at[me.sec, self.piece(k, me.y, 1 - me.x, 0, half)], self.rc.at[k, 0],
            C_SLOT + 2 * k, me.xn,
        )
        self.send(
            self.big.at[me.sec, self.piece(k, 1 - me.y, me.x, half, half)], self.rc.at[k, 1],
            C_SLOT + 2 * k + 1, me.yn,
        )

    def stage_d(self, k):
        me, half = self.me, self.half
        for j in range(2):
            self.arrived(self.rc.at[k, j], C_SLOT + 2 * k + j)
            where = self.piece(k, me.y, me.x, j * half, half)
            if k < PLANES - 1:
                self.join(where, self.rc[k, j])
            else:
                self.shard[j * half : (j + 1) * half, :] = (
                    self.big[me.sec, where, :].astype(F32) + self.rc[k, j].astype(F32)
                )
        if k < PLANES - 1:
            self.send(
                self.big.at[me.sec, self.piece(k, me.y, me.x, 0, self.part)], self.rd.at[k],
                D_SLOT + k, me.zpeer(1 + k),
            )

    def stage_e(self):
        for k in range(PLANES - 1):
            self.arrived(self.rd.at[k], D_SLOT + k)
        self.shard[...] = (
            self.shard[...]
            + self.rd[0].astype(F32) + (self.rd[1].astype(F32) + self.rd[2].astype(F32))
        )

    def steps(self):
        out = []
        for t in range(PLANES + 2):
            for stage, lag in ((self.stage_a, 0), (self.stage_c, 1), (self.stage_d, 2)):
                if 0 <= t - lag < PLANES:
                    out.append(lambda stage=stage, k=t - lag: stage(k))
        return out + [self.stage_e]

    def drain(self):
        for slot in range(R_SLOTS):
            if slot < B_SLOT:
                piece = self.sib.at[pl.ds(0, self.span)]
            elif slot < D_SLOT:
                piece = self.rb.at[0, 0]
            else:
                piece = self.rd.at[0]
            remote(piece, piece, self.ssem.at[slot], self.rsem.at[slot], self.me.sib).wait_send()


def reduce_scratch(part):
    half = part // 2
    return [
        pltpu.VMEM((ROWS, C), BF16),
        pltpu.VMEM((PLANES, 4, half, C), BF16),
        pltpu.VMEM((PLANES, 2, half, C), BF16),
        pltpu.VMEM((PLANES - 1, part, C), BF16),
        pltpu.SemaphoreType.DMA((R_SLOTS,)),
        pltpu.SemaphoreType.DMA((R_SLOTS,)),
    ]


class Totals:
    def __init__(self, me, buf, recv, ssem, rsem):
        self.me, self.buf, self.recv, self.ssem, self.rsem = me, buf, recv, ssem, rsem

    def send(self, src, dst, slot, target):
        remote(src, dst, self.ssem.at[slot], self.rsem.at[slot], target).start()

    def arrived(self, dst, slot):
        remote(dst, dst, self.ssem.at[slot], self.rsem.at[slot], self.me.sib).wait_recv()

    def begin(self, first):
        self.send(first, self.recv.at[0], 0, self.me.sib)

    def steps(self):
        me, buf, recv = self.me, self.buf, self.recv

        def one():
            self.arrived(recv.at[0], 0)
            buf[1] = buf[0] + recv[0]
            self.send(buf.at[1], recv.at[1], 1, me.xn)

        def two():
            self.arrived(recv.at[1], 1)
            buf[2] = buf[1] + recv[1]
            self.send(buf.at[2], recv.at[2], 2, me.yn)

        def three():
            self.arrived(recv.at[2], 2)
            buf[3] = buf[2] + recv[2]
            recv[3 + me.z] = buf[3]
            for j in (1, 2, 3):
                self.send(buf.at[3], recv.at[3 + me.z], 2 + j, me.zpeer(j))

        return [one, two, three]

    def result(self):
        for j in (1, 2, 3):
            self.arrived(self.recv.at[3 + self.me.plane(-j)], 2 + j)
        return (self.recv[3] + self.recv[4]) + (self.recv[5] + self.recv[6])

    def drain(self):
        for slot in range(6):
            piece = self.recv.at[0]
            remote(piece, piece, self.ssem.at[slot], self.rsem.at[slot], self.me.sib).wait_send()


def totals_scratch(shape):
    return [
        pltpu.VMEM((4,) + shape, F32),
        pltpu.VMEM((7,) + shape, F32),
        pltpu.SemaphoreType.DMA((6,)),
        pltpu.SemaphoreType.DMA((6,)),
    ]


def saved_scratch(images):
    return [pltpu.VMEM(a.shape, a.dtype) for a in saved_shapes(images)]


def backward_scratch(images):
    return scratch_forward(images) + [
        pltpu.VMEM((images, POS, C), F32),
        pltpu.VMEM((images, POS, 3 * C), BF16),
        pltpu.VMEM((C, images * POS), BF16),
    ]


GEN_TOTAL = SIGMA_INIT**2 + SIGMA_DATA**2
GEN_IN = GEN_TOTAL**-0.5
GEN_SKIP = SIGMA_DATA**2 / GEN_TOTAL
GEN_OUT = SIGMA_INIT * SIGMA_DATA * GEN_TOTAL**-0.5
T_IN, T_SKIP, T_OUT, T_SIGMA, T_FACTOR = range(5)


def score_kernel(*refs):
    (
        z_all, eps_all, gen_w, fake_w, teacher_w, smalls, gen_eo, score_eo, score_eot, tab,
        gw_out, sv_x, sv_h, sv_y, sv_q, sv_a, sv_o, sv_s, gen_cot, fshard, fsg, sums,
        *refs,
    ) = refs
    gen_out = (sv_x, sv_h, sv_y, sv_q, sv_a, sv_o, sv_s)
    w_gen, w_fake, w_teach = refs[:3]
    sv_one, sv_two = refs[3:10], refs[10:17]
    bufs, nbuf, qkvw, tmp, dn, dqkv, act_t = refs[17:24]
    zb, eb, g, stage, local_sem, send_sem, recv_sem, copy_sem = refs[24:32]
    sib, rb, rc, rd, ssem, rsem = refs[32:38]
    images = zb.shape[0]
    me = Place()
    start = me.sec * images

    def mine(ref):
        return ref.at[pl.ds(start, images)]

    loads = [
        pltpu.make_async_copy(mine(z_all), zb, copy_sem.at[0]),
        pltpu.make_async_copy(mine(eps_all), eb, copy_sem.at[1]),
    ]
    for copy in loads:
        copy.start()
    for n, w in enumerate((gen_w, fake_w, teacher_w)):
        stage[n] = w[...].astype(BF16)
    clear_pads(bufs)
    gathers = [
        Gather(me, net, stage.at[n], local_sem.at[n], send_sem.at[n], recv_sem.at[n])
        for n, net in enumerate((w_gen, w_fake, w_teach))
    ]
    me.meet()
    for gather in gathers:
        gather.begin()

    def run(steps):
        for step in steps:
            step()

    def forward(n, w, eo, sv, pump):
        def body(l, _):
            layer_forward(
                l, w, smalls.at[n], eo, *sv, bufs, nbuf, qkvw, tmp, True, pump
            )
            return 0

        lax.fori_loop(0, 2, body, 0)

    def backward(n, w, sv, cot, grad, sgrad, pump):
        def body(k, _):
            layer_backward(
                1 - k, w, smalls.at[n], score_eot, *sv, cot, bufs, nbuf, qkvw, tmp, dn, dqkv,
                act_t, grad, sgrad, pump,
            )
            return 0

        lax.fori_loop(0, 2, body, 0)

    def each(f):
        def body(i, carry):
            return f(i, [tab[start + i, k] for k in range(5)], carry)

        return lax.fori_loop(0, images, body, jnp.zeros((1, C), F32))

    run(gathers[0].phase1() + gathers[0].phase2() + gathers[1].phase1() + gathers[0].phase3())
    for copy in loads:
        copy.wait()
    sv_one[0][0] = zb[...] * (GEN_IN * SIGMA_INIT)
    run(gathers[0].finish())
    later = gathers[1].phase2()
    forward(0, w_gen, gen_eo, sv_one, Pump(later[:5], FORWARD_POINTS, (0, 1)))
    stores = [pltpu.make_async_copy(w_gen, gw_out, copy_sem.at[2])]
    for k, (src, dst) in enumerate(zip(sv_one, gen_out)):
        stores.append(pltpu.make_async_copy(src, dst, copy_sem.at[3 + k]))
    for copy in stores:
        copy.start()

    def noisy(i, t, carry):
        zb[i] = zb[i] * (GEN_SKIP * SIGMA_INIT) + GEN_OUT * sv_one[0][2, i]
        eb[i] = zb[i] + t[T_SIGMA] * eb[i]
        sv_two[0][0, i] = t[T_IN] * eb[i]
        return carry

    each(noisy)
    run(later[5:] + gathers[2].phase1() + gathers[1].phase3() + gathers[1].finish())
    later = gathers[2].phase2()
    forward(1, w_fake, score_eo, sv_two, Pump(later[:6], FORWARD_POINTS, (0, 1)))
    later = later[6:] + gathers[2].phase3()

    def fake_loss(i, t, total):
        den = t[T_SKIP] * eb[i] + t[T_OUT] * sv_two[0][2, i]
        sv_two[0][2, i] = den
        miss = den - zb[i]
        g[i] = (2.0 * t[T_OUT] * t[T_FACTOR]) * miss
        return total + t[T_FACTOR] * colsum(miss * miss)

    loss_fake = each(fake_loss)
    for copy in stores:
        copy.wait()
    gathers[0].drain()
    fsg[...] = jnp.zeros(fsg.shape, F32)
    backward(1, w_fake, sv_two, g, w_gen, fsg, Pump(later, BACKWARD_POINTS, (1, 0)))
    reduce = Reduce(me, w_gen, fshard, sib, rb, rc, rd, ssem, rsem)
    reduce.begin()
    run(gathers[2].finish())
    later = reduce.steps()
    sv_one[0][0] = sv_two[0][0]
    forward(2, w_teach, score_eo, sv_one, Pump(later[:5], FORWARD_POINTS, (0, 1), 0.2))

    def gen_loss(i, t, total):
        den = t[T_SKIP] * eb[i] + t[T_OUT] * sv_one[0][2, i]
        miss = sv_two[0][2, i] - zb[i]
        gap = den - sv_two[0][2, i]
        scale = t[T_OUT] * t[T_FACTOR]
        g[i] = scale * ((2.0 * (1.0 - ALPHA_MIX)) * gap + miss)
        gen_cot[i] = scale * ((1.0 - 2.0 * (1.0 - ALPHA_MIX)) * gap - miss)
        zb[i] = (t[T_FACTOR] * (t[T_SKIP] - 1.0)) * gap
        return total + t[T_FACTOR] * colsum(gap * ((1.0 - ALPHA_MIX) * gap + miss))

    loss_gen = each(gen_loss)
    backward(2, w_teach, sv_one, g, None, None, Pump(later[5:9], BACKWARD_POINTS, (1, 0)))
    backward(1, w_fake, sv_two, gen_cot, None, None, Pump(later[9:], BACKWARD_POINTS, (1, 0)))

    def gen_gradient(i, t, carry):
        gen_cot[i] = GEN_OUT * (zb[i] + t[T_IN] * (g[i] + gen_cot[i]))
        return carry

    each(gen_gradient)
    sums[...] = jnp.concatenate(
        [
            jnp.broadcast_to(jnp.sum(total, axis=1, keepdims=True), (1, C))
            for total in (loss_gen, loss_fake)
        ]
        + [jnp.zeros((6, C), F32)],
        axis=0,
    )
    for gather in gathers[1:]:
        gather.drain()
    reduce.drain()


def run_score(z, eps, gen_w, fake_w, teacher_w, smalls, gen_eo, score_eo, score_eot, tab):
    part = gen_w.shape[0]
    images = z.shape[0] // 2
    any_ = pl.BlockSpec(memory_space=pl.ANY)
    saved = saved_shapes(images)
    return pl.pallas_call(
        score_kernel,
        out_shape=[jax.ShapeDtypeStruct((2, ROWS, C), BF16)]
        + saved
        + [
            jax.ShapeDtypeStruct((images, POS, C), F32),
            jax.ShapeDtypeStruct((part, C), F32),
            jax.ShapeDtypeStruct((2, 16, C), F32),
            jax.ShapeDtypeStruct((8, C), F32),
        ],
        in_specs=[any_] * 2 + vm(7) + [pl.BlockSpec(memory_space=pltpu.SMEM)],
        out_specs=[any_] * 8 + vm(4),
        scratch_shapes=[pltpu.VMEM((2, ROWS, C), BF16)] * 3
        + saved_scratch(images) * 2
        + backward_scratch(images)
        + [pltpu.VMEM((images, POS, C), F32)] * 3
        + [
            pltpu.VMEM((3, part, C), BF16),
            pltpu.SemaphoreType.DMA((3,)),
            pltpu.SemaphoreType.DMA((3, SLOTS)),
            pltpu.SemaphoreType.DMA((3, SLOTS)),
            pltpu.SemaphoreType.DMA((10,)),
        ]
        + reduce_scratch(part),
        compiler_params=pltpu.CompilerParams(
            collective_id=0, has_side_effects=True, vmem_limit_bytes=VMEM_LIMIT
        ),
    )(z, eps, gen_w, fake_w, teacher_w, smalls, gen_eo, score_eo, score_eot, tab)


def gen_kernel(*refs):
    (
        cot, w, small, eot, xs, h1, y, qkv, att, o, st, fsg, sums, fshard,
        shard, stot, sqtot,
        big, g, bufs, nbuf, qkvw, tmp, dn, dqkv, act_t, *refs,
    ) = refs
    sib, rb, rc, rd, ssem, rsem = refs[:6]
    small_refs, square_refs = refs[6:10], refs[10:14]
    sgrad, part_sums = refs[14:16]
    me = Place()
    me.meet()
    clear_pads(bufs)
    g[...] = cot[...]
    sgrad[...] = jnp.zeros(sgrad.shape, F32)
    reduce = Reduce(me, big, shard, sib, rb, rc, rd, ssem, rsem)

    def body(k, _):
        layer_backward(
            1 - k, w, small, eot, xs, h1, y, qkv, att, o, st, g, bufs, nbuf, qkvw, tmp, dn, dqkv,
            act_t, big, sgrad, no_pump,
        )
        return 0

    lax.fori_loop(0, 2, body, 0)
    reduce.begin()
    for s in range(2):
        part_sums[s, 0:16, :] = sgrad[s]
        part_sums[s, 13:16, :] = sums[0:3, :]
        part_sums[s, 16:32, :] = fsg[s]
    small = Totals(me, *small_refs)
    small_refs[0][0] = part_sums[me.sec]
    small.begin(part_sums.at[1 - me.sec])
    steps = reduce.steps()
    for k, step in enumerate(steps):
        step()
        if k in (3, 5, 7):
            small.steps()[(k - 3) // 2]()
    stot[...] = small.result()
    lane = lax.broadcasted_iota(jnp.int32, (8, HALF), 1)
    tile = jnp.zeros((8, HALF), F32)
    for n, own in enumerate((shard, fshard)):
        big_sum = jnp.sum(own[...] * own[...])
        low = jnp.sum(stot[16 * n : 16 * n + 13, :] * stot[16 * n : 16 * n + 13, :])
        tile = jnp.where(lane == n, big_sum + jnp.where(me.d == 0, low, 0.0), tile)
    square = Totals(me, *square_refs)
    square_refs[0][0] = tile
    square.begin(square_refs[0].at[0])
    for step in square.steps():
        step()
    sqtot[...] = square.result()
    reduce.drain()
    small.drain()
    square.drain()


def run_gen(cot, w, small, eot, saved, fsg, sums, fshard):
    images = cot.shape[0]
    part = fshard.shape[0]
    return pl.pallas_call(
        gen_kernel,
        out_shape=[
            jax.ShapeDtypeStruct((part, C), F32),
            jax.ShapeDtypeStruct((32, C), F32),
            jax.ShapeDtypeStruct((8, HALF), F32),
        ],
        in_specs=vm(14),
        out_specs=vm(3),
        scratch_shapes=[pltpu.VMEM((2, ROWS, C), BF16), pltpu.VMEM((images, POS, C), F32)]
        + backward_scratch(images)
        + reduce_scratch(part)
        + totals_scratch((32, C))
        + totals_scratch((8, HALF))
        + [pltpu.VMEM((2, 16, C), F32), pltpu.VMEM((2, 32, C), F32)],
        compiler_params=pltpu.CompilerParams(
            collective_id=1, has_side_effects=True, vmem_limit_bytes=VMEM_LIMIT
        ),
    )(cot, w, small, eot, *saved, fsg, sums, fshard)


def adam_step(master, first_mom, second_mom, grad):
    first_new = BETA_ONE * first_mom + (1.0 - BETA_ONE) * grad
    second_new = BETA_TWO * second_mom + (1.0 - BETA_TWO) * grad * grad
    direction = (
        first_new
        / (1.0 - BETA_ONE**STEP)
        / (jnp.sqrt(second_new / (1.0 - BETA_TWO**STEP)) + ADAM_EPS)
    )
    return (master - LEARN_RATE * (direction + WEIGHT_DECAY * master), first_new, second_new)


EMA_RATE = 0.5 ** (20.0 / STEP)
SMALL_STATES = (4, 5, 6, 7, 11, 12, 13)


def update_kernel(gshard, fshard, stot, sqtot, *refs):
    ins, outs = refs[:14], refs[14:]
    nums = outs[14]
    count = stot[15:16, 0:1]
    sq = sqtot[0:1, :]
    lane = lax.broadcasted_iota(jnp.int32, sq.shape, 1)
    total = jnp.zeros_like(sq)
    scales = []
    for n in range(2):
        norm = jnp.sqrt(jnp.sum(jnp.where(lane == n, sq, 0.0), axis=1, keepdims=True)) / count
        scales.append(jnp.minimum(1.0, CLIP_NORM / norm) / count)
        total = jnp.where(lane == n, norm, total)
        total = jnp.where(lane == 2 + n, stot[13 + n : 14 + n, 0:1] / count, total)
    nums[...] = jnp.broadcast_to(total, nums.shape)

    def one(at, grad, w, m, v, ema, ow, om, ov, oe):
        new, first, second = adam_step(w[at], m[at], v[at], grad)
        ow[at] = new
        om[at] = first
        ov[at] = second
        if ema is not None:
            oe[at] = EMA_RATE * ema[at] + (1.0 - EMA_RATE) * new

    one(0, gshard[...] * scales[0], *ins[0:4], *outs[0:4])
    one(0, fshard[...] * scales[1], *ins[8:11], None, *outs[8:11], None)
    for k in range(13):
        one(k, stot[k : k + 1, :] * scales[0], *ins[4:8], *outs[4:8])
        one(k, stot[16 + k : 17 + k, :] * scales[1], *ins[11:14], None, *outs[11:14], None)


def update_nets(gshard, fshard, stot, sqtot, states):
    def turned(arrays):
        return [a.swapaxes(0, 1) if k in SMALL_STATES else a for k, a in enumerate(arrays)]

    states = turned(states)
    res = pl.pallas_call(
        update_kernel,
        out_shape=[jax.ShapeDtypeStruct(a.shape, F32) for a in states]
        + [jax.ShapeDtypeStruct((8, HALF), F32)],
        in_specs=vm(4 + len(states)),
        out_specs=vm(len(states) + 1),
        compiler_params=pltpu.CompilerParams(vmem_limit_bytes=VMEM_LIMIT),
    )(gshard, fshard, stot, sqtot, *states)
    nums = res[-1]
    return tuple(turned(res[:-1])) + (nums[0, 0:2], nums[0, 2:4])


def gather_plain(shard):
    rows = lax.all_gather(shard.astype(BF16), "dp", axis=1, tiled=True)
    return lax.all_gather(rows, "section", axis=0, tiled=True)


def reduce_plain(bigs, small):
    shards_, squares = [], []
    own = lax.psum_scatter(small, "section", scatter_dimension=0, tiled=True)
    stot = lax.psum(own, "dp")[0]
    first = lax.axis_index("dp") == 0
    for n, big in enumerate(bigs):
        own = lax.psum_scatter(big, "section", scatter_dimension=0, tiled=True)
        own = lax.psum_scatter(own, "dp", scatter_dimension=1, tiled=True)[0].astype(F32)
        shards_.append(own)
        low = jnp.sum(jnp.square(stot[16 * n : 16 * n + 13]))
        squares.append(jnp.sum(own * own) + jnp.where(first, low, 0.0))
    sq = lax.psum(jnp.stack(squares), ("section", "dp"))
    return *shards_, stot, jnp.zeros((8, HALF), F32).at[:, 0:2].set(sq)


def shards(
    z_noise, eps_noise, levels, counts,
    gen_w, gen_m, gen_v, gen_ema, gen_small, gen_small_m, gen_small_v, gen_small_ema,
    fake_w, fake_m, fake_v, fake_small, fake_small_m, fake_small_v,
    teacher_w, teacher_small,
):
    section_idx = lax.axis_index("section")
    per_group = z_noise.shape[0]
    images = per_group // lax.axis_size("section")
    start = section_idx * images

    def mine(a):
        return lax.dynamic_slice_in_dim(a, start, images, 0)

    valid = (jnp.arange(per_group) < counts[0]).astype(F32)
    sigma = sigma_levels(levels)
    s_in, s_skip, s_out, s_lam = precondition(sigma)
    factor = valid * s_lam / (POS * C)
    tab = jnp.stack([s_in, s_skip, s_out, sigma, factor] + [jnp.zeros_like(sigma)] * 3, axis=1)
    gen_eo = spread_embed(jnp.full((images,), SIGMA_INIT, F32))
    score_eo = spread_embed(mine(sigma))
    gen_eot, score_eot = gen_eo.astype(F32).T, score_eo.astype(F32).T
    smalls = lax.all_gather(
        jnp.concatenate([gen_small, fake_small, teacher_small]), "section", axis=1
    )
    valid_sum = jnp.sum(mine(valid))
    if lax.axis_size("dp") == PLANES * PLANE:
        gw, *saved, gen_cot, fshard, fsg, sums = run_score(
            z_noise, eps_noise, gen_w[0], fake_w[0], teacher_w[0], smalls,
            gen_eo, score_eo, score_eot, tab,
        )
        sums = sums.at[2].set(valid_sum)
        gshard, stot, sqtot = run_gen(gen_cot, gw, smalls[0], gen_eot, saved, fsg, sums, fshard)
        reduced = (gshard, fshard, stot, sqtot)
    else:
        reduced = plain_step(
            mine(z_noise), mine(eps_noise), gen_w, fake_w, teacher_w, smalls,
            gen_eo, gen_eot, score_eo, score_eot, mine(tab), valid_sum,
        )
    return update_nets(
        *reduced,
        (
            gen_w, gen_m, gen_v, gen_ema, gen_small, gen_small_m, gen_small_v, gen_small_ema,
            fake_w, fake_m, fake_v, fake_small, fake_small_m, fake_small_v,
        ),
    )


def plain_step(
    z, eps, gen_w, fake_w, teacher_w, smalls, gen_eo, gen_eot, score_eo, score_eot, tab, valid_sum
):
    gs, fs, ts = smalls[0], smalls[1], smalls[2]
    gw, fw, tw = gather_plain(gen_w), gather_plain(fake_w), gather_plain(teacher_w)
    s_in, s_skip, s_out, sigma, factor = [tab[:, k, None, None] for k in range(5)]
    raw = SIGMA_INIT * z
    gen_saved = run_forward(GEN_IN * raw, gw, gs, gen_eo)
    samples = GEN_SKIP * raw + GEN_OUT * gen_saved[0][2]
    noisy = samples + sigma * eps
    x0 = s_in * noisy
    fake_saved = run_forward(x0, fw, fs, score_eo)
    fake_den = s_skip * noisy + s_out * fake_saved[0][2]
    miss = fake_den - samples
    _, fake_g, fake_sg = run_backward(
        s_out * 2.0 * factor * miss, fw, fs, score_eot, fake_saved, True
    )
    teacher_saved = run_forward(x0, tw, ts, score_eo)
    teacher_den = s_skip * noisy + s_out * teacher_saved[0][2]
    gap = teacher_den - fake_den
    loss_gen = jnp.sum(factor * ((1.0 - ALPHA_MIX) * gap * gap + gap * miss))
    loss_fake = jnp.sum(factor * miss * miss)
    grad_teacher = factor * (2.0 * (1.0 - ALPHA_MIX) * gap + miss)
    grad_fake = factor * gap - grad_teacher
    direct = factor * gap * (s_skip - 1.0)
    (back_t,) = run_backward(s_out * grad_teacher, tw, ts, score_eot, teacher_saved, False)
    (back_f,) = run_backward(s_out * grad_fake, fw, fs, score_eot, fake_saved, False)
    gen_cot = GEN_OUT * (direct + s_in * (back_t + back_f))
    _, gen_g, gen_sg = run_backward(gen_cot, gw, gs, gen_eot, gen_saved, True)
    scalars = jnp.broadcast_to(jnp.stack([loss_gen, loss_fake, valid_sum])[:, None], (3, C))
    small_sums = jnp.concatenate(
        [gen_sg[:, :13], jnp.broadcast_to(scalars, (2, 3, C)), fake_sg], axis=1
    )
    return reduce_plain((gen_g, fake_g), small_sums)


def solution(mesh):
    images = P("dp", None, None)
    big = P("section", "dp", None)
    small = P("section", None, None)
    return jax.shard_map(
        shards,
        mesh=mesh,
        in_specs=(images, images, P("dp"), P("dp"))
        + (big,) * 4 + (small,) * 4 + (big,) * 3 + (small,) * 3 + (big, small),
        out_specs=(big,) * 4 + (small,) * 4 + (big,) * 3 + (small,) * 3 + (P(), P()),
        check_vma=False,
    )
```

```python
import functools

import jax
import jax.numpy as jnp
from jax import lax
from jax.experimental import pallas as pl
from jax.experimental.pallas import tpu as pltpu
from jax.sharding import PartitionSpec as P

GROUPS = 32
SIDE = 16
LEVELS = 1000
STEP = 10

SIGMA_DATA = 0.5
SIGMA_INIT = 2.5
SIGMA_LOW = 0.05
SIGMA_HIGH = 20.0
RHO_POWER = 7.0
ALPHA_MIX = 1.2
RS = 0.7071067811865476
NORM_EPS = 1e-05
CLIP_NORM = 0.001
LEARN_RATE = 0.15
BETA_ONE = 0.9
BETA_TWO = 0.999
ADAM_EPS = 1e-08
WEIGHT_DECAY = 0.01

C = 256
HALF = 128
POS = 256
ROWS = 26 * C
CHUNK = 64
PAD = SIDE
F32 = jnp.float32
BF16 = jnp.bfloat16
VMEM_LIMIT = 58 * 2**20
STEP_LIMIT = 63 * 2**20

R_CONV1, R_CONV2, R_EMB, R_QKV, R_PROJ = 0, 9 * C, 18 * C, 22 * C, 25 * C
S_M1, S_I1, S_M2, S_I2, S_M3, S_I3, S_MA, S_MB = range(8)


def sigma_levels(level_ids):
    fraction = level_ids.astype(F32) / (LEVELS - 1)
    top_root = SIGMA_HIGH ** (1.0 / RHO_POWER)
    bottom_root = SIGMA_LOW ** (1.0 / RHO_POWER)
    return (top_root + fraction * (bottom_root - top_root)) ** RHO_POWER


def precondition(sigma_vals):
    total = sigma_vals * sigma_vals + SIGMA_DATA**2
    return (
        lax.rsqrt(total),
        SIGMA_DATA**2 / total,
        sigma_vals * SIGMA_DATA * lax.rsqrt(total),
        total / (sigma_vals * sigma_vals * SIGMA_DATA**2),
    )


def noise_embed(sigma_vals, channel_count):
    frequency = (1.0 / 10000.0) ** (jnp.arange(channel_count, dtype=F32) / channel_count)
    angles = (jnp.log(sigma_vals) / 4.0)[..., None] * frequency
    return jnp.concatenate([jnp.cos(angles), jnp.sin(angles)], axis=-1)


def spread_embed(sigma_vals):
    emb = noise_embed(sigma_vals, C).astype(BF16)
    images = emb.shape[0]
    zero = jnp.zeros_like(emb)
    low = jnp.stack([emb, zero], axis=-1).reshape(images, 4 * C)
    high = jnp.stack([zero, emb], axis=-1).reshape(images, 4 * C)
    fill = jnp.zeros((4 - images, 4 * C), BF16)
    return jnp.concatenate([low, fill, high, fill], axis=0)


def dot_nn(a, b):
    return lax.dot_general(a, b, (((1,), (0,)), ((), ())), preferred_element_type=F32)


def dot_nt(a, b):
    return lax.dot_general(a, b, (((1,), (1,)), ((), ())), preferred_element_type=F32)


def dot_tn(a, b):
    return lax.dot_general(a, b, (((0,), (0,)), ((), ())), preferred_element_type=F32)


def group_mean(v):
    lane = lax.broadcasted_iota(jnp.int32, (8, C), 1)
    for sh in (1, 2, 4):
        v = v + jnp.where((lane & sh) != 0, pltpu.roll(v, sh, 1), pltpu.roll(v, C - sh, 1))
    return v * (1.0 / (POS * 8))


def colsum(v):
    return jnp.sum(v, axis=0, keepdims=True)


def no_pump(l):
    pass


FORWARD_POINTS, BACKWARD_POINTS = 10, 8


class Pump:
    def __init__(self, steps, points, layers, lo=0.0, hi=1.0):
        self.table = {l: [[] for _ in range(points)] for l in layers}
        self.at = 0
        for k, step in enumerate(steps):
            place = int((lo + (hi - lo) * (k + 0.5) / len(steps)) * points * len(layers))
            self.table[layers[place // points]][place % points].append(step)

    def __call__(self, l):
        for layer, points in self.table.items():
            if points[self.at]:

                @pl.when(l == layer)
                def _(todo=points[self.at]):
                    for step in todo:
                        step()

        self.at += 1


def put_shifted(bufs, i, r, v):
    rows = v.shape[0]
    col = lax.broadcasted_iota(jnp.int32, (rows, C), 0) & (SIDE - 1)
    at = pl.ds(PAD + r, rows)
    bufs[0, i, at, :] = jnp.where(col == 0, 0.0, pltpu.roll(v, 1, 0)).astype(BF16)
    bufs[1, i, at, :] = v.astype(BF16)
    bufs[2, i, at, :] = jnp.where(col == SIDE - 1, 0.0, pltpu.roll(v, rows - 1, 0)).astype(BF16)


def taps(bufs, flip):
    images = bufs.shape[1]
    out = []
    for dr in (-1, 0, 1):
        for dc in (-1, 0, 1):
            sr, sc = (-dr, -dc) if flip else (dr, dc)
            piece = bufs[sc + 1, :, PAD + SIDE * sr : PAD + SIDE * sr + POS, :]
            out.append(piece.reshape(images * POS, C))
    return out


def conv_forward(bufs, w, l, row):
    return dot_nn(jnp.concatenate(taps(bufs, False), axis=1), w[l, row : row + 9 * C, :])


def conv_input_grad(bufs, w, l, row):
    parts = [w[l, row + t * C : row + (t + 1) * C, :] for t in range(9)]
    return dot_nt(jnp.concatenate(taps(bufs, True), axis=1), jnp.concatenate(parts, axis=1))


def conv_weight_grad(act_t, bufs, grad, l, row):
    left = act_t[...]
    for t, piece in enumerate(taps(bufs, True)):
        grad[l, row + t * C : row + (t + 1) * C, :] = dot_nn(left, piece).astype(BF16)


def silu(v):
    h = 0.5 * v
    return h + h * jnp.tanh(h)


def silu_parts(v):
    s = 0.5 + 0.5 * jnp.tanh(0.5 * v)
    return s, s * (1.0 + v * (1.0 - s))


def clear_pads(bufs):
    zero = jnp.zeros(bufs.shape[:2] + (PAD, C), BF16)
    bufs[:, :, 0:PAD, :] = zero
    bufs[:, :, PAD + POS :, :] = zero


def split_qkv(w, l, qkvw, tmp):
    for h in range(2):
        tmp[h] = w[l, R_QKV : R_QKV + 3 * C, h * HALF : (h + 1) * HALF].astype(F32)
    for j in range(3):
        for h in range(2):
            at = j * C + h * HALF
            qkvw[:, at : at + HALF] = tmp[h, pl.ds(j, C, stride=3), :].astype(BF16)


def norm_stats(views):
    fill = [jnp.zeros((8 - len(views), C), F32)]
    sums = jnp.concatenate([colsum(x) for x in views] + fill, axis=0)
    mean = group_mean(sums)
    squares = [colsum(jnp.square(x - mean[i : i + 1])) for i, x in enumerate(views)]
    return mean, lax.rsqrt(group_mean(jnp.concatenate(squares + fill, axis=0)) + NORM_EPS)


def tap_rows(bufs, flip, which):
    out = []
    for dr in (-1, 0, 1):
        for dc in (-1, 0, 1):
            sr, sc = (-dr, -dc) if flip else (dr, dc)
            at = slice(PAD + SIDE * sr, PAD + SIDE * sr + POS)
            piece = jnp.concatenate([bufs[sc + 1, i, at, :] for i in which], axis=0)
            out.append(piece)
    return out


def layer_forward(l, w, small, eo, xs, h1, y, qkv, att, o, st, bufs, nbuf, qkvw, tmp, staged, pump):
    images = h1.shape[1]
    split_qkv(w, l, qkvw, tmp)
    mod = dot_nn(eo[...], w[l, R_EMB : R_EMB + 4 * C, :])
    ma = mod[0:4] + small[l, 5:6, :]
    mb = mod[4:8] + small[l, 6:7, :]
    for i in range(images):
        st[l, i, S_MA : S_MA + 1, :] = ma[i : i + 1]
        st[l, i, S_MB : S_MB + 1, :] = mb[i : i + 1]

    def row(k):
        return small[l, k : k + 1, :]

    def keep(which, mean, inv, at):
        for k, i in enumerate(which):
            st[l, i, at : at + 1, :] = mean[k : k + 1]
            st[l, i, at + 1 : at + 2, :] = inv[k : k + 1]

    def first(which):
        mean, inv = norm_stats([xs[l, i] for i in which])
        keep(which, mean, inv, S_M1)
        for k, i in enumerate(which):
            a = inv[k : k + 1] * row(0)
            for r in range(0, POS, CHUNK):
                v = (xs[l, i, r : r + CHUNK, :] - mean[k : k + 1]) * a + row(1)
                put_shifted(bufs, i, r, silu(v))

    def conv(which, at):
        left = jnp.concatenate(tap_rows(bufs, False, which), axis=1)
        return dot_nn(left, w[l, at : at + 9 * C, :])

    def conv_one(which):
        out = conv(which, R_CONV1) + row(2)
        for k, i in enumerate(which):
            h1[l, i] = out[k * POS : (k + 1) * POS]

    def second(which):
        mean, inv = norm_stats([h1[l, i] for i in which])
        keep(which, mean, inv, S_M2)
        for k, i in enumerate(which):
            gain = 1.0 + ma[i : i + 1]
            a = inv[k : k + 1] * row(3) * gain
            b = row(4) * gain + mb[i : i + 1]
            for r in range(0, POS, CHUNK):
                v = (h1[l, i, r : r + CHUNK, :] - mean[k : k + 1]) * a + b
                put_shifted(bufs, i, r, silu(v))

    def conv_two(which):
        out = conv(which, R_CONV2) + row(7)
        for k, i in enumerate(which):
            y[l, i] = (xs[l, i] + out[k * POS : (k + 1) * POS]) * RS

    def third(which):
        mean, inv = norm_stats([y[l, i] for i in which])
        keep(which, mean, inv, S_M3)
        for k, i in enumerate(which):
            a = inv[k : k + 1] * row(8)
            for r in range(0, POS, CHUNK):
                v = (y[l, i, r : r + CHUNK, :] - mean[k : k + 1]) * a + row(9)
                nbuf[i, r : r + CHUNK, :] = v.astype(BF16)

    def project_in(which):
        n = jnp.concatenate([nbuf[i] for i in which], axis=0)
        for j, at in ((0, 10), (1, None), (2, 11)):
            part = dot_nn(n, qkvw[:, j * C : (j + 1) * C])
            if at is not None:
                part = part + row(at)
            part = part.astype(BF16)
            for k, i in enumerate(which):
                qkv[l, i, :, j * C : (j + 1) * C] = part[k * POS : (k + 1) * POS]

    def attend(which):
        scores = [dot_nt(qkv[l, i, :, 0:C], qkv[l, i, :, C : 2 * C]) for i in which]
        for s, i in zip(scores, which):
            e = jnp.exp((s - jnp.max(s, axis=1, keepdims=True)) * (C**-0.5))
            p = (e * (1.0 / jnp.sum(e, axis=1, keepdims=True))).astype(BF16)
            att[l, i] = p
            o[l, i] = dot_nn(p, qkv[l, i, :, 2 * C :]).astype(BF16)

    def project_out(which):
        left = jnp.concatenate([o[l, i] for i in which], axis=0)
        out = dot_nn(left, w[l, R_PROJ:, :]) + row(12)
        for k, i in enumerate(which):
            xs[l + 1, i] = (y[l, i] + out[k * POS : (k + 1) * POS]) * RS

    steps = (first, conv_one, second, conv_two, third, project_in, attend, project_out)
    if not staged:
        for step in steps:
            step(range(images))
            pump(l)
    else:
        for t in range(len(steps) + images - 1):
            for i in range(images):
                if 0 <= t - i < len(steps):
                    steps[t - i]([i])
            pump(l)


def layer_backward(
    l, w, small, eo, xs, h1, y, qkv, att, o, st, g, bufs, nbuf, qkvw, tmp, dn, dqkv, act_t,
    grad, sgrad, pump, need_dx=None,
):
    want = grad is not None
    images = h1.shape[1]
    which = range(images)
    flat = images * POS
    scale = C**-0.5
    split_qkv(w, l, qkvw, tmp)

    def row(k):
        return small[l, k : k + 1, :]

    def rows8(rows):
        return jnp.concatenate(list(rows) + [jnp.zeros((8 - len(rows), C), F32)], axis=0)

    def stat(at):
        return [(st[l, i, at : at + 1, :], st[l, i, at + 1 : at + 2, :]) for i in which]

    gp = (g[...] * RS).astype(BF16).reshape(flat, C)
    nbuf[...] = dot_nt(gp, w[l, R_PROJ:, :]).astype(BF16).reshape(images, POS, C)
    if want:
        grad[l, R_PROJ:, :] = dot_tn(o[l].reshape(flat, C), gp).astype(BF16)
        sgrad[l, 12:13, :] = colsum(gp.astype(F32))
    dps = [dot_nt(nbuf[i], qkv[l, i, :, 2 * C :]) for i in which]
    for i, dp in zip(which, dps):
        p = att[l, i]
        pf = p.astype(F32)
        ds = (pf * (dp - jnp.sum(dp * pf, axis=1, keepdims=True))).astype(BF16)
        dqkv[i, :, 0:C] = (dot_nn(ds, qkv[l, i, :, C : 2 * C]) * scale).astype(BF16)
        dqkv[i, :, C : 2 * C] = (dot_tn(ds, qkv[l, i, :, 0:C]) * scale).astype(BF16)
        dqkv[i, :, 2 * C :] = dot_tn(p, nbuf[i]).astype(BF16)
    pump(l)
    dn[...] = dot_nt(dqkv[...].reshape(flat, 3 * C), qkvw[...]).reshape(images, POS, C)
    pump(l)

    stats = stat(S_M3)
    c1 = rows8([colsum(dn[i]) for i in which])
    c2 = rows8([colsum(dn[i] * ((y[l, i] - stats[i][0]) * stats[i][1])) for i in which])
    mg = group_mean(row(8) * c1)
    mc = group_mean(row(8) * c2)
    db7 = jnp.zeros((1, C), F32)
    for i in which:
        mean, inv = stats[i]
        for r in range(0, POS, CHUNK):
            nh = (y[l, i, r : r + CHUNK, :] - mean) * inv
            gm = g[i, r : r + CHUNK, :] * RS + inv * (
                row(8) * dn[i, r : r + CHUNK, :] - mg[i : i + 1] - nh * mc[i : i + 1]
            )
            gm = gm * RS
            g[i, r : r + CHUNK, :] = gm
            put_shifted(bufs, i, r, gm)
            if want:
                nbuf[i, r : r + CHUNK, :] = (nh * row(8) + row(9)).astype(BF16)
                db7 = db7 + colsum(gm)
    pump(l)
    if want:
        sgrad[l, 7:8, :] = db7
        sgrad[l, 8:9, :] = colsum(c2)
        sgrad[l, 9:10, :] = colsum(c1)
        act_t[...] = nbuf[...].reshape(flat, C).T
        for j in range(3):
            dj = dqkv[:, :, j * C : (j + 1) * C].reshape(flat, C)
            part = dot_nn(act_t[...], dj)
            for h in range(2):
                tmp[h, pl.ds(j, C, stride=3), :] = part[:, h * HALF : (h + 1) * HALF]
            if j != 1:
                sgrad[l, 10 + j // 2 : 11 + j // 2, :] = colsum(dj.astype(F32))
        for h in range(2):
            grad[l, R_QKV : R_QKV + 3 * C, h * HALF : (h + 1) * HALF] = tmp[h].astype(BF16)
    dn[...] = conv_input_grad(bufs, w, l, R_CONV2).reshape(images, POS, C)
    pump(l)

    stats = stat(S_M2)
    gains = [1.0 + st[l, i, S_MA : S_MA + 1, :] for i in which]
    p1, p2 = [], []
    for i in which:
        mean, inv = stats[i]
        a = row(3) * gains[i]
        b = row(4) * gains[i] + st[l, i, S_MB : S_MB + 1, :]
        s1 = jnp.zeros((1, C), F32)
        s2 = jnp.zeros((1, C), F32)
        for r in range(0, POS, CHUNK):
            nh = (h1[l, i, r : r + CHUNK, :] - mean) * inv
            pre = nh * a + b
            s, slope = silu_parts(pre)
            d = dn[i, r : r + CHUNK, :] * slope
            dn[i, r : r + CHUNK, :] = d
            s1 = s1 + colsum(d)
            s2 = s2 + colsum(d * nh)
            if want:
                nbuf[i, r : r + CHUNK, :] = (pre * s).astype(BF16)
        p1.append(s1)
        p2.append(s2)
    if want:
        act_t[...] = nbuf[...].reshape(flat, C).T
        conv_weight_grad(act_t, bufs, grad, l, R_CONV2)
    pump(l)
    full = rows8([row(3) * gains[i] for i in which])
    p18, p28 = rows8(p1), rows8(p2)
    mg = group_mean(full * p18)
    mc = group_mean(full * p28)
    db2 = jnp.zeros((1, C), F32)
    for i in which:
        mean, inv = stats[i]
        for r in range(0, POS, CHUNK):
            nh = (h1[l, i, r : r + CHUNK, :] - mean) * inv
            dh = inv * (full[i : i + 1] * dn[i, r : r + CHUNK, :] - mg[i : i + 1] - nh * mc[i : i + 1])
            put_shifted(bufs, i, r, dh)
            if want:
                db2 = db2 + colsum(dh)
    pump(l)
    if want:
        modgain = rows8(gains)
        dma = row(3) * p28 + row(4) * p18
        dm = jnp.concatenate([dma[0:4], p18[0:4]], axis=0)
        sgrad[l, 2:3, :] = db2
        sgrad[l, 3:4, :] = colsum(modgain * p28)
        sgrad[l, 4:5, :] = colsum(modgain * p18)
        sgrad[l, 5:6, :] = colsum(dma)
        sgrad[l, 6:7, :] = colsum(p18)
        grad[l, R_EMB : R_EMB + 4 * C, :] = lax.dot_general(
            eo[...].astype(F32), dm, (((0,), (0,)), ((), ())),
            precision=lax.Precision.HIGHEST, preferred_element_type=F32,
        ).astype(BF16)
    dn[...] = conv_input_grad(bufs, w, l, R_CONV1).reshape(images, POS, C)
    pump(l)

    stats = stat(S_M1)
    p1, p2 = [], []
    for i in which:
        mean, inv = stats[i]
        s1 = jnp.zeros((1, C), F32)
        s2 = jnp.zeros((1, C), F32)
        for r in range(0, POS, CHUNK):
            nh = (xs[l, i, r : r + CHUNK, :] - mean) * inv
            pre = nh * row(0) + row(1)
            s, slope = silu_parts(pre)
            d = dn[i, r : r + CHUNK, :] * slope
            dn[i, r : r + CHUNK, :] = d
            s1 = s1 + colsum(d)
            s2 = s2 + colsum(d * nh)
            if want:
                nbuf[i, r : r + CHUNK, :] = (pre * s).astype(BF16)
        p1.append(s1)
        p2.append(s2)
    if want:
        act_t[...] = nbuf[...].reshape(flat, C).T
        conv_weight_grad(act_t, bufs, grad, l, R_CONV1)
    pump(l)
    c1, c2 = rows8(p1), rows8(p2)

    def input_gradient():
        mg = group_mean(row(0) * c1)
        mc = group_mean(row(0) * c2)
        for i in which:
            mean, inv = stats[i]
            for r in range(0, POS, CHUNK):
                nh = (xs[l, i, r : r + CHUNK, :] - mean) * inv
                dx = inv * (row(0) * dn[i, r : r + CHUNK, :] - mg[i : i + 1] - nh * mc[i : i + 1])
                g[i, r : r + CHUNK, :] = g[i, r : r + CHUNK, :] + dx

    if want:
        pl.when(l == 1)(input_gradient)
    else:
        input_gradient()
    if want:
        sgrad[l, 0:1, :] = colsum(c2)
        sgrad[l, 1:2, :] = colsum(c1)


def saved_shapes(images):
    return [
        jax.ShapeDtypeStruct((3, images, POS, C), F32),
        jax.ShapeDtypeStruct((2, images, POS, C), F32),
        jax.ShapeDtypeStruct((2, images, POS, C), F32),
        jax.ShapeDtypeStruct((2, images, POS, 3 * C), BF16),
        jax.ShapeDtypeStruct((2, images, POS, POS), BF16),
        jax.ShapeDtypeStruct((2, images, POS, C), BF16),
        jax.ShapeDtypeStruct((2, images, 8, C), F32),
    ]


def forward_kernel(staged, x0, w, small, eo, xs, h1, y, qkv, att, o, st, bufs, nbuf, qkvw, tmp):
    clear_pads(bufs)
    xs[0] = x0[...]

    def body(l, _):
        layer_forward(
            l, w, small, eo, xs, h1, y, qkv, att, o, st, bufs, nbuf, qkvw, tmp, staged, no_pump
        )
        return 0

    lax.fori_loop(0, 2, body, 0)


def backward_kernel(want, *refs):
    cot, w, small, eo, xs, h1, y, qkv, att, o, st, g = refs[:12]
    refs = refs[12:]
    if want:
        grad, sgrad = refs[:2]
        refs = refs[2:]
    else:
        grad, sgrad = None, None
    bufs, nbuf, qkvw, tmp, dn, dqkv, act_t = refs
    clear_pads(bufs)
    g[...] = cot[...]
    if want:
        sgrad[...] = jnp.zeros(sgrad.shape, F32)

    def body(k, _):
        layer_backward(
            1 - k, w, small, eo, xs, h1, y, qkv, att, o, st, g, bufs, nbuf, qkvw, tmp, dn,
            dqkv, act_t, grad, sgrad, no_pump,
        )
        return 0

    lax.fori_loop(0, 2, body, 0)


def vm(n):
    return [pl.BlockSpec(memory_space=pltpu.VMEM)] * n


def scratch_forward(images):
    return [
        pltpu.VMEM((3, images, POS + 2 * PAD, C), BF16),
        pltpu.VMEM((images, POS, C), BF16),
        pltpu.VMEM((C, 3 * C), BF16),
        pltpu.VMEM((2, 3 * C, HALF), F32),
    ]


def run_forward(x0, w, small, eo, staged=False):
    images = x0.shape[0]
    return pl.pallas_call(
        functools.partial(forward_kernel, staged),
        out_shape=saved_shapes(images),
        in_specs=vm(4),
        out_specs=vm(7),
        scratch_shapes=scratch_forward(images),
        compiler_params=pltpu.CompilerParams(vmem_limit_bytes=VMEM_LIMIT),
    )(x0, w, small, eo)


def run_backward(cot, w, small, eo, saved, want):
    images = cot.shape[0]
    outs = [jax.ShapeDtypeStruct(cot.shape, F32)]
    if want:
        outs += [
            jax.ShapeDtypeStruct((2, ROWS, C), BF16),
            jax.ShapeDtypeStruct((2, 16, C), F32),
        ]
    return pl.pallas_call(
        functools.partial(backward_kernel, want),
        out_shape=outs,
        in_specs=vm(11),
        out_specs=vm(len(outs)),
        scratch_shapes=scratch_forward(images)
        + [
            pltpu.VMEM((images, POS, C), F32),
            pltpu.VMEM((images, POS, 3 * C), BF16),
            pltpu.VMEM((C, images * POS), BF16),
        ],
        compiler_params=pltpu.CompilerParams(vmem_limit_bytes=VMEM_LIMIT),
    )(cot, w, small, eo, *saved)


PLANES, PLANE = 4, 4
MESH = pl.DeviceIdType.MESH


class Place:
    def __init__(self):
        self.sec = lax.axis_index("section")
        self.d = lax.axis_index("dp")
        self.x = lax.rem(self.d, 2)
        self.y = lax.rem(self.d // 2, 2)
        self.z = self.d // PLANE
        self.sib = {"section": 1 - self.sec}
        self.xn = {"dp": self.d + 1 - 2 * self.x}
        self.yn = {"dp": self.d + 2 - 4 * self.y}

    def plane(self, j):
        return lax.rem(self.z + j + PLANES, PLANES)

    def zpeer(self, j):
        return {"dp": self.plane(j) * PLANE + lax.rem(self.d, PLANE)}

    def meet(self):
        barrier = pltpu.get_barrier_semaphore()
        others = [self.sib, self.xn, self.yn] + [self.zpeer(j) for j in (1, 2, 3)]
        for other in others:
            pl.semaphore_signal(barrier, inc=1, device_id=other, device_id_type=MESH)
        pl.semaphore_wait(barrier, len(others))


def remote(src, dst, send, recv, target):
    return pltpu.make_async_remote_copy(
        src_ref=src, dst_ref=dst, send_sem=send, recv_sem=recv,
        device_id=target, device_id_type=MESH,
    )


Z1, X1, Y1, X2, Y2, S_OWN, S_X, S_Y, S_DA, S_DB = 0, 3, 7, 11, 15, 19, 23, 27, 31, 35
SLOTS = 39


class Gather:
    def __init__(self, me, net, stage, local_sem, send_sem, recv_sem):
        self.me, self.net, self.stage = me, net, stage
        self.local_sem, self.send_sem, self.recv_sem = local_sem, send_sem, recv_sem
        self.part = stage.shape[0]
        self.half = self.part // 2

    def rows(self, plane, y, x, lo, count):
        at = (plane * PLANE + y * 2 + x) * self.part + lo
        return self.net.at[self.me.sec, pl.ds(pl.multiple_of(at, 16), count)]

    def own(self, j):
        return self.rows(self.me.plane(-j), self.me.y, self.me.x, 0, self.part)

    def send(self, slot, piece, target, src=None):
        src = piece if src is None else src
        remote(src, piece, self.send_sem.at[slot], self.recv_sem.at[slot], target).start()

    def arrived(self, slot, piece):
        remote(
            piece, piece, self.send_sem.at[slot], self.recv_sem.at[slot], self.me.sib
        ).wait_recv()

    def local(self):
        return pltpu.make_async_copy(self.stage, self.own(0), self.local_sem)

    def begin(self):
        me = self.me
        for j in (1, 2, 3):
            self.send(Z1 + j - 1, self.own(0), me.zpeer(j), self.stage)
        for slot, target in ((X1, me.xn), (Y1, me.yn), (S_OWN, me.sib)):
            self.send(slot, self.own(0), target, self.stage)
        self.local().start()

    def phase1(self):
        def step(j):
            me = self.me
            self.arrived(Z1 + j - 1, self.own(j))
            for slot, target in ((X1, me.xn), (Y1, me.yn), (S_OWN, me.sib)):
                self.send(slot + j, self.own(j), target)

        return [lambda j=j: step(j) for j in (1, 2, 3)]

    def phase2(self):
        me, part, half = self.me, self.part, self.half

        def step_x(j):
            plane = me.plane(-j)
            self.arrived(X1 + j, self.rows(plane, me.y, 1 - me.x, 0, part))
            self.send(Y2 + j, self.rows(plane, me.y, 1 - me.x, 0, half), me.yn)
            self.send(S_X + j, self.rows(plane, me.y, 1 - me.x, 0, part), me.sib)

        def step_y(j):
            plane = me.plane(-j)
            self.arrived(Y1 + j, self.rows(plane, 1 - me.y, me.x, 0, part))
            self.send(X2 + j, self.rows(plane, 1 - me.y, me.x, half, half), me.xn)
            self.send(S_Y + j, self.rows(plane, 1 - me.y, me.x, 0, part), me.sib)

        return [lambda f=f, j=j: f(j) for j in range(PLANES) for f in (step_x, step_y)]

    def phase3(self):
        def step(j, slot, to, lo):
            me = self.me
            where = self.rows(me.plane(-j), 1 - me.y, 1 - me.x, lo, self.half)
            self.arrived(slot + j, where)
            self.send(to + j, where, me.sib)

        return [
            lambda j=j, a=a: step(j, *a)
            for j in range(PLANES)
            for a in ((Y2, S_DA, 0), (X2, S_DB, self.half))
        ]

    def finish(self):
        def step():
            for slot in range(S_OWN, SLOTS):
                count = self.part if slot < S_DA else self.half
                self.arrived(slot, self.rows(0, 0, 0, 0, count))
            self.local().wait()

        return [step]

    def drain(self):
        for slot in range(SLOTS):
            whole = slot < X2 or S_OWN <= slot < S_DA
            piece = self.rows(0, 0, 0, 0, self.part if whole else self.half)
            remote(
                piece, piece, self.send_sem.at[slot], self.recv_sem.at[slot], self.me.sib
            ).wait_send()


A_SLOT, B_SLOT, C_SLOT, D_SLOT = 0, 4, 20, 28
R_SLOTS = 31


class Reduce:
    def __init__(self, me, big, shard, sib, there, rb, rc, rd, ssem, rsem):
        self.me, self.big, self.shard = me, big, shard
        self.sib, self.there, self.rb, self.rc, self.rd = sib, there, rb, rc, rd
        self.ssem, self.rsem = ssem, rsem
        self.part = shard.shape[0]
        self.half = self.part // 2
        self.span = PLANE * self.part

    def zt(self, k):
        return PLANES - 1 - k

    def block(self, k):
        return pl.ds(self.zt(k) * self.span, self.span)

    def piece(self, k, y, x, lo, count):
        at = (self.zt(k) * PLANE + y * 2 + x) * self.part + lo
        return pl.ds(pl.multiple_of(at, 16), count)

    def send(self, src, dst, slot, target):
        remote(src, dst, self.ssem.at[slot], self.rsem.at[slot], target).start()

    def arrived(self, dst, slot):
        remote(dst, dst, self.ssem.at[slot], self.rsem.at[slot], self.me.sib).wait_recv()

    def begin(self):
        for k in range(PLANES):
            self.begin_block(k)

    def begin_block(self, k):
        at = self.block(k)
        self.send(self.big.at[1 - self.me.sec, at], self.there.at[at], A_SLOT + k, self.me.sib)

    def stage_a(self, k):
        me, half = self.me, self.half
        self.arrived(self.sib.at[self.block(k)], A_SLOT + k)
        base = self.zt(k) * self.span

        def body(i, _):
            at = pl.ds(pl.multiple_of(base + i * half, 16), half)
            self.big[me.sec, at, :] = (
                self.big[me.sec, at, :].astype(F32) + self.sib[at, :].astype(F32)
            ).astype(BF16)
            return 0

        lax.fori_loop(0, 2 * PLANE, body, 0)
        for j in range(2):
            self.send(
                self.big.at[me.sec, self.piece(k, 1 - me.y, j, 0, half)], self.rb.at[k, j],
                B_SLOT + 4 * k + j, me.yn,
            )
            self.send(
                self.big.at[me.sec, self.piece(k, j, 1 - me.x, half, half)], self.rb.at[k, 2 + j],
                B_SLOT + 4 * k + 2 + j, me.xn,
            )

    def join(self, where, other):
        self.big[self.me.sec, where, :] = (
            self.big[self.me.sec, where, :].astype(F32) + other.astype(F32)
        ).astype(BF16)

    def stage_c(self, k):
        me, half = self.me, self.half
        for j in range(4):
            self.arrived(self.rb.at[k, j], B_SLOT + 4 * k + j)
            y, x, lo = (me.y, j, 0) if j < 2 else (j - 2, me.x, half)
            self.join(self.piece(k, y, x, lo, half), self.rb[k, j])
        self.send(
            self.big.at[me.sec, self.piece(k, me.y, 1 - me.x, 0, half)], self.rc.at[k, 0],
            C_SLOT + 2 * k, me.xn,
        )
        self.send(
            self.big.at[me.sec, self.piece(k, 1 - me.y, me.x, half, half)], self.rc.at[k, 1],
            C_SLOT + 2 * k + 1, me.yn,
        )

    def stage_d(self, k):
        me, half, zt = self.me, self.half, self.zt(k)
        for j in range(2):
            self.arrived(self.rc.at[k, j], C_SLOT + 2 * k + j)
            self.join(self.piece(k, me.y, me.x, j * half, half), self.rc[k, j])

        @pl.when(me.z != zt)
        def _():
            self.send(
                self.big.at[me.sec, self.piece(k, me.y, me.x, 0, self.part)],
                self.rd.at[lax.rem(zt - me.z + PLANES, PLANES) - 1],
                D_SLOT + lax.rem(zt - me.z + PLANES, PLANES) - 1,
                {"dp": zt * PLANE + lax.rem(me.d, PLANE)},
            )

    def stage_e(self):
        for j in range(PLANES - 1):
            self.arrived(self.rd.at[j], D_SLOT + j)
        at = pl.ds(pl.multiple_of(self.me.d * self.part, 16), self.part)
        self.shard[...] = (
            self.big[self.me.sec, at, :].astype(F32)
            + self.rd[0].astype(F32) + (self.rd[1].astype(F32) + self.rd[2].astype(F32))
        )

    def steps(self):
        out = []
        for t in range(PLANES + 2):
            for stage, lag in ((self.stage_a, 0), (self.stage_c, 1), (self.stage_d, 2)):
                if 0 <= t - lag < PLANES:
                    out.append(lambda stage=stage, k=t - lag: stage(k))
        return out

    def drain(self, lo=0, hi=R_SLOTS):
        for slot in range(lo, hi):
            if slot < B_SLOT:
                piece = self.there.at[pl.ds(0, self.span)]
            elif slot < D_SLOT:
                piece = self.rb.at[0, 0]
            else:
                piece = self.rd.at[0]
            remote(piece, piece, self.ssem.at[slot], self.rsem.at[slot], self.me.sib).wait_send()


def reduce_scratch(part):
    half = part // 2
    return [
        pltpu.VMEM((PLANES, 4, half, C), BF16),
        pltpu.VMEM((PLANES, 2, half, C), BF16),
        pltpu.VMEM((PLANES - 1, part, C), BF16),
        pltpu.SemaphoreType.DMA((R_SLOTS,)),
        pltpu.SemaphoreType.DMA((R_SLOTS,)),
    ]


class Totals:
    def __init__(self, me, buf, recv, ssem, rsem):
        self.me, self.buf, self.recv, self.ssem, self.rsem = me, buf, recv, ssem, rsem

    def send(self, src, dst, slot, target):
        remote(src, dst, self.ssem.at[slot], self.rsem.at[slot], target).start()

    def arrived(self, dst, slot):
        remote(dst, dst, self.ssem.at[slot], self.rsem.at[slot], self.me.sib).wait_recv()

    def begin(self, first):
        self.send(first, self.recv.at[0], 0, self.me.sib)

    def steps(self):
        me, buf, recv = self.me, self.buf, self.recv

        def one():
            self.arrived(recv.at[0], 0)
            buf[1] = buf[0] + recv[0]
            self.send(buf.at[1], recv.at[1], 1, me.xn)

        def two():
            self.arrived(recv.at[1], 1)
            buf[2] = buf[1] + recv[1]
            self.send(buf.at[2], recv.at[2], 2, me.yn)

        def three():
            self.arrived(recv.at[2], 2)
            buf[3] = buf[2] + recv[2]
            recv[3 + me.z] = buf[3]
            for j in (1, 2, 3):
                self.send(buf.at[3], recv.at[3 + me.z], 2 + j, me.zpeer(j))

        return [one, two, three]

    def result(self):
        for j in (1, 2, 3):
            self.arrived(self.recv.at[3 + self.me.plane(-j)], 2 + j)
        return (self.recv[3] + self.recv[4]) + (self.recv[5] + self.recv[6])

    def drain(self):
        for slot in range(6):
            piece = self.recv.at[0]
            remote(piece, piece, self.ssem.at[slot], self.rsem.at[slot], self.me.sib).wait_send()


def totals_scratch(shape):
    return [
        pltpu.VMEM((4,) + shape, F32),
        pltpu.VMEM((7,) + shape, F32),
        pltpu.SemaphoreType.DMA((6,)),
        pltpu.SemaphoreType.DMA((6,)),
    ]


def saved_scratch(images):
    return [pltpu.VMEM(a.shape, a.dtype) for a in saved_shapes(images)]


def backward_scratch(images):
    return scratch_forward(images) + [
        pltpu.VMEM((images, POS, C), F32),
        pltpu.VMEM((images, POS, 3 * C), BF16),
        pltpu.VMEM((C, images * POS), BF16),
    ]


GEN_TOTAL = SIGMA_INIT**2 + SIGMA_DATA**2
GEN_IN = GEN_TOTAL**-0.5
GEN_SKIP = SIGMA_DATA**2 / GEN_TOTAL
GEN_OUT = SIGMA_INIT * SIGMA_DATA * GEN_TOTAL**-0.5
T_IN, T_SKIP, T_OUT, T_SIGMA, T_FACTOR = range(5)


def fill_embed(eo, sigmas):
    at = lax.broadcasted_iota(jnp.int32, (8, 4 * C), 1)
    side = lax.broadcasted_iota(jnp.int32, (8, 4 * C), 0) // 4
    k = at // 2
    power = (k & (C - 1)).astype(F32) * (1.0 / C)
    rows = sigmas + [jnp.ones_like(sigmas[0])] * (4 - len(sigmas))
    angle = jnp.log(jnp.concatenate(rows + rows, axis=0)) * 0.25 * jnp.exp(power * -LOG_10000)
    wave = jnp.where(k < C, jnp.cos(angle), jnp.sin(angle))
    eo[...] = jnp.where((at & 1) == side, wave, 0.0).astype(BF16)


LOG_10000 = 9.210340371976184


def step_kernel(*refs):
    (
        z_all, eps_all, levels, counts, gen_w, fake_w, teacher_w, gen_small, fake_small,
        teacher_small,
        gw_out, sv_x, sv_h, sv_y, sv_q, sv_a, sv_o, sv_s, gshard, fshard, stot, sqtot,
        *refs,
    ) = refs
    gen_out = (sv_x, sv_h, sv_y, sv_q, sv_a, sv_o, sv_s)
    w_gen, w_fake, w_teach = refs[:3]
    sv_one, sv_two = refs[3:10], refs[10:17]
    bufs, nbuf, qkvw, tmp, dn, dqkv, act_t = refs[17:24]
    zb, eb, g, stage, local_sem, send_sem, recv_sem, copy_sem = refs[24:32]
    smalls, small_sem, gen_eo, score_eo, tab, sgrads, part_sums = refs[32:39]
    fake_refs, gen_refs = refs[39:44], refs[44:49]
    small_refs, square_refs = refs[49:53], refs[53:57]
    sib, free_sem = refs[57:59]
    g2 = sv_two[0].at[2]
    images = zb.shape[0]
    me = Place()
    start = me.sec * images

    def run(steps):
        for step in steps:
            step()

    def mine(ref):
        return ref.at[pl.ds(start, images)]

    loads = [
        pltpu.make_async_copy(mine(z_all), zb, copy_sem.at[0]),
        pltpu.make_async_copy(mine(eps_all), eb, copy_sem.at[1]),
    ]
    for copy in loads:
        copy.start()
    masters = [
        pltpu.make_async_copy(src, dst, copy_sem.at[2 + k])
        for k, (src, dst) in enumerate(((gen_w, gshard), (fake_w, fshard), (teacher_w, stage.at[2])))
    ]
    for copy in masters:
        copy.start()
    smalls[...] = jnp.zeros(smalls.shape, F32)
    for n, ref in enumerate((gen_small, fake_small, teacher_small)):
        for r in range(13):
            smalls[me.sec, n, r : r + 1, :] = ref[r]
    gathers = [
        Gather(me, net, stage.at[n], local_sem.at[n], send_sem.at[n], recv_sem.at[n])
        for n, net in enumerate((w_gen, w_fake, w_teach))
    ]
    for copy in masters:
        copy.wait()
    stage[0] = gshard[...].astype(BF16)
    stage[1] = fshard[...].astype(BF16)
    me.meet()
    for gather in gathers:
        gather.begin()
    swap = remote(
        smalls.at[me.sec], smalls.at[me.sec], small_sem.at[0], small_sem.at[1], me.sib
    )
    swap.start()

    clear_pads(bufs)
    sgrads[...] = jnp.zeros(sgrads.shape, F32)
    sigmas = []
    valid_sum = jnp.zeros((1, 4 * C), F32)
    for i in range(images):
        level = jnp.zeros((1, 4 * C), jnp.int32) + levels[start + i]
        sigma = SIGMA_TOP + level.astype(F32) / (LEVELS - 1) * (SIGMA_BOTTOM - SIGMA_TOP)
        square = sigma * sigma
        sigma = square * square * square * sigma
        sigmas.append(sigma)
        s_in, s_skip, s_out, s_lam = precondition(sigma)
        valid = jnp.where(jnp.zeros_like(level) + (start + i) < counts[0], 1.0, 0.0)
        valid_sum = valid_sum + valid
        rows = (s_in, s_skip, s_out, sigma, valid * s_lam * (1.0 / (POS * C)))
        for k, value in enumerate(rows):
            tab[i, k : k + 1, :] = value[:, :C]
    fill_embed(score_eo, sigmas)
    fill_embed(gen_eo, [jnp.full((1, 4 * C), SIGMA_INIT, F32)] * images)

    def forward(n, w, eo, sv, pump):
        def body(l, _):
            layer_forward(
                l, w, smalls.at[:, n], eo, *sv, bufs, nbuf, qkvw, tmp, True, pump
            )
            return 0

        lax.fori_loop(0, 2, body, 0)

    def backward(n, w, eo, sv, cot, grad, sgrad, pump):
        def body(k, _):
            layer_backward(
                1 - k, w, smalls.at[:, n], eo, *sv, cot, bufs, nbuf, qkvw, tmp, dn, dqkv,
                act_t, grad, sgrad, pump,
            )
            return 0

        lax.fori_loop(0, 2, body, 0)

    def each(f):
        def body(i, carry):
            return f(i, [tab[i, k : k + 1, :] for k in range(5)], carry)

        return lax.fori_loop(0, images, body, jnp.zeros((1, C), F32))

    run(gathers[0].phase1() + gathers[0].phase2() + gathers[1].phase1() + gathers[0].phase3())
    for copy in loads:
        copy.wait()
    sv_one[0][0] = zb[...] * (GEN_IN * SIGMA_INIT)
    swap.wait()
    run(gathers[0].finish())
    later = gathers[1].phase2()
    forward(0, w_gen, gen_eo, sv_one, Pump(later[:5], FORWARD_POINTS, (0, 1)))
    pairs = [(w_gen, gw_out)] + list(zip(sv_one, gen_out))
    stores = [
        pltpu.make_async_copy(src, dst, copy_sem.at[2 + k]) for k, (src, dst) in enumerate(pairs)
    ]
    for copy in stores:
        copy.start()

    def noisy(i, t, carry):
        zb[i] = zb[i] * (GEN_SKIP * SIGMA_INIT) + GEN_OUT * sv_one[0][2, i]
        eb[i] = zb[i] + t[T_SIGMA] * eb[i]
        sv_two[0][0, i] = t[T_IN] * eb[i]
        return carry

    each(noisy)
    run(later[5:] + gathers[2].phase1() + gathers[1].phase3() + gathers[1].finish())
    later = gathers[2].phase2()
    forward(1, w_fake, score_eo, sv_two, Pump(later[:6], FORWARD_POINTS, (0, 1)))
    later = later[6:] + gathers[2].phase3()

    def fake_loss(i, t, total):
        den = t[T_SKIP] * eb[i] + t[T_OUT] * sv_two[0][2, i]
        sv_two[0][2, i] = den
        miss = den - zb[i]
        g[i] = (2.0 * t[T_OUT] * t[T_FACTOR]) * miss
        return total + t[T_FACTOR] * colsum(miss * miss)

    loss_fake = each(fake_loss)
    for copy in stores:
        copy.wait()
    gathers[0].drain()
    backward(
        1, w_fake, score_eo, sv_two, g, w_gen, sgrads.at[:, 1],
        Pump(later, BACKWARD_POINTS, (1, 0)),
    )
    fake_sum = Reduce(me, w_gen, fshard, sib, sib, *fake_refs)
    fake_sum.begin()
    run(gathers[2].finish())
    later = fake_sum.steps()
    sv_one[0][0] = sv_two[0][0]
    forward(2, w_teach, score_eo, sv_one, Pump(later[:5], FORWARD_POINTS, (0, 1), 0.2))

    def gen_loss(i, t, total):
        den = t[T_SKIP] * eb[i] + t[T_OUT] * sv_one[0][2, i]
        fake_den = sv_two[0][2, i]
        miss = fake_den - zb[i]
        gap = den - fake_den
        scale = t[T_OUT] * t[T_FACTOR]
        g[i] = scale * ((2.0 * (1.0 - ALPHA_MIX)) * gap + miss)
        g2[i] = scale * ((1.0 - 2.0 * (1.0 - ALPHA_MIX)) * gap - miss)
        zb[i] = (t[T_FACTOR] * (t[T_SKIP] - 1.0)) * gap
        return total + t[T_FACTOR] * colsum(gap * ((1.0 - ALPHA_MIX) * gap + miss))

    loss_gen = each(gen_loss)
    backward(
        2, w_teach, score_eo, sv_one, g, None, None, Pump(later[5:9], BACKWARD_POINTS, (1, 0))
    )
    gathers[2].drain()
    fake_sum.drain(A_SLOT, B_SLOT)
    pl.semaphore_signal(free_sem, inc=1, device_id=me.sib, device_id_type=MESH)
    back = [
        pltpu.make_async_copy(src, dst, copy_sem.at[2 + k])
        for k, (dst, src) in enumerate([(w_teach, gw_out)] + list(zip(sv_one, gen_out)))
    ]
    for copy in back:
        copy.start()
    backward(
        1, w_fake, score_eo, sv_two, g2, None, None, Pump(later[9:], BACKWARD_POINTS, (1, 0))
    )

    def gen_gradient(i, t, carry):
        g[i] = GEN_OUT * (zb[i] + t[T_IN] * (g[i] + g2[i]))
        return carry

    each(gen_gradient)
    gathers[1].drain()
    for copy in back:
        copy.wait()

    gen_sum = Reduce(me, w_fake, gshard, w_gen.at[1 - me.sec], w_gen.at[me.sec], *gen_refs)
    later = gen_sum.steps()

    def on_section(s, steps):
        pl.when(me.sec == s)(lambda: run(steps))

    def hand_over():
        pl.semaphore_wait(free_sem, 1)
        gen_sum.begin()

    first = lambda: on_section(0, [hand_over])
    beside = [first] + [lambda step=step: on_section(1, [step]) for step in later]
    pump = Pump([], BACKWARD_POINTS, (1, 0))
    points = pump.table[0]
    points[0].append(beside[0])
    for k, step in enumerate(beside[1:]):
        points[1 + k * (BACKWARD_POINTS - 1) // len(later)].append(step)
    backward(0, w_teach, gen_eo, sv_one, g, w_fake, sgrads.at[:, 0], pump)
    on_section(1, [hand_over])

    def spread_sum(total):
        return jnp.broadcast_to(jnp.sum(total, axis=1, keepdims=True), (1, C))

    sums = jnp.concatenate([spread_sum(loss_gen), spread_sum(loss_fake), valid_sum[:, :C]], axis=0)
    for s in range(2):
        part_sums[s, 0:16, :] = sgrads[s, 0]
        part_sums[s, 13:16, :] = sums
        part_sums[s, 16:32, :] = sgrads[s, 1]
    small = Totals(me, *small_refs)
    small_refs[0][0] = part_sums[me.sec]
    small.begin(part_sums.at[1 - me.sec])
    fake_sum.stage_e()
    small_steps = small.steps()
    on_section(0, later[:4])
    run(small_steps[:1])
    on_section(0, later[4:6])
    run(small_steps[1:2])
    on_section(0, later[6:8])
    run(small_steps[2:])
    on_section(0, later[8:])
    stot[...] = small.result()
    gen_sum.stage_e()
    lane = lax.broadcasted_iota(jnp.int32, (8, HALF), 1)
    tile = jnp.zeros((8, HALF), F32)
    for n, own in enumerate((gshard, fshard)):
        big_sum = jnp.sum(own[...] * own[...])
        low = jnp.sum(stot[16 * n : 16 * n + 13, :] * stot[16 * n : 16 * n + 13, :])
        tile = jnp.where(lane == n, big_sum + jnp.where(me.d == 0, low, 0.0), tile)
    square = Totals(me, *square_refs)
    square_refs[0][0] = tile
    square.begin(square_refs[0].at[0])
    run(square.steps())
    sqtot[...] = square.result()
    fake_sum.drain(B_SLOT)
    for done in (gen_sum, small, square):
        done.drain()


SIGMA_TOP = SIGMA_HIGH ** (1.0 / RHO_POWER)
SIGMA_BOTTOM = SIGMA_LOW ** (1.0 / RHO_POWER)


def run_step(z, eps, levels, counts, gen_w, fake_w, teacher_w, smalls):
    part = gen_w.shape[0]
    images = z.shape[0] // 2
    any_ = pl.BlockSpec(memory_space=pl.ANY)
    smem = pl.BlockSpec(memory_space=pltpu.SMEM)
    saved = saved_shapes(images)
    return pl.pallas_call(
        step_kernel,
        out_shape=[jax.ShapeDtypeStruct((2, ROWS, C), BF16)]
        + saved
        + [
            jax.ShapeDtypeStruct((part, C), F32),
            jax.ShapeDtypeStruct((part, C), F32),
            jax.ShapeDtypeStruct((32, C), F32),
            jax.ShapeDtypeStruct((8, HALF), F32),
        ],
        in_specs=[any_] * 2 + [smem] * 2 + [any_] * 3 + vm(3),
        out_specs=[any_] * 8 + vm(4),
        scratch_shapes=[pltpu.VMEM((2, ROWS, C), BF16)] * 3
        + saved_scratch(images) * 2
        + backward_scratch(images)
        + [pltpu.VMEM((images, POS, C), F32)] * 3
        + [
            pltpu.VMEM((3, part, C), BF16),
            pltpu.SemaphoreType.DMA((3,)),
            pltpu.SemaphoreType.DMA((3, SLOTS)),
            pltpu.SemaphoreType.DMA((3, SLOTS)),
            pltpu.SemaphoreType.DMA((10,)),
            pltpu.VMEM((2, 3, 16, C), F32),
            pltpu.SemaphoreType.DMA((2,)),
            pltpu.VMEM((8, 4 * C), BF16),
            pltpu.VMEM((8, 4 * C), BF16),
            pltpu.VMEM((images, 8, C), F32),
            pltpu.VMEM((2, 2, 16, C), F32),
            pltpu.VMEM((2, 32, C), F32),
        ]
        + reduce_scratch(part) * 2
        + totals_scratch((32, C))
        + totals_scratch((8, HALF))
        + [pltpu.VMEM((ROWS, C), BF16), pltpu.SemaphoreType.REGULAR],
        compiler_params=pltpu.CompilerParams(
            collective_id=0, has_side_effects=True, vmem_limit_bytes=STEP_LIMIT
        ),
    )(z, eps, levels, counts, gen_w, fake_w, teacher_w, *smalls)[8:]


def adam_step(master, first_mom, second_mom, grad):
    first_new = BETA_ONE * first_mom + (1.0 - BETA_ONE) * grad
    second_new = BETA_TWO * second_mom + (1.0 - BETA_TWO) * grad * grad
    direction = (
        first_new
        / (1.0 - BETA_ONE**STEP)
        / (jnp.sqrt(second_new / (1.0 - BETA_TWO**STEP)) + ADAM_EPS)
    )
    return (master - LEARN_RATE * (direction + WEIGHT_DECAY * master), first_new, second_new)


EMA_RATE = 0.5 ** (20.0 / STEP)
SMALL_STATES = (4, 5, 6, 7, 11, 12, 13)


def update_kernel(gshard, fshard, stot, sqtot, *refs):
    ins, outs = refs[:14], refs[14:]
    norms, losses = outs[14:]
    count = stot[15:16, 0:1]
    sq = sqtot[0:1, :]
    lane = lax.broadcasted_iota(jnp.int32, sq.shape, 1)
    scales = []
    for n in range(2):
        norm = jnp.sqrt(jnp.sum(jnp.where(lane == n, sq, 0.0), axis=1, keepdims=True)) / count
        scales.append(jnp.minimum(1.0, CLIP_NORM / norm) / count)
        norms[n] = norm[0, 0]
        losses[n] = (stot[13 + n : 14 + n, 0:1] / count)[0, 0]

    def one(at, grad, w, m, v, ema, ow, om, ov, oe):
        new, first, second = adam_step(w[at], m[at], v[at], grad)
        ow[at] = new
        om[at] = first
        ov[at] = second
        if ema is not None:
            oe[at] = EMA_RATE * ema[at] + (1.0 - EMA_RATE) * new

    one(0, gshard[...] * scales[0], *ins[0:4], *outs[0:4])
    one(0, fshard[...] * scales[1], *ins[8:11], None, *outs[8:11], None)
    for k in range(13):
        one(k, stot[k : k + 1, :] * scales[0], *ins[4:8], *outs[4:8])
        one(k, stot[16 + k : 17 + k, :] * scales[1], *ins[11:14], None, *outs[11:14], None)


def update_nets(gshard, fshard, stot, sqtot, states):
    def turned(arrays):
        return [a.swapaxes(0, 1) if k in SMALL_STATES else a for k, a in enumerate(arrays)]

    states = turned(states)
    res = pl.pallas_call(
        update_kernel,
        out_shape=[jax.ShapeDtypeStruct(a.shape, F32) for a in states]
        + [jax.ShapeDtypeStruct((2,), F32)] * 2,
        in_specs=vm(4 + len(states)),
        out_specs=vm(len(states)) + [pl.BlockSpec(memory_space=pltpu.SMEM)] * 2,
        compiler_params=pltpu.CompilerParams(vmem_limit_bytes=VMEM_LIMIT),
    )(gshard, fshard, stot, sqtot, *states)
    return tuple(turned(res[:-2])) + tuple(res[-2:])


def gather_plain(shard):
    rows = lax.all_gather(shard.astype(BF16), "dp", axis=1, tiled=True)
    return lax.all_gather(rows, "section", axis=0, tiled=True)


def reduce_plain(bigs, small):
    shards_, squares = [], []
    own = lax.psum_scatter(small, "section", scatter_dimension=0, tiled=True)
    stot = lax.psum(own, "dp")[0]
    first = lax.axis_index("dp") == 0
    for n, big in enumerate(bigs):
        own = lax.psum_scatter(big, "section", scatter_dimension=0, tiled=True)
        own = lax.psum_scatter(own, "dp", scatter_dimension=1, tiled=True)[0].astype(F32)
        shards_.append(own)
        low = jnp.sum(jnp.square(stot[16 * n : 16 * n + 13]))
        squares.append(jnp.sum(own * own) + jnp.where(first, low, 0.0))
    sq = lax.psum(jnp.stack(squares), ("section", "dp"))
    return *shards_, stot, jnp.zeros((8, HALF), F32).at[:, 0:2].set(sq)


def shards(
    z_noise, eps_noise, levels, counts,
    gen_w, gen_m, gen_v, gen_ema, gen_small, gen_small_m, gen_small_v, gen_small_ema,
    fake_w, fake_m, fake_v, fake_small, fake_small_m, fake_small_v,
    teacher_w, teacher_small,
):
    if lax.axis_size("dp") == PLANES * PLANE:
        smalls = [a.swapaxes(0, 1) for a in (gen_small, fake_small, teacher_small)]
        reduced = run_step(
            z_noise, eps_noise, levels, counts, gen_w[0], fake_w[0], teacher_w[0], smalls
        )
    else:
        reduced = plain_step(
            z_noise, eps_noise, levels, counts, gen_w, fake_w, teacher_w,
            gen_small, fake_small, teacher_small,
        )
    return update_nets(
        *reduced,
        (
            gen_w, gen_m, gen_v, gen_ema, gen_small, gen_small_m, gen_small_v, gen_small_ema,
            fake_w, fake_m, fake_v, fake_small, fake_small_m, fake_small_v,
        ),
    )


def plain_step(
    z_noise, eps_noise, levels, counts, gen_w, fake_w, teacher_w,
    gen_small, fake_small, teacher_small,
):
    images = z_noise.shape[0] // lax.axis_size("section")
    start = lax.axis_index("section") * images

    def mine(a):
        return lax.dynamic_slice_in_dim(a, start, images, 0)

    z, eps = mine(z_noise), mine(eps_noise)
    sigma = sigma_levels(mine(levels))
    valid = (start + jnp.arange(images) < counts[0]).astype(F32)
    valid_sum = jnp.sum(valid)
    gen_eo = spread_embed(jnp.full((images,), SIGMA_INIT, F32))
    score_eo = spread_embed(sigma)
    gs, fs, ts = [
        lax.all_gather(a, "section", axis=0, tiled=True)
        for a in (gen_small, fake_small, teacher_small)
    ]
    gw, fw, tw = gather_plain(gen_w), gather_plain(fake_w), gather_plain(teacher_w)
    s_in, s_skip, s_out, s_lam = precondition(sigma)
    factor = valid * s_lam / (POS * C)
    s_in, s_skip, s_out, sigma, factor = [
        t[:, None, None] for t in (s_in, s_skip, s_out, sigma, factor)
    ]
    raw = SIGMA_INIT * z
    gen_saved = run_forward(GEN_IN * raw, gw, gs, gen_eo)
    samples = GEN_SKIP * raw + GEN_OUT * gen_saved[0][2]
    noisy = samples + sigma * eps
    x0 = s_in * noisy
    fake_saved = run_forward(x0, fw, fs, score_eo)
    fake_den = s_skip * noisy + s_out * fake_saved[0][2]
    miss = fake_den - samples
    _, fake_g, fake_sg = run_backward(
        s_out * 2.0 * factor * miss, fw, fs, score_eo, fake_saved, True
    )
    teacher_saved = run_forward(x0, tw, ts, score_eo)
    teacher_den = s_skip * noisy + s_out * teacher_saved[0][2]
    gap = teacher_den - fake_den
    loss_gen = jnp.sum(factor * ((1.0 - ALPHA_MIX) * gap * gap + gap * miss))
    loss_fake = jnp.sum(factor * miss * miss)
    grad_teacher = factor * (2.0 * (1.0 - ALPHA_MIX) * gap + miss)
    grad_fake = factor * gap - grad_teacher
    direct = factor * gap * (s_skip - 1.0)
    (back_t,) = run_backward(s_out * grad_teacher, tw, ts, score_eo, teacher_saved, False)
    (back_f,) = run_backward(s_out * grad_fake, fw, fs, score_eo, fake_saved, False)
    gen_cot = GEN_OUT * (direct + s_in * (back_t + back_f))
    _, gen_g, gen_sg = run_backward(gen_cot, gw, gs, gen_eo, gen_saved, True)
    scalars = jnp.broadcast_to(jnp.stack([loss_gen, loss_fake, valid_sum])[:, None], (3, C))
    small_sums = jnp.concatenate(
        [gen_sg[:, :13], jnp.broadcast_to(scalars, (2, 3, C)), fake_sg], axis=1
    )
    return reduce_plain((gen_g, fake_g), small_sums)


def solution(mesh):
    images = P("dp", None, None)
    big = P("section", "dp", None)
    small = P("section", None, None)
    return jax.shard_map(
        shards,
        mesh=mesh,
        in_specs=(images, images, P("dp"), P("dp"))
        + (big,) * 4 + (small,) * 4 + (big,) * 3 + (small,) * 3 + (big, small),
        out_specs=(big,) * 4 + (small,) * 4 + (big,) * 3 + (small,) * 3 + (P(), P()),
        check_vma=False,
    )
```

```python
import functools

import jax
import jax.numpy as jnp
from jax import lax
from jax.experimental import pallas as pl
from jax.experimental.pallas import tpu as pltpu
from jax.sharding import PartitionSpec as P

GROUPS = 32
SIDE = 16
LEVELS = 1000
STEP = 10

SIGMA_DATA = 0.5
SIGMA_INIT = 2.5
SIGMA_LOW = 0.05
SIGMA_HIGH = 20.0
RHO_POWER = 7.0
ALPHA_MIX = 1.2
RS = 0.7071067811865476
NORM_EPS = 1e-05
CLIP_NORM = 0.001
LEARN_RATE = 0.15
BETA_ONE = 0.9
BETA_TWO = 0.999
ADAM_EPS = 1e-08
WEIGHT_DECAY = 0.01

C = 256
HALF = 128
POS = 256
ROWS = 26 * C
CHUNK = 64
PAD = SIDE
F32 = jnp.float32
BF16 = jnp.bfloat16
VMEM_LIMIT = 58 * 2**20
STEP_LIMIT = 63 * 2**20

R_CONV1, R_CONV2, R_EMB, R_QKV, R_PROJ = 0, 9 * C, 18 * C, 22 * C, 25 * C
S_M1, S_I1, S_M2, S_I2, S_M3, S_I3, S_MA, S_MB = range(8)


def sigma_levels(level_ids):
    fraction = level_ids.astype(F32) / (LEVELS - 1)
    top_root = SIGMA_HIGH ** (1.0 / RHO_POWER)
    bottom_root = SIGMA_LOW ** (1.0 / RHO_POWER)
    return (top_root + fraction * (bottom_root - top_root)) ** RHO_POWER


def precondition(sigma_vals):
    total = sigma_vals * sigma_vals + SIGMA_DATA**2
    return (
        lax.rsqrt(total),
        SIGMA_DATA**2 / total,
        sigma_vals * SIGMA_DATA * lax.rsqrt(total),
        total / (sigma_vals * sigma_vals * SIGMA_DATA**2),
    )


def noise_embed(sigma_vals, channel_count):
    frequency = (1.0 / 10000.0) ** (jnp.arange(channel_count, dtype=F32) / channel_count)
    angles = (jnp.log(sigma_vals) / 4.0)[..., None] * frequency
    return jnp.concatenate([jnp.cos(angles), jnp.sin(angles)], axis=-1)


def spread_embed(sigma_vals):
    emb = noise_embed(sigma_vals, C).astype(BF16)
    images = emb.shape[0]
    zero = jnp.zeros_like(emb)
    low = jnp.stack([emb, zero], axis=-1).reshape(images, 4 * C)
    high = jnp.stack([zero, emb], axis=-1).reshape(images, 4 * C)
    fill = jnp.zeros((4 - images, 4 * C), BF16)
    return jnp.concatenate([low, fill, high, fill], axis=0)


def dot_nn(a, b):
    return lax.dot_general(a, b, (((1,), (0,)), ((), ())), preferred_element_type=F32)


def dot_nt(a, b):
    return lax.dot_general(a, b, (((1,), (1,)), ((), ())), preferred_element_type=F32)


def dot_tn(a, b):
    return lax.dot_general(a, b, (((0,), (0,)), ((), ())), preferred_element_type=F32)


def group_mean(v):
    lane = lax.broadcasted_iota(jnp.int32, (8, C), 1)
    for sh in (1, 2, 4):
        v = v + jnp.where((lane & sh) != 0, pltpu.roll(v, sh, 1), pltpu.roll(v, C - sh, 1))
    return v * (1.0 / (POS * 8))


def colsum(v):
    return jnp.sum(v, axis=0, keepdims=True)


def no_pump(l):
    pass


FORWARD_POINTS, BACKWARD_POINTS, WEIGHT_POINTS = 10, 12, 15


def stagger(steps, images, between):
    for t in range(len(steps) + images - 1):
        for i in range(images):
            if 0 <= t - i < len(steps):
                steps[t - i](i)
        between()


class Pump:
    def __init__(self, steps, points, layers, lo=0.0, hi=1.0):
        self.table = {l: [[] for _ in range(points)] for l in layers}
        self.at = 0
        for k, step in enumerate(steps):
            place = int((lo + (hi - lo) * (k + 0.5) / len(steps)) * points * len(layers))
            self.table[layers[place // points]][place % points].append(step)

    def __call__(self, l):
        for layer, points in self.table.items():
            if points[self.at]:

                @pl.when(l == layer)
                def _(todo=points[self.at]):
                    for step in todo:
                        step()

        self.at += 1


def put_shifted(bufs, i, r, v):
    rows = v.shape[0]
    at = pl.ds(PAD + r, rows)
    sub = lax.broadcasted_iota(jnp.int32, (rows // SIDE, 8, C), 1)
    x = v.reshape(rows // SIDE, 2, 8, C)
    low, high = x[:, 0], x[:, 1]
    low_up, high_up = pltpu.roll(low, 1, 1), pltpu.roll(high, 1, 1)
    low_down, high_down = pltpu.roll(low, 7, 1), pltpu.roll(high, 7, 1)
    left = (jnp.where(sub == 0, 0.0, low_up), jnp.where(sub == 0, low_up, high_up))
    right = (jnp.where(sub == 7, high_down, low_down), jnp.where(sub == 7, 0.0, high_down))
    bufs[0, i, at, :] = jnp.stack(left, axis=1).reshape(rows, C).astype(BF16)
    bufs[1, i, at, :] = v.astype(BF16)
    bufs[2, i, at, :] = jnp.stack(right, axis=1).reshape(rows, C).astype(BF16)


def taps(bufs, flip):
    images = bufs.shape[1]
    out = []
    for dr in (-1, 0, 1):
        for dc in (-1, 0, 1):
            sr, sc = (-dr, -dc) if flip else (dr, dc)
            piece = bufs[sc + 1, :, PAD + SIDE * sr : PAD + SIDE * sr + POS, :]
            out.append(piece.reshape(images * POS, C))
    return out


def conv_forward(bufs, w, l, row):
    return dot_nn(jnp.concatenate(taps(bufs, False), axis=1), w[l, row : row + 9 * C, :])


def conv_input_grad(bufs, w, l, row):
    parts = [w[l, row + t * C : row + (t + 1) * C, :] for t in range(9)]
    return dot_nt(jnp.concatenate(taps(bufs, True), axis=1), jnp.concatenate(parts, axis=1))


def conv_weight_grad(act_t, bufs, grad, l, row):
    left = act_t[...]
    for t, piece in enumerate(taps(bufs, True)):
        grad[l, row + t * C : row + (t + 1) * C, :] = dot_nn(left, piece).astype(BF16)


def silu(v):
    h = 0.5 * v
    return h + h * jnp.tanh(h)


def silu_parts(v):
    s = 0.5 + 0.5 * jnp.tanh(0.5 * v)
    return s, s * (1.0 + v * (1.0 - s))


def clear_pads(bufs):
    zero = jnp.zeros(bufs.shape[:2] + (PAD, C), BF16)
    bufs[:, :, 0:PAD, :] = zero
    bufs[:, :, PAD + POS :, :] = zero


def split_qkv(w, l, qkvw, tmp):
    for h in range(2):
        tmp[h] = w[l, R_QKV : R_QKV + 3 * C, h * HALF : (h + 1) * HALF].astype(F32)
    for j in range(3):
        for h in range(2):
            at = j * C + h * HALF
            qkvw[:, at : at + HALF] = tmp[h, pl.ds(j, C, stride=3), :].astype(BF16)


def norm_sums(x, pivot=None):
    if pivot is None:
        pivot = x[0:1]
        x = x - pivot
    return colsum(x), colsum(x * x), pivot


def norm_stats(sums):
    fill = [jnp.zeros((8 - len(sums), C), F32)]
    s1, s2, pivot = [jnp.concatenate([a[k] for a in sums] + fill, axis=0) for k in range(3)]
    centre = s1 * (1.0 / POS)
    channel = pivot + centre
    mean = group_mean(channel * POS)
    spread = jnp.maximum(s2 - s1 * centre, 0.0) + jnp.square(channel - mean) * POS
    return mean, lax.rsqrt(group_mean(spread) + NORM_EPS)


def tap_rows(bufs, flip, which):
    out = []
    for dr in (-1, 0, 1):
        for dc in (-1, 0, 1):
            sr, sc = (-dr, -dc) if flip else (dr, dc)
            at = slice(PAD + SIDE * sr, PAD + SIDE * sr + POS)
            piece = jnp.concatenate([bufs[sc + 1, i, at, :] for i in which], axis=0)
            out.append(piece)
    return out


def layer_forward(l, w, small, eo, xs, h1, y, qkv, att, o, st, bufs, nbuf, qkvw, tmp, staged, pump):
    images = h1.shape[1]
    split_qkv(w, l, qkvw, tmp)
    mod = dot_nn(eo[...], w[l, R_EMB : R_EMB + 4 * C, :])
    ma = mod[0:4] + small[l, 5:6, :]
    mb = mod[4:8] + small[l, 6:7, :]
    for i in range(images):
        st[l, i, S_MA : S_MA + 1, :] = ma[i : i + 1]
        st[l, i, S_MB : S_MB + 1, :] = mb[i : i + 1]

    sums = {}

    def row(k):
        return small[l, k : k + 1, :]

    def keep(which, mean, inv, at):
        for k, i in enumerate(which):
            st[l, i, at : at + 1, :] = mean[k : k + 1]
            st[l, i, at + 1 : at + 2, :] = inv[k : k + 1]

    def first(which):
        mean, inv = norm_stats([norm_sums(xs[l, i]) for i in which])
        keep(which, mean, inv, S_M1)
        for k, i in enumerate(which):
            a = inv[k : k + 1] * row(0)
            for r in range(0, POS, CHUNK):
                v = (xs[l, i, r : r + CHUNK, :] - mean[k : k + 1]) * a + row(1)
                put_shifted(bufs, i, r, silu(v))

    def conv(which, at):
        left = jnp.concatenate(tap_rows(bufs, False, which), axis=1)
        return dot_nn(left, w[l, at : at + 9 * C, :])

    def conv_one(which):
        out = conv(which, R_CONV1)
        for k, i in enumerate(which):
            own = out[k * POS : (k + 1) * POS]
            sums[i] = norm_sums(own, row(2))
            h1[l, i] = own + row(2)

    def second(which):
        mean, inv = norm_stats([sums[i] for i in which])
        keep(which, mean, inv, S_M2)
        for k, i in enumerate(which):
            gain = 1.0 + ma[i : i + 1]
            a = inv[k : k + 1] * row(3) * gain
            b = row(4) * gain + mb[i : i + 1]
            for r in range(0, POS, CHUNK):
                v = (h1[l, i, r : r + CHUNK, :] - mean[k : k + 1]) * a + b
                put_shifted(bufs, i, r, silu(v))

    def conv_two(which):
        out = conv(which, R_CONV2) + row(7)
        for k, i in enumerate(which):
            own = (xs[l, i] + out[k * POS : (k + 1) * POS]) * RS
            sums[i] = norm_sums(own)
            y[l, i] = own

    def third(which):
        mean, inv = norm_stats([sums[i] for i in which])
        keep(which, mean, inv, S_M3)
        for k, i in enumerate(which):
            a = inv[k : k + 1] * row(8)
            for r in range(0, POS, CHUNK):
                v = (y[l, i, r : r + CHUNK, :] - mean[k : k + 1]) * a + row(9)
                nbuf[i, r : r + CHUNK, :] = v.astype(BF16)

    def project_in(which):
        n = jnp.concatenate([nbuf[i] for i in which], axis=0)
        for j, at in ((0, 10), (1, None), (2, 11)):
            part = dot_nn(n, qkvw[:, j * C : (j + 1) * C])
            if at is not None:
                part = part + row(at)
            part = part.astype(BF16)
            for k, i in enumerate(which):
                qkv[l, i, :, j * C : (j + 1) * C] = part[k * POS : (k + 1) * POS]

    def attend(which):
        scores = [dot_nt(qkv[l, i, :, 0:C], qkv[l, i, :, C : 2 * C]) for i in which]
        for s, i in zip(scores, which):
            e = jnp.exp((s - jnp.max(s, axis=1, keepdims=True)) * (C**-0.5))
            p = (e * (1.0 / jnp.sum(e, axis=1, keepdims=True))).astype(BF16)
            att[l, i] = p
            o[l, i] = dot_nn(p, qkv[l, i, :, 2 * C :]).astype(BF16)

    def project_out(which):
        left = jnp.concatenate([o[l, i] for i in which], axis=0)
        out = dot_nn(left, w[l, R_PROJ:, :]) + row(12)
        for k, i in enumerate(which):
            xs[l + 1, i] = (y[l, i] + out[k * POS : (k + 1) * POS]) * RS

    steps = (first, conv_one, second, conv_two, third, project_in, attend, project_out)
    if not staged:
        for step in steps:
            step(range(images))
            pump(l)
    else:
        stagger([lambda i, step=step: step([i]) for step in steps], images, lambda: pump(l))


def layer_backward(
    l, w, small, eo, xs, h1, y, qkv, att, o, st, g, bufs, nbuf, qkvw, tmp, dn, dqkv, act_t,
    grad, sgrad, pump, need_dx=None,
):
    want = grad is not None
    images = h1.shape[1]
    which = range(images)
    flat = images * POS
    scale = C**-0.5
    split_qkv(w, l, qkvw, tmp)

    def row(k):
        return small[l, k : k + 1, :]

    def rows8(rows):
        return jnp.concatenate(list(rows) + [jnp.zeros((8 - len(rows), C), F32)], axis=0)

    zero = jnp.zeros((1, C), F32)
    gps, c1, c2, p1, p2 = {}, {}, {}, {}, {}
    total = {7: zero, 2: zero}
    gains = [1.0 + st[l, i, S_MA : S_MA + 1, :] for i in which]

    def one8(v):
        return jnp.broadcast_to(v, (8, C))

    def project_out(i):
        gps[i] = (g[i] * RS).astype(BF16)
        nbuf[i] = dot_nt(gps[i], w[l, R_PROJ:, :]).astype(BF16)

    def attend(i):
        p = att[l, i]
        pf = p.astype(F32)
        dp = dot_nt(nbuf[i], qkv[l, i, :, 2 * C :])
        ds = (pf * (dp - jnp.sum(dp * pf, axis=1, keepdims=True))).astype(BF16)
        dqkv[i, :, 0:C] = (dot_nn(ds, qkv[l, i, :, C : 2 * C]) * scale).astype(BF16)
        dqkv[i, :, C : 2 * C] = (dot_tn(ds, qkv[l, i, :, 0:C]) * scale).astype(BF16)
        dqkv[i, :, 2 * C :] = dot_tn(p, nbuf[i]).astype(BF16)

    def project_in(i):
        mean, inv = st[l, i, S_M3 : S_M3 + 1, :], st[l, i, S_I3 : S_I3 + 1, :]
        d = dot_nt(dqkv[i], qkvw[...])
        dn[i] = d
        c1[i] = colsum(d)
        c2[i] = colsum(d * ((y[l, i] - mean) * inv))

    def third(i):
        mean, inv = st[l, i, S_M3 : S_M3 + 1, :], st[l, i, S_I3 : S_I3 + 1, :]
        mg = group_mean(one8(row(8) * c1[i]))[0:1]
        mc = group_mean(one8(row(8) * c2[i]))[0:1]
        for r in range(0, POS, CHUNK):
            nh = (y[l, i, r : r + CHUNK, :] - mean) * inv
            gm = g[i, r : r + CHUNK, :] * RS + inv * (row(8) * dn[i, r : r + CHUNK, :] - mg - nh * mc)
            gm = gm * RS
            g[i, r : r + CHUNK, :] = gm
            put_shifted(bufs, i, r, gm)
            if want:
                nbuf[i, r : r + CHUNK, :] = (nh * row(8) + row(9)).astype(BF16)
                total[7] = total[7] + colsum(gm)

    def conv_grad(i, at):
        left = jnp.concatenate(tap_rows(bufs, True, [i]), axis=1)
        parts = [w[l, at + t * C : at + (t + 1) * C, :] for t in range(9)]
        dn[i] = dot_nt(left, jnp.concatenate(parts, axis=1))

    def activation(i, src, mean, inv, a, b, act):
        s1, s2 = zero, zero
        for r in range(0, POS, CHUNK):
            nh = (src[l, i, r : r + CHUNK, :] - mean) * inv
            pre = nh * a + b
            s, slope = silu_parts(pre)
            d = dn[i, r : r + CHUNK, :] * slope
            dn[i, r : r + CHUNK, :] = d
            s1 = s1 + colsum(d)
            s2 = s2 + colsum(d * nh)
            if want:
                act[i, r : r + CHUNK, :] = (pre * s).astype(BF16)
        p1[i], p2[i] = s1, s2

    def second_a(i):
        mean, inv = st[l, i, S_M2 : S_M2 + 1, :], st[l, i, S_I2 : S_I2 + 1, :]
        b = row(4) * gains[i] + st[l, i, S_MB : S_MB + 1, :]
        activation(i, h1, mean, inv, row(3) * gains[i], b, act_one)

    def second_b(i):
        mean, inv = st[l, i, S_M2 : S_M2 + 1, :], st[l, i, S_I2 : S_I2 + 1, :]
        full = row(3) * gains[i]
        mg = group_mean(one8(full * p1[i]))[0:1]
        mc = group_mean(one8(full * p2[i]))[0:1]
        for r in range(0, POS, CHUNK):
            nh = (h1[l, i, r : r + CHUNK, :] - mean) * inv
            dh = inv * (full * dn[i, r : r + CHUNK, :] - mg - nh * mc)
            put_shifted(bufs, i, r, dh)
            if want:
                total[2] = total[2] + colsum(dh)

    def first_a(i):
        mean, inv = st[l, i, S_M1 : S_M1 + 1, :], st[l, i, S_I1 : S_I1 + 1, :]
        activation(i, xs, mean, inv, row(0), row(1), nbuf)

    def first_b(i):
        mean, inv = st[l, i, S_M1 : S_M1 + 1, :], st[l, i, S_I1 : S_I1 + 1, :]
        mg = group_mean(one8(row(0) * p1[i]))[0:1]
        mc = group_mean(one8(row(0) * p2[i]))[0:1]
        for r in range(0, POS, CHUNK):
            nh = (xs[l, i, r : r + CHUNK, :] - mean) * inv
            dx = inv * (row(0) * dn[i, r : r + CHUNK, :] - mg - nh * mc)
            g[i, r : r + CHUNK, :] = g[i, r : r + CHUNK, :] + dx

    act_one = nbuf
    upper = [project_out, attend, project_in, third, lambda i: conv_grad(i, R_CONV2)]
    lower = [second_b, lambda i: conv_grad(i, R_CONV1), first_a]
    if not want:
        stagger(upper + [second_a] + lower + [first_b], images, lambda: pump(l))
        return
    stagger(upper, images, lambda: pump(l))
    gp = jnp.concatenate([gps[i] for i in which], axis=0)
    grad[l, R_PROJ:, :] = dot_tn(o[l].reshape(flat, C), gp).astype(BF16)
    sgrad[l, 12:13, :] = colsum(gp.astype(F32))
    sgrad[l, 7:8, :] = total[7]
    sgrad[l, 8:9, :] = colsum(rows8([c2[i] for i in which]))
    sgrad[l, 9:10, :] = colsum(rows8([c1[i] for i in which]))
    act_t[...] = nbuf[...].reshape(flat, C).T
    for j in range(3):
        dj = dqkv[:, :, j * C : (j + 1) * C].reshape(flat, C)
        part = dot_nn(act_t[...], dj)
        for h in range(2):
            tmp[h, pl.ds(j, C, stride=3), :] = part[:, h * HALF : (h + 1) * HALF]
        if j != 1:
            sgrad[l, 10 + j // 2 : 11 + j // 2, :] = colsum(dj.astype(F32))
    for h in range(2):
        grad[l, R_QKV : R_QKV + 3 * C, h * HALF : (h + 1) * HALF] = tmp[h].astype(BF16)
    for i in which:
        second_a(i)
    pump(l)
    act_t[...] = nbuf[...].reshape(flat, C).T
    conv_weight_grad(act_t, bufs, grad, l, R_CONV2)
    p18, p28, modgain = [rows8([a[i] for i in which]) for a in (p1, p2, gains)]
    dma = row(3) * p28 + row(4) * p18
    sgrad[l, 3:4, :] = colsum(modgain * p28)
    sgrad[l, 4:5, :] = colsum(modgain * p18)
    sgrad[l, 5:6, :] = colsum(dma)
    sgrad[l, 6:7, :] = colsum(p18)
    grad[l, R_EMB : R_EMB + 4 * C, :] = embed_grad(
        eo, jnp.concatenate([dma[0:4], p18[0:4]], axis=0)
    ).astype(BF16)
    pump(l)
    stagger(lower, images, lambda: pump(l))
    sgrad[l, 2:3, :] = total[2]
    sgrad[l, 0:1, :] = colsum(rows8([p2[i] for i in which]))
    sgrad[l, 1:2, :] = colsum(rows8([p1[i] for i in which]))
    act_t[...] = nbuf[...].reshape(flat, C).T
    conv_weight_grad(act_t, bufs, grad, l, R_CONV1)
    pump(l)

    @pl.when(l == 1)
    def _():
        for i in which:
            first_b(i)


def embed_grad(eo, dm):
    parts, rest = [], dm
    for _ in range(3):
        parts.append(rest.astype(BF16))
        rest = rest - parts[-1].astype(F32)
    left = eo[...]
    return dot_tn(jnp.concatenate([left, left], axis=0), jnp.concatenate(parts[:2], axis=0)) + dot_tn(
        left, parts[2]
    )


def saved_shapes(images):
    return [
        jax.ShapeDtypeStruct((3, images, POS, C), F32),
        jax.ShapeDtypeStruct((2, images, POS, C), F32),
        jax.ShapeDtypeStruct((2, images, POS, C), F32),
        jax.ShapeDtypeStruct((2, images, POS, 3 * C), BF16),
        jax.ShapeDtypeStruct((2, images, POS, POS), BF16),
        jax.ShapeDtypeStruct((2, images, POS, C), BF16),
        jax.ShapeDtypeStruct((2, images, 8, C), F32),
    ]


def forward_kernel(staged, x0, w, small, eo, xs, h1, y, qkv, att, o, st, bufs, nbuf, qkvw, tmp):
    clear_pads(bufs)
    xs[0] = x0[...]

    def body(l, _):
        layer_forward(
            l, w, small, eo, xs, h1, y, qkv, att, o, st, bufs, nbuf, qkvw, tmp, staged, no_pump
        )
        return 0

    lax.fori_loop(0, 2, body, 0)


def backward_kernel(want, *refs):
    cot, w, small, eo, xs, h1, y, qkv, att, o, st, g = refs[:12]
    refs = refs[12:]
    if want:
        grad, sgrad = refs[:2]
        refs = refs[2:]
    else:
        grad, sgrad = None, None
    bufs, nbuf, qkvw, tmp, dn, dqkv, act_t = refs
    clear_pads(bufs)
    g[...] = cot[...]
    if want:
        sgrad[...] = jnp.zeros(sgrad.shape, F32)

    def body(k, _):
        layer_backward(
            1 - k, w, small, eo, xs, h1, y, qkv, att, o, st, g, bufs, nbuf, qkvw, tmp, dn,
            dqkv, act_t, grad, sgrad, no_pump,
        )
        return 0

    lax.fori_loop(0, 2, body, 0)


def vm(n):
    return [pl.BlockSpec(memory_space=pltpu.VMEM)] * n


def scratch_forward(images):
    return [
        pltpu.VMEM((3, images, POS + 2 * PAD, C), BF16),
        pltpu.VMEM((images, POS, C), BF16),
        pltpu.VMEM((C, 3 * C), BF16),
        pltpu.VMEM((2, 3 * C, HALF), F32),
    ]


def run_forward(x0, w, small, eo, staged=False):
    images = x0.shape[0]
    return pl.pallas_call(
        functools.partial(forward_kernel, staged),
        out_shape=saved_shapes(images),
        in_specs=vm(4),
        out_specs=vm(7),
        scratch_shapes=scratch_forward(images),
        compiler_params=pltpu.CompilerParams(vmem_limit_bytes=VMEM_LIMIT),
    )(x0, w, small, eo)


def run_backward(cot, w, small, eo, saved, want):
    images = cot.shape[0]
    outs = [jax.ShapeDtypeStruct(cot.shape, F32)]
    if want:
        outs += [
            jax.ShapeDtypeStruct((2, ROWS, C), BF16),
            jax.ShapeDtypeStruct((2, 16, C), F32),
        ]
    return pl.pallas_call(
        functools.partial(backward_kernel, want),
        out_shape=outs,
        in_specs=vm(11),
        out_specs=vm(len(outs)),
        scratch_shapes=scratch_forward(images)
        + [
            pltpu.VMEM((images, POS, C), F32),
            pltpu.VMEM((images, POS, 3 * C), BF16),
            pltpu.VMEM((C, images * POS), BF16),
        ],
        compiler_params=pltpu.CompilerParams(vmem_limit_bytes=VMEM_LIMIT),
    )(cot, w, small, eo, *saved)


PLANES, PLANE = 4, 4
MESH = pl.DeviceIdType.MESH


class Place:
    def __init__(self):
        self.sec = lax.axis_index("section")
        self.d = lax.axis_index("dp")
        self.x = lax.rem(self.d, 2)
        self.y = lax.rem(self.d // 2, 2)
        self.z = self.d // PLANE
        self.sib = {"section": 1 - self.sec}
        self.xn = {"dp": self.d + 1 - 2 * self.x}
        self.yn = {"dp": self.d + 2 - 4 * self.y}

    def plane(self, j):
        return lax.rem(self.z + j + PLANES, PLANES)

    def zpeer(self, j):
        return {"dp": self.plane(j) * PLANE + lax.rem(self.d, PLANE)}

    def meet(self):
        barrier = pltpu.get_barrier_semaphore()
        others = [self.sib, self.xn, self.yn] + [self.zpeer(j) for j in (1, 2, 3)]
        for other in others:
            pl.semaphore_signal(barrier, inc=1, device_id=other, device_id_type=MESH)
        pl.semaphore_wait(barrier, len(others))


def remote(src, dst, send, recv, target):
    return pltpu.make_async_remote_copy(
        src_ref=src, dst_ref=dst, send_sem=send, recv_sem=recv,
        device_id=target, device_id_type=MESH,
    )


Z1, X1, Y1, X2, Y2, S_OWN, S_X, S_Y, S_DA, S_DB = 0, 3, 7, 11, 15, 19, 23, 27, 31, 35
SLOTS = 39


class Gather:
    def __init__(self, me, net, stage, local_sem, send_sem, recv_sem):
        self.me, self.net, self.stage = me, net, stage
        self.local_sem, self.send_sem, self.recv_sem = local_sem, send_sem, recv_sem
        self.part = stage.shape[0]
        self.half = self.part // 2

    def rows(self, plane, y, x, lo, count):
        at = (plane * PLANE + y * 2 + x) * self.part + lo
        return self.net.at[self.me.sec, pl.ds(pl.multiple_of(at, 16), count)]

    def own(self, j):
        return self.rows(self.me.plane(-j), self.me.y, self.me.x, 0, self.part)

    def send(self, slot, piece, target, src=None):
        src = piece if src is None else src
        remote(src, piece, self.send_sem.at[slot], self.recv_sem.at[slot], target).start()

    def arrived(self, slot, piece):
        remote(
            piece, piece, self.send_sem.at[slot], self.recv_sem.at[slot], self.me.sib
        ).wait_recv()

    def local(self):
        return pltpu.make_async_copy(self.stage, self.own(0), self.local_sem)

    def begin(self):
        me = self.me
        for j in (1, 2, 3):
            self.send(Z1 + j - 1, self.own(0), me.zpeer(j), self.stage)
        for slot, target in ((X1, me.xn), (Y1, me.yn), (S_OWN, me.sib)):
            self.send(slot, self.own(0), target, self.stage)
        self.local().start()

    def phase1(self):
        def step(j):
            me = self.me
            self.arrived(Z1 + j - 1, self.own(j))
            for slot, target in ((X1, me.xn), (Y1, me.yn), (S_OWN, me.sib)):
                self.send(slot + j, self.own(j), target)

        return [lambda j=j: step(j) for j in (1, 2, 3)]

    def phase2(self):
        me, part, half = self.me, self.part, self.half

        def step_x(j):
            plane = me.plane(-j)
            self.arrived(X1 + j, self.rows(plane, me.y, 1 - me.x, 0, part))
            self.send(Y2 + j, self.rows(plane, me.y, 1 - me.x, 0, half), me.yn)
            self.send(S_X + j, self.rows(plane, me.y, 1 - me.x, 0, part), me.sib)

        def step_y(j):
            plane = me.plane(-j)
            self.arrived(Y1 + j, self.rows(plane, 1 - me.y, me.x, 0, part))
            self.send(X2 + j, self.rows(plane, 1 - me.y, me.x, half, half), me.xn)
            self.send(S_Y + j, self.rows(plane, 1 - me.y, me.x, 0, part), me.sib)

        return [lambda f=f, j=j: f(j) for j in range(PLANES) for f in (step_x, step_y)]

    def phase3(self):
        def step(j, slot, to, lo):
            me = self.me
            where = self.rows(me.plane(-j), 1 - me.y, 1 - me.x, lo, self.half)
            self.arrived(slot + j, where)
            self.send(to + j, where, me.sib)

        return [
            lambda j=j, a=a: step(j, *a)
            for j in range(PLANES)
            for a in ((Y2, S_DA, 0), (X2, S_DB, self.half))
        ]

    def finish(self):
        def step():
            for slot in range(S_OWN, SLOTS):
                count = self.part if slot < S_DA else self.half
                self.arrived(slot, self.rows(0, 0, 0, 0, count))
            self.local().wait()

        return [step]

    def drain(self):
        for slot in range(SLOTS):
            whole = slot < X2 or S_OWN <= slot < S_DA
            piece = self.rows(0, 0, 0, 0, self.part if whole else self.half)
            remote(
                piece, piece, self.send_sem.at[slot], self.recv_sem.at[slot], self.me.sib
            ).wait_send()


A_SLOT, B_SLOT, C_SLOT, D_SLOT = 0, 4, 20, 28
R_SLOTS = 31


class Reduce:
    def __init__(self, me, big, shard, sib, there, rb, rc, rd, ssem, rsem):
        self.me, self.big, self.shard = me, big, shard
        self.sib, self.there, self.rb, self.rc, self.rd = sib, there, rb, rc, rd
        self.ssem, self.rsem = ssem, rsem
        self.part = shard.shape[0]
        self.half = self.part // 2
        self.span = PLANE * self.part

    def zt(self, k):
        return PLANES - 1 - k

    def block(self, k):
        return pl.ds(self.zt(k) * self.span, self.span)

    def piece(self, k, y, x, lo, count):
        at = (self.zt(k) * PLANE + y * 2 + x) * self.part + lo
        return pl.ds(pl.multiple_of(at, 16), count)

    def send(self, src, dst, slot, target):
        remote(src, dst, self.ssem.at[slot], self.rsem.at[slot], target).start()

    def arrived(self, dst, slot):
        remote(dst, dst, self.ssem.at[slot], self.rsem.at[slot], self.me.sib).wait_recv()

    def begin(self):
        for k in range(PLANES):
            self.begin_block(k)

    def begin_block(self, k):
        at = self.block(k)
        self.send(self.big.at[1 - self.me.sec, at], self.there.at[at], A_SLOT + k, self.me.sib)

    def stage_a(self, k):
        me, half = self.me, self.half
        self.arrived(self.sib.at[self.block(k)], A_SLOT + k)
        base = self.zt(k) * self.span

        def body(i, _):
            at = pl.ds(pl.multiple_of(base + i * half, 16), half)
            self.big[me.sec, at, :] = (
                self.big[me.sec, at, :].astype(F32) + self.sib[at, :].astype(F32)
            ).astype(BF16)
            return 0

        lax.fori_loop(0, 2 * PLANE, body, 0)
        for j in range(2):
            self.send(
                self.big.at[me.sec, self.piece(k, 1 - me.y, j, 0, half)], self.rb.at[k, j],
                B_SLOT + 4 * k + j, me.yn,
            )
            self.send(
                self.big.at[me.sec, self.piece(k, j, 1 - me.x, half, half)], self.rb.at[k, 2 + j],
                B_SLOT + 4 * k + 2 + j, me.xn,
            )

    def join(self, where, other):
        self.big[self.me.sec, where, :] = (
            self.big[self.me.sec, where, :].astype(F32) + other.astype(F32)
        ).astype(BF16)

    def stage_c(self, k):
        me, half = self.me, self.half
        for j in range(4):
            self.arrived(self.rb.at[k, j], B_SLOT + 4 * k + j)
            y, x, lo = (me.y, j, 0) if j < 2 else (j - 2, me.x, half)
            self.join(self.piece(k, y, x, lo, half), self.rb[k, j])
        self.send(
            self.big.at[me.sec, self.piece(k, me.y, 1 - me.x, 0, half)], self.rc.at[k, 0],
            C_SLOT + 2 * k, me.xn,
        )
        self.send(
            self.big.at[me.sec, self.piece(k, 1 - me.y, me.x, half, half)], self.rc.at[k, 1],
            C_SLOT + 2 * k + 1, me.yn,
        )

    def stage_d(self, k):
        me, half, zt = self.me, self.half, self.zt(k)
        for j in range(2):
            self.arrived(self.rc.at[k, j], C_SLOT + 2 * k + j)
            self.join(self.piece(k, me.y, me.x, j * half, half), self.rc[k, j])

        @pl.when(me.z != zt)
        def _():
            self.send(
                self.big.at[me.sec, self.piece(k, me.y, me.x, 0, self.part)],
                self.rd.at[lax.rem(zt - me.z + PLANES, PLANES) - 1],
                D_SLOT + lax.rem(zt - me.z + PLANES, PLANES) - 1,
                {"dp": zt * PLANE + lax.rem(me.d, PLANE)},
            )

    def stage_e(self):
        for j in range(PLANES - 1):
            self.arrived(self.rd.at[j], D_SLOT + j)
        at = pl.ds(pl.multiple_of(self.me.d * self.part, 16), self.part)
        self.shard[...] = (
            self.big[self.me.sec, at, :].astype(F32)
            + self.rd[0].astype(F32) + (self.rd[1].astype(F32) + self.rd[2].astype(F32))
        )

    def steps(self):
        out = []
        for t in range(PLANES + 2):
            for stage, lag in ((self.stage_a, 0), (self.stage_c, 1), (self.stage_d, 2)):
                if 0 <= t - lag < PLANES:
                    out.append(lambda stage=stage, k=t - lag: stage(k))
        return out

    def drain(self, lo=0, hi=R_SLOTS):
        for slot in range(lo, hi):
            if slot < B_SLOT:
                piece = self.there.at[pl.ds(0, self.span)]
            elif slot < D_SLOT:
                piece = self.rb.at[0, 0]
            else:
                piece = self.rd.at[0]
            remote(piece, piece, self.ssem.at[slot], self.rsem.at[slot], self.me.sib).wait_send()


def reduce_scratch(part):
    half = part // 2
    return [
        pltpu.VMEM((PLANES, 4, half, C), BF16),
        pltpu.VMEM((PLANES, 2, half, C), BF16),
        pltpu.VMEM((PLANES - 1, part, C), BF16),
        pltpu.SemaphoreType.DMA((R_SLOTS,)),
        pltpu.SemaphoreType.DMA((R_SLOTS,)),
    ]


class Totals:
    def __init__(self, me, buf, recv, ssem, rsem):
        self.me, self.buf, self.recv, self.ssem, self.rsem = me, buf, recv, ssem, rsem

    def send(self, src, dst, slot, target):
        remote(src, dst, self.ssem.at[slot], self.rsem.at[slot], target).start()

    def arrived(self, dst, slot):
        remote(dst, dst, self.ssem.at[slot], self.rsem.at[slot], self.me.sib).wait_recv()

    def begin(self, first):
        self.send(first, self.recv.at[0], 0, self.me.sib)

    def steps(self):
        me, buf, recv = self.me, self.buf, self.recv

        def one():
            self.arrived(recv.at[0], 0)
            buf[1] = buf[0] + recv[0]
            self.send(buf.at[1], recv.at[1], 1, me.xn)

        def two():
            self.arrived(recv.at[1], 1)
            buf[2] = buf[1] + recv[1]
            self.send(buf.at[2], recv.at[2], 2, me.yn)

        def three():
            self.arrived(recv.at[2], 2)
            buf[3] = buf[2] + recv[2]
            recv[3 + me.z] = buf[3]
            for j in (1, 2, 3):
                self.send(buf.at[3], recv.at[3 + me.z], 2 + j, me.zpeer(j))

        return [one, two, three]

    def result(self):
        for j in (1, 2, 3):
            self.arrived(self.recv.at[3 + self.me.plane(-j)], 2 + j)
        return (self.recv[3] + self.recv[4]) + (self.recv[5] + self.recv[6])

    def drain(self):
        for slot in range(6):
            piece = self.recv.at[0]
            remote(piece, piece, self.ssem.at[slot], self.rsem.at[slot], self.me.sib).wait_send()


def totals_scratch(shape):
    return [
        pltpu.VMEM((4,) + shape, F32),
        pltpu.VMEM((7,) + shape, F32),
        pltpu.SemaphoreType.DMA((6,)),
        pltpu.SemaphoreType.DMA((6,)),
    ]


def saved_scratch(images):
    return [pltpu.VMEM(a.shape, a.dtype) for a in saved_shapes(images)]


def backward_scratch(images):
    return scratch_forward(images) + [
        pltpu.VMEM((images, POS, C), F32),
        pltpu.VMEM((images, POS, 3 * C), BF16),
        pltpu.VMEM((C, images * POS), BF16),
    ]


GEN_TOTAL = SIGMA_INIT**2 + SIGMA_DATA**2
GEN_IN = GEN_TOTAL**-0.5
GEN_SKIP = SIGMA_DATA**2 / GEN_TOTAL
GEN_OUT = SIGMA_INIT * SIGMA_DATA * GEN_TOTAL**-0.5
T_IN, T_SKIP, T_OUT, T_SIGMA, T_FACTOR = range(5)


def fill_embed(eo, sigmas):
    at = lax.broadcasted_iota(jnp.int32, (8, 4 * C), 1)
    side = lax.broadcasted_iota(jnp.int32, (8, 4 * C), 0) // 4
    k = at // 2
    power = (k & (C - 1)).astype(F32) * (1.0 / C)
    rows = sigmas + [jnp.ones_like(sigmas[0])] * (4 - len(sigmas))
    angle = jnp.log(jnp.concatenate(rows + rows, axis=0)) * 0.25 * jnp.exp(power * -LOG_10000)
    wave = jnp.where(k < C, jnp.cos(angle), jnp.sin(angle))
    eo[...] = jnp.where((at & 1) == side, wave, 0.0).astype(BF16)


LOG_10000 = 9.210340371976184


def step_kernel(*refs):
    (
        z_all, eps_all, levels, counts, gen_w, fake_w, teacher_w, gen_small, fake_small,
        teacher_small,
        gw_out, sv_x, sv_h, sv_y, sv_q, sv_a, sv_o, sv_s, gshard, fshard, stot, sqtot,
        *refs,
    ) = refs
    gen_out = (sv_x, sv_h, sv_y, sv_q, sv_a, sv_o, sv_s)
    w_gen, w_fake, w_teach = refs[:3]
    sv_one, sv_two = refs[3:10], refs[10:17]
    bufs, nbuf, qkvw, tmp, dn, dqkv, act_t = refs[17:24]
    zb, eb, g, stage, local_sem, send_sem, recv_sem, copy_sem = refs[24:32]
    smalls, small_sem, gen_eo, score_eo, tab, sgrads, part_sums = refs[32:39]
    fake_refs, gen_refs = refs[39:44], refs[44:49]
    small_refs, square_refs = refs[49:53], refs[53:57]
    sib, free_sem = refs[57:59]
    g2 = sv_two[0].at[2]
    images = zb.shape[0]
    me = Place()
    start = me.sec * images

    def run(steps):
        for step in steps:
            step()

    def mine(ref):
        return ref.at[pl.ds(start, images)]

    loads = [
        pltpu.make_async_copy(mine(z_all), zb, copy_sem.at[0]),
        pltpu.make_async_copy(mine(eps_all), eb, copy_sem.at[1]),
    ]
    for copy in loads:
        copy.start()
    masters = [
        pltpu.make_async_copy(src, dst, copy_sem.at[2 + k])
        for k, (src, dst) in enumerate(((gen_w, gshard), (fake_w, fshard), (teacher_w, stage.at[2])))
    ]
    for copy in masters:
        copy.start()
    smalls[...] = jnp.zeros(smalls.shape, F32)
    for n, ref in enumerate((gen_small, fake_small, teacher_small)):
        for r in range(13):
            smalls[me.sec, n, r : r + 1, :] = ref[r]
    gathers = [
        Gather(me, net, stage.at[n], local_sem.at[n], send_sem.at[n], recv_sem.at[n])
        for n, net in enumerate((w_gen, w_fake, w_teach))
    ]
    for copy in masters:
        copy.wait()
    stage[0] = gshard[...].astype(BF16)
    stage[1] = fshard[...].astype(BF16)
    me.meet()
    gathers[0].begin()
    swap = remote(
        smalls.at[me.sec], smalls.at[me.sec], small_sem.at[0], small_sem.at[1], me.sib
    )
    swap.start()

    clear_pads(bufs)
    sgrads[...] = jnp.zeros(sgrads.shape, F32)
    sigmas = []
    valid_sum = jnp.zeros((1, 4 * C), F32)
    for i in range(images):
        level = jnp.zeros((1, 4 * C), jnp.int32) + levels[start + i]
        sigma = SIGMA_TOP + level.astype(F32) / (LEVELS - 1) * (SIGMA_BOTTOM - SIGMA_TOP)
        square = sigma * sigma
        sigma = square * square * square * sigma
        sigmas.append(sigma)
        s_in, s_skip, s_out, s_lam = precondition(sigma)
        valid = jnp.where(jnp.zeros_like(level) + (start + i) < counts[0], 1.0, 0.0)
        valid_sum = valid_sum + valid
        rows = (s_in, s_skip, s_out, sigma, valid * s_lam * (1.0 / (POS * C)))
        for k, value in enumerate(rows):
            tab[i, k : k + 1, :] = value[:, :C]
    fill_embed(score_eo, sigmas)
    fill_embed(gen_eo, [jnp.full((1, 4 * C), SIGMA_INIT, F32)] * images)

    def forward(n, w, eo, sv, pump):
        def body(l, _):
            layer_forward(
                l, w, smalls.at[:, n], eo, *sv, bufs, nbuf, qkvw, tmp, True, pump
            )
            return 0

        lax.fori_loop(0, 2, body, 0)

    def backward(n, w, eo, sv, cot, grad, sgrad, pump):
        def body(k, _):
            layer_backward(
                1 - k, w, smalls.at[:, n], eo, *sv, cot, bufs, nbuf, qkvw, tmp, dn, dqkv,
                act_t, grad, sgrad, pump,
            )
            return 0

        lax.fori_loop(0, 2, body, 0)

    def each(f):
        def body(i, carry):
            return f(i, [tab[i, k : k + 1, :] for k in range(5)], carry)

        return lax.fori_loop(0, images, body, jnp.zeros((1, C), F32))

    run(gathers[0].phase1() + [gathers[1].begin] + gathers[0].phase2() + gathers[0].phase3())
    for copy in loads:
        copy.wait()
    sv_one[0][0] = zb[...] * (GEN_IN * SIGMA_INIT)
    swap.wait()
    run(gathers[0].finish())
    later = gathers[1].phase1() + [gathers[2].begin] + gathers[1].phase2()
    forward(0, w_gen, gen_eo, sv_one, Pump(later[:8], FORWARD_POINTS, (0, 1)))
    pairs = [(w_gen, gw_out)] + list(zip(sv_one, gen_out))
    stores = [
        pltpu.make_async_copy(src, dst, copy_sem.at[2 + k]) for k, (src, dst) in enumerate(pairs)
    ]
    for copy in stores:
        copy.start()

    def noisy(i, t, carry):
        zb[i] = zb[i] * (GEN_SKIP * SIGMA_INIT) + GEN_OUT * sv_one[0][2, i]
        eb[i] = zb[i] + t[T_SIGMA] * eb[i]
        sv_two[0][0, i] = t[T_IN] * eb[i]
        return carry

    each(noisy)
    run(later[8:] + gathers[1].phase3() + gathers[1].finish())
    later = gathers[2].phase1() + gathers[2].phase2()
    forward(1, w_fake, score_eo, sv_two, Pump(later[:9], FORWARD_POINTS, (0, 1)))
    later = later[9:] + gathers[2].phase3()

    def fake_loss(i, t, total):
        den = t[T_SKIP] * eb[i] + t[T_OUT] * sv_two[0][2, i]
        sv_two[0][2, i] = den
        miss = den - zb[i]
        g[i] = (2.0 * t[T_OUT] * t[T_FACTOR]) * miss
        return total + t[T_FACTOR] * colsum(miss * miss)

    loss_fake = each(fake_loss)
    for copy in stores:
        copy.wait()
    gathers[0].drain()
    backward(
        1, w_fake, score_eo, sv_two, g, w_gen, sgrads.at[:, 1],
        Pump(later, WEIGHT_POINTS, (1, 0)),
    )
    fake_sum = Reduce(me, w_gen, fshard, sib, sib, *fake_refs)
    fake_sum.begin()
    run(gathers[2].finish())
    later = fake_sum.steps()
    sv_one[0][0] = sv_two[0][0]
    forward(2, w_teach, score_eo, sv_one, Pump(later[:5], FORWARD_POINTS, (0, 1), 0.2))

    def gen_loss(i, t, total):
        den = t[T_SKIP] * eb[i] + t[T_OUT] * sv_one[0][2, i]
        fake_den = sv_two[0][2, i]
        miss = fake_den - zb[i]
        gap = den - fake_den
        scale = t[T_OUT] * t[T_FACTOR]
        g[i] = scale * ((2.0 * (1.0 - ALPHA_MIX)) * gap + miss)
        g2[i] = scale * ((1.0 - 2.0 * (1.0 - ALPHA_MIX)) * gap - miss)
        zb[i] = (t[T_FACTOR] * (t[T_SKIP] - 1.0)) * gap
        return total + t[T_FACTOR] * colsum(gap * ((1.0 - ALPHA_MIX) * gap + miss))

    loss_gen = each(gen_loss)
    backward(
        2, w_teach, score_eo, sv_one, g, None, None, Pump(later[5:9], BACKWARD_POINTS, (1, 0))
    )
    gathers[2].drain()
    fake_sum.drain(A_SLOT, B_SLOT)
    pl.semaphore_signal(free_sem, inc=1, device_id=me.sib, device_id_type=MESH)
    back = [
        pltpu.make_async_copy(src, dst, copy_sem.at[2 + k])
        for k, (dst, src) in enumerate([(w_teach, gw_out)] + list(zip(sv_one, gen_out)))
    ]
    for copy in back:
        copy.start()
    backward(
        1, w_fake, score_eo, sv_two, g2, None, None, Pump(later[9:], BACKWARD_POINTS, (1, 0))
    )

    def gen_gradient(i, t, carry):
        g[i] = GEN_OUT * (zb[i] + t[T_IN] * (g[i] + g2[i]))
        return carry

    each(gen_gradient)
    gathers[1].drain()
    for copy in back:
        copy.wait()

    gen_sum = Reduce(me, w_fake, gshard, w_gen.at[1 - me.sec], w_gen.at[me.sec], *gen_refs)
    later = gen_sum.steps()

    def on_section(s, steps):
        pl.when(me.sec == s)(lambda: run(steps))

    def hand_over():
        pl.semaphore_wait(free_sem, 1)

    half_way, end = WEIGHT_POINTS - 7, WEIGHT_POINTS - 1
    pump = Pump([], WEIGHT_POINTS, (1, 0))

    def at(layer, point, section, steps):
        pump.table[layer][point].append(lambda: on_section(section, steps))

    at(1, half_way, 0, [hand_over, lambda: gen_sum.begin_block(0), lambda: gen_sum.begin_block(1)])
    at(1, end, 0, [lambda: gen_sum.begin_block(2), lambda: gen_sum.begin_block(3)])
    at(1, end - 2, 1, later[0:1])
    for k, step in enumerate(later[1:]):
        at(0, (k * end) // len(later), 1, [step])
    at(0, half_way, 1, [hand_over, lambda: gen_sum.begin_block(0), lambda: gen_sum.begin_block(1)])
    at(0, end - 2, 0, later[0:1])
    at(0, end, 0, later[1:3])
    at(0, end, 1, [lambda: gen_sum.begin_block(2), lambda: gen_sum.begin_block(3)])
    backward(0, w_teach, gen_eo, sv_one, g, w_fake, sgrads.at[:, 0], pump)

    def spread_sum(total):
        return jnp.broadcast_to(jnp.sum(total, axis=1, keepdims=True), (1, C))

    sums = jnp.concatenate([spread_sum(loss_gen), spread_sum(loss_fake), valid_sum[:, :C]], axis=0)
    for s in range(2):
        part_sums[s, 0:16, :] = sgrads[s, 0]
        part_sums[s, 13:16, :] = sums
        part_sums[s, 16:32, :] = sgrads[s, 1]
    small = Totals(me, *small_refs)
    small_refs[0][0] = part_sums[me.sec]
    small.begin(part_sums.at[1 - me.sec])
    fake_sum.stage_e()
    small_steps = small.steps()
    on_section(0, later[3:5])
    run(small_steps[:1])
    on_section(0, later[5:7])
    run(small_steps[1:2])
    on_section(0, later[7:9])
    run(small_steps[2:])
    on_section(0, later[9:])
    stot[...] = small.result()
    gen_sum.stage_e()
    lane = lax.broadcasted_iota(jnp.int32, (8, HALF), 1)
    tile = jnp.zeros((8, HALF), F32)
    for n, own in enumerate((gshard, fshard)):
        big_sum = jnp.sum(own[...] * own[...])
        low = jnp.sum(stot[16 * n : 16 * n + 13, :] * stot[16 * n : 16 * n + 13, :])
        tile = jnp.where(lane == n, big_sum + jnp.where(me.d == 0, low, 0.0), tile)
    square = Totals(me, *square_refs)
    square_refs[0][0] = tile
    square.begin(square_refs[0].at[0])
    run(square.steps())
    sqtot[...] = square.result()
    fake_sum.drain(B_SLOT)
    for done in (gen_sum, small, square):
        done.drain()


SIGMA_TOP = SIGMA_HIGH ** (1.0 / RHO_POWER)
SIGMA_BOTTOM = SIGMA_LOW ** (1.0 / RHO_POWER)


def run_step(z, eps, levels, counts, gen_w, fake_w, teacher_w, smalls):
    part = gen_w.shape[0]
    images = z.shape[0] // 2
    any_ = pl.BlockSpec(memory_space=pl.ANY)
    smem = pl.BlockSpec(memory_space=pltpu.SMEM)
    saved = saved_shapes(images)
    return pl.pallas_call(
        step_kernel,
        out_shape=[jax.ShapeDtypeStruct((2, ROWS, C), BF16)]
        + saved
        + [
            jax.ShapeDtypeStruct((part, C), F32),
            jax.ShapeDtypeStruct((part, C), F32),
            jax.ShapeDtypeStruct((32, C), F32),
            jax.ShapeDtypeStruct((8, HALF), F32),
        ],
        in_specs=[any_] * 2 + [smem] * 2 + [any_] * 3 + vm(3),
        out_specs=[any_] * 8 + vm(4),
        scratch_shapes=[pltpu.VMEM((2, ROWS, C), BF16)] * 3
        + saved_scratch(images) * 2
        + backward_scratch(images)
        + [pltpu.VMEM((images, POS, C), F32)] * 3
        + [
            pltpu.VMEM((3, part, C), BF16),
            pltpu.SemaphoreType.DMA((3,)),
            pltpu.SemaphoreType.DMA((3, SLOTS)),
            pltpu.SemaphoreType.DMA((3, SLOTS)),
            pltpu.SemaphoreType.DMA((10,)),
            pltpu.VMEM((2, 3, 16, C), F32),
            pltpu.SemaphoreType.DMA((2,)),
            pltpu.VMEM((8, 4 * C), BF16),
            pltpu.VMEM((8, 4 * C), BF16),
            pltpu.VMEM((images, 8, C), F32),
            pltpu.VMEM((2, 2, 16, C), F32),
            pltpu.VMEM((2, 32, C), F32),
        ]
        + reduce_scratch(part) * 2
        + totals_scratch((32, C))
        + totals_scratch((8, HALF))
        + [pltpu.VMEM((ROWS, C), BF16), pltpu.SemaphoreType.REGULAR],
        compiler_params=pltpu.CompilerParams(
            collective_id=0, has_side_effects=True, vmem_limit_bytes=STEP_LIMIT
        ),
    )(z, eps, levels, counts, gen_w, fake_w, teacher_w, *smalls)[8:]


def adam_step(master, first_mom, second_mom, grad):
    first_new = BETA_ONE * first_mom + (1.0 - BETA_ONE) * grad
    second_new = BETA_TWO * second_mom + (1.0 - BETA_TWO) * grad * grad
    direction = (
        first_new
        / (1.0 - BETA_ONE**STEP)
        / (jnp.sqrt(second_new / (1.0 - BETA_TWO**STEP)) + ADAM_EPS)
    )
    return (master - LEARN_RATE * (direction + WEIGHT_DECAY * master), first_new, second_new)


EMA_RATE = 0.5 ** (20.0 / STEP)
SMALL_STATES = (4, 5, 6, 7, 11, 12, 13)


def update_kernel(gshard, fshard, stot, sqtot, *refs):
    ins, outs = refs[:14], refs[14:]
    norms, losses = outs[14:]
    count = stot[15:16, 0:1]
    sq = sqtot[0:1, :]
    lane = lax.broadcasted_iota(jnp.int32, sq.shape, 1)
    scales = []
    for n in range(2):
        norm = jnp.sqrt(jnp.sum(jnp.where(lane == n, sq, 0.0), axis=1, keepdims=True)) / count
        scales.append(jnp.minimum(1.0, CLIP_NORM / norm) / count)
        norms[n] = norm[0, 0]
        losses[n] = (stot[13 + n : 14 + n, 0:1] / count)[0, 0]

    def one(at, grad, w, m, v, ema, ow, om, ov, oe):
        new, first, second = adam_step(w[at], m[at], v[at], grad)
        ow[at] = new
        om[at] = first
        ov[at] = second
        if ema is not None:
            oe[at] = EMA_RATE * ema[at] + (1.0 - EMA_RATE) * new

    one(0, gshard[...] * scales[0], *ins[0:4], *outs[0:4])
    one(0, fshard[...] * scales[1], *ins[8:11], None, *outs[8:11], None)
    for k in range(13):
        one(k, stot[k : k + 1, :] * scales[0], *ins[4:8], *outs[4:8])
        one(k, stot[16 + k : 17 + k, :] * scales[1], *ins[11:14], None, *outs[11:14], None)


def update_nets(gshard, fshard, stot, sqtot, states):
    def turned(arrays):
        return [a.swapaxes(0, 1) if k in SMALL_STATES else a for k, a in enumerate(arrays)]

    states = turned(states)
    res = pl.pallas_call(
        update_kernel,
        out_shape=[jax.ShapeDtypeStruct(a.shape, F32) for a in states]
        + [jax.ShapeDtypeStruct((2,), F32)] * 2,
        in_specs=vm(4 + len(states)),
        out_specs=vm(len(states)) + [pl.BlockSpec(memory_space=pltpu.SMEM)] * 2,
        compiler_params=pltpu.CompilerParams(vmem_limit_bytes=VMEM_LIMIT),
    )(gshard, fshard, stot, sqtot, *states)
    return tuple(turned(res[:-2])) + tuple(res[-2:])


def gather_plain(shard):
    rows = lax.all_gather(shard.astype(BF16), "dp", axis=1, tiled=True)
    return lax.all_gather(rows, "section", axis=0, tiled=True)


def reduce_plain(bigs, small):
    shards_, squares = [], []
    own = lax.psum_scatter(small, "section", scatter_dimension=0, tiled=True)
    stot = lax.psum(own, "dp")[0]
    first = lax.axis_index("dp") == 0
    for n, big in enumerate(bigs):
        own = lax.psum_scatter(big, "section", scatter_dimension=0, tiled=True)
        own = lax.psum_scatter(own, "dp", scatter_dimension=1, tiled=True)[0].astype(F32)
        shards_.append(own)
        low = jnp.sum(jnp.square(stot[16 * n : 16 * n + 13]))
        squares.append(jnp.sum(own * own) + jnp.where(first, low, 0.0))
    sq = lax.psum(jnp.stack(squares), ("section", "dp"))
    return *shards_, stot, jnp.zeros((8, HALF), F32).at[:, 0:2].set(sq)


def shards(
    z_noise, eps_noise, levels, counts,
    gen_w, gen_m, gen_v, gen_ema, gen_small, gen_small_m, gen_small_v, gen_small_ema,
    fake_w, fake_m, fake_v, fake_small, fake_small_m, fake_small_v,
    teacher_w, teacher_small,
):
    if lax.axis_size("dp") == PLANES * PLANE:
        smalls = [a.swapaxes(0, 1) for a in (gen_small, fake_small, teacher_small)]
        reduced = run_step(
            z_noise, eps_noise, levels, counts, gen_w[0], fake_w[0], teacher_w[0], smalls
        )
    else:
        reduced = plain_step(
            z_noise, eps_noise, levels, counts, gen_w, fake_w, teacher_w,
            gen_small, fake_small, teacher_small,
        )
    return update_nets(
        *reduced,
        (
            gen_w, gen_m, gen_v, gen_ema, gen_small, gen_small_m, gen_small_v, gen_small_ema,
            fake_w, fake_m, fake_v, fake_small, fake_small_m, fake_small_v,
        ),
    )


def plain_step(
    z_noise, eps_noise, levels, counts, gen_w, fake_w, teacher_w,
    gen_small, fake_small, teacher_small,
):
    images = z_noise.shape[0] // lax.axis_size("section")
    start = lax.axis_index("section") * images

    def mine(a):
        return lax.dynamic_slice_in_dim(a, start, images, 0)

    z, eps = mine(z_noise), mine(eps_noise)
    sigma = sigma_levels(mine(levels))
    valid = (start + jnp.arange(images) < counts[0]).astype(F32)
    valid_sum = jnp.sum(valid)
    gen_eo = spread_embed(jnp.full((images,), SIGMA_INIT, F32))
    score_eo = spread_embed(sigma)
    gs, fs, ts = [
        lax.all_gather(a, "section", axis=0, tiled=True)
        for a in (gen_small, fake_small, teacher_small)
    ]
    gw, fw, tw = gather_plain(gen_w), gather_plain(fake_w), gather_plain(teacher_w)
    s_in, s_skip, s_out, s_lam = precondition(sigma)
    factor = valid * s_lam / (POS * C)
    s_in, s_skip, s_out, sigma, factor = [
        t[:, None, None] for t in (s_in, s_skip, s_out, sigma, factor)
    ]
    raw = SIGMA_INIT * z
    gen_saved = run_forward(GEN_IN * raw, gw, gs, gen_eo)
    samples = GEN_SKIP * raw + GEN_OUT * gen_saved[0][2]
    noisy = samples + sigma * eps
    x0 = s_in * noisy
    fake_saved = run_forward(x0, fw, fs, score_eo)
    fake_den = s_skip * noisy + s_out * fake_saved[0][2]
    miss = fake_den - samples
    _, fake_g, fake_sg = run_backward(
        s_out * 2.0 * factor * miss, fw, fs, score_eo, fake_saved, True
    )
    teacher_saved = run_forward(x0, tw, ts, score_eo)
    teacher_den = s_skip * noisy + s_out * teacher_saved[0][2]
    gap = teacher_den - fake_den
    loss_gen = jnp.sum(factor * ((1.0 - ALPHA_MIX) * gap * gap + gap * miss))
    loss_fake = jnp.sum(factor * miss * miss)
    grad_teacher = factor * (2.0 * (1.0 - ALPHA_MIX) * gap + miss)
    grad_fake = factor * gap - grad_teacher
    direct = factor * gap * (s_skip - 1.0)
    (back_t,) = run_backward(s_out * grad_teacher, tw, ts, score_eo, teacher_saved, False)
    (back_f,) = run_backward(s_out * grad_fake, fw, fs, score_eo, fake_saved, False)
    gen_cot = GEN_OUT * (direct + s_in * (back_t + back_f))
    _, gen_g, gen_sg = run_backward(gen_cot, gw, gs, gen_eo, gen_saved, True)
    scalars = jnp.broadcast_to(jnp.stack([loss_gen, loss_fake, valid_sum])[:, None], (3, C))
    small_sums = jnp.concatenate(
        [gen_sg[:, :13], jnp.broadcast_to(scalars, (2, 3, C)), fake_sg], axis=1
    )
    return reduce_plain((gen_g, fake_g), small_sums)


def solution(mesh):
    images = P("dp", None, None)
    big = P("section", "dp", None)
    small = P("section", None, None)
    return jax.shard_map(
        shards,
        mesh=mesh,
        in_specs=(images, images, P("dp"), P("dp"))
        + (big,) * 4 + (small,) * 4 + (big,) * 3 + (small,) * 3 + (big, small),
        out_specs=(big,) * 4 + (small,) * 4 + (big,) * 3 + (small,) * 3 + (P(), P()),
        check_vma=False,
    )
```

```python
import functools

import jax
import jax.numpy as jnp
from jax import lax
from jax.experimental import pallas as pl
from jax.experimental.pallas import tpu as pltpu
from jax.sharding import PartitionSpec as P

GROUPS = 32
SIDE = 16
LEVELS = 1000
STEP = 10

SIGMA_DATA = 0.5
SIGMA_INIT = 2.5
SIGMA_LOW = 0.05
SIGMA_HIGH = 20.0
RHO_POWER = 7.0
ALPHA_MIX = 1.2
RS = 0.7071067811865476
NORM_EPS = 1e-05
CLIP_NORM = 0.001
LEARN_RATE = 0.15
BETA_ONE = 0.9
BETA_TWO = 0.999
ADAM_EPS = 1e-08
WEIGHT_DECAY = 0.01

C = 256
HALF = 128
POS = 256
ROWS = 26 * C
CHUNK = 64
PAD = SIDE
F32 = jnp.float32
BF16 = jnp.bfloat16
VMEM_LIMIT = 58 * 2**20
STEP_LIMIT = 63 * 2**20

R_CONV1, R_CONV2, R_EMB, R_QKV, R_PROJ = 0, 9 * C, 18 * C, 22 * C, 25 * C
S_M1, S_I1, S_M2, S_I2, S_M3, S_I3, S_MA, S_MB = range(8)


def sigma_levels(level_ids):
    fraction = level_ids.astype(F32) / (LEVELS - 1)
    top_root = SIGMA_HIGH ** (1.0 / RHO_POWER)
    bottom_root = SIGMA_LOW ** (1.0 / RHO_POWER)
    return (top_root + fraction * (bottom_root - top_root)) ** RHO_POWER


def precondition(sigma_vals):
    total = sigma_vals * sigma_vals + SIGMA_DATA**2
    return (
        lax.rsqrt(total),
        SIGMA_DATA**2 / total,
        sigma_vals * SIGMA_DATA * lax.rsqrt(total),
        total / (sigma_vals * sigma_vals * SIGMA_DATA**2),
    )


def noise_embed(sigma_vals, channel_count):
    frequency = (1.0 / 10000.0) ** (jnp.arange(channel_count, dtype=F32) / channel_count)
    angles = (jnp.log(sigma_vals) / 4.0)[..., None] * frequency
    return jnp.concatenate([jnp.cos(angles), jnp.sin(angles)], axis=-1)


def spread_embed(sigma_vals):
    emb = noise_embed(sigma_vals, C).astype(BF16)
    images = emb.shape[0]
    zero = jnp.zeros_like(emb)
    low = jnp.stack([emb, zero], axis=-1).reshape(images, 4 * C)
    high = jnp.stack([zero, emb], axis=-1).reshape(images, 4 * C)
    fill = jnp.zeros((4 - images, 4 * C), BF16)
    return jnp.concatenate([low, fill, high, fill], axis=0)


def dot_nn(a, b):
    return lax.dot_general(a, b, (((1,), (0,)), ((), ())), preferred_element_type=F32)


def dot_nt(a, b):
    return lax.dot_general(a, b, (((1,), (1,)), ((), ())), preferred_element_type=F32)


def dot_tn(a, b):
    return lax.dot_general(a, b, (((0,), (0,)), ((), ())), preferred_element_type=F32)


def group_mean(v):
    lane = lax.broadcasted_iota(jnp.int32, (8, C), 1)
    for sh in (1, 2, 4):
        v = v + jnp.where((lane & sh) != 0, pltpu.roll(v, sh, 1), pltpu.roll(v, C - sh, 1))
    return v * (1.0 / (POS * 8))


def colsum(v):
    return jnp.sum(v, axis=0, keepdims=True)


def no_pump(l):
    pass


FORWARD_POINTS, BACKWARD_POINTS, WEIGHT_POINTS = 10, 12, 18
HALF_WAY, READY = 8, 13


def stagger(steps, images, between):
    for t in range(len(steps) + images - 1):
        for i in range(images):
            if 0 <= t - i < len(steps):
                steps[t - i](i)
        between()


class Pump:
    def __init__(self, steps, points, layers, lo=0.0, hi=1.0):
        self.table = {l: [[] for _ in range(points)] for l in layers}
        self.at = 0
        for k, step in enumerate(steps):
            place = int((lo + (hi - lo) * (k + 0.5) / len(steps)) * points * len(layers))
            self.table[layers[place // points]][place % points].append(step)

    def __call__(self, l):
        for layer, points in self.table.items():
            if points[self.at]:

                @pl.when(l == layer)
                def _(todo=points[self.at]):
                    for step in todo:
                        step()

        self.at += 1


def put_shifted(bufs, i, r, v):
    rows = v.shape[0]
    at = pl.ds(PAD + r, rows)
    sub = lax.broadcasted_iota(jnp.int32, (rows // SIDE, 8, C), 1)
    x = v.reshape(rows // SIDE, 2, 8, C)
    low, high = x[:, 0], x[:, 1]
    low_up, high_up = pltpu.roll(low, 1, 1), pltpu.roll(high, 1, 1)
    low_down, high_down = pltpu.roll(low, 7, 1), pltpu.roll(high, 7, 1)
    left = (jnp.where(sub == 0, 0.0, low_up), jnp.where(sub == 0, low_up, high_up))
    right = (jnp.where(sub == 7, high_down, low_down), jnp.where(sub == 7, 0.0, high_down))
    bufs[0, i, at, :] = jnp.stack(left, axis=1).reshape(rows, C).astype(BF16)
    bufs[1, i, at, :] = v.astype(BF16)
    bufs[2, i, at, :] = jnp.stack(right, axis=1).reshape(rows, C).astype(BF16)


def taps(bufs, flip):
    images = bufs.shape[1]
    out = []
    for dr in (-1, 0, 1):
        for dc in (-1, 0, 1):
            sr, sc = (-dr, -dc) if flip else (dr, dc)
            piece = bufs[sc + 1, :, PAD + SIDE * sr : PAD + SIDE * sr + POS, :]
            out.append(piece.reshape(images * POS, C))
    return out


def conv_forward(bufs, w, l, row):
    return dot_nn(jnp.concatenate(taps(bufs, False), axis=1), w[l, row : row + 9 * C, :])


def conv_input_grad(bufs, w, l, row):
    parts = [w[l, row + t * C : row + (t + 1) * C, :] for t in range(9)]
    return dot_nt(jnp.concatenate(taps(bufs, True), axis=1), jnp.concatenate(parts, axis=1))


def conv_weight_grad(act_t, bufs, grad, l, row):
    left = act_t[...]
    for t, piece in enumerate(taps(bufs, True)):
        grad[l, row + t * C : row + (t + 1) * C, :] = dot_nn(left, piece).astype(BF16)


def silu(v):
    h = 0.5 * v
    return h + h * jnp.tanh(h)


def silu_parts(v):
    s = 0.5 + 0.5 * jnp.tanh(0.5 * v)
    return s, s * (1.0 + v * (1.0 - s))


def clear_pads(bufs):
    zero = jnp.zeros(bufs.shape[:2] + (PAD, C), BF16)
    bufs[:, :, 0:PAD, :] = zero
    bufs[:, :, PAD + POS :, :] = zero


def split_qkv(w, l, qkvw, tmp):
    for h in range(2):
        tmp[h] = w[l, R_QKV : R_QKV + 3 * C, h * HALF : (h + 1) * HALF].astype(F32)
    for j in range(3):
        for h in range(2):
            at = j * C + h * HALF
            qkvw[:, at : at + HALF] = tmp[h, pl.ds(j, C, stride=3), :].astype(BF16)


def norm_sums(x, pivot=None):
    if pivot is None:
        pivot = x[0:1]
        x = x - pivot
    return colsum(x), colsum(x * x), pivot


def norm_stats(sums):
    fill = [jnp.zeros((8 - len(sums), C), F32)]
    s1, s2, pivot = [jnp.concatenate([a[k] for a in sums] + fill, axis=0) for k in range(3)]
    centre = s1 * (1.0 / POS)
    channel = pivot + centre
    mean = group_mean(channel * POS)
    spread = jnp.maximum(s2 - s1 * centre, 0.0) + jnp.square(channel - mean) * POS
    return mean, lax.rsqrt(group_mean(spread) + NORM_EPS)


def tap_rows(bufs, flip, which):
    out = []
    for dr in (-1, 0, 1):
        for dc in (-1, 0, 1):
            sr, sc = (-dr, -dc) if flip else (dr, dc)
            at = slice(PAD + SIDE * sr, PAD + SIDE * sr + POS)
            piece = jnp.concatenate([bufs[sc + 1, i, at, :] for i in which], axis=0)
            out.append(piece)
    return out


def layer_forward(l, w, small, eo, xs, h1, y, qkv, att, o, st, bufs, nbuf, qkvw, tmp, staged, pump):
    images = h1.shape[1]
    split_qkv(w, l, qkvw, tmp)
    mod = dot_nn(eo[...], w[l, R_EMB : R_EMB + 4 * C, :])
    ma = mod[0:4] + small[l, 5:6, :]
    mb = mod[4:8] + small[l, 6:7, :]
    for i in range(images):
        st[l, i, S_MA : S_MA + 1, :] = ma[i : i + 1]
        st[l, i, S_MB : S_MB + 1, :] = mb[i : i + 1]

    sums = {}

    def row(k):
        return small[l, k : k + 1, :]

    def keep(which, mean, inv, at):
        for k, i in enumerate(which):
            st[l, i, at : at + 1, :] = mean[k : k + 1]
            st[l, i, at + 1 : at + 2, :] = inv[k : k + 1]

    def first(which):
        mean, inv = norm_stats([norm_sums(xs[l, i]) for i in which])
        keep(which, mean, inv, S_M1)
        for k, i in enumerate(which):
            a = inv[k : k + 1] * row(0)
            for r in range(0, POS, CHUNK):
                v = (xs[l, i, r : r + CHUNK, :] - mean[k : k + 1]) * a + row(1)
                put_shifted(bufs, i, r, silu(v))

    def conv(which, at):
        left = jnp.concatenate(tap_rows(bufs, False, which), axis=1)
        return dot_nn(left, w[l, at : at + 9 * C, :])

    def conv_one(which):
        out = conv(which, R_CONV1)
        for k, i in enumerate(which):
            own = out[k * POS : (k + 1) * POS]
            sums[i] = norm_sums(own, row(2))
            h1[l, i] = own + row(2)

    def second(which):
        mean, inv = norm_stats([sums[i] for i in which])
        keep(which, mean, inv, S_M2)
        for k, i in enumerate(which):
            gain = 1.0 + ma[i : i + 1]
            a = inv[k : k + 1] * row(3) * gain
            b = row(4) * gain + mb[i : i + 1]
            for r in range(0, POS, CHUNK):
                v = (h1[l, i, r : r + CHUNK, :] - mean[k : k + 1]) * a + b
                put_shifted(bufs, i, r, silu(v))

    def conv_two(which):
        out = conv(which, R_CONV2) + row(7)
        for k, i in enumerate(which):
            own = (xs[l, i] + out[k * POS : (k + 1) * POS]) * RS
            sums[i] = norm_sums(own)
            y[l, i] = own

    def third(which):
        mean, inv = norm_stats([sums[i] for i in which])
        keep(which, mean, inv, S_M3)
        for k, i in enumerate(which):
            a = inv[k : k + 1] * row(8)
            for r in range(0, POS, CHUNK):
                v = (y[l, i, r : r + CHUNK, :] - mean[k : k + 1]) * a + row(9)
                nbuf[i, r : r + CHUNK, :] = v.astype(BF16)

    def project_in(which):
        n = jnp.concatenate([nbuf[i] for i in which], axis=0)
        for j, at in ((0, 10), (1, None), (2, 11)):
            part = dot_nn(n, qkvw[:, j * C : (j + 1) * C])
            if at is not None:
                part = part + row(at)
            part = part.astype(BF16)
            for k, i in enumerate(which):
                qkv[l, i, :, j * C : (j + 1) * C] = part[k * POS : (k + 1) * POS]

    def attend(which):
        scores = [dot_nt(qkv[l, i, :, 0:C], qkv[l, i, :, C : 2 * C]) for i in which]
        for s, i in zip(scores, which):
            e = jnp.exp((s - jnp.max(s, axis=1, keepdims=True)) * (C**-0.5))
            p = (e * (1.0 / jnp.sum(e, axis=1, keepdims=True))).astype(BF16)
            att[l, i] = p
            o[l, i] = dot_nn(p, qkv[l, i, :, 2 * C :]).astype(BF16)

    def project_out(which):
        left = jnp.concatenate([o[l, i] for i in which], axis=0)
        out = dot_nn(left, w[l, R_PROJ:, :]) + row(12)
        for k, i in enumerate(which):
            xs[l + 1, i] = (y[l, i] + out[k * POS : (k + 1) * POS]) * RS

    steps = (first, conv_one, second, conv_two, third, project_in, attend, project_out)
    if not staged:
        for step in steps:
            step(range(images))
            pump(l)
    else:
        stagger([lambda i, step=step: step([i]) for step in steps], images, lambda: pump(l))


def layer_backward(
    l, w, small, eo, xs, h1, y, qkv, att, o, st, g, bufs, nbuf, qkvw, tmp, dn, dqkv, act_t,
    grad, sgrad, pump, need_dx=None,
):
    want = grad is not None
    images = h1.shape[1]
    which = range(images)
    flat = images * POS
    scale = C**-0.5
    split_qkv(w, l, qkvw, tmp)

    def row(k):
        return small[l, k : k + 1, :]

    def rows8(rows):
        return jnp.concatenate(list(rows) + [jnp.zeros((8 - len(rows), C), F32)], axis=0)

    zero = jnp.zeros((1, C), F32)
    gps, c1, c2, p1, p2 = {}, {}, {}, {}, {}
    total = {7: zero, 2: zero}
    gains = [1.0 + st[l, i, S_MA : S_MA + 1, :] for i in which]

    def one8(v):
        return jnp.broadcast_to(v, (8, C))

    def project_out(i):
        gps[i] = (g[i] * RS).astype(BF16)
        nbuf[i] = dot_nt(gps[i], w[l, R_PROJ:, :]).astype(BF16)

    def attend(i):
        p = att[l, i]
        pf = p.astype(F32)
        dp = dot_nt(nbuf[i], qkv[l, i, :, 2 * C :])
        ds = (pf * (dp - jnp.sum(dp * pf, axis=1, keepdims=True))).astype(BF16)
        dqkv[i, :, 0:C] = (dot_nn(ds, qkv[l, i, :, C : 2 * C]) * scale).astype(BF16)
        dqkv[i, :, C : 2 * C] = (dot_tn(ds, qkv[l, i, :, 0:C]) * scale).astype(BF16)
        dqkv[i, :, 2 * C :] = dot_tn(p, nbuf[i]).astype(BF16)

    def project_in(i):
        mean, inv = st[l, i, S_M3 : S_M3 + 1, :], st[l, i, S_I3 : S_I3 + 1, :]
        d = dot_nt(dqkv[i], qkvw[...])
        dn[i] = d
        c1[i] = colsum(d)
        c2[i] = colsum(d * ((y[l, i] - mean) * inv))

    def third(i):
        mean, inv = st[l, i, S_M3 : S_M3 + 1, :], st[l, i, S_I3 : S_I3 + 1, :]
        mg = group_mean(one8(row(8) * c1[i]))[0:1]
        mc = group_mean(one8(row(8) * c2[i]))[0:1]
        for r in range(0, POS, CHUNK):
            nh = (y[l, i, r : r + CHUNK, :] - mean) * inv
            gm = g[i, r : r + CHUNK, :] * RS + inv * (row(8) * dn[i, r : r + CHUNK, :] - mg - nh * mc)
            gm = gm * RS
            g[i, r : r + CHUNK, :] = gm
            put_shifted(bufs, i, r, gm)
            if want:
                nbuf[i, r : r + CHUNK, :] = (nh * row(8) + row(9)).astype(BF16)
                total[7] = total[7] + colsum(gm)

    def conv_grad(i, at):
        left = jnp.concatenate(tap_rows(bufs, True, [i]), axis=1)
        parts = [w[l, at + t * C : at + (t + 1) * C, :] for t in range(9)]
        dn[i] = dot_nt(left, jnp.concatenate(parts, axis=1))

    def activation(i, src, mean, inv, a, b, act=None):
        s1, s2 = zero, zero
        for r in range(0, POS, CHUNK):
            nh = (src[l, i, r : r + CHUNK, :] - mean) * inv
            pre = nh * a + b
            s, slope = silu_parts(pre)
            d = dn[i, r : r + CHUNK, :] * slope
            dn[i, r : r + CHUNK, :] = d
            s1 = s1 + colsum(d)
            s2 = s2 + colsum(d * nh)
            if act is not None:
                act[i, r : r + CHUNK, :] = (pre * s).astype(BF16)
        p1[i], p2[i] = s1, s2

    def second_a(i):
        mean, inv = st[l, i, S_M2 : S_M2 + 1, :], st[l, i, S_I2 : S_I2 + 1, :]
        b = row(4) * gains[i] + st[l, i, S_MB : S_MB + 1, :]
        activation(i, h1, mean, inv, row(3) * gains[i], b, nbuf if want else None)

    def second_b(i):
        mean, inv = st[l, i, S_M2 : S_M2 + 1, :], st[l, i, S_I2 : S_I2 + 1, :]
        full = row(3) * gains[i]
        mg = group_mean(one8(full * p1[i]))[0:1]
        mc = group_mean(one8(full * p2[i]))[0:1]
        for r in range(0, POS, CHUNK):
            nh = (h1[l, i, r : r + CHUNK, :] - mean) * inv
            dh = inv * (full * dn[i, r : r + CHUNK, :] - mg - nh * mc)
            put_shifted(bufs, i, r, dh)
            if want:
                total[2] = total[2] + colsum(dh)

    def first_a(i):
        mean, inv = st[l, i, S_M1 : S_M1 + 1, :], st[l, i, S_I1 : S_I1 + 1, :]
        activation(i, xs, mean, inv, row(0), row(1))

    def first_act(i):
        mean, inv = st[l, i, S_M1 : S_M1 + 1, :], st[l, i, S_I1 : S_I1 + 1, :]
        for r in range(0, POS, CHUNK):
            v = (xs[l, i, r : r + CHUNK, :] - mean) * (inv * row(0)) + row(1)
            nbuf[i, r : r + CHUNK, :] = silu(v).astype(BF16)

    def first_b(i):
        mean, inv = st[l, i, S_M1 : S_M1 + 1, :], st[l, i, S_I1 : S_I1 + 1, :]
        mg = group_mean(one8(row(0) * p1[i]))[0:1]
        mc = group_mean(one8(row(0) * p2[i]))[0:1]
        for r in range(0, POS, CHUNK):
            nh = (xs[l, i, r : r + CHUNK, :] - mean) * inv
            dx = inv * (row(0) * dn[i, r : r + CHUNK, :] - mg - nh * mc)
            g[i, r : r + CHUNK, :] = g[i, r : r + CHUNK, :] + dx

    upper = [project_out, attend, project_in, third, lambda i: conv_grad(i, R_CONV2)]
    lower = [lambda i: conv_grad(i, R_CONV1), first_a]
    if not want:
        stagger(upper + [second_a, second_b] + lower + [first_b], images, lambda: pump(l))
        return
    stagger(upper, images, lambda: pump(l))
    gp = jnp.concatenate([gps[i] for i in which], axis=0)
    grad[l, R_PROJ:, :] = dot_tn(o[l].reshape(flat, C), gp).astype(BF16)
    sgrad[l, 12:13, :] = colsum(gp.astype(F32))
    sgrad[l, 7:8, :] = total[7]
    sgrad[l, 8:9, :] = colsum(rows8([c2[i] for i in which]))
    sgrad[l, 9:10, :] = colsum(rows8([c1[i] for i in which]))
    act_t[...] = nbuf[...].reshape(flat, C).T
    for j in range(3):
        dj = dqkv[:, :, j * C : (j + 1) * C].reshape(flat, C)
        part = dot_nn(act_t[...], dj)
        for h in range(2):
            tmp[h, pl.ds(j, C, stride=3), :] = part[:, h * HALF : (h + 1) * HALF]
        if j != 1:
            sgrad[l, 10 + j // 2 : 11 + j // 2, :] = colsum(dj.astype(F32))
    for h in range(2):
        grad[l, R_QKV : R_QKV + 3 * C, h * HALF : (h + 1) * HALF] = tmp[h].astype(BF16)
    for i in which:
        second_a(i)
    pump(l)
    act_t[...] = nbuf[...].reshape(flat, C).T
    conv_weight_grad(act_t, bufs, grad, l, R_CONV2)
    p18, p28, modgain = [rows8([a[i] for i in which]) for a in (p1, p2, gains)]
    dma = row(3) * p28 + row(4) * p18
    sgrad[l, 3:4, :] = colsum(modgain * p28)
    sgrad[l, 4:5, :] = colsum(modgain * p18)
    sgrad[l, 5:6, :] = colsum(dma)
    sgrad[l, 6:7, :] = colsum(p18)
    grad[l, R_EMB : R_EMB + 4 * C, :] = embed_grad(
        eo, jnp.concatenate([dma[0:4], p18[0:4]], axis=0)
    ).astype(BF16)
    pump(l)
    stagger([second_b, first_act], images, lambda: pump(l))
    act_t[...] = nbuf[...].reshape(flat, C).T
    conv_weight_grad(act_t, bufs, grad, l, R_CONV1)
    pump(l)
    stagger(lower, images, lambda: pump(l))
    sgrad[l, 2:3, :] = total[2]
    sgrad[l, 0:1, :] = colsum(rows8([p2[i] for i in which]))
    sgrad[l, 1:2, :] = colsum(rows8([p1[i] for i in which]))

    @pl.when(l == 1)
    def _():
        for i in which:
            first_b(i)


def embed_grad(eo, dm):
    parts, rest = [], dm
    for _ in range(3):
        parts.append(rest.astype(BF16))
        rest = rest - parts[-1].astype(F32)
    left = eo[...]
    return dot_tn(jnp.concatenate([left, left], axis=0), jnp.concatenate(parts[:2], axis=0)) + dot_tn(
        left, parts[2]
    )


def saved_shapes(images):
    return [
        jax.ShapeDtypeStruct((3, images, POS, C), F32),
        jax.ShapeDtypeStruct((2, images, POS, C), F32),
        jax.ShapeDtypeStruct((2, images, POS, C), F32),
        jax.ShapeDtypeStruct((2, images, POS, 3 * C), BF16),
        jax.ShapeDtypeStruct((2, images, POS, POS), BF16),
        jax.ShapeDtypeStruct((2, images, POS, C), BF16),
        jax.ShapeDtypeStruct((2, images, 8, C), F32),
    ]


def forward_kernel(staged, x0, w, small, eo, xs, h1, y, qkv, att, o, st, bufs, nbuf, qkvw, tmp):
    clear_pads(bufs)
    xs[0] = x0[...]

    def body(l, _):
        layer_forward(
            l, w, small, eo, xs, h1, y, qkv, att, o, st, bufs, nbuf, qkvw, tmp, staged, no_pump
        )
        return 0

    lax.fori_loop(0, 2, body, 0)


def backward_kernel(want, *refs):
    cot, w, small, eo, xs, h1, y, qkv, att, o, st, g = refs[:12]
    refs = refs[12:]
    if want:
        grad, sgrad = refs[:2]
        refs = refs[2:]
    else:
        grad, sgrad = None, None
    bufs, nbuf, qkvw, tmp, dn, dqkv, act_t = refs
    clear_pads(bufs)
    g[...] = cot[...]
    if want:
        sgrad[...] = jnp.zeros(sgrad.shape, F32)

    def body(k, _):
        layer_backward(
            1 - k, w, small, eo, xs, h1, y, qkv, att, o, st, g, bufs, nbuf, qkvw, tmp, dn,
            dqkv, act_t, grad, sgrad, no_pump,
        )
        return 0

    lax.fori_loop(0, 2, body, 0)


def vm(n):
    return [pl.BlockSpec(memory_space=pltpu.VMEM)] * n


def scratch_forward(images):
    return [
        pltpu.VMEM((3, images, POS + 2 * PAD, C), BF16),
        pltpu.VMEM((images, POS, C), BF16),
        pltpu.VMEM((C, 3 * C), BF16),
        pltpu.VMEM((2, 3 * C, HALF), F32),
    ]


def run_forward(x0, w, small, eo, staged=False):
    images = x0.shape[0]
    return pl.pallas_call(
        functools.partial(forward_kernel, staged),
        out_shape=saved_shapes(images),
        in_specs=vm(4),
        out_specs=vm(7),
        scratch_shapes=scratch_forward(images),
        compiler_params=pltpu.CompilerParams(vmem_limit_bytes=VMEM_LIMIT),
    )(x0, w, small, eo)


def run_backward(cot, w, small, eo, saved, want):
    images = cot.shape[0]
    outs = [jax.ShapeDtypeStruct(cot.shape, F32)]
    if want:
        outs += [
            jax.ShapeDtypeStruct((2, ROWS, C), BF16),
            jax.ShapeDtypeStruct((2, 16, C), F32),
        ]
    return pl.pallas_call(
        functools.partial(backward_kernel, want),
        out_shape=outs,
        in_specs=vm(11),
        out_specs=vm(len(outs)),
        scratch_shapes=scratch_forward(images)
        + [
            pltpu.VMEM((images, POS, C), F32),
            pltpu.VMEM((images, POS, 3 * C), BF16),
            pltpu.VMEM((C, images * POS), BF16),
        ],
        compiler_params=pltpu.CompilerParams(vmem_limit_bytes=VMEM_LIMIT),
    )(cot, w, small, eo, *saved)


PLANES, PLANE = 4, 4
MESH = pl.DeviceIdType.MESH


class Place:
    def __init__(self):
        self.sec = lax.axis_index("section")
        self.d = lax.axis_index("dp")
        self.x = lax.rem(self.d, 2)
        self.y = lax.rem(self.d // 2, 2)
        self.z = self.d // PLANE
        self.seat = self.sec * PLANE + lax.rem(self.d, PLANE)
        self.sib = {"section": 1 - self.sec}
        self.xn = {"dp": self.d + 1 - 2 * self.x}
        self.yn = {"dp": self.d + 2 - 4 * self.y}

    def plane(self, j):
        return lax.rem(self.z + j + PLANES, PLANES)

    def zpeer(self, j):
        return {"dp": self.plane(j) * PLANE + lax.rem(self.d, PLANE)}

    def plane_peer(self, j):
        seat = lax.rem(self.seat + j, 2 * PLANE)
        return {"section": seat // PLANE, "dp": self.z * PLANE + lax.rem(seat, PLANE)}

    def meet(self):
        barrier = pltpu.get_barrier_semaphore()
        others = [self.plane_peer(j) for j in range(1, 8)] + [self.zpeer(j) for j in (1, 2, 3)]
        for other in others:
            pl.semaphore_signal(barrier, inc=1, device_id=other, device_id_type=MESH)
        pl.semaphore_wait(barrier, len(others))


def remote(src, dst, send, recv, target):
    return pltpu.make_async_remote_copy(
        src_ref=src, dst_ref=dst, send_sem=send, recv_sem=recv,
        device_id=target, device_id_type=MESH,
    )


Z1, X1, Y1, X2, Y2, SIB = 0, 3, 7, 11, 15, 19
SLOTS = 23


class Gather:
    def __init__(self, me, net, stage, local_sem, send_sem, recv_sem):
        self.me, self.net, self.stage = me, net, stage
        self.local_sem, self.send_sem, self.recv_sem = local_sem, send_sem, recv_sem
        self.part = stage.shape[0]
        self.half = self.part // 2

    def rows(self, plane, y, x, lo, count):
        at = (plane * PLANE + y * 2 + x) * self.part + lo
        return self.net.at[self.me.sec, pl.ds(pl.multiple_of(at, 16), count)]

    def own(self, j):
        return self.rows(self.me.plane(-j), self.me.y, self.me.x, 0, self.part)

    def send(self, slot, piece, target, src=None):
        src = piece if src is None else src
        remote(src, piece, self.send_sem.at[slot], self.recv_sem.at[slot], target).start()

    def arrived(self, slot, piece):
        remote(
            piece, piece, self.send_sem.at[slot], self.recv_sem.at[slot], self.me.sib
        ).wait_recv()

    def local(self):
        return pltpu.make_async_copy(self.stage, self.own(0), self.local_sem)

    def begin(self):
        me = self.me
        for j in (1, 2, 3):
            self.send(Z1 + j - 1, self.own(0), me.zpeer(j), self.stage)
        for slot, target in ((X1, me.xn), (Y1, me.yn)):
            self.send(slot, self.own(0), target, self.stage)
        self.local().start()

    def phase1(self):
        def step(j):
            me = self.me
            self.arrived(Z1 + j - 1, self.own(j))
            for slot, target in ((X1, me.xn), (Y1, me.yn)):
                self.send(slot + j, self.own(j), target)

        return [lambda j=j: step(j) for j in (1, 2, 3)]

    def phase2(self):
        me, part, half = self.me, self.part, self.half

        def step_x(j):
            plane = me.plane(-j)
            self.arrived(X1 + j, self.rows(plane, me.y, 1 - me.x, 0, part))
            self.send(Y2 + j, self.rows(plane, me.y, 1 - me.x, 0, half), me.yn)

        def step_y(j):
            plane = me.plane(-j)
            self.arrived(Y1 + j, self.rows(plane, 1 - me.y, me.x, 0, part))
            self.send(X2 + j, self.rows(plane, 1 - me.y, me.x, half, half), me.xn)

        return [lambda f=f, j=j: f(j) for j in range(PLANES) for f in (step_x, step_y)]

    def phase3(self):
        def step(j):
            me = self.me
            for slot, lo in ((Y2, 0), (X2, self.half)):
                self.arrived(slot + j, self.rows(me.plane(-j), 1 - me.y, 1 - me.x, lo, self.half))
            if j == 0:
                self.local().wait()
            self.send(SIB + j, self.rows(me.plane(-j), 0, 0, 0, PLANE * self.part), me.sib)

        return [lambda j=j: step(j) for j in range(PLANES)]

    def finish(self):
        def step():
            for j in range(PLANES):
                self.arrived(SIB + j, self.rows(0, 0, 0, 0, PLANE * self.part))

        return [step]

    def drain(self):
        for slot in range(SLOTS):
            count = self.part if slot < X2 else self.half if slot < SIB else PLANE * self.part
            piece = self.rows(0, 0, 0, 0, count)
            remote(
                piece, piece, self.send_sem.at[slot], self.recv_sem.at[slot], self.me.sib
            ).wait_send()


A_SLOT, B_SLOT, C_SLOT, D_SLOT = 0, 4, 20, 28
R_SLOTS = 31


class Reduce:
    def __init__(self, me, big, shard, sib, there, rb, rc, rd, ssem, rsem):
        self.me, self.big, self.shard = me, big, shard
        self.sib, self.there, self.rb, self.rc, self.rd = sib, there, rb, rc, rd
        self.ssem, self.rsem = ssem, rsem
        self.part = shard.shape[0]
        self.half = self.part // 2
        self.span = PLANE * self.part

    def zt(self, k):
        return (3, 2, 0, 1)[k]

    def block(self, k):
        return pl.ds(self.zt(k) * self.span, self.span)

    def piece(self, k, y, x, lo, count):
        at = (self.zt(k) * PLANE + y * 2 + x) * self.part + lo
        return pl.ds(pl.multiple_of(at, 16), count)

    def send(self, src, dst, slot, target):
        remote(src, dst, self.ssem.at[slot], self.rsem.at[slot], target).start()

    def arrived(self, dst, slot):
        remote(dst, dst, self.ssem.at[slot], self.rsem.at[slot], self.me.sib).wait_recv()

    def begin(self):
        for k in range(PLANES):
            self.begin_block(k)

    def begin_block(self, k):
        at = self.block(k)
        self.send(self.big.at[1 - self.me.sec, at], self.there.at[at], A_SLOT + k, self.me.sib)

    def stage_a(self, k):
        me, half = self.me, self.half
        self.arrived(self.sib.at[self.block(k)], A_SLOT + k)
        base = self.zt(k) * self.span

        def body(i, _):
            at = pl.ds(pl.multiple_of(base + i * half, 16), half)
            self.big[me.sec, at, :] = (
                self.big[me.sec, at, :].astype(F32) + self.sib[at, :].astype(F32)
            ).astype(BF16)
            return 0

        lax.fori_loop(0, 2 * PLANE, body, 0)
        for j in range(2):
            self.send(
                self.big.at[me.sec, self.piece(k, 1 - me.y, j, 0, half)], self.rb.at[k, j],
                B_SLOT + 4 * k + j, me.yn,
            )
            self.send(
                self.big.at[me.sec, self.piece(k, j, 1 - me.x, half, half)], self.rb.at[k, 2 + j],
                B_SLOT + 4 * k + 2 + j, me.xn,
            )

    def join(self, where, other):
        self.big[self.me.sec, where, :] = (
            self.big[self.me.sec, where, :].astype(F32) + other.astype(F32)
        ).astype(BF16)

    def stage_c(self, k):
        me, half = self.me, self.half
        for j in range(4):
            self.arrived(self.rb.at[k, j], B_SLOT + 4 * k + j)
            y, x, lo = (me.y, j, 0) if j < 2 else (j - 2, me.x, half)
            self.join(self.piece(k, y, x, lo, half), self.rb[k, j])
        self.send(
            self.big.at[me.sec, self.piece(k, me.y, 1 - me.x, 0, half)], self.rc.at[k, 0],
            C_SLOT + 2 * k, me.xn,
        )
        self.send(
            self.big.at[me.sec, self.piece(k, 1 - me.y, me.x, half, half)], self.rc.at[k, 1],
            C_SLOT + 2 * k + 1, me.yn,
        )

    def stage_d(self, k):
        me, half, zt = self.me, self.half, self.zt(k)
        for j in range(2):
            self.arrived(self.rc.at[k, j], C_SLOT + 2 * k + j)
            self.join(self.piece(k, me.y, me.x, j * half, half), self.rc[k, j])

        @pl.when(me.z != zt)
        def _():
            self.send(
                self.big.at[me.sec, self.piece(k, me.y, me.x, 0, self.part)],
                self.rd.at[lax.rem(zt - me.z + PLANES, PLANES) - 1],
                D_SLOT + lax.rem(zt - me.z + PLANES, PLANES) - 1,
                {"dp": zt * PLANE + lax.rem(me.d, PLANE)},
            )

    def stage_e(self):
        for j in range(PLANES - 1):
            self.arrived(self.rd.at[j], D_SLOT + j)
        at = pl.ds(pl.multiple_of(self.me.d * self.part, 16), self.part)
        self.shard[...] = (
            self.big[self.me.sec, at, :].astype(F32)
            + self.rd[0].astype(F32) + (self.rd[1].astype(F32) + self.rd[2].astype(F32))
        )

    def steps(self):
        out = []
        for t in range(PLANES + 2):
            for stage, lag in ((self.stage_a, 0), (self.stage_c, 1), (self.stage_d, 2)):
                if 0 <= t - lag < PLANES:
                    out.append(lambda stage=stage, k=t - lag: stage(k))
        return out

    def drain(self, lo=0, hi=R_SLOTS):
        for slot in range(lo, hi):
            if slot < B_SLOT:
                piece = self.there.at[pl.ds(0, self.span)]
            elif slot < D_SLOT:
                piece = self.rb.at[0, 0]
            else:
                piece = self.rd.at[0]
            remote(piece, piece, self.ssem.at[slot], self.rsem.at[slot], self.me.sib).wait_send()


def reduce_scratch(part):
    half = part // 2
    return [
        pltpu.VMEM((PLANES, 4, half, C), BF16),
        pltpu.VMEM((PLANES, 2, half, C), BF16),
        pltpu.VMEM((PLANES - 1, part, C), BF16),
        pltpu.SemaphoreType.DMA((R_SLOTS,)),
        pltpu.SemaphoreType.DMA((R_SLOTS,)),
    ]


class Totals:
    def __init__(self, me, buf, recv, ssem, rsem):
        self.me, self.buf, self.recv, self.ssem, self.rsem = me, buf, recv, ssem, rsem

    def send(self, src, dst, slot, target):
        remote(src, dst, self.ssem.at[slot], self.rsem.at[slot], target).start()

    def arrived(self, dst, slot):
        remote(dst, dst, self.ssem.at[slot], self.rsem.at[slot], self.me.sib).wait_recv()

    def begin(self, first):
        self.send(first, self.recv.at[0], 0, self.me.sib)

    def steps(self):
        me, buf, recv = self.me, self.buf, self.recv

        def one():
            self.arrived(recv.at[0], 0)
            buf[1] = buf[0] + recv[0]
            self.send(buf.at[1], recv.at[1], 1, me.xn)

        def two():
            self.arrived(recv.at[1], 1)
            buf[2] = buf[1] + recv[1]
            self.send(buf.at[2], recv.at[2], 2, me.yn)

        def three():
            self.arrived(recv.at[2], 2)
            buf[3] = buf[2] + recv[2]
            recv[3 + me.z] = buf[3]
            for j in (1, 2, 3):
                self.send(buf.at[3], recv.at[3 + me.z], 2 + j, me.zpeer(j))

        return [one, two, three]

    def result(self):
        for j in (1, 2, 3):
            self.arrived(self.recv.at[3 + self.me.plane(-j)], 2 + j)
        return (self.recv[3] + self.recv[4]) + (self.recv[5] + self.recv[6])

    def drain(self):
        for slot in range(6):
            piece = self.recv.at[0]
            remote(piece, piece, self.ssem.at[slot], self.rsem.at[slot], self.me.sib).wait_send()


class Squares:
    def __init__(self, me, own, recv, ssem, rsem):
        self.me, self.own, self.recv, self.ssem, self.rsem = me, own, recv, ssem, rsem

    def hop(self, src, base, mine, peers, slots):
        for j, target in peers:
            dst = self.recv.at[base + mine]
            remote(src, dst, self.ssem.at[slots + j], self.rsem.at[slots + j], target).start()
        self.recv[base + mine] = src[...]
        for j, _ in peers:
            dst = self.recv.at[base]
            remote(dst, dst, self.ssem.at[slots + j], self.rsem.at[slots + j], self.me.sib).wait_recv()

    def run(self):
        me, recv = self.me, self.recv
        self.hop(self.own.at[0], 0, me.seat, [(j, me.plane_peer(j)) for j in range(1, 8)], -1)
        pairs = [recv[2 * k] + recv[2 * k + 1] for k in range(4)]
        self.own[1] = (pairs[0] + pairs[1]) + (pairs[2] + pairs[3])
        self.hop(self.own.at[1], 8, me.z, [(j, me.zpeer(j)) for j in (1, 2, 3)], 6)
        return (recv[8] + recv[9]) + (recv[10] + recv[11])

    def drain(self):
        for slot in range(10):
            piece = self.recv.at[0]
            remote(piece, piece, self.ssem.at[slot], self.rsem.at[slot], self.me.sib).wait_send()


def squares_scratch(shape):
    return [
        pltpu.VMEM((2,) + shape, F32),
        pltpu.VMEM((12,) + shape, F32),
        pltpu.SemaphoreType.DMA((10,)),
        pltpu.SemaphoreType.DMA((10,)),
    ]


def totals_scratch(shape):
    return [
        pltpu.VMEM((4,) + shape, F32),
        pltpu.VMEM((7,) + shape, F32),
        pltpu.SemaphoreType.DMA((6,)),
        pltpu.SemaphoreType.DMA((6,)),
    ]


def saved_scratch(images):
    return [pltpu.VMEM(a.shape, a.dtype) for a in saved_shapes(images)]


def backward_scratch(images):
    return scratch_forward(images) + [
        pltpu.VMEM((images, POS, C), F32),
        pltpu.VMEM((images, POS, 3 * C), BF16),
        pltpu.VMEM((C, images * POS), BF16),
    ]


GEN_TOTAL = SIGMA_INIT**2 + SIGMA_DATA**2
GEN_IN = GEN_TOTAL**-0.5
GEN_SKIP = SIGMA_DATA**2 / GEN_TOTAL
GEN_OUT = SIGMA_INIT * SIGMA_DATA * GEN_TOTAL**-0.5
T_IN, T_SKIP, T_OUT, T_SIGMA, T_FACTOR = range(5)


def fill_embed(eo, sigmas):
    at = lax.broadcasted_iota(jnp.int32, (8, 4 * C), 1)
    side = lax.broadcasted_iota(jnp.int32, (8, 4 * C), 0) // 4
    k = at // 2
    power = (k & (C - 1)).astype(F32) * (1.0 / C)
    rows = sigmas + [jnp.ones_like(sigmas[0])] * (4 - len(sigmas))
    angle = jnp.log(jnp.concatenate(rows + rows, axis=0)) * 0.25 * jnp.exp(power * -LOG_10000)
    wave = jnp.where(k < C, jnp.cos(angle), jnp.sin(angle))
    eo[...] = jnp.where((at & 1) == side, wave, 0.0).astype(BF16)


LOG_10000 = 9.210340371976184


def step_kernel(*refs):
    (
        z_all, eps_all, levels, counts, gen_w, fake_w, teacher_w, gen_small, fake_small,
        teacher_small,
        gw_out, sv_x, sv_h, sv_y, sv_q, sv_a, sv_o, sv_s, gshard, fshard, stot, sqtot,
        *refs,
    ) = refs
    gen_out = (sv_x, sv_h, sv_y, sv_q, sv_a, sv_o, sv_s)
    w_gen, w_fake, w_teach = refs[:3]
    sv_one, sv_two = refs[3:10], refs[10:17]
    bufs, nbuf, qkvw, tmp, dn, dqkv, act_t = refs[17:24]
    zb, eb, g, stage, local_sem, send_sem, recv_sem, copy_sem = refs[24:32]
    smalls, small_sem, gen_eo, score_eo, tab, sgrads, part_sums = refs[32:39]
    fake_refs, gen_refs = refs[39:44], refs[44:49]
    small_refs, square_refs = refs[49:53], refs[53:57]
    sib, free_sem = refs[57:59]
    g2 = sv_two[0].at[2]
    images = zb.shape[0]
    me = Place()
    start = me.sec * images

    def run(steps):
        for step in steps:
            step()

    def mine(ref):
        return ref.at[pl.ds(start, images)]

    loads = [
        pltpu.make_async_copy(mine(z_all), zb, copy_sem.at[0]),
        pltpu.make_async_copy(mine(eps_all), eb, copy_sem.at[1]),
    ]
    for copy in loads:
        copy.start()
    masters = [
        pltpu.make_async_copy(src, dst, copy_sem.at[2 + k])
        for k, (src, dst) in enumerate(((gen_w, gshard), (fake_w, fshard), (teacher_w, stage.at[2])))
    ]
    for copy in masters:
        copy.start()
    smalls[...] = jnp.zeros(smalls.shape, F32)
    for n, ref in enumerate((gen_small, fake_small, teacher_small)):
        for r in range(13):
            smalls[me.sec, n, r : r + 1, :] = ref[r]
    gathers = [
        Gather(me, net, stage.at[n], local_sem.at[n], send_sem.at[n], recv_sem.at[n])
        for n, net in enumerate((w_gen, w_fake, w_teach))
    ]
    for copy in masters:
        copy.wait()
    stage[0] = gshard[...].astype(BF16)
    stage[1] = fshard[...].astype(BF16)
    me.meet()
    gathers[0].begin()
    swap = remote(
        smalls.at[me.sec], smalls.at[me.sec], small_sem.at[0], small_sem.at[1], me.sib
    )
    swap.start()

    clear_pads(bufs)
    sgrads[...] = jnp.zeros(sgrads.shape, F32)
    sigmas = []
    valid_sum = jnp.zeros((1, 4 * C), F32)
    for i in range(images):
        level = jnp.zeros((1, 4 * C), jnp.int32) + levels[start + i]
        sigma = SIGMA_TOP + level.astype(F32) / (LEVELS - 1) * (SIGMA_BOTTOM - SIGMA_TOP)
        square = sigma * sigma
        sigma = square * square * square * sigma
        sigmas.append(sigma)
        s_in, s_skip, s_out, s_lam = precondition(sigma)
        valid = jnp.where(jnp.zeros_like(level) + (start + i) < counts[0], 1.0, 0.0)
        valid_sum = valid_sum + valid
        rows = (s_in, s_skip, s_out, sigma, valid * s_lam * (1.0 / (POS * C)))
        for k, value in enumerate(rows):
            tab[i, k : k + 1, :] = value[:, :C]
    fill_embed(score_eo, sigmas)
    fill_embed(gen_eo, [jnp.full((1, 4 * C), SIGMA_INIT, F32)] * images)

    def forward(n, w, eo, sv, pump):
        def body(l, _):
            layer_forward(
                l, w, smalls.at[:, n], eo, *sv, bufs, nbuf, qkvw, tmp, True, pump
            )
            return 0

        lax.fori_loop(0, 2, body, 0)

    def backward(n, w, eo, sv, cot, grad, sgrad, pump):
        def body(k, _):
            layer_backward(
                1 - k, w, smalls.at[:, n], eo, *sv, cot, bufs, nbuf, qkvw, tmp, dn, dqkv,
                act_t, grad, sgrad, pump,
            )
            return 0

        lax.fori_loop(0, 2, body, 0)

    def each(f):
        def body(i, carry):
            return f(i, [tab[i, k : k + 1, :] for k in range(5)], carry)

        return lax.fori_loop(0, images, body, jnp.zeros((1, C), F32))

    run(gathers[0].phase1() + [gathers[1].begin] + gathers[0].phase2() + gathers[0].phase3())
    for copy in loads:
        copy.wait()
    sv_one[0][0] = zb[...] * (GEN_IN * SIGMA_INIT)
    swap.wait()
    run(gathers[0].finish())
    later = gathers[1].phase1() + [gathers[2].begin] + gathers[1].phase2()
    forward(0, w_gen, gen_eo, sv_one, Pump(later[:8], FORWARD_POINTS, (0, 1)))
    pairs = [(w_gen, gw_out)] + list(zip(sv_one, gen_out))
    stores = [
        pltpu.make_async_copy(src, dst, copy_sem.at[2 + k]) for k, (src, dst) in enumerate(pairs)
    ]
    for copy in stores:
        copy.start()

    def noisy(i, t, carry):
        zb[i] = zb[i] * (GEN_SKIP * SIGMA_INIT) + GEN_OUT * sv_one[0][2, i]
        eb[i] = zb[i] + t[T_SIGMA] * eb[i]
        sv_two[0][0, i] = t[T_IN] * eb[i]
        return carry

    each(noisy)
    run(later[8:] + gathers[1].phase3() + gathers[1].finish())
    later = gathers[2].phase1() + gathers[2].phase2()
    forward(1, w_fake, score_eo, sv_two, Pump(later[:9], FORWARD_POINTS, (0, 1)))
    later = later[9:] + gathers[2].phase3()

    def fake_loss(i, t, total):
        den = t[T_SKIP] * eb[i] + t[T_OUT] * sv_two[0][2, i]
        sv_two[0][2, i] = den
        miss = den - zb[i]
        g[i] = (2.0 * t[T_OUT] * t[T_FACTOR]) * miss
        return total + t[T_FACTOR] * colsum(miss * miss)

    loss_fake = each(fake_loss)
    for copy in stores:
        copy.wait()
    gathers[0].drain()
    backward(
        1, w_fake, score_eo, sv_two, g, w_gen, sgrads.at[:, 1],
        Pump(later, WEIGHT_POINTS, (1, 0)),
    )
    fake_sum = Reduce(me, w_gen, fshard, sib, sib, *fake_refs)
    fake_sum.begin()
    run(gathers[2].finish())
    later = fake_sum.steps()
    sv_one[0][0] = sv_two[0][0]
    forward(2, w_teach, score_eo, sv_one, Pump(later[:5], FORWARD_POINTS, (0, 1), 0.2))

    def gen_loss(i, t, total):
        den = t[T_SKIP] * eb[i] + t[T_OUT] * sv_one[0][2, i]
        fake_den = sv_two[0][2, i]
        miss = fake_den - zb[i]
        gap = den - fake_den
        scale = t[T_OUT] * t[T_FACTOR]
        g[i] = scale * ((2.0 * (1.0 - ALPHA_MIX)) * gap + miss)
        g2[i] = scale * ((1.0 - 2.0 * (1.0 - ALPHA_MIX)) * gap - miss)
        zb[i] = (t[T_FACTOR] * (t[T_SKIP] - 1.0)) * gap
        return total + t[T_FACTOR] * colsum(gap * ((1.0 - ALPHA_MIX) * gap + miss))

    loss_gen = each(gen_loss)
    backward(
        2, w_teach, score_eo, sv_one, g, None, None, Pump(later[5:9], BACKWARD_POINTS, (1, 0))
    )
    gathers[2].drain()
    fake_sum.drain(A_SLOT, B_SLOT)
    pl.semaphore_signal(free_sem, inc=1, device_id=me.sib, device_id_type=MESH)
    back = [
        pltpu.make_async_copy(src, dst, copy_sem.at[2 + k])
        for k, (dst, src) in enumerate([(w_teach, gw_out)] + list(zip(sv_one, gen_out)))
    ]
    for copy in back:
        copy.start()
    backward(
        1, w_fake, score_eo, sv_two, g2, None, None, Pump(later[9:], BACKWARD_POINTS, (1, 0))
    )

    def gen_gradient(i, t, carry):
        g[i] = GEN_OUT * (zb[i] + t[T_IN] * (g[i] + g2[i]))
        return carry

    each(gen_gradient)
    gathers[1].drain()
    for copy in back:
        copy.wait()

    gen_sum = Reduce(me, w_fake, gshard, w_gen.at[1 - me.sec], w_gen.at[me.sec], *gen_refs)
    later = gen_sum.steps()

    def on_section(s, steps):
        pl.when(me.sec == s)(lambda: run(steps))

    def hand_over():
        pl.semaphore_wait(free_sem, 1)

    pump = Pump([], WEIGHT_POINTS, (1, 0))

    def at(layer, point, section, steps):
        pump.table[layer][point].append(lambda: on_section(section, steps))

    upper = [hand_over, lambda: gen_sum.begin_block(0), lambda: gen_sum.begin_block(1)]
    lower = [lambda: gen_sum.begin_block(2), lambda: gen_sum.begin_block(3)]
    for layer, giver in ((1, 0), (0, 1)):
        at(layer, HALF_WAY, giver, upper)
        at(layer, READY - 1, 1 - giver, later[0:1])
        at(layer, READY, giver, lower)
        at(layer, READY, 1 - giver, later[1:3])
        at(layer, READY + 2, 1 - giver, later[3:4])
        at(layer, READY + 3, 1 - giver, later[4:6])
        at(layer, READY + 4, 1 - giver, later[6:7])
    for k in range(7, 12):
        at(0, k - 7, 1, later[k : k + 1])
    backward(0, w_teach, gen_eo, sv_one, g, w_fake, sgrads.at[:, 0], pump)

    def spread_sum(total):
        return jnp.broadcast_to(jnp.sum(total, axis=1, keepdims=True), (1, C))

    sums = jnp.concatenate([spread_sum(loss_gen), spread_sum(loss_fake), valid_sum[:, :C]], axis=0)
    for s in range(2):
        part_sums[s, 0:16, :] = sgrads[s, 0]
        part_sums[s, 13:16, :] = sums
        part_sums[s, 16:32, :] = sgrads[s, 1]
    small = Totals(me, *small_refs)
    small_refs[0][0] = part_sums[me.sec]
    small.begin(part_sums.at[1 - me.sec])
    fake_sum.stage_e()
    small_steps = small.steps()
    on_section(0, later[7:8])
    run(small_steps[:1])
    on_section(0, later[8:9])
    run(small_steps[1:2])
    on_section(0, later[9:10])
    run(small_steps[2:])
    on_section(0, later[10:])
    stot[...] = small.result()
    own = square_refs[0]
    keep = lax.broadcasted_iota(jnp.int32, (16, C), 0) < 13
    for n, rows in ((1, fshard), (0, gshard)):
        if n == 0:
            gen_sum.stage_e()
        low = jnp.square(jnp.where(keep, stot[16 * n : 16 * n + 16, :], 0.0))
        low = jnp.where(me.d == 0, low[0:8] + low[8:16], 0.0)
        big = jnp.sum(jnp.square(rows[...]).reshape(rows.shape[0] // 8, 8, C), axis=0)
        own[0, 8 * n : 8 * n + 8, :] = big + low
    square = Squares(me, *square_refs)
    sqtot[...] = square.run()
    fake_sum.drain(B_SLOT)
    for done in (gen_sum, small, square):
        done.drain()


SIGMA_TOP = SIGMA_HIGH ** (1.0 / RHO_POWER)
SIGMA_BOTTOM = SIGMA_LOW ** (1.0 / RHO_POWER)


def run_step(z, eps, levels, counts, gen_w, fake_w, teacher_w, smalls):
    part = gen_w.shape[0]
    images = z.shape[0] // 2
    any_ = pl.BlockSpec(memory_space=pl.ANY)
    smem = pl.BlockSpec(memory_space=pltpu.SMEM)
    saved = saved_shapes(images)
    return pl.pallas_call(
        step_kernel,
        out_shape=[jax.ShapeDtypeStruct((2, ROWS, C), BF16)]
        + saved
        + [
            jax.ShapeDtypeStruct((part, C), F32),
            jax.ShapeDtypeStruct((part, C), F32),
            jax.ShapeDtypeStruct((32, C), F32),
            jax.ShapeDtypeStruct((16, C), F32),
        ],
        in_specs=[any_] * 2 + [smem] * 2 + [any_] * 3 + vm(3),
        out_specs=[any_] * 8 + vm(4),
        scratch_shapes=[pltpu.VMEM((2, ROWS, C), BF16)] * 3
        + saved_scratch(images) * 2
        + backward_scratch(images)
        + [pltpu.VMEM((images, POS, C), F32)] * 3
        + [
            pltpu.VMEM((3, part, C), BF16),
            pltpu.SemaphoreType.DMA((3,)),
            pltpu.SemaphoreType.DMA((3, SLOTS)),
            pltpu.SemaphoreType.DMA((3, SLOTS)),
            pltpu.SemaphoreType.DMA((10,)),
            pltpu.VMEM((2, 3, 16, C), F32),
            pltpu.SemaphoreType.DMA((2,)),
            pltpu.VMEM((8, 4 * C), BF16),
            pltpu.VMEM((8, 4 * C), BF16),
            pltpu.VMEM((images, 8, C), F32),
            pltpu.VMEM((2, 2, 16, C), F32),
            pltpu.VMEM((2, 32, C), F32),
        ]
        + reduce_scratch(part) * 2
        + totals_scratch((32, C))
        + squares_scratch((16, C))
        + [pltpu.VMEM((ROWS, C), BF16), pltpu.SemaphoreType.REGULAR],
        compiler_params=pltpu.CompilerParams(
            collective_id=0, has_side_effects=True, vmem_limit_bytes=STEP_LIMIT
        ),
    )(z, eps, levels, counts, gen_w, fake_w, teacher_w, *smalls)[8:]


def adam_step(master, first_mom, second_mom, grad):
    first_new = BETA_ONE * first_mom + (1.0 - BETA_ONE) * grad
    second_new = BETA_TWO * second_mom + (1.0 - BETA_TWO) * grad * grad
    direction = (
        first_new
        / (1.0 - BETA_ONE**STEP)
        / (jnp.sqrt(second_new / (1.0 - BETA_TWO**STEP)) + ADAM_EPS)
    )
    return (master - LEARN_RATE * (direction + WEIGHT_DECAY * master), first_new, second_new)


EMA_RATE = 0.5 ** (20.0 / STEP)
SMALL_STATES = (4, 5, 6, 7, 11, 12, 13)


def update_kernel(gshard, fshard, stot, sqtot, *refs):
    ins, outs = refs[:14], refs[14:]
    norms, losses = outs[14:]
    count = stot[15:16, 0:1]
    norm_of, scales = [], []
    for n in range(2):
        rows = jnp.sum(sqtot[8 * n : 8 * n + 8, :], axis=0, keepdims=True)
        norm = jnp.sqrt(jnp.sum(rows, axis=1, keepdims=True)) / count
        scales.append(jnp.minimum(1.0, CLIP_NORM / norm) / count)
        norm_of.append(norm)

    def one(at, grad, w, m, v, ema, ow, om, ov, oe):
        new, first, second = adam_step(w[at], m[at], v[at], grad)
        ow[at] = new
        om[at] = first
        ov[at] = second
        if ema is not None:
            oe[at] = EMA_RATE * ema[at] + (1.0 - EMA_RATE) * new

    one(0, gshard[...] * scales[0], *ins[0:4], *outs[0:4])
    one(0, fshard[...] * scales[1], *ins[8:11], None, *outs[8:11], None)

    @pl.when(pl.program_id(0) == 0)
    def _():
        for n in range(2):
            norms[n] = norm_of[n][0, 0]
            losses[n] = (stot[13 + n : 14 + n, 0:1] / count)[0, 0]
        for k in range(13):
            one(k, stot[k : k + 1, :] * scales[0], *ins[4:8], *outs[4:8])
            one(k, stot[16 + k : 17 + k, :] * scales[1], *ins[11:14], None, *outs[11:14], None)


def update_nets(gshard, fshard, stot, sqtot, states):
    def turned(arrays):
        return [a.swapaxes(0, 1) if k in SMALL_STATES else a for k, a in enumerate(arrays)]

    part = gshard.shape[0]
    steps = 4 if part % 32 == 0 else 1
    big = pl.BlockSpec((1, part // steps, C), lambda i: (0, i, 0))
    low = pl.BlockSpec((13, 1, C), lambda i: (0, 0, 0))
    shard = pl.BlockSpec((part // steps, C), lambda i: (i, 0))
    whole = [pl.BlockSpec(a.shape, lambda i: (0, 0)) for a in (stot, sqtot)]
    specs = [low if k in SMALL_STATES else big for k in range(len(states))]
    states = turned(states)
    res = pl.pallas_call(
        update_kernel,
        grid=(steps,),
        out_shape=[jax.ShapeDtypeStruct(a.shape, F32) for a in states]
        + [jax.ShapeDtypeStruct((2,), F32)] * 2,
        in_specs=[shard] * 2 + whole + specs,
        out_specs=specs + [pl.BlockSpec(memory_space=pltpu.SMEM)] * 2,
        compiler_params=pltpu.CompilerParams(vmem_limit_bytes=VMEM_LIMIT),
    )(gshard, fshard, stot, sqtot, *states)
    return tuple(turned(res[:-2])) + tuple(res[-2:])


def gather_plain(shard):
    rows = lax.all_gather(shard.astype(BF16), "dp", axis=1, tiled=True)
    return lax.all_gather(rows, "section", axis=0, tiled=True)


def reduce_plain(bigs, small):
    shards_, squares = [], []
    own = lax.psum_scatter(small, "section", scatter_dimension=0, tiled=True)
    stot = lax.psum(own, "dp")[0]
    first = lax.axis_index("dp") == 0
    for n, big in enumerate(bigs):
        own = lax.psum_scatter(big, "section", scatter_dimension=0, tiled=True)
        own = lax.psum_scatter(own, "dp", scatter_dimension=1, tiled=True)[0].astype(F32)
        shards_.append(own)
        low = jnp.sum(jnp.square(stot[16 * n : 16 * n + 13]))
        squares.append(jnp.sum(own * own) + jnp.where(first, low, 0.0))
    sq = lax.psum(jnp.stack(squares), ("section", "dp"))
    return *shards_, stot, jnp.zeros((16, C), F32).at[jnp.array([0, 8]), 0].set(sq)


def shards(
    z_noise, eps_noise, levels, counts,
    gen_w, gen_m, gen_v, gen_ema, gen_small, gen_small_m, gen_small_v, gen_small_ema,
    fake_w, fake_m, fake_v, fake_small, fake_small_m, fake_small_v,
    teacher_w, teacher_small,
):
    if lax.axis_size("dp") == PLANES * PLANE:
        smalls = [a.swapaxes(0, 1) for a in (gen_small, fake_small, teacher_small)]
        reduced = run_step(
            z_noise, eps_noise, levels, counts, gen_w[0], fake_w[0], teacher_w[0], smalls
        )
    else:
        reduced = plain_step(
            z_noise, eps_noise, levels, counts, gen_w, fake_w, teacher_w,
            gen_small, fake_small, teacher_small,
        )
    return update_nets(
        *reduced,
        (
            gen_w, gen_m, gen_v, gen_ema, gen_small, gen_small_m, gen_small_v, gen_small_ema,
            fake_w, fake_m, fake_v, fake_small, fake_small_m, fake_small_v,
        ),
    )


def plain_step(
    z_noise, eps_noise, levels, counts, gen_w, fake_w, teacher_w,
    gen_small, fake_small, teacher_small,
):
    images = z_noise.shape[0] // lax.axis_size("section")
    start = lax.axis_index("section") * images

    def mine(a):
        return lax.dynamic_slice_in_dim(a, start, images, 0)

    z, eps = mine(z_noise), mine(eps_noise)
    sigma = sigma_levels(mine(levels))
    valid = (start + jnp.arange(images) < counts[0]).astype(F32)
    valid_sum = jnp.sum(valid)
    gen_eo = spread_embed(jnp.full((images,), SIGMA_INIT, F32))
    score_eo = spread_embed(sigma)
    gs, fs, ts = [
        lax.all_gather(a, "section", axis=0, tiled=True)
        for a in (gen_small, fake_small, teacher_small)
    ]
    gw, fw, tw = gather_plain(gen_w), gather_plain(fake_w), gather_plain(teacher_w)
    s_in, s_skip, s_out, s_lam = precondition(sigma)
    factor = valid * s_lam / (POS * C)
    s_in, s_skip, s_out, sigma, factor = [
        t[:, None, None] for t in (s_in, s_skip, s_out, sigma, factor)
    ]
    raw = SIGMA_INIT * z
    gen_saved = run_forward(GEN_IN * raw, gw, gs, gen_eo)
    samples = GEN_SKIP * raw + GEN_OUT * gen_saved[0][2]
    noisy = samples + sigma * eps
    x0 = s_in * noisy
    fake_saved = run_forward(x0, fw, fs, score_eo)
    fake_den = s_skip * noisy + s_out * fake_saved[0][2]
    miss = fake_den - samples
    _, fake_g, fake_sg = run_backward(
        s_out * 2.0 * factor * miss, fw, fs, score_eo, fake_saved, True
    )
    teacher_saved = run_forward(x0, tw, ts, score_eo)
    teacher_den = s_skip * noisy + s_out * teacher_saved[0][2]
    gap = teacher_den - fake_den
    loss_gen = jnp.sum(factor * ((1.0 - ALPHA_MIX) * gap * gap + gap * miss))
    loss_fake = jnp.sum(factor * miss * miss)
    grad_teacher = factor * (2.0 * (1.0 - ALPHA_MIX) * gap + miss)
    grad_fake = factor * gap - grad_teacher
    direct = factor * gap * (s_skip - 1.0)
    (back_t,) = run_backward(s_out * grad_teacher, tw, ts, score_eo, teacher_saved, False)
    (back_f,) = run_backward(s_out * grad_fake, fw, fs, score_eo, fake_saved, False)
    gen_cot = GEN_OUT * (direct + s_in * (back_t + back_f))
    _, gen_g, gen_sg = run_backward(gen_cot, gw, gs, gen_eo, gen_saved, True)
    scalars = jnp.broadcast_to(jnp.stack([loss_gen, loss_fake, valid_sum])[:, None], (3, C))
    small_sums = jnp.concatenate(
        [gen_sg[:, :13], jnp.broadcast_to(scalars, (2, 3, C)), fake_sg], axis=1
    )
    return reduce_plain((gen_g, fake_g), small_sums)


def solution(mesh):
    images = P("dp", None, None)
    big = P("section", "dp", None)
    small = P("section", None, None)
    return jax.shard_map(
        shards,
        mesh=mesh,
        in_specs=(images, images, P("dp"), P("dp"))
        + (big,) * 4 + (small,) * 4 + (big,) * 3 + (small,) * 3 + (big, small),
        out_specs=(big,) * 4 + (small,) * 4 + (big,) * 3 + (small,) * 3 + (P(), P()),
        check_vma=False,
    )
```

```python
import functools

import jax
import jax.numpy as jnp
from jax import lax
from jax.experimental import pallas as pl
from jax.experimental.pallas import tpu as pltpu
from jax.sharding import PartitionSpec as P

GROUPS = 32
SIDE = 16
LEVELS = 1000
STEP = 10

SIGMA_DATA = 0.5
SIGMA_INIT = 2.5
SIGMA_LOW = 0.05
SIGMA_HIGH = 20.0
RHO_POWER = 7.0
ALPHA_MIX = 1.2
RS = 0.7071067811865476
NORM_EPS = 1e-05
CLIP_NORM = 0.001
LEARN_RATE = 0.15
BETA_ONE = 0.9
BETA_TWO = 0.999
ADAM_EPS = 1e-08
WEIGHT_DECAY = 0.01

C = 256
HALF = 128
POS = 256
ROWS = 26 * C
CHUNK = 64
PAD = SIDE
F32 = jnp.float32
BF16 = jnp.bfloat16
VMEM_LIMIT = 58 * 2**20
STEP_LIMIT = 63 * 2**20

R_CONV1, R_CONV2, R_EMB, R_QKV, R_PROJ = 0, 9 * C, 18 * C, 22 * C, 25 * C
S_M1, S_I1, S_M2, S_I2, S_M3, S_I3, S_MA, S_MB = range(8)


def sigma_levels(level_ids):
    fraction = level_ids.astype(F32) / (LEVELS - 1)
    top_root = SIGMA_HIGH ** (1.0 / RHO_POWER)
    bottom_root = SIGMA_LOW ** (1.0 / RHO_POWER)
    return (top_root + fraction * (bottom_root - top_root)) ** RHO_POWER


def precondition(sigma_vals):
    total = sigma_vals * sigma_vals + SIGMA_DATA**2
    return (
        lax.rsqrt(total),
        SIGMA_DATA**2 / total,
        sigma_vals * SIGMA_DATA * lax.rsqrt(total),
        total / (sigma_vals * sigma_vals * SIGMA_DATA**2),
    )


def noise_embed(sigma_vals, channel_count):
    frequency = (1.0 / 10000.0) ** (jnp.arange(channel_count, dtype=F32) / channel_count)
    angles = (jnp.log(sigma_vals) / 4.0)[..., None] * frequency
    return jnp.concatenate([jnp.cos(angles), jnp.sin(angles)], axis=-1)


def spread_embed(sigma_vals):
    emb = noise_embed(sigma_vals, C).astype(BF16)
    images = emb.shape[0]
    zero = jnp.zeros_like(emb)
    low = jnp.stack([emb, zero], axis=-1).reshape(images, 4 * C)
    high = jnp.stack([zero, emb], axis=-1).reshape(images, 4 * C)
    fill = jnp.zeros((4 - images, 4 * C), BF16)
    return jnp.concatenate([low, fill, high, fill], axis=0)


def dot_nn(a, b):
    return lax.dot_general(a, b, (((1,), (0,)), ((), ())), preferred_element_type=F32)


def dot_nt(a, b):
    return lax.dot_general(a, b, (((1,), (1,)), ((), ())), preferred_element_type=F32)


def dot_tn(a, b):
    return lax.dot_general(a, b, (((0,), (0,)), ((), ())), preferred_element_type=F32)


def group_mean(v):
    lane = lax.broadcasted_iota(jnp.int32, (8, C), 1)
    for sh in (1, 2, 4):
        v = v + jnp.where((lane & sh) != 0, pltpu.roll(v, sh, 1), pltpu.roll(v, C - sh, 1))
    return v * (1.0 / (POS * 8))


def colsum(v):
    return jnp.sum(v, axis=0, keepdims=True)


def no_pump(l):
    pass


FORWARD_POINTS, BACKWARD_POINTS, WEIGHT_POINTS = 10, 12, 18
HALF_WAY, READY = 8, 13


def stagger(steps, images, between):
    for t in range(len(steps) + images - 1):
        for i in range(images):
            if 0 <= t - i < len(steps):
                steps[t - i](i)
        between()


class Pump:
    def __init__(self, steps, points, layers, lo=0.0, hi=1.0):
        self.table = {l: [[] for _ in range(points)] for l in layers}
        self.at = 0
        for k, step in enumerate(steps):
            place = int((lo + (hi - lo) * (k + 0.5) / len(steps)) * points * len(layers))
            self.table[layers[place // points]][place % points].append(step)

    def __call__(self, l):
        for layer, points in self.table.items():
            if points[self.at]:

                @pl.when(l == layer)
                def _(todo=points[self.at]):
                    for step in todo:
                        step()

        self.at += 1


def put_shifted(bufs, i, r, v):
    rows = v.shape[0]
    at = pl.ds(PAD + r, rows)
    sub = lax.broadcasted_iota(jnp.int32, (rows // SIDE, 8, C), 1)
    x = v.reshape(rows // SIDE, 2, 8, C)
    low, high = x[:, 0], x[:, 1]
    low_up, high_up = pltpu.roll(low, 1, 1), pltpu.roll(high, 1, 1)
    low_down, high_down = pltpu.roll(low, 7, 1), pltpu.roll(high, 7, 1)
    left = (jnp.where(sub == 0, 0.0, low_up), jnp.where(sub == 0, low_up, high_up))
    right = (jnp.where(sub == 7, high_down, low_down), jnp.where(sub == 7, 0.0, high_down))
    bufs[0, i, at, :] = jnp.stack(left, axis=1).reshape(rows, C).astype(BF16)
    bufs[1, i, at, :] = v.astype(BF16)
    bufs[2, i, at, :] = jnp.stack(right, axis=1).reshape(rows, C).astype(BF16)


def taps(bufs, flip):
    images = bufs.shape[1]
    out = []
    for dr in (-1, 0, 1):
        for dc in (-1, 0, 1):
            sr, sc = (-dr, -dc) if flip else (dr, dc)
            piece = bufs[sc + 1, :, PAD + SIDE * sr : PAD + SIDE * sr + POS, :]
            out.append(piece.reshape(images * POS, C))
    return out


def conv_forward(bufs, w, l, row):
    return dot_nn(jnp.concatenate(taps(bufs, False), axis=1), w[l, row : row + 9 * C, :])


def conv_input_grad(bufs, w, l, row):
    parts = [w[l, row + t * C : row + (t + 1) * C, :] for t in range(9)]
    return dot_nt(jnp.concatenate(taps(bufs, True), axis=1), jnp.concatenate(parts, axis=1))


def conv_weight_grad(act_t, bufs, grad, l, row):
    left = act_t[...]
    for t, piece in enumerate(taps(bufs, True)):
        grad[l, row + t * C : row + (t + 1) * C, :] = dot_nn(left, piece).astype(BF16)


def silu(v):
    h = 0.5 * v
    return h + h * jnp.tanh(h)


def silu_parts(v):
    s = 0.5 + 0.5 * jnp.tanh(0.5 * v)
    return s, s * (1.0 + v * (1.0 - s))


def clear_pads(bufs):
    zero = jnp.zeros(bufs.shape[:2] + (PAD, C), BF16)
    bufs[:, :, 0:PAD, :] = zero
    bufs[:, :, PAD + POS :, :] = zero


def split_qkv(w, l, qkvw, tmp):
    for h in range(2):
        tmp[h] = w[l, R_QKV : R_QKV + 3 * C, h * HALF : (h + 1) * HALF].astype(F32)
    for j in range(3):
        for h in range(2):
            at = j * C + h * HALF
            qkvw[:, at : at + HALF] = tmp[h, pl.ds(j, C, stride=3), :].astype(BF16)


def norm_sums(x, pivot=None):
    if pivot is None:
        pivot = x[0:1]
        x = x - pivot
    return colsum(x), colsum(x * x), pivot


def norm_stats(sums):
    fill = [jnp.zeros((8 - len(sums), C), F32)]
    s1, s2, pivot = [jnp.concatenate([a[k] for a in sums] + fill, axis=0) for k in range(3)]
    centre = s1 * (1.0 / POS)
    channel = pivot + centre
    mean = group_mean(channel * POS)
    spread = jnp.maximum(s2 - s1 * centre, 0.0) + jnp.square(channel - mean) * POS
    return mean, lax.rsqrt(group_mean(spread) + NORM_EPS)


def tap_rows(bufs, flip, which):
    out = []
    for dr in (-1, 0, 1):
        for dc in (-1, 0, 1):
            sr, sc = (-dr, -dc) if flip else (dr, dc)
            at = slice(PAD + SIDE * sr, PAD + SIDE * sr + POS)
            piece = jnp.concatenate([bufs[sc + 1, i, at, :] for i in which], axis=0)
            out.append(piece)
    return out


def layer_forward(l, w, small, eo, xs, h1, y, qkv, att, o, st, bufs, nbuf, qkvw, tmp, staged, pump):
    images = h1.shape[1]
    split_qkv(w, l, qkvw, tmp)
    mod = dot_nn(eo[...], w[l, R_EMB : R_EMB + 4 * C, :])
    ma = mod[0:4] + small[l, 5:6, :]
    mb = mod[4:8] + small[l, 6:7, :]
    for i in range(images):
        st[l, i, S_MA : S_MA + 1, :] = ma[i : i + 1]
        st[l, i, S_MB : S_MB + 1, :] = mb[i : i + 1]

    sums = {}

    def row(k):
        return small[l, k : k + 1, :]

    def keep(which, mean, inv, at):
        for k, i in enumerate(which):
            st[l, i, at : at + 1, :] = mean[k : k + 1]
            st[l, i, at + 1 : at + 2, :] = inv[k : k + 1]

    def first(which):
        mean, inv = norm_stats([norm_sums(xs[l, i]) for i in which])
        keep(which, mean, inv, S_M1)
        for k, i in enumerate(which):
            a = inv[k : k + 1] * row(0)
            for r in range(0, POS, CHUNK):
                v = (xs[l, i, r : r + CHUNK, :] - mean[k : k + 1]) * a + row(1)
                put_shifted(bufs, i, r, silu(v))

    def conv(which, at):
        left = jnp.concatenate(tap_rows(bufs, False, which), axis=1)
        return dot_nn(left, w[l, at : at + 9 * C, :])

    def conv_one(which):
        out = conv(which, R_CONV1)
        for k, i in enumerate(which):
            own = out[k * POS : (k + 1) * POS]
            sums[i] = norm_sums(own, row(2))
            h1[l, i] = own + row(2)

    def second(which):
        mean, inv = norm_stats([sums[i] for i in which])
        keep(which, mean, inv, S_M2)
        for k, i in enumerate(which):
            gain = 1.0 + ma[i : i + 1]
            a = inv[k : k + 1] * row(3) * gain
            b = row(4) * gain + mb[i : i + 1]
            for r in range(0, POS, CHUNK):
                v = (h1[l, i, r : r + CHUNK, :] - mean[k : k + 1]) * a + b
                put_shifted(bufs, i, r, silu(v))

    def conv_two(which):
        out = conv(which, R_CONV2) + row(7)
        for k, i in enumerate(which):
            own = (xs[l, i] + out[k * POS : (k + 1) * POS]) * RS
            sums[i] = norm_sums(own)
            y[l, i] = own

    def third(which):
        mean, inv = norm_stats([sums[i] for i in which])
        keep(which, mean, inv, S_M3)
        for k, i in enumerate(which):
            a = inv[k : k + 1] * row(8)
            for r in range(0, POS, CHUNK):
                v = (y[l, i, r : r + CHUNK, :] - mean[k : k + 1]) * a + row(9)
                nbuf[i, r : r + CHUNK, :] = v.astype(BF16)

    def project_in(which):
        n = jnp.concatenate([nbuf[i] for i in which], axis=0)
        for j, at in ((0, 10), (1, None), (2, 11)):
            part = dot_nn(n, qkvw[:, j * C : (j + 1) * C])
            if at is not None:
                part = part + row(at)
            part = part.astype(BF16)
            for k, i in enumerate(which):
                qkv[l, i, :, j * C : (j + 1) * C] = part[k * POS : (k + 1) * POS]

    def attend(which):
        scores = [dot_nt(qkv[l, i, :, 0:C], qkv[l, i, :, C : 2 * C]) for i in which]
        for s, i in zip(scores, which):
            e = jnp.exp((s - jnp.max(s, axis=1, keepdims=True)) * (C**-0.5))
            p = (e * (1.0 / jnp.sum(e, axis=1, keepdims=True))).astype(BF16)
            att[l, i] = p
            o[l, i] = dot_nn(p, qkv[l, i, :, 2 * C :]).astype(BF16)

    def project_out(which):
        left = jnp.concatenate([o[l, i] for i in which], axis=0)
        out = dot_nn(left, w[l, R_PROJ:, :]) + row(12)
        for k, i in enumerate(which):
            xs[l + 1, i] = (y[l, i] + out[k * POS : (k + 1) * POS]) * RS

    steps = (first, conv_one, second, conv_two, third, project_in, attend, project_out)
    if not staged:
        for step in steps:
            step(range(images))
            pump(l)
    else:
        stagger([lambda i, step=step: step([i]) for step in steps], images, lambda: pump(l))


def layer_backward(
    l, w, small, eo, xs, h1, y, qkv, att, o, st, g, bufs, nbuf, qkvw, tmp, dn, dqkv, act_t,
    grad, sgrad, pump, need_dx=None,
):
    want = grad is not None
    images = h1.shape[1]
    which = range(images)
    flat = images * POS
    scale = C**-0.5
    split_qkv(w, l, qkvw, tmp)

    def row(k):
        return small[l, k : k + 1, :]

    def rows8(rows):
        return jnp.concatenate(list(rows) + [jnp.zeros((8 - len(rows), C), F32)], axis=0)

    zero = jnp.zeros((1, C), F32)
    gps, c1, c2, p1, p2 = {}, {}, {}, {}, {}
    total = {7: zero, 2: zero}
    gains = [1.0 + st[l, i, S_MA : S_MA + 1, :] for i in which]

    def one8(v):
        return jnp.broadcast_to(v, (8, C))

    def project_out(i):
        gps[i] = (g[i] * RS).astype(BF16)
        nbuf[i] = dot_nt(gps[i], w[l, R_PROJ:, :]).astype(BF16)

    def attend(i):
        p = att[l, i]
        pf = p.astype(F32)
        dp = dot_nt(nbuf[i], qkv[l, i, :, 2 * C :])
        ds = (pf * (dp - jnp.sum(dp * pf, axis=1, keepdims=True))).astype(BF16)
        dqkv[i, :, 0:C] = (dot_nn(ds, qkv[l, i, :, C : 2 * C]) * scale).astype(BF16)
        dqkv[i, :, C : 2 * C] = (dot_tn(ds, qkv[l, i, :, 0:C]) * scale).astype(BF16)
        dqkv[i, :, 2 * C :] = dot_tn(p, nbuf[i]).astype(BF16)

    def project_in(i):
        mean, inv = st[l, i, S_M3 : S_M3 + 1, :], st[l, i, S_I3 : S_I3 + 1, :]
        d = dot_nt(dqkv[i], qkvw[...])
        dn[i] = d
        c1[i] = colsum(d)
        c2[i] = colsum(d * ((y[l, i] - mean) * inv))

    def third(i):
        mean, inv = st[l, i, S_M3 : S_M3 + 1, :], st[l, i, S_I3 : S_I3 + 1, :]
        mg = group_mean(one8(row(8) * c1[i]))[0:1]
        mc = group_mean(one8(row(8) * c2[i]))[0:1]
        for r in range(0, POS, CHUNK):
            nh = (y[l, i, r : r + CHUNK, :] - mean) * inv
            gm = g[i, r : r + CHUNK, :] * RS + inv * (row(8) * dn[i, r : r + CHUNK, :] - mg - nh * mc)
            gm = gm * RS
            g[i, r : r + CHUNK, :] = gm
            put_shifted(bufs, i, r, gm)
            if want:
                nbuf[i, r : r + CHUNK, :] = (nh * row(8) + row(9)).astype(BF16)
                total[7] = total[7] + colsum(gm)

    def conv_grad(i, at):
        left = jnp.concatenate(tap_rows(bufs, True, [i]), axis=1)
        parts = [w[l, at + t * C : at + (t + 1) * C, :] for t in range(9)]
        dn[i] = dot_nt(left, jnp.concatenate(parts, axis=1))

    def activation(i, src, mean, inv, a, b, act=None):
        s1, s2 = zero, zero
        for r in range(0, POS, CHUNK):
            nh = (src[l, i, r : r + CHUNK, :] - mean) * inv
            pre = nh * a + b
            s, slope = silu_parts(pre)
            d = dn[i, r : r + CHUNK, :] * slope
            dn[i, r : r + CHUNK, :] = d
            s1 = s1 + colsum(d)
            s2 = s2 + colsum(d * nh)
            if act is not None:
                act[i, r : r + CHUNK, :] = (pre * s).astype(BF16)
        p1[i], p2[i] = s1, s2

    def second_a(i):
        mean, inv = st[l, i, S_M2 : S_M2 + 1, :], st[l, i, S_I2 : S_I2 + 1, :]
        b = row(4) * gains[i] + st[l, i, S_MB : S_MB + 1, :]
        activation(i, h1, mean, inv, row(3) * gains[i], b, nbuf if want else None)

    def second_b(i):
        mean, inv = st[l, i, S_M2 : S_M2 + 1, :], st[l, i, S_I2 : S_I2 + 1, :]
        full = row(3) * gains[i]
        mg = group_mean(one8(full * p1[i]))[0:1]
        mc = group_mean(one8(full * p2[i]))[0:1]
        for r in range(0, POS, CHUNK):
            nh = (h1[l, i, r : r + CHUNK, :] - mean) * inv
            dh = inv * (full * dn[i, r : r + CHUNK, :] - mg - nh * mc)
            put_shifted(bufs, i, r, dh)
            if want:
                total[2] = total[2] + colsum(dh)

    def first_a(i):
        mean, inv = st[l, i, S_M1 : S_M1 + 1, :], st[l, i, S_I1 : S_I1 + 1, :]
        activation(i, xs, mean, inv, row(0), row(1))

    def first_act(i):
        mean, inv = st[l, i, S_M1 : S_M1 + 1, :], st[l, i, S_I1 : S_I1 + 1, :]
        for r in range(0, POS, CHUNK):
            v = (xs[l, i, r : r + CHUNK, :] - mean) * (inv * row(0)) + row(1)
            nbuf[i, r : r + CHUNK, :] = silu(v).astype(BF16)

    def first_b(i):
        mean, inv = st[l, i, S_M1 : S_M1 + 1, :], st[l, i, S_I1 : S_I1 + 1, :]
        mg = group_mean(one8(row(0) * p1[i]))[0:1]
        mc = group_mean(one8(row(0) * p2[i]))[0:1]
        for r in range(0, POS, CHUNK):
            nh = (xs[l, i, r : r + CHUNK, :] - mean) * inv
            dx = inv * (row(0) * dn[i, r : r + CHUNK, :] - mg - nh * mc)
            g[i, r : r + CHUNK, :] = g[i, r : r + CHUNK, :] + dx

    upper = [project_out, attend, project_in, third, lambda i: conv_grad(i, R_CONV2)]
    lower = [lambda i: conv_grad(i, R_CONV1), first_a]
    if not want:
        stagger(upper + [second_a, second_b] + lower + [first_b], images, lambda: pump(l))
        return
    stagger(upper, images, lambda: pump(l))
    gp = jnp.concatenate([gps[i] for i in which], axis=0)
    grad[l, R_PROJ:, :] = dot_tn(o[l].reshape(flat, C), gp).astype(BF16)
    sgrad[l, 12:13, :] = colsum(gp.astype(F32))
    sgrad[l, 7:8, :] = total[7]
    sgrad[l, 8:9, :] = colsum(rows8([c2[i] for i in which]))
    sgrad[l, 9:10, :] = colsum(rows8([c1[i] for i in which]))
    act_t[...] = nbuf[...].reshape(flat, C).T
    for j in range(3):
        dj = dqkv[:, :, j * C : (j + 1) * C].reshape(flat, C)
        part = dot_nn(act_t[...], dj)
        for h in range(2):
            tmp[h, pl.ds(j, C, stride=3), :] = part[:, h * HALF : (h + 1) * HALF]
        if j != 1:
            sgrad[l, 10 + j // 2 : 11 + j // 2, :] = colsum(dj.astype(F32))
    for h in range(2):
        grad[l, R_QKV : R_QKV + 3 * C, h * HALF : (h + 1) * HALF] = tmp[h].astype(BF16)
    for i in which:
        second_a(i)
    pump(l)
    act_t[...] = nbuf[...].reshape(flat, C).T
    conv_weight_grad(act_t, bufs, grad, l, R_CONV2)
    p18, p28, modgain = [rows8([a[i] for i in which]) for a in (p1, p2, gains)]
    dma = row(3) * p28 + row(4) * p18
    sgrad[l, 3:4, :] = colsum(modgain * p28)
    sgrad[l, 4:5, :] = colsum(modgain * p18)
    sgrad[l, 5:6, :] = colsum(dma)
    sgrad[l, 6:7, :] = colsum(p18)
    grad[l, R_EMB : R_EMB + 4 * C, :] = embed_grad(
        eo, jnp.concatenate([dma[0:4], p18[0:4]], axis=0)
    ).astype(BF16)
    pump(l)
    stagger([second_b, first_act], images, lambda: pump(l))
    act_t[...] = nbuf[...].reshape(flat, C).T
    conv_weight_grad(act_t, bufs, grad, l, R_CONV1)
    pump(l)
    stagger(lower, images, lambda: pump(l))
    sgrad[l, 2:3, :] = total[2]
    sgrad[l, 0:1, :] = colsum(rows8([p2[i] for i in which]))
    sgrad[l, 1:2, :] = colsum(rows8([p1[i] for i in which]))

    @pl.when(l == 1)
    def _():
        for i in which:
            first_b(i)


def embed_grad(eo, dm):
    parts, rest = [], dm
    for _ in range(3):
        parts.append(rest.astype(BF16))
        rest = rest - parts[-1].astype(F32)
    left = eo[...]
    return dot_tn(jnp.concatenate([left, left], axis=0), jnp.concatenate(parts[:2], axis=0)) + dot_tn(
        left, parts[2]
    )


def saved_shapes(images):
    return [
        jax.ShapeDtypeStruct((3, images, POS, C), F32),
        jax.ShapeDtypeStruct((2, images, POS, C), F32),
        jax.ShapeDtypeStruct((2, images, POS, C), F32),
        jax.ShapeDtypeStruct((2, images, POS, 3 * C), BF16),
        jax.ShapeDtypeStruct((2, images, POS, POS), BF16),
        jax.ShapeDtypeStruct((2, images, POS, C), BF16),
        jax.ShapeDtypeStruct((2, images, 8, C), F32),
    ]


def forward_kernel(staged, x0, w, small, eo, xs, h1, y, qkv, att, o, st, bufs, nbuf, qkvw, tmp):
    clear_pads(bufs)
    xs[0] = x0[...]

    def body(l, _):
        layer_forward(
            l, w, small, eo, xs, h1, y, qkv, att, o, st, bufs, nbuf, qkvw, tmp, staged, no_pump
        )
        return 0

    lax.fori_loop(0, 2, body, 0)


def backward_kernel(want, *refs):
    cot, w, small, eo, xs, h1, y, qkv, att, o, st, g = refs[:12]
    refs = refs[12:]
    if want:
        grad, sgrad = refs[:2]
        refs = refs[2:]
    else:
        grad, sgrad = None, None
    bufs, nbuf, qkvw, tmp, dn, dqkv, act_t = refs
    clear_pads(bufs)
    g[...] = cot[...]
    if want:
        sgrad[...] = jnp.zeros(sgrad.shape, F32)

    def body(k, _):
        layer_backward(
            1 - k, w, small, eo, xs, h1, y, qkv, att, o, st, g, bufs, nbuf, qkvw, tmp, dn,
            dqkv, act_t, grad, sgrad, no_pump,
        )
        return 0

    lax.fori_loop(0, 2, body, 0)


def vm(n):
    return [pl.BlockSpec(memory_space=pltpu.VMEM)] * n


def scratch_forward(images):
    return [
        pltpu.VMEM((3, images, POS + 2 * PAD, C), BF16),
        pltpu.VMEM((images, POS, C), BF16),
        pltpu.VMEM((C, 3 * C), BF16),
        pltpu.VMEM((2, 3 * C, HALF), F32),
    ]


def run_forward(x0, w, small, eo, staged=False):
    images = x0.shape[0]
    return pl.pallas_call(
        functools.partial(forward_kernel, staged),
        out_shape=saved_shapes(images),
        in_specs=vm(4),
        out_specs=vm(7),
        scratch_shapes=scratch_forward(images),
        compiler_params=pltpu.CompilerParams(vmem_limit_bytes=VMEM_LIMIT),
    )(x0, w, small, eo)


def run_backward(cot, w, small, eo, saved, want):
    images = cot.shape[0]
    outs = [jax.ShapeDtypeStruct(cot.shape, F32)]
    if want:
        outs += [
            jax.ShapeDtypeStruct((2, ROWS, C), BF16),
            jax.ShapeDtypeStruct((2, 16, C), F32),
        ]
    return pl.pallas_call(
        functools.partial(backward_kernel, want),
        out_shape=outs,
        in_specs=vm(11),
        out_specs=vm(len(outs)),
        scratch_shapes=scratch_forward(images)
        + [
            pltpu.VMEM((images, POS, C), F32),
            pltpu.VMEM((images, POS, 3 * C), BF16),
            pltpu.VMEM((C, images * POS), BF16),
        ],
        compiler_params=pltpu.CompilerParams(vmem_limit_bytes=VMEM_LIMIT),
    )(cot, w, small, eo, *saved)


PLANES, PLANE = 4, 4
MESH = pl.DeviceIdType.MESH


class Place:
    def __init__(self):
        self.sec = lax.axis_index("section")
        self.d = lax.axis_index("dp")
        self.x = lax.rem(self.d, 2)
        self.y = lax.rem(self.d // 2, 2)
        self.z = self.d // PLANE
        self.seat = self.sec * PLANE + lax.rem(self.d, PLANE)
        self.sib = {"section": 1 - self.sec}
        self.xn = {"dp": self.d + 1 - 2 * self.x}
        self.yn = {"dp": self.d + 2 - 4 * self.y}

    def plane(self, j):
        return lax.rem(self.z + j + PLANES, PLANES)

    def zpeer(self, j):
        return {"dp": self.plane(j) * PLANE + lax.rem(self.d, PLANE)}

    def plane_peer(self, j):
        seat = lax.rem(self.seat + j, 2 * PLANE)
        return {"section": seat // PLANE, "dp": self.z * PLANE + lax.rem(seat, PLANE)}

    def meet(self):
        barrier = pltpu.get_barrier_semaphore()
        others = [self.plane_peer(j) for j in range(1, 8)] + [self.zpeer(j) for j in (1, 2, 3)]
        for other in others:
            pl.semaphore_signal(barrier, inc=1, device_id=other, device_id_type=MESH)
        pl.semaphore_wait(barrier, len(others))


def remote(src, dst, send, recv, target):
    return pltpu.make_async_remote_copy(
        src_ref=src, dst_ref=dst, send_sem=send, recv_sem=recv,
        device_id=target, device_id_type=MESH,
    )


Z1, X1, Y1, X2, Y2, S_OWN, S_X, S_Y, S_DA, S_DB = 0, 3, 7, 11, 15, 19, 23, 27, 31, 35
SLOTS = 39


class Gather:
    def __init__(self, me, net, stage, local_sem, send_sem, recv_sem):
        self.me, self.net, self.stage = me, net, stage
        self.local_sem, self.send_sem, self.recv_sem = local_sem, send_sem, recv_sem
        self.part = stage.shape[0]
        self.half = self.part // 2

    def rows(self, plane, y, x, lo, count):
        at = (plane * PLANE + y * 2 + x) * self.part + lo
        return self.net.at[self.me.sec, pl.ds(pl.multiple_of(at, 16), count)]

    def own(self, j):
        return self.rows(self.me.plane(-j), self.me.y, self.me.x, 0, self.part)

    def send(self, slot, piece, target, src=None):
        src = piece if src is None else src
        remote(src, piece, self.send_sem.at[slot], self.recv_sem.at[slot], target).start()

    def arrived(self, slot, piece):
        remote(
            piece, piece, self.send_sem.at[slot], self.recv_sem.at[slot], self.me.sib
        ).wait_recv()

    def local(self):
        return pltpu.make_async_copy(self.stage, self.own(0), self.local_sem)

    def begin(self):
        me = self.me
        for j in (1, 2, 3):
            self.send(Z1 + j - 1, self.own(0), me.zpeer(j), self.stage)
        for slot, target in ((X1, me.xn), (Y1, me.yn), (S_OWN, me.sib)):
            self.send(slot, self.own(0), target, self.stage)
        self.local().start()

    def phase1(self):
        def step(j):
            me = self.me
            self.arrived(Z1 + j - 1, self.own(j))
            for slot, target in ((X1, me.xn), (Y1, me.yn), (S_OWN, me.sib)):
                self.send(slot + j, self.own(j), target)

        return [lambda j=j: step(j) for j in (1, 2, 3)]

    def phase2(self):
        me, part, half = self.me, self.part, self.half

        def step_x(j):
            plane = me.plane(-j)
            self.arrived(X1 + j, self.rows(plane, me.y, 1 - me.x, 0, part))
            self.send(Y2 + j, self.rows(plane, me.y, 1 - me.x, 0, half), me.yn)
            self.send(S_X + j, self.rows(plane, me.y, 1 - me.x, 0, part), me.sib)

        def step_y(j):
            plane = me.plane(-j)
            self.arrived(Y1 + j, self.rows(plane, 1 - me.y, me.x, 0, part))
            self.send(X2 + j, self.rows(plane, 1 - me.y, me.x, half, half), me.xn)
            self.send(S_Y + j, self.rows(plane, 1 - me.y, me.x, 0, part), me.sib)

        return [lambda f=f, j=j: f(j) for j in range(PLANES) for f in (step_x, step_y)]

    def phase3(self):
        def step(j, slot, to, lo):
            me = self.me
            where = self.rows(me.plane(-j), 1 - me.y, 1 - me.x, lo, self.half)
            self.arrived(slot + j, where)
            self.send(to + j, where, me.sib)

        return [
            lambda j=j, a=a: step(j, *a)
            for j in range(PLANES)
            for a in ((Y2, S_DA, 0), (X2, S_DB, self.half))
        ]

    def finish(self):
        def step():
            for slot in range(S_OWN, SLOTS):
                count = self.part if slot < S_DA else self.half
                self.arrived(slot, self.rows(0, 0, 0, 0, count))
            self.local().wait()

        return [step]

    def drain(self):
        for slot in range(SLOTS):
            whole = slot < X2 or S_OWN <= slot < S_DA
            piece = self.rows(0, 0, 0, 0, self.part if whole else self.half)
            remote(
                piece, piece, self.send_sem.at[slot], self.recv_sem.at[slot], self.me.sib
            ).wait_send()


A_SLOT, B_SLOT, C_SLOT, D_SLOT = 0, 4, 20, 28
R_SLOTS = 31


class Reduce:
    def __init__(self, me, big, shard, sib, there, rb, rc, rd, ssem, rsem):
        self.me, self.big, self.shard = me, big, shard
        self.sib, self.there, self.rb, self.rc, self.rd = sib, there, rb, rc, rd
        self.ssem, self.rsem = ssem, rsem
        self.part = shard.shape[0]
        self.half = self.part // 2
        self.span = PLANE * self.part

    def zt(self, k):
        return (3, 2, 0, 1)[k]

    def block(self, k):
        return pl.ds(self.zt(k) * self.span, self.span)

    def piece(self, k, y, x, lo, count):
        at = (self.zt(k) * PLANE + y * 2 + x) * self.part + lo
        return pl.ds(pl.multiple_of(at, 16), count)

    def send(self, src, dst, slot, target):
        remote(src, dst, self.ssem.at[slot], self.rsem.at[slot], target).start()

    def arrived(self, dst, slot):
        remote(dst, dst, self.ssem.at[slot], self.rsem.at[slot], self.me.sib).wait_recv()

    def begin(self):
        for k in range(PLANES):
            self.begin_block(k)

    def begin_block(self, k):
        at = self.block(k)
        self.send(self.big.at[1 - self.me.sec, at], self.there.at[at], A_SLOT + k, self.me.sib)

    def stage_a(self, k):
        me, half = self.me, self.half
        self.arrived(self.sib.at[self.block(k)], A_SLOT + k)
        base = self.zt(k) * self.span

        def body(i, _):
            at = pl.ds(pl.multiple_of(base + i * half, 16), half)
            self.big[me.sec, at, :] = (
                self.big[me.sec, at, :].astype(F32) + self.sib[at, :].astype(F32)
            ).astype(BF16)
            return 0

        lax.fori_loop(0, 2 * PLANE, body, 0)
        for j in range(2):
            self.send(
                self.big.at[me.sec, self.piece(k, 1 - me.y, j, 0, half)], self.rb.at[k, j],
                B_SLOT + 4 * k + j, me.yn,
            )
            self.send(
                self.big.at[me.sec, self.piece(k, j, 1 - me.x, half, half)], self.rb.at[k, 2 + j],
                B_SLOT + 4 * k + 2 + j, me.xn,
            )

    def join(self, where, other):
        self.big[self.me.sec, where, :] = (
            self.big[self.me.sec, where, :].astype(F32) + other.astype(F32)
        ).astype(BF16)

    def stage_c(self, k):
        me, half = self.me, self.half
        for j in range(4):
            self.arrived(self.rb.at[k, j], B_SLOT + 4 * k + j)
            y, x, lo = (me.y, j, 0) if j < 2 else (j - 2, me.x, half)
            self.join(self.piece(k, y, x, lo, half), self.rb[k, j])
        self.send(
            self.big.at[me.sec, self.piece(k, me.y, 1 - me.x, 0, half)], self.rc.at[k, 0],
            C_SLOT + 2 * k, me.xn,
        )
        self.send(
            self.big.at[me.sec, self.piece(k, 1 - me.y, me.x, half, half)], self.rc.at[k, 1],
            C_SLOT + 2 * k + 1, me.yn,
        )

    def stage_d(self, k):
        me, half, zt = self.me, self.half, self.zt(k)
        for j in range(2):
            self.arrived(self.rc.at[k, j], C_SLOT + 2 * k + j)
            self.join(self.piece(k, me.y, me.x, j * half, half), self.rc[k, j])

        @pl.when(me.z != zt)
        def _():
            self.send(
                self.big.at[me.sec, self.piece(k, me.y, me.x, 0, self.part)],
                self.rd.at[lax.rem(zt - me.z + PLANES, PLANES) - 1],
                D_SLOT + lax.rem(zt - me.z + PLANES, PLANES) - 1,
                {"dp": zt * PLANE + lax.rem(me.d, PLANE)},
            )

    def stage_e(self):
        for j in range(PLANES - 1):
            self.arrived(self.rd.at[j], D_SLOT + j)
        at = pl.ds(pl.multiple_of(self.me.d * self.part, 16), self.part)
        self.shard[...] = (
            self.big[self.me.sec, at, :].astype(F32)
            + self.rd[0].astype(F32) + (self.rd[1].astype(F32) + self.rd[2].astype(F32))
        )

    def steps(self):
        out = []
        for t in range(PLANES + 2):
            for stage, lag in ((self.stage_a, 0), (self.stage_c, 1), (self.stage_d, 2)):
                if 0 <= t - lag < PLANES:
                    out.append(lambda stage=stage, k=t - lag: stage(k))
        return out

    def drain(self, lo=0, hi=R_SLOTS):
        for slot in range(lo, hi):
            if slot < B_SLOT:
                piece = self.there.at[pl.ds(0, self.span)]
            elif slot < D_SLOT:
                piece = self.rb.at[0, 0]
            else:
                piece = self.rd.at[0]
            remote(piece, piece, self.ssem.at[slot], self.rsem.at[slot], self.me.sib).wait_send()


def reduce_scratch(part):
    half = part // 2
    return [
        pltpu.VMEM((PLANES, 4, half, C), BF16),
        pltpu.VMEM((PLANES, 2, half, C), BF16),
        pltpu.VMEM((PLANES - 1, part, C), BF16),
        pltpu.SemaphoreType.DMA((R_SLOTS,)),
        pltpu.SemaphoreType.DMA((R_SLOTS,)),
    ]


class Totals:
    def __init__(self, me, buf, recv, ssem, rsem):
        self.me, self.buf, self.recv, self.ssem, self.rsem = me, buf, recv, ssem, rsem

    def send(self, src, dst, slot, target):
        remote(src, dst, self.ssem.at[slot], self.rsem.at[slot], target).start()

    def arrived(self, dst, slot):
        remote(dst, dst, self.ssem.at[slot], self.rsem.at[slot], self.me.sib).wait_recv()

    def begin(self, first):
        self.send(first, self.recv.at[0], 0, self.me.sib)

    def steps(self):
        me, buf, recv = self.me, self.buf, self.recv

        def one():
            self.arrived(recv.at[0], 0)
            buf[1] = buf[0] + recv[0]
            self.send(buf.at[1], recv.at[1], 1, me.xn)

        def two():
            self.arrived(recv.at[1], 1)
            buf[2] = buf[1] + recv[1]
            self.send(buf.at[2], recv.at[2], 2, me.yn)

        def three():
            self.arrived(recv.at[2], 2)
            buf[3] = buf[2] + recv[2]
            recv[3 + me.z] = buf[3]
            for j in (1, 2, 3):
                self.send(buf.at[3], recv.at[3 + me.z], 2 + j, me.zpeer(j))

        return [one, two, three]

    def result(self):
        for j in (1, 2, 3):
            self.arrived(self.recv.at[3 + self.me.plane(-j)], 2 + j)
        return (self.recv[3] + self.recv[4]) + (self.recv[5] + self.recv[6])

    def drain(self):
        for slot in range(6):
            piece = self.recv.at[0]
            remote(piece, piece, self.ssem.at[slot], self.rsem.at[slot], self.me.sib).wait_send()


class Squares:
    def __init__(self, me, own, recv, ssem, rsem):
        self.me, self.own, self.recv, self.ssem, self.rsem = me, own, recv, ssem, rsem

    def hop(self, src, base, mine, peers, slots):
        for j, target in peers:
            dst = self.recv.at[base + mine]
            remote(src, dst, self.ssem.at[slots + j], self.rsem.at[slots + j], target).start()
        self.recv[base + mine] = src[...]
        for j, _ in peers:
            dst = self.recv.at[base]
            remote(dst, dst, self.ssem.at[slots + j], self.rsem.at[slots + j], self.me.sib).wait_recv()

    def run(self):
        me, recv = self.me, self.recv
        self.hop(self.own.at[0], 0, me.seat, [(j, me.plane_peer(j)) for j in range(1, 8)], -1)
        pairs = [recv[2 * k] + recv[2 * k + 1] for k in range(4)]
        self.own[1] = (pairs[0] + pairs[1]) + (pairs[2] + pairs[3])
        self.hop(self.own.at[1], 8, me.z, [(j, me.zpeer(j)) for j in (1, 2, 3)], 6)
        return (recv[8] + recv[9]) + (recv[10] + recv[11])

    def drain(self):
        for slot in range(10):
            piece = self.recv.at[0]
            remote(piece, piece, self.ssem.at[slot], self.rsem.at[slot], self.me.sib).wait_send()


def squares_scratch(shape):
    return [
        pltpu.VMEM((2,) + shape, F32),
        pltpu.VMEM((12,) + shape, F32),
        pltpu.SemaphoreType.DMA((10,)),
        pltpu.SemaphoreType.DMA((10,)),
    ]


def totals_scratch(shape):
    return [
        pltpu.VMEM((4,) + shape, F32),
        pltpu.VMEM((7,) + shape, F32),
        pltpu.SemaphoreType.DMA((6,)),
        pltpu.SemaphoreType.DMA((6,)),
    ]


def saved_scratch(images):
    return [pltpu.VMEM(a.shape, a.dtype) for a in saved_shapes(images)]


def backward_scratch(images):
    return scratch_forward(images) + [
        pltpu.VMEM((images, POS, C), F32),
        pltpu.VMEM((images, POS, 3 * C), BF16),
        pltpu.VMEM((C, images * POS), BF16),
    ]


GEN_TOTAL = SIGMA_INIT**2 + SIGMA_DATA**2
GEN_IN = GEN_TOTAL**-0.5
GEN_SKIP = SIGMA_DATA**2 / GEN_TOTAL
GEN_OUT = SIGMA_INIT * SIGMA_DATA * GEN_TOTAL**-0.5
T_IN, T_SKIP, T_OUT, T_SIGMA, T_FACTOR = range(5)


def fill_embed(eo, sigmas):
    at = lax.broadcasted_iota(jnp.int32, (8, 4 * C), 1)
    side = lax.broadcasted_iota(jnp.int32, (8, 4 * C), 0) // 4
    k = at // 2
    power = (k & (C - 1)).astype(F32) * (1.0 / C)
    rows = sigmas + [jnp.ones_like(sigmas[0])] * (4 - len(sigmas))
    angle = jnp.log(jnp.concatenate(rows + rows, axis=0)) * 0.25 * jnp.exp(power * -LOG_10000)
    wave = jnp.where(k < C, jnp.cos(angle), jnp.sin(angle))
    eo[...] = jnp.where((at & 1) == side, wave, 0.0).astype(BF16)


LOG_10000 = 9.210340371976184


def step_kernel(*refs):
    (
        z_all, eps_all, levels, counts, gen_w, fake_w, teacher_w, gen_small, fake_small,
        teacher_small,
        gw_out, sv_x, sv_h, sv_y, sv_q, sv_a, sv_o, sv_s, gshard, fshard, stot, sqtot,
        *refs,
    ) = refs
    gen_out = (sv_x, sv_h, sv_y, sv_q, sv_a, sv_o, sv_s)
    w_gen, w_fake, w_teach = refs[:3]
    sv_one, sv_two = refs[3:10], refs[10:17]
    bufs, nbuf, qkvw, tmp, dn, dqkv, act_t = refs[17:24]
    zb, eb, g, stage, local_sem, send_sem, recv_sem, copy_sem = refs[24:32]
    smalls, small_sem, gen_eo, score_eo, tab, sgrads, part_sums = refs[32:39]
    fake_refs, gen_refs = refs[39:44], refs[44:49]
    small_refs, square_refs = refs[49:53], refs[53:57]
    sib, free_sem = refs[57:59]
    g2 = sv_two[0].at[2]
    images = zb.shape[0]
    me = Place()
    start = me.sec * images

    def run(steps):
        for step in steps:
            step()

    def mine(ref):
        return ref.at[pl.ds(start, images)]

    loads = [
        pltpu.make_async_copy(mine(z_all), zb, copy_sem.at[0]),
        pltpu.make_async_copy(mine(eps_all), eb, copy_sem.at[1]),
    ]
    for copy in loads:
        copy.start()
    masters = [
        pltpu.make_async_copy(src, dst, copy_sem.at[2 + k])
        for k, (src, dst) in enumerate(((gen_w, gshard), (fake_w, fshard), (teacher_w, stage.at[2])))
    ]
    for copy in masters:
        copy.start()
    smalls[...] = jnp.zeros(smalls.shape, F32)
    for n, ref in enumerate((gen_small, fake_small, teacher_small)):
        for r in range(13):
            smalls[me.sec, n, r : r + 1, :] = ref[r]
    gathers = [
        Gather(me, net, stage.at[n], local_sem.at[n], send_sem.at[n], recv_sem.at[n])
        for n, net in enumerate((w_gen, w_fake, w_teach))
    ]
    for copy in masters:
        copy.wait()
    stage[0] = gshard[...].astype(BF16)
    stage[1] = fshard[...].astype(BF16)
    me.meet()
    gathers[0].begin()
    swap = remote(
        smalls.at[me.sec], smalls.at[me.sec], small_sem.at[0], small_sem.at[1], me.sib
    )
    swap.start()

    clear_pads(bufs)
    sgrads[...] = jnp.zeros(sgrads.shape, F32)
    sigmas = []
    valid_sum = jnp.zeros((1, 4 * C), F32)
    for i in range(images):
        level = jnp.zeros((1, 4 * C), jnp.int32) + levels[start + i]
        sigma = SIGMA_TOP + level.astype(F32) / (LEVELS - 1) * (SIGMA_BOTTOM - SIGMA_TOP)
        square = sigma * sigma
        sigma = square * square * square * sigma
        sigmas.append(sigma)
        s_in, s_skip, s_out, s_lam = precondition(sigma)
        valid = jnp.where(jnp.zeros_like(level) + (start + i) < counts[0], 1.0, 0.0)
        valid_sum = valid_sum + valid
        rows = (s_in, s_skip, s_out, sigma, valid * s_lam * (1.0 / (POS * C)))
        for k, value in enumerate(rows):
            tab[i, k : k + 1, :] = value[:, :C]
    fill_embed(score_eo, sigmas)
    fill_embed(gen_eo, [jnp.full((1, 4 * C), SIGMA_INIT, F32)] * images)

    def forward(n, w, eo, sv, pump):
        def body(l, _):
            layer_forward(
                l, w, smalls.at[:, n], eo, *sv, bufs, nbuf, qkvw, tmp, True, pump
            )
            return 0

        lax.fori_loop(0, 2, body, 0)

    def backward(n, w, eo, sv, cot, grad, sgrad, pump):
        def body(k, _):
            layer_backward(
                1 - k, w, smalls.at[:, n], eo, *sv, cot, bufs, nbuf, qkvw, tmp, dn, dqkv,
                act_t, grad, sgrad, pump,
            )
            return 0

        lax.fori_loop(0, 2, body, 0)

    def each(f):
        def body(i, carry):
            return f(i, [tab[i, k : k + 1, :] for k in range(5)], carry)

        return lax.fori_loop(0, images, body, jnp.zeros((1, C), F32))

    z_now, z_next = gathers[0].phase1(), gathers[1].phase1()
    run(z_now[:2] + [gathers[1].begin] + z_now[2:] + gathers[0].phase2() + z_next[:1])
    last = gathers[0].phase3()
    run(last[:4] + z_next[1:2] + [gathers[2].begin] + last[4:] + z_next[2:])
    for copy in loads:
        copy.wait()
    sv_one[0][0] = zb[...] * (GEN_IN * SIGMA_INIT)
    swap.wait()
    run(gathers[0].finish())
    later = gathers[1].phase2()
    forward(0, w_gen, gen_eo, sv_one, Pump(later[:5], FORWARD_POINTS, (0, 1)))
    pairs = [(w_gen, gw_out)] + list(zip(sv_one, gen_out))
    stores = [
        pltpu.make_async_copy(src, dst, copy_sem.at[2 + k]) for k, (src, dst) in enumerate(pairs)
    ]
    for copy in stores:
        copy.start()

    def noisy(i, t, carry):
        zb[i] = zb[i] * (GEN_SKIP * SIGMA_INIT) + GEN_OUT * sv_one[0][2, i]
        eb[i] = zb[i] + t[T_SIGMA] * eb[i]
        sv_two[0][0, i] = t[T_IN] * eb[i]
        return carry

    each(noisy)
    z_next, last = gathers[2].phase1(), gathers[1].phase3()
    run(later[5:] + z_next[:1] + last[:4] + z_next[1:2] + last[4:] + z_next[2:])
    run(gathers[1].finish())
    later = gathers[2].phase2()
    forward(1, w_fake, score_eo, sv_two, Pump(later[:5], FORWARD_POINTS, (0, 1)))
    later = later[5:] + gathers[2].phase3()

    def fake_loss(i, t, total):
        den = t[T_SKIP] * eb[i] + t[T_OUT] * sv_two[0][2, i]
        sv_two[0][2, i] = den
        miss = den - zb[i]
        g[i] = (2.0 * t[T_OUT] * t[T_FACTOR]) * miss
        return total + t[T_FACTOR] * colsum(miss * miss)

    loss_fake = each(fake_loss)
    for copy in stores:
        copy.wait()
    gathers[0].drain()
    backward(
        1, w_fake, score_eo, sv_two, g, w_gen, sgrads.at[:, 1],
        Pump(later, WEIGHT_POINTS, (1, 0), 0.0, 0.8),
    )
    fake_sum = Reduce(me, w_gen, fshard, sib, sib, *fake_refs)
    fake_sum.begin()
    run(gathers[2].finish())
    later = fake_sum.steps()
    sv_one[0][0] = sv_two[0][0]
    forward(2, w_teach, score_eo, sv_one, Pump(later[:5], FORWARD_POINTS, (0, 1), 0.2))

    def gen_loss(i, t, total):
        den = t[T_SKIP] * eb[i] + t[T_OUT] * sv_one[0][2, i]
        fake_den = sv_two[0][2, i]
        miss = fake_den - zb[i]
        gap = den - fake_den
        scale = t[T_OUT] * t[T_FACTOR]
        g[i] = scale * ((2.0 * (1.0 - ALPHA_MIX)) * gap + miss)
        g2[i] = scale * ((1.0 - 2.0 * (1.0 - ALPHA_MIX)) * gap - miss)
        zb[i] = (t[T_FACTOR] * (t[T_SKIP] - 1.0)) * gap
        return total + t[T_FACTOR] * colsum(gap * ((1.0 - ALPHA_MIX) * gap + miss))

    loss_gen = each(gen_loss)
    backward(
        2, w_teach, score_eo, sv_one, g, None, None, Pump(later[5:9], BACKWARD_POINTS, (1, 0))
    )
    gathers[2].drain()
    fake_sum.drain(A_SLOT, B_SLOT)
    pl.semaphore_signal(free_sem, inc=1, device_id=me.sib, device_id_type=MESH)
    back = [
        pltpu.make_async_copy(src, dst, copy_sem.at[2 + k])
        for k, (dst, src) in enumerate([(w_teach, gw_out)] + list(zip(sv_one, gen_out)))
    ]
    for copy in back:
        copy.start()
    backward(
        1, w_fake, score_eo, sv_two, g2, None, None, Pump(later[9:], BACKWARD_POINTS, (1, 0))
    )

    def gen_gradient(i, t, carry):
        g[i] = GEN_OUT * (zb[i] + t[T_IN] * (g[i] + g2[i]))
        return carry

    each(gen_gradient)
    gathers[1].drain()
    for copy in back:
        copy.wait()

    gen_sum = Reduce(me, w_fake, gshard, w_gen.at[1 - me.sec], w_gen.at[me.sec], *gen_refs)
    later = gen_sum.steps()

    def on_section(s, steps):
        pl.when(me.sec == s)(lambda: run(steps))

    def hand_over():
        pl.semaphore_wait(free_sem, 1)

    pump = Pump([], WEIGHT_POINTS, (1, 0))

    def at(layer, point, section, steps):
        pump.table[layer][point].append(lambda: on_section(section, steps))

    upper = [hand_over, lambda: gen_sum.begin_block(0), lambda: gen_sum.begin_block(1)]
    lower = [lambda: gen_sum.begin_block(2), lambda: gen_sum.begin_block(3)]
    for layer, giver in ((1, 0), (0, 1)):
        at(layer, HALF_WAY, giver, upper)
        at(layer, READY, giver, lower)
    for k, step in enumerate(later):
        at(0, k * READY // len(later), 1, [step])
    at(0, READY, 0, later[:1])
    at(0, READY + 2, 0, later[1:2])
    at(0, READY + 4, 0, later[2:3])
    backward(0, w_teach, gen_eo, sv_one, g, w_fake, sgrads.at[:, 0], pump)

    def spread_sum(total):
        return jnp.broadcast_to(jnp.sum(total, axis=1, keepdims=True), (1, C))

    sums = jnp.concatenate([spread_sum(loss_gen), spread_sum(loss_fake), valid_sum[:, :C]], axis=0)
    for s in range(2):
        part_sums[s, 0:16, :] = sgrads[s, 0]
        part_sums[s, 13:16, :] = sums
        part_sums[s, 16:32, :] = sgrads[s, 1]
    small = Totals(me, *small_refs)
    small_refs[0][0] = part_sums[me.sec]
    small.begin(part_sums.at[1 - me.sec])
    fake_sum.stage_e()
    small_steps = small.steps()
    on_section(0, later[3:6])
    run(small_steps[:1])
    on_section(0, later[6:8])
    run(small_steps[1:2])
    on_section(0, later[8:10])
    run(small_steps[2:])
    on_section(0, later[10:])
    stot[...] = small.result()
    own = square_refs[0]
    keep = lax.broadcasted_iota(jnp.int32, (16, C), 0) < 13
    for n, rows in ((1, fshard), (0, gshard)):
        if n == 0:
            gen_sum.stage_e()
        low = jnp.square(jnp.where(keep, stot[16 * n : 16 * n + 16, :], 0.0))
        low = jnp.where(me.d == 0, low[0:8] + low[8:16], 0.0)
        big = jnp.sum(jnp.square(rows[...]).reshape(rows.shape[0] // 8, 8, C), axis=0)
        own[0, 8 * n : 8 * n + 8, :] = big + low
    square = Squares(me, *square_refs)
    sqtot[...] = square.run()
    fake_sum.drain(B_SLOT)
    for done in (gen_sum, small, square):
        done.drain()


SIGMA_TOP = SIGMA_HIGH ** (1.0 / RHO_POWER)
SIGMA_BOTTOM = SIGMA_LOW ** (1.0 / RHO_POWER)


def run_step(z, eps, levels, counts, gen_w, fake_w, teacher_w, smalls):
    part = gen_w.shape[0]
    images = z.shape[0] // 2
    any_ = pl.BlockSpec(memory_space=pl.ANY)
    smem = pl.BlockSpec(memory_space=pltpu.SMEM)
    saved = saved_shapes(images)
    return pl.pallas_call(
        step_kernel,
        out_shape=[jax.ShapeDtypeStruct((2, ROWS, C), BF16)]
        + saved
        + [
            jax.ShapeDtypeStruct((part, C), F32),
            jax.ShapeDtypeStruct((part, C), F32),
            jax.ShapeDtypeStruct((32, C), F32),
            jax.ShapeDtypeStruct((16, C), F32),
        ],
        in_specs=[any_] * 2 + [smem] * 2 + [any_] * 3 + vm(3),
        out_specs=[any_] * 8 + vm(4),
        scratch_shapes=[pltpu.VMEM((2, ROWS, C), BF16)] * 3
        + saved_scratch(images) * 2
        + backward_scratch(images)
        + [pltpu.VMEM((images, POS, C), F32)] * 3
        + [
            pltpu.VMEM((3, part, C), BF16),
            pltpu.SemaphoreType.DMA((3,)),
            pltpu.SemaphoreType.DMA((3, SLOTS)),
            pltpu.SemaphoreType.DMA((3, SLOTS)),
            pltpu.SemaphoreType.DMA((10,)),
            pltpu.VMEM((2, 3, 16, C), F32),
            pltpu.SemaphoreType.DMA((2,)),
            pltpu.VMEM((8, 4 * C), BF16),
            pltpu.VMEM((8, 4 * C), BF16),
            pltpu.VMEM((images, 8, C), F32),
            pltpu.VMEM((2, 2, 16, C), F32),
            pltpu.VMEM((2, 32, C), F32),
        ]
        + reduce_scratch(part) * 2
        + totals_scratch((32, C))
        + squares_scratch((16, C))
        + [pltpu.VMEM((ROWS, C), BF16), pltpu.SemaphoreType.REGULAR],
        compiler_params=pltpu.CompilerParams(
            collective_id=0, has_side_effects=True, vmem_limit_bytes=STEP_LIMIT
        ),
    )(z, eps, levels, counts, gen_w, fake_w, teacher_w, *smalls)[8:]


def adam_step(master, first_mom, second_mom, grad):
    first_new = BETA_ONE * first_mom + (1.0 - BETA_ONE) * grad
    second_new = BETA_TWO * second_mom + (1.0 - BETA_TWO) * grad * grad
    direction = (
        first_new
        / (1.0 - BETA_ONE**STEP)
        / (jnp.sqrt(second_new / (1.0 - BETA_TWO**STEP)) + ADAM_EPS)
    )
    return (master - LEARN_RATE * (direction + WEIGHT_DECAY * master), first_new, second_new)


EMA_RATE = 0.5 ** (20.0 / STEP)
SMALL_STATES = (4, 5, 6, 7, 11, 12, 13)


def update_kernel(gshard, fshard, stot, sqtot, *refs):
    ins, outs = refs[:14], refs[14:]
    norms, losses = outs[14:]
    count = stot[15:16, 0:1]
    norm_of, scales = [], []
    for n in range(2):
        rows = jnp.sum(sqtot[8 * n : 8 * n + 8, :], axis=0, keepdims=True)
        norm = jnp.sqrt(jnp.sum(rows, axis=1, keepdims=True)) / count
        scales.append(jnp.minimum(1.0, CLIP_NORM / norm) / count)
        norm_of.append(norm)

    def one(at, grad, w, m, v, ema, ow, om, ov, oe):
        new, first, second = adam_step(w[at], m[at], v[at], grad)
        ow[at] = new
        om[at] = first
        ov[at] = second
        if ema is not None:
            oe[at] = EMA_RATE * ema[at] + (1.0 - EMA_RATE) * new

    one(0, gshard[...] * scales[0], *ins[0:4], *outs[0:4])
    one(0, fshard[...] * scales[1], *ins[8:11], None, *outs[8:11], None)

    @pl.when(pl.program_id(0) == 0)
    def _():
        for n in range(2):
            norms[n] = norm_of[n][0, 0]
            losses[n] = (stot[13 + n : 14 + n, 0:1] / count)[0, 0]
        for k in range(13):
            one(k, stot[k : k + 1, :] * scales[0], *ins[4:8], *outs[4:8])
            one(k, stot[16 + k : 17 + k, :] * scales[1], *ins[11:14], None, *outs[11:14], None)


def update_nets(gshard, fshard, stot, sqtot, states):
    def turned(arrays):
        return [a.swapaxes(0, 1) if k in SMALL_STATES else a for k, a in enumerate(arrays)]

    part = gshard.shape[0]
    steps = 1
    big = pl.BlockSpec((1, part // steps, C), lambda i: (0, i, 0))
    low = pl.BlockSpec((13, 1, C), lambda i: (0, 0, 0))
    shard = pl.BlockSpec((part // steps, C), lambda i: (i, 0))
    whole = [pl.BlockSpec(a.shape, lambda i: (0, 0)) for a in (stot, sqtot)]
    specs = [low if k in SMALL_STATES else big for k in range(len(states))]
    states = turned(states)
    res = pl.pallas_call(
        update_kernel,
        grid=(steps,),
        out_shape=[jax.ShapeDtypeStruct(a.shape, F32) for a in states]
        + [jax.ShapeDtypeStruct((2,), F32)] * 2,
        in_specs=[shard] * 2 + whole + specs,
        out_specs=specs + [pl.BlockSpec(memory_space=pltpu.SMEM)] * 2,
        compiler_params=pltpu.CompilerParams(vmem_limit_bytes=VMEM_LIMIT),
    )(gshard, fshard, stot, sqtot, *states)
    return tuple(turned(res[:-2])) + tuple(res[-2:])


def gather_plain(shard):
    rows = lax.all_gather(shard.astype(BF16), "dp", axis=1, tiled=True)
    return lax.all_gather(rows, "section", axis=0, tiled=True)


def reduce_plain(bigs, small):
    shards_, squares = [], []
    own = lax.psum_scatter(small, "section", scatter_dimension=0, tiled=True)
    stot = lax.psum(own, "dp")[0]
    first = lax.axis_index("dp") == 0
    for n, big in enumerate(bigs):
        own = lax.psum_scatter(big, "section", scatter_dimension=0, tiled=True)
        own = lax.psum_scatter(own, "dp", scatter_dimension=1, tiled=True)[0].astype(F32)
        shards_.append(own)
        low = jnp.sum(jnp.square(stot[16 * n : 16 * n + 13]))
        squares.append(jnp.sum(own * own) + jnp.where(first, low, 0.0))
    sq = lax.psum(jnp.stack(squares), ("section", "dp"))
    return *shards_, stot, jnp.zeros((16, C), F32).at[jnp.array([0, 8]), 0].set(sq)


def shards(
    z_noise, eps_noise, levels, counts,
    gen_w, gen_m, gen_v, gen_ema, gen_small, gen_small_m, gen_small_v, gen_small_ema,
    fake_w, fake_m, fake_v, fake_small, fake_small_m, fake_small_v,
    teacher_w, teacher_small,
):
    if lax.axis_size("dp") == PLANES * PLANE:
        smalls = [a.swapaxes(0, 1) for a in (gen_small, fake_small, teacher_small)]
        reduced = run_step(
            z_noise, eps_noise, levels, counts, gen_w[0], fake_w[0], teacher_w[0], smalls
        )
    else:
        reduced = plain_step(
            z_noise, eps_noise, levels, counts, gen_w, fake_w, teacher_w,
            gen_small, fake_small, teacher_small,
        )
    return update_nets(
        *reduced,
        (
            gen_w, gen_m, gen_v, gen_ema, gen_small, gen_small_m, gen_small_v, gen_small_ema,
            fake_w, fake_m, fake_v, fake_small, fake_small_m, fake_small_v,
        ),
    )


def plain_step(
    z_noise, eps_noise, levels, counts, gen_w, fake_w, teacher_w,
    gen_small, fake_small, teacher_small,
):
    images = z_noise.shape[0] // lax.axis_size("section")
    start = lax.axis_index("section") * images

    def mine(a):
        return lax.dynamic_slice_in_dim(a, start, images, 0)

    z, eps = mine(z_noise), mine(eps_noise)
    sigma = sigma_levels(mine(levels))
    valid = (start + jnp.arange(images) < counts[0]).astype(F32)
    valid_sum = jnp.sum(valid)
    gen_eo = spread_embed(jnp.full((images,), SIGMA_INIT, F32))
    score_eo = spread_embed(sigma)
    gs, fs, ts = [
        lax.all_gather(a, "section", axis=0, tiled=True)
        for a in (gen_small, fake_small, teacher_small)
    ]
    gw, fw, tw = gather_plain(gen_w), gather_plain(fake_w), gather_plain(teacher_w)
    s_in, s_skip, s_out, s_lam = precondition(sigma)
    factor = valid * s_lam / (POS * C)
    s_in, s_skip, s_out, sigma, factor = [
        t[:, None, None] for t in (s_in, s_skip, s_out, sigma, factor)
    ]
    raw = SIGMA_INIT * z
    gen_saved = run_forward(GEN_IN * raw, gw, gs, gen_eo)
    samples = GEN_SKIP * raw + GEN_OUT * gen_saved[0][2]
    noisy = samples + sigma * eps
    x0 = s_in * noisy
    fake_saved = run_forward(x0, fw, fs, score_eo)
    fake_den = s_skip * noisy + s_out * fake_saved[0][2]
    miss = fake_den - samples
    _, fake_g, fake_sg = run_backward(
        s_out * 2.0 * factor * miss, fw, fs, score_eo, fake_saved, True
    )
    teacher_saved = run_forward(x0, tw, ts, score_eo)
    teacher_den = s_skip * noisy + s_out * teacher_saved[0][2]
    gap = teacher_den - fake_den
    loss_gen = jnp.sum(factor * ((1.0 - ALPHA_MIX) * gap * gap + gap * miss))
    loss_fake = jnp.sum(factor * miss * miss)
    grad_teacher = factor * (2.0 * (1.0 - ALPHA_MIX) * gap + miss)
    grad_fake = factor * gap - grad_teacher
    direct = factor * gap * (s_skip - 1.0)
    (back_t,) = run_backward(s_out * grad_teacher, tw, ts, score_eo, teacher_saved, False)
    (back_f,) = run_backward(s_out * grad_fake, fw, fs, score_eo, fake_saved, False)
    gen_cot = GEN_OUT * (direct + s_in * (back_t + back_f))
    _, gen_g, gen_sg = run_backward(gen_cot, gw, gs, gen_eo, gen_saved, True)
    scalars = jnp.broadcast_to(jnp.stack([loss_gen, loss_fake, valid_sum])[:, None], (3, C))
    small_sums = jnp.concatenate(
        [gen_sg[:, :13], jnp.broadcast_to(scalars, (2, 3, C)), fake_sg], axis=1
    )
    return reduce_plain((gen_g, fake_g), small_sums)


def solution(mesh):
    images = P("dp", None, None)
    big = P("section", "dp", None)
    small = P("section", None, None)
    return jax.shard_map(
        shards,
        mesh=mesh,
        in_specs=(images, images, P("dp"), P("dp"))
        + (big,) * 4 + (small,) * 4 + (big,) * 3 + (small,) * 3 + (big, small),
        out_specs=(big,) * 4 + (small,) * 4 + (big,) * 3 + (small,) * 3 + (P(), P()),
        check_vma=False,
    )
```

```python
import functools

import jax
import jax.numpy as jnp
from jax import lax
from jax.experimental import pallas as pl
from jax.experimental.pallas import tpu as pltpu
from jax.sharding import PartitionSpec as P

GROUPS = 32
SIDE = 16
LEVELS = 1000
STEP = 10

SIGMA_DATA = 0.5
SIGMA_INIT = 2.5
SIGMA_LOW = 0.05
SIGMA_HIGH = 20.0
RHO_POWER = 7.0
ALPHA_MIX = 1.2
RS = 0.7071067811865476
NORM_EPS = 1e-05
CLIP_NORM = 0.001
LEARN_RATE = 0.15
BETA_ONE = 0.9
BETA_TWO = 0.999
ADAM_EPS = 1e-08
WEIGHT_DECAY = 0.01

C = 256
HALF = 128
POS = 256
ROWS = 26 * C
CHUNK = 64
PAD = SIDE
F32 = jnp.float32
BF16 = jnp.bfloat16
VMEM_LIMIT = 58 * 2**20
STEP_LIMIT = 63 * 2**20

R_CONV1, R_CONV2, R_EMB, R_QKV, R_PROJ = 0, 9 * C, 18 * C, 22 * C, 25 * C
S_M1, S_I1, S_M2, S_I2, S_M3, S_I3, S_MA, S_MB = range(8)


def sigma_levels(level_ids):
    fraction = level_ids.astype(F32) / (LEVELS - 1)
    top_root = SIGMA_HIGH ** (1.0 / RHO_POWER)
    bottom_root = SIGMA_LOW ** (1.0 / RHO_POWER)
    return (top_root + fraction * (bottom_root - top_root)) ** RHO_POWER


def precondition(sigma_vals):
    total = sigma_vals * sigma_vals + SIGMA_DATA**2
    return (
        lax.rsqrt(total),
        SIGMA_DATA**2 / total,
        sigma_vals * SIGMA_DATA * lax.rsqrt(total),
        total / (sigma_vals * sigma_vals * SIGMA_DATA**2),
    )


def noise_embed(sigma_vals, channel_count):
    frequency = (1.0 / 10000.0) ** (jnp.arange(channel_count, dtype=F32) / channel_count)
    angles = (jnp.log(sigma_vals) / 4.0)[..., None] * frequency
    return jnp.concatenate([jnp.cos(angles), jnp.sin(angles)], axis=-1)


def spread_embed(sigma_vals):
    emb = noise_embed(sigma_vals, C).astype(BF16)
    images = emb.shape[0]
    zero = jnp.zeros_like(emb)
    low = jnp.stack([emb, zero], axis=-1).reshape(images, 4 * C)
    high = jnp.stack([zero, emb], axis=-1).reshape(images, 4 * C)
    fill = jnp.zeros((4 - images, 4 * C), BF16)
    return jnp.concatenate([low, fill, high, fill], axis=0)


def dot_nn(a, b):
    return lax.dot_general(a, b, (((1,), (0,)), ((), ())), preferred_element_type=F32)


def dot_nt(a, b):
    return lax.dot_general(a, b, (((1,), (1,)), ((), ())), preferred_element_type=F32)


def dot_tn(a, b):
    return lax.dot_general(a, b, (((0,), (0,)), ((), ())), preferred_element_type=F32)


def group_mean(v):
    lane = lax.broadcasted_iota(jnp.int32, (8, C), 1)
    for sh in (1, 2, 4):
        v = v + jnp.where((lane & sh) != 0, pltpu.roll(v, sh, 1), pltpu.roll(v, C - sh, 1))
    return v * (1.0 / (POS * 8))


def colsum(v):
    return jnp.sum(v, axis=0, keepdims=True)


def no_pump(l):
    pass


FORWARD_POINTS, BACKWARD_POINTS, WEIGHT_POINTS = 10, 12, 18
HALF_WAY, READY = 8, 13


def stagger(steps, images, between):
    for t in range(len(steps) + images - 1):
        for i in range(images):
            if 0 <= t - i < len(steps):
                steps[t - i](i)
        between()


class Pump:
    def __init__(self, steps, points, layers, lo=0.0, hi=1.0):
        self.table = {l: [[] for _ in range(points)] for l in layers}
        self.at = 0
        for k, step in enumerate(steps):
            place = int((lo + (hi - lo) * (k + 0.5) / len(steps)) * points * len(layers))
            self.table[layers[place // points]][place % points].append(step)

    def __call__(self, l):
        for layer, points in self.table.items():
            if points[self.at]:

                @pl.when(l == layer)
                def _(todo=points[self.at]):
                    for step in todo:
                        step()

        self.at += 1


def put_shifted(bufs, i, r, v):
    rows = v.shape[0]
    at = pl.ds(PAD + r, rows)
    sub = lax.broadcasted_iota(jnp.int32, (rows // SIDE, 8, C), 1)
    x = v.reshape(rows // SIDE, 2, 8, C)
    low, high = x[:, 0], x[:, 1]
    low_up, high_up = pltpu.roll(low, 1, 1), pltpu.roll(high, 1, 1)
    low_down, high_down = pltpu.roll(low, 7, 1), pltpu.roll(high, 7, 1)
    left = (jnp.where(sub == 0, 0.0, low_up), jnp.where(sub == 0, low_up, high_up))
    right = (jnp.where(sub == 7, high_down, low_down), jnp.where(sub == 7, 0.0, high_down))
    bufs[0, i, at, :] = jnp.stack(left, axis=1).reshape(rows, C).astype(BF16)
    bufs[1, i, at, :] = v.astype(BF16)
    bufs[2, i, at, :] = jnp.stack(right, axis=1).reshape(rows, C).astype(BF16)


def taps(bufs, flip):
    images = bufs.shape[1]
    out = []
    for dr in (-1, 0, 1):
        for dc in (-1, 0, 1):
            sr, sc = (-dr, -dc) if flip else (dr, dc)
            piece = bufs[sc + 1, :, PAD + SIDE * sr : PAD + SIDE * sr + POS, :]
            out.append(piece.reshape(images * POS, C))
    return out


def conv_forward(bufs, w, l, row):
    return dot_nn(jnp.concatenate(taps(bufs, False), axis=1), w[l, row : row + 9 * C, :])


def conv_input_grad(bufs, w, l, row):
    parts = [w[l, row + t * C : row + (t + 1) * C, :] for t in range(9)]
    return dot_nt(jnp.concatenate(taps(bufs, True), axis=1), jnp.concatenate(parts, axis=1))


def conv_weight_grad(act_t, bufs, grad, l, row):
    left = act_t[...]
    for t, piece in enumerate(taps(bufs, True)):
        grad[l, row + t * C : row + (t + 1) * C, :] = dot_nn(left, piece).astype(BF16)


def silu(v):
    h = 0.5 * v
    return h + h * jnp.tanh(h)


def silu_parts(v):
    s = 0.5 + 0.5 * jnp.tanh(0.5 * v)
    return s, s * (1.0 + v * (1.0 - s))


def clear_pads(bufs):
    zero = jnp.zeros(bufs.shape[:2] + (PAD, C), BF16)
    bufs[:, :, 0:PAD, :] = zero
    bufs[:, :, PAD + POS :, :] = zero


def split_qkv(w, l, qkvw, tmp):
    for h in range(2):
        tmp[h] = w[l, R_QKV : R_QKV + 3 * C, h * HALF : (h + 1) * HALF].astype(F32)
    for j in range(3):
        for h in range(2):
            at = j * C + h * HALF
            qkvw[:, at : at + HALF] = tmp[h, pl.ds(j, C, stride=3), :].astype(BF16)


def norm_sums(x):
    pivot = x[0:1]
    d = x - pivot
    return colsum(d), colsum(d * d), pivot


def norm_stats(sums):
    fill = [jnp.zeros((4 - len(sums), C), F32)]
    s1, s2, pivot = [jnp.concatenate([a[k] for a in sums] + fill, axis=0) for k in range(3)]
    centre = group_mean(jnp.concatenate([pivot, pivot], axis=0) * POS)[0:4]
    off = pivot - centre
    first = s1 + POS * off
    second = s2 + off * (2.0 * s1 + POS * off)
    means = group_mean(jnp.concatenate([first, second], axis=0))
    spread = jnp.maximum(means[4:8] - jnp.square(means[0:4]), 0.0)
    return centre + means[0:4], lax.rsqrt(spread + NORM_EPS)


def two_means(a, b):
    rows = jnp.concatenate([a, b] * 4, axis=0)
    means = group_mean(rows)
    return means[0:1], means[1:2]


def tap_rows(bufs, flip, which):
    out = []
    for dr in (-1, 0, 1):
        for dc in (-1, 0, 1):
            sr, sc = (-dr, -dc) if flip else (dr, dc)
            at = slice(PAD + SIDE * sr, PAD + SIDE * sr + POS)
            piece = jnp.concatenate([bufs[sc + 1, i, at, :] for i in which], axis=0)
            out.append(piece)
    return out


def layer_forward(l, w, small, eo, xs, h1, y, qkv, att, o, st, bufs, nbuf, qkvw, tmp, staged, pump):
    images = h1.shape[1]
    split_qkv(w, l, qkvw, tmp)
    mod = dot_nn(eo[...], w[l, R_EMB : R_EMB + 4 * C, :])
    ma = mod[0:4] + small[l, 5:6, :]
    mb = mod[4:8] + small[l, 6:7, :]
    for i in range(images):
        st[l, i, S_MA : S_MA + 1, :] = ma[i : i + 1]
        st[l, i, S_MB : S_MB + 1, :] = mb[i : i + 1]

    sums = {}

    def row(k):
        return small[l, k : k + 1, :]

    def keep(which, mean, inv, at):
        for k, i in enumerate(which):
            st[l, i, at : at + 1, :] = mean[k : k + 1]
            st[l, i, at + 1 : at + 2, :] = inv[k : k + 1]

    def first(which):
        mean, inv = norm_stats([norm_sums(xs[l, i]) for i in which])
        keep(which, mean, inv, S_M1)
        for k, i in enumerate(which):
            a = inv[k : k + 1] * row(0)
            for r in range(0, POS, CHUNK):
                v = (xs[l, i, r : r + CHUNK, :] - mean[k : k + 1]) * a + row(1)
                put_shifted(bufs, i, r, silu(v))

    def conv(which, at):
        left = jnp.concatenate(tap_rows(bufs, False, which), axis=1)
        return dot_nn(left, w[l, at : at + 9 * C, :])

    def conv_one(which):
        out = conv(which, R_CONV1)
        for k, i in enumerate(which):
            own = out[k * POS : (k + 1) * POS]
            own = own + row(2)
            sums[i] = norm_sums(own)
            h1[l, i] = own

    def second(which):
        mean, inv = norm_stats([sums[i] for i in which])
        keep(which, mean, inv, S_M2)
        for k, i in enumerate(which):
            gain = 1.0 + ma[i : i + 1]
            a = inv[k : k + 1] * row(3) * gain
            b = row(4) * gain + mb[i : i + 1]
            for r in range(0, POS, CHUNK):
                v = (h1[l, i, r : r + CHUNK, :] - mean[k : k + 1]) * a + b
                put_shifted(bufs, i, r, silu(v))

    def conv_two(which):
        out = conv(which, R_CONV2) + row(7)
        for k, i in enumerate(which):
            own = (xs[l, i] + out[k * POS : (k + 1) * POS]) * RS
            sums[i] = norm_sums(own)
            y[l, i] = own

    def third(which):
        mean, inv = norm_stats([sums[i] for i in which])
        keep(which, mean, inv, S_M3)
        for k, i in enumerate(which):
            a = inv[k : k + 1] * row(8)
            for r in range(0, POS, CHUNK):
                v = (y[l, i, r : r + CHUNK, :] - mean[k : k + 1]) * a + row(9)
                nbuf[i, r : r + CHUNK, :] = v.astype(BF16)

    def project_in(which):
        n = jnp.concatenate([nbuf[i] for i in which], axis=0)
        for j, at in ((0, 10), (1, None), (2, 11)):
            part = dot_nn(n, qkvw[:, j * C : (j + 1) * C])
            if at is not None:
                part = part + row(at)
            part = part.astype(BF16)
            for k, i in enumerate(which):
                qkv[l, i, :, j * C : (j + 1) * C] = part[k * POS : (k + 1) * POS]

    def attend(which):
        scores = [dot_nt(qkv[l, i, :, 0:C], qkv[l, i, :, C : 2 * C]) for i in which]
        for s, i in zip(scores, which):
            e = jnp.exp((s - jnp.max(s, axis=1, keepdims=True)) * (C**-0.5))
            p = (e * (1.0 / jnp.sum(e, axis=1, keepdims=True))).astype(BF16)
            att[l, i] = p
            o[l, i] = dot_nn(p, qkv[l, i, :, 2 * C :]).astype(BF16)

    def project_out(which):
        left = jnp.concatenate([o[l, i] for i in which], axis=0)
        out = dot_nn(left, w[l, R_PROJ:, :]) + row(12)
        for k, i in enumerate(which):
            xs[l + 1, i] = (y[l, i] + out[k * POS : (k + 1) * POS]) * RS

    steps = (first, conv_one, second, conv_two, third, project_in, attend, project_out)
    if not staged:
        for step in steps:
            step(range(images))
            pump(l)
    else:
        stagger([lambda i, step=step: step([i]) for step in steps], images, lambda: pump(l))


def layer_backward(
    l, w, small, eo, xs, h1, y, qkv, att, o, st, g, bufs, nbuf, qkvw, tmp, dn, dqkv, act_t,
    grad, sgrad, pump, need_dx=None,
):
    want = grad is not None
    images = h1.shape[1]
    which = range(images)
    flat = images * POS
    scale = C**-0.5
    split_qkv(w, l, qkvw, tmp)

    def row(k):
        return small[l, k : k + 1, :]

    def rows8(rows):
        return jnp.concatenate(list(rows) + [jnp.zeros((8 - len(rows), C), F32)], axis=0)

    zero = jnp.zeros((1, C), F32)
    gps, c1, c2, p1, p2 = {}, {}, {}, {}, {}
    total = {7: zero, 2: zero}
    gains = [1.0 + st[l, i, S_MA : S_MA + 1, :] for i in which]

    def project_out(i):
        gps[i] = (g[i] * RS).astype(BF16)
        nbuf[i] = dot_nt(gps[i], w[l, R_PROJ:, :]).astype(BF16)

    def attend(i):
        p = att[l, i]
        pf = p.astype(F32)
        dp = dot_nt(nbuf[i], qkv[l, i, :, 2 * C :])
        ds = (pf * (dp - jnp.sum(dp * pf, axis=1, keepdims=True))).astype(BF16)
        dqkv[i, :, 0:C] = (dot_nn(ds, qkv[l, i, :, C : 2 * C]) * scale).astype(BF16)
        dqkv[i, :, C : 2 * C] = (dot_tn(ds, qkv[l, i, :, 0:C]) * scale).astype(BF16)
        dqkv[i, :, 2 * C :] = dot_tn(p, nbuf[i]).astype(BF16)

    def project_in(i):
        mean, inv = st[l, i, S_M3 : S_M3 + 1, :], st[l, i, S_I3 : S_I3 + 1, :]
        d = dot_nt(dqkv[i], qkvw[...])
        dn[i] = d
        c1[i] = colsum(d)
        c2[i] = colsum(d * ((y[l, i] - mean) * inv))

    def third(i):
        mean, inv = st[l, i, S_M3 : S_M3 + 1, :], st[l, i, S_I3 : S_I3 + 1, :]
        mg, mc = two_means(row(8) * c1[i], row(8) * c2[i])
        for r in range(0, POS, CHUNK):
            nh = (y[l, i, r : r + CHUNK, :] - mean) * inv
            gm = g[i, r : r + CHUNK, :] * RS + inv * (row(8) * dn[i, r : r + CHUNK, :] - mg - nh * mc)
            gm = gm * RS
            g[i, r : r + CHUNK, :] = gm
            put_shifted(bufs, i, r, gm)
            if want:
                nbuf[i, r : r + CHUNK, :] = (nh * row(8) + row(9)).astype(BF16)
                total[7] = total[7] + colsum(gm)

    def conv_grad(i, at):
        left = jnp.concatenate(tap_rows(bufs, True, [i]), axis=1)
        parts = [w[l, at + t * C : at + (t + 1) * C, :] for t in range(9)]
        dn[i] = dot_nt(left, jnp.concatenate(parts, axis=1))

    def activation(i, src, mean, inv, a, b, act=None):
        s1, s2 = zero, zero
        for r in range(0, POS, CHUNK):
            nh = (src[l, i, r : r + CHUNK, :] - mean) * inv
            pre = nh * a + b
            s, slope = silu_parts(pre)
            d = dn[i, r : r + CHUNK, :] * slope
            dn[i, r : r + CHUNK, :] = d
            s1 = s1 + colsum(d)
            s2 = s2 + colsum(d * nh)
            if act is not None:
                act[i, r : r + CHUNK, :] = (pre * s).astype(BF16)
        p1[i], p2[i] = s1, s2

    def second_a(i):
        mean, inv = st[l, i, S_M2 : S_M2 + 1, :], st[l, i, S_I2 : S_I2 + 1, :]
        b = row(4) * gains[i] + st[l, i, S_MB : S_MB + 1, :]
        activation(i, h1, mean, inv, row(3) * gains[i], b, nbuf if want else None)

    def second_b(i):
        mean, inv = st[l, i, S_M2 : S_M2 + 1, :], st[l, i, S_I2 : S_I2 + 1, :]
        full = row(3) * gains[i]
        mg, mc = two_means(full * p1[i], full * p2[i])
        for r in range(0, POS, CHUNK):
            nh = (h1[l, i, r : r + CHUNK, :] - mean) * inv
            dh = inv * (full * dn[i, r : r + CHUNK, :] - mg - nh * mc)
            put_shifted(bufs, i, r, dh)
            if want:
                total[2] = total[2] + colsum(dh)

    def first_a(i):
        mean, inv = st[l, i, S_M1 : S_M1 + 1, :], st[l, i, S_I1 : S_I1 + 1, :]
        activation(i, xs, mean, inv, row(0), row(1))

    def first_act(i):
        mean, inv = st[l, i, S_M1 : S_M1 + 1, :], st[l, i, S_I1 : S_I1 + 1, :]
        for r in range(0, POS, CHUNK):
            v = (xs[l, i, r : r + CHUNK, :] - mean) * (inv * row(0)) + row(1)
            nbuf[i, r : r + CHUNK, :] = silu(v).astype(BF16)

    def first_b(i):
        mean, inv = st[l, i, S_M1 : S_M1 + 1, :], st[l, i, S_I1 : S_I1 + 1, :]
        mg, mc = two_means(row(0) * p1[i], row(0) * p2[i])
        for r in range(0, POS, CHUNK):
            nh = (xs[l, i, r : r + CHUNK, :] - mean) * inv
            dx = inv * (row(0) * dn[i, r : r + CHUNK, :] - mg - nh * mc)
            g[i, r : r + CHUNK, :] = g[i, r : r + CHUNK, :] + dx

    upper = [project_out, attend, project_in, third, lambda i: conv_grad(i, R_CONV2)]
    lower = [lambda i: conv_grad(i, R_CONV1), first_a]
    if not want:
        stagger(upper + [second_a, second_b] + lower + [first_b], images, lambda: pump(l))
        return
    stagger(upper, images, lambda: pump(l))
    gp = jnp.concatenate([gps[i] for i in which], axis=0)
    grad[l, R_PROJ:, :] = dot_tn(o[l].reshape(flat, C), gp).astype(BF16)
    sgrad[l, 12:13, :] = colsum(gp.astype(F32))
    sgrad[l, 7:8, :] = total[7]
    sgrad[l, 8:9, :] = colsum(rows8([c2[i] for i in which]))
    sgrad[l, 9:10, :] = colsum(rows8([c1[i] for i in which]))
    act_t[...] = nbuf[...].reshape(flat, C).T
    for j in range(3):
        dj = dqkv[:, :, j * C : (j + 1) * C].reshape(flat, C)
        part = dot_nn(act_t[...], dj)
        for h in range(2):
            tmp[h, pl.ds(j, C, stride=3), :] = part[:, h * HALF : (h + 1) * HALF]
        if j != 1:
            sgrad[l, 10 + j // 2 : 11 + j // 2, :] = colsum(dj.astype(F32))
    for h in range(2):
        grad[l, R_QKV : R_QKV + 3 * C, h * HALF : (h + 1) * HALF] = tmp[h].astype(BF16)
    for i in which:
        second_a(i)
    pump(l)
    act_t[...] = nbuf[...].reshape(flat, C).T
    conv_weight_grad(act_t, bufs, grad, l, R_CONV2)
    p18, p28, modgain = [rows8([a[i] for i in which]) for a in (p1, p2, gains)]
    dma = row(3) * p28 + row(4) * p18
    sgrad[l, 3:4, :] = colsum(modgain * p28)
    sgrad[l, 4:5, :] = colsum(modgain * p18)
    sgrad[l, 5:6, :] = colsum(dma)
    sgrad[l, 6:7, :] = colsum(p18)
    grad[l, R_EMB : R_EMB + 4 * C, :] = embed_grad(
        eo, jnp.concatenate([dma[0:4], p18[0:4]], axis=0)
    ).astype(BF16)
    pump(l)
    stagger([second_b, first_act], images, lambda: pump(l))
    act_t[...] = nbuf[...].reshape(flat, C).T
    conv_weight_grad(act_t, bufs, grad, l, R_CONV1)
    pump(l)
    stagger(lower, images, lambda: pump(l))
    sgrad[l, 2:3, :] = total[2]
    sgrad[l, 0:1, :] = colsum(rows8([p2[i] for i in which]))
    sgrad[l, 1:2, :] = colsum(rows8([p1[i] for i in which]))

    @pl.when(l == 1)
    def _():
        for i in which:
            first_b(i)


def embed_grad(eo, dm):
    parts, rest = [], dm
    for _ in range(3):
        parts.append(rest.astype(BF16))
        rest = rest - parts[-1].astype(F32)
    left = eo[...]
    return dot_tn(jnp.concatenate([left, left], axis=0), jnp.concatenate(parts[:2], axis=0)) + dot_tn(
        left, parts[2]
    )


def saved_shapes(images):
    return [
        jax.ShapeDtypeStruct((3, images, POS, C), F32),
        jax.ShapeDtypeStruct((2, images, POS, C), F32),
        jax.ShapeDtypeStruct((2, images, POS, C), F32),
        jax.ShapeDtypeStruct((2, images, POS, 3 * C), BF16),
        jax.ShapeDtypeStruct((2, images, POS, POS), BF16),
        jax.ShapeDtypeStruct((2, images, POS, C), BF16),
        jax.ShapeDtypeStruct((2, images, 8, C), F32),
    ]


def forward_kernel(staged, x0, w, small, eo, xs, h1, y, qkv, att, o, st, bufs, nbuf, qkvw, tmp):
    clear_pads(bufs)
    xs[0] = x0[...]

    def body(l, _):
        layer_forward(
            l, w, small, eo, xs, h1, y, qkv, att, o, st, bufs, nbuf, qkvw, tmp, staged, no_pump
        )
        return 0

    lax.fori_loop(0, 2, body, 0)


def backward_kernel(want, *refs):
    cot, w, small, eo, xs, h1, y, qkv, att, o, st, g = refs[:12]
    refs = refs[12:]
    if want:
        grad, sgrad = refs[:2]
        refs = refs[2:]
    else:
        grad, sgrad = None, None
    bufs, nbuf, qkvw, tmp, dn, dqkv, act_t = refs
    clear_pads(bufs)
    g[...] = cot[...]
    if want:
        sgrad[...] = jnp.zeros(sgrad.shape, F32)

    def body(k, _):
        layer_backward(
            1 - k, w, small, eo, xs, h1, y, qkv, att, o, st, g, bufs, nbuf, qkvw, tmp, dn,
            dqkv, act_t, grad, sgrad, no_pump,
        )
        return 0

    lax.fori_loop(0, 2, body, 0)


def vm(n):
    return [pl.BlockSpec(memory_space=pltpu.VMEM)] * n


def scratch_forward(images):
    return [
        pltpu.VMEM((3, images, POS + 2 * PAD, C), BF16),
        pltpu.VMEM((images, POS, C), BF16),
        pltpu.VMEM((C, 3 * C), BF16),
        pltpu.VMEM((2, 3 * C, HALF), F32),
    ]


def run_forward(x0, w, small, eo, staged=False):
    images = x0.shape[0]
    return pl.pallas_call(
        functools.partial(forward_kernel, staged),
        out_shape=saved_shapes(images),
        in_specs=vm(4),
        out_specs=vm(7),
        scratch_shapes=scratch_forward(images),
        compiler_params=pltpu.CompilerParams(vmem_limit_bytes=VMEM_LIMIT),
    )(x0, w, small, eo)


def run_backward(cot, w, small, eo, saved, want):
    images = cot.shape[0]
    outs = [jax.ShapeDtypeStruct(cot.shape, F32)]
    if want:
        outs += [
            jax.ShapeDtypeStruct((2, ROWS, C), BF16),
            jax.ShapeDtypeStruct((2, 16, C), F32),
        ]
    return pl.pallas_call(
        functools.partial(backward_kernel, want),
        out_shape=outs,
        in_specs=vm(11),
        out_specs=vm(len(outs)),
        scratch_shapes=scratch_forward(images)
        + [
            pltpu.VMEM((images, POS, C), F32),
            pltpu.VMEM((images, POS, 3 * C), BF16),
            pltpu.VMEM((C, images * POS), BF16),
        ],
        compiler_params=pltpu.CompilerParams(vmem_limit_bytes=VMEM_LIMIT),
    )(cot, w, small, eo, *saved)


PLANES, PLANE = 4, 4
MESH = pl.DeviceIdType.MESH


class Place:
    def __init__(self):
        self.sec = lax.axis_index("section")
        self.d = lax.axis_index("dp")
        self.x = lax.rem(self.d, 2)
        self.y = lax.rem(self.d // 2, 2)
        self.z = self.d // PLANE
        self.seat = self.sec * PLANE + lax.rem(self.d, PLANE)
        self.sib = {"section": 1 - self.sec}
        self.xn = {"dp": self.d + 1 - 2 * self.x}
        self.yn = {"dp": self.d + 2 - 4 * self.y}

    def plane(self, j):
        return lax.rem(self.z + j + PLANES, PLANES)

    def zpeer(self, j):
        return {"dp": self.plane(j) * PLANE + lax.rem(self.d, PLANE)}

    def plane_peer(self, j):
        seat = lax.rem(self.seat + j, 2 * PLANE)
        return {"section": seat // PLANE, "dp": self.z * PLANE + lax.rem(seat, PLANE)}

    def meet(self):
        barrier = pltpu.get_barrier_semaphore()
        others = [self.plane_peer(j) for j in range(1, 8)] + [self.zpeer(j) for j in (1, 2, 3)]
        for other in others:
            pl.semaphore_signal(barrier, inc=1, device_id=other, device_id_type=MESH)
        pl.semaphore_wait(barrier, len(others))


def remote(src, dst, send, recv, target):
    return pltpu.make_async_remote_copy(
        src_ref=src, dst_ref=dst, send_sem=send, recv_sem=recv,
        device_id=target, device_id_type=MESH,
    )


Z1, X1, Y1, X2, Y2, S_OWN, S_X, S_Y, S_DA, S_DB = 0, 3, 7, 11, 15, 19, 23, 27, 31, 35
SLOTS = 39


class Gather:
    def __init__(self, me, net, stage, local_sem, send_sem, recv_sem):
        self.me, self.net, self.stage = me, net, stage
        self.local_sem, self.send_sem, self.recv_sem = local_sem, send_sem, recv_sem
        self.part = stage.shape[0]
        self.half = self.part // 2

    def rows(self, plane, y, x, lo, count):
        at = (plane * PLANE + y * 2 + x) * self.part + lo
        return self.net.at[self.me.sec, pl.ds(pl.multiple_of(at, 16), count)]

    def own(self, j):
        return self.rows(self.me.plane(-j), self.me.y, self.me.x, 0, self.part)

    def send(self, slot, piece, target, src=None):
        src = piece if src is None else src
        remote(src, piece, self.send_sem.at[slot], self.recv_sem.at[slot], target).start()

    def arrived(self, slot, piece):
        remote(
            piece, piece, self.send_sem.at[slot], self.recv_sem.at[slot], self.me.sib
        ).wait_recv()

    def local(self):
        return pltpu.make_async_copy(self.stage, self.own(0), self.local_sem)

    def begin(self):
        me = self.me
        for j in (1, 2, 3):
            self.send(Z1 + j - 1, self.own(0), me.zpeer(j), self.stage)
        for slot, target in ((X1, me.xn), (Y1, me.yn), (S_OWN, me.sib)):
            self.send(slot, self.own(0), target, self.stage)
        self.local().start()

    def phase1(self):
        def step(j):
            me = self.me
            self.arrived(Z1 + j - 1, self.own(j))
            for slot, target in ((X1, me.xn), (Y1, me.yn), (S_OWN, me.sib)):
                self.send(slot + j, self.own(j), target)

        return [lambda j=j: step(j) for j in (1, 2, 3)]

    def phase2(self):
        me, part, half = self.me, self.part, self.half

        def step_x(j):
            plane = me.plane(-j)
            self.arrived(X1 + j, self.rows(plane, me.y, 1 - me.x, 0, part))
            self.send(Y2 + j, self.rows(plane, me.y, 1 - me.x, 0, half), me.yn)
            self.send(S_X + j, self.rows(plane, me.y, 1 - me.x, 0, part), me.sib)

        def step_y(j):
            plane = me.plane(-j)
            self.arrived(Y1 + j, self.rows(plane, 1 - me.y, me.x, 0, part))
            self.send(X2 + j, self.rows(plane, 1 - me.y, me.x, half, half), me.xn)
            self.send(S_Y + j, self.rows(plane, 1 - me.y, me.x, 0, part), me.sib)

        return [lambda f=f, j=j: f(j) for j in range(PLANES) for f in (step_x, step_y)]

    def phase3(self):
        def step(j, slot, to, lo):
            me = self.me
            where = self.rows(me.plane(-j), 1 - me.y, 1 - me.x, lo, self.half)
            self.arrived(slot + j, where)
            self.send(to + j, where, me.sib)

        return [
            lambda j=j, a=a: step(j, *a)
            for j in range(PLANES)
            for a in ((Y2, S_DA, 0), (X2, S_DB, self.half))
        ]

    def finish(self):
        def step():
            for slot in range(S_OWN, SLOTS):
                count = self.part if slot < S_DA else self.half
                self.arrived(slot, self.rows(0, 0, 0, 0, count))
            self.local().wait()

        return [step]

    def drain(self):
        for slot in range(SLOTS):
            whole = slot < X2 or S_OWN <= slot < S_DA
            piece = self.rows(0, 0, 0, 0, self.part if whole else self.half)
            remote(
                piece, piece, self.send_sem.at[slot], self.recv_sem.at[slot], self.me.sib
            ).wait_send()


A_SLOT, B_SLOT, C_SLOT, D_SLOT = 0, 4, 20, 28
R_SLOTS = 31


class Reduce:
    def __init__(self, me, big, shard, sib, there, rb, rc, rd, ssem, rsem):
        self.me, self.big, self.shard = me, big, shard
        self.sib, self.there, self.rb, self.rc, self.rd = sib, there, rb, rc, rd
        self.ssem, self.rsem = ssem, rsem
        self.part = shard.shape[0]
        self.half = self.part // 2
        self.span = PLANE * self.part

    def zt(self, k):
        return (3, 2, 0, 1)[k]

    def block(self, k):
        return pl.ds(self.zt(k) * self.span, self.span)

    def piece(self, k, y, x, lo, count):
        at = (self.zt(k) * PLANE + y * 2 + x) * self.part + lo
        return pl.ds(pl.multiple_of(at, 16), count)

    def send(self, src, dst, slot, target):
        remote(src, dst, self.ssem.at[slot], self.rsem.at[slot], target).start()

    def arrived(self, dst, slot):
        remote(dst, dst, self.ssem.at[slot], self.rsem.at[slot], self.me.sib).wait_recv()

    def begin(self):
        for k in range(PLANES):
            self.begin_block(k)

    def begin_block(self, k):
        at = self.block(k)
        self.send(self.big.at[1 - self.me.sec, at], self.there.at[at], A_SLOT + k, self.me.sib)

    def stage_a(self, k):
        me, half = self.me, self.half
        self.arrived(self.sib.at[self.block(k)], A_SLOT + k)
        base = self.zt(k) * self.span

        def body(i, _):
            at = pl.ds(pl.multiple_of(base + i * half, 16), half)
            self.big[me.sec, at, :] = (
                self.big[me.sec, at, :].astype(F32) + self.sib[at, :].astype(F32)
            ).astype(BF16)
            return 0

        lax.fori_loop(0, 2 * PLANE, body, 0)
        for j in range(2):
            self.send(
                self.big.at[me.sec, self.piece(k, 1 - me.y, j, 0, half)], self.rb.at[k, j],
                B_SLOT + 4 * k + j, me.yn,
            )
            self.send(
                self.big.at[me.sec, self.piece(k, j, 1 - me.x, half, half)], self.rb.at[k, 2 + j],
                B_SLOT + 4 * k + 2 + j, me.xn,
            )

    def join(self, where, other):
        self.big[self.me.sec, where, :] = (
            self.big[self.me.sec, where, :].astype(F32) + other.astype(F32)
        ).astype(BF16)

    def stage_c(self, k):
        me, half = self.me, self.half
        for j in range(4):
            self.arrived(self.rb.at[k, j], B_SLOT + 4 * k + j)
            y, x, lo = (me.y, j, 0) if j < 2 else (j - 2, me.x, half)
            self.join(self.piece(k, y, x, lo, half), self.rb[k, j])
        self.send(
            self.big.at[me.sec, self.piece(k, me.y, 1 - me.x, 0, half)], self.rc.at[k, 0],
            C_SLOT + 2 * k, me.xn,
        )
        self.send(
            self.big.at[me.sec, self.piece(k, 1 - me.y, me.x, half, half)], self.rc.at[k, 1],
            C_SLOT + 2 * k + 1, me.yn,
        )

    def stage_d(self, k):
        me, half, zt = self.me, self.half, self.zt(k)
        for j in range(2):
            self.arrived(self.rc.at[k, j], C_SLOT + 2 * k + j)
            self.join(self.piece(k, me.y, me.x, j * half, half), self.rc[k, j])

        @pl.when(me.z != zt)
        def _():
            self.send(
                self.big.at[me.sec, self.piece(k, me.y, me.x, 0, self.part)],
                self.rd.at[lax.rem(zt - me.z + PLANES, PLANES) - 1],
                D_SLOT + lax.rem(zt - me.z + PLANES, PLANES) - 1,
                {"dp": zt * PLANE + lax.rem(me.d, PLANE)},
            )

    def stage_e(self):
        for j in range(PLANES - 1):
            self.arrived(self.rd.at[j], D_SLOT + j)
        at = pl.ds(pl.multiple_of(self.me.d * self.part, 16), self.part)
        self.shard[...] = (
            self.big[self.me.sec, at, :].astype(F32)
            + self.rd[0].astype(F32) + (self.rd[1].astype(F32) + self.rd[2].astype(F32))
        )

    def steps(self):
        out = []
        for t in range(PLANES + 2):
            for stage, lag in ((self.stage_a, 0), (self.stage_c, 1), (self.stage_d, 2)):
                if 0 <= t - lag < PLANES:
                    out.append(lambda stage=stage, k=t - lag: stage(k))
        return out

    def drain(self, lo=0, hi=R_SLOTS):
        for slot in range(lo, hi):
            if slot < B_SLOT:
                piece = self.there.at[pl.ds(0, self.span)]
            elif slot < D_SLOT:
                piece = self.rb.at[0, 0]
            else:
                piece = self.rd.at[0]
            remote(piece, piece, self.ssem.at[slot], self.rsem.at[slot], self.me.sib).wait_send()


def reduce_scratch(part):
    half = part // 2
    return [
        pltpu.VMEM((PLANES, 4, half, C), BF16),
        pltpu.VMEM((PLANES, 2, half, C), BF16),
        pltpu.VMEM((PLANES - 1, part, C), BF16),
        pltpu.SemaphoreType.DMA((R_SLOTS,)),
        pltpu.SemaphoreType.DMA((R_SLOTS,)),
    ]


class Totals:
    def __init__(self, me, buf, recv, ssem, rsem):
        self.me, self.buf, self.recv, self.ssem, self.rsem = me, buf, recv, ssem, rsem

    def send(self, src, dst, slot, target):
        remote(src, dst, self.ssem.at[slot], self.rsem.at[slot], target).start()

    def arrived(self, dst, slot):
        remote(dst, dst, self.ssem.at[slot], self.rsem.at[slot], self.me.sib).wait_recv()

    def begin(self, first):
        self.send(first, self.recv.at[0], 0, self.me.sib)

    def steps(self):
        me, buf, recv = self.me, self.buf, self.recv

        def one():
            self.arrived(recv.at[0], 0)
            buf[1] = buf[0] + recv[0]
            self.send(buf.at[1], recv.at[1], 1, me.xn)

        def two():
            self.arrived(recv.at[1], 1)
            buf[2] = buf[1] + recv[1]
            self.send(buf.at[2], recv.at[2], 2, me.yn)

        def three():
            self.arrived(recv.at[2], 2)
            buf[3] = buf[2] + recv[2]
            recv[3 + me.z] = buf[3]
            for j in (1, 2, 3):
                self.send(buf.at[3], recv.at[3 + me.z], 2 + j, me.zpeer(j))

        return [one, two, three]

    def result(self):
        for j in (1, 2, 3):
            self.arrived(self.recv.at[3 + self.me.plane(-j)], 2 + j)
        return (self.recv[3] + self.recv[4]) + (self.recv[5] + self.recv[6])

    def drain(self):
        for slot in range(6):
            piece = self.recv.at[0]
            remote(piece, piece, self.ssem.at[slot], self.rsem.at[slot], self.me.sib).wait_send()


class Squares:
    def __init__(self, me, own, recv, ssem, rsem):
        self.me, self.own, self.recv, self.ssem, self.rsem = me, own, recv, ssem, rsem

    def hop(self, src, base, mine, peers, slots):
        for j, target in peers:
            dst = self.recv.at[base + mine]
            remote(src, dst, self.ssem.at[slots + j], self.rsem.at[slots + j], target).start()
        self.recv[base + mine] = src[...]
        for j, _ in peers:
            dst = self.recv.at[base]
            remote(dst, dst, self.ssem.at[slots + j], self.rsem.at[slots + j], self.me.sib).wait_recv()

    def run(self):
        me, recv = self.me, self.recv
        self.hop(self.own.at[0], 0, me.seat, [(j, me.plane_peer(j)) for j in range(1, 8)], -1)
        pairs = [recv[2 * k] + recv[2 * k + 1] for k in range(4)]
        self.own[1] = (pairs[0] + pairs[1]) + (pairs[2] + pairs[3])
        self.hop(self.own.at[1], 8, me.z, [(j, me.zpeer(j)) for j in (1, 2, 3)], 6)
        return (recv[8] + recv[9]) + (recv[10] + recv[11])

    def drain(self):
        for slot in range(10):
            piece = self.recv.at[0]
            remote(piece, piece, self.ssem.at[slot], self.rsem.at[slot], self.me.sib).wait_send()


def squares_scratch(shape):
    return [
        pltpu.VMEM((2,) + shape, F32),
        pltpu.VMEM((12,) + shape, F32),
        pltpu.SemaphoreType.DMA((10,)),
        pltpu.SemaphoreType.DMA((10,)),
    ]


def totals_scratch(shape):
    return [
        pltpu.VMEM((4,) + shape, F32),
        pltpu.VMEM((7,) + shape, F32),
        pltpu.SemaphoreType.DMA((6,)),
        pltpu.SemaphoreType.DMA((6,)),
    ]


def saved_scratch(images):
    return [pltpu.VMEM(a.shape, a.dtype) for a in saved_shapes(images)]


def backward_scratch(images):
    return scratch_forward(images) + [
        pltpu.VMEM((images, POS, C), F32),
        pltpu.VMEM((images, POS, 3 * C), BF16),
        pltpu.VMEM((C, images * POS), BF16),
    ]


GEN_TOTAL = SIGMA_INIT**2 + SIGMA_DATA**2
GEN_IN = GEN_TOTAL**-0.5
GEN_SKIP = SIGMA_DATA**2 / GEN_TOTAL
GEN_OUT = SIGMA_INIT * SIGMA_DATA * GEN_TOTAL**-0.5
T_IN, T_SKIP, T_OUT, T_SIGMA, T_FACTOR = range(5)


def fill_embed(eo, sigmas):
    at = lax.broadcasted_iota(jnp.int32, (8, 4 * C), 1)
    side = lax.broadcasted_iota(jnp.int32, (8, 4 * C), 0) // 4
    k = at // 2
    power = (k & (C - 1)).astype(F32) * (1.0 / C)
    rows = sigmas + [jnp.ones_like(sigmas[0])] * (4 - len(sigmas))
    angle = jnp.log(jnp.concatenate(rows + rows, axis=0)) * 0.25 * jnp.exp(power * -LOG_10000)
    wave = jnp.where(k < C, jnp.cos(angle), jnp.sin(angle))
    eo[...] = jnp.where((at & 1) == side, wave, 0.0).astype(BF16)


LOG_10000 = 9.210340371976184


def step_kernel(*refs):
    (
        z_all, eps_all, levels, counts, gen_w, fake_w, teacher_w, gen_small, fake_small,
        teacher_small,
        gw_out, sv_x, sv_h, sv_y, sv_q, sv_a, sv_o, sv_s, gshard, fshard, stot, sqtot,
        *refs,
    ) = refs
    gen_out = (sv_x, sv_h, sv_y, sv_q, sv_a, sv_o, sv_s)
    w_gen, w_fake, w_teach = refs[:3]
    sv_one, sv_two = refs[3:10], refs[10:17]
    bufs, nbuf, qkvw, tmp, dn, dqkv, act_t = refs[17:24]
    zb, eb, g, stage, local_sem, send_sem, recv_sem, copy_sem = refs[24:32]
    smalls, small_sem, gen_eo, score_eo, tab, sgrads, part_sums = refs[32:39]
    fake_refs, gen_refs = refs[39:44], refs[44:49]
    small_refs, square_refs = refs[49:53], refs[53:57]
    sib, free_sem = refs[57:59]
    g2 = sv_two[0].at[2]
    images = zb.shape[0]
    me = Place()
    start = me.sec * images

    def run(steps):
        for step in steps:
            step()

    def mine(ref):
        return ref.at[pl.ds(start, images)]

    loads = [
        pltpu.make_async_copy(mine(z_all), zb, copy_sem.at[0]),
        pltpu.make_async_copy(mine(eps_all), eb, copy_sem.at[1]),
    ]
    for copy in loads:
        copy.start()
    masters = [
        pltpu.make_async_copy(src, dst, copy_sem.at[2 + k])
        for k, (src, dst) in enumerate(((gen_w, gshard), (fake_w, fshard), (teacher_w, stage.at[2])))
    ]
    for copy in masters:
        copy.start()
    smalls[...] = jnp.zeros(smalls.shape, F32)
    for n, ref in enumerate((gen_small, fake_small, teacher_small)):
        for r in range(13):
            smalls[me.sec, n, r : r + 1, :] = ref[r]
    gathers = [
        Gather(me, net, stage.at[n], local_sem.at[n], send_sem.at[n], recv_sem.at[n])
        for n, net in enumerate((w_gen, w_fake, w_teach))
    ]
    for copy in masters:
        copy.wait()
    stage[0] = gshard[...].astype(BF16)
    stage[1] = fshard[...].astype(BF16)
    me.meet()
    gathers[0].begin()
    swap = remote(
        smalls.at[me.sec], smalls.at[me.sec], small_sem.at[0], small_sem.at[1], me.sib
    )
    swap.start()

    clear_pads(bufs)
    sgrads[...] = jnp.zeros(sgrads.shape, F32)
    sigmas = []
    valid_sum = jnp.zeros((1, 4 * C), F32)
    for i in range(images):
        level = jnp.zeros((1, 4 * C), jnp.int32) + levels[start + i]
        sigma = SIGMA_TOP + level.astype(F32) / (LEVELS - 1) * (SIGMA_BOTTOM - SIGMA_TOP)
        square = sigma * sigma
        sigma = square * square * square * sigma
        sigmas.append(sigma)
        s_in, s_skip, s_out, s_lam = precondition(sigma)
        valid = jnp.where(jnp.zeros_like(level) + (start + i) < counts[0], 1.0, 0.0)
        valid_sum = valid_sum + valid
        rows = (s_in, s_skip, s_out, sigma, valid * s_lam * (1.0 / (POS * C)))
        for k, value in enumerate(rows):
            tab[i, k : k + 1, :] = value[:, :C]
    fill_embed(score_eo, sigmas)
    fill_embed(gen_eo, [jnp.full((1, 4 * C), SIGMA_INIT, F32)] * images)

    def forward(n, w, eo, sv, pump):
        def body(l, _):
            layer_forward(
                l, w, smalls.at[:, n], eo, *sv, bufs, nbuf, qkvw, tmp, True, pump
            )
            return 0

        lax.fori_loop(0, 2, body, 0)

    def backward(n, w, eo, sv, cot, grad, sgrad, pump):
        def body(k, _):
            layer_backward(
                1 - k, w, smalls.at[:, n], eo, *sv, cot, bufs, nbuf, qkvw, tmp, dn, dqkv,
                act_t, grad, sgrad, pump,
            )
            return 0

        lax.fori_loop(0, 2, body, 0)

    def each(f):
        def body(i, carry):
            return f(i, [tab[i, k : k + 1, :] for k in range(5)], carry)

        return lax.fori_loop(0, images, body, jnp.zeros((1, C), F32))

    z_now, z_next = gathers[0].phase1(), gathers[1].phase1()
    run(z_now[:2] + [gathers[1].begin] + z_now[2:] + gathers[0].phase2() + z_next[:1])
    last = gathers[0].phase3()
    run(last[:4] + z_next[1:2] + [gathers[2].begin] + last[4:] + z_next[2:])
    for copy in loads:
        copy.wait()
    sv_one[0][0] = zb[...] * (GEN_IN * SIGMA_INIT)
    swap.wait()
    run(gathers[0].finish())
    later = gathers[1].phase2()
    forward(0, w_gen, gen_eo, sv_one, Pump(later[:5], FORWARD_POINTS, (0, 1)))
    pairs = [(w_gen, gw_out)] + list(zip(sv_one, gen_out))
    stores = [
        pltpu.make_async_copy(src, dst, copy_sem.at[2 + k]) for k, (src, dst) in enumerate(pairs)
    ]
    for copy in stores:
        copy.start()

    def noisy(i, t, carry):
        zb[i] = zb[i] * (GEN_SKIP * SIGMA_INIT) + GEN_OUT * sv_one[0][2, i]
        eb[i] = zb[i] + t[T_SIGMA] * eb[i]
        sv_two[0][0, i] = t[T_IN] * eb[i]
        return carry

    each(noisy)
    z_next, last = gathers[2].phase1(), gathers[1].phase3()
    run(later[5:] + z_next[:1] + last[:4] + z_next[1:2] + last[4:] + z_next[2:])
    run(gathers[1].finish())
    later = gathers[2].phase2()
    forward(1, w_fake, score_eo, sv_two, Pump(later[:5], FORWARD_POINTS, (0, 1)))
    later = later[5:] + gathers[2].phase3()

    def fake_loss(i, t, total):
        den = t[T_SKIP] * eb[i] + t[T_OUT] * sv_two[0][2, i]
        sv_two[0][2, i] = den
        miss = den - zb[i]
        g[i] = (2.0 * t[T_OUT] * t[T_FACTOR]) * miss
        return total + t[T_FACTOR] * colsum(miss * miss)

    loss_fake = each(fake_loss)
    for copy in stores:
        copy.wait()
    gathers[0].drain()
    backward(
        1, w_fake, score_eo, sv_two, g, w_gen, sgrads.at[:, 1],
        Pump(later, WEIGHT_POINTS, (1, 0), 0.0, 0.8),
    )
    fake_sum = Reduce(me, w_gen, fshard, sib, sib, *fake_refs)
    fake_sum.begin()
    run(gathers[2].finish())
    later = fake_sum.steps()
    sv_one[0][0] = sv_two[0][0]
    forward(2, w_teach, score_eo, sv_one, Pump(later[:5], FORWARD_POINTS, (0, 1), 0.2))

    def gen_loss(i, t, total):
        den = t[T_SKIP] * eb[i] + t[T_OUT] * sv_one[0][2, i]
        fake_den = sv_two[0][2, i]
        miss = fake_den - zb[i]
        gap = den - fake_den
        scale = t[T_OUT] * t[T_FACTOR]
        g[i] = scale * ((2.0 * (1.0 - ALPHA_MIX)) * gap + miss)
        g2[i] = scale * ((1.0 - 2.0 * (1.0 - ALPHA_MIX)) * gap - miss)
        zb[i] = (t[T_FACTOR] * (t[T_SKIP] - 1.0)) * gap
        return total + t[T_FACTOR] * colsum(gap * ((1.0 - ALPHA_MIX) * gap + miss))

    loss_gen = each(gen_loss)
    backward(
        2, w_teach, score_eo, sv_one, g, None, None, Pump(later[5:9], BACKWARD_POINTS, (1, 0))
    )
    gathers[2].drain()
    fake_sum.drain(A_SLOT, B_SLOT)
    pl.semaphore_signal(free_sem, inc=1, device_id=me.sib, device_id_type=MESH)
    back = [
        pltpu.make_async_copy(src, dst, copy_sem.at[2 + k])
        for k, (dst, src) in enumerate([(w_teach, gw_out)] + list(zip(sv_one, gen_out)))
    ]
    for copy in back:
        copy.start()
    backward(
        1, w_fake, score_eo, sv_two, g2, None, None, Pump(later[9:], BACKWARD_POINTS, (1, 0))
    )

    def gen_gradient(i, t, carry):
        g[i] = GEN_OUT * (zb[i] + t[T_IN] * (g[i] + g2[i]))
        return carry

    each(gen_gradient)
    gathers[1].drain()
    for copy in back:
        copy.wait()

    gen_sum = Reduce(me, w_fake, gshard, w_gen.at[1 - me.sec], w_gen.at[me.sec], *gen_refs)
    later = gen_sum.steps()

    def on_section(s, steps):
        pl.when(me.sec == s)(lambda: run(steps))

    def hand_over():
        pl.semaphore_wait(free_sem, 1)

    pump = Pump([], WEIGHT_POINTS, (1, 0))

    def at(layer, point, section, steps):
        pump.table[layer][point].append(lambda: on_section(section, steps))

    upper = [hand_over, lambda: gen_sum.begin_block(0), lambda: gen_sum.begin_block(1)]
    lower = [lambda: gen_sum.begin_block(2), lambda: gen_sum.begin_block(3)]
    for layer, giver in ((1, 0), (0, 1)):
        at(layer, HALF_WAY, giver, upper)
        at(layer, READY, giver, lower)
    for k, step in enumerate(later):
        at(0, k * READY // len(later), 1, [step])
    at(0, READY, 0, later[:1])
    at(0, READY + 2, 0, later[1:2])
    at(0, READY + 4, 0, later[2:3])
    backward(0, w_teach, gen_eo, sv_one, g, w_fake, sgrads.at[:, 0], pump)

    def spread_sum(total):
        return jnp.broadcast_to(jnp.sum(total, axis=1, keepdims=True), (1, C))

    sums = jnp.concatenate([spread_sum(loss_gen), spread_sum(loss_fake), valid_sum[:, :C]], axis=0)
    for s in range(2):
        part_sums[s, 0:16, :] = sgrads[s, 0]
        part_sums[s, 13:16, :] = sums
        part_sums[s, 16:32, :] = sgrads[s, 1]
    small = Totals(me, *small_refs)
    small_refs[0][0] = part_sums[me.sec]
    small.begin(part_sums.at[1 - me.sec])
    fake_sum.stage_e()
    small_steps = small.steps()
    on_section(0, later[3:6])
    run(small_steps[:1])
    on_section(0, later[6:8])
    run(small_steps[1:2])
    on_section(0, later[8:10])
    run(small_steps[2:])
    on_section(0, later[10:])
    stot[...] = small.result()
    own = square_refs[0]
    keep = lax.broadcasted_iota(jnp.int32, (16, C), 0) < 13
    for n, rows in ((1, fshard), (0, gshard)):
        if n == 0:
            gen_sum.stage_e()
        low = jnp.square(jnp.where(keep, stot[16 * n : 16 * n + 16, :], 0.0))
        low = jnp.where(me.d == 0, low[0:8] + low[8:16], 0.0)
        big = jnp.sum(jnp.square(rows[...]).reshape(rows.shape[0] // 8, 8, C), axis=0)
        own[0, 8 * n : 8 * n + 8, :] = big + low
    square = Squares(me, *square_refs)
    sqtot[...] = square.run()
    fake_sum.drain(B_SLOT)
    for done in (gen_sum, small, square):
        done.drain()


SIGMA_TOP = SIGMA_HIGH ** (1.0 / RHO_POWER)
SIGMA_BOTTOM = SIGMA_LOW ** (1.0 / RHO_POWER)


def run_step(z, eps, levels, counts, gen_w, fake_w, teacher_w, smalls):
    part = gen_w.shape[0]
    images = z.shape[0] // 2
    any_ = pl.BlockSpec(memory_space=pl.ANY)
    smem = pl.BlockSpec(memory_space=pltpu.SMEM)
    saved = saved_shapes(images)
    return pl.pallas_call(
        step_kernel,
        out_shape=[jax.ShapeDtypeStruct((2, ROWS, C), BF16)]
        + saved
        + [
            jax.ShapeDtypeStruct((part, C), F32),
            jax.ShapeDtypeStruct((part, C), F32),
            jax.ShapeDtypeStruct((32, C), F32),
            jax.ShapeDtypeStruct((16, C), F32),
        ],
        in_specs=[any_] * 2 + [smem] * 2 + [any_] * 3 + vm(3),
        out_specs=[any_] * 8 + vm(4),
        scratch_shapes=[pltpu.VMEM((2, ROWS, C), BF16)] * 3
        + saved_scratch(images) * 2
        + backward_scratch(images)
        + [pltpu.VMEM((images, POS, C), F32)] * 3
        + [
            pltpu.VMEM((3, part, C), BF16),
            pltpu.SemaphoreType.DMA((3,)),
            pltpu.SemaphoreType.DMA((3, SLOTS)),
            pltpu.SemaphoreType.DMA((3, SLOTS)),
            pltpu.SemaphoreType.DMA((10,)),
            pltpu.VMEM((2, 3, 16, C), F32),
            pltpu.SemaphoreType.DMA((2,)),
            pltpu.VMEM((8, 4 * C), BF16),
            pltpu.VMEM((8, 4 * C), BF16),
            pltpu.VMEM((images, 8, C), F32),
            pltpu.VMEM((2, 2, 16, C), F32),
            pltpu.VMEM((2, 32, C), F32),
        ]
        + reduce_scratch(part) * 2
        + totals_scratch((32, C))
        + squares_scratch((16, C))
        + [pltpu.VMEM((ROWS, C), BF16), pltpu.SemaphoreType.REGULAR],
        compiler_params=pltpu.CompilerParams(
            collective_id=0, has_side_effects=True, vmem_limit_bytes=STEP_LIMIT
        ),
    )(z, eps, levels, counts, gen_w, fake_w, teacher_w, *smalls)[8:]


def adam_step(master, first_mom, second_mom, grad):
    first_new = BETA_ONE * first_mom + (1.0 - BETA_ONE) * grad
    second_new = BETA_TWO * second_mom + (1.0 - BETA_TWO) * grad * grad
    direction = (
        first_new
        / (1.0 - BETA_ONE**STEP)
        / (jnp.sqrt(second_new / (1.0 - BETA_TWO**STEP)) + ADAM_EPS)
    )
    return (master - LEARN_RATE * (direction + WEIGHT_DECAY * master), first_new, second_new)


EMA_RATE = 0.5 ** (20.0 / STEP)
SMALL_STATES = (4, 5, 6, 7, 11, 12, 13)


def update_kernel(gshard, fshard, stot, sqtot, *refs):
    ins, outs = refs[:14], refs[14:]
    norms, losses = outs[14:]
    count = stot[15:16, 0:1]
    norm_of, scales = [], []
    for n in range(2):
        rows = jnp.sum(sqtot[8 * n : 8 * n + 8, :], axis=0, keepdims=True)
        norm = jnp.sqrt(jnp.sum(rows, axis=1, keepdims=True)) / count
        scales.append(jnp.minimum(1.0, CLIP_NORM / norm) / count)
        norm_of.append(norm)

    def one(at, grad, w, m, v, ema, ow, om, ov, oe):
        new, first, second = adam_step(w[at], m[at], v[at], grad)
        ow[at] = new
        om[at] = first
        ov[at] = second
        if ema is not None:
            oe[at] = EMA_RATE * ema[at] + (1.0 - EMA_RATE) * new

    one(0, gshard[...] * scales[0], *ins[0:4], *outs[0:4])
    one(0, fshard[...] * scales[1], *ins[8:11], None, *outs[8:11], None)

    @pl.when(pl.program_id(0) == 0)
    def _():
        for n in range(2):
            norms[n] = norm_of[n][0, 0]
            losses[n] = (stot[13 + n : 14 + n, 0:1] / count)[0, 0]
        for k in range(13):
            one(k, stot[k : k + 1, :] * scales[0], *ins[4:8], *outs[4:8])
            one(k, stot[16 + k : 17 + k, :] * scales[1], *ins[11:14], None, *outs[11:14], None)


def update_nets(gshard, fshard, stot, sqtot, states):
    def turned(arrays):
        return [a.swapaxes(0, 1) if k in SMALL_STATES else a for k, a in enumerate(arrays)]

    part = gshard.shape[0]
    steps = 1
    big = pl.BlockSpec((1, part // steps, C), lambda i: (0, i, 0))
    low = pl.BlockSpec((13, 1, C), lambda i: (0, 0, 0))
    shard = pl.BlockSpec((part // steps, C), lambda i: (i, 0))
    whole = [pl.BlockSpec(a.shape, lambda i: (0, 0)) for a in (stot, sqtot)]
    specs = [low if k in SMALL_STATES else big for k in range(len(states))]
    states = turned(states)
    res = pl.pallas_call(
        update_kernel,
        grid=(steps,),
        out_shape=[jax.ShapeDtypeStruct(a.shape, F32) for a in states]
        + [jax.ShapeDtypeStruct((2,), F32)] * 2,
        in_specs=[shard] * 2 + whole + specs,
        out_specs=specs + [pl.BlockSpec(memory_space=pltpu.SMEM)] * 2,
        compiler_params=pltpu.CompilerParams(vmem_limit_bytes=VMEM_LIMIT),
    )(gshard, fshard, stot, sqtot, *states)
    return tuple(turned(res[:-2])) + tuple(res[-2:])


def gather_plain(shard):
    rows = lax.all_gather(shard.astype(BF16), "dp", axis=1, tiled=True)
    return lax.all_gather(rows, "section", axis=0, tiled=True)


def reduce_plain(bigs, small):
    shards_, squares = [], []
    own = lax.psum_scatter(small, "section", scatter_dimension=0, tiled=True)
    stot = lax.psum(own, "dp")[0]
    first = lax.axis_index("dp") == 0
    for n, big in enumerate(bigs):
        own = lax.psum_scatter(big, "section", scatter_dimension=0, tiled=True)
        own = lax.psum_scatter(own, "dp", scatter_dimension=1, tiled=True)[0].astype(F32)
        shards_.append(own)
        low = jnp.sum(jnp.square(stot[16 * n : 16 * n + 13]))
        squares.append(jnp.sum(own * own) + jnp.where(first, low, 0.0))
    sq = lax.psum(jnp.stack(squares), ("section", "dp"))
    return *shards_, stot, jnp.zeros((16, C), F32).at[jnp.array([0, 8]), 0].set(sq)


def shards(
    z_noise, eps_noise, levels, counts,
    gen_w, gen_m, gen_v, gen_ema, gen_small, gen_small_m, gen_small_v, gen_small_ema,
    fake_w, fake_m, fake_v, fake_small, fake_small_m, fake_small_v,
    teacher_w, teacher_small,
):
    if lax.axis_size("dp") == PLANES * PLANE:
        smalls = [a.swapaxes(0, 1) for a in (gen_small, fake_small, teacher_small)]
        reduced = run_step(
            z_noise, eps_noise, levels, counts, gen_w[0], fake_w[0], teacher_w[0], smalls
        )
    else:
        reduced = plain_step(
            z_noise, eps_noise, levels, counts, gen_w, fake_w, teacher_w,
            gen_small, fake_small, teacher_small,
        )
    return update_nets(
        *reduced,
        (
            gen_w, gen_m, gen_v, gen_ema, gen_small, gen_small_m, gen_small_v, gen_small_ema,
            fake_w, fake_m, fake_v, fake_small, fake_small_m, fake_small_v,
        ),
    )


def plain_step(
    z_noise, eps_noise, levels, counts, gen_w, fake_w, teacher_w,
    gen_small, fake_small, teacher_small,
):
    images = z_noise.shape[0] // lax.axis_size("section")
    start = lax.axis_index("section") * images

    def mine(a):
        return lax.dynamic_slice_in_dim(a, start, images, 0)

    z, eps = mine(z_noise), mine(eps_noise)
    sigma = sigma_levels(mine(levels))
    valid = (start + jnp.arange(images) < counts[0]).astype(F32)
    valid_sum = jnp.sum(valid)
    gen_eo = spread_embed(jnp.full((images,), SIGMA_INIT, F32))
    score_eo = spread_embed(sigma)
    gs, fs, ts = [
        lax.all_gather(a, "section", axis=0, tiled=True)
        for a in (gen_small, fake_small, teacher_small)
    ]
    gw, fw, tw = gather_plain(gen_w), gather_plain(fake_w), gather_plain(teacher_w)
    s_in, s_skip, s_out, s_lam = precondition(sigma)
    factor = valid * s_lam / (POS * C)
    s_in, s_skip, s_out, sigma, factor = [
        t[:, None, None] for t in (s_in, s_skip, s_out, sigma, factor)
    ]
    raw = SIGMA_INIT * z
    gen_saved = run_forward(GEN_IN * raw, gw, gs, gen_eo)
    samples = GEN_SKIP * raw + GEN_OUT * gen_saved[0][2]
    noisy = samples + sigma * eps
    x0 = s_in * noisy
    fake_saved = run_forward(x0, fw, fs, score_eo)
    fake_den = s_skip * noisy + s_out * fake_saved[0][2]
    miss = fake_den - samples
    _, fake_g, fake_sg = run_backward(
        s_out * 2.0 * factor * miss, fw, fs, score_eo, fake_saved, True
    )
    teacher_saved = run_forward(x0, tw, ts, score_eo)
    teacher_den = s_skip * noisy + s_out * teacher_saved[0][2]
    gap = teacher_den - fake_den
    loss_gen = jnp.sum(factor * ((1.0 - ALPHA_MIX) * gap * gap + gap * miss))
    loss_fake = jnp.sum(factor * miss * miss)
    grad_teacher = factor * (2.0 * (1.0 - ALPHA_MIX) * gap + miss)
    grad_fake = factor * gap - grad_teacher
    direct = factor * gap * (s_skip - 1.0)
    (back_t,) = run_backward(s_out * grad_teacher, tw, ts, score_eo, teacher_saved, False)
    (back_f,) = run_backward(s_out * grad_fake, fw, fs, score_eo, fake_saved, False)
    gen_cot = GEN_OUT * (direct + s_in * (back_t + back_f))
    _, gen_g, gen_sg = run_backward(gen_cot, gw, gs, gen_eo, gen_saved, True)
    scalars = jnp.broadcast_to(jnp.stack([loss_gen, loss_fake, valid_sum])[:, None], (3, C))
    small_sums = jnp.concatenate(
        [gen_sg[:, :13], jnp.broadcast_to(scalars, (2, 3, C)), fake_sg], axis=1
    )
    return reduce_plain((gen_g, fake_g), small_sums)


def solution(mesh):
    images = P("dp", None, None)
    big = P("section", "dp", None)
    small = P("section", None, None)
    return jax.shard_map(
        shards,
        mesh=mesh,
        in_specs=(images, images, P("dp"), P("dp"))
        + (big,) * 4 + (small,) * 4 + (big,) * 3 + (small,) * 3 + (big, small),
        out_specs=(big,) * 4 + (small,) * 4 + (big,) * 3 + (small,) * 3 + (P(), P()),
        check_vma=False,
    )
```

```python
import functools

import jax
import jax.numpy as jnp
from jax import lax
from jax.experimental import pallas as pl
from jax.experimental.pallas import tpu as pltpu
from jax.sharding import PartitionSpec as P

GROUPS = 32
SIDE = 16
LEVELS = 1000
STEP = 10

SIGMA_DATA = 0.5
SIGMA_INIT = 2.5
SIGMA_LOW = 0.05
SIGMA_HIGH = 20.0
RHO_POWER = 7.0
ALPHA_MIX = 1.2
RS = 0.7071067811865476
NORM_EPS = 1e-05
CLIP_NORM = 0.001
LEARN_RATE = 0.15
BETA_ONE = 0.9
BETA_TWO = 0.999
ADAM_EPS = 1e-08
WEIGHT_DECAY = 0.01

C = 256
HALF = 128
POS = 256
ROWS = 26 * C
CHUNK = 64
PAD = SIDE
F32 = jnp.float32
BF16 = jnp.bfloat16
VMEM_LIMIT = 58 * 2**20
STEP_LIMIT = 63 * 2**20

R_CONV1, R_CONV2, R_EMB, R_QKV, R_PROJ = 0, 9 * C, 18 * C, 22 * C, 25 * C
S_M1, S_I1, S_M2, S_I2, S_M3, S_I3, S_MA, S_MB = range(8)


def sigma_levels(level_ids):
    fraction = level_ids.astype(F32) / (LEVELS - 1)
    top_root = SIGMA_HIGH ** (1.0 / RHO_POWER)
    bottom_root = SIGMA_LOW ** (1.0 / RHO_POWER)
    return (top_root + fraction * (bottom_root - top_root)) ** RHO_POWER


def precondition(sigma_vals):
    total = sigma_vals * sigma_vals + SIGMA_DATA**2
    return (
        lax.rsqrt(total),
        SIGMA_DATA**2 / total,
        sigma_vals * SIGMA_DATA * lax.rsqrt(total),
        total / (sigma_vals * sigma_vals * SIGMA_DATA**2),
    )


def noise_embed(sigma_vals, channel_count):
    frequency = (1.0 / 10000.0) ** (jnp.arange(channel_count, dtype=F32) / channel_count)
    angles = (jnp.log(sigma_vals) / 4.0)[..., None] * frequency
    return jnp.concatenate([jnp.cos(angles), jnp.sin(angles)], axis=-1)


def spread_embed(sigma_vals):
    emb = noise_embed(sigma_vals, C).astype(BF16)
    images = emb.shape[0]
    zero = jnp.zeros_like(emb)
    low = jnp.stack([emb, zero], axis=-1).reshape(images, 4 * C)
    high = jnp.stack([zero, emb], axis=-1).reshape(images, 4 * C)
    fill = jnp.zeros((4 - images, 4 * C), BF16)
    return jnp.concatenate([low, fill, high, fill], axis=0)


def dot_nn(a, b):
    return lax.dot_general(a, b, (((1,), (0,)), ((), ())), preferred_element_type=F32)


def dot_nt(a, b):
    return lax.dot_general(a, b, (((1,), (1,)), ((), ())), preferred_element_type=F32)


def dot_tn(a, b):
    return lax.dot_general(a, b, (((0,), (0,)), ((), ())), preferred_element_type=F32)


def group_mean(v):
    lane = lax.broadcasted_iota(jnp.int32, (8, C), 1)
    for sh in (1, 2, 4):
        v = v + jnp.where((lane & sh) != 0, pltpu.roll(v, sh, 1), pltpu.roll(v, C - sh, 1))
    return v * (1.0 / (POS * 8))


def colsum(v):
    return jnp.sum(v, axis=0, keepdims=True)


def no_pump(l):
    pass


FORWARD_POINTS, BACKWARD_POINTS, WEIGHT_POINTS = 10, 12, 18
HALF_WAY, READY = 8, 13


def stagger(steps, images, between):
    for t in range(len(steps) + images - 1):
        for i in range(images):
            if 0 <= t - i < len(steps):
                steps[t - i](i)
        between()


class Pump:
    def __init__(self, steps, points, layers, lo=0.0, hi=1.0):
        self.table = {l: [[] for _ in range(points)] for l in layers}
        self.at = 0
        for k, step in enumerate(steps):
            place = int((lo + (hi - lo) * (k + 0.5) / len(steps)) * points * len(layers))
            self.table[layers[place // points]][place % points].append(step)

    def __call__(self, l):
        for layer, points in self.table.items():
            if points[self.at]:

                @pl.when(l == layer)
                def _(todo=points[self.at]):
                    for step in todo:
                        step()

        self.at += 1


def put_shifted(bufs, i, r, v):
    rows = v.shape[0]
    at = pl.ds(PAD + r, rows)
    sub = lax.broadcasted_iota(jnp.int32, (rows // SIDE, 8, C), 1)
    x = v.reshape(rows // SIDE, 2, 8, C)
    low, high = x[:, 0], x[:, 1]
    low_up, high_up = pltpu.roll(low, 1, 1), pltpu.roll(high, 1, 1)
    low_down, high_down = pltpu.roll(low, 7, 1), pltpu.roll(high, 7, 1)
    left = (jnp.where(sub == 0, 0.0, low_up), jnp.where(sub == 0, low_up, high_up))
    right = (jnp.where(sub == 7, high_down, low_down), jnp.where(sub == 7, 0.0, high_down))
    bufs[0, i, at, :] = jnp.stack(left, axis=1).reshape(rows, C).astype(BF16)
    bufs[1, i, at, :] = v.astype(BF16)
    bufs[2, i, at, :] = jnp.stack(right, axis=1).reshape(rows, C).astype(BF16)


def taps(bufs, flip):
    images = bufs.shape[1]
    out = []
    for dr in (-1, 0, 1):
        for dc in (-1, 0, 1):
            sr, sc = (-dr, -dc) if flip else (dr, dc)
            piece = bufs[sc + 1, :, PAD + SIDE * sr : PAD + SIDE * sr + POS, :]
            out.append(piece.reshape(images * POS, C))
    return out


def conv_forward(bufs, w, l, row):
    return dot_nn(jnp.concatenate(taps(bufs, False), axis=1), w[l, row : row + 9 * C, :])


def conv_input_grad(bufs, w, l, row):
    parts = [w[l, row + t * C : row + (t + 1) * C, :] for t in range(9)]
    return dot_nt(jnp.concatenate(taps(bufs, True), axis=1), jnp.concatenate(parts, axis=1))


def conv_weight_grad(act_t, bufs, grad, l, row):
    left = act_t[...]
    for t, piece in enumerate(taps(bufs, True)):
        grad[l, row + t * C : row + (t + 1) * C, :] = dot_nn(left, piece).astype(BF16)


def silu(v):
    h = 0.5 * v
    return h + h * jnp.tanh(h)


def silu_parts(v):
    s = 0.5 + 0.5 * jnp.tanh(0.5 * v)
    return s, s * (1.0 + v * (1.0 - s))


def clear_pads(bufs):
    zero = jnp.zeros(bufs.shape[:2] + (PAD, C), BF16)
    bufs[:, :, 0:PAD, :] = zero
    bufs[:, :, PAD + POS :, :] = zero


def split_qkv(w, l, qkvw, tmp):
    for h in range(2):
        tmp[h] = w[l, R_QKV : R_QKV + 3 * C, h * HALF : (h + 1) * HALF].astype(F32)
    for j in range(3):
        for h in range(2):
            at = j * C + h * HALF
            qkvw[:, at : at + HALF] = tmp[h, pl.ds(j, C, stride=3), :].astype(BF16)


def norm_sums(x):
    pivot = x[0:1]
    d = x - pivot
    return colsum(d), colsum(d * d), pivot


def norm_stats(sums):
    fill = [jnp.zeros((4 - len(sums), C), F32)]
    s1, s2, pivot = [jnp.concatenate([a[k] for a in sums] + fill, axis=0) for k in range(3)]
    centre = group_mean(jnp.concatenate([pivot, pivot], axis=0) * POS)[0:4]
    off = pivot - centre
    first = s1 + POS * off
    second = s2 + off * (2.0 * s1 + POS * off)
    means = group_mean(jnp.concatenate([first, second], axis=0))
    spread = jnp.maximum(means[4:8] - jnp.square(means[0:4]), 0.0)
    return centre + means[0:4], lax.rsqrt(spread + NORM_EPS)


def two_means(a, b):
    rows = jnp.concatenate([a, b] * 4, axis=0)
    means = group_mean(rows)
    return means[0:1], means[1:2]


def tap_rows(bufs, flip, which):
    out = []
    for dr in (-1, 0, 1):
        for dc in (-1, 0, 1):
            sr, sc = (-dr, -dc) if flip else (dr, dc)
            at = slice(PAD + SIDE * sr, PAD + SIDE * sr + POS)
            piece = jnp.concatenate([bufs[sc + 1, i, at, :] for i in which], axis=0)
            out.append(piece)
    return out


def layer_forward(l, w, small, eo, xs, h1, y, qkv, att, o, st, bufs, nbuf, qkvw, tmp, staged, pump):
    images = h1.shape[1]
    split_qkv(w, l, qkvw, tmp)
    mod = dot_nn(eo[...], w[l, R_EMB : R_EMB + 4 * C, :])
    ma = mod[0:4] + small[l, 5:6, :]
    mb = mod[4:8] + small[l, 6:7, :]
    for i in range(images):
        st[l, i, S_MA : S_MA + 1, :] = ma[i : i + 1]
        st[l, i, S_MB : S_MB + 1, :] = mb[i : i + 1]

    sums = {}

    def row(k):
        return small[l, k : k + 1, :]

    def keep(which, mean, inv, at):
        for k, i in enumerate(which):
            st[l, i, at : at + 1, :] = mean[k : k + 1]
            st[l, i, at + 1 : at + 2, :] = inv[k : k + 1]

    def first(which):
        mean, inv = norm_stats([norm_sums(xs[l, i]) for i in which])
        keep(which, mean, inv, S_M1)
        for k, i in enumerate(which):
            a = inv[k : k + 1] * row(0)
            for r in range(0, POS, CHUNK):
                v = (xs[l, i, r : r + CHUNK, :] - mean[k : k + 1]) * a + row(1)
                put_shifted(bufs, i, r, silu(v))

    def conv(which, at):
        left = jnp.concatenate(tap_rows(bufs, False, which), axis=1)
        return dot_nn(left, w[l, at : at + 9 * C, :])

    def conv_one(which):
        out = conv(which, R_CONV1)
        for k, i in enumerate(which):
            own = out[k * POS : (k + 1) * POS]
            own = own + row(2)
            sums[i] = norm_sums(own)
            h1[l, i] = own

    def second(which):
        mean, inv = norm_stats([sums[i] for i in which])
        keep(which, mean, inv, S_M2)
        for k, i in enumerate(which):
            gain = 1.0 + ma[i : i + 1]
            a = inv[k : k + 1] * row(3) * gain
            b = row(4) * gain + mb[i : i + 1]
            for r in range(0, POS, CHUNK):
                v = (h1[l, i, r : r + CHUNK, :] - mean[k : k + 1]) * a + b
                put_shifted(bufs, i, r, silu(v))

    def conv_two(which):
        out = conv(which, R_CONV2) + row(7)
        for k, i in enumerate(which):
            own = (xs[l, i] + out[k * POS : (k + 1) * POS]) * RS
            sums[i] = norm_sums(own)
            y[l, i] = own

    def third(which):
        mean, inv = norm_stats([sums[i] for i in which])
        keep(which, mean, inv, S_M3)
        for k, i in enumerate(which):
            a = inv[k : k + 1] * row(8)
            for r in range(0, POS, CHUNK):
                v = (y[l, i, r : r + CHUNK, :] - mean[k : k + 1]) * a + row(9)
                nbuf[i, r : r + CHUNK, :] = v.astype(BF16)

    def project_in(which):
        n = jnp.concatenate([nbuf[i] for i in which], axis=0)
        for j, at in ((0, 10), (1, None), (2, 11)):
            part = dot_nn(n, qkvw[:, j * C : (j + 1) * C])
            if at is not None:
                part = part + row(at)
            part = part.astype(BF16)
            for k, i in enumerate(which):
                qkv[l, i, :, j * C : (j + 1) * C] = part[k * POS : (k + 1) * POS]

    def attend(which):
        scores = [dot_nt(qkv[l, i, :, 0:C], qkv[l, i, :, C : 2 * C]) for i in which]
        for s, i in zip(scores, which):
            e = jnp.exp((s - jnp.max(s, axis=1, keepdims=True)) * (C**-0.5))
            p = (e * (1.0 / jnp.sum(e, axis=1, keepdims=True))).astype(BF16)
            att[l, i] = p
            o[l, i] = dot_nn(p, qkv[l, i, :, 2 * C :]).astype(BF16)

    def project_out(which):
        left = jnp.concatenate([o[l, i] for i in which], axis=0)
        out = dot_nn(left, w[l, R_PROJ:, :]) + row(12)
        for k, i in enumerate(which):
            xs[l + 1, i] = (y[l, i] + out[k * POS : (k + 1) * POS]) * RS

    steps = (first, conv_one, second, conv_two, third, project_in, attend, project_out)
    if not staged:
        for step in steps:
            step(range(images))
            pump(l)
    else:
        stagger([lambda i, step=step: step([i]) for step in steps], images, lambda: pump(l))


def layer_backward(
    l, w, small, eo, xs, h1, y, qkv, att, o, st, g, bufs, nbuf, qkvw, tmp, dn, dqkv, act_t,
    grad, sgrad, pump, need_dx=None,
):
    want = grad is not None
    images = h1.shape[1]
    which = range(images)
    flat = images * POS
    scale = C**-0.5
    split_qkv(w, l, qkvw, tmp)

    def row(k):
        return small[l, k : k + 1, :]

    def rows8(rows):
        return jnp.concatenate(list(rows) + [jnp.zeros((8 - len(rows), C), F32)], axis=0)

    zero = jnp.zeros((1, C), F32)
    gps, c1, c2, p1, p2 = {}, {}, {}, {}, {}
    total = {7: zero, 2: zero}
    gains = [1.0 + st[l, i, S_MA : S_MA + 1, :] for i in which]

    def project_out(i):
        gps[i] = (g[i] * RS).astype(BF16)
        nbuf[i] = dot_nt(gps[i], w[l, R_PROJ:, :]).astype(BF16)

    def attend(i):
        p = att[l, i]
        pf = p.astype(F32)
        dp = dot_nt(nbuf[i], qkv[l, i, :, 2 * C :])
        ds = (pf * (dp - jnp.sum(dp * pf, axis=1, keepdims=True))).astype(BF16)
        dqkv[i, :, 0:C] = (dot_nn(ds, qkv[l, i, :, C : 2 * C]) * scale).astype(BF16)
        dqkv[i, :, C : 2 * C] = (dot_tn(ds, qkv[l, i, :, 0:C]) * scale).astype(BF16)
        dqkv[i, :, 2 * C :] = dot_tn(p, nbuf[i]).astype(BF16)

    def project_in(i):
        mean, inv = st[l, i, S_M3 : S_M3 + 1, :], st[l, i, S_I3 : S_I3 + 1, :]
        d = dot_nt(dqkv[i], qkvw[...])
        dn[i] = d
        c1[i] = colsum(d)
        c2[i] = colsum(d * ((y[l, i] - mean) * inv))

    def third(i):
        mean, inv = st[l, i, S_M3 : S_M3 + 1, :], st[l, i, S_I3 : S_I3 + 1, :]
        mg, mc = two_means(row(8) * c1[i], row(8) * c2[i])
        for r in range(0, POS, CHUNK):
            nh = (y[l, i, r : r + CHUNK, :] - mean) * inv
            gm = g[i, r : r + CHUNK, :] * RS + inv * (row(8) * dn[i, r : r + CHUNK, :] - mg - nh * mc)
            gm = gm * RS
            g[i, r : r + CHUNK, :] = gm
            put_shifted(bufs, i, r, gm)
            if want:
                nbuf[i, r : r + CHUNK, :] = (nh * row(8) + row(9)).astype(BF16)
                total[7] = total[7] + colsum(gm)

    def conv_grad(i, at):
        left = jnp.concatenate(tap_rows(bufs, True, [i]), axis=1)
        parts = [w[l, at + t * C : at + (t + 1) * C, :] for t in range(9)]
        dn[i] = dot_nt(left, jnp.concatenate(parts, axis=1))

    def activation(i, src, mean, inv, a, b, act=None):
        s1, s2 = zero, zero
        for r in range(0, POS, CHUNK):
            nh = (src[l, i, r : r + CHUNK, :] - mean) * inv
            pre = nh * a + b
            s, slope = silu_parts(pre)
            d = dn[i, r : r + CHUNK, :] * slope
            dn[i, r : r + CHUNK, :] = d
            s1 = s1 + colsum(d)
            s2 = s2 + colsum(d * nh)
            if act is not None:
                act[i, r : r + CHUNK, :] = (pre * s).astype(BF16)
        p1[i], p2[i] = s1, s2

    def second_a(i):
        mean, inv = st[l, i, S_M2 : S_M2 + 1, :], st[l, i, S_I2 : S_I2 + 1, :]
        b = row(4) * gains[i] + st[l, i, S_MB : S_MB + 1, :]
        activation(i, h1, mean, inv, row(3) * gains[i], b, nbuf if want else None)

    def second_b(i):
        mean, inv = st[l, i, S_M2 : S_M2 + 1, :], st[l, i, S_I2 : S_I2 + 1, :]
        full = row(3) * gains[i]
        mg, mc = two_means(full * p1[i], full * p2[i])
        for r in range(0, POS, CHUNK):
            nh = (h1[l, i, r : r + CHUNK, :] - mean) * inv
            dh = inv * (full * dn[i, r : r + CHUNK, :] - mg - nh * mc)
            put_shifted(bufs, i, r, dh)
            if want:
                total[2] = total[2] + colsum(dh)

    def first_a(i):
        mean, inv = st[l, i, S_M1 : S_M1 + 1, :], st[l, i, S_I1 : S_I1 + 1, :]
        activation(i, xs, mean, inv, row(0), row(1))

    def first_act(i):
        mean, inv = st[l, i, S_M1 : S_M1 + 1, :], st[l, i, S_I1 : S_I1 + 1, :]
        for r in range(0, POS, CHUNK):
            v = (xs[l, i, r : r + CHUNK, :] - mean) * (inv * row(0)) + row(1)
            nbuf[i, r : r + CHUNK, :] = silu(v).astype(BF16)

    def first_b(i):
        mean, inv = st[l, i, S_M1 : S_M1 + 1, :], st[l, i, S_I1 : S_I1 + 1, :]
        mg, mc = two_means(row(0) * p1[i], row(0) * p2[i])
        for r in range(0, POS, CHUNK):
            nh = (xs[l, i, r : r + CHUNK, :] - mean) * inv
            dx = inv * (row(0) * dn[i, r : r + CHUNK, :] - mg - nh * mc)
            g[i, r : r + CHUNK, :] = g[i, r : r + CHUNK, :] + dx

    upper = [project_out, attend, project_in, third, lambda i: conv_grad(i, R_CONV2)]
    lower = [lambda i: conv_grad(i, R_CONV1), first_a]
    if not want:
        stagger(upper + [second_a, second_b] + lower + [first_b], images, lambda: pump(l))
        return
    stagger(upper, images, lambda: pump(l))
    gp = jnp.concatenate([gps[i] for i in which], axis=0)
    grad[l, R_PROJ:, :] = dot_tn(o[l].reshape(flat, C), gp).astype(BF16)
    sgrad[l, 12:13, :] = colsum(gp.astype(F32))
    sgrad[l, 7:8, :] = total[7]
    sgrad[l, 8:9, :] = colsum(rows8([c2[i] for i in which]))
    sgrad[l, 9:10, :] = colsum(rows8([c1[i] for i in which]))
    act_t[...] = nbuf[...].reshape(flat, C).T
    for j in range(3):
        dj = dqkv[:, :, j * C : (j + 1) * C].reshape(flat, C)
        part = dot_nn(act_t[...], dj)
        for h in range(2):
            tmp[h, pl.ds(j, C, stride=3), :] = part[:, h * HALF : (h + 1) * HALF]
        if j != 1:
            sgrad[l, 10 + j // 2 : 11 + j // 2, :] = colsum(dj.astype(F32))
    for h in range(2):
        grad[l, R_QKV : R_QKV + 3 * C, h * HALF : (h + 1) * HALF] = tmp[h].astype(BF16)
    for i in which:
        second_a(i)
    pump(l)
    act_t[...] = nbuf[...].reshape(flat, C).T
    conv_weight_grad(act_t, bufs, grad, l, R_CONV2)
    p18, p28, modgain = [rows8([a[i] for i in which]) for a in (p1, p2, gains)]
    dma = row(3) * p28 + row(4) * p18
    sgrad[l, 3:4, :] = colsum(modgain * p28)
    sgrad[l, 4:5, :] = colsum(modgain * p18)
    sgrad[l, 5:6, :] = colsum(dma)
    sgrad[l, 6:7, :] = colsum(p18)
    grad[l, R_EMB : R_EMB + 4 * C, :] = embed_grad(
        eo, jnp.concatenate([dma[0:4], p18[0:4]], axis=0)
    ).astype(BF16)
    pump(l)
    stagger([second_b, first_act], images, lambda: pump(l))
    act_t[...] = nbuf[...].reshape(flat, C).T
    conv_weight_grad(act_t, bufs, grad, l, R_CONV1)
    pump(l)
    stagger(lower, images, lambda: pump(l))
    sgrad[l, 2:3, :] = total[2]
    sgrad[l, 0:1, :] = colsum(rows8([p2[i] for i in which]))
    sgrad[l, 1:2, :] = colsum(rows8([p1[i] for i in which]))

    @pl.when(l == 1)
    def _():
        for i in which:
            first_b(i)


def embed_grad(eo, dm):
    parts, rest = [], dm
    for _ in range(3):
        parts.append(rest.astype(BF16))
        rest = rest - parts[-1].astype(F32)
    left = eo[...]
    return dot_tn(jnp.concatenate([left, left], axis=0), jnp.concatenate(parts[:2], axis=0)) + dot_tn(
        left, parts[2]
    )


def saved_shapes(images):
    return [
        jax.ShapeDtypeStruct((3, images, POS, C), F32),
        jax.ShapeDtypeStruct((2, images, POS, C), F32),
        jax.ShapeDtypeStruct((2, images, POS, C), F32),
        jax.ShapeDtypeStruct((2, images, POS, 3 * C), BF16),
        jax.ShapeDtypeStruct((2, images, POS, POS), BF16),
        jax.ShapeDtypeStruct((2, images, POS, C), BF16),
        jax.ShapeDtypeStruct((2, images, 8, C), F32),
    ]


def forward_kernel(staged, x0, w, small, eo, xs, h1, y, qkv, att, o, st, bufs, nbuf, qkvw, tmp):
    clear_pads(bufs)
    xs[0] = x0[...]

    def body(l, _):
        layer_forward(
            l, w, small, eo, xs, h1, y, qkv, att, o, st, bufs, nbuf, qkvw, tmp, staged, no_pump
        )
        return 0

    lax.fori_loop(0, 2, body, 0)


def backward_kernel(want, *refs):
    cot, w, small, eo, xs, h1, y, qkv, att, o, st, g = refs[:12]
    refs = refs[12:]
    if want:
        grad, sgrad = refs[:2]
        refs = refs[2:]
    else:
        grad, sgrad = None, None
    bufs, nbuf, qkvw, tmp, dn, dqkv, act_t = refs
    clear_pads(bufs)
    g[...] = cot[...]
    if want:
        sgrad[...] = jnp.zeros(sgrad.shape, F32)

    def body(k, _):
        layer_backward(
            1 - k, w, small, eo, xs, h1, y, qkv, att, o, st, g, bufs, nbuf, qkvw, tmp, dn,
            dqkv, act_t, grad, sgrad, no_pump,
        )
        return 0

    lax.fori_loop(0, 2, body, 0)


def vm(n):
    return [pl.BlockSpec(memory_space=pltpu.VMEM)] * n


def scratch_forward(images):
    return [
        pltpu.VMEM((3, images, POS + 2 * PAD, C), BF16),
        pltpu.VMEM((images, POS, C), BF16),
        pltpu.VMEM((C, 3 * C), BF16),
        pltpu.VMEM((2, 3 * C, HALF), F32),
    ]


def run_forward(x0, w, small, eo, staged=False):
    images = x0.shape[0]
    return pl.pallas_call(
        functools.partial(forward_kernel, staged),
        out_shape=saved_shapes(images),
        in_specs=vm(4),
        out_specs=vm(7),
        scratch_shapes=scratch_forward(images),
        compiler_params=pltpu.CompilerParams(vmem_limit_bytes=VMEM_LIMIT),
    )(x0, w, small, eo)


def run_backward(cot, w, small, eo, saved, want):
    images = cot.shape[0]
    outs = [jax.ShapeDtypeStruct(cot.shape, F32)]
    if want:
        outs += [
            jax.ShapeDtypeStruct((2, ROWS, C), BF16),
            jax.ShapeDtypeStruct((2, 16, C), F32),
        ]
    return pl.pallas_call(
        functools.partial(backward_kernel, want),
        out_shape=outs,
        in_specs=vm(11),
        out_specs=vm(len(outs)),
        scratch_shapes=scratch_forward(images)
        + [
            pltpu.VMEM((images, POS, C), F32),
            pltpu.VMEM((images, POS, 3 * C), BF16),
            pltpu.VMEM((C, images * POS), BF16),
        ],
        compiler_params=pltpu.CompilerParams(vmem_limit_bytes=VMEM_LIMIT),
    )(cot, w, small, eo, *saved)


PLANES, PLANE = 4, 4
MESH = pl.DeviceIdType.MESH


class Place:
    def __init__(self):
        self.sec = lax.axis_index("section")
        self.d = lax.axis_index("dp")
        self.x = lax.rem(self.d, 2)
        self.y = lax.rem(self.d // 2, 2)
        self.z = self.d // PLANE
        self.seat = self.sec * PLANE + lax.rem(self.d, PLANE)
        self.sib = {"section": 1 - self.sec}
        self.xn = {"dp": self.d + 1 - 2 * self.x}
        self.yn = {"dp": self.d + 2 - 4 * self.y}

    def plane(self, j):
        return lax.rem(self.z + j + PLANES, PLANES)

    def zpeer(self, j):
        return {"dp": self.plane(j) * PLANE + lax.rem(self.d, PLANE)}

    def plane_peer(self, j):
        seat = lax.rem(self.seat + j, 2 * PLANE)
        return {"section": seat // PLANE, "dp": self.z * PLANE + lax.rem(seat, PLANE)}

    def meet(self):
        barrier = pltpu.get_barrier_semaphore()
        others = [self.plane_peer(j) for j in range(1, 8)] + [self.zpeer(j) for j in (1, 2, 3)]
        for other in others:
            pl.semaphore_signal(barrier, inc=1, device_id=other, device_id_type=MESH)
        pl.semaphore_wait(barrier, len(others))


def remote(src, dst, send, recv, target):
    return pltpu.make_async_remote_copy(
        src_ref=src, dst_ref=dst, send_sem=send, recv_sem=recv,
        device_id=target, device_id_type=MESH,
    )


Z1, X1, Y1, X2, Y2, S_OWN, S_X, S_Y, S_DA, S_DB = 0, 3, 7, 11, 15, 19, 23, 27, 31, 35
SLOTS = 39


class Gather:
    def __init__(self, me, net, stage, local_sem, send_sem, recv_sem):
        self.me, self.net, self.stage = me, net, stage
        self.local_sem, self.send_sem, self.recv_sem = local_sem, send_sem, recv_sem
        self.part = stage.shape[0]
        self.half = self.part // 2

    def rows(self, plane, y, x, lo, count):
        at = (plane * PLANE + y * 2 + x) * self.part + lo
        return self.net.at[self.me.sec, pl.ds(pl.multiple_of(at, 16), count)]

    def own(self, j):
        return self.rows(self.me.plane(-j), self.me.y, self.me.x, 0, self.part)

    def send(self, slot, piece, target, src=None):
        src = piece if src is None else src
        remote(src, piece, self.send_sem.at[slot], self.recv_sem.at[slot], target).start()

    def arrived(self, slot, piece):
        remote(
            piece, piece, self.send_sem.at[slot], self.recv_sem.at[slot], self.me.sib
        ).wait_recv()

    def local(self):
        return pltpu.make_async_copy(self.stage, self.own(0), self.local_sem)

    def begin(self):
        me = self.me
        for j in (1, 2, 3):
            self.send(Z1 + j - 1, self.own(0), me.zpeer(j), self.stage)
        for slot, target in ((X1, me.xn), (Y1, me.yn), (S_OWN, me.sib)):
            self.send(slot, self.own(0), target, self.stage)
        self.local().start()

    def phase1(self):
        def step(j):
            me = self.me
            self.arrived(Z1 + j - 1, self.own(j))
            for slot, target in ((X1, me.xn), (Y1, me.yn), (S_OWN, me.sib)):
                self.send(slot + j, self.own(j), target)

        return [lambda j=j: step(j) for j in (1, 2, 3)]

    def phase2(self):
        me, part, half = self.me, self.part, self.half

        def step_x(j):
            plane = me.plane(-j)
            self.arrived(X1 + j, self.rows(plane, me.y, 1 - me.x, 0, part))
            self.send(Y2 + j, self.rows(plane, me.y, 1 - me.x, 0, half), me.yn)
            self.send(S_X + j, self.rows(plane, me.y, 1 - me.x, 0, part), me.sib)

        def step_y(j):
            plane = me.plane(-j)
            self.arrived(Y1 + j, self.rows(plane, 1 - me.y, me.x, 0, part))
            self.send(X2 + j, self.rows(plane, 1 - me.y, me.x, half, half), me.xn)
            self.send(S_Y + j, self.rows(plane, 1 - me.y, me.x, 0, part), me.sib)

        return [lambda f=f, j=j: f(j) for j in range(PLANES) for f in (step_x, step_y)]

    def phase3(self):
        def step(j, slot, to, lo):
            me = self.me
            where = self.rows(me.plane(-j), 1 - me.y, 1 - me.x, lo, self.half)
            self.arrived(slot + j, where)
            self.send(to + j, where, me.sib)

        return [
            lambda j=j, a=a: step(j, *a)
            for j in range(PLANES)
            for a in ((Y2, S_DA, 0), (X2, S_DB, self.half))
        ]

    def finish(self):
        def step():
            for slot in range(S_OWN, SLOTS):
                count = self.part if slot < S_DA else self.half
                self.arrived(slot, self.rows(0, 0, 0, 0, count))
            self.local().wait()

        return [step]

    def drain(self):
        for slot in range(SLOTS):
            whole = slot < X2 or S_OWN <= slot < S_DA
            piece = self.rows(0, 0, 0, 0, self.part if whole else self.half)
            remote(
                piece, piece, self.send_sem.at[slot], self.recv_sem.at[slot], self.me.sib
            ).wait_send()


A_SLOT, B_SLOT, C_SLOT, D_SLOT = 0, 4, 20, 28
R_SLOTS = 31


class Reduce:
    def __init__(self, me, big, shard, sib, there, rb, rc, rd, ssem, rsem):
        self.me, self.big, self.shard = me, big, shard
        self.sib, self.there, self.rb, self.rc, self.rd = sib, there, rb, rc, rd
        self.ssem, self.rsem = ssem, rsem
        self.part = shard.shape[0]
        self.half = self.part // 2
        self.span = PLANE * self.part

    def zt(self, k):
        return (3, 2, 0, 1)[k]

    def block(self, k):
        return pl.ds(self.zt(k) * self.span, self.span)

    def piece(self, k, y, x, lo, count):
        at = (self.zt(k) * PLANE + y * 2 + x) * self.part + lo
        return pl.ds(pl.multiple_of(at, 16), count)

    def send(self, src, dst, slot, target):
        remote(src, dst, self.ssem.at[slot], self.rsem.at[slot], target).start()

    def arrived(self, dst, slot):
        remote(dst, dst, self.ssem.at[slot], self.rsem.at[slot], self.me.sib).wait_recv()

    def begin(self):
        for k in range(PLANES):
            self.begin_block(k)

    def begin_block(self, k):
        at = self.block(k)
        self.send(self.big.at[1 - self.me.sec, at], self.there.at[at], A_SLOT + k, self.me.sib)

    def stage_a(self, k):
        me, half = self.me, self.half
        self.arrived(self.sib.at[self.block(k)], A_SLOT + k)
        base = self.zt(k) * self.span

        def body(i, _):
            at = pl.ds(pl.multiple_of(base + i * half, 16), half)
            self.big[me.sec, at, :] = (
                self.big[me.sec, at, :].astype(F32) + self.sib[at, :].astype(F32)
            ).astype(BF16)
            return 0

        lax.fori_loop(0, 2 * PLANE, body, 0)
        for j in range(2):
            self.send(
                self.big.at[me.sec, self.piece(k, 1 - me.y, j, 0, half)], self.rb.at[k, j],
                B_SLOT + 4 * k + j, me.yn,
            )
            self.send(
                self.big.at[me.sec, self.piece(k, j, 1 - me.x, half, half)], self.rb.at[k, 2 + j],
                B_SLOT + 4 * k + 2 + j, me.xn,
            )

    def join(self, where, other):
        self.big[self.me.sec, where, :] = (
            self.big[self.me.sec, where, :].astype(F32) + other.astype(F32)
        ).astype(BF16)

    def stage_c(self, k):
        me, half = self.me, self.half
        for j in range(4):
            self.arrived(self.rb.at[k, j], B_SLOT + 4 * k + j)
            y, x, lo = (me.y, j, 0) if j < 2 else (j - 2, me.x, half)
            self.join(self.piece(k, y, x, lo, half), self.rb[k, j])
        self.send(
            self.big.at[me.sec, self.piece(k, me.y, 1 - me.x, 0, half)], self.rc.at[k, 0],
            C_SLOT + 2 * k, me.xn,
        )
        self.send(
            self.big.at[me.sec, self.piece(k, 1 - me.y, me.x, half, half)], self.rc.at[k, 1],
            C_SLOT + 2 * k + 1, me.yn,
        )

    def stage_d(self, k):
        me, half, zt = self.me, self.half, self.zt(k)
        for j in range(2):
            self.arrived(self.rc.at[k, j], C_SLOT + 2 * k + j)
            self.join(self.piece(k, me.y, me.x, j * half, half), self.rc[k, j])

        @pl.when(me.z != zt)
        def _():
            self.send(
                self.big.at[me.sec, self.piece(k, me.y, me.x, 0, self.part)],
                self.rd.at[lax.rem(zt - me.z + PLANES, PLANES) - 1],
                D_SLOT + lax.rem(zt - me.z + PLANES, PLANES) - 1,
                {"dp": zt * PLANE + lax.rem(me.d, PLANE)},
            )

    def stage_e(self):
        for j in range(PLANES - 1):
            self.arrived(self.rd.at[j], D_SLOT + j)
        at = pl.ds(pl.multiple_of(self.me.d * self.part, 16), self.part)
        self.shard[...] = (
            self.big[self.me.sec, at, :].astype(F32)
            + self.rd[0].astype(F32) + (self.rd[1].astype(F32) + self.rd[2].astype(F32))
        )

    def in_rows(self):
        stages = (self.stage_a, self.stage_c, self.stage_d)
        return [lambda stage=stage, k=k: stage(k) for stage in stages for k in range(PLANES)]

    def steps(self):
        out = []
        for t in range(PLANES + 2):
            for stage, lag in ((self.stage_a, 0), (self.stage_c, 1), (self.stage_d, 2)):
                if 0 <= t - lag < PLANES:
                    out.append(lambda stage=stage, k=t - lag: stage(k))
        return out

    def drain(self, lo=0, hi=R_SLOTS):
        for slot in range(lo, hi):
            if slot < B_SLOT:
                piece = self.there.at[pl.ds(0, self.span)]
            elif slot < D_SLOT:
                piece = self.rb.at[0, 0]
            else:
                piece = self.rd.at[0]
            remote(piece, piece, self.ssem.at[slot], self.rsem.at[slot], self.me.sib).wait_send()


def reduce_scratch(part):
    half = part // 2
    return [
        pltpu.VMEM((PLANES, 4, half, C), BF16),
        pltpu.VMEM((PLANES, 2, half, C), BF16),
        pltpu.VMEM((PLANES - 1, part, C), BF16),
        pltpu.SemaphoreType.DMA((R_SLOTS,)),
        pltpu.SemaphoreType.DMA((R_SLOTS,)),
    ]


class Totals:
    def __init__(self, me, buf, recv, ssem, rsem):
        self.me, self.buf, self.recv, self.ssem, self.rsem = me, buf, recv, ssem, rsem

    def send(self, src, dst, slot, target):
        remote(src, dst, self.ssem.at[slot], self.rsem.at[slot], target).start()

    def arrived(self, dst, slot):
        remote(dst, dst, self.ssem.at[slot], self.rsem.at[slot], self.me.sib).wait_recv()

    def begin(self, first):
        self.send(first, self.recv.at[0], 0, self.me.sib)

    def steps(self):
        me, buf, recv = self.me, self.buf, self.recv

        def one():
            self.arrived(recv.at[0], 0)
            buf[1] = buf[0] + recv[0]
            self.send(buf.at[1], recv.at[1], 1, me.xn)

        def two():
            self.arrived(recv.at[1], 1)
            buf[2] = buf[1] + recv[1]
            self.send(buf.at[2], recv.at[2], 2, me.yn)

        def three():
            self.arrived(recv.at[2], 2)
            buf[3] = buf[2] + recv[2]
            recv[3 + me.z] = buf[3]
            for j in (1, 2, 3):
                self.send(buf.at[3], recv.at[3 + me.z], 2 + j, me.zpeer(j))

        return [one, two, three]

    def result(self):
        for j in (1, 2, 3):
            self.arrived(self.recv.at[3 + self.me.plane(-j)], 2 + j)
        return (self.recv[3] + self.recv[4]) + (self.recv[5] + self.recv[6])

    def drain(self):
        for slot in range(6):
            piece = self.recv.at[0]
            remote(piece, piece, self.ssem.at[slot], self.rsem.at[slot], self.me.sib).wait_send()


class Squares:
    def __init__(self, me, own, recv, ssem, rsem):
        self.me, self.own, self.recv, self.ssem, self.rsem = me, own, recv, ssem, rsem

    def hop(self, src, base, mine, peers, slots):
        for j, target in peers:
            dst = self.recv.at[base + mine]
            remote(src, dst, self.ssem.at[slots + j], self.rsem.at[slots + j], target).start()
        self.recv[base + mine] = src[...]
        for j, _ in peers:
            dst = self.recv.at[base]
            remote(dst, dst, self.ssem.at[slots + j], self.rsem.at[slots + j], self.me.sib).wait_recv()

    def run(self):
        me, recv = self.me, self.recv
        self.hop(self.own.at[0], 0, me.seat, [(j, me.plane_peer(j)) for j in range(1, 8)], -1)
        pairs = [recv[2 * k] + recv[2 * k + 1] for k in range(4)]
        self.own[1] = (pairs[0] + pairs[1]) + (pairs[2] + pairs[3])
        self.hop(self.own.at[1], 8, me.z, [(j, me.zpeer(j)) for j in (1, 2, 3)], 6)
        return (recv[8] + recv[9]) + (recv[10] + recv[11])

    def drain(self):
        for slot in range(10):
            piece = self.recv.at[0]
            remote(piece, piece, self.ssem.at[slot], self.rsem.at[slot], self.me.sib).wait_send()


def squares_scratch(shape):
    return [
        pltpu.VMEM((2,) + shape, F32),
        pltpu.VMEM((12,) + shape, F32),
        pltpu.SemaphoreType.DMA((10,)),
        pltpu.SemaphoreType.DMA((10,)),
    ]


def totals_scratch(shape):
    return [
        pltpu.VMEM((4,) + shape, F32),
        pltpu.VMEM((7,) + shape, F32),
        pltpu.SemaphoreType.DMA((6,)),
        pltpu.SemaphoreType.DMA((6,)),
    ]


def saved_scratch(images):
    return [pltpu.VMEM(a.shape, a.dtype) for a in saved_shapes(images)]


def backward_scratch(images):
    return scratch_forward(images) + [
        pltpu.VMEM((images, POS, C), F32),
        pltpu.VMEM((images, POS, 3 * C), BF16),
        pltpu.VMEM((C, images * POS), BF16),
    ]


GEN_TOTAL = SIGMA_INIT**2 + SIGMA_DATA**2
GEN_IN = GEN_TOTAL**-0.5
GEN_SKIP = SIGMA_DATA**2 / GEN_TOTAL
GEN_OUT = SIGMA_INIT * SIGMA_DATA * GEN_TOTAL**-0.5
T_IN, T_SKIP, T_OUT, T_SIGMA, T_FACTOR = range(5)


def fill_embed(eo, sigmas):
    at = lax.broadcasted_iota(jnp.int32, (8, 4 * C), 1)
    side = lax.broadcasted_iota(jnp.int32, (8, 4 * C), 0) // 4
    k = at // 2
    power = (k & (C - 1)).astype(F32) * (1.0 / C)
    rows = sigmas + [jnp.ones_like(sigmas[0])] * (4 - len(sigmas))
    angle = jnp.log(jnp.concatenate(rows + rows, axis=0)) * 0.25 * jnp.exp(power * -LOG_10000)
    wave = jnp.where(k < C, jnp.cos(angle), jnp.sin(angle))
    eo[...] = jnp.where((at & 1) == side, wave, 0.0).astype(BF16)


LOG_10000 = 9.210340371976184


def step_kernel(*refs):
    (
        z_all, eps_all, levels, counts, gen_w, fake_w, teacher_w, gen_small, fake_small,
        teacher_small,
        gw_out, sv_x, sv_h, sv_y, sv_q, sv_a, sv_o, sv_s, gshard, fshard, stot, sqtot,
        *refs,
    ) = refs
    gen_out = (sv_x, sv_h, sv_y, sv_q, sv_a, sv_o, sv_s)
    w_gen, w_fake, w_teach = refs[:3]
    sv_one, sv_two = refs[3:10], refs[10:17]
    bufs, nbuf, qkvw, tmp, dn, dqkv, act_t = refs[17:24]
    zb, eb, g, stage, local_sem, send_sem, recv_sem, copy_sem = refs[24:32]
    smalls, small_sem, gen_eo, score_eo, tab, sgrads, part_sums = refs[32:39]
    fake_refs, gen_refs = refs[39:44], refs[44:49]
    small_refs, square_refs = refs[49:53], refs[53:57]
    sib, free_sem = refs[57:59]
    g2 = sv_two[0].at[2]
    images = zb.shape[0]
    me = Place()
    start = me.sec * images

    def run(steps):
        for step in steps:
            step()

    def mine(ref):
        return ref.at[pl.ds(start, images)]

    loads = [
        pltpu.make_async_copy(mine(z_all), zb, copy_sem.at[0]),
        pltpu.make_async_copy(mine(eps_all), eb, copy_sem.at[1]),
    ]
    for copy in loads:
        copy.start()
    masters = [
        pltpu.make_async_copy(src, dst, copy_sem.at[2 + k])
        for k, (src, dst) in enumerate(((gen_w, gshard), (fake_w, fshard), (teacher_w, stage.at[2])))
    ]
    for copy in masters:
        copy.start()
    smalls[...] = jnp.zeros(smalls.shape, F32)
    for n, ref in enumerate((gen_small, fake_small, teacher_small)):
        for r in range(13):
            smalls[me.sec, n, r : r + 1, :] = ref[r]
    gathers = [
        Gather(me, net, stage.at[n], local_sem.at[n], send_sem.at[n], recv_sem.at[n])
        for n, net in enumerate((w_gen, w_fake, w_teach))
    ]
    for copy in masters:
        copy.wait()
    stage[0] = gshard[...].astype(BF16)
    stage[1] = fshard[...].astype(BF16)
    me.meet()
    gathers[0].begin()
    swap = remote(
        smalls.at[me.sec], smalls.at[me.sec], small_sem.at[0], small_sem.at[1], me.sib
    )
    swap.start()

    clear_pads(bufs)
    sgrads[...] = jnp.zeros(sgrads.shape, F32)
    sigmas = []
    valid_sum = jnp.zeros((1, 4 * C), F32)
    for i in range(images):
        level = jnp.zeros((1, 4 * C), jnp.int32) + levels[start + i]
        sigma = SIGMA_TOP + level.astype(F32) / (LEVELS - 1) * (SIGMA_BOTTOM - SIGMA_TOP)
        square = sigma * sigma
        sigma = square * square * square * sigma
        sigmas.append(sigma)
        s_in, s_skip, s_out, s_lam = precondition(sigma)
        valid = jnp.where(jnp.zeros_like(level) + (start + i) < counts[0], 1.0, 0.0)
        valid_sum = valid_sum + valid
        rows = (s_in, s_skip, s_out, sigma, valid * s_lam * (1.0 / (POS * C)))
        for k, value in enumerate(rows):
            tab[i, k : k + 1, :] = value[:, :C]
    fill_embed(score_eo, sigmas)
    fill_embed(gen_eo, [jnp.full((1, 4 * C), SIGMA_INIT, F32)] * images)

    def forward(n, w, eo, sv, pump):
        def body(l, _):
            layer_forward(
                l, w, smalls.at[:, n], eo, *sv, bufs, nbuf, qkvw, tmp, True, pump
            )
            return 0

        lax.fori_loop(0, 2, body, 0)

    def backward(n, w, eo, sv, cot, grad, sgrad, pump):
        def body(k, _):
            layer_backward(
                1 - k, w, smalls.at[:, n], eo, *sv, cot, bufs, nbuf, qkvw, tmp, dn, dqkv,
                act_t, grad, sgrad, pump,
            )
            return 0

        lax.fori_loop(0, 2, body, 0)

    def each(f):
        def body(i, carry):
            return f(i, [tab[i, k : k + 1, :] for k in range(5)], carry)

        return lax.fori_loop(0, images, body, jnp.zeros((1, C), F32))

    z_now, z_next = gathers[0].phase1(), gathers[1].phase1()
    run(z_now[:2] + [gathers[1].begin] + z_now[2:] + gathers[0].phase2() + z_next[:1])
    last = gathers[0].phase3()
    run(last[:4] + z_next[1:2] + [gathers[2].begin] + last[4:] + z_next[2:])
    for copy in loads:
        copy.wait()
    sv_one[0][0] = zb[...] * (GEN_IN * SIGMA_INIT)
    swap.wait()
    run(gathers[0].finish())
    later = gathers[1].phase2()
    forward(0, w_gen, gen_eo, sv_one, Pump(later[:5], FORWARD_POINTS, (0, 1)))
    pairs = [(w_gen, gw_out)] + list(zip(sv_one, gen_out))
    stores = [
        pltpu.make_async_copy(src, dst, copy_sem.at[2 + k]) for k, (src, dst) in enumerate(pairs)
    ]
    for copy in stores:
        copy.start()

    def noisy(i, t, carry):
        zb[i] = zb[i] * (GEN_SKIP * SIGMA_INIT) + GEN_OUT * sv_one[0][2, i]
        eb[i] = zb[i] + t[T_SIGMA] * eb[i]
        sv_two[0][0, i] = t[T_IN] * eb[i]
        return carry

    each(noisy)
    z_next, last = gathers[2].phase1(), gathers[1].phase3()
    run(later[5:] + z_next[:1] + last[:4] + z_next[1:2] + last[4:] + z_next[2:])
    run(gathers[1].finish())
    later = gathers[2].phase2()
    forward(1, w_fake, score_eo, sv_two, Pump(later[:5], FORWARD_POINTS, (0, 1)))
    later = later[5:] + gathers[2].phase3()

    def fake_loss(i, t, total):
        den = t[T_SKIP] * eb[i] + t[T_OUT] * sv_two[0][2, i]
        sv_two[0][2, i] = den
        miss = den - zb[i]
        g[i] = (2.0 * t[T_OUT] * t[T_FACTOR]) * miss
        return total + t[T_FACTOR] * colsum(miss * miss)

    loss_fake = each(fake_loss)
    for copy in stores:
        copy.wait()
    gathers[0].drain()
    backward(
        1, w_fake, score_eo, sv_two, g, w_gen, sgrads.at[:, 1],
        Pump(later, WEIGHT_POINTS, (1, 0), 0.0, 0.8),
    )
    fake_sum = Reduce(me, w_gen, fshard, sib, sib, *fake_refs)
    fake_sum.begin()
    run(gathers[2].finish())
    later = fake_sum.in_rows()
    sv_one[0][0] = sv_two[0][0]
    forward(2, w_teach, score_eo, sv_one, Pump(later[:4], FORWARD_POINTS, (0, 1), 0.2))

    def gen_loss(i, t, total):
        den = t[T_SKIP] * eb[i] + t[T_OUT] * sv_one[0][2, i]
        fake_den = sv_two[0][2, i]
        miss = fake_den - zb[i]
        gap = den - fake_den
        scale = t[T_OUT] * t[T_FACTOR]
        g[i] = scale * ((2.0 * (1.0 - ALPHA_MIX)) * gap + miss)
        g2[i] = scale * ((1.0 - 2.0 * (1.0 - ALPHA_MIX)) * gap - miss)
        zb[i] = (t[T_FACTOR] * (t[T_SKIP] - 1.0)) * gap
        return total + t[T_FACTOR] * colsum(gap * ((1.0 - ALPHA_MIX) * gap + miss))

    loss_gen = each(gen_loss)
    backward(
        2, w_teach, score_eo, sv_one, g, None, None, Pump(later[4:8], BACKWARD_POINTS, (1, 0), 0.1)
    )
    gathers[2].drain()
    fake_sum.drain(A_SLOT, B_SLOT)
    pl.semaphore_signal(free_sem, inc=1, device_id=me.sib, device_id_type=MESH)
    back = [
        pltpu.make_async_copy(src, dst, copy_sem.at[2 + k])
        for k, (dst, src) in enumerate([(w_teach, gw_out)] + list(zip(sv_one, gen_out)))
    ]
    for copy in back:
        copy.start()
    backward(
        1, w_fake, score_eo, sv_two, g2, None, None, Pump(later[8:], BACKWARD_POINTS, (1, 0))
    )

    def gen_gradient(i, t, carry):
        g[i] = GEN_OUT * (zb[i] + t[T_IN] * (g[i] + g2[i]))
        return carry

    each(gen_gradient)
    gathers[1].drain()
    for copy in back:
        copy.wait()

    gen_sum = Reduce(me, w_fake, gshard, w_gen.at[1 - me.sec], w_gen.at[me.sec], *gen_refs)
    later = gen_sum.steps()

    def on_section(s, steps):
        pl.when(me.sec == s)(lambda: run(steps))

    def hand_over():
        pl.semaphore_wait(free_sem, 1)

    pump = Pump([], WEIGHT_POINTS, (1, 0))

    def at(layer, point, section, steps):
        pump.table[layer][point].append(lambda: on_section(section, steps))

    upper = [hand_over, lambda: gen_sum.begin_block(0), lambda: gen_sum.begin_block(1)]
    lower = [lambda: gen_sum.begin_block(2), lambda: gen_sum.begin_block(3)]
    for layer, giver in ((1, 0), (0, 1)):
        at(layer, HALF_WAY, giver, upper)
        at(layer, READY, giver, lower)
    rows = gen_sum.in_rows()
    for k, point in enumerate((1, 3, 5, 6, 8, 11, 14, 17)):
        at(0, point, 1, rows[k : k + 1])
    at(0, READY, 0, later[:1])
    at(0, READY + 2, 0, later[1:2])
    at(0, READY + 4, 0, later[2:3])
    backward(0, w_teach, gen_eo, sv_one, g, w_fake, sgrads.at[:, 0], pump)

    def spread_sum(total):
        return jnp.broadcast_to(jnp.sum(total, axis=1, keepdims=True), (1, C))

    sums = jnp.concatenate([spread_sum(loss_gen), spread_sum(loss_fake), valid_sum[:, :C]], axis=0)
    for s in range(2):
        part_sums[s, 0:16, :] = sgrads[s, 0]
        part_sums[s, 13:16, :] = sums
        part_sums[s, 16:32, :] = sgrads[s, 1]
    small = Totals(me, *small_refs)
    small_refs[0][0] = part_sums[me.sec]
    small.begin(part_sums.at[1 - me.sec])
    fake_sum.stage_e()
    small_steps = small.steps()
    on_section(0, later[3:6])
    on_section(1, rows[8:])
    run(small_steps[:1])
    on_section(0, later[6:8])
    run(small_steps[1:2])
    on_section(0, later[8:10])
    run(small_steps[2:])
    on_section(0, later[10:])
    stot[...] = small.result()
    own = square_refs[0]
    keep = lax.broadcasted_iota(jnp.int32, (16, C), 0) < 13
    for n, rows in ((1, fshard), (0, gshard)):
        if n == 0:
            gen_sum.stage_e()
        low = jnp.square(jnp.where(keep, stot[16 * n : 16 * n + 16, :], 0.0))
        low = jnp.where(me.d == 0, low[0:8] + low[8:16], 0.0)
        big = jnp.sum(jnp.square(rows[...]).reshape(rows.shape[0] // 8, 8, C), axis=0)
        own[0, 8 * n : 8 * n + 8, :] = big + low
    square = Squares(me, *square_refs)
    sqtot[...] = square.run()
    fake_sum.drain(B_SLOT)
    for done in (gen_sum, small, square):
        done.drain()


SIGMA_TOP = SIGMA_HIGH ** (1.0 / RHO_POWER)
SIGMA_BOTTOM = SIGMA_LOW ** (1.0 / RHO_POWER)


def run_step(z, eps, levels, counts, gen_w, fake_w, teacher_w, smalls):
    part = gen_w.shape[0]
    images = z.shape[0] // 2
    any_ = pl.BlockSpec(memory_space=pl.ANY)
    smem = pl.BlockSpec(memory_space=pltpu.SMEM)
    saved = saved_shapes(images)
    return pl.pallas_call(
        step_kernel,
        out_shape=[jax.ShapeDtypeStruct((2, ROWS, C), BF16)]
        + saved
        + [
            jax.ShapeDtypeStruct((part, C), F32),
            jax.ShapeDtypeStruct((part, C), F32),
            jax.ShapeDtypeStruct((32, C), F32),
            jax.ShapeDtypeStruct((16, C), F32),
        ],
        in_specs=[any_] * 2 + [smem] * 2 + [any_] * 3 + vm(3),
        out_specs=[any_] * 8 + vm(4),
        scratch_shapes=[pltpu.VMEM((2, ROWS, C), BF16)] * 3
        + saved_scratch(images) * 2
        + backward_scratch(images)
        + [pltpu.VMEM((images, POS, C), F32)] * 3
        + [
            pltpu.VMEM((3, part, C), BF16),
            pltpu.SemaphoreType.DMA((3,)),
            pltpu.SemaphoreType.DMA((3, SLOTS)),
            pltpu.SemaphoreType.DMA((3, SLOTS)),
            pltpu.SemaphoreType.DMA((10,)),
            pltpu.VMEM((2, 3, 16, C), F32),
            pltpu.SemaphoreType.DMA((2,)),
            pltpu.VMEM((8, 4 * C), BF16),
            pltpu.VMEM((8, 4 * C), BF16),
            pltpu.VMEM((images, 8, C), F32),
            pltpu.VMEM((2, 2, 16, C), F32),
            pltpu.VMEM((2, 32, C), F32),
        ]
        + reduce_scratch(part) * 2
        + totals_scratch((32, C))
        + squares_scratch((16, C))
        + [pltpu.VMEM((ROWS, C), BF16), pltpu.SemaphoreType.REGULAR],
        compiler_params=pltpu.CompilerParams(
            collective_id=0, has_side_effects=True, vmem_limit_bytes=STEP_LIMIT
        ),
    )(z, eps, levels, counts, gen_w, fake_w, teacher_w, *smalls)[8:]


def adam_step(master, first_mom, second_mom, grad):
    first_new = BETA_ONE * first_mom + (1.0 - BETA_ONE) * grad
    second_new = BETA_TWO * second_mom + (1.0 - BETA_TWO) * grad * grad
    direction = (
        first_new
        / (1.0 - BETA_ONE**STEP)
        / (jnp.sqrt(second_new / (1.0 - BETA_TWO**STEP)) + ADAM_EPS)
    )
    return (master - LEARN_RATE * (direction + WEIGHT_DECAY * master), first_new, second_new)


EMA_RATE = 0.5 ** (20.0 / STEP)
SMALL_STATES = (4, 5, 6, 7, 11, 12, 13)


def update_kernel(gshard, fshard, stot, sqtot, *refs):
    ins, outs = refs[:14], refs[14:]
    norms, losses = outs[14:]
    count = stot[15:16, 0:1]
    norm_of, scales = [], []
    for n in range(2):
        rows = jnp.sum(sqtot[8 * n : 8 * n + 8, :], axis=0, keepdims=True)
        norm = jnp.sqrt(jnp.sum(rows, axis=1, keepdims=True)) / count
        scales.append(jnp.minimum(1.0, CLIP_NORM / norm) / count)
        norm_of.append(norm)

    def one(at, grad, w, m, v, ema, ow, om, ov, oe):
        new, first, second = adam_step(w[at], m[at], v[at], grad)
        ow[at] = new
        om[at] = first
        ov[at] = second
        if ema is not None:
            oe[at] = EMA_RATE * ema[at] + (1.0 - EMA_RATE) * new

    one(0, gshard[...] * scales[0], *ins[0:4], *outs[0:4])
    one(0, fshard[...] * scales[1], *ins[8:11], None, *outs[8:11], None)

    @pl.when(pl.program_id(0) == 0)
    def _():
        for n in range(2):
            norms[n] = norm_of[n][0, 0]
            losses[n] = (stot[13 + n : 14 + n, 0:1] / count)[0, 0]
        for k in range(13):
            one(k, stot[k : k + 1, :] * scales[0], *ins[4:8], *outs[4:8])
            one(k, stot[16 + k : 17 + k, :] * scales[1], *ins[11:14], None, *outs[11:14], None)


def update_nets(gshard, fshard, stot, sqtot, states):
    def turned(arrays):
        return [a.swapaxes(0, 1) if k in SMALL_STATES else a for k, a in enumerate(arrays)]

    part = gshard.shape[0]
    steps = 1
    big = pl.BlockSpec((1, part // steps, C), lambda i: (0, i, 0))
    low = pl.BlockSpec((13, 1, C), lambda i: (0, 0, 0))
    shard = pl.BlockSpec((part // steps, C), lambda i: (i, 0))
    whole = [pl.BlockSpec(a.shape, lambda i: (0, 0)) for a in (stot, sqtot)]
    specs = [low if k in SMALL_STATES else big for k in range(len(states))]
    states = turned(states)
    res = pl.pallas_call(
        update_kernel,
        grid=(steps,),
        out_shape=[jax.ShapeDtypeStruct(a.shape, F32) for a in states]
        + [jax.ShapeDtypeStruct((2,), F32)] * 2,
        in_specs=[shard] * 2 + whole + specs,
        out_specs=specs + [pl.BlockSpec(memory_space=pltpu.SMEM)] * 2,
        compiler_params=pltpu.CompilerParams(vmem_limit_bytes=VMEM_LIMIT),
    )(gshard, fshard, stot, sqtot, *states)
    return tuple(turned(res[:-2])) + tuple(res[-2:])


def gather_plain(shard):
    rows = lax.all_gather(shard.astype(BF16), "dp", axis=1, tiled=True)
    return lax.all_gather(rows, "section", axis=0, tiled=True)


def reduce_plain(bigs, small):
    shards_, squares = [], []
    own = lax.psum_scatter(small, "section", scatter_dimension=0, tiled=True)
    stot = lax.psum(own, "dp")[0]
    first = lax.axis_index("dp") == 0
    for n, big in enumerate(bigs):
        own = lax.psum_scatter(big, "section", scatter_dimension=0, tiled=True)
        own = lax.psum_scatter(own, "dp", scatter_dimension=1, tiled=True)[0].astype(F32)
        shards_.append(own)
        low = jnp.sum(jnp.square(stot[16 * n : 16 * n + 13]))
        squares.append(jnp.sum(own * own) + jnp.where(first, low, 0.0))
    sq = lax.psum(jnp.stack(squares), ("section", "dp"))
    return *shards_, stot, jnp.zeros((16, C), F32).at[jnp.array([0, 8]), 0].set(sq)


def shards(
    z_noise, eps_noise, levels, counts,
    gen_w, gen_m, gen_v, gen_ema, gen_small, gen_small_m, gen_small_v, gen_small_ema,
    fake_w, fake_m, fake_v, fake_small, fake_small_m, fake_small_v,
    teacher_w, teacher_small,
):
    if lax.axis_size("dp") == PLANES * PLANE:
        smalls = [a.swapaxes(0, 1) for a in (gen_small, fake_small, teacher_small)]
        reduced = run_step(
            z_noise, eps_noise, levels, counts, gen_w[0], fake_w[0], teacher_w[0], smalls
        )
    else:
        reduced = plain_step(
            z_noise, eps_noise, levels, counts, gen_w, fake_w, teacher_w,
            gen_small, fake_small, teacher_small,
        )
    return update_nets(
        *reduced,
        (
            gen_w, gen_m, gen_v, gen_ema, gen_small, gen_small_m, gen_small_v, gen_small_ema,
            fake_w, fake_m, fake_v, fake_small, fake_small_m, fake_small_v,
        ),
    )


def plain_step(
    z_noise, eps_noise, levels, counts, gen_w, fake_w, teacher_w,
    gen_small, fake_small, teacher_small,
):
    images = z_noise.shape[0] // lax.axis_size("section")
    start = lax.axis_index("section") * images

    def mine(a):
        return lax.dynamic_slice_in_dim(a, start, images, 0)

    z, eps = mine(z_noise), mine(eps_noise)
    sigma = sigma_levels(mine(levels))
    valid = (start + jnp.arange(images) < counts[0]).astype(F32)
    valid_sum = jnp.sum(valid)
    gen_eo = spread_embed(jnp.full((images,), SIGMA_INIT, F32))
    score_eo = spread_embed(sigma)
    gs, fs, ts = [
        lax.all_gather(a, "section", axis=0, tiled=True)
        for a in (gen_small, fake_small, teacher_small)
    ]
    gw, fw, tw = gather_plain(gen_w), gather_plain(fake_w), gather_plain(teacher_w)
    s_in, s_skip, s_out, s_lam = precondition(sigma)
    factor = valid * s_lam / (POS * C)
    s_in, s_skip, s_out, sigma, factor = [
        t[:, None, None] for t in (s_in, s_skip, s_out, sigma, factor)
    ]
    raw = SIGMA_INIT * z
    gen_saved = run_forward(GEN_IN * raw, gw, gs, gen_eo)
    samples = GEN_SKIP * raw + GEN_OUT * gen_saved[0][2]
    noisy = samples + sigma * eps
    x0 = s_in * noisy
    fake_saved = run_forward(x0, fw, fs, score_eo)
    fake_den = s_skip * noisy + s_out * fake_saved[0][2]
    miss = fake_den - samples
    _, fake_g, fake_sg = run_backward(
        s_out * 2.0 * factor * miss, fw, fs, score_eo, fake_saved, True
    )
    teacher_saved = run_forward(x0, tw, ts, score_eo)
    teacher_den = s_skip * noisy + s_out * teacher_saved[0][2]
    gap = teacher_den - fake_den
    loss_gen = jnp.sum(factor * ((1.0 - ALPHA_MIX) * gap * gap + gap * miss))
    loss_fake = jnp.sum(factor * miss * miss)
    grad_teacher = factor * (2.0 * (1.0 - ALPHA_MIX) * gap + miss)
    grad_fake = factor * gap - grad_teacher
    direct = factor * gap * (s_skip - 1.0)
    (back_t,) = run_backward(s_out * grad_teacher, tw, ts, score_eo, teacher_saved, False)
    (back_f,) = run_backward(s_out * grad_fake, fw, fs, score_eo, fake_saved, False)
    gen_cot = GEN_OUT * (direct + s_in * (back_t + back_f))
    _, gen_g, gen_sg = run_backward(gen_cot, gw, gs, gen_eo, gen_saved, True)
    scalars = jnp.broadcast_to(jnp.stack([loss_gen, loss_fake, valid_sum])[:, None], (3, C))
    small_sums = jnp.concatenate(
        [gen_sg[:, :13], jnp.broadcast_to(scalars, (2, 3, C)), fake_sg], axis=1
    )
    return reduce_plain((gen_g, fake_g), small_sums)


def solution(mesh):
    images = P("dp", None, None)
    big = P("section", "dp", None)
    small = P("section", None, None)
    return jax.shard_map(
        shards,
        mesh=mesh,
        in_specs=(images, images, P("dp"), P("dp"))
        + (big,) * 4 + (small,) * 4 + (big,) * 3 + (small,) * 3 + (big, small),
        out_specs=(big,) * 4 + (small,) * 4 + (big,) * 3 + (small,) * 3 + (P(), P()),
        check_vma=False,
    )
```

```python
import functools

import jax
import jax.numpy as jnp
from jax import lax
from jax.experimental import pallas as pl
from jax.experimental.pallas import tpu as pltpu
from jax.sharding import PartitionSpec as P

GROUPS = 32
SIDE = 16
LEVELS = 1000
STEP = 10

SIGMA_DATA = 0.5
SIGMA_INIT = 2.5
SIGMA_LOW = 0.05
SIGMA_HIGH = 20.0
RHO_POWER = 7.0
ALPHA_MIX = 1.2
RS = 0.7071067811865476
NORM_EPS = 1e-05
CLIP_NORM = 0.001
LEARN_RATE = 0.15
BETA_ONE = 0.9
BETA_TWO = 0.999
ADAM_EPS = 1e-08
WEIGHT_DECAY = 0.01

C = 256
HALF = 128
POS = 256
ROWS = 26 * C
CHUNK = 64
PAD = SIDE
F32 = jnp.float32
BF16 = jnp.bfloat16
VMEM_LIMIT = 58 * 2**20
STEP_LIMIT = 63 * 2**20

R_CONV1, R_CONV2, R_EMB, R_QKV, R_PROJ = 0, 9 * C, 18 * C, 22 * C, 25 * C
S_M1, S_I1, S_M2, S_I2, S_M3, S_I3, S_MA, S_MB = range(8)


def sigma_levels(level_ids):
    fraction = level_ids.astype(F32) / (LEVELS - 1)
    top_root = SIGMA_HIGH ** (1.0 / RHO_POWER)
    bottom_root = SIGMA_LOW ** (1.0 / RHO_POWER)
    return (top_root + fraction * (bottom_root - top_root)) ** RHO_POWER


def precondition(sigma_vals):
    total = sigma_vals * sigma_vals + SIGMA_DATA**2
    return (
        lax.rsqrt(total),
        SIGMA_DATA**2 / total,
        sigma_vals * SIGMA_DATA * lax.rsqrt(total),
        total / (sigma_vals * sigma_vals * SIGMA_DATA**2),
    )


def noise_embed(sigma_vals, channel_count):
    frequency = (1.0 / 10000.0) ** (jnp.arange(channel_count, dtype=F32) / channel_count)
    angles = (jnp.log(sigma_vals) / 4.0)[..., None] * frequency
    return jnp.concatenate([jnp.cos(angles), jnp.sin(angles)], axis=-1)


def spread_embed(sigma_vals):
    emb = noise_embed(sigma_vals, C).astype(BF16)
    images = emb.shape[0]
    zero = jnp.zeros_like(emb)
    low = jnp.stack([emb, zero], axis=-1).reshape(images, 4 * C)
    high = jnp.stack([zero, emb], axis=-1).reshape(images, 4 * C)
    fill = jnp.zeros((4 - images, 4 * C), BF16)
    return jnp.concatenate([low, fill, high, fill], axis=0)


def dot_nn(a, b):
    return lax.dot_general(a, b, (((1,), (0,)), ((), ())), preferred_element_type=F32)


def dot_nt(a, b):
    return lax.dot_general(a, b, (((1,), (1,)), ((), ())), preferred_element_type=F32)


def dot_tn(a, b):
    return lax.dot_general(a, b, (((0,), (0,)), ((), ())), preferred_element_type=F32)


def group_mean(v):
    lane = lax.broadcasted_iota(jnp.int32, (8, C), 1)
    for sh in (1, 2, 4):
        v = v + jnp.where((lane & sh) != 0, pltpu.roll(v, sh, 1), pltpu.roll(v, C - sh, 1))
    return v * (1.0 / (POS * 8))


def colsum(v):
    return jnp.sum(v, axis=0, keepdims=True)


def no_pump(l):
    pass


FORWARD_POINTS, BACKWARD_POINTS, WEIGHT_POINTS = 10, 12, 18
HALF_WAY, READY = 8, 13


def stagger(steps, images, between):
    for t in range(len(steps) + images - 1):
        for i in range(images):
            if 0 <= t - i < len(steps):
                steps[t - i](i)
        between()


class Pump:
    def __init__(self, steps, points, layers, lo=0.0, hi=1.0):
        self.table = {l: [[] for _ in range(points)] for l in layers}
        self.at = 0
        for k, step in enumerate(steps):
            place = int((lo + (hi - lo) * (k + 0.5) / len(steps)) * points * len(layers))
            self.table[layers[place // points]][place % points].append(step)

    def __call__(self, l):
        for layer, points in self.table.items():
            if points[self.at]:

                @pl.when(l == layer)
                def _(todo=points[self.at]):
                    for step in todo:
                        step()

        self.at += 1


def put_shifted(bufs, i, r, v):
    rows = v.shape[0]
    at = pl.ds(PAD + r, rows)
    sub = lax.broadcasted_iota(jnp.int32, (rows // SIDE, 8, C), 1)
    x = v.reshape(rows // SIDE, 2, 8, C)
    low, high = x[:, 0], x[:, 1]
    low_up, high_up = pltpu.roll(low, 1, 1), pltpu.roll(high, 1, 1)
    low_down, high_down = pltpu.roll(low, 7, 1), pltpu.roll(high, 7, 1)
    left = (jnp.where(sub == 0, 0.0, low_up), jnp.where(sub == 0, low_up, high_up))
    right = (jnp.where(sub == 7, high_down, low_down), jnp.where(sub == 7, 0.0, high_down))
    bufs[0, i, at, :] = jnp.stack(left, axis=1).reshape(rows, C).astype(BF16)
    bufs[1, i, at, :] = v.astype(BF16)
    bufs[2, i, at, :] = jnp.stack(right, axis=1).reshape(rows, C).astype(BF16)


def taps(bufs, flip):
    images = bufs.shape[1]
    out = []
    for dr in (-1, 0, 1):
        for dc in (-1, 0, 1):
            sr, sc = (-dr, -dc) if flip else (dr, dc)
            piece = bufs[sc + 1, :, PAD + SIDE * sr : PAD + SIDE * sr + POS, :]
            out.append(piece.reshape(images * POS, C))
    return out


def conv_forward(bufs, w, l, row):
    return dot_nn(jnp.concatenate(taps(bufs, False), axis=1), w[l, row : row + 9 * C, :])


def conv_input_grad(bufs, w, l, row):
    parts = [w[l, row + t * C : row + (t + 1) * C, :] for t in range(9)]
    return dot_nt(jnp.concatenate(taps(bufs, True), axis=1), jnp.concatenate(parts, axis=1))


def conv_weight_grad(act_t, bufs, grad, l, row):
    left = act_t[...]
    for t, piece in enumerate(taps(bufs, True)):
        grad[l, row + t * C : row + (t + 1) * C, :] = dot_nn(left, piece).astype(BF16)


def silu(v):
    h = 0.5 * v
    return h + h * jnp.tanh(h)


def silu_parts(v):
    s = 0.5 + 0.5 * jnp.tanh(0.5 * v)
    return s, s * (1.0 + v * (1.0 - s))


def clear_pads(bufs):
    zero = jnp.zeros(bufs.shape[:2] + (PAD, C), BF16)
    bufs[:, :, 0:PAD, :] = zero
    bufs[:, :, PAD + POS :, :] = zero


def split_qkv(w, l, qkvw, tmp):
    for h in range(2):
        tmp[h] = w[l, R_QKV : R_QKV + 3 * C, h * HALF : (h + 1) * HALF].astype(F32)
    for j in range(3):
        for h in range(2):
            at = j * C + h * HALF
            qkvw[:, at : at + HALF] = tmp[h, pl.ds(j, C, stride=3), :].astype(BF16)


def norm_sums(x):
    pivot = x[0:1]
    d = x - pivot
    return colsum(d), colsum(d * d), pivot


def norm_stats(sums):
    fill = [jnp.zeros((4 - len(sums), C), F32)]
    s1, s2, pivot = [jnp.concatenate([a[k] for a in sums] + fill, axis=0) for k in range(3)]
    centre = group_mean(jnp.concatenate([pivot, pivot], axis=0) * POS)[0:4]
    off = pivot - centre
    first = s1 + POS * off
    second = s2 + off * (2.0 * s1 + POS * off)
    means = group_mean(jnp.concatenate([first, second], axis=0))
    spread = jnp.maximum(means[4:8] - jnp.square(means[0:4]), 0.0)
    return centre + means[0:4], lax.rsqrt(spread + NORM_EPS)


def two_means(a, b):
    rows = jnp.concatenate([a, b] * 4, axis=0)
    means = group_mean(rows)
    return means[0:1], means[1:2]


def tap_rows(bufs, flip, which):
    out = []
    for dr in (-1, 0, 1):
        for dc in (-1, 0, 1):
            sr, sc = (-dr, -dc) if flip else (dr, dc)
            at = slice(PAD + SIDE * sr, PAD + SIDE * sr + POS)
            piece = jnp.concatenate([bufs[sc + 1, i, at, :] for i in which], axis=0)
            out.append(piece)
    return out


def layer_forward(l, w, small, eo, xs, h1, y, qkv, att, o, st, bufs, nbuf, qkvw, tmp, staged, pump):
    images = h1.shape[1]
    split_qkv(w, l, qkvw, tmp)
    mod = dot_nn(eo[...], w[l, R_EMB : R_EMB + 4 * C, :])
    ma = mod[0:4] + small[l, 5:6, :]
    mb = mod[4:8] + small[l, 6:7, :]
    for i in range(images):
        st[l, i, S_MA : S_MA + 1, :] = ma[i : i + 1]
        st[l, i, S_MB : S_MB + 1, :] = mb[i : i + 1]

    sums = {}

    def row(k):
        return small[l, k : k + 1, :]

    def keep(which, mean, inv, at):
        for k, i in enumerate(which):
            st[l, i, at : at + 1, :] = mean[k : k + 1]
            st[l, i, at + 1 : at + 2, :] = inv[k : k + 1]

    def first(which):
        mean, inv = norm_stats([norm_sums(xs[l, i]) for i in which])
        keep(which, mean, inv, S_M1)
        for k, i in enumerate(which):
            a = inv[k : k + 1] * row(0)
            for r in range(0, POS, CHUNK):
                v = (xs[l, i, r : r + CHUNK, :] - mean[k : k + 1]) * a + row(1)
                put_shifted(bufs, i, r, silu(v))

    def conv(which, at):
        left = jnp.concatenate(tap_rows(bufs, False, which), axis=1)
        return dot_nn(left, w[l, at : at + 9 * C, :])

    def conv_one(which):
        out = conv(which, R_CONV1)
        for k, i in enumerate(which):
            own = out[k * POS : (k + 1) * POS]
            own = own + row(2)
            sums[i] = norm_sums(own)
            h1[l, i] = own

    def second(which):
        mean, inv = norm_stats([sums[i] for i in which])
        keep(which, mean, inv, S_M2)
        for k, i in enumerate(which):
            gain = 1.0 + ma[i : i + 1]
            a = inv[k : k + 1] * row(3) * gain
            b = row(4) * gain + mb[i : i + 1]
            for r in range(0, POS, CHUNK):
                v = (h1[l, i, r : r + CHUNK, :] - mean[k : k + 1]) * a + b
                put_shifted(bufs, i, r, silu(v))

    def conv_two(which):
        out = conv(which, R_CONV2) + row(7)
        for k, i in enumerate(which):
            own = (xs[l, i] + out[k * POS : (k + 1) * POS]) * RS
            sums[i] = norm_sums(own)
            y[l, i] = own

    def third(which):
        mean, inv = norm_stats([sums[i] for i in which])
        keep(which, mean, inv, S_M3)
        for k, i in enumerate(which):
            a = inv[k : k + 1] * row(8)
            for r in range(0, POS, CHUNK):
                v = (y[l, i, r : r + CHUNK, :] - mean[k : k + 1]) * a + row(9)
                nbuf[i, r : r + CHUNK, :] = v.astype(BF16)

    def project_in(which):
        n = jnp.concatenate([nbuf[i] for i in which], axis=0)
        for j, at in ((0, 10), (1, None), (2, 11)):
            part = dot_nn(n, qkvw[:, j * C : (j + 1) * C])
            if at is not None:
                part = part + row(at)
            part = part.astype(BF16)
            for k, i in enumerate(which):
                qkv[l, i, :, j * C : (j + 1) * C] = part[k * POS : (k + 1) * POS]

    def attend(which):
        scores = [dot_nt(qkv[l, i, :, 0:C], qkv[l, i, :, C : 2 * C]) for i in which]
        for s, i in zip(scores, which):
            e = jnp.exp((s - jnp.max(s, axis=1, keepdims=True)) * (C**-0.5))
            p = (e * (1.0 / jnp.sum(e, axis=1, keepdims=True))).astype(BF16)
            att[l, i] = p
            o[l, i] = dot_nn(p, qkv[l, i, :, 2 * C :]).astype(BF16)

    def project_out(which):
        left = jnp.concatenate([o[l, i] for i in which], axis=0)
        out = dot_nn(left, w[l, R_PROJ:, :]) + row(12)
        for k, i in enumerate(which):
            xs[l + 1, i] = (y[l, i] + out[k * POS : (k + 1) * POS]) * RS

    steps = (first, conv_one, second, conv_two, third, project_in, attend, project_out)
    if not staged:
        for step in steps:
            step(range(images))
            pump(l)
    else:
        stagger([lambda i, step=step: step([i]) for step in steps], images, lambda: pump(l))


def layer_backward(
    l, w, small, eo, xs, h1, y, qkv, att, o, st, g, bufs, nbuf, qkvw, tmp, dn, dqkv, act_t,
    grad, sgrad, pump, need_dx=None,
):
    want = grad is not None
    images = h1.shape[1]
    which = range(images)
    flat = images * POS
    scale = C**-0.5
    split_qkv(w, l, qkvw, tmp)

    def row(k):
        return small[l, k : k + 1, :]

    def rows8(rows):
        return jnp.concatenate(list(rows) + [jnp.zeros((8 - len(rows), C), F32)], axis=0)

    zero = jnp.zeros((1, C), F32)
    gps, c1, c2, p1, p2 = {}, {}, {}, {}, {}
    total = {7: zero, 2: zero}
    gains = [1.0 + st[l, i, S_MA : S_MA + 1, :] for i in which]

    def project_out(i):
        gps[i] = (g[i] * RS).astype(BF16)
        nbuf[i] = dot_nt(gps[i], w[l, R_PROJ:, :]).astype(BF16)

    def attend(i):
        p = att[l, i]
        pf = p.astype(F32)
        dp = dot_nt(nbuf[i], qkv[l, i, :, 2 * C :])
        ds = (pf * (dp - jnp.sum(dp * pf, axis=1, keepdims=True))).astype(BF16)
        dqkv[i, :, 0:C] = (dot_nn(ds, qkv[l, i, :, C : 2 * C]) * scale).astype(BF16)
        dqkv[i, :, C : 2 * C] = (dot_tn(ds, qkv[l, i, :, 0:C]) * scale).astype(BF16)
        dqkv[i, :, 2 * C :] = dot_tn(p, nbuf[i]).astype(BF16)

    def project_in(i):
        mean, inv = st[l, i, S_M3 : S_M3 + 1, :], st[l, i, S_I3 : S_I3 + 1, :]
        d = dot_nt(dqkv[i], qkvw[...])
        dn[i] = d
        c1[i] = colsum(d)
        c2[i] = colsum(d * ((y[l, i] - mean) * inv))

    def third(i):
        mean, inv = st[l, i, S_M3 : S_M3 + 1, :], st[l, i, S_I3 : S_I3 + 1, :]
        mg, mc = two_means(row(8) * c1[i], row(8) * c2[i])
        for r in range(0, POS, CHUNK):
            nh = (y[l, i, r : r + CHUNK, :] - mean) * inv
            gm = g[i, r : r + CHUNK, :] * RS + inv * (row(8) * dn[i, r : r + CHUNK, :] - mg - nh * mc)
            gm = gm * RS
            g[i, r : r + CHUNK, :] = gm
            put_shifted(bufs, i, r, gm)
            if want:
                nbuf[i, r : r + CHUNK, :] = (nh * row(8) + row(9)).astype(BF16)
                total[7] = total[7] + colsum(gm)

    def conv_grad(i, at):
        left = jnp.concatenate(tap_rows(bufs, True, [i]), axis=1)
        parts = [w[l, at + t * C : at + (t + 1) * C, :] for t in range(9)]
        dn[i] = dot_nt(left, jnp.concatenate(parts, axis=1))

    def activation(i, src, mean, inv, a, b, act=None):
        s1, s2 = zero, zero
        for r in range(0, POS, CHUNK):
            nh = (src[l, i, r : r + CHUNK, :] - mean) * inv
            pre = nh * a + b
            s, slope = silu_parts(pre)
            d = dn[i, r : r + CHUNK, :] * slope
            dn[i, r : r + CHUNK, :] = d
            s1 = s1 + colsum(d)
            s2 = s2 + colsum(d * nh)
            if act is not None:
                act[i, r : r + CHUNK, :] = (pre * s).astype(BF16)
        p1[i], p2[i] = s1, s2

    def second_a(i):
        mean, inv = st[l, i, S_M2 : S_M2 + 1, :], st[l, i, S_I2 : S_I2 + 1, :]
        b = row(4) * gains[i] + st[l, i, S_MB : S_MB + 1, :]
        activation(i, h1, mean, inv, row(3) * gains[i], b, nbuf if want else None)

    def second_b(i):
        mean, inv = st[l, i, S_M2 : S_M2 + 1, :], st[l, i, S_I2 : S_I2 + 1, :]
        full = row(3) * gains[i]
        mg, mc = two_means(full * p1[i], full * p2[i])
        for r in range(0, POS, CHUNK):
            nh = (h1[l, i, r : r + CHUNK, :] - mean) * inv
            dh = inv * (full * dn[i, r : r + CHUNK, :] - mg - nh * mc)
            put_shifted(bufs, i, r, dh)
            if want:
                total[2] = total[2] + colsum(dh)

    def first_a(i):
        mean, inv = st[l, i, S_M1 : S_M1 + 1, :], st[l, i, S_I1 : S_I1 + 1, :]
        activation(i, xs, mean, inv, row(0), row(1))

    def first_act(i):
        mean, inv = st[l, i, S_M1 : S_M1 + 1, :], st[l, i, S_I1 : S_I1 + 1, :]
        for r in range(0, POS, CHUNK):
            v = (xs[l, i, r : r + CHUNK, :] - mean) * (inv * row(0)) + row(1)
            nbuf[i, r : r + CHUNK, :] = silu(v).astype(BF16)

    def first_b(i):
        mean, inv = st[l, i, S_M1 : S_M1 + 1, :], st[l, i, S_I1 : S_I1 + 1, :]
        mg, mc = two_means(row(0) * p1[i], row(0) * p2[i])
        for r in range(0, POS, CHUNK):
            nh = (xs[l, i, r : r + CHUNK, :] - mean) * inv
            dx = inv * (row(0) * dn[i, r : r + CHUNK, :] - mg - nh * mc)
            g[i, r : r + CHUNK, :] = g[i, r : r + CHUNK, :] + dx

    upper = [project_out, attend, project_in, third, lambda i: conv_grad(i, R_CONV2)]
    lower = [lambda i: conv_grad(i, R_CONV1), first_a]
    if not want:
        stagger(upper + [second_a, second_b] + lower + [first_b], images, lambda: pump(l))
        return
    stagger(upper, images, lambda: pump(l))
    gp = jnp.concatenate([gps[i] for i in which], axis=0)
    grad[l, R_PROJ:, :] = dot_tn(o[l].reshape(flat, C), gp).astype(BF16)
    sgrad[l, 12:13, :] = colsum(gp.astype(F32))
    sgrad[l, 7:8, :] = total[7]
    sgrad[l, 8:9, :] = colsum(rows8([c2[i] for i in which]))
    sgrad[l, 9:10, :] = colsum(rows8([c1[i] for i in which]))
    act_t[...] = nbuf[...].reshape(flat, C).T
    for j in range(3):
        dj = dqkv[:, :, j * C : (j + 1) * C].reshape(flat, C)
        part = dot_nn(act_t[...], dj)
        for h in range(2):
            tmp[h, pl.ds(j, C, stride=3), :] = part[:, h * HALF : (h + 1) * HALF]
        if j != 1:
            sgrad[l, 10 + j // 2 : 11 + j // 2, :] = colsum(dj.astype(F32))
    for h in range(2):
        grad[l, R_QKV : R_QKV + 3 * C, h * HALF : (h + 1) * HALF] = tmp[h].astype(BF16)
    for i in which:
        second_a(i)
    pump(l)
    act_t[...] = nbuf[...].reshape(flat, C).T
    conv_weight_grad(act_t, bufs, grad, l, R_CONV2)
    p18, p28, modgain = [rows8([a[i] for i in which]) for a in (p1, p2, gains)]
    dma = row(3) * p28 + row(4) * p18
    sgrad[l, 3:4, :] = colsum(modgain * p28)
    sgrad[l, 4:5, :] = colsum(modgain * p18)
    sgrad[l, 5:6, :] = colsum(dma)
    sgrad[l, 6:7, :] = colsum(p18)
    grad[l, R_EMB : R_EMB + 4 * C, :] = embed_grad(
        eo, jnp.concatenate([dma[0:4], p18[0:4]], axis=0)
    ).astype(BF16)
    pump(l)
    stagger([second_b, first_act], images, lambda: pump(l))
    act_t[...] = nbuf[...].reshape(flat, C).T
    conv_weight_grad(act_t, bufs, grad, l, R_CONV1)
    pump(l)
    stagger(lower, images, lambda: pump(l))
    sgrad[l, 2:3, :] = total[2]
    sgrad[l, 0:1, :] = colsum(rows8([p2[i] for i in which]))
    sgrad[l, 1:2, :] = colsum(rows8([p1[i] for i in which]))

    @pl.when(l == 1)
    def _():
        for i in which:
            first_b(i)


def embed_grad(eo, dm):
    parts, rest = [], dm
    for _ in range(3):
        parts.append(rest.astype(BF16))
        rest = rest - parts[-1].astype(F32)
    left = eo[...]
    return dot_tn(jnp.concatenate([left, left], axis=0), jnp.concatenate(parts[:2], axis=0)) + dot_tn(
        left, parts[2]
    )


def saved_shapes(images):
    return [
        jax.ShapeDtypeStruct((3, images, POS, C), F32),
        jax.ShapeDtypeStruct((2, images, POS, C), F32),
        jax.ShapeDtypeStruct((2, images, POS, C), F32),
        jax.ShapeDtypeStruct((2, images, POS, 3 * C), BF16),
        jax.ShapeDtypeStruct((2, images, POS, POS), BF16),
        jax.ShapeDtypeStruct((2, images, POS, C), BF16),
        jax.ShapeDtypeStruct((2, images, 8, C), F32),
    ]


def forward_kernel(staged, x0, w, small, eo, xs, h1, y, qkv, att, o, st, bufs, nbuf, qkvw, tmp):
    clear_pads(bufs)
    xs[0] = x0[...]

    def body(l, _):
        layer_forward(
            l, w, small, eo, xs, h1, y, qkv, att, o, st, bufs, nbuf, qkvw, tmp, staged, no_pump
        )
        return 0

    lax.fori_loop(0, 2, body, 0)


def backward_kernel(want, *refs):
    cot, w, small, eo, xs, h1, y, qkv, att, o, st, g = refs[:12]
    refs = refs[12:]
    if want:
        grad, sgrad = refs[:2]
        refs = refs[2:]
    else:
        grad, sgrad = None, None
    bufs, nbuf, qkvw, tmp, dn, dqkv, act_t = refs
    clear_pads(bufs)
    g[...] = cot[...]
    if want:
        sgrad[...] = jnp.zeros(sgrad.shape, F32)

    def body(k, _):
        layer_backward(
            1 - k, w, small, eo, xs, h1, y, qkv, att, o, st, g, bufs, nbuf, qkvw, tmp, dn,
            dqkv, act_t, grad, sgrad, no_pump,
        )
        return 0

    lax.fori_loop(0, 2, body, 0)


def vm(n):
    return [pl.BlockSpec(memory_space=pltpu.VMEM)] * n


def scratch_forward(images):
    return [
        pltpu.VMEM((3, images, POS + 2 * PAD, C), BF16),
        pltpu.VMEM((images, POS, C), BF16),
        pltpu.VMEM((C, 3 * C), BF16),
        pltpu.VMEM((2, 3 * C, HALF), F32),
    ]


def run_forward(x0, w, small, eo, staged=False):
    images = x0.shape[0]
    return pl.pallas_call(
        functools.partial(forward_kernel, staged),
        out_shape=saved_shapes(images),
        in_specs=vm(4),
        out_specs=vm(7),
        scratch_shapes=scratch_forward(images),
        compiler_params=pltpu.CompilerParams(vmem_limit_bytes=VMEM_LIMIT),
    )(x0, w, small, eo)


def run_backward(cot, w, small, eo, saved, want):
    images = cot.shape[0]
    outs = [jax.ShapeDtypeStruct(cot.shape, F32)]
    if want:
        outs += [
            jax.ShapeDtypeStruct((2, ROWS, C), BF16),
            jax.ShapeDtypeStruct((2, 16, C), F32),
        ]
    return pl.pallas_call(
        functools.partial(backward_kernel, want),
        out_shape=outs,
        in_specs=vm(11),
        out_specs=vm(len(outs)),
        scratch_shapes=scratch_forward(images)
        + [
            pltpu.VMEM((images, POS, C), F32),
            pltpu.VMEM((images, POS, 3 * C), BF16),
            pltpu.VMEM((C, images * POS), BF16),
        ],
        compiler_params=pltpu.CompilerParams(vmem_limit_bytes=VMEM_LIMIT),
    )(cot, w, small, eo, *saved)


PLANES, PLANE = 4, 4
MESH = pl.DeviceIdType.MESH


class Place:
    def __init__(self):
        self.sec = lax.axis_index("section")
        self.d = lax.axis_index("dp")
        self.x = lax.rem(self.d, 2)
        self.y = lax.rem(self.d // 2, 2)
        self.z = self.d // PLANE
        self.seat = self.sec * PLANE + lax.rem(self.d, PLANE)
        self.sib = {"section": 1 - self.sec}
        self.xn = {"dp": self.d + 1 - 2 * self.x}
        self.yn = {"dp": self.d + 2 - 4 * self.y}

    def plane(self, j):
        return lax.rem(self.z + j + PLANES, PLANES)

    def zpeer(self, j):
        return {"dp": self.plane(j) * PLANE + lax.rem(self.d, PLANE)}

    def plane_peer(self, j):
        seat = lax.rem(self.seat + j, 2 * PLANE)
        return {"section": seat // PLANE, "dp": self.z * PLANE + lax.rem(seat, PLANE)}

    def meet(self):
        barrier = pltpu.get_barrier_semaphore()
        others = [self.plane_peer(j) for j in range(1, 8)] + [self.zpeer(j) for j in (1, 2, 3)]
        for other in others:
            pl.semaphore_signal(barrier, inc=1, device_id=other, device_id_type=MESH)
        pl.semaphore_wait(barrier, len(others))


def remote(src, dst, send, recv, target):
    return pltpu.make_async_remote_copy(
        src_ref=src, dst_ref=dst, send_sem=send, recv_sem=recv,
        device_id=target, device_id_type=MESH,
    )


Z1, X1, Y1, X2, Y2, S_OWN, S_X, S_Y, S_DA, S_DB = 0, 3, 7, 11, 15, 19, 23, 27, 31, 35
SLOTS = 39


class Gather:
    def __init__(self, me, net, stage, local_sem, send_sem, recv_sem):
        self.me, self.net, self.stage = me, net, stage
        self.local_sem, self.send_sem, self.recv_sem = local_sem, send_sem, recv_sem
        self.part = stage.shape[0]
        self.half = self.part // 2

    def rows(self, plane, y, x, lo, count):
        at = (plane * PLANE + y * 2 + x) * self.part + lo
        return self.net.at[self.me.sec, pl.ds(pl.multiple_of(at, 16), count)]

    def own(self, j):
        return self.rows(self.me.plane(-j), self.me.y, self.me.x, 0, self.part)

    def send(self, slot, piece, target, src=None):
        src = piece if src is None else src
        remote(src, piece, self.send_sem.at[slot], self.recv_sem.at[slot], target).start()

    def arrived(self, slot, piece):
        remote(
            piece, piece, self.send_sem.at[slot], self.recv_sem.at[slot], self.me.sib
        ).wait_recv()

    def local(self):
        return pltpu.make_async_copy(self.stage, self.own(0), self.local_sem)

    def begin(self):
        me = self.me
        for j in (1, 2, 3):
            self.send(Z1 + j - 1, self.own(0), me.zpeer(j), self.stage)
        for slot, target in ((X1, me.xn), (Y1, me.yn), (S_OWN, me.sib)):
            self.send(slot, self.own(0), target, self.stage)
        self.local().start()

    def phase1(self):
        def step(j):
            me = self.me
            self.arrived(Z1 + j - 1, self.own(j))
            for slot, target in ((X1, me.xn), (Y1, me.yn), (S_OWN, me.sib)):
                self.send(slot + j, self.own(j), target)

        return [lambda j=j: step(j) for j in (1, 2, 3)]

    def phase2(self):
        me, part, half = self.me, self.part, self.half

        def step_x(j):
            plane = me.plane(-j)
            self.arrived(X1 + j, self.rows(plane, me.y, 1 - me.x, 0, part))
            self.send(Y2 + j, self.rows(plane, me.y, 1 - me.x, 0, half), me.yn)
            self.send(S_X + j, self.rows(plane, me.y, 1 - me.x, 0, part), me.sib)

        def step_y(j):
            plane = me.plane(-j)
            self.arrived(Y1 + j, self.rows(plane, 1 - me.y, me.x, 0, part))
            self.send(X2 + j, self.rows(plane, 1 - me.y, me.x, half, half), me.xn)
            self.send(S_Y + j, self.rows(plane, 1 - me.y, me.x, 0, part), me.sib)

        return [lambda f=f, j=j: f(j) for j in range(PLANES) for f in (step_x, step_y)]

    def phase3(self):
        def step(j, slot, to, lo):
            me = self.me
            where = self.rows(me.plane(-j), 1 - me.y, 1 - me.x, lo, self.half)
            self.arrived(slot + j, where)
            self.send(to + j, where, me.sib)

        return [
            lambda j=j, a=a: step(j, *a)
            for j in range(PLANES)
            for a in ((Y2, S_DA, 0), (X2, S_DB, self.half))
        ]

    def finish(self):
        def step():
            for slot in range(S_OWN, SLOTS):
                count = self.part if slot < S_DA else self.half
                self.arrived(slot, self.rows(0, 0, 0, 0, count))
            self.local().wait()

        return [step]

    def drain(self):
        for slot in range(SLOTS):
            whole = slot < X2 or S_OWN <= slot < S_DA
            piece = self.rows(0, 0, 0, 0, self.part if whole else self.half)
            remote(
                piece, piece, self.send_sem.at[slot], self.recv_sem.at[slot], self.me.sib
            ).wait_send()


A_SLOT, B_SLOT, C_SLOT, D_SLOT = 0, 4, 20, 28
R_SLOTS = 31


class Reduce:
    def __init__(self, me, big, shard, sib, there, rb, rc, rd, ssem, rsem):
        self.me, self.big, self.shard = me, big, shard
        self.sib, self.there, self.rb, self.rc, self.rd = sib, there, rb, rc, rd
        self.ssem, self.rsem = ssem, rsem
        self.part = shard.shape[0]
        self.half = self.part // 2
        self.span = PLANE * self.part

    def zt(self, k):
        return (3, 2, 0, 1)[k]

    def block(self, k):
        return pl.ds(self.zt(k) * self.span, self.span)

    def piece(self, k, y, x, lo, count):
        at = (self.zt(k) * PLANE + y * 2 + x) * self.part + lo
        return pl.ds(pl.multiple_of(at, 16), count)

    def send(self, src, dst, slot, target):
        remote(src, dst, self.ssem.at[slot], self.rsem.at[slot], target).start()

    def arrived(self, dst, slot):
        remote(dst, dst, self.ssem.at[slot], self.rsem.at[slot], self.me.sib).wait_recv()

    def begin(self):
        for k in range(PLANES):
            self.begin_block(k)

    def begin_block(self, k):
        at = self.block(k)
        self.send(self.big.at[1 - self.me.sec, at], self.there.at[at], A_SLOT + k, self.me.sib)

    def stage_a(self, k):
        me, half = self.me, self.half
        self.arrived(self.sib.at[self.block(k)], A_SLOT + k)
        base = self.zt(k) * self.span

        def body(i, _):
            at = pl.ds(pl.multiple_of(base + i * half, 16), half)
            self.big[me.sec, at, :] = (
                self.big[me.sec, at, :].astype(F32) + self.sib[at, :].astype(F32)
            ).astype(BF16)
            return 0

        lax.fori_loop(0, 2 * PLANE, body, 0)
        for j in range(2):
            self.send(
                self.big.at[me.sec, self.piece(k, 1 - me.y, j, 0, half)], self.rb.at[k, j],
                B_SLOT + 4 * k + j, me.yn,
            )
            self.send(
                self.big.at[me.sec, self.piece(k, j, 1 - me.x, half, half)], self.rb.at[k, 2 + j],
                B_SLOT + 4 * k + 2 + j, me.xn,
            )

    def join(self, where, other):
        self.big[self.me.sec, where, :] = (
            self.big[self.me.sec, where, :].astype(F32) + other.astype(F32)
        ).astype(BF16)

    def stage_c(self, k):
        me, half = self.me, self.half
        for j in range(4):
            self.arrived(self.rb.at[k, j], B_SLOT + 4 * k + j)
            y, x, lo = (me.y, j, 0) if j < 2 else (j - 2, me.x, half)
            self.join(self.piece(k, y, x, lo, half), self.rb[k, j])
        self.send(
            self.big.at[me.sec, self.piece(k, me.y, 1 - me.x, 0, half)], self.rc.at[k, 0],
            C_SLOT + 2 * k, me.xn,
        )
        self.send(
            self.big.at[me.sec, self.piece(k, 1 - me.y, me.x, half, half)], self.rc.at[k, 1],
            C_SLOT + 2 * k + 1, me.yn,
        )

    def stage_d(self, k):
        me, half, zt = self.me, self.half, self.zt(k)
        for j in range(2):
            self.arrived(self.rc.at[k, j], C_SLOT + 2 * k + j)
            self.join(self.piece(k, me.y, me.x, j * half, half), self.rc[k, j])

        @pl.when(me.z != zt)
        def _():
            self.send(
                self.big.at[me.sec, self.piece(k, me.y, me.x, 0, self.part)],
                self.rd.at[lax.rem(zt - me.z + PLANES, PLANES) - 1],
                D_SLOT + lax.rem(zt - me.z + PLANES, PLANES) - 1,
                {"dp": zt * PLANE + lax.rem(me.d, PLANE)},
            )

    def stage_e(self):
        for j in range(PLANES - 1):
            self.arrived(self.rd.at[j], D_SLOT + j)
        at = pl.ds(pl.multiple_of(self.me.d * self.part, 16), self.part)
        self.shard[...] = (
            self.big[self.me.sec, at, :].astype(F32)
            + self.rd[0].astype(F32) + (self.rd[1].astype(F32) + self.rd[2].astype(F32))
        )

    def steps(self):
        out = []
        for t in range(PLANES + 2):
            for stage, lag in ((self.stage_a, 0), (self.stage_c, 1), (self.stage_d, 2)):
                if 0 <= t - lag < PLANES:
                    out.append(lambda stage=stage, k=t - lag: stage(k))
        return out

    def drain(self, lo=0, hi=R_SLOTS):
        for slot in range(lo, hi):
            if slot < B_SLOT:
                piece = self.there.at[pl.ds(0, self.span)]
            elif slot < D_SLOT:
                piece = self.rb.at[0, 0]
            else:
                piece = self.rd.at[0]
            remote(piece, piece, self.ssem.at[slot], self.rsem.at[slot], self.me.sib).wait_send()


def reduce_scratch(part):
    half = part // 2
    return [
        pltpu.VMEM((PLANES, 4, half, C), BF16),
        pltpu.VMEM((PLANES, 2, half, C), BF16),
        pltpu.VMEM((PLANES - 1, part, C), BF16),
        pltpu.SemaphoreType.DMA((R_SLOTS,)),
        pltpu.SemaphoreType.DMA((R_SLOTS,)),
    ]


class Totals:
    def __init__(self, me, buf, recv, ssem, rsem):
        self.me, self.buf, self.recv, self.ssem, self.rsem = me, buf, recv, ssem, rsem

    def send(self, src, dst, slot, target):
        remote(src, dst, self.ssem.at[slot], self.rsem.at[slot], target).start()

    def arrived(self, dst, slot):
        remote(dst, dst, self.ssem.at[slot], self.rsem.at[slot], self.me.sib).wait_recv()

    def begin(self, first):
        self.send(first, self.recv.at[0], 0, self.me.sib)

    def steps(self):
        me, buf, recv = self.me, self.buf, self.recv

        def one():
            self.arrived(recv.at[0], 0)
            buf[1] = buf[0] + recv[0]
            self.send(buf.at[1], recv.at[1], 1, me.xn)

        def two():
            self.arrived(recv.at[1], 1)
            buf[2] = buf[1] + recv[1]
            self.send(buf.at[2], recv.at[2], 2, me.yn)

        def three():
            self.arrived(recv.at[2], 2)
            buf[3] = buf[2] + recv[2]
            recv[3 + me.z] = buf[3]
            for j in (1, 2, 3):
                self.send(buf.at[3], recv.at[3 + me.z], 2 + j, me.zpeer(j))

        return [one, two, three]

    def result(self):
        for j in (1, 2, 3):
            self.arrived(self.recv.at[3 + self.me.plane(-j)], 2 + j)
        return (self.recv[3] + self.recv[4]) + (self.recv[5] + self.recv[6])

    def drain(self):
        for slot in range(6):
            piece = self.recv.at[0]
            remote(piece, piece, self.ssem.at[slot], self.rsem.at[slot], self.me.sib).wait_send()


class Squares:
    def __init__(self, me, own, recv, ssem, rsem):
        self.me, self.own, self.recv, self.ssem, self.rsem = me, own, recv, ssem, rsem

    def hop(self, src, base, mine, peers, slots):
        for j, target in peers:
            dst = self.recv.at[base + mine]
            remote(src, dst, self.ssem.at[slots + j], self.rsem.at[slots + j], target).start()
        self.recv[base + mine] = src[...]
        for j, _ in peers:
            dst = self.recv.at[base]
            remote(dst, dst, self.ssem.at[slots + j], self.rsem.at[slots + j], self.me.sib).wait_recv()

    def run(self):
        me, recv = self.me, self.recv
        self.hop(self.own.at[0], 0, me.seat, [(j, me.plane_peer(j)) for j in range(1, 8)], -1)
        pairs = [recv[2 * k] + recv[2 * k + 1] for k in range(4)]
        self.own[1] = (pairs[0] + pairs[1]) + (pairs[2] + pairs[3])
        self.hop(self.own.at[1], 8, me.z, [(j, me.zpeer(j)) for j in (1, 2, 3)], 6)
        return (recv[8] + recv[9]) + (recv[10] + recv[11])

    def drain(self):
        for slot in range(10):
            piece = self.recv.at[0]
            remote(piece, piece, self.ssem.at[slot], self.rsem.at[slot], self.me.sib).wait_send()


def squares_scratch(shape):
    return [
        pltpu.VMEM((2,) + shape, F32),
        pltpu.VMEM((12,) + shape, F32),
        pltpu.SemaphoreType.DMA((10,)),
        pltpu.SemaphoreType.DMA((10,)),
    ]


def totals_scratch(shape):
    return [
        pltpu.VMEM((4,) + shape, F32),
        pltpu.VMEM((7,) + shape, F32),
        pltpu.SemaphoreType.DMA((6,)),
        pltpu.SemaphoreType.DMA((6,)),
    ]


def saved_scratch(images):
    return [pltpu.VMEM(a.shape, a.dtype) for a in saved_shapes(images)]


def backward_scratch(images):
    return scratch_forward(images) + [
        pltpu.VMEM((images, POS, C), F32),
        pltpu.VMEM((images, POS, 3 * C), BF16),
        pltpu.VMEM((C, images * POS), BF16),
    ]


GEN_TOTAL = SIGMA_INIT**2 + SIGMA_DATA**2
GEN_IN = GEN_TOTAL**-0.5
GEN_SKIP = SIGMA_DATA**2 / GEN_TOTAL
GEN_OUT = SIGMA_INIT * SIGMA_DATA * GEN_TOTAL**-0.5
T_IN, T_SKIP, T_OUT, T_SIGMA, T_FACTOR = range(5)


def fill_embed(eo, sigmas):
    at = lax.broadcasted_iota(jnp.int32, (8, 4 * C), 1)
    side = lax.broadcasted_iota(jnp.int32, (8, 4 * C), 0) // 4
    k = at // 2
    power = (k & (C - 1)).astype(F32) * (1.0 / C)
    rows = sigmas + [jnp.ones_like(sigmas[0])] * (4 - len(sigmas))
    angle = jnp.log(jnp.concatenate(rows + rows, axis=0)) * 0.25 * jnp.exp(power * -LOG_10000)
    wave = jnp.where(k < C, jnp.cos(angle), jnp.sin(angle))
    eo[...] = jnp.where((at & 1) == side, wave, 0.0).astype(BF16)


LOG_10000 = 9.210340371976184


def step_kernel(*refs):
    (
        z_all, eps_all, levels, counts, gen_w, fake_w, teacher_w, gen_small, fake_small,
        teacher_small,
        gw_out, sv_x, sv_h, sv_y, sv_q, sv_a, sv_o, sv_s, gshard, fshard, stot, sqtot,
        *refs,
    ) = refs
    gen_out = (sv_x, sv_h, sv_y, sv_q, sv_a, sv_o, sv_s)
    w_gen, w_fake, w_teach = refs[:3]
    sv_one, sv_two = refs[3:10], refs[10:17]
    bufs, nbuf, qkvw, tmp, dn, dqkv, act_t = refs[17:24]
    zb, eb, g, stage, local_sem, send_sem, recv_sem, copy_sem = refs[24:32]
    smalls, small_sem, gen_eo, score_eo, tab, sgrads, part_sums = refs[32:39]
    fake_refs, gen_refs = refs[39:44], refs[44:49]
    small_refs, square_refs = refs[49:53], refs[53:57]
    sib, free_sem = refs[57:59]
    g2 = sv_two[0].at[2]
    images = zb.shape[0]
    me = Place()
    start = me.sec * images

    def run(steps):
        for step in steps:
            step()

    def mine(ref):
        return ref.at[pl.ds(start, images)]

    loads = [
        pltpu.make_async_copy(mine(z_all), zb, copy_sem.at[0]),
        pltpu.make_async_copy(mine(eps_all), eb, copy_sem.at[1]),
    ]
    for copy in loads:
        copy.start()
    masters = [
        pltpu.make_async_copy(src, dst, copy_sem.at[2 + k])
        for k, (src, dst) in enumerate(((gen_w, gshard), (fake_w, fshard), (teacher_w, stage.at[2])))
    ]
    for copy in masters:
        copy.start()
    smalls[...] = jnp.zeros(smalls.shape, F32)
    for n, ref in enumerate((gen_small, fake_small, teacher_small)):
        for r in range(13):
            smalls[me.sec, n, r : r + 1, :] = ref[r]
    gathers = [
        Gather(me, net, stage.at[n], local_sem.at[n], send_sem.at[n], recv_sem.at[n])
        for n, net in enumerate((w_gen, w_fake, w_teach))
    ]
    for copy in masters:
        copy.wait()
    stage[0] = gshard[...].astype(BF16)
    stage[1] = fshard[...].astype(BF16)
    me.meet()
    gathers[0].begin()
    swap = remote(
        smalls.at[me.sec], smalls.at[me.sec], small_sem.at[0], small_sem.at[1], me.sib
    )
    swap.start()

    clear_pads(bufs)
    sgrads[...] = jnp.zeros(sgrads.shape, F32)
    sigmas = []
    valid_sum = jnp.zeros((1, 4 * C), F32)
    for i in range(images):
        level = jnp.zeros((1, 4 * C), jnp.int32) + levels[start + i]
        sigma = SIGMA_TOP + level.astype(F32) / (LEVELS - 1) * (SIGMA_BOTTOM - SIGMA_TOP)
        square = sigma * sigma
        sigma = square * square * square * sigma
        sigmas.append(sigma)
        s_in, s_skip, s_out, s_lam = precondition(sigma)
        valid = jnp.where(jnp.zeros_like(level) + (start + i) < counts[0], 1.0, 0.0)
        valid_sum = valid_sum + valid
        rows = (s_in, s_skip, s_out, sigma, valid * s_lam * (1.0 / (POS * C)))
        for k, value in enumerate(rows):
            tab[i, k : k + 1, :] = value[:, :C]
    fill_embed(score_eo, sigmas)
    fill_embed(gen_eo, [jnp.full((1, 4 * C), SIGMA_INIT, F32)] * images)

    def forward(n, w, eo, sv, pump):
        def body(l, _):
            layer_forward(
                l, w, smalls.at[:, n], eo, *sv, bufs, nbuf, qkvw, tmp, True, pump
            )
            return 0

        lax.fori_loop(0, 2, body, 0)

    def backward(n, w, eo, sv, cot, grad, sgrad, pump):
        def body(k, _):
            layer_backward(
                1 - k, w, smalls.at[:, n], eo, *sv, cot, bufs, nbuf, qkvw, tmp, dn, dqkv,
                act_t, grad, sgrad, pump,
            )
            return 0

        lax.fori_loop(0, 2, body, 0)

    def each(f):
        def body(i, carry):
            return f(i, [tab[i, k : k + 1, :] for k in range(5)], carry)

        return lax.fori_loop(0, images, body, jnp.zeros((1, C), F32))

    z_now, z_next = gathers[0].phase1(), gathers[1].phase1()
    run(z_now[:2] + [gathers[1].begin] + z_now[2:] + gathers[0].phase2() + z_next[:1])
    run(z_next[1:2] + gathers[0].phase3())
    for copy in loads:
        copy.wait()
    sv_one[0][0] = zb[...] * (GEN_IN * SIGMA_INIT)
    swap.wait()
    run(gathers[0].finish())
    later = z_next[2:] + gathers[1].phase2()
    forward(0, w_gen, gen_eo, sv_one, Pump(later[:5], FORWARD_POINTS, (0, 1)))
    pairs = [(w_gen, gw_out)] + list(zip(sv_one, gen_out))
    stores = [
        pltpu.make_async_copy(src, dst, copy_sem.at[2 + k]) for k, (src, dst) in enumerate(pairs)
    ]
    for copy in stores:
        copy.start()

    def noisy(i, t, carry):
        zb[i] = zb[i] * (GEN_SKIP * SIGMA_INIT) + GEN_OUT * sv_one[0][2, i]
        eb[i] = zb[i] + t[T_SIGMA] * eb[i]
        sv_two[0][0, i] = t[T_IN] * eb[i]
        return carry

    each(noisy)
    z_next, last = gathers[2].phase1(), gathers[1].phase3()
    run(later[5:] + [gathers[2].begin] + last + z_next[:1])
    run(gathers[1].finish())
    later = z_next[1:] + gathers[2].phase2()
    forward(1, w_fake, score_eo, sv_two, Pump(later[:6], FORWARD_POINTS, (0, 1)))
    later = later[6:] + gathers[2].phase3()

    def fake_loss(i, t, total):
        den = t[T_SKIP] * eb[i] + t[T_OUT] * sv_two[0][2, i]
        sv_two[0][2, i] = den
        miss = den - zb[i]
        g[i] = (2.0 * t[T_OUT] * t[T_FACTOR]) * miss
        return total + t[T_FACTOR] * colsum(miss * miss)

    loss_fake = each(fake_loss)
    for copy in stores:
        copy.wait()
    gathers[0].drain()
    backward(
        1, w_fake, score_eo, sv_two, g, w_gen, sgrads.at[:, 1],
        Pump(later, WEIGHT_POINTS, (1, 0), 0.0, 0.8),
    )
    fake_sum = Reduce(me, w_gen, fshard, sib, sib, *fake_refs)
    fake_sum.begin()
    run(gathers[2].finish())
    later = fake_sum.steps()
    sv_one[0][0] = sv_two[0][0]
    forward(2, w_teach, score_eo, sv_one, no_pump)

    def gen_loss(i, t, total):
        den = t[T_SKIP] * eb[i] + t[T_OUT] * sv_one[0][2, i]
        fake_den = sv_two[0][2, i]
        miss = fake_den - zb[i]
        gap = den - fake_den
        scale = t[T_OUT] * t[T_FACTOR]
        g[i] = scale * ((2.0 * (1.0 - ALPHA_MIX)) * gap + miss)
        g2[i] = scale * ((1.0 - 2.0 * (1.0 - ALPHA_MIX)) * gap - miss)
        zb[i] = (t[T_FACTOR] * (t[T_SKIP] - 1.0)) * gap
        return total + t[T_FACTOR] * colsum(gap * ((1.0 - ALPHA_MIX) * gap + miss))

    loss_gen = each(gen_loss)
    backward(
        2, w_teach, score_eo, sv_one, g, None, None, Pump(later[:4], BACKWARD_POINTS, (1, 0), 0.2)
    )
    gathers[2].drain()
    fake_sum.drain(A_SLOT, B_SLOT)
    pl.semaphore_signal(free_sem, inc=1, device_id=me.sib, device_id_type=MESH)
    back = [
        pltpu.make_async_copy(src, dst, copy_sem.at[2 + k])
        for k, (dst, src) in enumerate([(w_teach, gw_out)] + list(zip(sv_one, gen_out)))
    ]
    for copy in back:
        copy.start()
    backward(
        1, w_fake, score_eo, sv_two, g2, None, None, Pump(later[4:8], BACKWARD_POINTS, (1, 0))
    )

    def gen_gradient(i, t, carry):
        g[i] = GEN_OUT * (zb[i] + t[T_IN] * (g[i] + g2[i]))
        return carry

    each(gen_gradient)
    gathers[1].drain()
    for copy in back:
        copy.wait()

    gen_sum = Reduce(me, w_fake, gshard, w_gen.at[1 - me.sec], w_gen.at[me.sec], *gen_refs)
    fake_steps, later = later, gen_sum.steps()

    def on_section(s, steps):
        pl.when(me.sec == s)(lambda: run(steps))

    def hand_over():
        pl.semaphore_wait(free_sem, 1)

    pump = Pump([], WEIGHT_POINTS, (1, 0))

    def at(layer, point, section, steps):
        pump.table[layer][point].append(lambda: on_section(section, steps))

    upper = [hand_over, lambda: gen_sum.begin_block(0), lambda: gen_sum.begin_block(1)]
    lower = [lambda: gen_sum.begin_block(2), lambda: gen_sum.begin_block(3)]
    for layer, giver in ((1, 0), (0, 1)):
        at(layer, HALF_WAY, giver, upper)
        at(layer, READY, giver, lower)
    for k, point in enumerate((2, 9, 15)):
        pump.table[1][point].append(fake_steps[8 + k])
    pump.table[0][3].append(fake_steps[11])
    for k, point in enumerate((1, 3, 6, 8, 9, 10, 11, 12, 13, 14, 16, 17)):
        at(0, point, 1, later[k : k + 1])
    backward(0, w_teach, gen_eo, sv_one, g, w_fake, sgrads.at[:, 0], pump)

    def spread_sum(total):
        return jnp.broadcast_to(jnp.sum(total, axis=1, keepdims=True), (1, C))

    sums = jnp.concatenate([spread_sum(loss_gen), spread_sum(loss_fake), valid_sum[:, :C]], axis=0)
    for s in range(2):
        part_sums[s, 0:16, :] = sgrads[s, 0]
        part_sums[s, 13:16, :] = sums
        part_sums[s, 16:32, :] = sgrads[s, 1]
    small = Totals(me, *small_refs)
    small_refs[0][0] = part_sums[me.sec]
    small.begin(part_sums.at[1 - me.sec])
    fake_sum.stage_e()
    small_steps = small.steps()
    on_section(0, later[:3])
    run(small_steps[:1])
    on_section(0, later[3:6])
    run(small_steps[1:2])
    on_section(0, later[6:9])
    run(small_steps[2:])
    on_section(0, later[9:])
    stot[...] = small.result()
    own = square_refs[0]
    keep = lax.broadcasted_iota(jnp.int32, (16, C), 0) < 13
    for n, rows in ((1, fshard), (0, gshard)):
        if n == 0:
            gen_sum.stage_e()
        low = jnp.square(jnp.where(keep, stot[16 * n : 16 * n + 16, :], 0.0))
        low = jnp.where(me.d == 0, low[0:8] + low[8:16], 0.0)
        big = jnp.sum(jnp.square(rows[...]).reshape(rows.shape[0] // 8, 8, C), axis=0)
        own[0, 8 * n : 8 * n + 8, :] = big + low
    square = Squares(me, *square_refs)
    sqtot[...] = square.run()
    fake_sum.drain(B_SLOT)
    for done in (gen_sum, small, square):
        done.drain()


SIGMA_TOP = SIGMA_HIGH ** (1.0 / RHO_POWER)
SIGMA_BOTTOM = SIGMA_LOW ** (1.0 / RHO_POWER)


def run_step(z, eps, levels, counts, gen_w, fake_w, teacher_w, smalls):
    part = gen_w.shape[0]
    images = z.shape[0] // 2
    any_ = pl.BlockSpec(memory_space=pl.ANY)
    smem = pl.BlockSpec(memory_space=pltpu.SMEM)
    saved = saved_shapes(images)
    return pl.pallas_call(
        step_kernel,
        out_shape=[jax.ShapeDtypeStruct((2, ROWS, C), BF16)]
        + saved
        + [
            jax.ShapeDtypeStruct((part, C), F32),
            jax.ShapeDtypeStruct((part, C), F32),
            jax.ShapeDtypeStruct((32, C), F32),
            jax.ShapeDtypeStruct((16, C), F32),
        ],
        in_specs=[any_] * 2 + [smem] * 2 + [any_] * 3 + vm(3),
        out_specs=[any_] * 8 + vm(4),
        scratch_shapes=[pltpu.VMEM((2, ROWS, C), BF16)] * 3
        + saved_scratch(images) * 2
        + backward_scratch(images)
        + [pltpu.VMEM((images, POS, C), F32)] * 3
        + [
            pltpu.VMEM((3, part, C), BF16),
            pltpu.SemaphoreType.DMA((3,)),
            pltpu.SemaphoreType.DMA((3, SLOTS)),
            pltpu.SemaphoreType.DMA((3, SLOTS)),
            pltpu.SemaphoreType.DMA((10,)),
            pltpu.VMEM((2, 3, 16, C), F32),
            pltpu.SemaphoreType.DMA((2,)),
            pltpu.VMEM((8, 4 * C), BF16),
            pltpu.VMEM((8, 4 * C), BF16),
            pltpu.VMEM((images, 8, C), F32),
            pltpu.VMEM((2, 2, 16, C), F32),
            pltpu.VMEM((2, 32, C), F32),
        ]
        + reduce_scratch(part) * 2
        + totals_scratch((32, C))
        + squares_scratch((16, C))
        + [pltpu.VMEM((ROWS, C), BF16), pltpu.SemaphoreType.REGULAR],
        compiler_params=pltpu.CompilerParams(
            collective_id=0, has_side_effects=True, vmem_limit_bytes=STEP_LIMIT
        ),
    )(z, eps, levels, counts, gen_w, fake_w, teacher_w, *smalls)[8:]


def adam_step(master, first_mom, second_mom, grad):
    first_new = BETA_ONE * first_mom + (1.0 - BETA_ONE) * grad
    second_new = BETA_TWO * second_mom + (1.0 - BETA_TWO) * grad * grad
    direction = (
        first_new
        / (1.0 - BETA_ONE**STEP)
        / (jnp.sqrt(second_new / (1.0 - BETA_TWO**STEP)) + ADAM_EPS)
    )
    return (master - LEARN_RATE * (direction + WEIGHT_DECAY * master), first_new, second_new)


EMA_RATE = 0.5 ** (20.0 / STEP)
SMALL_STATES = (4, 5, 6, 7, 11, 12, 13)


def update_kernel(gshard, fshard, stot, sqtot, *refs):
    ins, outs = refs[:14], refs[14:]
    norms, losses = outs[14:]
    count = stot[15:16, 0:1]
    norm_of, scales = [], []
    for n in range(2):
        rows = jnp.sum(sqtot[8 * n : 8 * n + 8, :], axis=0, keepdims=True)
        norm = jnp.sqrt(jnp.sum(rows, axis=1, keepdims=True)) / count
        scales.append(jnp.minimum(1.0, CLIP_NORM / norm) / count)
        norm_of.append(norm)

    def one(at, grad, w, m, v, ema, ow, om, ov, oe):
        new, first, second = adam_step(w[at], m[at], v[at], grad)
        ow[at] = new
        om[at] = first
        ov[at] = second
        if ema is not None:
            oe[at] = EMA_RATE * ema[at] + (1.0 - EMA_RATE) * new

    one(0, gshard[...] * scales[0], *ins[0:4], *outs[0:4])
    one(0, fshard[...] * scales[1], *ins[8:11], None, *outs[8:11], None)

    @pl.when(pl.program_id(0) == 0)
    def _():
        for n in range(2):
            norms[n] = norm_of[n][0, 0]
            losses[n] = (stot[13 + n : 14 + n, 0:1] / count)[0, 0]
        for k in range(13):
            one(k, stot[k : k + 1, :] * scales[0], *ins[4:8], *outs[4:8])
            one(k, stot[16 + k : 17 + k, :] * scales[1], *ins[11:14], None, *outs[11:14], None)


def update_nets(gshard, fshard, stot, sqtot, states):
    def turned(arrays):
        return [a.swapaxes(0, 1) if k in SMALL_STATES else a for k, a in enumerate(arrays)]

    part = gshard.shape[0]
    steps = 1
    big = pl.BlockSpec((1, part // steps, C), lambda i: (0, i, 0))
    low = pl.BlockSpec((13, 1, C), lambda i: (0, 0, 0))
    shard = pl.BlockSpec((part // steps, C), lambda i: (i, 0))
    whole = [pl.BlockSpec(a.shape, lambda i: (0, 0)) for a in (stot, sqtot)]
    specs = [low if k in SMALL_STATES else big for k in range(len(states))]
    states = turned(states)
    res = pl.pallas_call(
        update_kernel,
        grid=(steps,),
        out_shape=[jax.ShapeDtypeStruct(a.shape, F32) for a in states]
        + [jax.ShapeDtypeStruct((2,), F32)] * 2,
        in_specs=[shard] * 2 + whole + specs,
        out_specs=specs + [pl.BlockSpec(memory_space=pltpu.SMEM)] * 2,
        compiler_params=pltpu.CompilerParams(vmem_limit_bytes=VMEM_LIMIT),
    )(gshard, fshard, stot, sqtot, *states)
    return tuple(turned(res[:-2])) + tuple(res[-2:])


def gather_plain(shard):
    rows = lax.all_gather(shard.astype(BF16), "dp", axis=1, tiled=True)
    return lax.all_gather(rows, "section", axis=0, tiled=True)


def reduce_plain(bigs, small):
    shards_, squares = [], []
    own = lax.psum_scatter(small, "section", scatter_dimension=0, tiled=True)
    stot = lax.psum(own, "dp")[0]
    first = lax.axis_index("dp") == 0
    for n, big in enumerate(bigs):
        own = lax.psum_scatter(big, "section", scatter_dimension=0, tiled=True)
        own = lax.psum_scatter(own, "dp", scatter_dimension=1, tiled=True)[0].astype(F32)
        shards_.append(own)
        low = jnp.sum(jnp.square(stot[16 * n : 16 * n + 13]))
        squares.append(jnp.sum(own * own) + jnp.where(first, low, 0.0))
    sq = lax.psum(jnp.stack(squares), ("section", "dp"))
    return *shards_, stot, jnp.zeros((16, C), F32).at[jnp.array([0, 8]), 0].set(sq)


def shards(
    z_noise, eps_noise, levels, counts,
    gen_w, gen_m, gen_v, gen_ema, gen_small, gen_small_m, gen_small_v, gen_small_ema,
    fake_w, fake_m, fake_v, fake_small, fake_small_m, fake_small_v,
    teacher_w, teacher_small,
):
    if lax.axis_size("dp") == PLANES * PLANE:
        smalls = [a.swapaxes(0, 1) for a in (gen_small, fake_small, teacher_small)]
        reduced = run_step(
            z_noise, eps_noise, levels, counts, gen_w[0], fake_w[0], teacher_w[0], smalls
        )
    else:
        reduced = plain_step(
            z_noise, eps_noise, levels, counts, gen_w, fake_w, teacher_w,
            gen_small, fake_small, teacher_small,
        )
    return update_nets(
        *reduced,
        (
            gen_w, gen_m, gen_v, gen_ema, gen_small, gen_small_m, gen_small_v, gen_small_ema,
            fake_w, fake_m, fake_v, fake_small, fake_small_m, fake_small_v,
        ),
    )


def plain_step(
    z_noise, eps_noise, levels, counts, gen_w, fake_w, teacher_w,
    gen_small, fake_small, teacher_small,
):
    images = z_noise.shape[0] // lax.axis_size("section")
    start = lax.axis_index("section") * images

    def mine(a):
        return lax.dynamic_slice_in_dim(a, start, images, 0)

    z, eps = mine(z_noise), mine(eps_noise)
    sigma = sigma_levels(mine(levels))
    valid = (start + jnp.arange(images) < counts[0]).astype(F32)
    valid_sum = jnp.sum(valid)
    gen_eo = spread_embed(jnp.full((images,), SIGMA_INIT, F32))
    score_eo = spread_embed(sigma)
    gs, fs, ts = [
        lax.all_gather(a, "section", axis=0, tiled=True)
        for a in (gen_small, fake_small, teacher_small)
    ]
    gw, fw, tw = gather_plain(gen_w), gather_plain(fake_w), gather_plain(teacher_w)
    s_in, s_skip, s_out, s_lam = precondition(sigma)
    factor = valid * s_lam / (POS * C)
    s_in, s_skip, s_out, sigma, factor = [
        t[:, None, None] for t in (s_in, s_skip, s_out, sigma, factor)
    ]
    raw = SIGMA_INIT * z
    gen_saved = run_forward(GEN_IN * raw, gw, gs, gen_eo)
    samples = GEN_SKIP * raw + GEN_OUT * gen_saved[0][2]
    noisy = samples + sigma * eps
    x0 = s_in * noisy
    fake_saved = run_forward(x0, fw, fs, score_eo)
    fake_den = s_skip * noisy + s_out * fake_saved[0][2]
    miss = fake_den - samples
    _, fake_g, fake_sg = run_backward(
        s_out * 2.0 * factor * miss, fw, fs, score_eo, fake_saved, True
    )
    teacher_saved = run_forward(x0, tw, ts, score_eo)
    teacher_den = s_skip * noisy + s_out * teacher_saved[0][2]
    gap = teacher_den - fake_den
    loss_gen = jnp.sum(factor * ((1.0 - ALPHA_MIX) * gap * gap + gap * miss))
    loss_fake = jnp.sum(factor * miss * miss)
    grad_teacher = factor * (2.0 * (1.0 - ALPHA_MIX) * gap + miss)
    grad_fake = factor * gap - grad_teacher
    direct = factor * gap * (s_skip - 1.0)
    (back_t,) = run_backward(s_out * grad_teacher, tw, ts, score_eo, teacher_saved, False)
    (back_f,) = run_backward(s_out * grad_fake, fw, fs, score_eo, fake_saved, False)
    gen_cot = GEN_OUT * (direct + s_in * (back_t + back_f))
    _, gen_g, gen_sg = run_backward(gen_cot, gw, gs, gen_eo, gen_saved, True)
    scalars = jnp.broadcast_to(jnp.stack([loss_gen, loss_fake, valid_sum])[:, None], (3, C))
    small_sums = jnp.concatenate(
        [gen_sg[:, :13], jnp.broadcast_to(scalars, (2, 3, C)), fake_sg], axis=1
    )
    return reduce_plain((gen_g, fake_g), small_sums)


def solution(mesh):
    images = P("dp", None, None)
    big = P("section", "dp", None)
    small = P("section", None, None)
    return jax.shard_map(
        shards,
        mesh=mesh,
        in_specs=(images, images, P("dp"), P("dp"))
        + (big,) * 4 + (small,) * 4 + (big,) * 3 + (small,) * 3 + (big, small),
        out_specs=(big,) * 4 + (small,) * 4 + (big,) * 3 + (small,) * 3 + (P(), P()),
        check_vma=False,
    )
```

```python
import functools

import jax
import jax.numpy as jnp
from jax import lax
from jax.experimental import pallas as pl
from jax.experimental.pallas import tpu as pltpu
from jax.sharding import PartitionSpec as P

GROUPS = 32
SIDE = 16
LEVELS = 1000
STEP = 10

SIGMA_DATA = 0.5
SIGMA_INIT = 2.5
SIGMA_LOW = 0.05
SIGMA_HIGH = 20.0
RHO_POWER = 7.0
ALPHA_MIX = 1.2
RS = 0.7071067811865476
NORM_EPS = 1e-05
CLIP_NORM = 0.001
LEARN_RATE = 0.15
BETA_ONE = 0.9
BETA_TWO = 0.999
ADAM_EPS = 1e-08
WEIGHT_DECAY = 0.01

C = 256
HALF = 128
POS = 256
ROWS = 26 * C
CHUNK = 64
PAD = SIDE
F32 = jnp.float32
BF16 = jnp.bfloat16
VMEM_LIMIT = 58 * 2**20
STEP_LIMIT = 63 * 2**20

R_CONV1, R_CONV2, R_EMB, R_QKV, R_PROJ = 0, 9 * C, 18 * C, 22 * C, 25 * C
S_M1, S_I1, S_M2, S_I2, S_M3, S_I3, S_MA, S_MB = range(8)


def sigma_levels(level_ids):
    fraction = level_ids.astype(F32) / (LEVELS - 1)
    top_root = SIGMA_HIGH ** (1.0 / RHO_POWER)
    bottom_root = SIGMA_LOW ** (1.0 / RHO_POWER)
    return (top_root + fraction * (bottom_root - top_root)) ** RHO_POWER


def precondition(sigma_vals):
    total = sigma_vals * sigma_vals + SIGMA_DATA**2
    return (
        lax.rsqrt(total),
        SIGMA_DATA**2 / total,
        sigma_vals * SIGMA_DATA * lax.rsqrt(total),
        total / (sigma_vals * sigma_vals * SIGMA_DATA**2),
    )


def noise_embed(sigma_vals, channel_count):
    frequency = (1.0 / 10000.0) ** (jnp.arange(channel_count, dtype=F32) / channel_count)
    angles = (jnp.log(sigma_vals) / 4.0)[..., None] * frequency
    return jnp.concatenate([jnp.cos(angles), jnp.sin(angles)], axis=-1)


def spread_embed(sigma_vals):
    emb = noise_embed(sigma_vals, C).astype(BF16)
    images = emb.shape[0]
    zero = jnp.zeros_like(emb)
    low = jnp.stack([emb, zero], axis=-1).reshape(images, 4 * C)
    high = jnp.stack([zero, emb], axis=-1).reshape(images, 4 * C)
    fill = jnp.zeros((4 - images, 4 * C), BF16)
    return jnp.concatenate([low, fill, high, fill], axis=0)


def dot_nn(a, b):
    return lax.dot_general(a, b, (((1,), (0,)), ((), ())), preferred_element_type=F32)


def dot_nt(a, b):
    return lax.dot_general(a, b, (((1,), (1,)), ((), ())), preferred_element_type=F32)


def dot_tn(a, b):
    return lax.dot_general(a, b, (((0,), (0,)), ((), ())), preferred_element_type=F32)


def group_mean(v):
    lane = lax.broadcasted_iota(jnp.int32, (8, C), 1)
    for sh in (1, 2, 4):
        v = v + jnp.where((lane & sh) != 0, pltpu.roll(v, sh, 1), pltpu.roll(v, C - sh, 1))
    return v * (1.0 / (POS * 8))


def colsum(v):
    return jnp.sum(v, axis=0, keepdims=True)


def no_pump(l):
    pass


FORWARD_POINTS, BACKWARD_POINTS, WEIGHT_POINTS = 10, 12, 18
HALF_WAY, READY = 8, 13


def stagger(steps, images, between):
    for t in range(len(steps) + images - 1):
        for i in range(images):
            if 0 <= t - i < len(steps):
                steps[t - i](i)
        between()


class Pump:
    def __init__(self, steps, points, layers, lo=0.0, hi=1.0):
        self.table = {l: [[] for _ in range(points)] for l in layers}
        self.at = 0
        for k, step in enumerate(steps):
            place = int((lo + (hi - lo) * (k + 0.5) / len(steps)) * points * len(layers))
            self.table[layers[place // points]][place % points].append(step)

    def __call__(self, l):
        for layer, points in self.table.items():
            if points[self.at]:

                @pl.when(l == layer)
                def _(todo=points[self.at]):
                    for step in todo:
                        step()

        self.at += 1


def put_shifted(bufs, i, r, v):
    rows = v.shape[0]
    at = pl.ds(PAD + r, rows)
    sub = lax.broadcasted_iota(jnp.int32, (rows // SIDE, 8, C), 1)
    x = v.reshape(rows // SIDE, 2, 8, C)
    low, high = x[:, 0], x[:, 1]
    low_up, high_up = pltpu.roll(low, 1, 1), pltpu.roll(high, 1, 1)
    low_down, high_down = pltpu.roll(low, 7, 1), pltpu.roll(high, 7, 1)
    left = (jnp.where(sub == 0, 0.0, low_up), jnp.where(sub == 0, low_up, high_up))
    right = (jnp.where(sub == 7, high_down, low_down), jnp.where(sub == 7, 0.0, high_down))
    bufs[0, i, at, :] = jnp.stack(left, axis=1).reshape(rows, C).astype(BF16)
    bufs[1, i, at, :] = v.astype(BF16)
    bufs[2, i, at, :] = jnp.stack(right, axis=1).reshape(rows, C).astype(BF16)


def taps(bufs, flip):
    images = bufs.shape[1]
    out = []
    for dr in (-1, 0, 1):
        for dc in (-1, 0, 1):
            sr, sc = (-dr, -dc) if flip else (dr, dc)
            piece = bufs[sc + 1, :, PAD + SIDE * sr : PAD + SIDE * sr + POS, :]
            out.append(piece.reshape(images * POS, C))
    return out


def conv_forward(bufs, w, l, row):
    return dot_nn(jnp.concatenate(taps(bufs, False), axis=1), w[l, row : row + 9 * C, :])


def conv_input_grad(bufs, w, l, row):
    parts = [w[l, row + t * C : row + (t + 1) * C, :] for t in range(9)]
    return dot_nt(jnp.concatenate(taps(bufs, True), axis=1), jnp.concatenate(parts, axis=1))


def conv_weight_grad(act_t, bufs, grad, l, row):
    left = act_t[...]
    for t, piece in enumerate(taps(bufs, True)):
        grad[l, row + t * C : row + (t + 1) * C, :] = dot_nn(left, piece).astype(BF16)


def silu(v):
    h = 0.5 * v
    return h + h * jnp.tanh(h)


def silu_parts(v):
    h = 0.5 * v
    t = jnp.tanh(h)
    return h + h * t, (1.0 + t) + h * (1.0 - t * t)


def clear_pads(bufs):
    zero = jnp.zeros(bufs.shape[:2] + (PAD, C), BF16)
    bufs[:, :, 0:PAD, :] = zero
    bufs[:, :, PAD + POS :, :] = zero


def split_qkv(w, l, qkvw, tmp):
    for h in range(2):
        tmp[h] = w[l, R_QKV : R_QKV + 3 * C, h * HALF : (h + 1) * HALF].astype(F32)
    for j in range(3):
        for h in range(2):
            at = j * C + h * HALF
            qkvw[:, at : at + HALF] = tmp[h, pl.ds(j, C, stride=3), :].astype(BF16)


def norm_sums(x):
    pivot = x[0:1]
    d = x - pivot
    return colsum(d), colsum(d * d), pivot


def norm_stats(sums):
    fill = [jnp.zeros((4 - len(sums), C), F32)]
    s1, s2, pivot = [jnp.concatenate([a[k] for a in sums] + fill, axis=0) for k in range(3)]
    centre = group_mean(jnp.concatenate([pivot, pivot], axis=0) * POS)[0:4]
    off = pivot - centre
    first = s1 + POS * off
    second = s2 + off * (2.0 * s1 + POS * off)
    means = group_mean(jnp.concatenate([first, second], axis=0))
    spread = jnp.maximum(means[4:8] - jnp.square(means[0:4]), 0.0)
    return centre + means[0:4], lax.rsqrt(spread + NORM_EPS)


def norm_map(gain, mg, mc, mean, inv):
    on_value = inv * inv * mc
    return inv * gain, on_value, inv * mg - mean * on_value


def two_means(a, b):
    rows = jnp.concatenate([a, b] * 4, axis=0)
    means = group_mean(rows)
    return means[0:1], means[1:2]


def tap_rows(bufs, flip, which):
    out = []
    for dr in (-1, 0, 1):
        for dc in (-1, 0, 1):
            sr, sc = (-dr, -dc) if flip else (dr, dc)
            at = slice(PAD + SIDE * sr, PAD + SIDE * sr + POS)
            piece = jnp.concatenate([bufs[sc + 1, i, at, :] for i in which], axis=0)
            out.append(piece)
    return out


def layer_forward(l, w, small, eo, xs, h1, y, qkv, att, o, st, bufs, nbuf, qkvw, tmp, staged, pump):
    images = h1.shape[1]
    split_qkv(w, l, qkvw, tmp)
    mod = dot_nn(eo[...], w[l, R_EMB : R_EMB + 4 * C, :])
    ma = mod[0:4] + small[l, 5:6, :]
    mb = mod[4:8] + small[l, 6:7, :]
    for i in range(images):
        st[l, i, S_MA : S_MA + 1, :] = ma[i : i + 1]
        st[l, i, S_MB : S_MB + 1, :] = mb[i : i + 1]

    sums = {}

    def row(k):
        return small[l, k : k + 1, :]

    def keep(which, mean, inv, at):
        for k, i in enumerate(which):
            st[l, i, at : at + 1, :] = mean[k : k + 1]
            st[l, i, at + 1 : at + 2, :] = inv[k : k + 1]

    def first(which):
        mean, inv = norm_stats([norm_sums(xs[l, i]) for i in which])
        keep(which, mean, inv, S_M1)
        for k, i in enumerate(which):
            a = inv[k : k + 1] * row(0)
            b = row(1) - mean[k : k + 1] * a
            for r in range(0, POS, CHUNK):
                v = xs[l, i, r : r + CHUNK, :] * a + b
                put_shifted(bufs, i, r, silu(v))

    def conv(which, at):
        left = jnp.concatenate(tap_rows(bufs, False, which), axis=1)
        return dot_nn(left, w[l, at : at + 9 * C, :])

    def conv_one(which):
        out = conv(which, R_CONV1)
        for k, i in enumerate(which):
            own = out[k * POS : (k + 1) * POS]
            own = own + row(2)
            sums[i] = norm_sums(own)
            h1[l, i] = own

    def second(which):
        mean, inv = norm_stats([sums[i] for i in which])
        keep(which, mean, inv, S_M2)
        for k, i in enumerate(which):
            gain = 1.0 + ma[i : i + 1]
            a = inv[k : k + 1] * row(3) * gain
            b = row(4) * gain + mb[i : i + 1] - mean[k : k + 1] * a
            for r in range(0, POS, CHUNK):
                v = h1[l, i, r : r + CHUNK, :] * a + b
                put_shifted(bufs, i, r, silu(v))

    def conv_two(which):
        out = conv(which, R_CONV2) + row(7)
        for k, i in enumerate(which):
            own = (xs[l, i] + out[k * POS : (k + 1) * POS]) * RS
            sums[i] = norm_sums(own)
            y[l, i] = own

    def third(which):
        mean, inv = norm_stats([sums[i] for i in which])
        keep(which, mean, inv, S_M3)
        for k, i in enumerate(which):
            a = inv[k : k + 1] * row(8)
            b = row(9) - mean[k : k + 1] * a
            for r in range(0, POS, CHUNK):
                v = y[l, i, r : r + CHUNK, :] * a + b
                nbuf[i, r : r + CHUNK, :] = v.astype(BF16)

    def project_in(which):
        n = jnp.concatenate([nbuf[i] for i in which], axis=0)
        for j, at in ((0, 10), (1, None), (2, 11)):
            part = dot_nn(n, qkvw[:, j * C : (j + 1) * C])
            if at is not None:
                part = part + row(at)
            part = part.astype(BF16)
            for k, i in enumerate(which):
                qkv[l, i, :, j * C : (j + 1) * C] = part[k * POS : (k + 1) * POS]

    def attend(which):
        scores = [dot_nt(qkv[l, i, :, 0:C], qkv[l, i, :, C : 2 * C]) for i in which]
        for s, i in zip(scores, which):
            e = jnp.exp((s - jnp.max(s, axis=1, keepdims=True)) * (C**-0.5))
            p = (e * (1.0 / jnp.sum(e, axis=1, keepdims=True))).astype(BF16)
            att[l, i] = p
            o[l, i] = dot_nn(p, qkv[l, i, :, 2 * C :]).astype(BF16)

    def project_out(which):
        left = jnp.concatenate([o[l, i] for i in which], axis=0)
        out = dot_nn(left, w[l, R_PROJ:, :]) + row(12)
        for k, i in enumerate(which):
            xs[l + 1, i] = (y[l, i] + out[k * POS : (k + 1) * POS]) * RS

    steps = (first, conv_one, second, conv_two, third, project_in, attend, project_out)
    if not staged:
        for step in steps:
            step(range(images))
            pump(l)
    else:
        stagger([lambda i, step=step: step([i]) for step in steps], images, lambda: pump(l))


def layer_backward(
    l, w, small, eo, xs, h1, y, qkv, att, o, st, g, bufs, nbuf, qkvw, tmp, dn, dqkv, act_t,
    grad, sgrad, pump, need_dx=None,
):
    want = grad is not None
    images = h1.shape[1]
    which = range(images)
    flat = images * POS
    scale = C**-0.5
    split_qkv(w, l, qkvw, tmp)

    def row(k):
        return small[l, k : k + 1, :]

    def rows8(rows):
        return jnp.concatenate(list(rows) + [jnp.zeros((8 - len(rows), C), F32)], axis=0)

    zero = jnp.zeros((1, C), F32)
    gps, c1, c2, p1, p2 = {}, {}, {}, {}, {}
    total = {7: zero, 2: zero}
    gains = [1.0 + st[l, i, S_MA : S_MA + 1, :] for i in which]

    def project_out(i):
        gps[i] = (g[i] * RS).astype(BF16)
        nbuf[i] = dot_nt(gps[i], w[l, R_PROJ:, :]).astype(BF16)

    def attend(i):
        p = att[l, i]
        pf = p.astype(F32)
        dp = dot_nt(nbuf[i], qkv[l, i, :, 2 * C :])
        ds = (pf * (dp - jnp.sum(dp * pf, axis=1, keepdims=True))).astype(BF16)
        dqkv[i, :, 0:C] = (dot_nn(ds, qkv[l, i, :, C : 2 * C]) * scale).astype(BF16)
        dqkv[i, :, C : 2 * C] = (dot_tn(ds, qkv[l, i, :, 0:C]) * scale).astype(BF16)
        dqkv[i, :, 2 * C :] = dot_tn(p, nbuf[i]).astype(BF16)

    def project_in(i):
        mean, inv = st[l, i, S_M3 : S_M3 + 1, :], st[l, i, S_I3 : S_I3 + 1, :]
        d = dot_nt(dqkv[i], qkvw[...])
        dn[i] = d
        c1[i] = colsum(d)
        c2[i] = colsum(d * (y[l, i] - mean)) * inv

    def third(i):
        mean, inv = st[l, i, S_M3 : S_M3 + 1, :], st[l, i, S_I3 : S_I3 + 1, :]
        mg, mc = two_means(row(8) * c1[i], row(8) * c2[i])
        on_grad, on_value, offset = norm_map(row(8) * RS, mg * RS, mc * RS, mean, inv)
        act_a = inv * row(8)
        act_b = row(9) - mean * act_a
        for r in range(0, POS, CHUNK):
            value = y[l, i, r : r + CHUNK, :]
            gm = g[i, r : r + CHUNK, :] * (RS * RS) + dn[i, r : r + CHUNK, :] * on_grad
            gm = gm - (value * on_value + offset)
            g[i, r : r + CHUNK, :] = gm
            put_shifted(bufs, i, r, gm)
            if want:
                nbuf[i, r : r + CHUNK, :] = (value * act_a + act_b).astype(BF16)
                total[7] = total[7] + colsum(gm)

    def conv_grad(i, at):
        left = jnp.concatenate(tap_rows(bufs, True, [i]), axis=1)
        parts = [w[l, at + t * C : at + (t + 1) * C, :] for t in range(9)]
        dn[i] = dot_nt(left, jnp.concatenate(parts, axis=1))

    def activation(i, src, mean, inv, a, b, act=None):
        s1, s2 = zero, zero
        for r in range(0, POS, CHUNK):
            u = src[l, i, r : r + CHUNK, :] - mean
            act_value, slope = silu_parts(u * (inv * a) + b)
            d = dn[i, r : r + CHUNK, :] * slope
            dn[i, r : r + CHUNK, :] = d
            s1 = s1 + colsum(d)
            s2 = s2 + colsum(d * u)
            if act is not None:
                act[i, r : r + CHUNK, :] = act_value.astype(BF16)
        p1[i], p2[i] = s1 * 0.5, s2 * (0.5 * inv)

    def second_a(i):
        mean, inv = st[l, i, S_M2 : S_M2 + 1, :], st[l, i, S_I2 : S_I2 + 1, :]
        b = row(4) * gains[i] + st[l, i, S_MB : S_MB + 1, :]
        activation(i, h1, mean, inv, row(3) * gains[i], b, nbuf if want else None)

    def second_b(i):
        mean, inv = st[l, i, S_M2 : S_M2 + 1, :], st[l, i, S_I2 : S_I2 + 1, :]
        full = row(3) * gains[i]
        mg, mc = two_means(full * p1[i], full * p2[i])
        on_grad, on_value, offset = norm_map(full, mg, mc, mean, inv)
        for r in range(0, POS, CHUNK):
            dh = dn[i, r : r + CHUNK, :] * (0.5 * on_grad) - (
                h1[l, i, r : r + CHUNK, :] * on_value + offset
            )
            put_shifted(bufs, i, r, dh)
            if want:
                total[2] = total[2] + colsum(dh)

    def first_a(i):
        mean, inv = st[l, i, S_M1 : S_M1 + 1, :], st[l, i, S_I1 : S_I1 + 1, :]
        activation(i, xs, mean, inv, row(0), row(1))

    def first_act(i):
        mean, inv = st[l, i, S_M1 : S_M1 + 1, :], st[l, i, S_I1 : S_I1 + 1, :]
        a = inv * row(0)
        b = row(1) - mean * a
        for r in range(0, POS, CHUNK):
            v = xs[l, i, r : r + CHUNK, :] * a + b
            nbuf[i, r : r + CHUNK, :] = silu(v).astype(BF16)

    def first_b(i):
        mean, inv = st[l, i, S_M1 : S_M1 + 1, :], st[l, i, S_I1 : S_I1 + 1, :]
        mg, mc = two_means(row(0) * p1[i], row(0) * p2[i])
        on_grad, on_value, offset = norm_map(row(0), mg, mc, mean, inv)
        for r in range(0, POS, CHUNK):
            dx = dn[i, r : r + CHUNK, :] * (0.5 * on_grad) - (
                xs[l, i, r : r + CHUNK, :] * on_value + offset
            )
            g[i, r : r + CHUNK, :] = g[i, r : r + CHUNK, :] + dx

    upper = [project_out, attend, project_in, third, lambda i: conv_grad(i, R_CONV2)]
    lower = [lambda i: conv_grad(i, R_CONV1), first_a]
    if not want:
        stagger(upper + [second_a, second_b] + lower + [first_b], images, lambda: pump(l))
        return
    stagger(upper, images, lambda: pump(l))
    gp = jnp.concatenate([gps[i] for i in which], axis=0)
    grad[l, R_PROJ:, :] = dot_tn(o[l].reshape(flat, C), gp).astype(BF16)
    sgrad[l, 12:13, :] = colsum(gp.astype(F32))
    sgrad[l, 7:8, :] = total[7]
    sgrad[l, 8:9, :] = colsum(rows8([c2[i] for i in which]))
    sgrad[l, 9:10, :] = colsum(rows8([c1[i] for i in which]))
    act_t[...] = nbuf[...].reshape(flat, C).T
    for j in range(3):
        dj = dqkv[:, :, j * C : (j + 1) * C].reshape(flat, C)
        part = dot_nn(act_t[...], dj)
        for h in range(2):
            tmp[h, pl.ds(j, C, stride=3), :] = part[:, h * HALF : (h + 1) * HALF]
        if j != 1:
            sgrad[l, 10 + j // 2 : 11 + j // 2, :] = colsum(dj.astype(F32))
    for h in range(2):
        grad[l, R_QKV : R_QKV + 3 * C, h * HALF : (h + 1) * HALF] = tmp[h].astype(BF16)
    for i in which:
        second_a(i)
    pump(l)
    act_t[...] = nbuf[...].reshape(flat, C).T
    conv_weight_grad(act_t, bufs, grad, l, R_CONV2)
    p18, p28, modgain = [rows8([a[i] for i in which]) for a in (p1, p2, gains)]
    dma = row(3) * p28 + row(4) * p18
    sgrad[l, 3:4, :] = colsum(modgain * p28)
    sgrad[l, 4:5, :] = colsum(modgain * p18)
    sgrad[l, 5:6, :] = colsum(dma)
    sgrad[l, 6:7, :] = colsum(p18)
    grad[l, R_EMB : R_EMB + 4 * C, :] = embed_grad(
        eo, jnp.concatenate([dma[0:4], p18[0:4]], axis=0)
    ).astype(BF16)
    pump(l)
    stagger([second_b, first_act], images, lambda: pump(l))
    act_t[...] = nbuf[...].reshape(flat, C).T
    conv_weight_grad(act_t, bufs, grad, l, R_CONV1)
    pump(l)
    stagger(lower, images, lambda: pump(l))
    sgrad[l, 2:3, :] = total[2]
    sgrad[l, 0:1, :] = colsum(rows8([p2[i] for i in which]))
    sgrad[l, 1:2, :] = colsum(rows8([p1[i] for i in which]))

    @pl.when(l == 1)
    def _():
        for i in which:
            first_b(i)


def embed_grad(eo, dm):
    parts, rest = [], dm
    for _ in range(3):
        parts.append(rest.astype(BF16))
        rest = rest - parts[-1].astype(F32)
    left = eo[...]
    return dot_tn(jnp.concatenate([left, left], axis=0), jnp.concatenate(parts[:2], axis=0)) + dot_tn(
        left, parts[2]
    )


def saved_shapes(images):
    return [
        jax.ShapeDtypeStruct((3, images, POS, C), F32),
        jax.ShapeDtypeStruct((2, images, POS, C), F32),
        jax.ShapeDtypeStruct((2, images, POS, C), F32),
        jax.ShapeDtypeStruct((2, images, POS, 3 * C), BF16),
        jax.ShapeDtypeStruct((2, images, POS, POS), BF16),
        jax.ShapeDtypeStruct((2, images, POS, C), BF16),
        jax.ShapeDtypeStruct((2, images, 8, C), F32),
    ]


def forward_kernel(staged, x0, w, small, eo, xs, h1, y, qkv, att, o, st, bufs, nbuf, qkvw, tmp):
    clear_pads(bufs)
    xs[0] = x0[...]

    def body(l, _):
        layer_forward(
            l, w, small, eo, xs, h1, y, qkv, att, o, st, bufs, nbuf, qkvw, tmp, staged, no_pump
        )
        return 0

    lax.fori_loop(0, 2, body, 0)


def backward_kernel(want, *refs):
    cot, w, small, eo, xs, h1, y, qkv, att, o, st, g = refs[:12]
    refs = refs[12:]
    if want:
        grad, sgrad = refs[:2]
        refs = refs[2:]
    else:
        grad, sgrad = None, None
    bufs, nbuf, qkvw, tmp, dn, dqkv, act_t = refs
    clear_pads(bufs)
    g[...] = cot[...]
    if want:
        sgrad[...] = jnp.zeros(sgrad.shape, F32)

    def body(k, _):
        layer_backward(
            1 - k, w, small, eo, xs, h1, y, qkv, att, o, st, g, bufs, nbuf, qkvw, tmp, dn,
            dqkv, act_t, grad, sgrad, no_pump,
        )
        return 0

    lax.fori_loop(0, 2, body, 0)


def vm(n):
    return [pl.BlockSpec(memory_space=pltpu.VMEM)] * n


def scratch_forward(images):
    return [
        pltpu.VMEM((3, images, POS + 2 * PAD, C), BF16),
        pltpu.VMEM((images, POS, C), BF16),
        pltpu.VMEM((C, 3 * C), BF16),
        pltpu.VMEM((2, 3 * C, HALF), F32),
    ]


def run_forward(x0, w, small, eo, staged=False):
    images = x0.shape[0]
    return pl.pallas_call(
        functools.partial(forward_kernel, staged),
        out_shape=saved_shapes(images),
        in_specs=vm(4),
        out_specs=vm(7),
        scratch_shapes=scratch_forward(images),
        compiler_params=pltpu.CompilerParams(vmem_limit_bytes=VMEM_LIMIT),
    )(x0, w, small, eo)


def run_backward(cot, w, small, eo, saved, want):
    images = cot.shape[0]
    outs = [jax.ShapeDtypeStruct(cot.shape, F32)]
    if want:
        outs += [
            jax.ShapeDtypeStruct((2, ROWS, C), BF16),
            jax.ShapeDtypeStruct((2, 16, C), F32),
        ]
    return pl.pallas_call(
        functools.partial(backward_kernel, want),
        out_shape=outs,
        in_specs=vm(11),
        out_specs=vm(len(outs)),
        scratch_shapes=scratch_forward(images)
        + [
            pltpu.VMEM((images, POS, C), F32),
            pltpu.VMEM((images, POS, 3 * C), BF16),
            pltpu.VMEM((C, images * POS), BF16),
        ],
        compiler_params=pltpu.CompilerParams(vmem_limit_bytes=VMEM_LIMIT),
    )(cot, w, small, eo, *saved)


PLANES, PLANE = 4, 4
MESH = pl.DeviceIdType.MESH


class Place:
    def __init__(self):
        self.sec = lax.axis_index("section")
        self.d = lax.axis_index("dp")
        self.x = lax.rem(self.d, 2)
        self.y = lax.rem(self.d // 2, 2)
        self.z = self.d // PLANE
        self.seat = self.sec * PLANE + lax.rem(self.d, PLANE)
        self.sib = {"section": 1 - self.sec}
        self.xn = {"dp": self.d + 1 - 2 * self.x}
        self.yn = {"dp": self.d + 2 - 4 * self.y}

    def plane(self, j):
        return lax.rem(self.z + j + PLANES, PLANES)

    def zpeer(self, j):
        return {"dp": self.plane(j) * PLANE + lax.rem(self.d, PLANE)}

    def plane_peer(self, j):
        seat = lax.rem(self.seat + j, 2 * PLANE)
        return {"section": seat // PLANE, "dp": self.z * PLANE + lax.rem(seat, PLANE)}

    def meet(self):
        barrier = pltpu.get_barrier_semaphore()
        others = [self.plane_peer(j) for j in range(1, 8)] + [self.zpeer(j) for j in (1, 2, 3)]
        for other in others:
            pl.semaphore_signal(barrier, inc=1, device_id=other, device_id_type=MESH)
        pl.semaphore_wait(barrier, len(others))


def remote(src, dst, send, recv, target):
    return pltpu.make_async_remote_copy(
        src_ref=src, dst_ref=dst, send_sem=send, recv_sem=recv,
        device_id=target, device_id_type=MESH,
    )


Z1, X1, Y1, X2, Y2, S_OWN, S_X, S_Y, S_DA, S_DB = 0, 3, 7, 11, 15, 19, 23, 27, 31, 35
SLOTS = 39


class Gather:
    def __init__(self, me, net, stage, local_sem, send_sem, recv_sem):
        self.me, self.net, self.stage = me, net, stage
        self.local_sem, self.send_sem, self.recv_sem = local_sem, send_sem, recv_sem
        self.part = stage.shape[0]
        self.half = self.part // 2

    def rows(self, plane, y, x, lo, count):
        at = (plane * PLANE + y * 2 + x) * self.part + lo
        return self.net.at[self.me.sec, pl.ds(pl.multiple_of(at, 16), count)]

    def own(self, j):
        return self.rows(self.me.plane(-j), self.me.y, self.me.x, 0, self.part)

    def send(self, slot, piece, target, src=None):
        src = piece if src is None else src
        remote(src, piece, self.send_sem.at[slot], self.recv_sem.at[slot], target).start()

    def arrived(self, slot, piece):
        remote(
            piece, piece, self.send_sem.at[slot], self.recv_sem.at[slot], self.me.sib
        ).wait_recv()

    def local(self):
        return pltpu.make_async_copy(self.stage, self.own(0), self.local_sem)

    def begin(self):
        me = self.me
        for j in (1, 2, 3):
            self.send(Z1 + j - 1, self.own(0), me.zpeer(j), self.stage)
        for slot, target in ((X1, me.xn), (Y1, me.yn), (S_OWN, me.sib)):
            self.send(slot, self.own(0), target, self.stage)
        self.local().start()

    def phase1(self):
        def step(j):
            me = self.me
            self.arrived(Z1 + j - 1, self.own(j))
            for slot, target in ((X1, me.xn), (Y1, me.yn), (S_OWN, me.sib)):
                self.send(slot + j, self.own(j), target)

        return [lambda j=j: step(j) for j in (1, 2, 3)]

    def phase2(self):
        me, part, half = self.me, self.part, self.half

        def step_x(j):
            plane = me.plane(-j)
            self.arrived(X1 + j, self.rows(plane, me.y, 1 - me.x, 0, part))
            self.send(Y2 + j, self.rows(plane, me.y, 1 - me.x, 0, half), me.yn)
            self.send(S_X + j, self.rows(plane, me.y, 1 - me.x, 0, part), me.sib)

        def step_y(j):
            plane = me.plane(-j)
            self.arrived(Y1 + j, self.rows(plane, 1 - me.y, me.x, 0, part))
            self.send(X2 + j, self.rows(plane, 1 - me.y, me.x, half, half), me.xn)
            self.send(S_Y + j, self.rows(plane, 1 - me.y, me.x, 0, part), me.sib)

        return [lambda f=f, j=j: f(j) for j in range(PLANES) for f in (step_x, step_y)]

    def phase3(self):
        def step(j, slot, to, lo):
            me = self.me
            where = self.rows(me.plane(-j), 1 - me.y, 1 - me.x, lo, self.half)
            self.arrived(slot + j, where)
            self.send(to + j, where, me.sib)

        return [
            lambda j=j, a=a: step(j, *a)
            for j in range(PLANES)
            for a in ((Y2, S_DA, 0), (X2, S_DB, self.half))
        ]

    def finish(self):
        def step():
            for slot in range(S_OWN, SLOTS):
                count = self.part if slot < S_DA else self.half
                self.arrived(slot, self.rows(0, 0, 0, 0, count))
            self.local().wait()

        return [step]

    def drain(self):
        for slot in range(SLOTS):
            whole = slot < X2 or S_OWN <= slot < S_DA
            piece = self.rows(0, 0, 0, 0, self.part if whole else self.half)
            remote(
                piece, piece, self.send_sem.at[slot], self.recv_sem.at[slot], self.me.sib
            ).wait_send()


A_SLOT, B_SLOT, C_SLOT, D_SLOT = 0, 4, 20, 28
R_SLOTS = 31


class Reduce:
    def __init__(self, me, big, shard, sib, there, rb, rc, rd, ssem, rsem):
        self.me, self.big, self.shard = me, big, shard
        self.sib, self.there, self.rb, self.rc, self.rd = sib, there, rb, rc, rd
        self.ssem, self.rsem = ssem, rsem
        self.part = shard.shape[0]
        self.half = self.part // 2
        self.span = PLANE * self.part

    def zt(self, k):
        return (3, 2, 0, 1)[k]

    def block(self, k):
        return pl.ds(self.zt(k) * self.span, self.span)

    def piece(self, k, y, x, lo, count):
        at = (self.zt(k) * PLANE + y * 2 + x) * self.part + lo
        return pl.ds(pl.multiple_of(at, 16), count)

    def send(self, src, dst, slot, target):
        remote(src, dst, self.ssem.at[slot], self.rsem.at[slot], target).start()

    def arrived(self, dst, slot):
        remote(dst, dst, self.ssem.at[slot], self.rsem.at[slot], self.me.sib).wait_recv()

    def begin(self):
        for k in range(PLANES):
            self.begin_block(k)

    def begin_block(self, k):
        at = self.block(k)
        self.send(self.big.at[1 - self.me.sec, at], self.there.at[at], A_SLOT + k, self.me.sib)

    def stage_a(self, k):
        me, half = self.me, self.half
        self.arrived(self.sib.at[self.block(k)], A_SLOT + k)
        base = self.zt(k) * self.span

        def body(i, _):
            at = pl.ds(pl.multiple_of(base + i * half, 16), half)
            self.big[me.sec, at, :] = (
                self.big[me.sec, at, :].astype(F32) + self.sib[at, :].astype(F32)
            ).astype(BF16)
            return 0

        lax.fori_loop(0, 2 * PLANE, body, 0)
        for j in range(2):
            self.send(
                self.big.at[me.sec, self.piece(k, 1 - me.y, j, 0, half)], self.rb.at[k, j],
                B_SLOT + 4 * k + j, me.yn,
            )
            self.send(
                self.big.at[me.sec, self.piece(k, j, 1 - me.x, half, half)], self.rb.at[k, 2 + j],
                B_SLOT + 4 * k + 2 + j, me.xn,
            )

    def join(self, where, other):
        self.big[self.me.sec, where, :] = (
            self.big[self.me.sec, where, :].astype(F32) + other.astype(F32)
        ).astype(BF16)

    def stage_c(self, k):
        me, half = self.me, self.half
        for j in range(4):
            self.arrived(self.rb.at[k, j], B_SLOT + 4 * k + j)
            y, x, lo = (me.y, j, 0) if j < 2 else (j - 2, me.x, half)
            self.join(self.piece(k, y, x, lo, half), self.rb[k, j])
        self.send(
            self.big.at[me.sec, self.piece(k, me.y, 1 - me.x, 0, half)], self.rc.at[k, 0],
            C_SLOT + 2 * k, me.xn,
        )
        self.send(
            self.big.at[me.sec, self.piece(k, 1 - me.y, me.x, half, half)], self.rc.at[k, 1],
            C_SLOT + 2 * k + 1, me.yn,
        )

    def stage_d(self, k):
        me, half, zt = self.me, self.half, self.zt(k)
        for j in range(2):
            self.arrived(self.rc.at[k, j], C_SLOT + 2 * k + j)
            self.join(self.piece(k, me.y, me.x, j * half, half), self.rc[k, j])

        @pl.when(me.z != zt)
        def _():
            self.send(
                self.big.at[me.sec, self.piece(k, me.y, me.x, 0, self.part)],
                self.rd.at[lax.rem(zt - me.z + PLANES, PLANES) - 1],
                D_SLOT + lax.rem(zt - me.z + PLANES, PLANES) - 1,
                {"dp": zt * PLANE + lax.rem(me.d, PLANE)},
            )

    def stage_e(self):
        for j in range(PLANES - 1):
            self.arrived(self.rd.at[j], D_SLOT + j)
        at = pl.ds(pl.multiple_of(self.me.d * self.part, 16), self.part)
        self.shard[...] = (
            self.big[self.me.sec, at, :].astype(F32)
            + self.rd[0].astype(F32) + (self.rd[1].astype(F32) + self.rd[2].astype(F32))
        )

    def steps(self):
        out = []
        for t in range(PLANES + 2):
            for stage, lag in ((self.stage_a, 0), (self.stage_c, 1), (self.stage_d, 2)):
                if 0 <= t - lag < PLANES:
                    out.append(lambda stage=stage, k=t - lag: stage(k))
        return out

    def drain(self, lo=0, hi=R_SLOTS):
        for slot in range(lo, hi):
            if slot < B_SLOT:
                piece = self.there.at[pl.ds(0, self.span)]
            elif slot < D_SLOT:
                piece = self.rb.at[0, 0]
            else:
                piece = self.rd.at[0]
            remote(piece, piece, self.ssem.at[slot], self.rsem.at[slot], self.me.sib).wait_send()


def reduce_scratch(part):
    half = part // 2
    return [
        pltpu.VMEM((PLANES, 4, half, C), BF16),
        pltpu.VMEM((PLANES, 2, half, C), BF16),
        pltpu.VMEM((PLANES - 1, part, C), BF16),
        pltpu.SemaphoreType.DMA((R_SLOTS,)),
        pltpu.SemaphoreType.DMA((R_SLOTS,)),
    ]


class Totals:
    def __init__(self, me, buf, recv, ssem, rsem):
        self.me, self.buf, self.recv, self.ssem, self.rsem = me, buf, recv, ssem, rsem

    def send(self, src, dst, slot, target):
        remote(src, dst, self.ssem.at[slot], self.rsem.at[slot], target).start()

    def arrived(self, dst, slot):
        remote(dst, dst, self.ssem.at[slot], self.rsem.at[slot], self.me.sib).wait_recv()

    def begin(self, first):
        self.send(first, self.recv.at[0], 0, self.me.sib)

    def steps(self):
        me, buf, recv = self.me, self.buf, self.recv

        def one():
            self.arrived(recv.at[0], 0)
            buf[1] = buf[0] + recv[0]
            self.send(buf.at[1], recv.at[1], 1, me.xn)

        def two():
            self.arrived(recv.at[1], 1)
            buf[2] = buf[1] + recv[1]
            self.send(buf.at[2], recv.at[2], 2, me.yn)

        def three():
            self.arrived(recv.at[2], 2)
            buf[3] = buf[2] + recv[2]
            recv[3 + me.z] = buf[3]
            for j in (1, 2, 3):
                self.send(buf.at[3], recv.at[3 + me.z], 2 + j, me.zpeer(j))

        return [one, two, three]

    def result(self):
        for j in (1, 2, 3):
            self.arrived(self.recv.at[3 + self.me.plane(-j)], 2 + j)
        return (self.recv[3] + self.recv[4]) + (self.recv[5] + self.recv[6])

    def drain(self):
        for slot in range(6):
            piece = self.recv.at[0]
            remote(piece, piece, self.ssem.at[slot], self.rsem.at[slot], self.me.sib).wait_send()


class Squares:
    def __init__(self, me, own, recv, ssem, rsem):
        self.me, self.own, self.recv, self.ssem, self.rsem = me, own, recv, ssem, rsem

    def hop(self, src, base, mine, peers, slots):
        for j, target in peers:
            dst = self.recv.at[base + mine]
            remote(src, dst, self.ssem.at[slots + j], self.rsem.at[slots + j], target).start()
        self.recv[base + mine] = src[...]
        for j, _ in peers:
            dst = self.recv.at[base]
            remote(dst, dst, self.ssem.at[slots + j], self.rsem.at[slots + j], self.me.sib).wait_recv()

    def run(self):
        me, recv = self.me, self.recv
        self.hop(self.own.at[0], 0, me.seat, [(j, me.plane_peer(j)) for j in range(1, 8)], -1)
        pairs = [recv[2 * k] + recv[2 * k + 1] for k in range(4)]
        self.own[1] = (pairs[0] + pairs[1]) + (pairs[2] + pairs[3])
        self.hop(self.own.at[1], 8, me.z, [(j, me.zpeer(j)) for j in (1, 2, 3)], 6)
        return (recv[8] + recv[9]) + (recv[10] + recv[11])

    def drain(self):
        for slot in range(10):
            piece = self.recv.at[0]
            remote(piece, piece, self.ssem.at[slot], self.rsem.at[slot], self.me.sib).wait_send()


def squares_scratch(shape):
    return [
        pltpu.VMEM((2,) + shape, F32),
        pltpu.VMEM((12,) + shape, F32),
        pltpu.SemaphoreType.DMA((10,)),
        pltpu.SemaphoreType.DMA((10,)),
    ]


def totals_scratch(shape):
    return [
        pltpu.VMEM((4,) + shape, F32),
        pltpu.VMEM((7,) + shape, F32),
        pltpu.SemaphoreType.DMA((6,)),
        pltpu.SemaphoreType.DMA((6,)),
    ]


def saved_scratch(images):
    return [pltpu.VMEM(a.shape, a.dtype) for a in saved_shapes(images)]


def backward_scratch(images):
    return scratch_forward(images) + [
        pltpu.VMEM((images, POS, C), F32),
        pltpu.VMEM((images, POS, 3 * C), BF16),
        pltpu.VMEM((C, images * POS), BF16),
    ]


GEN_TOTAL = SIGMA_INIT**2 + SIGMA_DATA**2
GEN_IN = GEN_TOTAL**-0.5
GEN_SKIP = SIGMA_DATA**2 / GEN_TOTAL
GEN_OUT = SIGMA_INIT * SIGMA_DATA * GEN_TOTAL**-0.5
T_IN, T_SKIP, T_OUT, T_SIGMA, T_FACTOR = range(5)


def fill_embed(eo, sigmas):
    at = lax.broadcasted_iota(jnp.int32, (8, 4 * C), 1)
    side = lax.broadcasted_iota(jnp.int32, (8, 4 * C), 0) // 4
    k = at // 2
    power = (k & (C - 1)).astype(F32) * (1.0 / C)
    rows = sigmas + [jnp.ones_like(sigmas[0])] * (4 - len(sigmas))
    angle = jnp.log(jnp.concatenate(rows + rows, axis=0)) * 0.25 * jnp.exp(power * -LOG_10000)
    wave = jnp.where(k < C, jnp.cos(angle), jnp.sin(angle))
    eo[...] = jnp.where((at & 1) == side, wave, 0.0).astype(BF16)


LOG_10000 = 9.210340371976184


def step_kernel(*refs):
    (
        z_all, eps_all, levels, counts, gen_w, fake_w, teacher_w, gen_small, fake_small,
        teacher_small,
        gw_out, sv_x, sv_h, sv_y, sv_q, sv_a, sv_o, sv_s, gshard, fshard, stot, sqtot,
        *refs,
    ) = refs
    gen_out = (sv_x, sv_h, sv_y, sv_q, sv_a, sv_o, sv_s)
    w_gen, w_fake, w_teach = refs[:3]
    sv_one, sv_two = refs[3:10], refs[10:17]
    bufs, nbuf, qkvw, tmp, dn, dqkv, act_t = refs[17:24]
    zb, eb, g, stage, local_sem, send_sem, recv_sem, copy_sem = refs[24:32]
    smalls, small_sem, gen_eo, score_eo, tab, sgrads, part_sums = refs[32:39]
    fake_refs, gen_refs = refs[39:44], refs[44:49]
    small_refs, square_refs = refs[49:53], refs[53:57]
    sib, free_sem = refs[57:59]
    g2 = sv_two[0].at[2]
    images = zb.shape[0]
    me = Place()
    start = me.sec * images

    def run(steps):
        for step in steps:
            step()

    def mine(ref):
        return ref.at[pl.ds(start, images)]

    loads = [
        pltpu.make_async_copy(mine(z_all), zb, copy_sem.at[0]),
        pltpu.make_async_copy(mine(eps_all), eb, copy_sem.at[1]),
    ]
    for copy in loads:
        copy.start()
    masters = [
        pltpu.make_async_copy(src, dst, copy_sem.at[2 + k])
        for k, (src, dst) in enumerate(((gen_w, gshard), (fake_w, fshard), (teacher_w, stage.at[2])))
    ]
    for copy in masters:
        copy.start()
    smalls[...] = jnp.zeros(smalls.shape, F32)
    for n, ref in enumerate((gen_small, fake_small, teacher_small)):
        for r in range(13):
            smalls[me.sec, n, r : r + 1, :] = ref[r]
    gathers = [
        Gather(me, net, stage.at[n], local_sem.at[n], send_sem.at[n], recv_sem.at[n])
        for n, net in enumerate((w_gen, w_fake, w_teach))
    ]
    for copy in masters:
        copy.wait()
    stage[0] = gshard[...].astype(BF16)
    stage[1] = fshard[...].astype(BF16)
    me.meet()
    gathers[0].begin()
    swap = remote(
        smalls.at[me.sec], smalls.at[me.sec], small_sem.at[0], small_sem.at[1], me.sib
    )
    swap.start()

    clear_pads(bufs)
    sgrads[...] = jnp.zeros(sgrads.shape, F32)
    sigmas = []
    valid_sum = jnp.zeros((1, 4 * C), F32)
    for i in range(images):
        level = jnp.zeros((1, 4 * C), jnp.int32) + levels[start + i]
        sigma = SIGMA_TOP + level.astype(F32) / (LEVELS - 1) * (SIGMA_BOTTOM - SIGMA_TOP)
        square = sigma * sigma
        sigma = square * square * square * sigma
        sigmas.append(sigma)
        s_in, s_skip, s_out, s_lam = precondition(sigma)
        valid = jnp.where(jnp.zeros_like(level) + (start + i) < counts[0], 1.0, 0.0)
        valid_sum = valid_sum + valid
        rows = (s_in, s_skip, s_out, sigma, valid * s_lam * (1.0 / (POS * C)))
        for k, value in enumerate(rows):
            tab[i, k : k + 1, :] = value[:, :C]
    fill_embed(score_eo, sigmas)
    fill_embed(gen_eo, [jnp.full((1, 4 * C), SIGMA_INIT, F32)] * images)

    def forward(n, w, eo, sv, pump):
        def body(l, _):
            layer_forward(
                l, w, smalls.at[:, n], eo, *sv, bufs, nbuf, qkvw, tmp, True, pump
            )
            return 0

        lax.fori_loop(0, 2, body, 0)

    def backward(n, w, eo, sv, cot, grad, sgrad, pump):
        def body(k, _):
            layer_backward(
                1 - k, w, smalls.at[:, n], eo, *sv, cot, bufs, nbuf, qkvw, tmp, dn, dqkv,
                act_t, grad, sgrad, pump,
            )
            return 0

        lax.fori_loop(0, 2, body, 0)

    def each(f):
        def body(i, carry):
            return f(i, [tab[i, k : k + 1, :] for k in range(5)], carry)

        return lax.fori_loop(0, images, body, jnp.zeros((1, C), F32))

    z_now, z_next = gathers[0].phase1(), gathers[1].phase1()
    run(z_now[:2] + [gathers[1].begin] + z_now[2:] + gathers[0].phase2() + z_next[:1])
    last = gathers[0].phase3()
    run(last[:4] + z_next[1:2] + [gathers[2].begin] + last[4:] + z_next[2:])
    for copy in loads:
        copy.wait()
    sv_one[0][0] = zb[...] * (GEN_IN * SIGMA_INIT)
    swap.wait()
    run(gathers[0].finish())
    later = gathers[1].phase2()
    forward(0, w_gen, gen_eo, sv_one, Pump(later[:5], FORWARD_POINTS, (0, 1)))
    pairs = [(w_gen, gw_out)] + list(zip(sv_one, gen_out))
    stores = [
        pltpu.make_async_copy(src, dst, copy_sem.at[2 + k]) for k, (src, dst) in enumerate(pairs)
    ]
    for copy in stores:
        copy.start()

    def noisy(i, t, carry):
        zb[i] = zb[i] * (GEN_SKIP * SIGMA_INIT) + GEN_OUT * sv_one[0][2, i]
        eb[i] = zb[i] + t[T_SIGMA] * eb[i]
        sv_two[0][0, i] = t[T_IN] * eb[i]
        return carry

    each(noisy)
    z_next, last = gathers[2].phase1(), gathers[1].phase3()
    run(later[5:] + z_next[:1] + last[:4] + z_next[1:2] + last[4:] + z_next[2:])
    run(gathers[1].finish())
    later = gathers[2].phase2()
    forward(1, w_fake, score_eo, sv_two, Pump(later[:5], FORWARD_POINTS, (0, 1)))
    later = later[5:] + gathers[2].phase3()

    def fake_loss(i, t, total):
        den = t[T_SKIP] * eb[i] + t[T_OUT] * sv_two[0][2, i]
        sv_two[0][2, i] = den
        miss = den - zb[i]
        g[i] = (2.0 * t[T_OUT] * t[T_FACTOR]) * miss
        return total + t[T_FACTOR] * colsum(miss * miss)

    loss_fake = each(fake_loss)
    for copy in stores:
        copy.wait()
    gathers[0].drain()
    backward(
        1, w_fake, score_eo, sv_two, g, w_gen, sgrads.at[:, 1],
        Pump(later, WEIGHT_POINTS, (1, 0), 0.0, 0.8),
    )
    fake_sum = Reduce(me, w_gen, fshard, sib, sib, *fake_refs)
    fake_sum.begin()
    run(gathers[2].finish())
    later = fake_sum.steps()
    sv_one[0][0] = sv_two[0][0]
    forward(2, w_teach, score_eo, sv_one, no_pump)

    def gen_loss(i, t, total):
        den = t[T_SKIP] * eb[i] + t[T_OUT] * sv_one[0][2, i]
        fake_den = sv_two[0][2, i]
        miss = fake_den - zb[i]
        gap = den - fake_den
        scale = t[T_OUT] * t[T_FACTOR]
        g[i] = scale * ((2.0 * (1.0 - ALPHA_MIX)) * gap + miss)
        g2[i] = scale * ((1.0 - 2.0 * (1.0 - ALPHA_MIX)) * gap - miss)
        zb[i] = (t[T_FACTOR] * (t[T_SKIP] - 1.0)) * gap
        return total + t[T_FACTOR] * colsum(gap * ((1.0 - ALPHA_MIX) * gap + miss))

    loss_gen = each(gen_loss)
    backward(
        2, w_teach, score_eo, sv_one, g, None, None, Pump(later[:4], BACKWARD_POINTS, (1, 0), 0.2)
    )
    gathers[2].drain()
    fake_sum.drain(A_SLOT, B_SLOT)
    pl.semaphore_signal(free_sem, inc=1, device_id=me.sib, device_id_type=MESH)
    back = [
        pltpu.make_async_copy(src, dst, copy_sem.at[2 + k])
        for k, (dst, src) in enumerate([(w_teach, gw_out)] + list(zip(sv_one, gen_out)))
    ]
    for copy in back:
        copy.start()
    backward(
        1, w_fake, score_eo, sv_two, g2, None, None, Pump(later[4:8], BACKWARD_POINTS, (1, 0))
    )

    def gen_gradient(i, t, carry):
        g[i] = GEN_OUT * (zb[i] + t[T_IN] * (g[i] + g2[i]))
        return carry

    each(gen_gradient)
    gathers[1].drain()
    for copy in back:
        copy.wait()

    gen_sum = Reduce(me, w_fake, gshard, w_gen.at[1 - me.sec], w_gen.at[me.sec], *gen_refs)
    fake_steps, later = later, gen_sum.steps()

    def on_section(s, steps):
        pl.when(me.sec == s)(lambda: run(steps))

    def hand_over():
        pl.semaphore_wait(free_sem, 1)

    pump = Pump([], WEIGHT_POINTS, (1, 0))

    def at(layer, point, section, steps):
        pump.table[layer][point].append(lambda: on_section(section, steps))

    upper = [hand_over, lambda: gen_sum.begin_block(0), lambda: gen_sum.begin_block(1)]
    lower = [lambda: gen_sum.begin_block(2), lambda: gen_sum.begin_block(3)]
    for layer, giver in ((1, 0), (0, 1)):
        at(layer, HALF_WAY, giver, upper)
        at(layer, READY, giver, lower)
    for k, point in enumerate((2, 9, 15)):
        pump.table[1][point].append(fake_steps[8 + k])
    pump.table[0][3].append(fake_steps[11])
    for k, point in enumerate((1, 3, 6, 8, 9, 10, 11, 12, 13, 14, 16, 17)):
        at(0, point, 1, later[k : k + 1])
    backward(0, w_teach, gen_eo, sv_one, g, w_fake, sgrads.at[:, 0], pump)

    def spread_sum(total):
        return jnp.broadcast_to(jnp.sum(total, axis=1, keepdims=True), (1, C))

    sums = jnp.concatenate([spread_sum(loss_gen), spread_sum(loss_fake), valid_sum[:, :C]], axis=0)
    for s in range(2):
        part_sums[s, 0:16, :] = sgrads[s, 0]
        part_sums[s, 13:16, :] = sums
        part_sums[s, 16:32, :] = sgrads[s, 1]
    small = Totals(me, *small_refs)
    small_refs[0][0] = part_sums[me.sec]
    small.begin(part_sums.at[1 - me.sec])
    fake_sum.stage_e()
    small_steps = small.steps()
    on_section(0, later[:3])
    run(small_steps[:1])
    on_section(0, later[3:6])
    run(small_steps[1:2])
    on_section(0, later[6:9])
    run(small_steps[2:])
    on_section(0, later[9:])
    stot[...] = small.result()
    own = square_refs[0]
    keep = lax.broadcasted_iota(jnp.int32, (16, C), 0) < 13
    for n, rows in ((1, fshard), (0, gshard)):
        if n == 0:
            gen_sum.stage_e()
        low = jnp.square(jnp.where(keep, stot[16 * n : 16 * n + 16, :], 0.0))
        low = jnp.where(me.d == 0, low[0:8] + low[8:16], 0.0)
        big = jnp.sum(jnp.square(rows[...]).reshape(rows.shape[0] // 8, 8, C), axis=0)
        own[0, 8 * n : 8 * n + 8, :] = big + low
    square = Squares(me, *square_refs)
    sqtot[...] = square.run()
    fake_sum.drain(B_SLOT)
    for done in (gen_sum, small, square):
        done.drain()


SIGMA_TOP = SIGMA_HIGH ** (1.0 / RHO_POWER)
SIGMA_BOTTOM = SIGMA_LOW ** (1.0 / RHO_POWER)


def run_step(z, eps, levels, counts, gen_w, fake_w, teacher_w, smalls):
    part = gen_w.shape[0]
    images = z.shape[0] // 2
    any_ = pl.BlockSpec(memory_space=pl.ANY)
    smem = pl.BlockSpec(memory_space=pltpu.SMEM)
    saved = saved_shapes(images)
    return pl.pallas_call(
        step_kernel,
        out_shape=[jax.ShapeDtypeStruct((2, ROWS, C), BF16)]
        + saved
        + [
            jax.ShapeDtypeStruct((part, C), F32),
            jax.ShapeDtypeStruct((part, C), F32),
            jax.ShapeDtypeStruct((32, C), F32),
            jax.ShapeDtypeStruct((16, C), F32),
        ],
        in_specs=[any_] * 2 + [smem] * 2 + [any_] * 3 + vm(3),
        out_specs=[any_] * 8 + vm(4),
        scratch_shapes=[pltpu.VMEM((2, ROWS, C), BF16)] * 3
        + saved_scratch(images) * 2
        + backward_scratch(images)
        + [pltpu.VMEM((images, POS, C), F32)] * 3
        + [
            pltpu.VMEM((3, part, C), BF16),
            pltpu.SemaphoreType.DMA((3,)),
            pltpu.SemaphoreType.DMA((3, SLOTS)),
            pltpu.SemaphoreType.DMA((3, SLOTS)),
            pltpu.SemaphoreType.DMA((10,)),
            pltpu.VMEM((2, 3, 16, C), F32),
            pltpu.SemaphoreType.DMA((2,)),
            pltpu.VMEM((8, 4 * C), BF16),
            pltpu.VMEM((8, 4 * C), BF16),
            pltpu.VMEM((images, 8, C), F32),
            pltpu.VMEM((2, 2, 16, C), F32),
            pltpu.VMEM((2, 32, C), F32),
        ]
        + reduce_scratch(part) * 2
        + totals_scratch((32, C))
        + squares_scratch((16, C))
        + [pltpu.VMEM((ROWS, C), BF16), pltpu.SemaphoreType.REGULAR],
        compiler_params=pltpu.CompilerParams(
            collective_id=0, has_side_effects=True, vmem_limit_bytes=STEP_LIMIT
        ),
    )(z, eps, levels, counts, gen_w, fake_w, teacher_w, *smalls)[8:]


def adam_step(master, first_mom, second_mom, grad):
    first_new = BETA_ONE * first_mom + (1.0 - BETA_ONE) * grad
    second_new = BETA_TWO * second_mom + (1.0 - BETA_TWO) * grad * grad
    direction = (
        first_new
        / (1.0 - BETA_ONE**STEP)
        / (jnp.sqrt(second_new / (1.0 - BETA_TWO**STEP)) + ADAM_EPS)
    )
    return (master - LEARN_RATE * (direction + WEIGHT_DECAY * master), first_new, second_new)


EMA_RATE = 0.5 ** (20.0 / STEP)
SMALL_STATES = (4, 5, 6, 7, 11, 12, 13)


def update_kernel(gshard, fshard, stot, sqtot, *refs):
    ins, outs = refs[:14], refs[14:]
    norms, losses = outs[14:]
    count = stot[15:16, 0:1]
    norm_of, scales = [], []
    for n in range(2):
        rows = jnp.sum(sqtot[8 * n : 8 * n + 8, :], axis=0, keepdims=True)
        norm = jnp.sqrt(jnp.sum(rows, axis=1, keepdims=True)) / count
        scales.append(jnp.minimum(1.0, CLIP_NORM / norm) / count)
        norm_of.append(norm)

    def one(at, grad, w, m, v, ema, ow, om, ov, oe):
        new, first, second = adam_step(w[at], m[at], v[at], grad)
        ow[at] = new
        om[at] = first
        ov[at] = second
        if ema is not None:
            oe[at] = EMA_RATE * ema[at] + (1.0 - EMA_RATE) * new

    one(0, gshard[...] * scales[0], *ins[0:4], *outs[0:4])
    one(0, fshard[...] * scales[1], *ins[8:11], None, *outs[8:11], None)

    @pl.when(pl.program_id(0) == 0)
    def _():
        for n in range(2):
            norms[n] = norm_of[n][0, 0]
            losses[n] = (stot[13 + n : 14 + n, 0:1] / count)[0, 0]
        for k in range(13):
            one(k, stot[k : k + 1, :] * scales[0], *ins[4:8], *outs[4:8])
            one(k, stot[16 + k : 17 + k, :] * scales[1], *ins[11:14], None, *outs[11:14], None)


def update_nets(gshard, fshard, stot, sqtot, states):
    def turned(arrays):
        return [a.swapaxes(0, 1) if k in SMALL_STATES else a for k, a in enumerate(arrays)]

    part = gshard.shape[0]
    steps = 1
    big = pl.BlockSpec((1, part // steps, C), lambda i: (0, i, 0))
    low = pl.BlockSpec((13, 1, C), lambda i: (0, 0, 0))
    shard = pl.BlockSpec((part // steps, C), lambda i: (i, 0))
    whole = [pl.BlockSpec(a.shape, lambda i: (0, 0)) for a in (stot, sqtot)]
    specs = [low if k in SMALL_STATES else big for k in range(len(states))]
    states = turned(states)
    res = pl.pallas_call(
        update_kernel,
        grid=(steps,),
        out_shape=[jax.ShapeDtypeStruct(a.shape, F32) for a in states]
        + [jax.ShapeDtypeStruct((2,), F32)] * 2,
        in_specs=[shard] * 2 + whole + specs,
        out_specs=specs + [pl.BlockSpec(memory_space=pltpu.SMEM)] * 2,
        compiler_params=pltpu.CompilerParams(vmem_limit_bytes=VMEM_LIMIT),
    )(gshard, fshard, stot, sqtot, *states)
    return tuple(turned(res[:-2])) + tuple(res[-2:])


def gather_plain(shard):
    rows = lax.all_gather(shard.astype(BF16), "dp", axis=1, tiled=True)
    return lax.all_gather(rows, "section", axis=0, tiled=True)


def reduce_plain(bigs, small):
    shards_, squares = [], []
    own = lax.psum_scatter(small, "section", scatter_dimension=0, tiled=True)
    stot = lax.psum(own, "dp")[0]
    first = lax.axis_index("dp") == 0
    for n, big in enumerate(bigs):
        own = lax.psum_scatter(big, "section", scatter_dimension=0, tiled=True)
        own = lax.psum_scatter(own, "dp", scatter_dimension=1, tiled=True)[0].astype(F32)
        shards_.append(own)
        low = jnp.sum(jnp.square(stot[16 * n : 16 * n + 13]))
        squares.append(jnp.sum(own * own) + jnp.where(first, low, 0.0))
    sq = lax.psum(jnp.stack(squares), ("section", "dp"))
    return *shards_, stot, jnp.zeros((16, C), F32).at[jnp.array([0, 8]), 0].set(sq)


def shards(
    z_noise, eps_noise, levels, counts,
    gen_w, gen_m, gen_v, gen_ema, gen_small, gen_small_m, gen_small_v, gen_small_ema,
    fake_w, fake_m, fake_v, fake_small, fake_small_m, fake_small_v,
    teacher_w, teacher_small,
):
    if lax.axis_size("dp") == PLANES * PLANE:
        smalls = [a.swapaxes(0, 1) for a in (gen_small, fake_small, teacher_small)]
        reduced = run_step(
            z_noise, eps_noise, levels, counts, gen_w[0], fake_w[0], teacher_w[0], smalls
        )
    else:
        reduced = plain_step(
            z_noise, eps_noise, levels, counts, gen_w, fake_w, teacher_w,
            gen_small, fake_small, teacher_small,
        )
    return update_nets(
        *reduced,
        (
            gen_w, gen_m, gen_v, gen_ema, gen_small, gen_small_m, gen_small_v, gen_small_ema,
            fake_w, fake_m, fake_v, fake_small, fake_small_m, fake_small_v,
        ),
    )


def plain_step(
    z_noise, eps_noise, levels, counts, gen_w, fake_w, teacher_w,
    gen_small, fake_small, teacher_small,
):
    images = z_noise.shape[0] // lax.axis_size("section")
    start = lax.axis_index("section") * images

    def mine(a):
        return lax.dynamic_slice_in_dim(a, start, images, 0)

    z, eps = mine(z_noise), mine(eps_noise)
    sigma = sigma_levels(mine(levels))
    valid = (start + jnp.arange(images) < counts[0]).astype(F32)
    valid_sum = jnp.sum(valid)
    gen_eo = spread_embed(jnp.full((images,), SIGMA_INIT, F32))
    score_eo = spread_embed(sigma)
    gs, fs, ts = [
        lax.all_gather(a, "section", axis=0, tiled=True)
        for a in (gen_small, fake_small, teacher_small)
    ]
    gw, fw, tw = gather_plain(gen_w), gather_plain(fake_w), gather_plain(teacher_w)
    s_in, s_skip, s_out, s_lam = precondition(sigma)
    factor = valid * s_lam / (POS * C)
    s_in, s_skip, s_out, sigma, factor = [
        t[:, None, None] for t in (s_in, s_skip, s_out, sigma, factor)
    ]
    raw = SIGMA_INIT * z
    gen_saved = run_forward(GEN_IN * raw, gw, gs, gen_eo)
    samples = GEN_SKIP * raw + GEN_OUT * gen_saved[0][2]
    noisy = samples + sigma * eps
    x0 = s_in * noisy
    fake_saved = run_forward(x0, fw, fs, score_eo)
    fake_den = s_skip * noisy + s_out * fake_saved[0][2]
    miss = fake_den - samples
    _, fake_g, fake_sg = run_backward(
        s_out * 2.0 * factor * miss, fw, fs, score_eo, fake_saved, True
    )
    teacher_saved = run_forward(x0, tw, ts, score_eo)
    teacher_den = s_skip * noisy + s_out * teacher_saved[0][2]
    gap = teacher_den - fake_den
    loss_gen = jnp.sum(factor * ((1.0 - ALPHA_MIX) * gap * gap + gap * miss))
    loss_fake = jnp.sum(factor * miss * miss)
    grad_teacher = factor * (2.0 * (1.0 - ALPHA_MIX) * gap + miss)
    grad_fake = factor * gap - grad_teacher
    direct = factor * gap * (s_skip - 1.0)
    (back_t,) = run_backward(s_out * grad_teacher, tw, ts, score_eo, teacher_saved, False)
    (back_f,) = run_backward(s_out * grad_fake, fw, fs, score_eo, fake_saved, False)
    gen_cot = GEN_OUT * (direct + s_in * (back_t + back_f))
    _, gen_g, gen_sg = run_backward(gen_cot, gw, gs, gen_eo, gen_saved, True)
    scalars = jnp.broadcast_to(jnp.stack([loss_gen, loss_fake, valid_sum])[:, None], (3, C))
    small_sums = jnp.concatenate(
        [gen_sg[:, :13], jnp.broadcast_to(scalars, (2, 3, C)), fake_sg], axis=1
    )
    return reduce_plain((gen_g, fake_g), small_sums)


def solution(mesh):
    images = P("dp", None, None)
    big = P("section", "dp", None)
    small = P("section", None, None)
    return jax.shard_map(
        shards,
        mesh=mesh,
        in_specs=(images, images, P("dp"), P("dp"))
        + (big,) * 4 + (small,) * 4 + (big,) * 3 + (small,) * 3 + (big, small),
        out_specs=(big,) * 4 + (small,) * 4 + (big,) * 3 + (small,) * 3 + (P(), P()),
        check_vma=False,
    )
```

```python
import functools

import jax
import jax.numpy as jnp
from jax import lax
from jax.experimental import pallas as pl
from jax.experimental.pallas import tpu as pltpu
from jax.sharding import PartitionSpec as P

GROUPS = 32
SIDE = 16
LEVELS = 1000
STEP = 10

SIGMA_DATA = 0.5
SIGMA_INIT = 2.5
SIGMA_LOW = 0.05
SIGMA_HIGH = 20.0
RHO_POWER = 7.0
ALPHA_MIX = 1.2
RS = 0.7071067811865476
NORM_EPS = 1e-05
CLIP_NORM = 0.001
LEARN_RATE = 0.15
BETA_ONE = 0.9
BETA_TWO = 0.999
ADAM_EPS = 1e-08
WEIGHT_DECAY = 0.01

C = 256
HALF = 128
POS = 256
ROWS = 26 * C
CHUNK = 64
PAD = SIDE
F32 = jnp.float32
BF16 = jnp.bfloat16
VMEM_LIMIT = 58 * 2**20
STEP_LIMIT = 63 * 2**20

R_CONV1, R_CONV2, R_EMB, R_QKV, R_PROJ = 0, 9 * C, 18 * C, 22 * C, 25 * C
S_M1, S_I1, S_M2, S_I2, S_M3, S_I3, S_MA, S_MB = range(8)


def sigma_levels(level_ids):
    fraction = level_ids.astype(F32) / (LEVELS - 1)
    top_root = SIGMA_HIGH ** (1.0 / RHO_POWER)
    bottom_root = SIGMA_LOW ** (1.0 / RHO_POWER)
    return (top_root + fraction * (bottom_root - top_root)) ** RHO_POWER


def precondition(sigma_vals):
    total = sigma_vals * sigma_vals + SIGMA_DATA**2
    return (
        lax.rsqrt(total),
        SIGMA_DATA**2 / total,
        sigma_vals * SIGMA_DATA * lax.rsqrt(total),
        total / (sigma_vals * sigma_vals * SIGMA_DATA**2),
    )


def noise_embed(sigma_vals, channel_count):
    frequency = (1.0 / 10000.0) ** (jnp.arange(channel_count, dtype=F32) / channel_count)
    angles = (jnp.log(sigma_vals) / 4.0)[..., None] * frequency
    return jnp.concatenate([jnp.cos(angles), jnp.sin(angles)], axis=-1)


def spread_embed(sigma_vals):
    emb = noise_embed(sigma_vals, C).astype(BF16)
    images = emb.shape[0]
    zero = jnp.zeros_like(emb)
    low = jnp.stack([emb, zero], axis=-1).reshape(images, 4 * C)
    high = jnp.stack([zero, emb], axis=-1).reshape(images, 4 * C)
    fill = jnp.zeros((4 - images, 4 * C), BF16)
    return jnp.concatenate([low, fill, high, fill], axis=0)


def dot_nn(a, b):
    return lax.dot_general(a, b, (((1,), (0,)), ((), ())), preferred_element_type=F32)


def dot_nt(a, b):
    return lax.dot_general(a, b, (((1,), (1,)), ((), ())), preferred_element_type=F32)


def dot_tn(a, b):
    return lax.dot_general(a, b, (((0,), (0,)), ((), ())), preferred_element_type=F32)


def group_mean(v):
    lane = lax.broadcasted_iota(jnp.int32, (8, C), 1)
    for sh in (1, 2, 4):
        v = v + jnp.where((lane & sh) != 0, pltpu.roll(v, sh, 1), pltpu.roll(v, C - sh, 1))
    return v * (1.0 / (POS * 8))


def colsum(v):
    return jnp.sum(v, axis=0, keepdims=True)


def no_pump(l):
    pass


FORWARD_POINTS, BACKWARD_POINTS, WEIGHT_POINTS = 10, 12, 18
HALF_WAY, READY = 8, 13


def stagger(steps, images, between):
    for t in range(len(steps) + images - 1):
        for i in range(images):
            if 0 <= t - i < len(steps):
                steps[t - i](i)
        between()


class Pump:
    def __init__(self, steps, points, layers, lo=0.0, hi=1.0):
        self.table = {l: [[] for _ in range(points)] for l in layers}
        self.at = 0
        for k, step in enumerate(steps):
            place = int((lo + (hi - lo) * (k + 0.5) / len(steps)) * points * len(layers))
            self.table[layers[place // points]][place % points].append(step)

    def __call__(self, l):
        for layer, points in self.table.items():
            if points[self.at]:

                @pl.when(l == layer)
                def _(todo=points[self.at]):
                    for step in todo:
                        step()

        self.at += 1


def put_shifted(bufs, i, r, v):
    rows = v.shape[0]
    at = pl.ds(PAD + r, rows)
    sub = lax.broadcasted_iota(jnp.int32, (rows // SIDE, 8, C), 1)
    x = v.reshape(rows // SIDE, 2, 8, C)
    low, high = x[:, 0], x[:, 1]
    low_up, high_up = pltpu.roll(low, 1, 1), pltpu.roll(high, 1, 1)
    low_down, high_down = pltpu.roll(low, 7, 1), pltpu.roll(high, 7, 1)
    left = (jnp.where(sub == 0, 0.0, low_up), jnp.where(sub == 0, low_up, high_up))
    right = (jnp.where(sub == 7, high_down, low_down), jnp.where(sub == 7, 0.0, high_down))
    bufs[0, i, at, :] = jnp.stack(left, axis=1).reshape(rows, C).astype(BF16)
    bufs[1, i, at, :] = v.astype(BF16)
    bufs[2, i, at, :] = jnp.stack(right, axis=1).reshape(rows, C).astype(BF16)


def taps(bufs, flip):
    images = bufs.shape[1]
    out = []
    for dr in (-1, 0, 1):
        for dc in (-1, 0, 1):
            sr, sc = (-dr, -dc) if flip else (dr, dc)
            piece = bufs[sc + 1, :, PAD + SIDE * sr : PAD + SIDE * sr + POS, :]
            out.append(piece.reshape(images * POS, C))
    return out


def conv_forward(bufs, w, l, row):
    return dot_nn(jnp.concatenate(taps(bufs, False), axis=1), w[l, row : row + 9 * C, :])


def conv_input_grad(bufs, w, l, row):
    parts = [w[l, row + t * C : row + (t + 1) * C, :] for t in range(9)]
    return dot_nt(jnp.concatenate(taps(bufs, True), axis=1), jnp.concatenate(parts, axis=1))


def conv_weight_grad(act_t, bufs, grad, l, row):
    left = act_t[...]
    for t, piece in enumerate(taps(bufs, True)):
        grad[l, row + t * C : row + (t + 1) * C, :] = dot_nn(left, piece).astype(BF16)


def silu(v):
    h = 0.5 * v
    return h + h * jnp.tanh(h)


def silu_parts(v):
    h = 0.5 * v
    t = jnp.tanh(h)
    return h + h * t, (1.0 + t) + h * (1.0 - t * t)


def clear_pads(bufs):
    zero = jnp.zeros(bufs.shape[:2] + (PAD, C), BF16)
    bufs[:, :, 0:PAD, :] = zero
    bufs[:, :, PAD + POS :, :] = zero


def split_qkv(w, l, qkvw, tmp):
    for h in range(2):
        tmp[h] = w[l, R_QKV : R_QKV + 3 * C, h * HALF : (h + 1) * HALF].astype(F32)
    for j in range(3):
        for h in range(2):
            at = j * C + h * HALF
            qkvw[:, at : at + HALF] = tmp[h, pl.ds(j, C, stride=3), :].astype(BF16)


def norm_sums(x):
    pivot = x[0:1]
    d = x - pivot
    return colsum(d), colsum(d * d), pivot


def norm_stats(sums):
    fill = [jnp.zeros((4 - len(sums), C), F32)]
    s1, s2, pivot = [jnp.concatenate([a[k] for a in sums] + fill, axis=0) for k in range(3)]
    centre = group_mean(jnp.concatenate([pivot, pivot], axis=0) * POS)[0:4]
    off = pivot - centre
    first = s1 + POS * off
    second = s2 + off * (2.0 * s1 + POS * off)
    means = group_mean(jnp.concatenate([first, second], axis=0))
    spread = jnp.maximum(means[4:8] - jnp.square(means[0:4]), 0.0)
    return centre + means[0:4], lax.rsqrt(spread + NORM_EPS)


def norm_map(gain, mg, mc, mean, inv):
    on_value = inv * inv * mc
    return inv * gain, on_value, inv * mg - mean * on_value


def two_means(a, b):
    rows = jnp.concatenate([a, b] * 4, axis=0)
    means = group_mean(rows)
    return means[0:1], means[1:2]


def tap_rows(bufs, flip, which):
    out = []
    for dr in (-1, 0, 1):
        for dc in (-1, 0, 1):
            sr, sc = (-dr, -dc) if flip else (dr, dc)
            at = slice(PAD + SIDE * sr, PAD + SIDE * sr + POS)
            piece = jnp.concatenate([bufs[sc + 1, i, at, :] for i in which], axis=0)
            out.append(piece)
    return out


def layer_forward(l, w, small, eo, xs, h1, y, qkv, att, o, st, bufs, nbuf, qkvw, tmp, staged, pump):
    images = h1.shape[1]
    split_qkv(w, l, qkvw, tmp)
    mod = dot_nn(eo[...], w[l, R_EMB : R_EMB + 4 * C, :])
    ma = mod[0:4] + small[l, 5:6, :]
    mb = mod[4:8] + small[l, 6:7, :]
    for i in range(images):
        st[l, i, S_MA : S_MA + 1, :] = ma[i : i + 1]
        st[l, i, S_MB : S_MB + 1, :] = mb[i : i + 1]

    sums = {}

    def row(k):
        return small[l, k : k + 1, :]

    def keep(which, mean, inv, at):
        for k, i in enumerate(which):
            st[l, i, at : at + 1, :] = mean[k : k + 1]
            st[l, i, at + 1 : at + 2, :] = inv[k : k + 1]

    def first(which):
        mean, inv = norm_stats([norm_sums(xs[l, i]) for i in which])
        keep(which, mean, inv, S_M1)
        for k, i in enumerate(which):
            a = inv[k : k + 1] * row(0)
            b = row(1) - mean[k : k + 1] * a
            for r in range(0, POS, CHUNK):
                v = xs[l, i, r : r + CHUNK, :] * a + b
                put_shifted(bufs, i, r, silu(v))

    def conv(which, at):
        left = jnp.concatenate(tap_rows(bufs, False, which), axis=1)
        return dot_nn(left, w[l, at : at + 9 * C, :])

    def conv_one(which):
        out = conv(which, R_CONV1)
        for k, i in enumerate(which):
            own = out[k * POS : (k + 1) * POS]
            own = own + row(2)
            sums[i] = norm_sums(own)
            h1[l, i] = own

    def second(which):
        mean, inv = norm_stats([sums[i] for i in which])
        keep(which, mean, inv, S_M2)
        for k, i in enumerate(which):
            gain = 1.0 + ma[i : i + 1]
            a = inv[k : k + 1] * row(3) * gain
            b = row(4) * gain + mb[i : i + 1] - mean[k : k + 1] * a
            for r in range(0, POS, CHUNK):
                v = h1[l, i, r : r + CHUNK, :] * a + b
                put_shifted(bufs, i, r, silu(v))

    def conv_two(which):
        out = conv(which, R_CONV2) + row(7)
        for k, i in enumerate(which):
            own = (xs[l, i] + out[k * POS : (k + 1) * POS]) * RS
            sums[i] = norm_sums(own)
            y[l, i] = own

    def third(which):
        mean, inv = norm_stats([sums[i] for i in which])
        keep(which, mean, inv, S_M3)
        for k, i in enumerate(which):
            a = inv[k : k + 1] * row(8)
            b = row(9) - mean[k : k + 1] * a
            for r in range(0, POS, CHUNK):
                v = y[l, i, r : r + CHUNK, :] * a + b
                nbuf[i, r : r + CHUNK, :] = v.astype(BF16)

    def project_in(which):
        n = jnp.concatenate([nbuf[i] for i in which], axis=0)
        for j, at in ((0, 10), (1, None), (2, 11)):
            part = dot_nn(n, qkvw[:, j * C : (j + 1) * C])
            if at is not None:
                part = part + row(at)
            part = part.astype(BF16)
            for k, i in enumerate(which):
                qkv[l, i, :, j * C : (j + 1) * C] = part[k * POS : (k + 1) * POS]

    def attend(which):
        scores = [dot_nt(qkv[l, i, :, 0:C], qkv[l, i, :, C : 2 * C]) for i in which]
        for s, i in zip(scores, which):
            e = jnp.exp((s - jnp.max(s, axis=1, keepdims=True)) * (C**-0.5))
            p = (e * (1.0 / jnp.sum(e, axis=1, keepdims=True))).astype(BF16)
            att[l, i] = p
            o[l, i] = dot_nn(p, qkv[l, i, :, 2 * C :]).astype(BF16)

    def project_out(which):
        left = jnp.concatenate([o[l, i] for i in which], axis=0)
        out = dot_nn(left, w[l, R_PROJ:, :]) + row(12)
        for k, i in enumerate(which):
            xs[l + 1, i] = (y[l, i] + out[k * POS : (k + 1) * POS]) * RS

    steps = (first, conv_one, second, conv_two, third, project_in, attend, project_out)
    if not staged:
        for step in steps:
            step(range(images))
            pump(l)
    else:
        stagger([lambda i, step=step: step([i]) for step in steps], images, lambda: pump(l))


def layer_backward(
    l, w, small, eo, xs, h1, y, qkv, att, o, st, g, bufs, nbuf, qkvw, tmp, dn, dqkv, act_t,
    grad, sgrad, pump, need_dx=None,
):
    want = grad is not None
    images = h1.shape[1]
    which = range(images)
    flat = images * POS
    scale = C**-0.5
    split_qkv(w, l, qkvw, tmp)

    def row(k):
        return small[l, k : k + 1, :]

    def rows8(rows):
        return jnp.concatenate(list(rows) + [jnp.zeros((8 - len(rows), C), F32)], axis=0)

    zero = jnp.zeros((1, C), F32)
    gps, c1, c2, p1, p2 = {}, {}, {}, {}, {}
    total = {7: zero, 2: zero}
    gains = [1.0 + st[l, i, S_MA : S_MA + 1, :] for i in which]

    def project_out(i):
        gps[i] = (g[i] * RS).astype(BF16)
        nbuf[i] = dot_nt(gps[i], w[l, R_PROJ:, :]).astype(BF16)

    def attend(i):
        p = att[l, i]
        pf = p.astype(F32)
        dp = dot_nt(nbuf[i], qkv[l, i, :, 2 * C :])
        ds = (pf * (dp - jnp.sum(dp * pf, axis=1, keepdims=True))).astype(BF16)
        dqkv[i, :, 0:C] = (dot_nn(ds, qkv[l, i, :, C : 2 * C]) * scale).astype(BF16)
        dqkv[i, :, C : 2 * C] = (dot_tn(ds, qkv[l, i, :, 0:C]) * scale).astype(BF16)
        dqkv[i, :, 2 * C :] = dot_tn(p, nbuf[i]).astype(BF16)

    def project_in(i):
        mean, inv = st[l, i, S_M3 : S_M3 + 1, :], st[l, i, S_I3 : S_I3 + 1, :]
        d = dot_nt(dqkv[i], qkvw[...])
        dn[i] = d
        c1[i] = colsum(d)
        c2[i] = colsum(d * (y[l, i] - mean)) * inv

    def third(i):
        mean, inv = st[l, i, S_M3 : S_M3 + 1, :], st[l, i, S_I3 : S_I3 + 1, :]
        mg, mc = two_means(row(8) * c1[i], row(8) * c2[i])
        on_grad, on_value, offset = norm_map(row(8) * RS, mg * RS, mc * RS, mean, inv)
        act_a = inv * row(8)
        act_b = row(9) - mean * act_a
        for r in range(0, POS, CHUNK):
            value = y[l, i, r : r + CHUNK, :]
            gm = g[i, r : r + CHUNK, :] * (RS * RS) + dn[i, r : r + CHUNK, :] * on_grad
            gm = gm - (value * on_value + offset)
            g[i, r : r + CHUNK, :] = gm
            put_shifted(bufs, i, r, gm)
            if want:
                nbuf[i, r : r + CHUNK, :] = (value * act_a + act_b).astype(BF16)
                total[7] = total[7] + colsum(gm)

    def conv_grad(i, at):
        left = jnp.concatenate(tap_rows(bufs, True, [i]), axis=1)
        parts = [w[l, at + t * C : at + (t + 1) * C, :] for t in range(9)]
        dn[i] = dot_nt(left, jnp.concatenate(parts, axis=1))

    def activation(i, src, mean, inv, a, b, act=None):
        s1, s2 = zero, zero
        for r in range(0, POS, CHUNK):
            u = src[l, i, r : r + CHUNK, :] - mean
            act_value, slope = silu_parts(u * (inv * a) + b)
            d = dn[i, r : r + CHUNK, :] * slope
            dn[i, r : r + CHUNK, :] = d
            s1 = s1 + colsum(d)
            s2 = s2 + colsum(d * u)
            if act is not None:
                act[i, r : r + CHUNK, :] = act_value.astype(BF16)
        p1[i], p2[i] = s1 * 0.5, s2 * (0.5 * inv)

    def second_a(i):
        mean, inv = st[l, i, S_M2 : S_M2 + 1, :], st[l, i, S_I2 : S_I2 + 1, :]
        b = row(4) * gains[i] + st[l, i, S_MB : S_MB + 1, :]
        activation(i, h1, mean, inv, row(3) * gains[i], b, nbuf if want else None)

    def second_b(i):
        mean, inv = st[l, i, S_M2 : S_M2 + 1, :], st[l, i, S_I2 : S_I2 + 1, :]
        full = row(3) * gains[i]
        mg, mc = two_means(full * p1[i], full * p2[i])
        on_grad, on_value, offset = norm_map(full, mg, mc, mean, inv)
        for r in range(0, POS, CHUNK):
            dh = dn[i, r : r + CHUNK, :] * (0.5 * on_grad) - (
                h1[l, i, r : r + CHUNK, :] * on_value + offset
            )
            put_shifted(bufs, i, r, dh)
            if want:
                total[2] = total[2] + colsum(dh)

    def first_a(i):
        mean, inv = st[l, i, S_M1 : S_M1 + 1, :], st[l, i, S_I1 : S_I1 + 1, :]
        activation(i, xs, mean, inv, row(0), row(1))

    def first_act(i):
        mean, inv = st[l, i, S_M1 : S_M1 + 1, :], st[l, i, S_I1 : S_I1 + 1, :]
        a = inv * row(0)
        b = row(1) - mean * a
        for r in range(0, POS, CHUNK):
            v = xs[l, i, r : r + CHUNK, :] * a + b
            nbuf[i, r : r + CHUNK, :] = silu(v).astype(BF16)

    def first_b(i):
        mean, inv = st[l, i, S_M1 : S_M1 + 1, :], st[l, i, S_I1 : S_I1 + 1, :]
        mg, mc = two_means(row(0) * p1[i], row(0) * p2[i])
        on_grad, on_value, offset = norm_map(row(0), mg, mc, mean, inv)
        for r in range(0, POS, CHUNK):
            dx = dn[i, r : r + CHUNK, :] * (0.5 * on_grad) - (
                xs[l, i, r : r + CHUNK, :] * on_value + offset
            )
            g[i, r : r + CHUNK, :] = g[i, r : r + CHUNK, :] + dx

    upper = [project_out, attend, project_in, third, lambda i: conv_grad(i, R_CONV2)]
    lower = [lambda i: conv_grad(i, R_CONV1), first_a]
    if not want:
        stagger(upper + [second_a, second_b] + lower + [first_b], images, lambda: pump(l))
        return
    stagger(upper, images, lambda: pump(l))
    gp = jnp.concatenate([gps[i] for i in which], axis=0)
    grad[l, R_PROJ:, :] = dot_tn(o[l].reshape(flat, C), gp).astype(BF16)
    sgrad[l, 12:13, :] = colsum(gp.astype(F32))
    sgrad[l, 7:8, :] = total[7]
    sgrad[l, 8:9, :] = colsum(rows8([c2[i] for i in which]))
    sgrad[l, 9:10, :] = colsum(rows8([c1[i] for i in which]))
    act_t[...] = nbuf[...].reshape(flat, C).T
    for j in range(3):
        dj = dqkv[:, :, j * C : (j + 1) * C].reshape(flat, C)
        part = dot_nn(act_t[...], dj)
        for h in range(2):
            tmp[h, pl.ds(j, C, stride=3), :] = part[:, h * HALF : (h + 1) * HALF]
        if j != 1:
            sgrad[l, 10 + j // 2 : 11 + j // 2, :] = colsum(dj.astype(F32))
    for h in range(2):
        grad[l, R_QKV : R_QKV + 3 * C, h * HALF : (h + 1) * HALF] = tmp[h].astype(BF16)
    for i in which:
        second_a(i)
    pump(l)
    act_t[...] = nbuf[...].reshape(flat, C).T
    conv_weight_grad(act_t, bufs, grad, l, R_CONV2)
    p18, p28, modgain = [rows8([a[i] for i in which]) for a in (p1, p2, gains)]
    dma = row(3) * p28 + row(4) * p18
    sgrad[l, 3:4, :] = colsum(modgain * p28)
    sgrad[l, 4:5, :] = colsum(modgain * p18)
    sgrad[l, 5:6, :] = colsum(dma)
    sgrad[l, 6:7, :] = colsum(p18)
    grad[l, R_EMB : R_EMB + 4 * C, :] = embed_grad(
        eo, jnp.concatenate([dma[0:4], p18[0:4]], axis=0)
    ).astype(BF16)
    pump(l)
    stagger([second_b, first_act], images, lambda: pump(l))
    act_t[...] = nbuf[...].reshape(flat, C).T
    conv_weight_grad(act_t, bufs, grad, l, R_CONV1)
    pump(l)
    stagger(lower, images, lambda: pump(l))
    sgrad[l, 2:3, :] = total[2]
    sgrad[l, 0:1, :] = colsum(rows8([p2[i] for i in which]))
    sgrad[l, 1:2, :] = colsum(rows8([p1[i] for i in which]))

    @pl.when(l == 1)
    def _():
        for i in which:
            first_b(i)


def embed_grad(eo, dm):
    parts, rest = [], dm
    for _ in range(3):
        parts.append(rest.astype(BF16))
        rest = rest - parts[-1].astype(F32)
    left = eo[...]
    return dot_tn(jnp.concatenate([left, left], axis=0), jnp.concatenate(parts[:2], axis=0)) + dot_tn(
        left, parts[2]
    )


def saved_shapes(images):
    return [
        jax.ShapeDtypeStruct((3, images, POS, C), F32),
        jax.ShapeDtypeStruct((2, images, POS, C), F32),
        jax.ShapeDtypeStruct((2, images, POS, C), F32),
        jax.ShapeDtypeStruct((2, images, POS, 3 * C), BF16),
        jax.ShapeDtypeStruct((2, images, POS, POS), BF16),
        jax.ShapeDtypeStruct((2, images, POS, C), BF16),
        jax.ShapeDtypeStruct((2, images, 8, C), F32),
    ]


def forward_kernel(staged, x0, w, small, eo, xs, h1, y, qkv, att, o, st, bufs, nbuf, qkvw, tmp):
    clear_pads(bufs)
    xs[0] = x0[...]

    def body(l, _):
        layer_forward(
            l, w, small, eo, xs, h1, y, qkv, att, o, st, bufs, nbuf, qkvw, tmp, staged, no_pump
        )
        return 0

    lax.fori_loop(0, 2, body, 0)


def backward_kernel(want, *refs):
    cot, w, small, eo, xs, h1, y, qkv, att, o, st, g = refs[:12]
    refs = refs[12:]
    if want:
        grad, sgrad = refs[:2]
        refs = refs[2:]
    else:
        grad, sgrad = None, None
    bufs, nbuf, qkvw, tmp, dn, dqkv, act_t = refs
    clear_pads(bufs)
    g[...] = cot[...]
    if want:
        sgrad[...] = jnp.zeros(sgrad.shape, F32)

    def body(k, _):
        layer_backward(
            1 - k, w, small, eo, xs, h1, y, qkv, att, o, st, g, bufs, nbuf, qkvw, tmp, dn,
            dqkv, act_t, grad, sgrad, no_pump,
        )
        return 0

    lax.fori_loop(0, 2, body, 0)


def vm(n):
    return [pl.BlockSpec(memory_space=pltpu.VMEM)] * n


def scratch_forward(images):
    return [
        pltpu.VMEM((3, images, POS + 2 * PAD, C), BF16),
        pltpu.VMEM((images, POS, C), BF16),
        pltpu.VMEM((C, 3 * C), BF16),
        pltpu.VMEM((2, 3 * C, HALF), F32),
    ]


def run_forward(x0, w, small, eo, staged=False):
    images = x0.shape[0]
    return pl.pallas_call(
        functools.partial(forward_kernel, staged),
        out_shape=saved_shapes(images),
        in_specs=vm(4),
        out_specs=vm(7),
        scratch_shapes=scratch_forward(images),
        compiler_params=pltpu.CompilerParams(vmem_limit_bytes=VMEM_LIMIT),
    )(x0, w, small, eo)


def run_backward(cot, w, small, eo, saved, want):
    images = cot.shape[0]
    outs = [jax.ShapeDtypeStruct(cot.shape, F32)]
    if want:
        outs += [
            jax.ShapeDtypeStruct((2, ROWS, C), BF16),
            jax.ShapeDtypeStruct((2, 16, C), F32),
        ]
    return pl.pallas_call(
        functools.partial(backward_kernel, want),
        out_shape=outs,
        in_specs=vm(11),
        out_specs=vm(len(outs)),
        scratch_shapes=scratch_forward(images)
        + [
            pltpu.VMEM((images, POS, C), F32),
            pltpu.VMEM((images, POS, 3 * C), BF16),
            pltpu.VMEM((C, images * POS), BF16),
        ],
        compiler_params=pltpu.CompilerParams(vmem_limit_bytes=VMEM_LIMIT),
    )(cot, w, small, eo, *saved)


PLANES, PLANE = 4, 4
MESH = pl.DeviceIdType.MESH


class Place:
    def __init__(self):
        self.sec = lax.axis_index("section")
        self.d = lax.axis_index("dp")
        self.x = lax.rem(self.d, 2)
        self.y = lax.rem(self.d // 2, 2)
        self.z = self.d // PLANE
        self.seat = self.sec * PLANE + lax.rem(self.d, PLANE)
        self.sib = {"section": 1 - self.sec}
        self.xn = {"dp": self.d + 1 - 2 * self.x}
        self.yn = {"dp": self.d + 2 - 4 * self.y}

    def plane(self, j):
        return lax.rem(self.z + j + PLANES, PLANES)

    def zpeer(self, j):
        return {"dp": self.plane(j) * PLANE + lax.rem(self.d, PLANE)}

    def plane_peer(self, j):
        seat = lax.rem(self.seat + j, 2 * PLANE)
        return {"section": seat // PLANE, "dp": self.z * PLANE + lax.rem(seat, PLANE)}

    def meet(self):
        barrier = pltpu.get_barrier_semaphore()
        others = [self.plane_peer(j) for j in range(1, 8)] + [self.zpeer(j) for j in (1, 2, 3)]
        for other in others:
            pl.semaphore_signal(barrier, inc=1, device_id=other, device_id_type=MESH)
        pl.semaphore_wait(barrier, len(others))


def remote(src, dst, send, recv, target):
    return pltpu.make_async_remote_copy(
        src_ref=src, dst_ref=dst, send_sem=send, recv_sem=recv,
        device_id=target, device_id_type=MESH,
    )


Z1, X1, Y1, X2, Y2, S_OWN, S_X, S_Y, S_DA, S_DB = 0, 3, 7, 11, 15, 19, 23, 27, 31, 35
SLOTS = 39


class Gather:
    def __init__(self, me, net, stage, local_sem, send_sem, recv_sem):
        self.me, self.net, self.stage = me, net, stage
        self.local_sem, self.send_sem, self.recv_sem = local_sem, send_sem, recv_sem
        self.part = stage.shape[0]
        self.half = self.part // 2

    def rows(self, plane, y, x, lo, count):
        at = (plane * PLANE + y * 2 + x) * self.part + lo
        return self.net.at[self.me.sec, pl.ds(pl.multiple_of(at, 16), count)]

    def own(self, j):
        return self.rows(self.me.plane(-j), self.me.y, self.me.x, 0, self.part)

    def send(self, slot, piece, target, src=None):
        src = piece if src is None else src
        remote(src, piece, self.send_sem.at[slot], self.recv_sem.at[slot], target).start()

    def arrived(self, slot, piece):
        remote(
            piece, piece, self.send_sem.at[slot], self.recv_sem.at[slot], self.me.sib
        ).wait_recv()

    def local(self):
        return pltpu.make_async_copy(self.stage, self.own(0), self.local_sem)

    def begin(self):
        me = self.me
        for j in (1, 2, 3):
            self.send(Z1 + j - 1, self.own(0), me.zpeer(j), self.stage)
        for slot, target in ((X1, me.xn), (Y1, me.yn), (S_OWN, me.sib)):
            self.send(slot, self.own(0), target, self.stage)
        self.local().start()

    def phase1(self):
        def step(j):
            me = self.me
            self.arrived(Z1 + j - 1, self.own(j))
            for slot, target in ((X1, me.xn), (Y1, me.yn), (S_OWN, me.sib)):
                self.send(slot + j, self.own(j), target)

        return [lambda j=j: step(j) for j in (1, 2, 3)]

    def phase2(self):
        me, part, half = self.me, self.part, self.half

        def step_x(j):
            plane = me.plane(-j)
            self.arrived(X1 + j, self.rows(plane, me.y, 1 - me.x, 0, part))
            self.send(Y2 + j, self.rows(plane, me.y, 1 - me.x, 0, half), me.yn)
            self.send(S_X + j, self.rows(plane, me.y, 1 - me.x, 0, part), me.sib)

        def step_y(j):
            plane = me.plane(-j)
            self.arrived(Y1 + j, self.rows(plane, 1 - me.y, me.x, 0, part))
            self.send(X2 + j, self.rows(plane, 1 - me.y, me.x, half, half), me.xn)
            self.send(S_Y + j, self.rows(plane, 1 - me.y, me.x, 0, part), me.sib)

        return [lambda f=f, j=j: f(j) for j in range(PLANES) for f in (step_x, step_y)]

    def phase3(self):
        def step(j, slot, to, lo):
            me = self.me
            where = self.rows(me.plane(-j), 1 - me.y, 1 - me.x, lo, self.half)
            self.arrived(slot + j, where)
            self.send(to + j, where, me.sib)

        return [
            lambda j=j, a=a: step(j, *a)
            for j in range(PLANES)
            for a in ((Y2, S_DA, 0), (X2, S_DB, self.half))
        ]

    def finish(self):
        def step():
            for slot in range(S_OWN, SLOTS):
                count = self.part if slot < S_DA else self.half
                self.arrived(slot, self.rows(0, 0, 0, 0, count))
            self.local().wait()

        return [step]

    def drain(self):
        for slot in range(SLOTS):
            whole = slot < X2 or S_OWN <= slot < S_DA
            piece = self.rows(0, 0, 0, 0, self.part if whole else self.half)
            remote(
                piece, piece, self.send_sem.at[slot], self.recv_sem.at[slot], self.me.sib
            ).wait_send()


A_SLOT, B_SLOT, C_SLOT, D_SLOT = 0, 4, 20, 28
R_SLOTS = 31


class Reduce:
    def __init__(self, me, big, shard, sib, there, rb, rc, rd, ssem, rsem):
        self.me, self.big, self.shard = me, big, shard
        self.sib, self.there, self.rb, self.rc, self.rd = sib, there, rb, rc, rd
        self.ssem, self.rsem = ssem, rsem
        self.part = shard.shape[0]
        self.half = self.part // 2
        self.span = PLANE * self.part

    def zt(self, k):
        return (3, 2, 0, 1)[k]

    def block(self, k):
        return pl.ds(self.zt(k) * self.span, self.span)

    def piece(self, k, y, x, lo, count):
        at = (self.zt(k) * PLANE + y * 2 + x) * self.part + lo
        return pl.ds(pl.multiple_of(at, 16), count)

    def send(self, src, dst, slot, target):
        remote(src, dst, self.ssem.at[slot], self.rsem.at[slot], target).start()

    def arrived(self, dst, slot):
        remote(dst, dst, self.ssem.at[slot], self.rsem.at[slot], self.me.sib).wait_recv()

    def begin(self):
        for k in range(PLANES):
            self.begin_block(k)

    def begin_block(self, k):
        at = self.block(k)
        self.send(self.big.at[1 - self.me.sec, at], self.there.at[at], A_SLOT + k, self.me.sib)

    def stage_a(self, k):
        me, half = self.me, self.half
        self.arrived(self.sib.at[self.block(k)], A_SLOT + k)
        base = self.zt(k) * self.span

        def body(i, _):
            at = pl.ds(pl.multiple_of(base + i * half, 16), half)
            self.big[me.sec, at, :] = (
                self.big[me.sec, at, :].astype(F32) + self.sib[at, :].astype(F32)
            ).astype(BF16)
            return 0

        lax.fori_loop(0, 2 * PLANE, body, 0)
        for j in range(2):
            self.send(
                self.big.at[me.sec, self.piece(k, 1 - me.y, j, 0, half)], self.rb.at[k, j],
                B_SLOT + 4 * k + j, me.yn,
            )
            self.send(
                self.big.at[me.sec, self.piece(k, j, 1 - me.x, half, half)], self.rb.at[k, 2 + j],
                B_SLOT + 4 * k + 2 + j, me.xn,
            )

    def join(self, where, other):
        self.big[self.me.sec, where, :] = (
            self.big[self.me.sec, where, :].astype(F32) + other.astype(F32)
        ).astype(BF16)

    def stage_c(self, k):
        me, half = self.me, self.half
        for j in range(4):
            self.arrived(self.rb.at[k, j], B_SLOT + 4 * k + j)
            y, x, lo = (me.y, j, 0) if j < 2 else (j - 2, me.x, half)
            self.join(self.piece(k, y, x, lo, half), self.rb[k, j])
        self.send(
            self.big.at[me.sec, self.piece(k, me.y, 1 - me.x, 0, half)], self.rc.at[k, 0],
            C_SLOT + 2 * k, me.xn,
        )
        self.send(
            self.big.at[me.sec, self.piece(k, 1 - me.y, me.x, half, half)], self.rc.at[k, 1],
            C_SLOT + 2 * k + 1, me.yn,
        )

    def stage_d(self, k):
        me, half, zt = self.me, self.half, self.zt(k)
        for j in range(2):
            self.arrived(self.rc.at[k, j], C_SLOT + 2 * k + j)
            self.join(self.piece(k, me.y, me.x, j * half, half), self.rc[k, j])

        @pl.when(me.z != zt)
        def _():
            self.send(
                self.big.at[me.sec, self.piece(k, me.y, me.x, 0, self.part)],
                self.rd.at[lax.rem(zt - me.z + PLANES, PLANES) - 1],
                D_SLOT + lax.rem(zt - me.z + PLANES, PLANES) - 1,
                {"dp": zt * PLANE + lax.rem(me.d, PLANE)},
            )

    def stage_e(self):
        for j in range(PLANES - 1):
            self.arrived(self.rd.at[j], D_SLOT + j)
        at = pl.ds(pl.multiple_of(self.me.d * self.part, 16), self.part)
        self.shard[...] = (
            self.big[self.me.sec, at, :].astype(F32)
            + self.rd[0].astype(F32) + (self.rd[1].astype(F32) + self.rd[2].astype(F32))
        )

    def in_rows(self):
        stages = (self.stage_a, self.stage_c, self.stage_d)
        return [lambda stage=stage, k=k: stage(k) for stage in stages for k in range(PLANES)]

    def steps(self):
        out = []
        for t in range(PLANES + 2):
            for stage, lag in ((self.stage_a, 0), (self.stage_c, 1), (self.stage_d, 2)):
                if 0 <= t - lag < PLANES:
                    out.append(lambda stage=stage, k=t - lag: stage(k))
        return out

    def drain(self, lo=0, hi=R_SLOTS):
        for slot in range(lo, hi):
            if slot < B_SLOT:
                piece = self.there.at[pl.ds(0, self.span)]
            elif slot < D_SLOT:
                piece = self.rb.at[0, 0]
            else:
                piece = self.rd.at[0]
            remote(piece, piece, self.ssem.at[slot], self.rsem.at[slot], self.me.sib).wait_send()


def reduce_scratch(part):
    half = part // 2
    return [
        pltpu.VMEM((PLANES, 4, half, C), BF16),
        pltpu.VMEM((PLANES, 2, half, C), BF16),
        pltpu.VMEM((PLANES - 1, part, C), BF16),
        pltpu.SemaphoreType.DMA((R_SLOTS,)),
        pltpu.SemaphoreType.DMA((R_SLOTS,)),
    ]


class Totals:
    def __init__(self, me, buf, recv, ssem, rsem):
        self.me, self.buf, self.recv, self.ssem, self.rsem = me, buf, recv, ssem, rsem

    def send(self, src, dst, slot, target):
        remote(src, dst, self.ssem.at[slot], self.rsem.at[slot], target).start()

    def arrived(self, dst, slot):
        remote(dst, dst, self.ssem.at[slot], self.rsem.at[slot], self.me.sib).wait_recv()

    def begin(self, first):
        self.send(first, self.recv.at[0], 0, self.me.sib)

    def steps(self):
        me, buf, recv = self.me, self.buf, self.recv

        def one():
            self.arrived(recv.at[0], 0)
            buf[1] = buf[0] + recv[0]
            self.send(buf.at[1], recv.at[1], 1, me.xn)

        def two():
            self.arrived(recv.at[1], 1)
            buf[2] = buf[1] + recv[1]
            self.send(buf.at[2], recv.at[2], 2, me.yn)

        def three():
            self.arrived(recv.at[2], 2)
            buf[3] = buf[2] + recv[2]
            recv[3 + me.z] = buf[3]
            for j in (1, 2, 3):
                self.send(buf.at[3], recv.at[3 + me.z], 2 + j, me.zpeer(j))

        return [one, two, three]

    def result(self):
        for j in (1, 2, 3):
            self.arrived(self.recv.at[3 + self.me.plane(-j)], 2 + j)
        return (self.recv[3] + self.recv[4]) + (self.recv[5] + self.recv[6])

    def drain(self):
        for slot in range(6):
            piece = self.recv.at[0]
            remote(piece, piece, self.ssem.at[slot], self.rsem.at[slot], self.me.sib).wait_send()


class Squares:
    def __init__(self, me, own, recv, ssem, rsem):
        self.me, self.own, self.recv, self.ssem, self.rsem = me, own, recv, ssem, rsem

    def hop(self, src, base, mine, peers, slots):
        for j, target in peers:
            dst = self.recv.at[base + mine]
            remote(src, dst, self.ssem.at[slots + j], self.rsem.at[slots + j], target).start()
        self.recv[base + mine] = src[...]
        for j, _ in peers:
            dst = self.recv.at[base]
            remote(dst, dst, self.ssem.at[slots + j], self.rsem.at[slots + j], self.me.sib).wait_recv()

    def run(self):
        me, recv = self.me, self.recv
        self.hop(self.own.at[0], 0, me.seat, [(j, me.plane_peer(j)) for j in range(1, 8)], -1)
        pairs = [recv[2 * k] + recv[2 * k + 1] for k in range(4)]
        self.own[1] = (pairs[0] + pairs[1]) + (pairs[2] + pairs[3])
        self.hop(self.own.at[1], 8, me.z, [(j, me.zpeer(j)) for j in (1, 2, 3)], 6)
        return (recv[8] + recv[9]) + (recv[10] + recv[11])

    def drain(self):
        for slot in range(10):
            piece = self.recv.at[0]
            remote(piece, piece, self.ssem.at[slot], self.rsem.at[slot], self.me.sib).wait_send()


def squares_scratch(shape):
    return [
        pltpu.VMEM((2,) + shape, F32),
        pltpu.VMEM((12,) + shape, F32),
        pltpu.SemaphoreType.DMA((10,)),
        pltpu.SemaphoreType.DMA((10,)),
    ]


def totals_scratch(shape):
    return [
        pltpu.VMEM((4,) + shape, F32),
        pltpu.VMEM((7,) + shape, F32),
        pltpu.SemaphoreType.DMA((6,)),
        pltpu.SemaphoreType.DMA((6,)),
    ]


def saved_scratch(images):
    return [pltpu.VMEM(a.shape, a.dtype) for a in saved_shapes(images)]


def backward_scratch(images):
    return scratch_forward(images) + [
        pltpu.VMEM((images, POS, C), F32),
        pltpu.VMEM((images, POS, 3 * C), BF16),
        pltpu.VMEM((C, images * POS), BF16),
    ]


GEN_TOTAL = SIGMA_INIT**2 + SIGMA_DATA**2
GEN_IN = GEN_TOTAL**-0.5
GEN_SKIP = SIGMA_DATA**2 / GEN_TOTAL
GEN_OUT = SIGMA_INIT * SIGMA_DATA * GEN_TOTAL**-0.5
T_IN, T_SKIP, T_OUT, T_SIGMA, T_FACTOR = range(5)


def fill_embed(eo, sigmas):
    at = lax.broadcasted_iota(jnp.int32, (8, 4 * C), 1)
    side = lax.broadcasted_iota(jnp.int32, (8, 4 * C), 0) // 4
    k = at // 2
    power = (k & (C - 1)).astype(F32) * (1.0 / C)
    rows = sigmas + [jnp.ones_like(sigmas[0])] * (4 - len(sigmas))
    angle = jnp.log(jnp.concatenate(rows + rows, axis=0)) * 0.25 * jnp.exp(power * -LOG_10000)
    wave = jnp.where(k < C, jnp.cos(angle), jnp.sin(angle))
    eo[...] = jnp.where((at & 1) == side, wave, 0.0).astype(BF16)


LOG_10000 = 9.210340371976184


def step_kernel(*refs):
    (
        z_all, eps_all, levels, counts, gen_w, fake_w, teacher_w, gen_small, fake_small,
        teacher_small,
        gw_out, sv_x, sv_h, sv_y, sv_q, sv_a, sv_o, sv_s, gshard, fshard, stot, sqtot,
        *refs,
    ) = refs
    gen_out = (sv_x, sv_h, sv_y, sv_q, sv_a, sv_o, sv_s)
    w_gen, w_fake, w_teach = refs[:3]
    sv_one, sv_two = refs[3:10], refs[10:17]
    bufs, nbuf, qkvw, tmp, dn, dqkv, act_t = refs[17:24]
    zb, eb, g, stage, local_sem, send_sem, recv_sem, copy_sem = refs[24:32]
    smalls, small_sem, gen_eo, score_eo, tab, sgrads, part_sums = refs[32:39]
    fake_refs, gen_refs = refs[39:44], refs[44:49]
    small_refs, square_refs = refs[49:53], refs[53:57]
    sib, free_sem = refs[57:59]
    g2 = sv_two[0].at[2]
    images = zb.shape[0]
    me = Place()
    start = me.sec * images

    def run(steps):
        for step in steps:
            step()

    def mine(ref):
        return ref.at[pl.ds(start, images)]

    loads = [
        pltpu.make_async_copy(mine(z_all), zb, copy_sem.at[0]),
        pltpu.make_async_copy(mine(eps_all), eb, copy_sem.at[1]),
    ]
    for copy in loads:
        copy.start()
    masters = [
        pltpu.make_async_copy(src, dst, copy_sem.at[2 + k])
        for k, (src, dst) in enumerate(((gen_w, gshard), (fake_w, fshard), (teacher_w, stage.at[2])))
    ]
    for copy in masters:
        copy.start()
    smalls[...] = jnp.zeros(smalls.shape, F32)
    for n, ref in enumerate((gen_small, fake_small, teacher_small)):
        for r in range(13):
            smalls[me.sec, n, r : r + 1, :] = ref[r]
    gathers = [
        Gather(me, net, stage.at[n], local_sem.at[n], send_sem.at[n], recv_sem.at[n])
        for n, net in enumerate((w_gen, w_fake, w_teach))
    ]
    for copy in masters:
        copy.wait()
    stage[0] = gshard[...].astype(BF16)
    stage[1] = fshard[...].astype(BF16)
    me.meet()
    gathers[0].begin()
    swap = remote(
        smalls.at[me.sec], smalls.at[me.sec], small_sem.at[0], small_sem.at[1], me.sib
    )
    swap.start()

    clear_pads(bufs)
    sgrads[...] = jnp.zeros(sgrads.shape, F32)
    sigmas = []
    valid_sum = jnp.zeros((1, 4 * C), F32)
    for i in range(images):
        level = jnp.zeros((1, 4 * C), jnp.int32) + levels[start + i]
        sigma = SIGMA_TOP + level.astype(F32) / (LEVELS - 1) * (SIGMA_BOTTOM - SIGMA_TOP)
        square = sigma * sigma
        sigma = square * square * square * sigma
        sigmas.append(sigma)
        s_in, s_skip, s_out, s_lam = precondition(sigma)
        valid = jnp.where(jnp.zeros_like(level) + (start + i) < counts[0], 1.0, 0.0)
        valid_sum = valid_sum + valid
        rows = (s_in, s_skip, s_out, sigma, valid * s_lam * (1.0 / (POS * C)))
        for k, value in enumerate(rows):
            tab[i, k : k + 1, :] = value[:, :C]
    fill_embed(score_eo, sigmas)
    fill_embed(gen_eo, [jnp.full((1, 4 * C), SIGMA_INIT, F32)] * images)

    def forward(n, w, eo, sv, pump):
        def body(l, _):
            layer_forward(
                l, w, smalls.at[:, n], eo, *sv, bufs, nbuf, qkvw, tmp, True, pump
            )
            return 0

        lax.fori_loop(0, 2, body, 0)

    def backward(n, w, eo, sv, cot, grad, sgrad, pump):
        def body(k, _):
            layer_backward(
                1 - k, w, smalls.at[:, n], eo, *sv, cot, bufs, nbuf, qkvw, tmp, dn, dqkv,
                act_t, grad, sgrad, pump,
            )
            return 0

        lax.fori_loop(0, 2, body, 0)

    def each(f):
        def body(i, carry):
            return f(i, [tab[i, k : k + 1, :] for k in range(5)], carry)

        return lax.fori_loop(0, images, body, jnp.zeros((1, C), F32))

    z_now, z_next = gathers[0].phase1(), gathers[1].phase1()
    run(z_now[:2] + [gathers[1].begin] + z_now[2:] + gathers[0].phase2() + z_next[:1])
    last = gathers[0].phase3()
    run(last[:4] + z_next[1:2] + [gathers[2].begin] + last[4:] + z_next[2:])
    for copy in loads:
        copy.wait()
    sv_one[0][0] = zb[...] * (GEN_IN * SIGMA_INIT)
    swap.wait()
    run(gathers[0].finish())
    later = gathers[1].phase2()
    forward(0, w_gen, gen_eo, sv_one, Pump(later[:5], FORWARD_POINTS, (0, 1)))
    pairs = [(w_gen, gw_out)] + list(zip(sv_one, gen_out))
    stores = [
        pltpu.make_async_copy(src, dst, copy_sem.at[2 + k]) for k, (src, dst) in enumerate(pairs)
    ]
    for copy in stores:
        copy.start()

    def noisy(i, t, carry):
        zb[i] = zb[i] * (GEN_SKIP * SIGMA_INIT) + GEN_OUT * sv_one[0][2, i]
        eb[i] = zb[i] + t[T_SIGMA] * eb[i]
        sv_two[0][0, i] = t[T_IN] * eb[i]
        return carry

    each(noisy)
    z_next, last = gathers[2].phase1(), gathers[1].phase3()
    run(later[5:] + z_next[:1] + last[:4] + z_next[1:2] + last[4:] + z_next[2:])
    run(gathers[1].finish())
    later = gathers[2].phase2()
    forward(1, w_fake, score_eo, sv_two, Pump(later[:5], FORWARD_POINTS, (0, 1)))
    later = later[5:] + gathers[2].phase3()

    def fake_loss(i, t, total):
        den = t[T_SKIP] * eb[i] + t[T_OUT] * sv_two[0][2, i]
        sv_two[0][2, i] = den
        miss = den - zb[i]
        g[i] = (2.0 * t[T_OUT] * t[T_FACTOR]) * miss
        return total + t[T_FACTOR] * colsum(miss * miss)

    loss_fake = each(fake_loss)
    for copy in stores:
        copy.wait()
    gathers[0].drain()
    backward(
        1, w_fake, score_eo, sv_two, g, w_gen, sgrads.at[:, 1],
        Pump(later, WEIGHT_POINTS, (1, 0), 0.0, 0.8),
    )
    fake_sum = Reduce(me, w_gen, fshard, sib, sib, *fake_refs)
    fake_sum.begin()
    run(gathers[2].finish())
    later = fake_sum.in_rows()
    sv_one[0][0] = sv_two[0][0]
    forward(2, w_teach, score_eo, sv_one, Pump(later[:4], FORWARD_POINTS, (0, 1), 0.2))

    def gen_loss(i, t, total):
        den = t[T_SKIP] * eb[i] + t[T_OUT] * sv_one[0][2, i]
        fake_den = sv_two[0][2, i]
        miss = fake_den - zb[i]
        gap = den - fake_den
        scale = t[T_OUT] * t[T_FACTOR]
        g[i] = scale * ((2.0 * (1.0 - ALPHA_MIX)) * gap + miss)
        g2[i] = scale * ((1.0 - 2.0 * (1.0 - ALPHA_MIX)) * gap - miss)
        zb[i] = (t[T_FACTOR] * (t[T_SKIP] - 1.0)) * gap
        return total + t[T_FACTOR] * colsum(gap * ((1.0 - ALPHA_MIX) * gap + miss))

    loss_gen = each(gen_loss)
    backward(
        2, w_teach, score_eo, sv_one, g, None, None, Pump(later[4:8], BACKWARD_POINTS, (1, 0), 0.1)
    )
    gathers[2].drain()
    fake_sum.drain(A_SLOT, B_SLOT)
    pl.semaphore_signal(free_sem, inc=1, device_id=me.sib, device_id_type=MESH)
    back = [
        pltpu.make_async_copy(src, dst, copy_sem.at[2 + k])
        for k, (dst, src) in enumerate([(w_teach, gw_out)] + list(zip(sv_one, gen_out)))
    ]
    for copy in back:
        copy.start()
    backward(
        1, w_fake, score_eo, sv_two, g2, None, None, Pump(later[8:], BACKWARD_POINTS, (1, 0))
    )

    def gen_gradient(i, t, carry):
        g[i] = GEN_OUT * (zb[i] + t[T_IN] * (g[i] + g2[i]))
        return carry

    each(gen_gradient)
    gathers[1].drain()
    for copy in back:
        copy.wait()

    gen_sum = Reduce(me, w_fake, gshard, w_gen.at[1 - me.sec], w_gen.at[me.sec], *gen_refs)
    later = gen_sum.steps()

    def on_section(s, steps):
        pl.when(me.sec == s)(lambda: run(steps))

    def hand_over():
        pl.semaphore_wait(free_sem, 1)

    pump = Pump([], WEIGHT_POINTS, (1, 0))

    def at(layer, point, section, steps):
        pump.table[layer][point].append(lambda: on_section(section, steps))

    upper = [hand_over, lambda: gen_sum.begin_block(0), lambda: gen_sum.begin_block(1)]
    lower = [lambda: gen_sum.begin_block(2), lambda: gen_sum.begin_block(3)]
    for layer, giver in ((1, 0), (0, 1)):
        at(layer, HALF_WAY, giver, upper)
        at(layer, READY, giver, lower)
    rows = gen_sum.in_rows()
    for k, point in enumerate((1, 3, 5, 6, 8, 11, 14, 17)):
        at(0, point, 1, rows[k : k + 1])
    at(0, READY, 0, later[:1])
    at(0, READY + 2, 0, later[1:2])
    at(0, READY + 4, 0, later[2:3])
    backward(0, w_teach, gen_eo, sv_one, g, w_fake, sgrads.at[:, 0], pump)

    def spread_sum(total):
        return jnp.broadcast_to(jnp.sum(total, axis=1, keepdims=True), (1, C))

    sums = jnp.concatenate([spread_sum(loss_gen), spread_sum(loss_fake), valid_sum[:, :C]], axis=0)
    for s in range(2):
        part_sums[s, 0:16, :] = sgrads[s, 0]
        part_sums[s, 13:16, :] = sums
        part_sums[s, 16:32, :] = sgrads[s, 1]
    small = Totals(me, *small_refs)
    small_refs[0][0] = part_sums[me.sec]
    small.begin(part_sums.at[1 - me.sec])
    fake_sum.stage_e()
    small_steps = small.steps()
    on_section(0, later[3:6])
    on_section(1, rows[8:])
    run(small_steps[:1])
    on_section(0, later[6:8])
    run(small_steps[1:2])
    on_section(0, later[8:10])
    run(small_steps[2:])
    on_section(0, later[10:])
    stot[...] = small.result()
    own = square_refs[0]
    keep = lax.broadcasted_iota(jnp.int32, (16, C), 0) < 13
    for n, rows in ((1, fshard), (0, gshard)):
        if n == 0:
            gen_sum.stage_e()
        low = jnp.square(jnp.where(keep, stot[16 * n : 16 * n + 16, :], 0.0))
        low = jnp.where(me.d == 0, low[0:8] + low[8:16], 0.0)
        big = jnp.sum(jnp.square(rows[...]).reshape(rows.shape[0] // 8, 8, C), axis=0)
        own[0, 8 * n : 8 * n + 8, :] = big + low
    square = Squares(me, *square_refs)
    sqtot[...] = square.run()
    fake_sum.drain(B_SLOT)
    for done in (gen_sum, small, square):
        done.drain()


SIGMA_TOP = SIGMA_HIGH ** (1.0 / RHO_POWER)
SIGMA_BOTTOM = SIGMA_LOW ** (1.0 / RHO_POWER)


def run_step(z, eps, levels, counts, gen_w, fake_w, teacher_w, smalls):
    part = gen_w.shape[0]
    images = z.shape[0] // 2
    any_ = pl.BlockSpec(memory_space=pl.ANY)
    smem = pl.BlockSpec(memory_space=pltpu.SMEM)
    saved = saved_shapes(images)
    return pl.pallas_call(
        step_kernel,
        out_shape=[jax.ShapeDtypeStruct((2, ROWS, C), BF16)]
        + saved
        + [
            jax.ShapeDtypeStruct((part, C), F32),
            jax.ShapeDtypeStruct((part, C), F32),
            jax.ShapeDtypeStruct((32, C), F32),
            jax.ShapeDtypeStruct((16, C), F32),
        ],
        in_specs=[any_] * 2 + [smem] * 2 + [any_] * 3 + vm(3),
        out_specs=[any_] * 8 + vm(4),
        scratch_shapes=[pltpu.VMEM((2, ROWS, C), BF16)] * 3
        + saved_scratch(images) * 2
        + backward_scratch(images)
        + [pltpu.VMEM((images, POS, C), F32)] * 3
        + [
            pltpu.VMEM((3, part, C), BF16),
            pltpu.SemaphoreType.DMA((3,)),
            pltpu.SemaphoreType.DMA((3, SLOTS)),
            pltpu.SemaphoreType.DMA((3, SLOTS)),
            pltpu.SemaphoreType.DMA((10,)),
            pltpu.VMEM((2, 3, 16, C), F32),
            pltpu.SemaphoreType.DMA((2,)),
            pltpu.VMEM((8, 4 * C), BF16),
            pltpu.VMEM((8, 4 * C), BF16),
            pltpu.VMEM((images, 8, C), F32),
            pltpu.VMEM((2, 2, 16, C), F32),
            pltpu.VMEM((2, 32, C), F32),
        ]
        + reduce_scratch(part) * 2
        + totals_scratch((32, C))
        + squares_scratch((16, C))
        + [pltpu.VMEM((ROWS, C), BF16), pltpu.SemaphoreType.REGULAR],
        compiler_params=pltpu.CompilerParams(
            collective_id=0, has_side_effects=True, vmem_limit_bytes=STEP_LIMIT
        ),
    )(z, eps, levels, counts, gen_w, fake_w, teacher_w, *smalls)[8:]


def adam_step(master, first_mom, second_mom, grad):
    first_new = BETA_ONE * first_mom + (1.0 - BETA_ONE) * grad
    second_new = BETA_TWO * second_mom + (1.0 - BETA_TWO) * grad * grad
    direction = (
        first_new
        / (1.0 - BETA_ONE**STEP)
        / (jnp.sqrt(second_new / (1.0 - BETA_TWO**STEP)) + ADAM_EPS)
    )
    return (master - LEARN_RATE * (direction + WEIGHT_DECAY * master), first_new, second_new)


EMA_RATE = 0.5 ** (20.0 / STEP)
SMALL_STATES = (4, 5, 6, 7, 11, 12, 13)


def update_kernel(gshard, fshard, stot, sqtot, *refs):
    ins, outs = refs[:14], refs[14:]
    norms, losses = outs[14:]
    count = stot[15:16, 0:1]
    norm_of, scales = [], []
    for n in range(2):
        rows = jnp.sum(sqtot[8 * n : 8 * n + 8, :], axis=0, keepdims=True)
        norm = jnp.sqrt(jnp.sum(rows, axis=1, keepdims=True)) / count
        scales.append(jnp.minimum(1.0, CLIP_NORM / norm) / count)
        norm_of.append(norm)

    def one(at, grad, w, m, v, ema, ow, om, ov, oe):
        new, first, second = adam_step(w[at], m[at], v[at], grad)
        ow[at] = new
        om[at] = first
        ov[at] = second
        if ema is not None:
            oe[at] = EMA_RATE * ema[at] + (1.0 - EMA_RATE) * new

    one(0, gshard[...] * scales[0], *ins[0:4], *outs[0:4])
    one(0, fshard[...] * scales[1], *ins[8:11], None, *outs[8:11], None)

    first = lax.broadcasted_iota(jnp.int32, (1, 2), 1) == 0
    norms[...] = jnp.where(first, norm_of[0], norm_of[1])
    losses[...] = jnp.where(first, stot[13:14, 0:1], stot[14:15, 0:1]) / count
    for k in range(13):
        one(k, stot[k : k + 1, :] * scales[0], *ins[4:8], *outs[4:8])
        one(k, stot[16 + k : 17 + k, :] * scales[1], *ins[11:14], None, *outs[11:14], None)


def update_nets(gshard, fshard, stot, sqtot, states):
    def turned(arrays):
        return [a.swapaxes(0, 1) if k in SMALL_STATES else a for k, a in enumerate(arrays)]

    states = turned(states)
    res = pl.pallas_call(
        update_kernel,
        out_shape=[jax.ShapeDtypeStruct(a.shape, F32) for a in states]
        + [jax.ShapeDtypeStruct((1, 2), F32)] * 2,
        in_specs=vm(4 + len(states)),
        out_specs=vm(2 + len(states)),
        compiler_params=pltpu.CompilerParams(vmem_limit_bytes=VMEM_LIMIT),
    )(gshard, fshard, stot, sqtot, *states)
    return tuple(turned(res[:-2])) + (res[-2][0], res[-1][0])


def gather_plain(shard):
    rows = lax.all_gather(shard.astype(BF16), "dp", axis=1, tiled=True)
    return lax.all_gather(rows, "section", axis=0, tiled=True)


def reduce_plain(bigs, small):
    shards_, squares = [], []
    own = lax.psum_scatter(small, "section", scatter_dimension=0, tiled=True)
    stot = lax.psum(own, "dp")[0]
    first = lax.axis_index("dp") == 0
    for n, big in enumerate(bigs):
        own = lax.psum_scatter(big, "section", scatter_dimension=0, tiled=True)
        own = lax.psum_scatter(own, "dp", scatter_dimension=1, tiled=True)[0].astype(F32)
        shards_.append(own)
        low = jnp.sum(jnp.square(stot[16 * n : 16 * n + 13]))
        squares.append(jnp.sum(own * own) + jnp.where(first, low, 0.0))
    sq = lax.psum(jnp.stack(squares), ("section", "dp"))
    return *shards_, stot, jnp.zeros((16, C), F32).at[jnp.array([0, 8]), 0].set(sq)


def shards(
    z_noise, eps_noise, levels, counts,
    gen_w, gen_m, gen_v, gen_ema, gen_small, gen_small_m, gen_small_v, gen_small_ema,
    fake_w, fake_m, fake_v, fake_small, fake_small_m, fake_small_v,
    teacher_w, teacher_small,
):
    if lax.axis_size("dp") == PLANES * PLANE:
        smalls = [a.swapaxes(0, 1) for a in (gen_small, fake_small, teacher_small)]
        reduced = run_step(
            z_noise, eps_noise, levels, counts, gen_w[0], fake_w[0], teacher_w[0], smalls
        )
    else:
        reduced = plain_step(
            z_noise, eps_noise, levels, counts, gen_w, fake_w, teacher_w,
            gen_small, fake_small, teacher_small,
        )
    return update_nets(
        *reduced,
        (
            gen_w, gen_m, gen_v, gen_ema, gen_small, gen_small_m, gen_small_v, gen_small_ema,
            fake_w, fake_m, fake_v, fake_small, fake_small_m, fake_small_v,
        ),
    )


def plain_step(
    z_noise, eps_noise, levels, counts, gen_w, fake_w, teacher_w,
    gen_small, fake_small, teacher_small,
):
    images = z_noise.shape[0] // lax.axis_size("section")
    start = lax.axis_index("section") * images

    def mine(a):
        return lax.dynamic_slice_in_dim(a, start, images, 0)

    z, eps = mine(z_noise), mine(eps_noise)
    sigma = sigma_levels(mine(levels))
    valid = (start + jnp.arange(images) < counts[0]).astype(F32)
    valid_sum = jnp.sum(valid)
    gen_eo = spread_embed(jnp.full((images,), SIGMA_INIT, F32))
    score_eo = spread_embed(sigma)
    gs, fs, ts = [
        lax.all_gather(a, "section", axis=0, tiled=True)
        for a in (gen_small, fake_small, teacher_small)
    ]
    gw, fw, tw = gather_plain(gen_w), gather_plain(fake_w), gather_plain(teacher_w)
    s_in, s_skip, s_out, s_lam = precondition(sigma)
    factor = valid * s_lam / (POS * C)
    s_in, s_skip, s_out, sigma, factor = [
        t[:, None, None] for t in (s_in, s_skip, s_out, sigma, factor)
    ]
    raw = SIGMA_INIT * z
    gen_saved = run_forward(GEN_IN * raw, gw, gs, gen_eo)
    samples = GEN_SKIP * raw + GEN_OUT * gen_saved[0][2]
    noisy = samples + sigma * eps
    x0 = s_in * noisy
    fake_saved = run_forward(x0, fw, fs, score_eo)
    fake_den = s_skip * noisy + s_out * fake_saved[0][2]
    miss = fake_den - samples
    _, fake_g, fake_sg = run_backward(
        s_out * 2.0 * factor * miss, fw, fs, score_eo, fake_saved, True
    )
    teacher_saved = run_forward(x0, tw, ts, score_eo)
    teacher_den = s_skip * noisy + s_out * teacher_saved[0][2]
    gap = teacher_den - fake_den
    loss_gen = jnp.sum(factor * ((1.0 - ALPHA_MIX) * gap * gap + gap * miss))
    loss_fake = jnp.sum(factor * miss * miss)
    grad_teacher = factor * (2.0 * (1.0 - ALPHA_MIX) * gap + miss)
    grad_fake = factor * gap - grad_teacher
    direct = factor * gap * (s_skip - 1.0)
    (back_t,) = run_backward(s_out * grad_teacher, tw, ts, score_eo, teacher_saved, False)
    (back_f,) = run_backward(s_out * grad_fake, fw, fs, score_eo, fake_saved, False)
    gen_cot = GEN_OUT * (direct + s_in * (back_t + back_f))
    _, gen_g, gen_sg = run_backward(gen_cot, gw, gs, gen_eo, gen_saved, True)
    scalars = jnp.broadcast_to(jnp.stack([loss_gen, loss_fake, valid_sum])[:, None], (3, C))
    small_sums = jnp.concatenate(
        [gen_sg[:, :13], jnp.broadcast_to(scalars, (2, 3, C)), fake_sg], axis=1
    )
    return reduce_plain((gen_g, fake_g), small_sums)


def solution(mesh):
    images = P("dp", None, None)
    big = P("section", "dp", None)
    small = P("section", None, None)
    return jax.shard_map(
        shards,
        mesh=mesh,
        in_specs=(images, images, P("dp"), P("dp"))
        + (big,) * 4 + (small,) * 4 + (big,) * 3 + (small,) * 3 + (big, small),
        out_specs=(big,) * 4 + (small,) * 4 + (big,) * 3 + (small,) * 3 + (P(), P()),
        check_vma=False,
    )
```

```python
import functools

import jax
import jax.numpy as jnp
from jax import lax
from jax.experimental import pallas as pl
from jax.experimental.pallas import tpu as pltpu
from jax.sharding import PartitionSpec as P

GROUPS = 32
SIDE = 16
LEVELS = 1000
STEP = 10

SIGMA_DATA = 0.5
SIGMA_INIT = 2.5
SIGMA_LOW = 0.05
SIGMA_HIGH = 20.0
RHO_POWER = 7.0
ALPHA_MIX = 1.2
RS = 0.7071067811865476
NORM_EPS = 1e-05
CLIP_NORM = 0.001
LEARN_RATE = 0.15
BETA_ONE = 0.9
BETA_TWO = 0.999
ADAM_EPS = 1e-08
WEIGHT_DECAY = 0.01

C = 256
HALF = 128
POS = 256
ROWS = 26 * C
CHUNK = 64
PAD = SIDE
F32 = jnp.float32
BF16 = jnp.bfloat16
VMEM_LIMIT = 58 * 2**20
STEP_LIMIT = 63 * 2**20

R_CONV1, R_CONV2, R_EMB, R_QKV, R_PROJ = 0, 9 * C, 18 * C, 22 * C, 25 * C
S_M1, S_I1, S_M2, S_I2, S_M3, S_I3, S_MA, S_MB = range(8)


def sigma_levels(level_ids):
    fraction = level_ids.astype(F32) / (LEVELS - 1)
    top_root = SIGMA_HIGH ** (1.0 / RHO_POWER)
    bottom_root = SIGMA_LOW ** (1.0 / RHO_POWER)
    return (top_root + fraction * (bottom_root - top_root)) ** RHO_POWER


def precondition(sigma_vals):
    total = sigma_vals * sigma_vals + SIGMA_DATA**2
    return (
        lax.rsqrt(total),
        SIGMA_DATA**2 / total,
        sigma_vals * SIGMA_DATA * lax.rsqrt(total),
        total / (sigma_vals * sigma_vals * SIGMA_DATA**2),
    )


def noise_embed(sigma_vals, channel_count):
    frequency = (1.0 / 10000.0) ** (jnp.arange(channel_count, dtype=F32) / channel_count)
    angles = (jnp.log(sigma_vals) / 4.0)[..., None] * frequency
    return jnp.concatenate([jnp.cos(angles), jnp.sin(angles)], axis=-1)


def spread_embed(sigma_vals):
    emb = noise_embed(sigma_vals, C).astype(BF16)
    images = emb.shape[0]
    zero = jnp.zeros_like(emb)
    low = jnp.stack([emb, zero], axis=-1).reshape(images, 4 * C)
    high = jnp.stack([zero, emb], axis=-1).reshape(images, 4 * C)
    fill = jnp.zeros((4 - images, 4 * C), BF16)
    return jnp.concatenate([low, fill, high, fill], axis=0)


def dot_nn(a, b):
    return lax.dot_general(a, b, (((1,), (0,)), ((), ())), preferred_element_type=F32)


def dot_nt(a, b):
    return lax.dot_general(a, b, (((1,), (1,)), ((), ())), preferred_element_type=F32)


def dot_tn(a, b):
    return lax.dot_general(a, b, (((0,), (0,)), ((), ())), preferred_element_type=F32)


def group_mean(v):
    lane = lax.broadcasted_iota(jnp.int32, (8, C), 1)
    for sh in (1, 2, 4):
        v = v + jnp.where((lane & sh) != 0, pltpu.roll(v, sh, 1), pltpu.roll(v, C - sh, 1))
    return v * (1.0 / (POS * 8))


def colsum(v):
    return jnp.sum(v, axis=0, keepdims=True)


def no_pump(l):
    pass


FORWARD_POINTS, BACKWARD_POINTS, WEIGHT_POINTS = 10, 12, 18
HALF_WAY, READY = 8, 13


def stagger(steps, images, between):
    for t in range(len(steps) + images - 1):
        for i in range(images):
            if 0 <= t - i < len(steps):
                steps[t - i](i)
        between()


class Pump:
    def __init__(self, steps, points, layers, lo=0.0, hi=1.0):
        self.table = {l: [[] for _ in range(points)] for l in layers}
        self.at = 0
        for k, step in enumerate(steps):
            place = int((lo + (hi - lo) * (k + 0.5) / len(steps)) * points * len(layers))
            self.table[layers[place // points]][place % points].append(step)

    def __call__(self, l):
        for layer, points in self.table.items():
            if points[self.at]:

                @pl.when(l == layer)
                def _(todo=points[self.at]):
                    for step in todo:
                        step()

        self.at += 1


def put_shifted(bufs, i, r, v):
    rows = v.shape[0]
    at = pl.ds(PAD + r, rows)
    sub = lax.broadcasted_iota(jnp.int32, (rows // SIDE, 8, C), 1)
    x = v.reshape(rows // SIDE, 2, 8, C)
    low, high = x[:, 0], x[:, 1]
    low_up, high_up = pltpu.roll(low, 1, 1), pltpu.roll(high, 1, 1)
    low_down, high_down = pltpu.roll(low, 7, 1), pltpu.roll(high, 7, 1)
    left = (jnp.where(sub == 0, 0.0, low_up), jnp.where(sub == 0, low_up, high_up))
    right = (jnp.where(sub == 7, high_down, low_down), jnp.where(sub == 7, 0.0, high_down))
    bufs[0, i, at, :] = jnp.stack(left, axis=1).reshape(rows, C).astype(BF16)
    bufs[1, i, at, :] = v.astype(BF16)
    bufs[2, i, at, :] = jnp.stack(right, axis=1).reshape(rows, C).astype(BF16)


def taps(bufs, flip):
    images = bufs.shape[1]
    out = []
    for dr in (-1, 0, 1):
        for dc in (-1, 0, 1):
            sr, sc = (-dr, -dc) if flip else (dr, dc)
            piece = bufs[sc + 1, :, PAD + SIDE * sr : PAD + SIDE * sr + POS, :]
            out.append(piece.reshape(images * POS, C))
    return out


def conv_forward(bufs, w, l, row):
    return dot_nn(jnp.concatenate(taps(bufs, False), axis=1), w[l, row : row + 9 * C, :])


def conv_input_grad(bufs, w, l, row):
    parts = [w[l, row + t * C : row + (t + 1) * C, :] for t in range(9)]
    return dot_nt(jnp.concatenate(taps(bufs, True), axis=1), jnp.concatenate(parts, axis=1))


def conv_weight_grad(act_t, bufs, grad, l, row):
    left = act_t[...]
    for t, piece in enumerate(taps(bufs, True)):
        grad[l, row + t * C : row + (t + 1) * C, :] = dot_nn(left, piece).astype(BF16)


def silu(v):
    h = 0.5 * v
    return h + h * jnp.tanh(h)


def silu_parts(v):
    h = 0.5 * v
    t = jnp.tanh(h)
    return h + h * t, (1.0 + t) + h * (1.0 - t * t)


def clear_pads(bufs):
    zero = jnp.zeros(bufs.shape[:2] + (PAD, C), BF16)
    bufs[:, :, 0:PAD, :] = zero
    bufs[:, :, PAD + POS :, :] = zero


def split_qkv(w, l, qkvw, tmp):
    for h in range(2):
        tmp[h] = w[l, R_QKV : R_QKV + 3 * C, h * HALF : (h + 1) * HALF].astype(F32)
    for j in range(3):
        for h in range(2):
            at = j * C + h * HALF
            qkvw[:, at : at + HALF] = tmp[h, pl.ds(j, C, stride=3), :].astype(BF16)


def norm_sums(x):
    pivot = x[0:1]
    d = x - pivot
    return colsum(d), colsum(d * d), pivot


def norm_stats(sums):
    fill = [jnp.zeros((4 - len(sums), C), F32)]
    s1, s2, pivot = [jnp.concatenate([a[k] for a in sums] + fill, axis=0) for k in range(3)]
    centre = group_mean(jnp.concatenate([pivot, pivot], axis=0) * POS)[0:4]
    off = pivot - centre
    first = s1 + POS * off
    second = s2 + off * (2.0 * s1 + POS * off)
    means = group_mean(jnp.concatenate([first, second], axis=0))
    spread = jnp.maximum(means[4:8] - jnp.square(means[0:4]), 0.0)
    return centre + means[0:4], lax.rsqrt(spread + NORM_EPS)


def norm_map(gain, mg, mc, mean, inv):
    on_value = inv * inv * mc
    return inv * gain, on_value, inv * mg - mean * on_value


def two_means(a, b):
    rows = jnp.concatenate([a, b] * 4, axis=0)
    means = group_mean(rows)
    return means[0:1], means[1:2]


def tap_rows(bufs, flip, which):
    out = []
    for dr in (-1, 0, 1):
        for dc in (-1, 0, 1):
            sr, sc = (-dr, -dc) if flip else (dr, dc)
            at = slice(PAD + SIDE * sr, PAD + SIDE * sr + POS)
            piece = jnp.concatenate([bufs[sc + 1, i, at, :] for i in which], axis=0)
            out.append(piece)
    return out


def layer_forward(l, w, small, eo, xs, h1, y, qkv, att, o, st, bufs, nbuf, qkvw, tmp, staged, pump):
    images = h1.shape[1]
    split_qkv(w, l, qkvw, tmp)
    mod = dot_nn(eo[...], w[l, R_EMB : R_EMB + 4 * C, :])
    ma = mod[0:4] + small[l, 5:6, :]
    mb = mod[4:8] + small[l, 6:7, :]
    for i in range(images):
        st[l, i, S_MA : S_MA + 1, :] = ma[i : i + 1]
        st[l, i, S_MB : S_MB + 1, :] = mb[i : i + 1]

    sums = {}

    def row(k):
        return small[l, k : k + 1, :]

    def keep(which, mean, inv, at):
        for k, i in enumerate(which):
            st[l, i, at : at + 1, :] = mean[k : k + 1]
            st[l, i, at + 1 : at + 2, :] = inv[k : k + 1]

    def first(which):
        mean, inv = norm_stats([norm_sums(xs[l, i]) for i in which])
        keep(which, mean, inv, S_M1)
        for k, i in enumerate(which):
            a = inv[k : k + 1] * row(0)
            b = row(1) - mean[k : k + 1] * a
            for r in range(0, POS, CHUNK):
                v = xs[l, i, r : r + CHUNK, :] * a + b
                put_shifted(bufs, i, r, silu(v))

    def conv(which, at):
        left = jnp.concatenate(tap_rows(bufs, False, which), axis=1)
        return dot_nn(left, w[l, at : at + 9 * C, :])

    def conv_one(which):
        out = conv(which, R_CONV1)
        for k, i in enumerate(which):
            own = out[k * POS : (k + 1) * POS]
            own = own + row(2)
            sums[i] = norm_sums(own)
            h1[l, i] = own

    def second(which):
        mean, inv = norm_stats([sums[i] for i in which])
        keep(which, mean, inv, S_M2)
        for k, i in enumerate(which):
            gain = 1.0 + ma[i : i + 1]
            a = inv[k : k + 1] * row(3) * gain
            b = row(4) * gain + mb[i : i + 1] - mean[k : k + 1] * a
            for r in range(0, POS, CHUNK):
                v = h1[l, i, r : r + CHUNK, :] * a + b
                put_shifted(bufs, i, r, silu(v))

    def conv_two(which):
        out = conv(which, R_CONV2) + row(7)
        for k, i in enumerate(which):
            own = (xs[l, i] + out[k * POS : (k + 1) * POS]) * RS
            sums[i] = norm_sums(own)
            y[l, i] = own

    def third(which):
        mean, inv = norm_stats([sums[i] for i in which])
        keep(which, mean, inv, S_M3)
        for k, i in enumerate(which):
            a = inv[k : k + 1] * row(8)
            b = row(9) - mean[k : k + 1] * a
            for r in range(0, POS, CHUNK):
                v = y[l, i, r : r + CHUNK, :] * a + b
                nbuf[i, r : r + CHUNK, :] = v.astype(BF16)

    def project_in(which):
        n = jnp.concatenate([nbuf[i] for i in which], axis=0)
        for j, at in ((0, 10), (1, None), (2, 11)):
            part = dot_nn(n, qkvw[:, j * C : (j + 1) * C])
            if at is not None:
                part = part + row(at)
            part = part.astype(BF16)
            for k, i in enumerate(which):
                qkv[l, i, :, j * C : (j + 1) * C] = part[k * POS : (k + 1) * POS]

    def attend(which):
        scores = [dot_nt(qkv[l, i, :, 0:C], qkv[l, i, :, C : 2 * C]) for i in which]
        for s, i in zip(scores, which):
            e = jnp.exp((s - jnp.max(s, axis=1, keepdims=True)) * (C**-0.5))
            p = (e * (1.0 / jnp.sum(e, axis=1, keepdims=True))).astype(BF16)
            att[l, i] = p
            o[l, i] = dot_nn(p, qkv[l, i, :, 2 * C :]).astype(BF16)

    def project_out(which):
        left = jnp.concatenate([o[l, i] for i in which], axis=0)
        out = dot_nn(left, w[l, R_PROJ:, :]) + row(12)
        for k, i in enumerate(which):
            xs[l + 1, i] = (y[l, i] + out[k * POS : (k + 1) * POS]) * RS

    steps = (first, conv_one, second, conv_two, third, project_in, attend, project_out)
    if not staged:
        for step in steps:
            step(range(images))
            pump(l)
    else:
        stagger([lambda i, step=step: step([i]) for step in steps], images, lambda: pump(l))


def layer_backward(
    l, w, small, eo, xs, h1, y, qkv, att, o, st, g, bufs, nbuf, qkvw, tmp, dn, dqkv, act_t,
    grad, sgrad, pump, need_dx=None,
):
    want = grad is not None
    images = h1.shape[1]
    which = range(images)
    flat = images * POS
    scale = C**-0.5
    split_qkv(w, l, qkvw, tmp)

    def row(k):
        return small[l, k : k + 1, :]

    def rows8(rows):
        return jnp.concatenate(list(rows) + [jnp.zeros((8 - len(rows), C), F32)], axis=0)

    zero = jnp.zeros((1, C), F32)
    gps, c1, c2, p1, p2 = {}, {}, {}, {}, {}
    total = {7: zero, 2: zero}
    gains = [1.0 + st[l, i, S_MA : S_MA + 1, :] for i in which]

    def project_out(i):
        gps[i] = (g[i] * RS).astype(BF16)
        nbuf[i] = dot_nt(gps[i], w[l, R_PROJ:, :]).astype(BF16)

    def attend(i):
        p = att[l, i]
        pf = p.astype(F32)
        dp = dot_nt(nbuf[i], qkv[l, i, :, 2 * C :])
        ds = (pf * (dp - jnp.sum(dp * pf, axis=1, keepdims=True))).astype(BF16)
        dqkv[i, :, 0:C] = (dot_nn(ds, qkv[l, i, :, C : 2 * C]) * scale).astype(BF16)
        dqkv[i, :, C : 2 * C] = (dot_tn(ds, qkv[l, i, :, 0:C]) * scale).astype(BF16)
        dqkv[i, :, 2 * C :] = dot_tn(p, nbuf[i]).astype(BF16)

    def project_in(i):
        mean, inv = st[l, i, S_M3 : S_M3 + 1, :], st[l, i, S_I3 : S_I3 + 1, :]
        d = dot_nt(dqkv[i], qkvw[...])
        dn[i] = d
        c1[i] = colsum(d)
        c2[i] = colsum(d * (y[l, i] - mean)) * inv

    def third(i):
        mean, inv = st[l, i, S_M3 : S_M3 + 1, :], st[l, i, S_I3 : S_I3 + 1, :]
        mg, mc = two_means(row(8) * c1[i], row(8) * c2[i])
        on_grad, on_value, offset = norm_map(row(8) * RS, mg * RS, mc * RS, mean, inv)
        act_a = inv * row(8)
        act_b = row(9) - mean * act_a
        for r in range(0, POS, CHUNK):
            value = y[l, i, r : r + CHUNK, :]
            gm = g[i, r : r + CHUNK, :] * (RS * RS) + dn[i, r : r + CHUNK, :] * on_grad
            gm = gm - (value * on_value + offset)
            g[i, r : r + CHUNK, :] = gm
            put_shifted(bufs, i, r, gm)
            if want:
                nbuf[i, r : r + CHUNK, :] = (value * act_a + act_b).astype(BF16)
                total[7] = total[7] + colsum(gm)

    def conv_grad(i, at):
        left = jnp.concatenate(tap_rows(bufs, True, [i]), axis=1)
        parts = [w[l, at + t * C : at + (t + 1) * C, :] for t in range(9)]
        dn[i] = dot_nt(left, jnp.concatenate(parts, axis=1))

    def activation(i, src, mean, inv, a, b, act=None):
        s1, s2 = zero, zero
        for r in range(0, POS, CHUNK):
            u = src[l, i, r : r + CHUNK, :] - mean
            act_value, slope = silu_parts(u * (inv * a) + b)
            d = dn[i, r : r + CHUNK, :] * slope
            dn[i, r : r + CHUNK, :] = d
            s1 = s1 + colsum(d)
            s2 = s2 + colsum(d * u)
            if act is not None:
                act[i, r : r + CHUNK, :] = act_value.astype(BF16)
        p1[i], p2[i] = s1 * 0.5, s2 * (0.5 * inv)

    def second_a(i):
        mean, inv = st[l, i, S_M2 : S_M2 + 1, :], st[l, i, S_I2 : S_I2 + 1, :]
        b = row(4) * gains[i] + st[l, i, S_MB : S_MB + 1, :]
        activation(i, h1, mean, inv, row(3) * gains[i], b, nbuf if want else None)

    def second_b(i):
        mean, inv = st[l, i, S_M2 : S_M2 + 1, :], st[l, i, S_I2 : S_I2 + 1, :]
        full = row(3) * gains[i]
        mg, mc = two_means(full * p1[i], full * p2[i])
        on_grad, on_value, offset = norm_map(full, mg, mc, mean, inv)
        for r in range(0, POS, CHUNK):
            dh = dn[i, r : r + CHUNK, :] * (0.5 * on_grad) - (
                h1[l, i, r : r + CHUNK, :] * on_value + offset
            )
            put_shifted(bufs, i, r, dh)
            if want:
                total[2] = total[2] + colsum(dh)

    def first_a(i):
        mean, inv = st[l, i, S_M1 : S_M1 + 1, :], st[l, i, S_I1 : S_I1 + 1, :]
        activation(i, xs, mean, inv, row(0), row(1))

    def first_act(i):
        mean, inv = st[l, i, S_M1 : S_M1 + 1, :], st[l, i, S_I1 : S_I1 + 1, :]
        a = inv * row(0)
        b = row(1) - mean * a
        for r in range(0, POS, CHUNK):
            v = xs[l, i, r : r + CHUNK, :] * a + b
            nbuf[i, r : r + CHUNK, :] = silu(v).astype(BF16)

    def first_b(i):
        mean, inv = st[l, i, S_M1 : S_M1 + 1, :], st[l, i, S_I1 : S_I1 + 1, :]
        mg, mc = two_means(row(0) * p1[i], row(0) * p2[i])
        on_grad, on_value, offset = norm_map(row(0), mg, mc, mean, inv)
        for r in range(0, POS, CHUNK):
            dx = dn[i, r : r + CHUNK, :] * (0.5 * on_grad) - (
                xs[l, i, r : r + CHUNK, :] * on_value + offset
            )
            g[i, r : r + CHUNK, :] = g[i, r : r + CHUNK, :] + dx

    upper = [project_out, attend, project_in, third, lambda i: conv_grad(i, R_CONV2)]
    lower = [lambda i: conv_grad(i, R_CONV1), first_a]
    if not want:
        stagger(upper + [second_a, second_b] + lower + [first_b], images, lambda: pump(l))
        return
    stagger(upper, images, lambda: pump(l))
    gp = jnp.concatenate([gps[i] for i in which], axis=0)
    grad[l, R_PROJ:, :] = dot_tn(o[l].reshape(flat, C), gp).astype(BF16)
    sgrad[l, 12:13, :] = colsum(gp.astype(F32))
    sgrad[l, 7:8, :] = total[7]
    sgrad[l, 8:9, :] = colsum(rows8([c2[i] for i in which]))
    sgrad[l, 9:10, :] = colsum(rows8([c1[i] for i in which]))
    act_t[...] = nbuf[...].reshape(flat, C).T
    for j in range(3):
        dj = dqkv[:, :, j * C : (j + 1) * C].reshape(flat, C)
        part = dot_nn(act_t[...], dj)
        for h in range(2):
            tmp[h, pl.ds(j, C, stride=3), :] = part[:, h * HALF : (h + 1) * HALF]
        if j != 1:
            sgrad[l, 10 + j // 2 : 11 + j // 2, :] = colsum(dj.astype(F32))
    for h in range(2):
        grad[l, R_QKV : R_QKV + 3 * C, h * HALF : (h + 1) * HALF] = tmp[h].astype(BF16)
    for i in which:
        second_a(i)
    pump(l)
    act_t[...] = nbuf[...].reshape(flat, C).T
    conv_weight_grad(act_t, bufs, grad, l, R_CONV2)
    p18, p28, modgain = [rows8([a[i] for i in which]) for a in (p1, p2, gains)]
    dma = row(3) * p28 + row(4) * p18
    sgrad[l, 3:4, :] = colsum(modgain * p28)
    sgrad[l, 4:5, :] = colsum(modgain * p18)
    sgrad[l, 5:6, :] = colsum(dma)
    sgrad[l, 6:7, :] = colsum(p18)
    grad[l, R_EMB : R_EMB + 4 * C, :] = embed_grad(
        eo, jnp.concatenate([dma[0:4], p18[0:4]], axis=0)
    ).astype(BF16)
    pump(l)
    stagger([second_b, first_act], images, lambda: pump(l))
    act_t[...] = nbuf[...].reshape(flat, C).T
    conv_weight_grad(act_t, bufs, grad, l, R_CONV1)
    pump(l)
    stagger(lower, images, lambda: pump(l))
    sgrad[l, 2:3, :] = total[2]
    sgrad[l, 0:1, :] = colsum(rows8([p2[i] for i in which]))
    sgrad[l, 1:2, :] = colsum(rows8([p1[i] for i in which]))

    @pl.when(l == 1)
    def _():
        for i in which:
            first_b(i)


def embed_grad(eo, dm):
    parts, rest = [], dm
    for _ in range(3):
        parts.append(rest.astype(BF16))
        rest = rest - parts[-1].astype(F32)
    left = eo[...]
    return dot_tn(jnp.concatenate([left, left], axis=0), jnp.concatenate(parts[:2], axis=0)) + dot_tn(
        left, parts[2]
    )


def saved_shapes(images):
    return [
        jax.ShapeDtypeStruct((3, images, POS, C), F32),
        jax.ShapeDtypeStruct((2, images, POS, C), F32),
        jax.ShapeDtypeStruct((2, images, POS, C), F32),
        jax.ShapeDtypeStruct((2, images, POS, 3 * C), BF16),
        jax.ShapeDtypeStruct((2, images, POS, POS), BF16),
        jax.ShapeDtypeStruct((2, images, POS, C), BF16),
        jax.ShapeDtypeStruct((2, images, 8, C), F32),
    ]


def forward_kernel(staged, x0, w, small, eo, xs, h1, y, qkv, att, o, st, bufs, nbuf, qkvw, tmp):
    clear_pads(bufs)
    xs[0] = x0[...]

    def body(l, _):
        layer_forward(
            l, w, small, eo, xs, h1, y, qkv, att, o, st, bufs, nbuf, qkvw, tmp, staged, no_pump
        )
        return 0

    lax.fori_loop(0, 2, body, 0)


def backward_kernel(want, *refs):
    cot, w, small, eo, xs, h1, y, qkv, att, o, st, g = refs[:12]
    refs = refs[12:]
    if want:
        grad, sgrad = refs[:2]
        refs = refs[2:]
    else:
        grad, sgrad = None, None
    bufs, nbuf, qkvw, tmp, dn, dqkv, act_t = refs
    clear_pads(bufs)
    g[...] = cot[...]
    if want:
        sgrad[...] = jnp.zeros(sgrad.shape, F32)

    def body(k, _):
        layer_backward(
            1 - k, w, small, eo, xs, h1, y, qkv, att, o, st, g, bufs, nbuf, qkvw, tmp, dn,
            dqkv, act_t, grad, sgrad, no_pump,
        )
        return 0

    lax.fori_loop(0, 2, body, 0)


def vm(n):
    return [pl.BlockSpec(memory_space=pltpu.VMEM)] * n


def scratch_forward(images):
    return [
        pltpu.VMEM((3, images, POS + 2 * PAD, C), BF16),
        pltpu.VMEM((images, POS, C), BF16),
        pltpu.VMEM((C, 3 * C), BF16),
        pltpu.VMEM((2, 3 * C, HALF), F32),
    ]


def run_forward(x0, w, small, eo, staged=False):
    images = x0.shape[0]
    return pl.pallas_call(
        functools.partial(forward_kernel, staged),
        out_shape=saved_shapes(images),
        in_specs=vm(4),
        out_specs=vm(7),
        scratch_shapes=scratch_forward(images),
        compiler_params=pltpu.CompilerParams(vmem_limit_bytes=VMEM_LIMIT),
    )(x0, w, small, eo)


def run_backward(cot, w, small, eo, saved, want):
    images = cot.shape[0]
    outs = [jax.ShapeDtypeStruct(cot.shape, F32)]
    if want:
        outs += [
            jax.ShapeDtypeStruct((2, ROWS, C), BF16),
            jax.ShapeDtypeStruct((2, 16, C), F32),
        ]
    return pl.pallas_call(
        functools.partial(backward_kernel, want),
        out_shape=outs,
        in_specs=vm(11),
        out_specs=vm(len(outs)),
        scratch_shapes=scratch_forward(images)
        + [
            pltpu.VMEM((images, POS, C), F32),
            pltpu.VMEM((images, POS, 3 * C), BF16),
            pltpu.VMEM((C, images * POS), BF16),
        ],
        compiler_params=pltpu.CompilerParams(vmem_limit_bytes=VMEM_LIMIT),
    )(cot, w, small, eo, *saved)


PLANES, PLANE = 4, 4
MESH = pl.DeviceIdType.MESH


class Place:
    def __init__(self):
        self.sec = lax.axis_index("section")
        self.d = lax.axis_index("dp")
        self.x = lax.rem(self.d, 2)
        self.y = lax.rem(self.d // 2, 2)
        self.z = self.d // PLANE
        self.seat = self.sec * PLANE + lax.rem(self.d, PLANE)
        self.sib = {"section": 1 - self.sec}
        self.xn = {"dp": self.d + 1 - 2 * self.x}
        self.yn = {"dp": self.d + 2 - 4 * self.y}

    def plane(self, j):
        return lax.rem(self.z + j + PLANES, PLANES)

    def zpeer(self, j):
        return {"dp": self.plane(j) * PLANE + lax.rem(self.d, PLANE)}

    def plane_peer(self, j):
        seat = lax.rem(self.seat + j, 2 * PLANE)
        return {"section": seat // PLANE, "dp": self.z * PLANE + lax.rem(seat, PLANE)}

    def meet(self):
        barrier = pltpu.get_barrier_semaphore()
        others = [self.plane_peer(j) for j in range(1, 8)] + [self.zpeer(j) for j in (1, 2, 3)]
        for other in others:
            pl.semaphore_signal(barrier, inc=1, device_id=other, device_id_type=MESH)
        pl.semaphore_wait(barrier, len(others))


def remote(src, dst, send, recv, target):
    return pltpu.make_async_remote_copy(
        src_ref=src, dst_ref=dst, send_sem=send, recv_sem=recv,
        device_id=target, device_id_type=MESH,
    )


Z1, X1, Y1, X2, Y2, S_OWN, S_X, S_Y, S_DA, S_DB = range(0, 40, 4)
Z_UP, Z_DOWN = 40, 41
SLOTS = 42


class Gather:
    def __init__(self, me, net, stage, local_sem, send_sem, recv_sem):
        self.me, self.net, self.stage = me, net, stage
        self.local_sem, self.send_sem, self.recv_sem = local_sem, send_sem, recv_sem
        self.part = stage.shape[0]
        self.half = self.part // 2

    def near(self, k):
        z = self.me.z
        if k == 1:
            return z + 1 - 2 * lax.rem(z, 2), 3 - z
        return (z, z) if k == 0 else (2 - z // 2 if k == 2 else 3 - 3 * (z // 2), 3 * z - 3)

    def rows(self, plane, y, x, lo, count):
        at = (plane * PLANE + y * 2 + x) * self.part + lo
        return self.net.at[self.me.sec, pl.ds(pl.multiple_of(at, 16), count)]

    def own(self, plane):
        return self.rows(plane, self.me.y, self.me.x, 0, self.part)

    def at_plane(self, plane):
        return {"dp": plane * PLANE + lax.rem(self.me.d, PLANE)}

    def send(self, slot, piece, target, src=None, sent=None):
        src = piece if src is None else src
        sent = slot if sent is None else sent
        remote(src, piece, self.send_sem.at[sent], self.recv_sem.at[slot], target).start()

    def arrived(self, slot, piece):
        remote(
            piece, piece, self.send_sem.at[slot], self.recv_sem.at[slot], self.me.sib
        ).wait_recv()

    def local(self):
        return pltpu.make_async_copy(self.stage, self.own(self.me.z), self.local_sem)

    def begin(self):
        me = self.me
        z, own = me.z, self.own(me.z)
        pl.when(z < 3)(lambda: self.send(Z1 + z, own, self.at_plane(z + 1), self.stage, Z_UP))
        pl.when(z > 0)(lambda: self.send(Z1 + z, own, self.at_plane(z - 1), self.stage, Z_DOWN))
        for slot, target in ((X1, me.xn), (Y1, me.yn), (S_OWN, me.sib)):
            self.send(slot + z, own, target, self.stage)
        self.local().start()

    def phase1(self):
        def step(k):
            me = self.me
            plane, target = self.near(k)
            rows = self.own(plane)
            self.arrived(Z1 + plane, rows)
            pl.when(me.z * (3 - me.z) > 0)(
                lambda: self.send(Z1 + plane, rows, self.at_plane(target))
            )
            for slot, to in ((X1, me.xn), (Y1, me.yn), (S_OWN, me.sib)):
                self.send(slot + plane, rows, to)

        return [lambda k=k: step(k) for k in (1, 2, 3)]

    def phase2(self):
        me, part, half = self.me, self.part, self.half

        def step_x(k):
            plane, _ = self.near(k)
            self.arrived(X1 + plane, self.rows(plane, me.y, 1 - me.x, 0, part))
            self.send(Y2 + plane, self.rows(plane, me.y, 1 - me.x, 0, half), me.yn)
            self.send(S_X + plane, self.rows(plane, me.y, 1 - me.x, 0, part), me.sib)

        def step_y(k):
            plane, _ = self.near(k)
            self.arrived(Y1 + plane, self.rows(plane, 1 - me.y, me.x, 0, part))
            self.send(X2 + plane, self.rows(plane, 1 - me.y, me.x, half, half), me.xn)
            self.send(S_Y + plane, self.rows(plane, 1 - me.y, me.x, 0, part), me.sib)

        return [lambda f=f, k=k: f(k) for k in range(PLANES) for f in (step_x, step_y)]

    def phase3(self):
        def step(k, slot, to, lo):
            me = self.me
            plane, _ = self.near(k)
            where = self.rows(plane, 1 - me.y, 1 - me.x, lo, self.half)
            self.arrived(slot + plane, where)
            self.send(to + plane, where, me.sib)

        return [
            lambda k=k, a=a: step(k, *a)
            for k in range(PLANES)
            for a in ((Y2, S_DA, 0), (X2, S_DB, self.half))
        ]

    def finish(self):
        def step():
            for slot in range(S_OWN, Z_UP):
                count = self.part if slot < S_DA else self.half
                self.arrived(slot, self.rows(0, 0, 0, 0, count))
            self.local().wait()

        return [step]

    def sent(self, slot, count):
        piece = self.rows(0, 0, 0, 0, count)
        remote(
            piece, piece, self.send_sem.at[slot], self.recv_sem.at[0], self.me.sib
        ).wait_send()

    def drain(self):
        me, part = self.me, self.part
        pl.when(me.z < 3)(lambda: self.sent(Z_UP, part))
        pl.when(me.z > 0)(lambda: self.sent(Z_DOWN, part))

        @pl.when(me.z * (3 - me.z) > 0)
        def _():
            for k in (1, 2, 3):
                self.sent(Z1 + self.near(k)[0], part)

        for slot in range(X1, Z_UP):
            whole = slot < X2 or S_OWN <= slot < S_DA
            self.sent(slot, part if whole else self.half)


A_SLOT, B_SLOT, C_SLOT, D_SLOT = 0, 4, 20, 28
R_SLOTS = 31


class Reduce:
    def __init__(self, me, big, shard, sib, there, rb, rc, rd, ssem, rsem):
        self.me, self.big, self.shard = me, big, shard
        self.sib, self.there, self.rb, self.rc, self.rd = sib, there, rb, rc, rd
        self.ssem, self.rsem = ssem, rsem
        self.part = shard.shape[0]
        self.half = self.part // 2
        self.span = PLANE * self.part

    def zt(self, k):
        return (3, 2, 0, 1)[k]

    def block(self, k):
        return pl.ds(self.zt(k) * self.span, self.span)

    def piece(self, k, y, x, lo, count):
        at = (self.zt(k) * PLANE + y * 2 + x) * self.part + lo
        return pl.ds(pl.multiple_of(at, 16), count)

    def send(self, src, dst, slot, target):
        remote(src, dst, self.ssem.at[slot], self.rsem.at[slot], target).start()

    def arrived(self, dst, slot):
        remote(dst, dst, self.ssem.at[slot], self.rsem.at[slot], self.me.sib).wait_recv()

    def begin(self):
        for k in range(PLANES):
            self.begin_block(k)

    def begin_block(self, k):
        at = self.block(k)
        self.send(self.big.at[1 - self.me.sec, at], self.there.at[at], A_SLOT + k, self.me.sib)

    def stage_a(self, k):
        me, half = self.me, self.half
        self.arrived(self.sib.at[self.block(k)], A_SLOT + k)
        base = self.zt(k) * self.span

        def body(i, _):
            at = pl.ds(pl.multiple_of(base + i * half, 16), half)
            self.big[me.sec, at, :] = (
                self.big[me.sec, at, :].astype(F32) + self.sib[at, :].astype(F32)
            ).astype(BF16)
            return 0

        lax.fori_loop(0, 2 * PLANE, body, 0)
        for j in range(2):
            self.send(
                self.big.at[me.sec, self.piece(k, 1 - me.y, j, 0, half)], self.rb.at[k, j],
                B_SLOT + 4 * k + j, me.yn,
            )
            self.send(
                self.big.at[me.sec, self.piece(k, j, 1 - me.x, half, half)], self.rb.at[k, 2 + j],
                B_SLOT + 4 * k + 2 + j, me.xn,
            )

    def join(self, where, other):
        self.big[self.me.sec, where, :] = (
            self.big[self.me.sec, where, :].astype(F32) + other.astype(F32)
        ).astype(BF16)

    def stage_c(self, k):
        me, half = self.me, self.half
        for j in range(4):
            self.arrived(self.rb.at[k, j], B_SLOT + 4 * k + j)
            y, x, lo = (me.y, j, 0) if j < 2 else (j - 2, me.x, half)
            self.join(self.piece(k, y, x, lo, half), self.rb[k, j])
        self.send(
            self.big.at[me.sec, self.piece(k, me.y, 1 - me.x, 0, half)], self.rc.at[k, 0],
            C_SLOT + 2 * k, me.xn,
        )
        self.send(
            self.big.at[me.sec, self.piece(k, 1 - me.y, me.x, half, half)], self.rc.at[k, 1],
            C_SLOT + 2 * k + 1, me.yn,
        )

    def stage_d(self, k):
        me, half, zt = self.me, self.half, self.zt(k)
        for j in range(2):
            self.arrived(self.rc.at[k, j], C_SLOT + 2 * k + j)
            self.join(self.piece(k, me.y, me.x, j * half, half), self.rc[k, j])

        @pl.when(me.z != zt)
        def _():
            self.send(
                self.big.at[me.sec, self.piece(k, me.y, me.x, 0, self.part)],
                self.rd.at[lax.rem(zt - me.z + PLANES, PLANES) - 1],
                D_SLOT + lax.rem(zt - me.z + PLANES, PLANES) - 1,
                {"dp": zt * PLANE + lax.rem(me.d, PLANE)},
            )

    def stage_e(self):
        for j in range(PLANES - 1):
            self.arrived(self.rd.at[j], D_SLOT + j)
        at = pl.ds(pl.multiple_of(self.me.d * self.part, 16), self.part)
        self.shard[...] = (
            self.big[self.me.sec, at, :].astype(F32)
            + self.rd[0].astype(F32) + (self.rd[1].astype(F32) + self.rd[2].astype(F32))
        )

    def in_rows(self):
        stages = (self.stage_a, self.stage_c, self.stage_d)
        return [lambda stage=stage, k=k: stage(k) for stage in stages for k in range(PLANES)]

    def steps(self):
        out = []
        for t in range(PLANES + 2):
            for stage, lag in ((self.stage_a, 0), (self.stage_c, 1), (self.stage_d, 2)):
                if 0 <= t - lag < PLANES:
                    out.append(lambda stage=stage, k=t - lag: stage(k))
        return out

    def drain(self, lo=0, hi=R_SLOTS):
        for slot in range(lo, hi):
            if slot < B_SLOT:
                piece = self.there.at[pl.ds(0, self.span)]
            elif slot < D_SLOT:
                piece = self.rb.at[0, 0]
            else:
                piece = self.rd.at[0]
            remote(piece, piece, self.ssem.at[slot], self.rsem.at[slot], self.me.sib).wait_send()


def reduce_scratch(part):
    half = part // 2
    return [
        pltpu.VMEM((PLANES, 4, half, C), BF16),
        pltpu.VMEM((PLANES, 2, half, C), BF16),
        pltpu.VMEM((PLANES - 1, part, C), BF16),
        pltpu.SemaphoreType.DMA((R_SLOTS,)),
        pltpu.SemaphoreType.DMA((R_SLOTS,)),
    ]


class Totals:
    def __init__(self, me, buf, recv, ssem, rsem):
        self.me, self.buf, self.recv, self.ssem, self.rsem = me, buf, recv, ssem, rsem

    def send(self, src, dst, slot, target):
        remote(src, dst, self.ssem.at[slot], self.rsem.at[slot], target).start()

    def arrived(self, dst, slot):
        remote(dst, dst, self.ssem.at[slot], self.rsem.at[slot], self.me.sib).wait_recv()

    def begin(self, first):
        self.send(first, self.recv.at[0], 0, self.me.sib)

    def steps(self):
        me, buf, recv = self.me, self.buf, self.recv

        def one():
            self.arrived(recv.at[0], 0)
            buf[1] = buf[0] + recv[0]
            self.send(buf.at[1], recv.at[1], 1, me.xn)

        def two():
            self.arrived(recv.at[1], 1)
            buf[2] = buf[1] + recv[1]
            self.send(buf.at[2], recv.at[2], 2, me.yn)

        def three():
            self.arrived(recv.at[2], 2)
            buf[3] = buf[2] + recv[2]
            recv[3 + me.z] = buf[3]
            for j in (1, 2, 3):
                self.send(buf.at[3], recv.at[3 + me.z], 2 + j, me.zpeer(j))

        return [one, two, three]

    def result(self):
        for j in (1, 2, 3):
            self.arrived(self.recv.at[3 + self.me.plane(-j)], 2 + j)
        return (self.recv[3] + self.recv[4]) + (self.recv[5] + self.recv[6])

    def drain(self):
        for slot in range(6):
            piece = self.recv.at[0]
            remote(piece, piece, self.ssem.at[slot], self.rsem.at[slot], self.me.sib).wait_send()


class Squares:
    def __init__(self, me, own, recv, ssem, rsem):
        self.me, self.own, self.recv, self.ssem, self.rsem = me, own, recv, ssem, rsem

    def hop(self, src, base, mine, peers, slots):
        for j, target in peers:
            dst = self.recv.at[base + mine]
            remote(src, dst, self.ssem.at[slots + j], self.rsem.at[slots + j], target).start()
        self.recv[base + mine] = src[...]
        for j, _ in peers:
            dst = self.recv.at[base]
            remote(dst, dst, self.ssem.at[slots + j], self.rsem.at[slots + j], self.me.sib).wait_recv()

    def run(self):
        me, recv = self.me, self.recv
        self.hop(self.own.at[0], 0, me.seat, [(j, me.plane_peer(j)) for j in range(1, 8)], -1)
        pairs = [recv[2 * k] + recv[2 * k + 1] for k in range(4)]
        self.own[1] = (pairs[0] + pairs[1]) + (pairs[2] + pairs[3])
        self.hop(self.own.at[1], 8, me.z, [(j, me.zpeer(j)) for j in (1, 2, 3)], 6)
        return (recv[8] + recv[9]) + (recv[10] + recv[11])

    def drain(self):
        for slot in range(10):
            piece = self.recv.at[0]
            remote(piece, piece, self.ssem.at[slot], self.rsem.at[slot], self.me.sib).wait_send()


def squares_scratch(shape):
    return [
        pltpu.VMEM((2,) + shape, F32),
        pltpu.VMEM((12,) + shape, F32),
        pltpu.SemaphoreType.DMA((10,)),
        pltpu.SemaphoreType.DMA((10,)),
    ]


def totals_scratch(shape):
    return [
        pltpu.VMEM((4,) + shape, F32),
        pltpu.VMEM((7,) + shape, F32),
        pltpu.SemaphoreType.DMA((6,)),
        pltpu.SemaphoreType.DMA((6,)),
    ]


def saved_scratch(images):
    return [pltpu.VMEM(a.shape, a.dtype) for a in saved_shapes(images)]


def backward_scratch(images):
    return scratch_forward(images) + [
        pltpu.VMEM((images, POS, C), F32),
        pltpu.VMEM((images, POS, 3 * C), BF16),
        pltpu.VMEM((C, images * POS), BF16),
    ]


GEN_TOTAL = SIGMA_INIT**2 + SIGMA_DATA**2
GEN_IN = GEN_TOTAL**-0.5
GEN_SKIP = SIGMA_DATA**2 / GEN_TOTAL
GEN_OUT = SIGMA_INIT * SIGMA_DATA * GEN_TOTAL**-0.5
T_IN, T_SKIP, T_OUT, T_SIGMA, T_FACTOR = range(5)


def fill_embed(eo, sigmas):
    at = lax.broadcasted_iota(jnp.int32, (8, 4 * C), 1)
    side = lax.broadcasted_iota(jnp.int32, (8, 4 * C), 0) // 4
    k = at // 2
    power = (k & (C - 1)).astype(F32) * (1.0 / C)
    rows = sigmas + [jnp.ones_like(sigmas[0])] * (4 - len(sigmas))
    angle = jnp.log(jnp.concatenate(rows + rows, axis=0)) * 0.25 * jnp.exp(power * -LOG_10000)
    wave = jnp.where(k < C, jnp.cos(angle), jnp.sin(angle))
    eo[...] = jnp.where((at & 1) == side, wave, 0.0).astype(BF16)


LOG_10000 = 9.210340371976184


def step_kernel(*refs):
    (
        z_all, eps_all, levels, counts, gen_w, fake_w, teacher_w, gen_small, fake_small,
        teacher_small,
        gw_out, sv_x, sv_h, sv_y, sv_q, sv_a, sv_o, sv_s, gshard, fshard, stot, sqtot,
        *refs,
    ) = refs
    gen_out = (sv_x, sv_h, sv_y, sv_q, sv_a, sv_o, sv_s)
    w_gen, w_fake, w_teach = refs[:3]
    sv_one, sv_two = refs[3:10], refs[10:17]
    bufs, nbuf, qkvw, tmp, dn, dqkv, act_t = refs[17:24]
    zb, eb, g, stage, local_sem, send_sem, recv_sem, copy_sem = refs[24:32]
    smalls, small_sem, gen_eo, score_eo, tab, sgrads, part_sums = refs[32:39]
    fake_refs, gen_refs = refs[39:44], refs[44:49]
    small_refs, square_refs = refs[49:53], refs[53:57]
    sib, free_sem = refs[57:59]
    g2 = sv_two[0].at[2]
    images = zb.shape[0]
    me = Place()
    start = me.sec * images

    def run(steps):
        for step in steps:
            step()

    def mine(ref):
        return ref.at[pl.ds(start, images)]

    loads = [
        pltpu.make_async_copy(mine(z_all), zb, copy_sem.at[0]),
        pltpu.make_async_copy(mine(eps_all), eb, copy_sem.at[1]),
    ]
    for copy in loads:
        copy.start()
    masters = [
        pltpu.make_async_copy(src, dst, copy_sem.at[2 + k])
        for k, (src, dst) in enumerate(((gen_w, gshard), (fake_w, fshard), (teacher_w, stage.at[2])))
    ]
    for copy in masters:
        copy.start()
    smalls[...] = jnp.zeros(smalls.shape, F32)
    for n, ref in enumerate((gen_small, fake_small, teacher_small)):
        for r in range(13):
            smalls[me.sec, n, r : r + 1, :] = ref[r]
    gathers = [
        Gather(me, net, stage.at[n], local_sem.at[n], send_sem.at[n], recv_sem.at[n])
        for n, net in enumerate((w_gen, w_fake, w_teach))
    ]
    for copy in masters:
        copy.wait()
    stage[0] = gshard[...].astype(BF16)
    stage[1] = fshard[...].astype(BF16)
    me.meet()
    gathers[0].begin()
    swap = remote(
        smalls.at[me.sec], smalls.at[me.sec], small_sem.at[0], small_sem.at[1], me.sib
    )
    swap.start()

    clear_pads(bufs)
    sgrads[...] = jnp.zeros(sgrads.shape, F32)
    sigmas = []
    valid_sum = jnp.zeros((1, 4 * C), F32)
    for i in range(images):
        level = jnp.zeros((1, 4 * C), jnp.int32) + levels[start + i]
        sigma = SIGMA_TOP + level.astype(F32) / (LEVELS - 1) * (SIGMA_BOTTOM - SIGMA_TOP)
        square = sigma * sigma
        sigma = square * square * square * sigma
        sigmas.append(sigma)
        s_in, s_skip, s_out, s_lam = precondition(sigma)
        valid = jnp.where(jnp.zeros_like(level) + (start + i) < counts[0], 1.0, 0.0)
        valid_sum = valid_sum + valid
        rows = (s_in, s_skip, s_out, sigma, valid * s_lam * (1.0 / (POS * C)))
        for k, value in enumerate(rows):
            tab[i, k : k + 1, :] = value[:, :C]
    fill_embed(score_eo, sigmas)
    fill_embed(gen_eo, [jnp.full((1, 4 * C), SIGMA_INIT, F32)] * images)

    def forward(n, w, eo, sv, pump):
        def body(l, _):
            layer_forward(
                l, w, smalls.at[:, n], eo, *sv, bufs, nbuf, qkvw, tmp, True, pump
            )
            return 0

        lax.fori_loop(0, 2, body, 0)

    def backward(n, w, eo, sv, cot, grad, sgrad, pump):
        def body(k, _):
            layer_backward(
                1 - k, w, smalls.at[:, n], eo, *sv, cot, bufs, nbuf, qkvw, tmp, dn, dqkv,
                act_t, grad, sgrad, pump,
            )
            return 0

        lax.fori_loop(0, 2, body, 0)

    def each(f):
        def body(i, carry):
            return f(i, [tab[i, k : k + 1, :] for k in range(5)], carry)

        return lax.fori_loop(0, images, body, jnp.zeros((1, C), F32))

    last = gathers[0].phase3()
    run(gathers[0].phase1() + gathers[0].phase2() + last[:6] + [gathers[1].begin] + last[6:])
    for copy in loads:
        copy.wait()
    sv_one[0][0] = zb[...] * (GEN_IN * SIGMA_INIT)
    swap.wait()
    run(gathers[0].finish())
    later = gathers[1].phase1() + gathers[1].phase2()
    forward(0, w_gen, gen_eo, sv_one, Pump(later[:7], FORWARD_POINTS, (0, 1)))
    pairs = [(w_gen, gw_out)] + list(zip(sv_one, gen_out))
    stores = [
        pltpu.make_async_copy(src, dst, copy_sem.at[2 + k]) for k, (src, dst) in enumerate(pairs)
    ]
    for copy in stores:
        copy.start()

    def noisy(i, t, carry):
        zb[i] = zb[i] * (GEN_SKIP * SIGMA_INIT) + GEN_OUT * sv_one[0][2, i]
        eb[i] = zb[i] + t[T_SIGMA] * eb[i]
        sv_two[0][0, i] = t[T_IN] * eb[i]
        return carry

    each(noisy)
    z_next = gathers[2].phase1()
    run(later[7:] + [gathers[2].begin] + z_next[:1] + gathers[1].phase3() + gathers[1].finish())
    later = z_next[1:] + gathers[2].phase2()
    forward(1, w_fake, score_eo, sv_two, Pump(later[:5], FORWARD_POINTS, (0, 1)))
    later = later[5:] + gathers[2].phase3()

    def fake_loss(i, t, total):
        den = t[T_SKIP] * eb[i] + t[T_OUT] * sv_two[0][2, i]
        sv_two[0][2, i] = den
        miss = den - zb[i]
        g[i] = (2.0 * t[T_OUT] * t[T_FACTOR]) * miss
        return total + t[T_FACTOR] * colsum(miss * miss)

    loss_fake = each(fake_loss)
    for copy in stores:
        copy.wait()
    gathers[0].drain()
    backward(
        1, w_fake, score_eo, sv_two, g, w_gen, sgrads.at[:, 1],
        Pump(later, WEIGHT_POINTS, (1, 0), 0.0, 0.8),
    )
    fake_sum = Reduce(me, w_gen, fshard, sib, sib, *fake_refs)
    fake_sum.begin()
    run(gathers[2].finish())
    later = fake_sum.in_rows()
    sv_one[0][0] = sv_two[0][0]
    forward(2, w_teach, score_eo, sv_one, Pump(later[:4], FORWARD_POINTS, (0, 1), 0.2))

    def gen_loss(i, t, total):
        den = t[T_SKIP] * eb[i] + t[T_OUT] * sv_one[0][2, i]
        fake_den = sv_two[0][2, i]
        miss = fake_den - zb[i]
        gap = den - fake_den
        scale = t[T_OUT] * t[T_FACTOR]
        g[i] = scale * ((2.0 * (1.0 - ALPHA_MIX)) * gap + miss)
        g2[i] = scale * ((1.0 - 2.0 * (1.0 - ALPHA_MIX)) * gap - miss)
        zb[i] = (t[T_FACTOR] * (t[T_SKIP] - 1.0)) * gap
        return total + t[T_FACTOR] * colsum(gap * ((1.0 - ALPHA_MIX) * gap + miss))

    loss_gen = each(gen_loss)
    backward(
        2, w_teach, score_eo, sv_one, g, None, None, Pump(later[4:8], BACKWARD_POINTS, (1, 0), 0.1)
    )
    gathers[2].drain()
    fake_sum.drain(A_SLOT, B_SLOT)
    pl.semaphore_signal(free_sem, inc=1, device_id=me.sib, device_id_type=MESH)
    back = [
        pltpu.make_async_copy(src, dst, copy_sem.at[2 + k])
        for k, (dst, src) in enumerate([(w_teach, gw_out)] + list(zip(sv_one, gen_out)))
    ]
    for copy in back:
        copy.start()
    backward(
        1, w_fake, score_eo, sv_two, g2, None, None, Pump(later[8:], BACKWARD_POINTS, (1, 0))
    )

    def gen_gradient(i, t, carry):
        g[i] = GEN_OUT * (zb[i] + t[T_IN] * (g[i] + g2[i]))
        return carry

    each(gen_gradient)
    gathers[1].drain()
    for copy in back:
        copy.wait()

    gen_sum = Reduce(me, w_fake, gshard, w_gen.at[1 - me.sec], w_gen.at[me.sec], *gen_refs)
    later = gen_sum.steps()

    def on_section(s, steps):
        pl.when(me.sec == s)(lambda: run(steps))

    def hand_over():
        pl.semaphore_wait(free_sem, 1)

    pump = Pump([], WEIGHT_POINTS, (1, 0))

    def at(layer, point, section, steps):
        pump.table[layer][point].append(lambda: on_section(section, steps))

    upper = [hand_over, lambda: gen_sum.begin_block(0), lambda: gen_sum.begin_block(1)]
    lower = [lambda: gen_sum.begin_block(2), lambda: gen_sum.begin_block(3)]
    for layer, giver in ((1, 0), (0, 1)):
        at(layer, HALF_WAY, giver, upper)
        at(layer, READY, giver, lower)
    rows = gen_sum.in_rows()
    for k, point in enumerate((1, 3, 5, 6, 8, 11, 14, 17)):
        at(0, point, 1, rows[k : k + 1])
    at(0, READY, 0, later[:1])
    at(0, READY + 2, 0, later[1:2])
    at(0, READY + 4, 0, later[2:3])
    backward(0, w_teach, gen_eo, sv_one, g, w_fake, sgrads.at[:, 0], pump)

    def spread_sum(total):
        return jnp.broadcast_to(jnp.sum(total, axis=1, keepdims=True), (1, C))

    sums = jnp.concatenate([spread_sum(loss_gen), spread_sum(loss_fake), valid_sum[:, :C]], axis=0)
    for s in range(2):
        part_sums[s, 0:16, :] = sgrads[s, 0]
        part_sums[s, 13:16, :] = sums
        part_sums[s, 16:32, :] = sgrads[s, 1]
    small = Totals(me, *small_refs)
    small_refs[0][0] = part_sums[me.sec]
    small.begin(part_sums.at[1 - me.sec])
    fake_sum.stage_e()
    small_steps = small.steps()
    on_section(0, later[3:6])
    on_section(1, rows[8:])
    run(small_steps[:1])
    on_section(0, later[6:8])
    run(small_steps[1:2])
    on_section(0, later[8:10])
    run(small_steps[2:])
    on_section(0, later[10:])
    stot[...] = small.result()
    own = square_refs[0]
    keep = lax.broadcasted_iota(jnp.int32, (16, C), 0) < 13
    for n, rows in ((1, fshard), (0, gshard)):
        if n == 0:
            gen_sum.stage_e()
        low = jnp.square(jnp.where(keep, stot[16 * n : 16 * n + 16, :], 0.0))
        low = jnp.where(me.d == 0, low[0:8] + low[8:16], 0.0)
        big = jnp.sum(jnp.square(rows[...]).reshape(rows.shape[0] // 8, 8, C), axis=0)
        own[0, 8 * n : 8 * n + 8, :] = big + low
    square = Squares(me, *square_refs)
    sqtot[...] = square.run()
    fake_sum.drain(B_SLOT)
    for done in (gen_sum, small, square):
        done.drain()


SIGMA_TOP = SIGMA_HIGH ** (1.0 / RHO_POWER)
SIGMA_BOTTOM = SIGMA_LOW ** (1.0 / RHO_POWER)


def run_step(z, eps, levels, counts, gen_w, fake_w, teacher_w, smalls):
    part = gen_w.shape[0]
    images = z.shape[0] // 2
    any_ = pl.BlockSpec(memory_space=pl.ANY)
    smem = pl.BlockSpec(memory_space=pltpu.SMEM)
    saved = saved_shapes(images)
    return pl.pallas_call(
        step_kernel,
        out_shape=[jax.ShapeDtypeStruct((2, ROWS, C), BF16)]
        + saved
        + [
            jax.ShapeDtypeStruct((part, C), F32),
            jax.ShapeDtypeStruct((part, C), F32),
            jax.ShapeDtypeStruct((32, C), F32),
            jax.ShapeDtypeStruct((16, C), F32),
        ],
        in_specs=[any_] * 2 + [smem] * 2 + [any_] * 3 + vm(3),
        out_specs=[any_] * 8 + vm(4),
        scratch_shapes=[pltpu.VMEM((2, ROWS, C), BF16)] * 3
        + saved_scratch(images) * 2
        + backward_scratch(images)
        + [pltpu.VMEM((images, POS, C), F32)] * 3
        + [
            pltpu.VMEM((3, part, C), BF16),
            pltpu.SemaphoreType.DMA((3,)),
            pltpu.SemaphoreType.DMA((3, SLOTS)),
            pltpu.SemaphoreType.DMA((3, SLOTS)),
            pltpu.SemaphoreType.DMA((10,)),
            pltpu.VMEM((2, 3, 16, C), F32),
            pltpu.SemaphoreType.DMA((2,)),
            pltpu.VMEM((8, 4 * C), BF16),
            pltpu.VMEM((8, 4 * C), BF16),
            pltpu.VMEM((images, 8, C), F32),
            pltpu.VMEM((2, 2, 16, C), F32),
            pltpu.VMEM((2, 32, C), F32),
        ]
        + reduce_scratch(part) * 2
        + totals_scratch((32, C))
        + squares_scratch((16, C))
        + [pltpu.VMEM((ROWS, C), BF16), pltpu.SemaphoreType.REGULAR],
        compiler_params=pltpu.CompilerParams(
            collective_id=0, has_side_effects=True, vmem_limit_bytes=STEP_LIMIT
        ),
    )(z, eps, levels, counts, gen_w, fake_w, teacher_w, *smalls)[8:]


def adam_step(master, first_mom, second_mom, grad):
    first_new = BETA_ONE * first_mom + (1.0 - BETA_ONE) * grad
    second_new = BETA_TWO * second_mom + (1.0 - BETA_TWO) * grad * grad
    direction = (
        first_new
        / (1.0 - BETA_ONE**STEP)
        / (jnp.sqrt(second_new / (1.0 - BETA_TWO**STEP)) + ADAM_EPS)
    )
    return (master - LEARN_RATE * (direction + WEIGHT_DECAY * master), first_new, second_new)


EMA_RATE = 0.5 ** (20.0 / STEP)
SMALL_STATES = (4, 5, 6, 7, 11, 12, 13)


def update_kernel(gshard, fshard, stot, sqtot, *refs):
    ins, outs = refs[:14], refs[14:]
    norms, losses = outs[14:]
    count = stot[15:16, 0:1]
    norm_of, scales = [], []
    for n in range(2):
        rows = jnp.sum(sqtot[8 * n : 8 * n + 8, :], axis=0, keepdims=True)
        norm = jnp.sqrt(jnp.sum(rows, axis=1, keepdims=True)) / count
        scales.append(jnp.minimum(1.0, CLIP_NORM / norm) / count)
        norm_of.append(norm)

    def one(at, grad, w, m, v, ema, ow, om, ov, oe):
        new, first, second = adam_step(w[at], m[at], v[at], grad)
        ow[at] = new
        om[at] = first
        ov[at] = second
        if ema is not None:
            oe[at] = EMA_RATE * ema[at] + (1.0 - EMA_RATE) * new

    one(0, gshard[...] * scales[0], *ins[0:4], *outs[0:4])
    one(0, fshard[...] * scales[1], *ins[8:11], None, *outs[8:11], None)

    first = lax.broadcasted_iota(jnp.int32, (1, 2), 1) == 0
    norms[...] = jnp.where(first, norm_of[0], norm_of[1])
    losses[...] = jnp.where(first, stot[13:14, 0:1], stot[14:15, 0:1]) / count
    for k in range(13):
        one(k, stot[k : k + 1, :] * scales[0], *ins[4:8], *outs[4:8])
        one(k, stot[16 + k : 17 + k, :] * scales[1], *ins[11:14], None, *outs[11:14], None)


def update_nets(gshard, fshard, stot, sqtot, states):
    def turned(arrays):
        return [a.swapaxes(0, 1) if k in SMALL_STATES else a for k, a in enumerate(arrays)]

    states = turned(states)
    res = pl.pallas_call(
        update_kernel,
        out_shape=[jax.ShapeDtypeStruct(a.shape, F32) for a in states]
        + [jax.ShapeDtypeStruct((1, 2), F32)] * 2,
        in_specs=vm(4 + len(states)),
        out_specs=vm(2 + len(states)),
        compiler_params=pltpu.CompilerParams(vmem_limit_bytes=VMEM_LIMIT),
    )(gshard, fshard, stot, sqtot, *states)
    return tuple(turned(res[:-2])) + (res[-2][0], res[-1][0])


def gather_plain(shard):
    rows = lax.all_gather(shard.astype(BF16), "dp", axis=1, tiled=True)
    return lax.all_gather(rows, "section", axis=0, tiled=True)


def reduce_plain(bigs, small):
    shards_, squares = [], []
    own = lax.psum_scatter(small, "section", scatter_dimension=0, tiled=True)
    stot = lax.psum(own, "dp")[0]
    first = lax.axis_index("dp") == 0
    for n, big in enumerate(bigs):
        own = lax.psum_scatter(big, "section", scatter_dimension=0, tiled=True)
        own = lax.psum_scatter(own, "dp", scatter_dimension=1, tiled=True)[0].astype(F32)
        shards_.append(own)
        low = jnp.sum(jnp.square(stot[16 * n : 16 * n + 13]))
        squares.append(jnp.sum(own * own) + jnp.where(first, low, 0.0))
    sq = lax.psum(jnp.stack(squares), ("section", "dp"))
    return *shards_, stot, jnp.zeros((16, C), F32).at[jnp.array([0, 8]), 0].set(sq)


def shards(
    z_noise, eps_noise, levels, counts,
    gen_w, gen_m, gen_v, gen_ema, gen_small, gen_small_m, gen_small_v, gen_small_ema,
    fake_w, fake_m, fake_v, fake_small, fake_small_m, fake_small_v,
    teacher_w, teacher_small,
):
    if lax.axis_size("dp") == PLANES * PLANE:
        smalls = [a.swapaxes(0, 1) for a in (gen_small, fake_small, teacher_small)]
        reduced = run_step(
            z_noise, eps_noise, levels, counts, gen_w[0], fake_w[0], teacher_w[0], smalls
        )
    else:
        reduced = plain_step(
            z_noise, eps_noise, levels, counts, gen_w, fake_w, teacher_w,
            gen_small, fake_small, teacher_small,
        )
    return update_nets(
        *reduced,
        (
            gen_w, gen_m, gen_v, gen_ema, gen_small, gen_small_m, gen_small_v, gen_small_ema,
            fake_w, fake_m, fake_v, fake_small, fake_small_m, fake_small_v,
        ),
    )


def plain_step(
    z_noise, eps_noise, levels, counts, gen_w, fake_w, teacher_w,
    gen_small, fake_small, teacher_small,
):
    images = z_noise.shape[0] // lax.axis_size("section")
    start = lax.axis_index("section") * images

    def mine(a):
        return lax.dynamic_slice_in_dim(a, start, images, 0)

    z, eps = mine(z_noise), mine(eps_noise)
    sigma = sigma_levels(mine(levels))
    valid = (start + jnp.arange(images) < counts[0]).astype(F32)
    valid_sum = jnp.sum(valid)
    gen_eo = spread_embed(jnp.full((images,), SIGMA_INIT, F32))
    score_eo = spread_embed(sigma)
    gs, fs, ts = [
        lax.all_gather(a, "section", axis=0, tiled=True)
        for a in (gen_small, fake_small, teacher_small)
    ]
    gw, fw, tw = gather_plain(gen_w), gather_plain(fake_w), gather_plain(teacher_w)
    s_in, s_skip, s_out, s_lam = precondition(sigma)
    factor = valid * s_lam / (POS * C)
    s_in, s_skip, s_out, sigma, factor = [
        t[:, None, None] for t in (s_in, s_skip, s_out, sigma, factor)
    ]
    raw = SIGMA_INIT * z
    gen_saved = run_forward(GEN_IN * raw, gw, gs, gen_eo)
    samples = GEN_SKIP * raw + GEN_OUT * gen_saved[0][2]
    noisy = samples + sigma * eps
    x0 = s_in * noisy
    fake_saved = run_forward(x0, fw, fs, score_eo)
    fake_den = s_skip * noisy + s_out * fake_saved[0][2]
    miss = fake_den - samples
    _, fake_g, fake_sg = run_backward(
        s_out * 2.0 * factor * miss, fw, fs, score_eo, fake_saved, True
    )
    teacher_saved = run_forward(x0, tw, ts, score_eo)
    teacher_den = s_skip * noisy + s_out * teacher_saved[0][2]
    gap = teacher_den - fake_den
    loss_gen = jnp.sum(factor * ((1.0 - ALPHA_MIX) * gap * gap + gap * miss))
    loss_fake = jnp.sum(factor * miss * miss)
    grad_teacher = factor * (2.0 * (1.0 - ALPHA_MIX) * gap + miss)
    grad_fake = factor * gap - grad_teacher
    direct = factor * gap * (s_skip - 1.0)
    (back_t,) = run_backward(s_out * grad_teacher, tw, ts, score_eo, teacher_saved, False)
    (back_f,) = run_backward(s_out * grad_fake, fw, fs, score_eo, fake_saved, False)
    gen_cot = GEN_OUT * (direct + s_in * (back_t + back_f))
    _, gen_g, gen_sg = run_backward(gen_cot, gw, gs, gen_eo, gen_saved, True)
    scalars = jnp.broadcast_to(jnp.stack([loss_gen, loss_fake, valid_sum])[:, None], (3, C))
    small_sums = jnp.concatenate(
        [gen_sg[:, :13], jnp.broadcast_to(scalars, (2, 3, C)), fake_sg], axis=1
    )
    return reduce_plain((gen_g, fake_g), small_sums)


def solution(mesh):
    images = P("dp", None, None)
    big = P("section", "dp", None)
    small = P("section", None, None)
    return jax.shard_map(
        shards,
        mesh=mesh,
        in_specs=(images, images, P("dp"), P("dp"))
        + (big,) * 4 + (small,) * 4 + (big,) * 3 + (small,) * 3 + (big, small),
        out_specs=(big,) * 4 + (small,) * 4 + (big,) * 3 + (small,) * 3 + (P(), P()),
        check_vma=False,
    )
```

```python
import functools

import jax
import jax.numpy as jnp
from jax import lax
from jax.experimental import pallas as pl
from jax.experimental.pallas import tpu as pltpu
from jax.sharding import PartitionSpec as P

GROUPS = 32
SIDE = 16
LEVELS = 1000
STEP = 10

SIGMA_DATA = 0.5
SIGMA_INIT = 2.5
SIGMA_LOW = 0.05
SIGMA_HIGH = 20.0
RHO_POWER = 7.0
ALPHA_MIX = 1.2
RS = 0.7071067811865476
NORM_EPS = 1e-05
CLIP_NORM = 0.001
LEARN_RATE = 0.15
BETA_ONE = 0.9
BETA_TWO = 0.999
ADAM_EPS = 1e-08
WEIGHT_DECAY = 0.01

C = 256
HALF = 128
POS = 256
ROWS = 26 * C
CHUNK = 64
PAD = SIDE
F32 = jnp.float32
BF16 = jnp.bfloat16
VMEM_LIMIT = 58 * 2**20
STEP_LIMIT = 63 * 2**20

R_CONV1, R_CONV2, R_EMB, R_QKV, R_PROJ = 0, 9 * C, 18 * C, 22 * C, 25 * C
S_M1, S_I1, S_M2, S_I2, S_M3, S_I3, S_MA, S_MB = range(8)


def sigma_levels(level_ids):
    fraction = level_ids.astype(F32) / (LEVELS - 1)
    top_root = SIGMA_HIGH ** (1.0 / RHO_POWER)
    bottom_root = SIGMA_LOW ** (1.0 / RHO_POWER)
    return (top_root + fraction * (bottom_root - top_root)) ** RHO_POWER


def precondition(sigma_vals):
    total = sigma_vals * sigma_vals + SIGMA_DATA**2
    return (
        lax.rsqrt(total),
        SIGMA_DATA**2 / total,
        sigma_vals * SIGMA_DATA * lax.rsqrt(total),
        total / (sigma_vals * sigma_vals * SIGMA_DATA**2),
    )


def noise_embed(sigma_vals, channel_count):
    frequency = (1.0 / 10000.0) ** (jnp.arange(channel_count, dtype=F32) / channel_count)
    angles = (jnp.log(sigma_vals) / 4.0)[..., None] * frequency
    return jnp.concatenate([jnp.cos(angles), jnp.sin(angles)], axis=-1)


def spread_embed(sigma_vals):
    emb = noise_embed(sigma_vals, C).astype(BF16)
    images = emb.shape[0]
    zero = jnp.zeros_like(emb)
    low = jnp.stack([emb, zero], axis=-1).reshape(images, 4 * C)
    high = jnp.stack([zero, emb], axis=-1).reshape(images, 4 * C)
    fill = jnp.zeros((4 - images, 4 * C), BF16)
    return jnp.concatenate([low, fill, high, fill], axis=0)


def dot_nn(a, b):
    return lax.dot_general(a, b, (((1,), (0,)), ((), ())), preferred_element_type=F32)


def dot_nt(a, b):
    return lax.dot_general(a, b, (((1,), (1,)), ((), ())), preferred_element_type=F32)


def dot_tn(a, b):
    return lax.dot_general(a, b, (((0,), (0,)), ((), ())), preferred_element_type=F32)


def group_mean(v):
    lane = lax.broadcasted_iota(jnp.int32, (8, C), 1)
    for sh in (1, 2, 4):
        v = v + jnp.where((lane & sh) != 0, pltpu.roll(v, sh, 1), pltpu.roll(v, C - sh, 1))
    return v * (1.0 / (POS * 8))


def colsum(v):
    return jnp.sum(v, axis=0, keepdims=True)


def no_pump(l):
    pass


FORWARD_POINTS, BACKWARD_POINTS, WEIGHT_POINTS = 10, 12, 18
HALF_WAY, READY = 8, 13


def stagger(steps, images, between):
    for t in range(len(steps) + images - 1):
        for i in range(images):
            if 0 <= t - i < len(steps):
                steps[t - i](i)
        between()


class Pump:
    def __init__(self, steps, points, layers, lo=0.0, hi=1.0):
        self.table = {l: [[] for _ in range(points)] for l in layers}
        self.at = 0
        for k, step in enumerate(steps):
            place = int((lo + (hi - lo) * (k + 0.5) / len(steps)) * points * len(layers))
            self.table[layers[place // points]][place % points].append(step)

    def __call__(self, l):
        for layer, points in self.table.items():
            if points[self.at]:

                @pl.when(l == layer)
                def _(todo=points[self.at]):
                    for step in todo:
                        step()

        self.at += 1


def put_shifted(bufs, i, r, v):
    rows = v.shape[0]
    at = pl.ds(PAD + r, rows)
    sub = lax.broadcasted_iota(jnp.int32, (rows // SIDE, 8, C), 1)
    x = v.reshape(rows // SIDE, 2, 8, C)
    low, high = x[:, 0], x[:, 1]
    low_up, high_up = pltpu.roll(low, 1, 1), pltpu.roll(high, 1, 1)
    low_down, high_down = pltpu.roll(low, 7, 1), pltpu.roll(high, 7, 1)
    left = (jnp.where(sub == 0, 0.0, low_up), jnp.where(sub == 0, low_up, high_up))
    right = (jnp.where(sub == 7, high_down, low_down), jnp.where(sub == 7, 0.0, high_down))
    bufs[0, i, at, :] = jnp.stack(left, axis=1).reshape(rows, C).astype(BF16)
    bufs[1, i, at, :] = v.astype(BF16)
    bufs[2, i, at, :] = jnp.stack(right, axis=1).reshape(rows, C).astype(BF16)


def taps(bufs, flip):
    images = bufs.shape[1]
    out = []
    for dr in (-1, 0, 1):
        for dc in (-1, 0, 1):
            sr, sc = (-dr, -dc) if flip else (dr, dc)
            piece = bufs[sc + 1, :, PAD + SIDE * sr : PAD + SIDE * sr + POS, :]
            out.append(piece.reshape(images * POS, C))
    return out


def conv_forward(bufs, w, l, row):
    return dot_nn(jnp.concatenate(taps(bufs, False), axis=1), w[l, row : row + 9 * C, :])


def conv_input_grad(bufs, w, l, row):
    parts = [w[l, row + t * C : row + (t + 1) * C, :] for t in range(9)]
    return dot_nt(jnp.concatenate(taps(bufs, True), axis=1), jnp.concatenate(parts, axis=1))


def conv_weight_grad(act_t, bufs, grad, l, row):
    left = act_t[...]
    for t, piece in enumerate(taps(bufs, True)):
        grad[l, row + t * C : row + (t + 1) * C, :] = dot_nn(left, piece).astype(BF16)


def silu(v):
    h = 0.5 * v
    return h + h * jnp.tanh(h)


def silu_parts(v):
    h = 0.5 * v
    t = jnp.tanh(h)
    return h + h * t, (1.0 + t) + h * (1.0 - t * t)


def clear_pads(bufs):
    zero = jnp.zeros(bufs.shape[:2] + (PAD, C), BF16)
    bufs[:, :, 0:PAD, :] = zero
    bufs[:, :, PAD + POS :, :] = zero


def split_qkv(w, l, qkvw, tmp):
    for h in range(2):
        tmp[h] = w[l, R_QKV : R_QKV + 3 * C, h * HALF : (h + 1) * HALF].astype(F32)
    for j in range(3):
        for h in range(2):
            at = j * C + h * HALF
            qkvw[:, at : at + HALF] = tmp[h, pl.ds(j, C, stride=3), :].astype(BF16)


def norm_sums(x):
    pivot = x[0:1]
    d = x - pivot
    return colsum(d), colsum(d * d), pivot


def norm_stats(sums):
    fill = [jnp.zeros((4 - len(sums), C), F32)]
    s1, s2, pivot = [jnp.concatenate([a[k] for a in sums] + fill, axis=0) for k in range(3)]
    centre = group_mean(jnp.concatenate([pivot, pivot], axis=0) * POS)[0:4]
    off = pivot - centre
    first = s1 + POS * off
    second = s2 + off * (2.0 * s1 + POS * off)
    means = group_mean(jnp.concatenate([first, second], axis=0))
    spread = jnp.maximum(means[4:8] - jnp.square(means[0:4]), 0.0)
    return centre + means[0:4], lax.rsqrt(spread + NORM_EPS)


def norm_map(gain, mg, mc, mean, inv):
    on_value = inv * inv * mc
    return inv * gain, on_value, inv * mg - mean * on_value


def two_means(a, b):
    rows = jnp.concatenate([a, b] * 4, axis=0)
    means = group_mean(rows)
    return means[0:1], means[1:2]


def tap_rows(bufs, flip, which):
    out = []
    for dr in (-1, 0, 1):
        for dc in (-1, 0, 1):
            sr, sc = (-dr, -dc) if flip else (dr, dc)
            at = slice(PAD + SIDE * sr, PAD + SIDE * sr + POS)
            piece = jnp.concatenate([bufs[sc + 1, i, at, :] for i in which], axis=0)
            out.append(piece)
    return out


def layer_forward(l, w, small, eo, xs, h1, y, qkv, att, o, st, bufs, nbuf, qkvw, tmp, staged, pump):
    images = h1.shape[1]
    split_qkv(w, l, qkvw, tmp)
    mod = dot_nn(eo[...], w[l, R_EMB : R_EMB + 4 * C, :])
    ma = mod[0:4] + small[l, 5:6, :]
    mb = mod[4:8] + small[l, 6:7, :]
    for i in range(images):
        st[l, i, S_MA : S_MA + 1, :] = ma[i : i + 1]
        st[l, i, S_MB : S_MB + 1, :] = mb[i : i + 1]

    sums = {}

    def row(k):
        return small[l, k : k + 1, :]

    def keep(which, mean, inv, at):
        for k, i in enumerate(which):
            st[l, i, at : at + 1, :] = mean[k : k + 1]
            st[l, i, at + 1 : at + 2, :] = inv[k : k + 1]

    def first(which):
        mean, inv = norm_stats([norm_sums(xs[l, i]) for i in which])
        keep(which, mean, inv, S_M1)
        for k, i in enumerate(which):
            a = inv[k : k + 1] * row(0)
            b = row(1) - mean[k : k + 1] * a
            for r in range(0, POS, CHUNK):
                v = xs[l, i, r : r + CHUNK, :] * a + b
                put_shifted(bufs, i, r, silu(v))

    def conv(which, at):
        left = jnp.concatenate(tap_rows(bufs, False, which), axis=1)
        return dot_nn(left, w[l, at : at + 9 * C, :])

    def conv_one(which):
        out = conv(which, R_CONV1)
        for k, i in enumerate(which):
            own = out[k * POS : (k + 1) * POS]
            own = own + row(2)
            sums[i] = norm_sums(own)
            h1[l, i] = own

    def second(which):
        mean, inv = norm_stats([sums[i] for i in which])
        keep(which, mean, inv, S_M2)
        for k, i in enumerate(which):
            gain = 1.0 + ma[i : i + 1]
            a = inv[k : k + 1] * row(3) * gain
            b = row(4) * gain + mb[i : i + 1] - mean[k : k + 1] * a
            for r in range(0, POS, CHUNK):
                v = h1[l, i, r : r + CHUNK, :] * a + b
                put_shifted(bufs, i, r, silu(v))

    def conv_two(which):
        out = conv(which, R_CONV2) + row(7)
        for k, i in enumerate(which):
            own = (xs[l, i] + out[k * POS : (k + 1) * POS]) * RS
            sums[i] = norm_sums(own)
            y[l, i] = own

    def third(which):
        mean, inv = norm_stats([sums[i] for i in which])
        keep(which, mean, inv, S_M3)
        for k, i in enumerate(which):
            a = inv[k : k + 1] * row(8)
            b = row(9) - mean[k : k + 1] * a
            for r in range(0, POS, CHUNK):
                v = y[l, i, r : r + CHUNK, :] * a + b
                nbuf[i, r : r + CHUNK, :] = v.astype(BF16)

    def project_in(which):
        n = jnp.concatenate([nbuf[i] for i in which], axis=0)
        for j, at in ((0, 10), (1, None), (2, 11)):
            part = dot_nn(n, qkvw[:, j * C : (j + 1) * C])
            if at is not None:
                part = part + row(at)
            part = part.astype(BF16)
            for k, i in enumerate(which):
                qkv[l, i, :, j * C : (j + 1) * C] = part[k * POS : (k + 1) * POS]

    def attend(which):
        scores = [dot_nt(qkv[l, i, :, 0:C], qkv[l, i, :, C : 2 * C]) for i in which]
        for s, i in zip(scores, which):
            e = jnp.exp((s - jnp.max(s, axis=1, keepdims=True)) * (C**-0.5))
            p = (e * (1.0 / jnp.sum(e, axis=1, keepdims=True))).astype(BF16)
            att[l, i] = p
            o[l, i] = dot_nn(p, qkv[l, i, :, 2 * C :]).astype(BF16)

    def project_out(which):
        left = jnp.concatenate([o[l, i] for i in which], axis=0)
        out = dot_nn(left, w[l, R_PROJ:, :]) + row(12)
        for k, i in enumerate(which):
            xs[l + 1, i] = (y[l, i] + out[k * POS : (k + 1) * POS]) * RS

    steps = (first, conv_one, second, conv_two, third, project_in, attend, project_out)
    if not staged:
        for step in steps:
            step(range(images))
            pump(l)
    else:
        stagger([lambda i, step=step: step([i]) for step in steps], images, lambda: pump(l))


def layer_backward(
    l, w, small, eo, xs, h1, y, qkv, att, o, st, g, bufs, nbuf, qkvw, tmp, dn, dqkv, act_t,
    grad, sgrad, pump, need_dx=None,
):
    want = grad is not None
    images = h1.shape[1]
    which = range(images)
    flat = images * POS
    scale = C**-0.5
    split_qkv(w, l, qkvw, tmp)

    def row(k):
        return small[l, k : k + 1, :]

    def rows8(rows):
        return jnp.concatenate(list(rows) + [jnp.zeros((8 - len(rows), C), F32)], axis=0)

    zero = jnp.zeros((1, C), F32)
    gps, c1, c2, p1, p2 = {}, {}, {}, {}, {}
    total = {7: zero, 2: zero}
    gains = [1.0 + st[l, i, S_MA : S_MA + 1, :] for i in which]

    def project_out(i):
        gps[i] = (g[i] * RS).astype(BF16)
        nbuf[i] = dot_nt(gps[i], w[l, R_PROJ:, :]).astype(BF16)

    def attend(i):
        p = att[l, i]
        pf = p.astype(F32)
        dp = dot_nt(nbuf[i], qkv[l, i, :, 2 * C :])
        ds = (pf * (dp - jnp.sum(dp * pf, axis=1, keepdims=True))).astype(BF16)
        dqkv[i, :, 0:C] = (dot_nn(ds, qkv[l, i, :, C : 2 * C]) * scale).astype(BF16)
        dqkv[i, :, C : 2 * C] = (dot_tn(ds, qkv[l, i, :, 0:C]) * scale).astype(BF16)
        dqkv[i, :, 2 * C :] = dot_tn(p, nbuf[i]).astype(BF16)

    def project_in(i):
        mean, inv = st[l, i, S_M3 : S_M3 + 1, :], st[l, i, S_I3 : S_I3 + 1, :]
        d = dot_nt(dqkv[i], qkvw[...])
        dn[i] = d
        c1[i] = colsum(d)
        c2[i] = colsum(d * (y[l, i] - mean)) * inv

    def third(i):
        mean, inv = st[l, i, S_M3 : S_M3 + 1, :], st[l, i, S_I3 : S_I3 + 1, :]
        mg, mc = two_means(row(8) * c1[i], row(8) * c2[i])
        on_grad, on_value, offset = norm_map(row(8) * RS, mg * RS, mc * RS, mean, inv)
        act_a = inv * row(8)
        act_b = row(9) - mean * act_a
        for r in range(0, POS, CHUNK):
            value = y[l, i, r : r + CHUNK, :]
            gm = g[i, r : r + CHUNK, :] * (RS * RS) + dn[i, r : r + CHUNK, :] * on_grad
            gm = gm - (value * on_value + offset)
            g[i, r : r + CHUNK, :] = gm
            put_shifted(bufs, i, r, gm)
            if want:
                nbuf[i, r : r + CHUNK, :] = (value * act_a + act_b).astype(BF16)
                total[7] = total[7] + colsum(gm)

    def conv_grad(i, at):
        left = jnp.concatenate(tap_rows(bufs, True, [i]), axis=1)
        parts = [w[l, at + t * C : at + (t + 1) * C, :] for t in range(9)]
        dn[i] = dot_nt(left, jnp.concatenate(parts, axis=1))

    def activation(i, src, mean, inv, a, b, act=None):
        s1, s2 = zero, zero
        for r in range(0, POS, CHUNK):
            u = src[l, i, r : r + CHUNK, :] - mean
            act_value, slope = silu_parts(u * (inv * a) + b)
            d = dn[i, r : r + CHUNK, :] * slope
            dn[i, r : r + CHUNK, :] = d
            s1 = s1 + colsum(d)
            s2 = s2 + colsum(d * u)
            if act is not None:
                act[i, r : r + CHUNK, :] = act_value.astype(BF16)
        p1[i], p2[i] = s1 * 0.5, s2 * (0.5 * inv)

    def second_a(i):
        mean, inv = st[l, i, S_M2 : S_M2 + 1, :], st[l, i, S_I2 : S_I2 + 1, :]
        b = row(4) * gains[i] + st[l, i, S_MB : S_MB + 1, :]
        activation(i, h1, mean, inv, row(3) * gains[i], b, nbuf if want else None)

    def second_b(i):
        mean, inv = st[l, i, S_M2 : S_M2 + 1, :], st[l, i, S_I2 : S_I2 + 1, :]
        full = row(3) * gains[i]
        mg, mc = two_means(full * p1[i], full * p2[i])
        on_grad, on_value, offset = norm_map(full, mg, mc, mean, inv)
        for r in range(0, POS, CHUNK):
            dh = dn[i, r : r + CHUNK, :] * (0.5 * on_grad) - (
                h1[l, i, r : r + CHUNK, :] * on_value + offset
            )
            put_shifted(bufs, i, r, dh)
            if want:
                total[2] = total[2] + colsum(dh)

    def first_a(i):
        mean, inv = st[l, i, S_M1 : S_M1 + 1, :], st[l, i, S_I1 : S_I1 + 1, :]
        activation(i, xs, mean, inv, row(0), row(1))

    def first_act(i):
        mean, inv = st[l, i, S_M1 : S_M1 + 1, :], st[l, i, S_I1 : S_I1 + 1, :]
        a = inv * row(0)
        b = row(1) - mean * a
        for r in range(0, POS, CHUNK):
            v = xs[l, i, r : r + CHUNK, :] * a + b
            nbuf[i, r : r + CHUNK, :] = silu(v).astype(BF16)

    def first_b(i):
        mean, inv = st[l, i, S_M1 : S_M1 + 1, :], st[l, i, S_I1 : S_I1 + 1, :]
        mg, mc = two_means(row(0) * p1[i], row(0) * p2[i])
        on_grad, on_value, offset = norm_map(row(0), mg, mc, mean, inv)
        for r in range(0, POS, CHUNK):
            dx = dn[i, r : r + CHUNK, :] * (0.5 * on_grad) - (
                xs[l, i, r : r + CHUNK, :] * on_value + offset
            )
            g[i, r : r + CHUNK, :] = g[i, r : r + CHUNK, :] + dx

    upper = [project_out, attend, project_in, third, lambda i: conv_grad(i, R_CONV2)]
    lower = [lambda i: conv_grad(i, R_CONV1), first_a]
    if not want:
        stagger(upper + [second_a, second_b] + lower + [first_b], images, lambda: pump(l))
        return
    stagger(upper, images, lambda: pump(l))
    gp = jnp.concatenate([gps[i] for i in which], axis=0)
    grad[l, R_PROJ:, :] = dot_tn(o[l].reshape(flat, C), gp).astype(BF16)
    sgrad[l, 12:13, :] = colsum(gp.astype(F32))
    sgrad[l, 7:8, :] = total[7]
    sgrad[l, 8:9, :] = colsum(rows8([c2[i] for i in which]))
    sgrad[l, 9:10, :] = colsum(rows8([c1[i] for i in which]))
    act_t[...] = nbuf[...].reshape(flat, C).T
    for j in range(3):
        dj = dqkv[:, :, j * C : (j + 1) * C].reshape(flat, C)
        part = dot_nn(act_t[...], dj)
        for h in range(2):
            tmp[h, pl.ds(j, C, stride=3), :] = part[:, h * HALF : (h + 1) * HALF]
        if j != 1:
            sgrad[l, 10 + j // 2 : 11 + j // 2, :] = colsum(dj.astype(F32))
    for h in range(2):
        grad[l, R_QKV : R_QKV + 3 * C, h * HALF : (h + 1) * HALF] = tmp[h].astype(BF16)
    for i in which:
        second_a(i)
    pump(l)
    act_t[...] = nbuf[...].reshape(flat, C).T
    conv_weight_grad(act_t, bufs, grad, l, R_CONV2)
    p18, p28, modgain = [rows8([a[i] for i in which]) for a in (p1, p2, gains)]
    dma = row(3) * p28 + row(4) * p18
    sgrad[l, 3:4, :] = colsum(modgain * p28)
    sgrad[l, 4:5, :] = colsum(modgain * p18)
    sgrad[l, 5:6, :] = colsum(dma)
    sgrad[l, 6:7, :] = colsum(p18)
    grad[l, R_EMB : R_EMB + 4 * C, :] = embed_grad(
        eo, jnp.concatenate([dma[0:4], p18[0:4]], axis=0)
    ).astype(BF16)
    pump(l)
    stagger([second_b, first_act], images, lambda: pump(l))
    act_t[...] = nbuf[...].reshape(flat, C).T
    conv_weight_grad(act_t, bufs, grad, l, R_CONV1)
    pump(l)
    stagger(lower, images, lambda: pump(l))
    sgrad[l, 2:3, :] = total[2]
    sgrad[l, 0:1, :] = colsum(rows8([p2[i] for i in which]))
    sgrad[l, 1:2, :] = colsum(rows8([p1[i] for i in which]))

    @pl.when(l == 1)
    def _():
        for i in which:
            first_b(i)


def embed_grad(eo, dm):
    parts, rest = [], dm
    for _ in range(3):
        parts.append(rest.astype(BF16))
        rest = rest - parts[-1].astype(F32)
    left = eo[...]
    return dot_tn(jnp.concatenate([left, left], axis=0), jnp.concatenate(parts[:2], axis=0)) + dot_tn(
        left, parts[2]
    )


def saved_shapes(images):
    return [
        jax.ShapeDtypeStruct((3, images, POS, C), F32),
        jax.ShapeDtypeStruct((2, images, POS, C), F32),
        jax.ShapeDtypeStruct((2, images, POS, C), F32),
        jax.ShapeDtypeStruct((2, images, POS, 3 * C), BF16),
        jax.ShapeDtypeStruct((2, images, POS, POS), BF16),
        jax.ShapeDtypeStruct((2, images, POS, C), BF16),
        jax.ShapeDtypeStruct((2, images, 8, C), F32),
    ]


def forward_kernel(staged, x0, w, small, eo, xs, h1, y, qkv, att, o, st, bufs, nbuf, qkvw, tmp):
    clear_pads(bufs)
    xs[0] = x0[...]

    def body(l, _):
        layer_forward(
            l, w, small, eo, xs, h1, y, qkv, att, o, st, bufs, nbuf, qkvw, tmp, staged, no_pump
        )
        return 0

    lax.fori_loop(0, 2, body, 0)


def backward_kernel(want, *refs):
    cot, w, small, eo, xs, h1, y, qkv, att, o, st, g = refs[:12]
    refs = refs[12:]
    if want:
        grad, sgrad = refs[:2]
        refs = refs[2:]
    else:
        grad, sgrad = None, None
    bufs, nbuf, qkvw, tmp, dn, dqkv, act_t = refs
    clear_pads(bufs)
    g[...] = cot[...]
    if want:
        sgrad[...] = jnp.zeros(sgrad.shape, F32)

    def body(k, _):
        layer_backward(
            1 - k, w, small, eo, xs, h1, y, qkv, att, o, st, g, bufs, nbuf, qkvw, tmp, dn,
            dqkv, act_t, grad, sgrad, no_pump,
        )
        return 0

    lax.fori_loop(0, 2, body, 0)


def vm(n):
    return [pl.BlockSpec(memory_space=pltpu.VMEM)] * n


def scratch_forward(images):
    return [
        pltpu.VMEM((3, images, POS + 2 * PAD, C), BF16),
        pltpu.VMEM((images, POS, C), BF16),
        pltpu.VMEM((C, 3 * C), BF16),
        pltpu.VMEM((2, 3 * C, HALF), F32),
    ]


def run_forward(x0, w, small, eo, staged=False):
    images = x0.shape[0]
    return pl.pallas_call(
        functools.partial(forward_kernel, staged),
        out_shape=saved_shapes(images),
        in_specs=vm(4),
        out_specs=vm(7),
        scratch_shapes=scratch_forward(images),
        compiler_params=pltpu.CompilerParams(vmem_limit_bytes=VMEM_LIMIT),
    )(x0, w, small, eo)


def run_backward(cot, w, small, eo, saved, want):
    images = cot.shape[0]
    outs = [jax.ShapeDtypeStruct(cot.shape, F32)]
    if want:
        outs += [
            jax.ShapeDtypeStruct((2, ROWS, C), BF16),
            jax.ShapeDtypeStruct((2, 16, C), F32),
        ]
    return pl.pallas_call(
        functools.partial(backward_kernel, want),
        out_shape=outs,
        in_specs=vm(11),
        out_specs=vm(len(outs)),
        scratch_shapes=scratch_forward(images)
        + [
            pltpu.VMEM((images, POS, C), F32),
            pltpu.VMEM((images, POS, 3 * C), BF16),
            pltpu.VMEM((C, images * POS), BF16),
        ],
        compiler_params=pltpu.CompilerParams(vmem_limit_bytes=VMEM_LIMIT),
    )(cot, w, small, eo, *saved)


PLANES, PLANE = 4, 4
MESH = pl.DeviceIdType.MESH


class Place:
    def __init__(self):
        self.sec = lax.axis_index("section")
        self.d = lax.axis_index("dp")
        self.x = lax.rem(self.d, 2)
        self.y = lax.rem(self.d // 2, 2)
        self.z = self.d // PLANE
        self.seat = self.sec * PLANE + lax.rem(self.d, PLANE)
        self.sib = {"section": 1 - self.sec}
        self.xn = {"dp": self.d + 1 - 2 * self.x}
        self.yn = {"dp": self.d + 2 - 4 * self.y}

    def plane(self, j):
        return lax.rem(self.z + j + PLANES, PLANES)

    def zpeer(self, j):
        return {"dp": self.plane(j) * PLANE + lax.rem(self.d, PLANE)}

    def plane_peer(self, j):
        seat = lax.rem(self.seat + j, 2 * PLANE)
        return {"section": seat // PLANE, "dp": self.z * PLANE + lax.rem(seat, PLANE)}

    def meet(self):
        barrier = pltpu.get_barrier_semaphore()
        others = [self.plane_peer(j) for j in range(1, 8)] + [self.zpeer(j) for j in (1, 2, 3)]
        for other in others:
            pl.semaphore_signal(barrier, inc=1, device_id=other, device_id_type=MESH)
        pl.semaphore_wait(barrier, len(others))


def remote(src, dst, send, recv, target):
    return pltpu.make_async_remote_copy(
        src_ref=src, dst_ref=dst, send_sem=send, recv_sem=recv,
        device_id=target, device_id_type=MESH,
    )


Z1, X1, Y1, X2, Y2, S_OWN, S_X, S_Y, S_DA, S_DB = range(0, 40, 4)
Z_UP, Z_DOWN = 40, 41
SLOTS = 42


class Gather:
    def __init__(self, me, net, stage, local_sem, send_sem, recv_sem):
        self.me, self.net, self.stage = me, net, stage
        self.local_sem, self.send_sem, self.recv_sem = local_sem, send_sem, recv_sem
        self.part = stage.shape[0]
        self.half = self.part // 2

    def near(self, k):
        z = self.me.z
        if k == 1:
            return z + 1 - 2 * lax.rem(z, 2), 3 - z
        return (z, z) if k == 0 else (2 - z // 2 if k == 2 else 3 - 3 * (z // 2), 3 * z - 3)

    def rows(self, plane, y, x, lo, count):
        at = (plane * PLANE + y * 2 + x) * self.part + lo
        return self.net.at[self.me.sec, pl.ds(pl.multiple_of(at, 16), count)]

    def own(self, plane):
        return self.rows(plane, self.me.y, self.me.x, 0, self.part)

    def at_plane(self, plane):
        return {"dp": plane * PLANE + lax.rem(self.me.d, PLANE)}

    def send(self, slot, piece, target, src=None, sent=None):
        src = piece if src is None else src
        sent = slot if sent is None else sent
        remote(src, piece, self.send_sem.at[sent], self.recv_sem.at[slot], target).start()

    def arrived(self, slot, piece):
        remote(
            piece, piece, self.send_sem.at[slot], self.recv_sem.at[slot], self.me.sib
        ).wait_recv()

    def local(self):
        return pltpu.make_async_copy(self.stage, self.own(self.me.z), self.local_sem)

    def begin(self):
        me = self.me
        z, own = me.z, self.own(me.z)
        pl.when(z < 3)(lambda: self.send(Z1 + z, own, self.at_plane(z + 1), self.stage, Z_UP))
        pl.when(z > 0)(lambda: self.send(Z1 + z, own, self.at_plane(z - 1), self.stage, Z_DOWN))
        for slot, target in ((X1, me.xn), (Y1, me.yn), (S_OWN, me.sib)):
            self.send(slot + z, own, target, self.stage)
        self.local().start()

    def phase1(self):
        def step(k):
            me = self.me
            plane, target = self.near(k)
            rows = self.own(plane)
            self.arrived(Z1 + plane, rows)
            pl.when(me.z * (3 - me.z) > 0)(
                lambda: self.send(Z1 + plane, rows, self.at_plane(target))
            )
            for slot, to in ((X1, me.xn), (Y1, me.yn), (S_OWN, me.sib)):
                self.send(slot + plane, rows, to)

        return [lambda k=k: step(k) for k in (1, 2, 3)]

    def phase2(self):
        me, part, half = self.me, self.part, self.half

        def step_x(k):
            plane, _ = self.near(k)
            self.arrived(X1 + plane, self.rows(plane, me.y, 1 - me.x, 0, part))
            self.send(Y2 + plane, self.rows(plane, me.y, 1 - me.x, 0, half), me.yn)
            self.send(S_X + plane, self.rows(plane, me.y, 1 - me.x, 0, part), me.sib)

        def step_y(k):
            plane, _ = self.near(k)
            self.arrived(Y1 + plane, self.rows(plane, 1 - me.y, me.x, 0, part))
            self.send(X2 + plane, self.rows(plane, 1 - me.y, me.x, half, half), me.xn)
            self.send(S_Y + plane, self.rows(plane, 1 - me.y, me.x, 0, part), me.sib)

        return [lambda f=f, k=k: f(k) for k in range(PLANES) for f in (step_x, step_y)]

    def phase3(self):
        def step(k, slot, to, lo):
            me = self.me
            plane, _ = self.near(k)
            where = self.rows(plane, 1 - me.y, 1 - me.x, lo, self.half)
            self.arrived(slot + plane, where)
            self.send(to + plane, where, me.sib)

        return [
            lambda k=k, a=a: step(k, *a)
            for k in range(PLANES)
            for a in ((Y2, S_DA, 0), (X2, S_DB, self.half))
        ]

    def finish(self):
        def step():
            for slot in range(S_OWN, Z_UP):
                count = self.part if slot < S_DA else self.half
                self.arrived(slot, self.rows(0, 0, 0, 0, count))
            self.local().wait()

        return [step]

    def sent(self, slot, count):
        piece = self.rows(0, 0, 0, 0, count)
        remote(
            piece, piece, self.send_sem.at[slot], self.recv_sem.at[0], self.me.sib
        ).wait_send()

    def drain(self):
        me, part = self.me, self.part
        pl.when(me.z < 3)(lambda: self.sent(Z_UP, part))
        pl.when(me.z > 0)(lambda: self.sent(Z_DOWN, part))

        @pl.when(me.z * (3 - me.z) > 0)
        def _():
            for k in (1, 2, 3):
                self.sent(Z1 + self.near(k)[0], part)

        for slot in range(X1, Z_UP):
            whole = slot < X2 or S_OWN <= slot < S_DA
            self.sent(slot, part if whole else self.half)


A_SLOT, B_SLOT, C_SLOT, D_SLOT = 0, 4, 20, 28
R_SLOTS = 31


class Reduce:
    def __init__(self, me, big, shard, sib, there, rb, rc, rd, ssem, rsem):
        self.me, self.big, self.shard = me, big, shard
        self.sib, self.there, self.rb, self.rc, self.rd = sib, there, rb, rc, rd
        self.ssem, self.rsem = ssem, rsem
        self.part = shard.shape[0]
        self.half = self.part // 2
        self.span = PLANE * self.part

    def zt(self, k):
        return (3, 2, 0, 1)[k]

    def block(self, k):
        return pl.ds(self.zt(k) * self.span, self.span)

    def piece(self, k, y, x, lo, count):
        at = (self.zt(k) * PLANE + y * 2 + x) * self.part + lo
        return pl.ds(pl.multiple_of(at, 16), count)

    def send(self, src, dst, slot, target):
        remote(src, dst, self.ssem.at[slot], self.rsem.at[slot], target).start()

    def arrived(self, dst, slot):
        remote(dst, dst, self.ssem.at[slot], self.rsem.at[slot], self.me.sib).wait_recv()

    def begin(self):
        for k in range(PLANES):
            self.begin_block(k)

    def begin_block(self, k):
        at = self.block(k)
        self.send(self.big.at[1 - self.me.sec, at], self.there.at[at], A_SLOT + k, self.me.sib)

    def stage_a(self, k):
        me, half = self.me, self.half
        self.arrived(self.sib.at[self.block(k)], A_SLOT + k)
        base = self.zt(k) * self.span

        def body(i, _):
            at = pl.ds(pl.multiple_of(base + i * half, 16), half)
            self.big[me.sec, at, :] = (
                self.big[me.sec, at, :].astype(F32) + self.sib[at, :].astype(F32)
            ).astype(BF16)
            return 0

        lax.fori_loop(0, 2 * PLANE, body, 0)
        for j in range(2):
            self.send(
                self.big.at[me.sec, self.piece(k, 1 - me.y, j, 0, half)], self.rb.at[k, j],
                B_SLOT + 4 * k + j, me.yn,
            )
            self.send(
                self.big.at[me.sec, self.piece(k, j, 1 - me.x, half, half)], self.rb.at[k, 2 + j],
                B_SLOT + 4 * k + 2 + j, me.xn,
            )

    def join(self, where, other):
        self.big[self.me.sec, where, :] = (
            self.big[self.me.sec, where, :].astype(F32) + other.astype(F32)
        ).astype(BF16)

    def stage_c(self, k):
        me, half = self.me, self.half
        for j in range(4):
            self.arrived(self.rb.at[k, j], B_SLOT + 4 * k + j)
            y, x, lo = (me.y, j, 0) if j < 2 else (j - 2, me.x, half)
            self.join(self.piece(k, y, x, lo, half), self.rb[k, j])
        self.send(
            self.big.at[me.sec, self.piece(k, me.y, 1 - me.x, 0, half)], self.rc.at[k, 0],
            C_SLOT + 2 * k, me.xn,
        )
        self.send(
            self.big.at[me.sec, self.piece(k, 1 - me.y, me.x, half, half)], self.rc.at[k, 1],
            C_SLOT + 2 * k + 1, me.yn,
        )

    def stage_d(self, k):
        me, half, zt = self.me, self.half, self.zt(k)
        for j in range(2):
            self.arrived(self.rc.at[k, j], C_SLOT + 2 * k + j)
            self.join(self.piece(k, me.y, me.x, j * half, half), self.rc[k, j])

        @pl.when(me.z != zt)
        def _():
            self.send(
                self.big.at[me.sec, self.piece(k, me.y, me.x, 0, self.part)],
                self.rd.at[lax.rem(zt - me.z + PLANES, PLANES) - 1],
                D_SLOT + lax.rem(zt - me.z + PLANES, PLANES) - 1,
                {"dp": zt * PLANE + lax.rem(me.d, PLANE)},
            )

    def stage_e(self):
        for j in range(PLANES - 1):
            self.arrived(self.rd.at[j], D_SLOT + j)
        at = pl.ds(pl.multiple_of(self.me.d * self.part, 16), self.part)
        self.shard[...] = (
            self.big[self.me.sec, at, :].astype(F32)
            + self.rd[0].astype(F32) + (self.rd[1].astype(F32) + self.rd[2].astype(F32))
        )

    def steps(self):
        out = []
        for t in range(PLANES + 2):
            for stage, lag in ((self.stage_a, 0), (self.stage_c, 1), (self.stage_d, 2)):
                if 0 <= t - lag < PLANES:
                    out.append(lambda stage=stage, k=t - lag: stage(k))
        return out

    def drain(self, lo=0, hi=R_SLOTS):
        for slot in range(lo, hi):
            if slot < B_SLOT:
                piece = self.there.at[pl.ds(0, self.span)]
            elif slot < D_SLOT:
                piece = self.rb.at[0, 0]
            else:
                piece = self.rd.at[0]
            remote(piece, piece, self.ssem.at[slot], self.rsem.at[slot], self.me.sib).wait_send()


def reduce_scratch(part):
    half = part // 2
    return [
        pltpu.VMEM((PLANES, 4, half, C), BF16),
        pltpu.VMEM((PLANES, 2, half, C), BF16),
        pltpu.VMEM((PLANES - 1, part, C), BF16),
        pltpu.SemaphoreType.DMA((R_SLOTS,)),
        pltpu.SemaphoreType.DMA((R_SLOTS,)),
    ]


class Totals:
    def __init__(self, me, buf, recv, ssem, rsem):
        self.me, self.buf, self.recv, self.ssem, self.rsem = me, buf, recv, ssem, rsem

    def send(self, src, dst, slot, target):
        remote(src, dst, self.ssem.at[slot], self.rsem.at[slot], target).start()

    def arrived(self, dst, slot):
        remote(dst, dst, self.ssem.at[slot], self.rsem.at[slot], self.me.sib).wait_recv()

    def begin(self, first):
        self.send(first, self.recv.at[0], 0, self.me.sib)

    def steps(self):
        me, buf, recv = self.me, self.buf, self.recv

        def one():
            self.arrived(recv.at[0], 0)
            buf[1] = buf[0] + recv[0]
            self.send(buf.at[1], recv.at[1], 1, me.xn)

        def two():
            self.arrived(recv.at[1], 1)
            buf[2] = buf[1] + recv[1]
            self.send(buf.at[2], recv.at[2], 2, me.yn)

        def three():
            self.arrived(recv.at[2], 2)
            buf[3] = buf[2] + recv[2]
            recv[3 + me.z] = buf[3]
            for j in (1, 2, 3):
                self.send(buf.at[3], recv.at[3 + me.z], 2 + j, me.zpeer(j))

        return [one, two, three]

    def result(self):
        for j in (1, 2, 3):
            self.arrived(self.recv.at[3 + self.me.plane(-j)], 2 + j)
        return (self.recv[3] + self.recv[4]) + (self.recv[5] + self.recv[6])

    def drain(self):
        for slot in range(6):
            piece = self.recv.at[0]
            remote(piece, piece, self.ssem.at[slot], self.rsem.at[slot], self.me.sib).wait_send()


class Squares:
    def __init__(self, me, own, recv, ssem, rsem):
        self.me, self.own, self.recv, self.ssem, self.rsem = me, own, recv, ssem, rsem

    def hop(self, src, base, mine, peers, slots):
        for j, target in peers:
            dst = self.recv.at[base + mine]
            remote(src, dst, self.ssem.at[slots + j], self.rsem.at[slots + j], target).start()
        self.recv[base + mine] = src[...]
        for j, _ in peers:
            dst = self.recv.at[base]
            remote(dst, dst, self.ssem.at[slots + j], self.rsem.at[slots + j], self.me.sib).wait_recv()

    def run(self):
        me, recv = self.me, self.recv
        self.hop(self.own.at[0], 0, me.seat, [(j, me.plane_peer(j)) for j in range(1, 8)], -1)
        pairs = [recv[2 * k] + recv[2 * k + 1] for k in range(4)]
        self.own[1] = (pairs[0] + pairs[1]) + (pairs[2] + pairs[3])
        self.hop(self.own.at[1], 8, me.z, [(j, me.zpeer(j)) for j in (1, 2, 3)], 6)
        return (recv[8] + recv[9]) + (recv[10] + recv[11])

    def drain(self):
        for slot in range(10):
            piece = self.recv.at[0]
            remote(piece, piece, self.ssem.at[slot], self.rsem.at[slot], self.me.sib).wait_send()


def squares_scratch(shape):
    return [
        pltpu.VMEM((2,) + shape, F32),
        pltpu.VMEM((12,) + shape, F32),
        pltpu.SemaphoreType.DMA((10,)),
        pltpu.SemaphoreType.DMA((10,)),
    ]


def totals_scratch(shape):
    return [
        pltpu.VMEM((4,) + shape, F32),
        pltpu.VMEM((7,) + shape, F32),
        pltpu.SemaphoreType.DMA((6,)),
        pltpu.SemaphoreType.DMA((6,)),
    ]


def saved_scratch(images):
    return [pltpu.VMEM(a.shape, a.dtype) for a in saved_shapes(images)]


def backward_scratch(images):
    return scratch_forward(images) + [
        pltpu.VMEM((images, POS, C), F32),
        pltpu.VMEM((images, POS, 3 * C), BF16),
        pltpu.VMEM((C, images * POS), BF16),
    ]


GEN_TOTAL = SIGMA_INIT**2 + SIGMA_DATA**2
GEN_IN = GEN_TOTAL**-0.5
GEN_SKIP = SIGMA_DATA**2 / GEN_TOTAL
GEN_OUT = SIGMA_INIT * SIGMA_DATA * GEN_TOTAL**-0.5
T_IN, T_SKIP, T_OUT, T_SIGMA, T_FACTOR = range(5)


def fill_embed(eo, sigmas):
    at = lax.broadcasted_iota(jnp.int32, (8, 4 * C), 1)
    side = lax.broadcasted_iota(jnp.int32, (8, 4 * C), 0) // 4
    k = at // 2
    power = (k & (C - 1)).astype(F32) * (1.0 / C)
    rows = sigmas + [jnp.ones_like(sigmas[0])] * (4 - len(sigmas))
    angle = jnp.log(jnp.concatenate(rows + rows, axis=0)) * 0.25 * jnp.exp(power * -LOG_10000)
    wave = jnp.where(k < C, jnp.cos(angle), jnp.sin(angle))
    eo[...] = jnp.where((at & 1) == side, wave, 0.0).astype(BF16)


LOG_10000 = 9.210340371976184


def step_kernel(*refs):
    (
        z_all, eps_all, levels, counts, gen_w, fake_w, teacher_w, gen_small, fake_small,
        teacher_small,
        gw_out, sv_x, sv_h, sv_y, sv_q, sv_a, sv_o, sv_s, gshard, fshard, stot, sqtot,
        *refs,
    ) = refs
    gen_out = (sv_x, sv_h, sv_y, sv_q, sv_a, sv_o, sv_s)
    w_gen, w_fake, w_teach = refs[:3]
    sv_one, sv_two = refs[3:10], refs[10:17]
    bufs, nbuf, qkvw, tmp, dn, dqkv, act_t = refs[17:24]
    zb, eb, g, stage, local_sem, send_sem, recv_sem, copy_sem = refs[24:32]
    smalls, small_sem, gen_eo, score_eo, tab, sgrads, part_sums = refs[32:39]
    fake_refs, gen_refs = refs[39:44], refs[44:49]
    small_refs, square_refs = refs[49:53], refs[53:57]
    sib, free_sem = refs[57:59]
    g2 = sv_two[0].at[2]
    images = zb.shape[0]
    me = Place()
    start = me.sec * images

    def run(steps):
        for step in steps:
            step()

    def mine(ref):
        return ref.at[pl.ds(start, images)]

    loads = [
        pltpu.make_async_copy(mine(z_all), zb, copy_sem.at[0]),
        pltpu.make_async_copy(mine(eps_all), eb, copy_sem.at[1]),
    ]
    for copy in loads:
        copy.start()
    masters = [
        pltpu.make_async_copy(src, dst, copy_sem.at[2 + k])
        for k, (src, dst) in enumerate(((gen_w, gshard), (fake_w, fshard), (teacher_w, stage.at[2])))
    ]
    for copy in masters:
        copy.start()
    smalls[...] = jnp.zeros(smalls.shape, F32)
    for n, ref in enumerate((gen_small, fake_small, teacher_small)):
        for r in range(13):
            smalls[me.sec, n, r : r + 1, :] = ref[r]
    gathers = [
        Gather(me, net, stage.at[n], local_sem.at[n], send_sem.at[n], recv_sem.at[n])
        for n, net in enumerate((w_gen, w_fake, w_teach))
    ]
    for copy in masters:
        copy.wait()
    stage[0] = gshard[...].astype(BF16)
    stage[1] = fshard[...].astype(BF16)
    me.meet()
    gathers[0].begin()
    swap = remote(
        smalls.at[me.sec], smalls.at[me.sec], small_sem.at[0], small_sem.at[1], me.sib
    )
    swap.start()

    clear_pads(bufs)
    sgrads[...] = jnp.zeros(sgrads.shape, F32)
    sigmas = []
    valid_sum = jnp.zeros((1, 4 * C), F32)
    for i in range(images):
        level = jnp.zeros((1, 4 * C), jnp.int32) + levels[start + i]
        sigma = SIGMA_TOP + level.astype(F32) / (LEVELS - 1) * (SIGMA_BOTTOM - SIGMA_TOP)
        square = sigma * sigma
        sigma = square * square * square * sigma
        sigmas.append(sigma)
        s_in, s_skip, s_out, s_lam = precondition(sigma)
        valid = jnp.where(jnp.zeros_like(level) + (start + i) < counts[0], 1.0, 0.0)
        valid_sum = valid_sum + valid
        rows = (s_in, s_skip, s_out, sigma, valid * s_lam * (1.0 / (POS * C)))
        for k, value in enumerate(rows):
            tab[i, k : k + 1, :] = value[:, :C]
    fill_embed(score_eo, sigmas)
    fill_embed(gen_eo, [jnp.full((1, 4 * C), SIGMA_INIT, F32)] * images)

    def forward(n, w, eo, sv, pump):
        def body(l, _):
            layer_forward(
                l, w, smalls.at[:, n], eo, *sv, bufs, nbuf, qkvw, tmp, True, pump
            )
            return 0

        lax.fori_loop(0, 2, body, 0)

    def backward(n, w, eo, sv, cot, grad, sgrad, pump):
        def body(k, _):
            layer_backward(
                1 - k, w, smalls.at[:, n], eo, *sv, cot, bufs, nbuf, qkvw, tmp, dn, dqkv,
                act_t, grad, sgrad, pump,
            )
            return 0

        lax.fori_loop(0, 2, body, 0)

    def each(f):
        def body(i, carry):
            return f(i, [tab[i, k : k + 1, :] for k in range(5)], carry)

        return lax.fori_loop(0, images, body, jnp.zeros((1, C), F32))

    last = gathers[0].phase3()
    run(gathers[0].phase1() + gathers[0].phase2() + last[:6] + [gathers[1].begin] + last[6:])
    for copy in loads:
        copy.wait()
    sv_one[0][0] = zb[...] * (GEN_IN * SIGMA_INIT)
    swap.wait()
    run(gathers[0].finish())
    later = gathers[1].phase1() + gathers[1].phase2()
    forward(0, w_gen, gen_eo, sv_one, Pump(later[:7], FORWARD_POINTS, (0, 1)))
    pairs = [(w_gen, gw_out)] + list(zip(sv_one, gen_out))
    stores = [
        pltpu.make_async_copy(src, dst, copy_sem.at[2 + k]) for k, (src, dst) in enumerate(pairs)
    ]
    for copy in stores:
        copy.start()

    def noisy(i, t, carry):
        zb[i] = zb[i] * (GEN_SKIP * SIGMA_INIT) + GEN_OUT * sv_one[0][2, i]
        eb[i] = zb[i] + t[T_SIGMA] * eb[i]
        sv_two[0][0, i] = t[T_IN] * eb[i]
        return carry

    each(noisy)
    z_next = gathers[2].phase1()
    run(later[7:] + [gathers[2].begin] + z_next[:1] + gathers[1].phase3() + gathers[1].finish())
    later = z_next[1:] + gathers[2].phase2()
    forward(1, w_fake, score_eo, sv_two, Pump(later[:5], FORWARD_POINTS, (0, 1)))
    later = later[5:] + gathers[2].phase3()

    def fake_loss(i, t, total):
        den = t[T_SKIP] * eb[i] + t[T_OUT] * sv_two[0][2, i]
        sv_two[0][2, i] = den
        miss = den - zb[i]
        g[i] = (2.0 * t[T_OUT] * t[T_FACTOR]) * miss
        return total + t[T_FACTOR] * colsum(miss * miss)

    loss_fake = each(fake_loss)
    for copy in stores:
        copy.wait()
    gathers[0].drain()
    backward(
        1, w_fake, score_eo, sv_two, g, w_gen, sgrads.at[:, 1],
        Pump(later, WEIGHT_POINTS, (1, 0), 0.0, 0.8),
    )
    fake_sum = Reduce(me, w_gen, fshard, sib, sib, *fake_refs)
    fake_sum.begin()
    run(gathers[2].finish())
    later = fake_sum.steps()
    sv_one[0][0] = sv_two[0][0]
    forward(2, w_teach, score_eo, sv_one, no_pump)

    def gen_loss(i, t, total):
        den = t[T_SKIP] * eb[i] + t[T_OUT] * sv_one[0][2, i]
        fake_den = sv_two[0][2, i]
        miss = fake_den - zb[i]
        gap = den - fake_den
        scale = t[T_OUT] * t[T_FACTOR]
        g[i] = scale * ((2.0 * (1.0 - ALPHA_MIX)) * gap + miss)
        g2[i] = scale * ((1.0 - 2.0 * (1.0 - ALPHA_MIX)) * gap - miss)
        zb[i] = (t[T_FACTOR] * (t[T_SKIP] - 1.0)) * gap
        return total + t[T_FACTOR] * colsum(gap * ((1.0 - ALPHA_MIX) * gap + miss))

    loss_gen = each(gen_loss)
    backward(
        2, w_teach, score_eo, sv_one, g, None, None, Pump(later[:4], BACKWARD_POINTS, (1, 0))
    )
    gathers[2].drain()
    fake_sum.drain(A_SLOT, B_SLOT)
    pl.semaphore_signal(free_sem, inc=1, device_id=me.sib, device_id_type=MESH)
    back = [
        pltpu.make_async_copy(src, dst, copy_sem.at[2 + k])
        for k, (dst, src) in enumerate([(w_teach, gw_out)] + list(zip(sv_one, gen_out)))
    ]
    for copy in back:
        copy.start()
    backward(
        1, w_fake, score_eo, sv_two, g2, None, None, Pump(later[4:8], BACKWARD_POINTS, (1, 0))
    )

    def gen_gradient(i, t, carry):
        g[i] = GEN_OUT * (zb[i] + t[T_IN] * (g[i] + g2[i]))
        return carry

    each(gen_gradient)
    gathers[1].drain()
    for copy in back:
        copy.wait()

    gen_sum = Reduce(me, w_fake, gshard, w_gen.at[1 - me.sec], w_gen.at[me.sec], *gen_refs)
    fake_steps, later = later, gen_sum.steps()

    def on_section(s, steps):
        pl.when(me.sec == s)(lambda: run(steps))

    def hand_over():
        pl.semaphore_wait(free_sem, 1)

    pump = Pump([], WEIGHT_POINTS, (1, 0))

    def at(layer, point, section, steps):
        pump.table[layer][point].append(lambda: on_section(section, steps))

    upper = [hand_over, lambda: gen_sum.begin_block(0), lambda: gen_sum.begin_block(1)]
    lower = [lambda: gen_sum.begin_block(2), lambda: gen_sum.begin_block(3)]
    for layer, giver in ((1, 0), (0, 1)):
        at(layer, HALF_WAY, giver, upper)
        at(layer, READY, giver, lower)
    for k, point in enumerate((2, 7, 12, 16)):
        pump.table[1][point].append(fake_steps[8 + k])
    for k, point in enumerate((1, 2, 5, 6, 7, 9, 10, 13, 16)):
        at(0, point, 1, later[k : k + 1])
    backward(0, w_teach, gen_eo, sv_one, g, w_fake, sgrads.at[:, 0], pump)

    def spread_sum(total):
        return jnp.broadcast_to(jnp.sum(total, axis=1, keepdims=True), (1, C))

    sums = jnp.concatenate([spread_sum(loss_gen), spread_sum(loss_fake), valid_sum[:, :C]], axis=0)
    for s in range(2):
        part_sums[s, 0:16, :] = sgrads[s, 0]
        part_sums[s, 13:16, :] = sums
        part_sums[s, 16:32, :] = sgrads[s, 1]
    small = Totals(me, *small_refs)
    small_refs[0][0] = part_sums[me.sec]
    small.begin(part_sums.at[1 - me.sec])
    fake_sum.stage_e()
    small_steps = small.steps()
    on_section(0, later[:3])
    on_section(1, later[9:])
    run(small_steps[:1])
    on_section(0, later[3:6])
    run(small_steps[1:2])
    on_section(0, later[6:9])
    run(small_steps[2:])
    on_section(0, later[9:])
    stot[...] = small.result()
    own = square_refs[0]
    keep = lax.broadcasted_iota(jnp.int32, (16, C), 0) < 13
    for n, rows in ((1, fshard), (0, gshard)):
        if n == 0:
            gen_sum.stage_e()
        low = jnp.square(jnp.where(keep, stot[16 * n : 16 * n + 16, :], 0.0))
        low = jnp.where(me.d == 0, low[0:8] + low[8:16], 0.0)
        big = jnp.sum(jnp.square(rows[...]).reshape(rows.shape[0] // 8, 8, C), axis=0)
        own[0, 8 * n : 8 * n + 8, :] = big + low
    square = Squares(me, *square_refs)
    sqtot[...] = square.run()
    fake_sum.drain(B_SLOT)
    for done in (gen_sum, small, square):
        done.drain()


SIGMA_TOP = SIGMA_HIGH ** (1.0 / RHO_POWER)
SIGMA_BOTTOM = SIGMA_LOW ** (1.0 / RHO_POWER)


def run_step(z, eps, levels, counts, gen_w, fake_w, teacher_w, smalls):
    part = gen_w.shape[0]
    images = z.shape[0] // 2
    any_ = pl.BlockSpec(memory_space=pl.ANY)
    smem = pl.BlockSpec(memory_space=pltpu.SMEM)
    saved = saved_shapes(images)
    return pl.pallas_call(
        step_kernel,
        out_shape=[jax.ShapeDtypeStruct((2, ROWS, C), BF16)]
        + saved
        + [
            jax.ShapeDtypeStruct((part, C), F32),
            jax.ShapeDtypeStruct((part, C), F32),
            jax.ShapeDtypeStruct((32, C), F32),
            jax.ShapeDtypeStruct((16, C), F32),
        ],
        in_specs=[any_] * 2 + [smem] * 2 + [any_] * 3 + vm(3),
        out_specs=[any_] * 8 + vm(4),
        scratch_shapes=[pltpu.VMEM((2, ROWS, C), BF16)] * 3
        + saved_scratch(images) * 2
        + backward_scratch(images)
        + [pltpu.VMEM((images, POS, C), F32)] * 3
        + [
            pltpu.VMEM((3, part, C), BF16),
            pltpu.SemaphoreType.DMA((3,)),
            pltpu.SemaphoreType.DMA((3, SLOTS)),
            pltpu.SemaphoreType.DMA((3, SLOTS)),
            pltpu.SemaphoreType.DMA((10,)),
            pltpu.VMEM((2, 3, 16, C), F32),
            pltpu.SemaphoreType.DMA((2,)),
            pltpu.VMEM((8, 4 * C), BF16),
            pltpu.VMEM((8, 4 * C), BF16),
            pltpu.VMEM((images, 8, C), F32),
            pltpu.VMEM((2, 2, 16, C), F32),
            pltpu.VMEM((2, 32, C), F32),
        ]
        + reduce_scratch(part) * 2
        + totals_scratch((32, C))
        + squares_scratch((16, C))
        + [pltpu.VMEM((ROWS, C), BF16), pltpu.SemaphoreType.REGULAR],
        compiler_params=pltpu.CompilerParams(
            collective_id=0, has_side_effects=True, vmem_limit_bytes=STEP_LIMIT
        ),
    )(z, eps, levels, counts, gen_w, fake_w, teacher_w, *smalls)[8:]


def adam_step(master, first_mom, second_mom, grad):
    first_new = BETA_ONE * first_mom + (1.0 - BETA_ONE) * grad
    second_new = BETA_TWO * second_mom + (1.0 - BETA_TWO) * grad * grad
    direction = (
        first_new
        / (1.0 - BETA_ONE**STEP)
        / (jnp.sqrt(second_new / (1.0 - BETA_TWO**STEP)) + ADAM_EPS)
    )
    return (master - LEARN_RATE * (direction + WEIGHT_DECAY * master), first_new, second_new)


EMA_RATE = 0.5 ** (20.0 / STEP)
SMALL_STATES = (4, 5, 6, 7, 11, 12, 13)


def update_kernel(gshard, fshard, stot, sqtot, *refs):
    ins, outs = refs[:14], refs[14:]
    norms, losses = outs[14:]
    count = stot[15:16, 0:1]
    norm_of, scales = [], []
    for n in range(2):
        rows = jnp.sum(sqtot[8 * n : 8 * n + 8, :], axis=0, keepdims=True)
        norm = jnp.sqrt(jnp.sum(rows, axis=1, keepdims=True)) / count
        scales.append(jnp.minimum(1.0, CLIP_NORM / norm) / count)
        norm_of.append(norm)

    def one(at, grad, w, m, v, ema, ow, om, ov, oe):
        new, first, second = adam_step(w[at], m[at], v[at], grad)
        ow[at] = new
        om[at] = first
        ov[at] = second
        if ema is not None:
            oe[at] = EMA_RATE * ema[at] + (1.0 - EMA_RATE) * new

    one(0, gshard[...] * scales[0], *ins[0:4], *outs[0:4])
    one(0, fshard[...] * scales[1], *ins[8:11], None, *outs[8:11], None)

    first = lax.broadcasted_iota(jnp.int32, (1, 2), 1) == 0
    norms[...] = jnp.where(first, norm_of[0], norm_of[1])
    losses[...] = jnp.where(first, stot[13:14, 0:1], stot[14:15, 0:1]) / count
    for k in range(13):
        one(k, stot[k : k + 1, :] * scales[0], *ins[4:8], *outs[4:8])
        one(k, stot[16 + k : 17 + k, :] * scales[1], *ins[11:14], None, *outs[11:14], None)


def update_nets(gshard, fshard, stot, sqtot, states):
    def turned(arrays):
        return [a.swapaxes(0, 1) if k in SMALL_STATES else a for k, a in enumerate(arrays)]

    states = turned(states)
    res = pl.pallas_call(
        update_kernel,
        out_shape=[jax.ShapeDtypeStruct(a.shape, F32) for a in states]
        + [jax.ShapeDtypeStruct((1, 2), F32)] * 2,
        in_specs=vm(4 + len(states)),
        out_specs=vm(2 + len(states)),
        compiler_params=pltpu.CompilerParams(vmem_limit_bytes=VMEM_LIMIT),
    )(gshard, fshard, stot, sqtot, *states)
    return tuple(turned(res[:-2])) + (res[-2][0], res[-1][0])


def gather_plain(shard):
    rows = lax.all_gather(shard.astype(BF16), "dp", axis=1, tiled=True)
    return lax.all_gather(rows, "section", axis=0, tiled=True)


def reduce_plain(bigs, small):
    shards_, squares = [], []
    own = lax.psum_scatter(small, "section", scatter_dimension=0, tiled=True)
    stot = lax.psum(own, "dp")[0]
    first = lax.axis_index("dp") == 0
    for n, big in enumerate(bigs):
        own = lax.psum_scatter(big, "section", scatter_dimension=0, tiled=True)
        own = lax.psum_scatter(own, "dp", scatter_dimension=1, tiled=True)[0].astype(F32)
        shards_.append(own)
        low = jnp.sum(jnp.square(stot[16 * n : 16 * n + 13]))
        squares.append(jnp.sum(own * own) + jnp.where(first, low, 0.0))
    sq = lax.psum(jnp.stack(squares), ("section", "dp"))
    return *shards_, stot, jnp.zeros((16, C), F32).at[jnp.array([0, 8]), 0].set(sq)


def shards(
    z_noise, eps_noise, levels, counts,
    gen_w, gen_m, gen_v, gen_ema, gen_small, gen_small_m, gen_small_v, gen_small_ema,
    fake_w, fake_m, fake_v, fake_small, fake_small_m, fake_small_v,
    teacher_w, teacher_small,
):
    if lax.axis_size("dp") == PLANES * PLANE:
        smalls = [a.swapaxes(0, 1) for a in (gen_small, fake_small, teacher_small)]
        reduced = run_step(
            z_noise, eps_noise, levels, counts, gen_w[0], fake_w[0], teacher_w[0], smalls
        )
    else:
        reduced = plain_step(
            z_noise, eps_noise, levels, counts, gen_w, fake_w, teacher_w,
            gen_small, fake_small, teacher_small,
        )
    return update_nets(
        *reduced,
        (
            gen_w, gen_m, gen_v, gen_ema, gen_small, gen_small_m, gen_small_v, gen_small_ema,
            fake_w, fake_m, fake_v, fake_small, fake_small_m, fake_small_v,
        ),
    )


def plain_step(
    z_noise, eps_noise, levels, counts, gen_w, fake_w, teacher_w,
    gen_small, fake_small, teacher_small,
):
    images = z_noise.shape[0] // lax.axis_size("section")
    start = lax.axis_index("section") * images

    def mine(a):
        return lax.dynamic_slice_in_dim(a, start, images, 0)

    z, eps = mine(z_noise), mine(eps_noise)
    sigma = sigma_levels(mine(levels))
    valid = (start + jnp.arange(images) < counts[0]).astype(F32)
    valid_sum = jnp.sum(valid)
    gen_eo = spread_embed(jnp.full((images,), SIGMA_INIT, F32))
    score_eo = spread_embed(sigma)
    gs, fs, ts = [
        lax.all_gather(a, "section", axis=0, tiled=True)
        for a in (gen_small, fake_small, teacher_small)
    ]
    gw, fw, tw = gather_plain(gen_w), gather_plain(fake_w), gather_plain(teacher_w)
    s_in, s_skip, s_out, s_lam = precondition(sigma)
    factor = valid * s_lam / (POS * C)
    s_in, s_skip, s_out, sigma, factor = [
        t[:, None, None] for t in (s_in, s_skip, s_out, sigma, factor)
    ]
    raw = SIGMA_INIT * z
    gen_saved = run_forward(GEN_IN * raw, gw, gs, gen_eo)
    samples = GEN_SKIP * raw + GEN_OUT * gen_saved[0][2]
    noisy = samples + sigma * eps
    x0 = s_in * noisy
    fake_saved = run_forward(x0, fw, fs, score_eo)
    fake_den = s_skip * noisy + s_out * fake_saved[0][2]
    miss = fake_den - samples
    _, fake_g, fake_sg = run_backward(
        s_out * 2.0 * factor * miss, fw, fs, score_eo, fake_saved, True
    )
    teacher_saved = run_forward(x0, tw, ts, score_eo)
    teacher_den = s_skip * noisy + s_out * teacher_saved[0][2]
    gap = teacher_den - fake_den
    loss_gen = jnp.sum(factor * ((1.0 - ALPHA_MIX) * gap * gap + gap * miss))
    loss_fake = jnp.sum(factor * miss * miss)
    grad_teacher = factor * (2.0 * (1.0 - ALPHA_MIX) * gap + miss)
    grad_fake = factor * gap - grad_teacher
    direct = factor * gap * (s_skip - 1.0)
    (back_t,) = run_backward(s_out * grad_teacher, tw, ts, score_eo, teacher_saved, False)
    (back_f,) = run_backward(s_out * grad_fake, fw, fs, score_eo, fake_saved, False)
    gen_cot = GEN_OUT * (direct + s_in * (back_t + back_f))
    _, gen_g, gen_sg = run_backward(gen_cot, gw, gs, gen_eo, gen_saved, True)
    scalars = jnp.broadcast_to(jnp.stack([loss_gen, loss_fake, valid_sum])[:, None], (3, C))
    small_sums = jnp.concatenate(
        [gen_sg[:, :13], jnp.broadcast_to(scalars, (2, 3, C)), fake_sg], axis=1
    )
    return reduce_plain((gen_g, fake_g), small_sums)


def solution(mesh):
    images = P("dp", None, None)
    big = P("section", "dp", None)
    small = P("section", None, None)
    return jax.shard_map(
        shards,
        mesh=mesh,
        in_specs=(images, images, P("dp"), P("dp"))
        + (big,) * 4 + (small,) * 4 + (big,) * 3 + (small,) * 3 + (big, small),
        out_specs=(big,) * 4 + (small,) * 4 + (big,) * 3 + (small,) * 3 + (P(), P()),
        check_vma=False,
    )
```

```python
import functools

import jax
import jax.numpy as jnp
from jax import lax
from jax.experimental import pallas as pl
from jax.experimental.pallas import tpu as pltpu
from jax.sharding import PartitionSpec as P

GROUPS = 32
SIDE = 16
LEVELS = 1000
STEP = 10

SIGMA_DATA = 0.5
SIGMA_INIT = 2.5
SIGMA_LOW = 0.05
SIGMA_HIGH = 20.0
RHO_POWER = 7.0
ALPHA_MIX = 1.2
RS = 0.7071067811865476
NORM_EPS = 1e-05
CLIP_NORM = 0.001
LEARN_RATE = 0.15
BETA_ONE = 0.9
BETA_TWO = 0.999
ADAM_EPS = 1e-08
WEIGHT_DECAY = 0.01

C = 256
HALF = 128
POS = 256
ROWS = 26 * C
CHUNK = 64
PAD = SIDE
F32 = jnp.float32
BF16 = jnp.bfloat16
VMEM_LIMIT = 58 * 2**20
STEP_LIMIT = 63 * 2**20

R_CONV1, R_CONV2, R_EMB, R_QKV, R_PROJ = 0, 9 * C, 18 * C, 22 * C, 25 * C
S_M1, S_I1, S_M2, S_I2, S_M3, S_I3, S_MA, S_MB = range(8)


def sigma_levels(level_ids):
    fraction = level_ids.astype(F32) / (LEVELS - 1)
    top_root = SIGMA_HIGH ** (1.0 / RHO_POWER)
    bottom_root = SIGMA_LOW ** (1.0 / RHO_POWER)
    return (top_root + fraction * (bottom_root - top_root)) ** RHO_POWER


def precondition(sigma_vals):
    total = sigma_vals * sigma_vals + SIGMA_DATA**2
    return (
        lax.rsqrt(total),
        SIGMA_DATA**2 / total,
        sigma_vals * SIGMA_DATA * lax.rsqrt(total),
        total / (sigma_vals * sigma_vals * SIGMA_DATA**2),
    )


def noise_embed(sigma_vals, channel_count):
    frequency = (1.0 / 10000.0) ** (jnp.arange(channel_count, dtype=F32) / channel_count)
    angles = (jnp.log(sigma_vals) / 4.0)[..., None] * frequency
    return jnp.concatenate([jnp.cos(angles), jnp.sin(angles)], axis=-1)


def spread_embed(sigma_vals):
    emb = noise_embed(sigma_vals, C).astype(BF16)
    images = emb.shape[0]
    zero = jnp.zeros_like(emb)
    low = jnp.stack([emb, zero], axis=-1).reshape(images, 4 * C)
    high = jnp.stack([zero, emb], axis=-1).reshape(images, 4 * C)
    fill = jnp.zeros((4 - images, 4 * C), BF16)
    return jnp.concatenate([low, fill, high, fill], axis=0)


def dot_nn(a, b):
    return lax.dot_general(a, b, (((1,), (0,)), ((), ())), preferred_element_type=F32)


def dot_nt(a, b):
    return lax.dot_general(a, b, (((1,), (1,)), ((), ())), preferred_element_type=F32)


def dot_tn(a, b):
    return lax.dot_general(a, b, (((0,), (0,)), ((), ())), preferred_element_type=F32)


def group_mean(v):
    lane = lax.broadcasted_iota(jnp.int32, (8, C), 1)
    for sh in (1, 2, 4):
        v = v + jnp.where((lane & sh) != 0, pltpu.roll(v, sh, 1), pltpu.roll(v, C - sh, 1))
    return v * (1.0 / (POS * 8))


def colsum(v):
    return jnp.sum(v, axis=0, keepdims=True)


def no_pump(l):
    pass


FORWARD_POINTS, BACKWARD_POINTS, WEIGHT_POINTS = 10, 12, 18
HALF_WAY, READY = 8, 13


def stagger(steps, images, between):
    for t in range(len(steps) + images - 1):
        for i in range(images):
            if 0 <= t - i < len(steps):
                steps[t - i](i)
        between()


class Pump:
    def __init__(self, steps, points, layers, lo=0.0, hi=1.0):
        self.table = {l: [[] for _ in range(points)] for l in layers}
        self.at = 0
        for k, step in enumerate(steps):
            place = int((lo + (hi - lo) * (k + 0.5) / len(steps)) * points * len(layers))
            self.table[layers[place // points]][place % points].append(step)

    def __call__(self, l):
        for layer, points in self.table.items():
            if points[self.at]:

                @pl.when(l == layer)
                def _(todo=points[self.at]):
                    for step in todo:
                        step()

        self.at += 1


def put_shifted(bufs, i, r, v):
    rows = v.shape[0]
    at = pl.ds(PAD + r, rows)
    sub = lax.broadcasted_iota(jnp.int32, (rows // SIDE, 8, C), 1)
    x = v.reshape(rows // SIDE, 2, 8, C)
    low, high = x[:, 0], x[:, 1]
    low_up, high_up = pltpu.roll(low, 1, 1), pltpu.roll(high, 1, 1)
    low_down, high_down = pltpu.roll(low, 7, 1), pltpu.roll(high, 7, 1)
    left = (jnp.where(sub == 0, 0.0, low_up), jnp.where(sub == 0, low_up, high_up))
    right = (jnp.where(sub == 7, high_down, low_down), jnp.where(sub == 7, 0.0, high_down))
    bufs[0, i, at, :] = jnp.stack(left, axis=1).reshape(rows, C).astype(BF16)
    bufs[1, i, at, :] = v.astype(BF16)
    bufs[2, i, at, :] = jnp.stack(right, axis=1).reshape(rows, C).astype(BF16)


def taps(bufs, flip):
    images = bufs.shape[1]
    out = []
    for dr in (-1, 0, 1):
        for dc in (-1, 0, 1):
            sr, sc = (-dr, -dc) if flip else (dr, dc)
            piece = bufs[sc + 1, :, PAD + SIDE * sr : PAD + SIDE * sr + POS, :]
            out.append(piece.reshape(images * POS, C))
    return out


def conv_forward(bufs, w, l, row):
    return dot_nn(jnp.concatenate(taps(bufs, False), axis=1), w[l, row : row + 9 * C, :])


def conv_input_grad(bufs, w, l, row):
    parts = [w[l, row + t * C : row + (t + 1) * C, :] for t in range(9)]
    return dot_nt(jnp.concatenate(taps(bufs, True), axis=1), jnp.concatenate(parts, axis=1))


def conv_weight_grad(act_t, bufs, grad, l, row):
    left = act_t[...]
    for t, piece in enumerate(taps(bufs, True)):
        grad[l, row + t * C : row + (t + 1) * C, :] = dot_nn(left, piece).astype(BF16)


def silu(v):
    h = 0.5 * v
    return h + h * jnp.tanh(h)


def silu_parts(v):
    h = 0.5 * v
    t = jnp.tanh(h)
    return h + h * t, (1.0 + t) + h * (1.0 - t * t)


def clear_pads(bufs):
    zero = jnp.zeros(bufs.shape[:2] + (PAD, C), BF16)
    bufs[:, :, 0:PAD, :] = zero
    bufs[:, :, PAD + POS :, :] = zero


def split_qkv(w, l, qkvw, tmp):
    for h in range(2):
        tmp[h] = w[l, R_QKV : R_QKV + 3 * C, h * HALF : (h + 1) * HALF].astype(F32)
    for j in range(3):
        for h in range(2):
            at = j * C + h * HALF
            qkvw[:, at : at + HALF] = tmp[h, pl.ds(j, C, stride=3), :].astype(BF16)


def norm_sums(x):
    pivot = x[0:1]
    d = x - pivot
    return colsum(d), colsum(d * d), pivot


def norm_stats(sums):
    fill = [jnp.zeros((4 - len(sums), C), F32)]
    s1, s2, pivot = [jnp.concatenate([a[k] for a in sums] + fill, axis=0) for k in range(3)]
    centre = group_mean(jnp.concatenate([pivot, pivot], axis=0) * POS)[0:4]
    off = pivot - centre
    first = s1 + POS * off
    second = s2 + off * (2.0 * s1 + POS * off)
    means = group_mean(jnp.concatenate([first, second], axis=0))
    spread = jnp.maximum(means[4:8] - jnp.square(means[0:4]), 0.0)
    return centre + means[0:4], lax.rsqrt(spread + NORM_EPS)


def norm_map(gain, mg, mc, mean, inv):
    on_value = inv * inv * mc
    return inv * gain, on_value, inv * mg - mean * on_value


def two_means(a, b):
    rows = jnp.concatenate([a, b] * 4, axis=0)
    means = group_mean(rows)
    return means[0:1], means[1:2]


def tap_rows(bufs, flip, which):
    out = []
    for dr in (-1, 0, 1):
        for dc in (-1, 0, 1):
            sr, sc = (-dr, -dc) if flip else (dr, dc)
            at = slice(PAD + SIDE * sr, PAD + SIDE * sr + POS)
            piece = jnp.concatenate([bufs[sc + 1, i, at, :] for i in which], axis=0)
            out.append(piece)
    return out


def layer_forward(l, w, small, eo, xs, h1, y, qkv, att, o, st, bufs, nbuf, qkvw, tmp, staged, pump):
    images = h1.shape[1]
    split_qkv(w, l, qkvw, tmp)
    mod = dot_nn(eo[...], w[l, R_EMB : R_EMB + 4 * C, :])
    ma = mod[0:4] + small[l, 5:6, :]
    mb = mod[4:8] + small[l, 6:7, :]
    for i in range(images):
        st[l, i, S_MA : S_MA + 1, :] = ma[i : i + 1]
        st[l, i, S_MB : S_MB + 1, :] = mb[i : i + 1]

    sums = {}

    def row(k):
        return small[l, k : k + 1, :]

    def keep(which, mean, inv, at):
        for k, i in enumerate(which):
            st[l, i, at : at + 1, :] = mean[k : k + 1]
            st[l, i, at + 1 : at + 2, :] = inv[k : k + 1]

    def first(which):
        mean, inv = norm_stats([norm_sums(xs[l, i]) for i in which])
        keep(which, mean, inv, S_M1)
        for k, i in enumerate(which):
            a = inv[k : k + 1] * row(0)
            b = row(1) - mean[k : k + 1] * a
            for r in range(0, POS, CHUNK):
                v = xs[l, i, r : r + CHUNK, :] * a + b
                put_shifted(bufs, i, r, silu(v))

    def conv(which, at):
        left = jnp.concatenate(tap_rows(bufs, False, which), axis=1)
        return dot_nn(left, w[l, at : at + 9 * C, :])

    def conv_one(which):
        out = conv(which, R_CONV1)
        for k, i in enumerate(which):
            own = out[k * POS : (k + 1) * POS]
            own = own + row(2)
            sums[i] = norm_sums(own)
            h1[l, i] = own

    def second(which):
        mean, inv = norm_stats([sums[i] for i in which])
        keep(which, mean, inv, S_M2)
        for k, i in enumerate(which):
            gain = 1.0 + ma[i : i + 1]
            a = inv[k : k + 1] * row(3) * gain
            b = row(4) * gain + mb[i : i + 1] - mean[k : k + 1] * a
            for r in range(0, POS, CHUNK):
                v = h1[l, i, r : r + CHUNK, :] * a + b
                put_shifted(bufs, i, r, silu(v))

    def conv_two(which):
        out = conv(which, R_CONV2) + row(7)
        for k, i in enumerate(which):
            own = (xs[l, i] + out[k * POS : (k + 1) * POS]) * RS
            sums[i] = norm_sums(own)
            y[l, i] = own

    def third(which):
        mean, inv = norm_stats([sums[i] for i in which])
        keep(which, mean, inv, S_M3)
        for k, i in enumerate(which):
            a = inv[k : k + 1] * row(8)
            b = row(9) - mean[k : k + 1] * a
            for r in range(0, POS, CHUNK):
                v = y[l, i, r : r + CHUNK, :] * a + b
                nbuf[i, r : r + CHUNK, :] = v.astype(BF16)

    def project_in(which):
        n = jnp.concatenate([nbuf[i] for i in which], axis=0)
        for j, at in ((0, 10), (1, None), (2, 11)):
            part = dot_nn(n, qkvw[:, j * C : (j + 1) * C])
            if at is not None:
                part = part + row(at)
            part = part.astype(BF16)
            for k, i in enumerate(which):
                qkv[l, i, :, j * C : (j + 1) * C] = part[k * POS : (k + 1) * POS]

    def attend(which):
        scores = [dot_nt(qkv[l, i, :, 0:C], qkv[l, i, :, C : 2 * C]) for i in which]
        for s, i in zip(scores, which):
            e = jnp.exp((s - jnp.max(s, axis=1, keepdims=True)) * (C**-0.5))
            p = (e * (1.0 / jnp.sum(e, axis=1, keepdims=True))).astype(BF16)
            att[l, i] = p
            o[l, i] = dot_nn(p, qkv[l, i, :, 2 * C :]).astype(BF16)

    def project_out(which):
        left = jnp.concatenate([o[l, i] for i in which], axis=0)
        out = dot_nn(left, w[l, R_PROJ:, :]) + row(12)
        for k, i in enumerate(which):
            xs[l + 1, i] = (y[l, i] + out[k * POS : (k + 1) * POS]) * RS

    steps = (first, conv_one, second, conv_two, third, project_in, attend, project_out)
    if not staged:
        for step in steps:
            step(range(images))
            pump(l)
    else:
        stagger([lambda i, step=step: step([i]) for step in steps], images, lambda: pump(l))


def layer_backward(
    l, w, small, eo, xs, h1, y, qkv, att, o, st, g, bufs, nbuf, qkvw, tmp, dn, dqkv, act_t,
    grad, sgrad, pump, need_dx=None,
):
    want = grad is not None
    images = h1.shape[1]
    which = range(images)
    flat = images * POS
    scale = C**-0.5
    split_qkv(w, l, qkvw, tmp)

    def row(k):
        return small[l, k : k + 1, :]

    def rows8(rows):
        return jnp.concatenate(list(rows) + [jnp.zeros((8 - len(rows), C), F32)], axis=0)

    zero = jnp.zeros((1, C), F32)
    gps, c1, c2, p1, p2 = {}, {}, {}, {}, {}
    total = {7: zero, 2: zero}
    gains = [1.0 + st[l, i, S_MA : S_MA + 1, :] for i in which]

    def project_out(i):
        gps[i] = (g[i] * RS).astype(BF16)
        nbuf[i] = dot_nt(gps[i], w[l, R_PROJ:, :]).astype(BF16)

    def attend(i):
        p = att[l, i]
        pf = p.astype(F32)
        dp = dot_nt(nbuf[i], qkv[l, i, :, 2 * C :])
        ds = (pf * (dp - jnp.sum(dp * pf, axis=1, keepdims=True))).astype(BF16)
        dqkv[i, :, 0:C] = (dot_nn(ds, qkv[l, i, :, C : 2 * C]) * scale).astype(BF16)
        dqkv[i, :, C : 2 * C] = (dot_tn(ds, qkv[l, i, :, 0:C]) * scale).astype(BF16)
        dqkv[i, :, 2 * C :] = dot_tn(p, nbuf[i]).astype(BF16)

    def project_in(i):
        mean, inv = st[l, i, S_M3 : S_M3 + 1, :], st[l, i, S_I3 : S_I3 + 1, :]
        d = dot_nt(dqkv[i], qkvw[...])
        dn[i] = d
        c1[i] = colsum(d)
        c2[i] = colsum(d * (y[l, i] - mean)) * inv

    def third(i):
        mean, inv = st[l, i, S_M3 : S_M3 + 1, :], st[l, i, S_I3 : S_I3 + 1, :]
        mg, mc = two_means(row(8) * c1[i], row(8) * c2[i])
        on_grad, on_value, offset = norm_map(row(8) * RS, mg * RS, mc * RS, mean, inv)
        act_a = inv * row(8)
        act_b = row(9) - mean * act_a
        for r in range(0, POS, CHUNK):
            value = y[l, i, r : r + CHUNK, :]
            gm = g[i, r : r + CHUNK, :] * (RS * RS) + dn[i, r : r + CHUNK, :] * on_grad
            gm = gm - (value * on_value + offset)
            g[i, r : r + CHUNK, :] = gm
            put_shifted(bufs, i, r, gm)
            if want:
                nbuf[i, r : r + CHUNK, :] = (value * act_a + act_b).astype(BF16)
                total[7] = total[7] + colsum(gm)

    def conv_grad(i, at):
        left = jnp.concatenate(tap_rows(bufs, True, [i]), axis=1)
        parts = [w[l, at + t * C : at + (t + 1) * C, :] for t in range(9)]
        dn[i] = dot_nt(left, jnp.concatenate(parts, axis=1))

    def activation(i, src, mean, inv, a, b, act=None):
        s1, s2 = zero, zero
        for r in range(0, POS, CHUNK):
            u = src[l, i, r : r + CHUNK, :] - mean
            act_value, slope = silu_parts(u * (inv * a) + b)
            d = dn[i, r : r + CHUNK, :] * slope
            dn[i, r : r + CHUNK, :] = d
            s1 = s1 + colsum(d)
            s2 = s2 + colsum(d * u)
            if act is not None:
                act[i, r : r + CHUNK, :] = act_value.astype(BF16)
        p1[i], p2[i] = s1 * 0.5, s2 * (0.5 * inv)

    def second_a(i):
        mean, inv = st[l, i, S_M2 : S_M2 + 1, :], st[l, i, S_I2 : S_I2 + 1, :]
        b = row(4) * gains[i] + st[l, i, S_MB : S_MB + 1, :]
        activation(i, h1, mean, inv, row(3) * gains[i], b, nbuf if want else None)

    def second_b(i):
        mean, inv = st[l, i, S_M2 : S_M2 + 1, :], st[l, i, S_I2 : S_I2 + 1, :]
        full = row(3) * gains[i]
        mg, mc = two_means(full * p1[i], full * p2[i])
        on_grad, on_value, offset = norm_map(full, mg, mc, mean, inv)
        for r in range(0, POS, CHUNK):
            dh = dn[i, r : r + CHUNK, :] * (0.5 * on_grad) - (
                h1[l, i, r : r + CHUNK, :] * on_value + offset
            )
            put_shifted(bufs, i, r, dh)
            if want:
                total[2] = total[2] + colsum(dh)

    def first_a(i):
        mean, inv = st[l, i, S_M1 : S_M1 + 1, :], st[l, i, S_I1 : S_I1 + 1, :]
        activation(i, xs, mean, inv, row(0), row(1))

    def first_act(i):
        mean, inv = st[l, i, S_M1 : S_M1 + 1, :], st[l, i, S_I1 : S_I1 + 1, :]
        a = inv * row(0)
        b = row(1) - mean * a
        for r in range(0, POS, CHUNK):
            v = xs[l, i, r : r + CHUNK, :] * a + b
            nbuf[i, r : r + CHUNK, :] = silu(v).astype(BF16)

    def first_b(i):
        mean, inv = st[l, i, S_M1 : S_M1 + 1, :], st[l, i, S_I1 : S_I1 + 1, :]
        mg, mc = two_means(row(0) * p1[i], row(0) * p2[i])
        on_grad, on_value, offset = norm_map(row(0), mg, mc, mean, inv)
        for r in range(0, POS, CHUNK):
            dx = dn[i, r : r + CHUNK, :] * (0.5 * on_grad) - (
                xs[l, i, r : r + CHUNK, :] * on_value + offset
            )
            g[i, r : r + CHUNK, :] = g[i, r : r + CHUNK, :] + dx

    upper = [project_out, attend, project_in, third, lambda i: conv_grad(i, R_CONV2)]
    lower = [lambda i: conv_grad(i, R_CONV1), first_a]
    if not want:
        stagger(upper + [second_a, second_b] + lower + [first_b], images, lambda: pump(l))
        return
    stagger(upper, images, lambda: pump(l))
    gp = jnp.concatenate([gps[i] for i in which], axis=0)
    grad[l, R_PROJ:, :] = dot_tn(o[l].reshape(flat, C), gp).astype(BF16)
    sgrad[l, 12:13, :] = colsum(gp.astype(F32))
    sgrad[l, 7:8, :] = total[7]
    sgrad[l, 8:9, :] = colsum(rows8([c2[i] for i in which]))
    sgrad[l, 9:10, :] = colsum(rows8([c1[i] for i in which]))
    act_t[...] = nbuf[...].reshape(flat, C).T
    for j in range(3):
        dj = dqkv[:, :, j * C : (j + 1) * C].reshape(flat, C)
        part = dot_nn(act_t[...], dj)
        for h in range(2):
            tmp[h, pl.ds(j, C, stride=3), :] = part[:, h * HALF : (h + 1) * HALF]
        if j != 1:
            sgrad[l, 10 + j // 2 : 11 + j // 2, :] = colsum(dj.astype(F32))
    for h in range(2):
        grad[l, R_QKV : R_QKV + 3 * C, h * HALF : (h + 1) * HALF] = tmp[h].astype(BF16)
    for i in which:
        second_a(i)
    pump(l)
    act_t[...] = nbuf[...].reshape(flat, C).T
    conv_weight_grad(act_t, bufs, grad, l, R_CONV2)
    p18, p28, modgain = [rows8([a[i] for i in which]) for a in (p1, p2, gains)]
    dma = row(3) * p28 + row(4) * p18
    sgrad[l, 3:4, :] = colsum(modgain * p28)
    sgrad[l, 4:5, :] = colsum(modgain * p18)
    sgrad[l, 5:6, :] = colsum(dma)
    sgrad[l, 6:7, :] = colsum(p18)
    grad[l, R_EMB : R_EMB + 4 * C, :] = embed_grad(
        eo, jnp.concatenate([dma[0:4], p18[0:4]], axis=0)
    ).astype(BF16)
    pump(l)
    stagger([second_b, first_act], images, lambda: pump(l))
    act_t[...] = nbuf[...].reshape(flat, C).T
    conv_weight_grad(act_t, bufs, grad, l, R_CONV1)
    pump(l)
    stagger(lower, images, lambda: pump(l))
    sgrad[l, 2:3, :] = total[2]
    sgrad[l, 0:1, :] = colsum(rows8([p2[i] for i in which]))
    sgrad[l, 1:2, :] = colsum(rows8([p1[i] for i in which]))

    @pl.when(l == 1)
    def _():
        for i in which:
            first_b(i)


def embed_grad(eo, dm):
    parts, rest = [], dm
    for _ in range(3):
        parts.append(rest.astype(BF16))
        rest = rest - parts[-1].astype(F32)
    left = eo[...]
    return dot_tn(jnp.concatenate([left, left], axis=0), jnp.concatenate(parts[:2], axis=0)) + dot_tn(
        left, parts[2]
    )


def saved_shapes(images):
    return [
        jax.ShapeDtypeStruct((3, images, POS, C), F32),
        jax.ShapeDtypeStruct((2, images, POS, C), F32),
        jax.ShapeDtypeStruct((2, images, POS, C), F32),
        jax.ShapeDtypeStruct((2, images, POS, 3 * C), BF16),
        jax.ShapeDtypeStruct((2, images, POS, POS), BF16),
        jax.ShapeDtypeStruct((2, images, POS, C), BF16),
        jax.ShapeDtypeStruct((2, images, 8, C), F32),
    ]


def forward_kernel(staged, x0, w, small, eo, xs, h1, y, qkv, att, o, st, bufs, nbuf, qkvw, tmp):
    clear_pads(bufs)
    xs[0] = x0[...]

    def body(l, _):
        layer_forward(
            l, w, small, eo, xs, h1, y, qkv, att, o, st, bufs, nbuf, qkvw, tmp, staged, no_pump
        )
        return 0

    lax.fori_loop(0, 2, body, 0)


def backward_kernel(want, *refs):
    cot, w, small, eo, xs, h1, y, qkv, att, o, st, g = refs[:12]
    refs = refs[12:]
    if want:
        grad, sgrad = refs[:2]
        refs = refs[2:]
    else:
        grad, sgrad = None, None
    bufs, nbuf, qkvw, tmp, dn, dqkv, act_t = refs
    clear_pads(bufs)
    g[...] = cot[...]
    if want:
        sgrad[...] = jnp.zeros(sgrad.shape, F32)

    def body(k, _):
        layer_backward(
            1 - k, w, small, eo, xs, h1, y, qkv, att, o, st, g, bufs, nbuf, qkvw, tmp, dn,
            dqkv, act_t, grad, sgrad, no_pump,
        )
        return 0

    lax.fori_loop(0, 2, body, 0)


def vm(n):
    return [pl.BlockSpec(memory_space=pltpu.VMEM)] * n


def scratch_forward(images):
    return [
        pltpu.VMEM((3, images, POS + 2 * PAD, C), BF16),
        pltpu.VMEM((images, POS, C), BF16),
        pltpu.VMEM((C, 3 * C), BF16),
        pltpu.VMEM((2, 3 * C, HALF), F32),
    ]


def run_forward(x0, w, small, eo, staged=False):
    images = x0.shape[0]
    return pl.pallas_call(
        functools.partial(forward_kernel, staged),
        out_shape=saved_shapes(images),
        in_specs=vm(4),
        out_specs=vm(7),
        scratch_shapes=scratch_forward(images),
        compiler_params=pltpu.CompilerParams(vmem_limit_bytes=VMEM_LIMIT),
    )(x0, w, small, eo)


def run_backward(cot, w, small, eo, saved, want):
    images = cot.shape[0]
    outs = [jax.ShapeDtypeStruct(cot.shape, F32)]
    if want:
        outs += [
            jax.ShapeDtypeStruct((2, ROWS, C), BF16),
            jax.ShapeDtypeStruct((2, 16, C), F32),
        ]
    return pl.pallas_call(
        functools.partial(backward_kernel, want),
        out_shape=outs,
        in_specs=vm(11),
        out_specs=vm(len(outs)),
        scratch_shapes=scratch_forward(images)
        + [
            pltpu.VMEM((images, POS, C), F32),
            pltpu.VMEM((images, POS, 3 * C), BF16),
            pltpu.VMEM((C, images * POS), BF16),
        ],
        compiler_params=pltpu.CompilerParams(vmem_limit_bytes=VMEM_LIMIT),
    )(cot, w, small, eo, *saved)


PLANES, PLANE = 4, 4
MESH = pl.DeviceIdType.MESH


class Place:
    def __init__(self):
        self.sec = lax.axis_index("section")
        self.d = lax.axis_index("dp")
        self.x = lax.rem(self.d, 2)
        self.y = lax.rem(self.d // 2, 2)
        self.z = self.d // PLANE
        self.seat = self.sec * PLANE + lax.rem(self.d, PLANE)
        self.sib = {"section": 1 - self.sec}
        self.xn = {"dp": self.d + 1 - 2 * self.x}
        self.yn = {"dp": self.d + 2 - 4 * self.y}

    def plane(self, j):
        return lax.rem(self.z + j + PLANES, PLANES)

    def zpeer(self, j):
        return {"dp": self.plane(j) * PLANE + lax.rem(self.d, PLANE)}

    def plane_peer(self, j):
        seat = lax.rem(self.seat + j, 2 * PLANE)
        return {"section": seat // PLANE, "dp": self.z * PLANE + lax.rem(seat, PLANE)}

    def meet(self):
        barrier = pltpu.get_barrier_semaphore()
        others = [self.plane_peer(j) for j in range(1, 8)] + [self.zpeer(j) for j in (1, 2, 3)]
        for other in others:
            pl.semaphore_signal(barrier, inc=1, device_id=other, device_id_type=MESH)
        pl.semaphore_wait(barrier, len(others))


def remote(src, dst, send, recv, target):
    return pltpu.make_async_remote_copy(
        src_ref=src, dst_ref=dst, send_sem=send, recv_sem=recv,
        device_id=target, device_id_type=MESH,
    )


Z1, X1, Y1, X2, Y2, S_OWN, S_X, S_Y, S_DA, S_DB = range(0, 40, 4)
Z_UP, Z_DOWN = 40, 41
SLOTS = 42


class Gather:
    def __init__(self, me, net, stage, local_sem, send_sem, recv_sem):
        self.me, self.net, self.stage = me, net, stage
        self.local_sem, self.send_sem, self.recv_sem = local_sem, send_sem, recv_sem
        self.part = stage.shape[0]
        self.half = self.part // 2

    def near(self, k):
        z = self.me.z
        if k == 1:
            return z + 1 - 2 * lax.rem(z, 2), 3 - z
        return (z, z) if k == 0 else (2 - z // 2 if k == 2 else 3 - 3 * (z // 2), 3 * z - 3)

    def rows(self, plane, y, x, lo, count):
        at = (plane * PLANE + y * 2 + x) * self.part + lo
        return self.net.at[self.me.sec, pl.ds(pl.multiple_of(at, 16), count)]

    def own(self, plane):
        return self.rows(plane, self.me.y, self.me.x, 0, self.part)

    def at_plane(self, plane):
        return {"dp": plane * PLANE + lax.rem(self.me.d, PLANE)}

    def send(self, slot, piece, target, src=None, sent=None):
        src = piece if src is None else src
        sent = slot if sent is None else sent
        remote(src, piece, self.send_sem.at[sent], self.recv_sem.at[slot], target).start()

    def arrived(self, slot, piece):
        remote(
            piece, piece, self.send_sem.at[slot], self.recv_sem.at[slot], self.me.sib
        ).wait_recv()

    def local(self):
        return pltpu.make_async_copy(self.stage, self.own(self.me.z), self.local_sem)

    def begin(self):
        me = self.me
        z, own = me.z, self.own(me.z)
        pl.when(z < 3)(lambda: self.send(Z1 + z, own, self.at_plane(z + 1), self.stage, Z_UP))
        pl.when(z > 0)(lambda: self.send(Z1 + z, own, self.at_plane(z - 1), self.stage, Z_DOWN))
        for slot, target in ((X1, me.xn), (Y1, me.yn), (S_OWN, me.sib)):
            self.send(slot + z, own, target, self.stage)
        self.local().start()

    def phase1(self):
        def step(k):
            me = self.me
            plane, target = self.near(k)
            rows = self.own(plane)
            self.arrived(Z1 + plane, rows)
            pl.when(me.z * (3 - me.z) > 0)(
                lambda: self.send(Z1 + plane, rows, self.at_plane(target))
            )
            for slot, to in ((X1, me.xn), (Y1, me.yn), (S_OWN, me.sib)):
                self.send(slot + plane, rows, to)

        return [lambda k=k: step(k) for k in (1, 2, 3)]

    def phase2(self):
        me, part, half = self.me, self.part, self.half

        def step_x(k):
            plane, _ = self.near(k)
            self.arrived(X1 + plane, self.rows(plane, me.y, 1 - me.x, 0, part))
            self.send(Y2 + plane, self.rows(plane, me.y, 1 - me.x, 0, half), me.yn)
            self.send(S_X + plane, self.rows(plane, me.y, 1 - me.x, 0, part), me.sib)

        def step_y(k):
            plane, _ = self.near(k)
            self.arrived(Y1 + plane, self.rows(plane, 1 - me.y, me.x, 0, part))
            self.send(X2 + plane, self.rows(plane, 1 - me.y, me.x, half, half), me.xn)
            self.send(S_Y + plane, self.rows(plane, 1 - me.y, me.x, 0, part), me.sib)

        return [lambda f=f, k=k: f(k) for k in range(PLANES) for f in (step_x, step_y)]

    def phase3(self):
        def step(k, slot, to, lo):
            me = self.me
            plane, _ = self.near(k)
            where = self.rows(plane, 1 - me.y, 1 - me.x, lo, self.half)
            self.arrived(slot + plane, where)
            self.send(to + plane, where, me.sib)

        return [
            lambda k=k, a=a: step(k, *a)
            for k in range(PLANES)
            for a in ((Y2, S_DA, 0), (X2, S_DB, self.half))
        ]

    def finish(self):
        def step():
            for slot in range(S_OWN, Z_UP):
                count = self.part if slot < S_DA else self.half
                self.arrived(slot, self.rows(0, 0, 0, 0, count))
            self.local().wait()

        return [step]

    def sent(self, slot, count):
        piece = self.rows(0, 0, 0, 0, count)
        remote(
            piece, piece, self.send_sem.at[slot], self.recv_sem.at[0], self.me.sib
        ).wait_send()

    def drain(self):
        me, part = self.me, self.part
        pl.when(me.z < 3)(lambda: self.sent(Z_UP, part))
        pl.when(me.z > 0)(lambda: self.sent(Z_DOWN, part))

        @pl.when(me.z * (3 - me.z) > 0)
        def _():
            for k in (1, 2, 3):
                self.sent(Z1 + self.near(k)[0], part)

        for slot in range(X1, Z_UP):
            whole = slot < X2 or S_OWN <= slot < S_DA
            self.sent(slot, part if whole else self.half)


A_SLOT, B_SLOT, C_SLOT, D_SLOT = 0, 4, 20, 28
R_SLOTS = 31


class Reduce:
    def __init__(self, me, big, shard, sib, there, rb, rc, rd, ssem, rsem):
        self.me, self.big, self.shard = me, big, shard
        self.sib, self.there, self.rb, self.rc, self.rd = sib, there, rb, rc, rd
        self.ssem, self.rsem = ssem, rsem
        self.part = shard.shape[0]
        self.half = self.part // 2
        self.span = PLANE * self.part

    def zt(self, k):
        return (3, 2, 0, 1)[k]

    def block(self, k):
        return pl.ds(self.zt(k) * self.span, self.span)

    def piece(self, k, y, x, lo, count):
        at = (self.zt(k) * PLANE + y * 2 + x) * self.part + lo
        return pl.ds(pl.multiple_of(at, 16), count)

    def send(self, src, dst, slot, target):
        remote(src, dst, self.ssem.at[slot], self.rsem.at[slot], target).start()

    def arrived(self, dst, slot):
        remote(dst, dst, self.ssem.at[slot], self.rsem.at[slot], self.me.sib).wait_recv()

    def begin(self):
        for k in range(PLANES):
            self.begin_block(k)

    def begin_block(self, k):
        at = self.block(k)
        self.send(self.big.at[1 - self.me.sec, at], self.there.at[at], A_SLOT + k, self.me.sib)

    def stage_a(self, k):
        me, half = self.me, self.half
        self.arrived(self.sib.at[self.block(k)], A_SLOT + k)
        base = self.zt(k) * self.span

        def body(i, _):
            at = pl.ds(pl.multiple_of(base + i * half, 16), half)
            self.big[me.sec, at, :] = (
                self.big[me.sec, at, :].astype(F32) + self.sib[at, :].astype(F32)
            ).astype(BF16)
            return 0

        lax.fori_loop(0, 2 * PLANE, body, 0)
        for j in range(2):
            self.send(
                self.big.at[me.sec, self.piece(k, 1 - me.y, j, 0, half)], self.rb.at[k, j],
                B_SLOT + 4 * k + j, me.yn,
            )
            self.send(
                self.big.at[me.sec, self.piece(k, j, 1 - me.x, half, half)], self.rb.at[k, 2 + j],
                B_SLOT + 4 * k + 2 + j, me.xn,
            )

    def join(self, where, other):
        self.big[self.me.sec, where, :] = (
            self.big[self.me.sec, where, :].astype(F32) + other.astype(F32)
        ).astype(BF16)

    def stage_c(self, k):
        me, half = self.me, self.half
        for j in range(4):
            self.arrived(self.rb.at[k, j], B_SLOT + 4 * k + j)
            y, x, lo = (me.y, j, 0) if j < 2 else (j - 2, me.x, half)
            self.join(self.piece(k, y, x, lo, half), self.rb[k, j])
        self.send(
            self.big.at[me.sec, self.piece(k, me.y, 1 - me.x, 0, half)], self.rc.at[k, 0],
            C_SLOT + 2 * k, me.xn,
        )
        self.send(
            self.big.at[me.sec, self.piece(k, 1 - me.y, me.x, half, half)], self.rc.at[k, 1],
            C_SLOT + 2 * k + 1, me.yn,
        )

    def stage_d(self, k):
        me, half, zt = self.me, self.half, self.zt(k)
        for j in range(2):
            self.arrived(self.rc.at[k, j], C_SLOT + 2 * k + j)
            self.join(self.piece(k, me.y, me.x, j * half, half), self.rc[k, j])

        @pl.when(me.z != zt)
        def _():
            self.send(
                self.big.at[me.sec, self.piece(k, me.y, me.x, 0, self.part)],
                self.rd.at[lax.rem(zt - me.z + PLANES, PLANES) - 1],
                D_SLOT + lax.rem(zt - me.z + PLANES, PLANES) - 1,
                {"dp": zt * PLANE + lax.rem(me.d, PLANE)},
            )

    def stage_e(self):
        for j in range(PLANES - 1):
            self.arrived(self.rd.at[j], D_SLOT + j)
        at = pl.ds(pl.multiple_of(self.me.d * self.part, 16), self.part)
        self.shard[...] = (
            self.big[self.me.sec, at, :].astype(F32)
            + self.rd[0].astype(F32) + (self.rd[1].astype(F32) + self.rd[2].astype(F32))
        )

    def steps(self):
        out = []
        for t in range(PLANES + 2):
            for stage, lag in ((self.stage_a, 0), (self.stage_c, 1), (self.stage_d, 2)):
                if 0 <= t - lag < PLANES:
                    out.append(lambda stage=stage, k=t - lag: stage(k))
        return out

    def drain(self, lo=0, hi=R_SLOTS):
        for slot in range(lo, hi):
            if slot < B_SLOT:
                piece = self.there.at[pl.ds(0, self.span)]
            elif slot < D_SLOT:
                piece = self.rb.at[0, 0]
            else:
                piece = self.rd.at[0]
            remote(piece, piece, self.ssem.at[slot], self.rsem.at[slot], self.me.sib).wait_send()


def reduce_scratch(part):
    half = part // 2
    return [
        pltpu.VMEM((PLANES, 4, half, C), BF16),
        pltpu.VMEM((PLANES, 2, half, C), BF16),
        pltpu.VMEM((PLANES - 1, part, C), BF16),
        pltpu.SemaphoreType.DMA((R_SLOTS,)),
        pltpu.SemaphoreType.DMA((R_SLOTS,)),
    ]


class Totals:
    def __init__(self, me, buf, recv, ssem, rsem):
        self.me, self.buf, self.recv, self.ssem, self.rsem = me, buf, recv, ssem, rsem

    def send(self, src, dst, slot, target):
        remote(src, dst, self.ssem.at[slot], self.rsem.at[slot], target).start()

    def arrived(self, dst, slot):
        remote(dst, dst, self.ssem.at[slot], self.rsem.at[slot], self.me.sib).wait_recv()

    def begin(self, first):
        self.send(first, self.recv.at[0], 0, self.me.sib)

    def steps(self):
        me, buf, recv = self.me, self.buf, self.recv

        def one():
            self.arrived(recv.at[0], 0)
            buf[1] = buf[0] + recv[0]
            self.send(buf.at[1], recv.at[1], 1, me.xn)

        def two():
            self.arrived(recv.at[1], 1)
            buf[2] = buf[1] + recv[1]
            self.send(buf.at[2], recv.at[2], 2, me.yn)

        def three():
            self.arrived(recv.at[2], 2)
            buf[3] = buf[2] + recv[2]
            recv[3 + me.z] = buf[3]
            for j in (1, 2, 3):
                self.send(buf.at[3], recv.at[3 + me.z], 2 + j, me.zpeer(j))

        return [one, two, three]

    def result(self):
        for j in (1, 2, 3):
            self.arrived(self.recv.at[3 + self.me.plane(-j)], 2 + j)
        return (self.recv[3] + self.recv[4]) + (self.recv[5] + self.recv[6])

    def drain(self):
        for slot in range(6):
            piece = self.recv.at[0]
            remote(piece, piece, self.ssem.at[slot], self.rsem.at[slot], self.me.sib).wait_send()


class Squares:
    def __init__(self, me, own, recv, ssem, rsem):
        self.me, self.own, self.recv, self.ssem, self.rsem = me, own, recv, ssem, rsem

    def hop(self, src, base, mine, peers, slots):
        for j, target in peers:
            dst = self.recv.at[base + mine]
            remote(src, dst, self.ssem.at[slots + j], self.rsem.at[slots + j], target).start()
        self.recv[base + mine] = src[...]
        for j, _ in peers:
            dst = self.recv.at[base]
            remote(dst, dst, self.ssem.at[slots + j], self.rsem.at[slots + j], self.me.sib).wait_recv()

    def run(self):
        me, recv = self.me, self.recv
        self.hop(self.own.at[0], 0, me.seat, [(j, me.plane_peer(j)) for j in range(1, 8)], -1)
        pairs = [recv[2 * k] + recv[2 * k + 1] for k in range(4)]
        self.own[1] = (pairs[0] + pairs[1]) + (pairs[2] + pairs[3])
        self.hop(self.own.at[1], 8, me.z, [(j, me.zpeer(j)) for j in (1, 2, 3)], 6)
        return (recv[8] + recv[9]) + (recv[10] + recv[11])

    def drain(self):
        for slot in range(10):
            piece = self.recv.at[0]
            remote(piece, piece, self.ssem.at[slot], self.rsem.at[slot], self.me.sib).wait_send()


def squares_scratch(shape):
    return [
        pltpu.VMEM((2,) + shape, F32),
        pltpu.VMEM((12,) + shape, F32),
        pltpu.SemaphoreType.DMA((10,)),
        pltpu.SemaphoreType.DMA((10,)),
    ]


def totals_scratch(shape):
    return [
        pltpu.VMEM((4,) + shape, F32),
        pltpu.VMEM((7,) + shape, F32),
        pltpu.SemaphoreType.DMA((6,)),
        pltpu.SemaphoreType.DMA((6,)),
    ]


def saved_scratch(images):
    return [pltpu.VMEM(a.shape, a.dtype) for a in saved_shapes(images)]


def backward_scratch(images):
    return scratch_forward(images) + [
        pltpu.VMEM((images, POS, C), F32),
        pltpu.VMEM((images, POS, 3 * C), BF16),
        pltpu.VMEM((C, images * POS), BF16),
    ]


GEN_TOTAL = SIGMA_INIT**2 + SIGMA_DATA**2
GEN_IN = GEN_TOTAL**-0.5
GEN_SKIP = SIGMA_DATA**2 / GEN_TOTAL
GEN_OUT = SIGMA_INIT * SIGMA_DATA * GEN_TOTAL**-0.5
T_IN, T_SKIP, T_OUT, T_SIGMA, T_FACTOR = range(5)


def fill_embed(eo, sigmas):
    at = lax.broadcasted_iota(jnp.int32, (8, 4 * C), 1)
    side = lax.broadcasted_iota(jnp.int32, (8, 4 * C), 0) // 4
    k = at // 2
    power = (k & (C - 1)).astype(F32) * (1.0 / C)
    rows = sigmas + [jnp.ones_like(sigmas[0])] * (4 - len(sigmas))
    angle = jnp.log(jnp.concatenate(rows + rows, axis=0)) * 0.25 * jnp.exp(power * -LOG_10000)
    wave = jnp.where(k < C, jnp.cos(angle), jnp.sin(angle))
    eo[...] = jnp.where((at & 1) == side, wave, 0.0).astype(BF16)


LOG_10000 = 9.210340371976184


def step_kernel(*refs):
    (
        z_all, eps_all, levels, counts, gen_w, fake_w, teacher_w, gen_small, fake_small,
        teacher_small,
        gw_out, sv_x, sv_h, sv_y, sv_q, sv_a, sv_o, sv_s, gshard, fshard, stot, sqtot,
        *refs,
    ) = refs
    gen_out = (sv_x, sv_h, sv_y, sv_q, sv_a, sv_o, sv_s)
    w_gen, w_fake, w_teach = refs[:3]
    sv_one, sv_two = refs[3:10], refs[10:17]
    bufs, nbuf, qkvw, tmp, dn, dqkv, act_t = refs[17:24]
    zb, eb, g, stage, local_sem, send_sem, recv_sem, copy_sem = refs[24:32]
    smalls, small_sem, gen_eo, score_eo, tab, sgrads, part_sums = refs[32:39]
    fake_refs, gen_refs = refs[39:44], refs[44:49]
    small_refs, square_refs = refs[49:53], refs[53:57]
    sib, free_sem = refs[57:59]
    g2 = sv_two[0].at[2]
    images = zb.shape[0]
    me = Place()
    start = me.sec * images

    def run(steps):
        for step in steps:
            step()

    def mine(ref):
        return ref.at[pl.ds(start, images)]

    loads = [
        pltpu.make_async_copy(mine(z_all), zb, copy_sem.at[0]),
        pltpu.make_async_copy(mine(eps_all), eb, copy_sem.at[1]),
    ]
    for copy in loads:
        copy.start()
    masters = [
        pltpu.make_async_copy(src, dst, copy_sem.at[2 + k])
        for k, (src, dst) in enumerate(((gen_w, gshard), (fake_w, fshard), (teacher_w, stage.at[2])))
    ]
    for copy in masters:
        copy.start()
    smalls[...] = jnp.zeros(smalls.shape, F32)
    for n, ref in enumerate((gen_small, fake_small, teacher_small)):
        for r in range(13):
            smalls[me.sec, n, r : r + 1, :] = ref[r]
    gathers = [
        Gather(me, net, stage.at[n], local_sem.at[n], send_sem.at[n], recv_sem.at[n])
        for n, net in enumerate((w_gen, w_fake, w_teach))
    ]
    for copy in masters:
        copy.wait()
    stage[0] = gshard[...].astype(BF16)
    stage[1] = fshard[...].astype(BF16)
    me.meet()
    gathers[0].begin()
    swap = remote(
        smalls.at[me.sec], smalls.at[me.sec], small_sem.at[0], small_sem.at[1], me.sib
    )
    swap.start()

    clear_pads(bufs)
    sgrads[...] = jnp.zeros(sgrads.shape, F32)
    sigmas = []
    valid_sum = jnp.zeros((1, 4 * C), F32)
    for i in range(images):
        level = jnp.zeros((1, 4 * C), jnp.int32) + levels[start + i]
        sigma = SIGMA_TOP + level.astype(F32) / (LEVELS - 1) * (SIGMA_BOTTOM - SIGMA_TOP)
        square = sigma * sigma
        sigma = square * square * square * sigma
        sigmas.append(sigma)
        s_in, s_skip, s_out, s_lam = precondition(sigma)
        valid = jnp.where(jnp.zeros_like(level) + (start + i) < counts[0], 1.0, 0.0)
        valid_sum = valid_sum + valid
        rows = (s_in, s_skip, s_out, sigma, valid * s_lam * (1.0 / (POS * C)))
        for k, value in enumerate(rows):
            tab[i, k : k + 1, :] = value[:, :C]
    fill_embed(score_eo, sigmas)
    fill_embed(gen_eo, [jnp.full((1, 4 * C), SIGMA_INIT, F32)] * images)

    def forward(n, w, eo, sv, pump):
        def body(l, _):
            layer_forward(
                l, w, smalls.at[:, n], eo, *sv, bufs, nbuf, qkvw, tmp, True, pump
            )
            return 0

        lax.fori_loop(0, 2, body, 0)

    def backward(n, w, eo, sv, cot, grad, sgrad, pump):
        def body(k, _):
            layer_backward(
                1 - k, w, smalls.at[:, n], eo, *sv, cot, bufs, nbuf, qkvw, tmp, dn, dqkv,
                act_t, grad, sgrad, pump,
            )
            return 0

        lax.fori_loop(0, 2, body, 0)

    def each(f):
        def body(i, carry):
            return f(i, [tab[i, k : k + 1, :] for k in range(5)], carry)

        return lax.fori_loop(0, images, body, jnp.zeros((1, C), F32))

    last = gathers[0].phase3()
    run(gathers[0].phase1() + gathers[0].phase2() + last[:6] + [gathers[1].begin] + last[6:])
    for copy in loads:
        copy.wait()
    sv_one[0][0] = zb[...] * (GEN_IN * SIGMA_INIT)
    swap.wait()
    run(gathers[0].finish())
    later = gathers[1].phase1() + gathers[1].phase2()
    forward(0, w_gen, gen_eo, sv_one, Pump(later[:5], FORWARD_POINTS, (0, 1)))
    pairs = [(w_gen, gw_out)] + list(zip(sv_one, gen_out))
    stores = [
        pltpu.make_async_copy(src, dst, copy_sem.at[2 + k]) for k, (src, dst) in enumerate(pairs)
    ]
    for copy in stores:
        copy.start()

    def noisy(i, t, carry):
        zb[i] = zb[i] * (GEN_SKIP * SIGMA_INIT) + GEN_OUT * sv_one[0][2, i]
        eb[i] = zb[i] + t[T_SIGMA] * eb[i]
        sv_two[0][0, i] = t[T_IN] * eb[i]
        return carry

    each(noisy)
    last = gathers[1].phase3()
    run(later[5:] + last[:4] + [gathers[2].begin] + last[4:] + gathers[1].finish())
    later = gathers[2].phase1() + gathers[2].phase2()
    forward(1, w_fake, score_eo, sv_two, Pump(later[:3], FORWARD_POINTS, (0, 1)))
    later = later[3:] + gathers[2].phase3()

    def fake_loss(i, t, total):
        den = t[T_SKIP] * eb[i] + t[T_OUT] * sv_two[0][2, i]
        sv_two[0][2, i] = den
        miss = den - zb[i]
        g[i] = (2.0 * t[T_OUT] * t[T_FACTOR]) * miss
        return total + t[T_FACTOR] * colsum(miss * miss)

    loss_fake = each(fake_loss)
    for copy in stores:
        copy.wait()
    gathers[0].drain()
    backward(
        1, w_fake, score_eo, sv_two, g, w_gen, sgrads.at[:, 1],
        Pump(later, WEIGHT_POINTS, (1, 0), 0.0, 0.8),
    )
    fake_sum = Reduce(me, w_gen, fshard, sib, sib, *fake_refs)
    fake_sum.begin()
    run(gathers[2].finish())
    later = fake_sum.steps()
    sv_one[0][0] = sv_two[0][0]
    forward(2, w_teach, score_eo, sv_one, no_pump)

    def gen_loss(i, t, total):
        den = t[T_SKIP] * eb[i] + t[T_OUT] * sv_one[0][2, i]
        fake_den = sv_two[0][2, i]
        miss = fake_den - zb[i]
        gap = den - fake_den
        scale = t[T_OUT] * t[T_FACTOR]
        g[i] = scale * ((2.0 * (1.0 - ALPHA_MIX)) * gap + miss)
        g2[i] = scale * ((1.0 - 2.0 * (1.0 - ALPHA_MIX)) * gap - miss)
        zb[i] = (t[T_FACTOR] * (t[T_SKIP] - 1.0)) * gap
        return total + t[T_FACTOR] * colsum(gap * ((1.0 - ALPHA_MIX) * gap + miss))

    loss_gen = each(gen_loss)
    backward(
        2, w_teach, score_eo, sv_one, g, None, None, Pump(later[:4], BACKWARD_POINTS, (1, 0))
    )
    gathers[2].drain()
    fake_sum.drain(A_SLOT, B_SLOT)
    pl.semaphore_signal(free_sem, inc=1, device_id=me.sib, device_id_type=MESH)
    back = [
        pltpu.make_async_copy(src, dst, copy_sem.at[2 + k])
        for k, (dst, src) in enumerate([(w_teach, gw_out)] + list(zip(sv_one, gen_out)))
    ]
    for copy in back:
        copy.start()
    backward(
        1, w_fake, score_eo, sv_two, g2, None, None, Pump(later[4:8], BACKWARD_POINTS, (1, 0))
    )

    def gen_gradient(i, t, carry):
        g[i] = GEN_OUT * (zb[i] + t[T_IN] * (g[i] + g2[i]))
        return carry

    each(gen_gradient)
    gathers[1].drain()
    for copy in back:
        copy.wait()

    gen_sum = Reduce(me, w_fake, gshard, w_gen.at[1 - me.sec], w_gen.at[me.sec], *gen_refs)
    fake_steps, later = later, gen_sum.steps()

    def on_section(s, steps):
        pl.when(me.sec == s)(lambda: run(steps))

    def hand_over():
        pl.semaphore_wait(free_sem, 1)

    pump = Pump([], WEIGHT_POINTS, (1, 0))

    def at(layer, point, section, steps):
        pump.table[layer][point].append(lambda: on_section(section, steps))

    upper = [hand_over, lambda: gen_sum.begin_block(0), lambda: gen_sum.begin_block(1)]
    lower = [lambda: gen_sum.begin_block(2), lambda: gen_sum.begin_block(3)]
    for layer, giver in ((1, 0), (0, 1)):
        at(layer, HALF_WAY, giver, upper)
        at(layer, READY, giver, lower)
    for k, point in enumerate((2, 7, 12, 16)):
        pump.table[1][point].append(fake_steps[8 + k])
    for k, point in enumerate((1, 2, 5, 6, 7, 9, 10, 13, 16)):
        at(0, point, 1, later[k : k + 1])
    backward(0, w_teach, gen_eo, sv_one, g, w_fake, sgrads.at[:, 0], pump)

    def spread_sum(total):
        return jnp.broadcast_to(jnp.sum(total, axis=1, keepdims=True), (1, C))

    sums = jnp.concatenate([spread_sum(loss_gen), spread_sum(loss_fake), valid_sum[:, :C]], axis=0)
    for s in range(2):
        part_sums[s, 0:16, :] = sgrads[s, 0]
        part_sums[s, 13:16, :] = sums
        part_sums[s, 16:32, :] = sgrads[s, 1]
    small = Totals(me, *small_refs)
    small_refs[0][0] = part_sums[me.sec]
    small.begin(part_sums.at[1 - me.sec])
    fake_sum.stage_e()
    small_steps = small.steps()
    on_section(0, later[:3])
    on_section(1, later[9:])
    run(small_steps[:1])
    on_section(0, later[3:6])
    run(small_steps[1:2])
    on_section(0, later[6:9])
    run(small_steps[2:])
    on_section(0, later[9:])
    stot[...] = small.result()
    own = square_refs[0]
    keep = lax.broadcasted_iota(jnp.int32, (16, C), 0) < 13
    for n, rows in ((1, fshard), (0, gshard)):
        if n == 0:
            gen_sum.stage_e()
        low = jnp.square(jnp.where(keep, stot[16 * n : 16 * n + 16, :], 0.0))
        low = jnp.where(me.d == 0, low[0:8] + low[8:16], 0.0)
        big = jnp.sum(jnp.square(rows[...]).reshape(rows.shape[0] // 8, 8, C), axis=0)
        own[0, 8 * n : 8 * n + 8, :] = big + low
    square = Squares(me, *square_refs)
    sqtot[...] = square.run()
    fake_sum.drain(B_SLOT)
    for done in (gen_sum, small, square):
        done.drain()


SIGMA_TOP = SIGMA_HIGH ** (1.0 / RHO_POWER)
SIGMA_BOTTOM = SIGMA_LOW ** (1.0 / RHO_POWER)


def run_step(z, eps, levels, counts, gen_w, fake_w, teacher_w, smalls):
    part = gen_w.shape[0]
    images = z.shape[0] // 2
    any_ = pl.BlockSpec(memory_space=pl.ANY)
    smem = pl.BlockSpec(memory_space=pltpu.SMEM)
    saved = saved_shapes(images)
    return pl.pallas_call(
        step_kernel,
        out_shape=[jax.ShapeDtypeStruct((2, ROWS, C), BF16)]
        + saved
        + [
            jax.ShapeDtypeStruct((part, C), F32),
            jax.ShapeDtypeStruct((part, C), F32),
            jax.ShapeDtypeStruct((32, C), F32),
            jax.ShapeDtypeStruct((16, C), F32),
        ],
        in_specs=[any_] * 2 + [smem] * 2 + [any_] * 3 + vm(3),
        out_specs=[any_] * 8 + vm(4),
        scratch_shapes=[pltpu.VMEM((2, ROWS, C), BF16)] * 3
        + saved_scratch(images) * 2
        + backward_scratch(images)
        + [pltpu.VMEM((images, POS, C), F32)] * 3
        + [
            pltpu.VMEM((3, part, C), BF16),
            pltpu.SemaphoreType.DMA((3,)),
            pltpu.SemaphoreType.DMA((3, SLOTS)),
            pltpu.SemaphoreType.DMA((3, SLOTS)),
            pltpu.SemaphoreType.DMA((10,)),
            pltpu.VMEM((2, 3, 16, C), F32),
            pltpu.SemaphoreType.DMA((2,)),
            pltpu.VMEM((8, 4 * C), BF16),
            pltpu.VMEM((8, 4 * C), BF16),
            pltpu.VMEM((images, 8, C), F32),
            pltpu.VMEM((2, 2, 16, C), F32),
            pltpu.VMEM((2, 32, C), F32),
        ]
        + reduce_scratch(part) * 2
        + totals_scratch((32, C))
        + squares_scratch((16, C))
        + [pltpu.VMEM((ROWS, C), BF16), pltpu.SemaphoreType.REGULAR],
        compiler_params=pltpu.CompilerParams(
            collective_id=0, has_side_effects=True, vmem_limit_bytes=STEP_LIMIT
        ),
    )(z, eps, levels, counts, gen_w, fake_w, teacher_w, *smalls)[8:]


def adam_step(master, first_mom, second_mom, grad):
    first_new = BETA_ONE * first_mom + (1.0 - BETA_ONE) * grad
    second_new = BETA_TWO * second_mom + (1.0 - BETA_TWO) * grad * grad
    direction = (
        first_new
        / (1.0 - BETA_ONE**STEP)
        / (jnp.sqrt(second_new / (1.0 - BETA_TWO**STEP)) + ADAM_EPS)
    )
    return (master - LEARN_RATE * (direction + WEIGHT_DECAY * master), first_new, second_new)


EMA_RATE = 0.5 ** (20.0 / STEP)
SMALL_STATES = (4, 5, 6, 7, 11, 12, 13)


def update_kernel(gshard, fshard, stot, sqtot, *refs):
    ins, outs = refs[:14], refs[14:]
    norms, losses = outs[14:]
    count = stot[15:16, 0:1]
    norm_of, scales = [], []
    for n in range(2):
        rows = jnp.sum(sqtot[8 * n : 8 * n + 8, :], axis=0, keepdims=True)
        norm = jnp.sqrt(jnp.sum(rows, axis=1, keepdims=True)) / count
        scales.append(jnp.minimum(1.0, CLIP_NORM / norm) / count)
        norm_of.append(norm)

    def one(at, grad, w, m, v, ema, ow, om, ov, oe):
        new, first, second = adam_step(w[at], m[at], v[at], grad)
        ow[at] = new
        om[at] = first
        ov[at] = second
        if ema is not None:
            oe[at] = EMA_RATE * ema[at] + (1.0 - EMA_RATE) * new

    one(0, gshard[...] * scales[0], *ins[0:4], *outs[0:4])
    one(0, fshard[...] * scales[1], *ins[8:11], None, *outs[8:11], None)

    first = lax.broadcasted_iota(jnp.int32, (1, 2), 1) == 0
    norms[...] = jnp.where(first, norm_of[0], norm_of[1])
    losses[...] = jnp.where(first, stot[13:14, 0:1], stot[14:15, 0:1]) / count
    for k in range(13):
        one(k, stot[k : k + 1, :] * scales[0], *ins[4:8], *outs[4:8])
        one(k, stot[16 + k : 17 + k, :] * scales[1], *ins[11:14], None, *outs[11:14], None)


def update_nets(gshard, fshard, stot, sqtot, states):
    def turned(arrays):
        return [a.swapaxes(0, 1) if k in SMALL_STATES else a for k, a in enumerate(arrays)]

    states = turned(states)
    res = pl.pallas_call(
        update_kernel,
        out_shape=[jax.ShapeDtypeStruct(a.shape, F32) for a in states]
        + [jax.ShapeDtypeStruct((1, 2), F32)] * 2,
        in_specs=vm(4 + len(states)),
        out_specs=vm(2 + len(states)),
        compiler_params=pltpu.CompilerParams(vmem_limit_bytes=VMEM_LIMIT),
    )(gshard, fshard, stot, sqtot, *states)
    return tuple(turned(res[:-2])) + (res[-2][0], res[-1][0])


def gather_plain(shard):
    rows = lax.all_gather(shard.astype(BF16), "dp", axis=1, tiled=True)
    return lax.all_gather(rows, "section", axis=0, tiled=True)


def reduce_plain(bigs, small):
    shards_, squares = [], []
    own = lax.psum_scatter(small, "section", scatter_dimension=0, tiled=True)
    stot = lax.psum(own, "dp")[0]
    first = lax.axis_index("dp") == 0
    for n, big in enumerate(bigs):
        own = lax.psum_scatter(big, "section", scatter_dimension=0, tiled=True)
        own = lax.psum_scatter(own, "dp", scatter_dimension=1, tiled=True)[0].astype(F32)
        shards_.append(own)
        low = jnp.sum(jnp.square(stot[16 * n : 16 * n + 13]))
        squares.append(jnp.sum(own * own) + jnp.where(first, low, 0.0))
    sq = lax.psum(jnp.stack(squares), ("section", "dp"))
    return *shards_, stot, jnp.zeros((16, C), F32).at[jnp.array([0, 8]), 0].set(sq)


def shards(
    z_noise, eps_noise, levels, counts,
    gen_w, gen_m, gen_v, gen_ema, gen_small, gen_small_m, gen_small_v, gen_small_ema,
    fake_w, fake_m, fake_v, fake_small, fake_small_m, fake_small_v,
    teacher_w, teacher_small,
):
    if lax.axis_size("dp") == PLANES * PLANE:
        smalls = [a.swapaxes(0, 1) for a in (gen_small, fake_small, teacher_small)]
        reduced = run_step(
            z_noise, eps_noise, levels, counts, gen_w[0], fake_w[0], teacher_w[0], smalls
        )
    else:
        reduced = plain_step(
            z_noise, eps_noise, levels, counts, gen_w, fake_w, teacher_w,
            gen_small, fake_small, teacher_small,
        )
    return update_nets(
        *reduced,
        (
            gen_w, gen_m, gen_v, gen_ema, gen_small, gen_small_m, gen_small_v, gen_small_ema,
            fake_w, fake_m, fake_v, fake_small, fake_small_m, fake_small_v,
        ),
    )


def plain_step(
    z_noise, eps_noise, levels, counts, gen_w, fake_w, teacher_w,
    gen_small, fake_small, teacher_small,
):
    images = z_noise.shape[0] // lax.axis_size("section")
    start = lax.axis_index("section") * images

    def mine(a):
        return lax.dynamic_slice_in_dim(a, start, images, 0)

    z, eps = mine(z_noise), mine(eps_noise)
    sigma = sigma_levels(mine(levels))
    valid = (start + jnp.arange(images) < counts[0]).astype(F32)
    valid_sum = jnp.sum(valid)
    gen_eo = spread_embed(jnp.full((images,), SIGMA_INIT, F32))
    score_eo = spread_embed(sigma)
    gs, fs, ts = [
        lax.all_gather(a, "section", axis=0, tiled=True)
        for a in (gen_small, fake_small, teacher_small)
    ]
    gw, fw, tw = gather_plain(gen_w), gather_plain(fake_w), gather_plain(teacher_w)
    s_in, s_skip, s_out, s_lam = precondition(sigma)
    factor = valid * s_lam / (POS * C)
    s_in, s_skip, s_out, sigma, factor = [
        t[:, None, None] for t in (s_in, s_skip, s_out, sigma, factor)
    ]
    raw = SIGMA_INIT * z
    gen_saved = run_forward(GEN_IN * raw, gw, gs, gen_eo)
    samples = GEN_SKIP * raw + GEN_OUT * gen_saved[0][2]
    noisy = samples + sigma * eps
    x0 = s_in * noisy
    fake_saved = run_forward(x0, fw, fs, score_eo)
    fake_den = s_skip * noisy + s_out * fake_saved[0][2]
    miss = fake_den - samples
    _, fake_g, fake_sg = run_backward(
        s_out * 2.0 * factor * miss, fw, fs, score_eo, fake_saved, True
    )
    teacher_saved = run_forward(x0, tw, ts, score_eo)
    teacher_den = s_skip * noisy + s_out * teacher_saved[0][2]
    gap = teacher_den - fake_den
    loss_gen = jnp.sum(factor * ((1.0 - ALPHA_MIX) * gap * gap + gap * miss))
    loss_fake = jnp.sum(factor * miss * miss)
    grad_teacher = factor * (2.0 * (1.0 - ALPHA_MIX) * gap + miss)
    grad_fake = factor * gap - grad_teacher
    direct = factor * gap * (s_skip - 1.0)
    (back_t,) = run_backward(s_out * grad_teacher, tw, ts, score_eo, teacher_saved, False)
    (back_f,) = run_backward(s_out * grad_fake, fw, fs, score_eo, fake_saved, False)
    gen_cot = GEN_OUT * (direct + s_in * (back_t + back_f))
    _, gen_g, gen_sg = run_backward(gen_cot, gw, gs, gen_eo, gen_saved, True)
    scalars = jnp.broadcast_to(jnp.stack([loss_gen, loss_fake, valid_sum])[:, None], (3, C))
    small_sums = jnp.concatenate(
        [gen_sg[:, :13], jnp.broadcast_to(scalars, (2, 3, C)), fake_sg], axis=1
    )
    return reduce_plain((gen_g, fake_g), small_sums)


def solution(mesh):
    images = P("dp", None, None)
    big = P("section", "dp", None)
    small = P("section", None, None)
    return jax.shard_map(
        shards,
        mesh=mesh,
        in_specs=(images, images, P("dp"), P("dp"))
        + (big,) * 4 + (small,) * 4 + (big,) * 3 + (small,) * 3 + (big, small),
        out_specs=(big,) * 4 + (small,) * 4 + (big,) * 3 + (small,) * 3 + (P(), P()),
        check_vma=False,
    )
```
